32 devices in a mesh: img: 2 (over x), row: 4 (over y, core), col: 4 (over z).
Axes of the slice: x: 2, y: 2, z: 4, core: 2. Of those that a mesh axis runs over, the one named last changes fastest.
Arguments:
- grid_elements: bfloat16 [256, 128, 768], P(('img', 'row'), 'col'), parts along dimension 0, may hold values from -6 to 6
- summary_vectors: bfloat16 [16, 8, 768], P(('img', 'row'), 'col'), parts along dimension 0, may hold values from -6 to 6
- triple_projection: bfloat16 [768, 2304], P(None, 'row'), may hold values from -0.375 to 0.375
- final_projection: bfloat16 [768, 768], P(None, 'row'), may hold values from -0.21875 to 0.21875
- genuine_flags: int32 [256, 128], P(('img', 'row'), 'col'), parts along dimension 0, may hold values 0 or 1
Outputs:
- element_result: bfloat16 [256, 128, 768], P(('img', 'row'), 'col'), parts along dimension 0
- summary_result: bfloat16 [16, 8, 768], P(('img', 'row'), 'col'), parts along dimension 0
The draws below stay inside these ranges and needn't reach their ends.
There are 2 independent parts, one for each index of `img`. The reference program is written for one: setup_inputs(seed, part) draws one part's arguments, and reference() takes and returns one part's arrays. A program takes and returns all parts, laid end to end along the dimension named above; an argument that names none is the same for every part. Nothing has to cross between parts.
All inputs are finite; a program needn't handle non-finite values. No bound on the sum of `genuine_flags` on one device may be relied on, other than what follows from the above.
Results may differ from the reference program's by a relative error of at most 0.0096.
Values may be sent and summed in bfloat16 or wider, within the bound.
No kernel may reach another device: no remote copies, remote signals or barrier semaphores. Data moves between devices by JAX's collectives and lax.ppermute only.
A program may use at most 64 MiB of HBM per device.

```python
import jax
import jax.numpy as jnp
from jax import lax

EMBED_SPAN = 768
HEAD_DIM = 64
HEADS = 12
PATCH_SIDE = 16
RADIUS = 4
GRID_TALL = 128
GRID_BROAD = 128
SUMMARY_TALL = 8
SUMMARY_BROAD = 8
KT = 24


def set_ends(drawn, key, smallest, top_value):
    shape = drawn.shape
    place = [jax.random.randint(jax.random.fold_in(key, axis), (), 0, shape[axis]) for axis in range(len(shape))]
    drawn = drawn.at[tuple(place)].set(smallest)
    longest = shape.index(max(shape))
    place[longest] = (place[longest] + 1) % shape[longest]
    return drawn.at[tuple(place)].set(top_value)


def shard_levels(rng, extent, pieces, smallest, top_value):
    loudness, own = 1.0, jax.random.fold_in(rng, 6)
    for position, shards_of in pieces:
        draws = jnp.exp(jax.random.uniform(jax.random.fold_in(own, position), (shards_of,), jnp.float32, smallest / len(pieces), top_value / len(pieces)))
        loudness = loudness * jnp.repeat(draws, extent[position] // shards_of).reshape([-1 if axis == position else 1 for axis in range(len(extent))])
    return loudness


def centred(key, dims, scale, most, pieces=(), held_as=jnp.bfloat16):
    drawn = jax.random.normal(key, dims, jnp.float32) * scale
    if len(pieces) > 0:
        drawn = shard_levels(key, dims, pieces, -0.22, 0.18) * drawn
    return jnp.clip(drawn, min=-most, max=most).astype(held_as)


def setup_inputs(seed: int = 0, part: int = 0) -> dict:
    streams_of = jax.random.split(jax.random.key(seed), 6)
    own_keys = jax.random.split(jax.random.fold_in(streams_of[5], part), 6)
    grid_elements = centred(own_keys[0], (GRID_TALL, GRID_BROAD, EMBED_SPAN), 1.0, 6.0, ((0, 4), (1, 4)))
    summary_vectors = centred(own_keys[1], (SUMMARY_TALL, SUMMARY_BROAD, EMBED_SPAN), 1.0, 6.0, ((0, 4), (1, 4)))
    triple_projection = centred(streams_of[2], (EMBED_SPAN, 3 * EMBED_SPAN), (EMBED_SPAN // 3) ** -0.5, 0.375, ((1, 4),))
    final_projection = centred(streams_of[3], (EMBED_SPAN, EMBED_SPAN), EMBED_SPAN ** -0.5, 0.21875, ((1, 4),))
    genuine_flags = set_ends((jax.random.randint(own_keys[4], (GRID_TALL, GRID_BROAD), 0, 4) < 3).astype(jnp.int32), jax.random.fold_in(own_keys[4], 1), 0, 1)
    return {"grid_elements": grid_elements, "summary_vectors": summary_vectors, "triple_projection": triple_projection, "final_projection": final_projection, "genuine_flags": genuine_flags}


def layer_normalise(payload_lines):
    payload_lines = payload_lines.astype(jnp.float32)
    center = payload_lines - lax.optimization_barrier(jnp.mean(payload_lines, axis=-1, keepdims=True))
    spread = lax.optimization_barrier(jnp.mean(center * center, axis=-1, keepdims=True))
    return center * lax.rsqrt(spread + 1e-05)

def summary_attention(asking_lines, lookup_lines, payload_lines, attention_branches, logit_factor):
    query_count = asking_lines.shape[0]
    key_count = lookup_lines.shape[0]
    asking_branches = asking_lines.astype(jnp.float32).reshape(query_count, attention_branches, -1)
    k_heads = lookup_lines.astype(jnp.float32).reshape(key_count, attention_branches, -1)
    v_heads = payload_lines.astype(jnp.float32).reshape(key_count, attention_branches, -1)
    scores = jnp.einsum('qhd,khd->hqk', asking_branches, k_heads) * logit_factor
    logit_exponential = jnp.exp(scores)
    weights = (logit_exponential / lax.optimization_barrier(jnp.sum(logit_exponential, axis=-1, keepdims=True))).astype(jnp.bfloat16)
    blended_channels = jnp.einsum('hqk,khd->qhd', weights.astype(jnp.float32), v_heads)
    return blended_channels.reshape(query_count, -1).astype(jnp.bfloat16)

def band_mask(window_side, tile_side, reach):
    query_pos = jnp.arange(window_side * window_side, dtype=jnp.int32)
    key_pos = jnp.arange(tile_side * tile_side, dtype=jnp.int32)
    row_step = key_pos[None, :] // tile_side - query_pos[:, None] // window_side
    col_step = key_pos[None, :] % tile_side - query_pos[:, None] % window_side
    return (row_step >= 0) & (row_step <= 2 * reach) & (col_step >= 0) & (col_step <= 2 * reach)

def local_attention(asking_lines, lookup_lines, payload_lines, visibility_matrix, summary_lookup, summary_payload, attention_branches, logit_factor):
    query_count = asking_lines.shape[0]
    key_count = lookup_lines.shape[0]
    asking_branches = asking_lines.astype(jnp.float32).reshape(query_count, attention_branches, -1)
    k_heads = lookup_lines.astype(jnp.float32).reshape(key_count, attention_branches, -1)
    v_heads = payload_lines.astype(jnp.float32).reshape(key_count, attention_branches, -1)
    summary_lookup_lines = summary_lookup.astype(jnp.float32).reshape(attention_branches, -1)
    summary_payload_lines = summary_payload.astype(jnp.float32).reshape(attention_branches, -1)
    scores = jnp.einsum('qhd,khd->hqk', asking_branches, k_heads) * logit_factor
    summary_logits = jnp.einsum('zry,ry->rz', asking_branches, summary_lookup_lines) * logit_factor
    logit_exponential = jnp.where(visibility_matrix[None, :, :], jnp.exp(scores), 0.0)
    summary_exponential = jnp.exp(summary_logits)
    normaliser_total = lax.optimization_barrier(jnp.sum(logit_exponential, axis=-1)) + summary_exponential
    weights = (logit_exponential / normaliser_total[:, :, None]).astype(jnp.bfloat16)
    summary_attention_dist = (summary_exponential / normaliser_total).astype(jnp.bfloat16)
    blended_channels = jnp.einsum('hqk,khd->qhd', weights.astype(jnp.float32), v_heads)
    blended_channels = blended_channels + jnp.einsum('qh,qv->hqv', summary_attention_dist.astype(jnp.float32), summary_payload_lines)
    return blended_channels.reshape(query_count, -1).astype(jnp.bfloat16)

def reference(grid_elements, summary_vectors, triple_projection, final_projection, genuine_flags):
    attention_branches = HEADS
    logit_factor = HEAD_DIM ** (-0.5)
    summary_sequence = summary_vectors.reshape(SUMMARY_TALL * SUMMARY_BROAD, EMBED_SPAN)
    summary_gain_vector = layer_normalise(summary_sequence).astype(jnp.bfloat16)
    summary_projected_triple = jnp.dot(summary_gain_vector, triple_projection, preferred_element_type=jnp.float32).astype(jnp.bfloat16)
    blended_summaries = summary_attention(summary_projected_triple[:, :EMBED_SPAN], summary_projected_triple[:, EMBED_SPAN:2 * EMBED_SPAN], summary_projected_triple[:, 2 * EMBED_SPAN:], attention_branches, logit_factor)
    renewed_summaries = summary_sequence.astype(jnp.float32) + jnp.dot(blended_summaries, final_projection, preferred_element_type=jnp.float32)
    summary_result = renewed_summaries.astype(jnp.bfloat16).reshape(SUMMARY_TALL, SUMMARY_BROAD, EMBED_SPAN)
    summary_lookup_payload = jnp.dot(layer_normalise(renewed_summaries).astype(jnp.bfloat16), triple_projection[:, EMBED_SPAN:], preferred_element_type=jnp.float32).astype(jnp.bfloat16)
    token_norm = layer_normalise(grid_elements.reshape(GRID_TALL * GRID_BROAD, EMBED_SPAN)).astype(jnp.bfloat16)
    token_qkv = jnp.dot(token_norm, triple_projection, preferred_element_type=jnp.float32).astype(jnp.bfloat16).reshape(GRID_TALL, GRID_BROAD, 3 * EMBED_SPAN)
    padded_kv = jnp.pad(token_qkv[:, :, EMBED_SPAN:], ((RADIUS, RADIUS), (RADIUS, RADIUS), (0, 0)))
    padded_valid = jnp.pad(genuine_flags, ((RADIUS, RADIUS), (RADIUS, RADIUS)))
    allowed_band = band_mask(PATCH_SIDE, KT, RADIUS)
    zero_index = jnp.zeros((), jnp.int32)

    def single_patch(patch_position):
        patch_line = (patch_position // SUMMARY_BROAD).astype(jnp.int32) * PATCH_SIDE
        patch_column = (patch_position % SUMMARY_BROAD).astype(jnp.int32) * PATCH_SIDE
        asking_lines = lax.dynamic_slice(token_qkv, (patch_line, patch_column, zero_index), (PATCH_SIDE, PATCH_SIDE, EMBED_SPAN)).reshape(PATCH_SIDE * PATCH_SIDE, EMBED_SPAN)
        patch_lookups = lax.dynamic_slice(padded_kv, (patch_line, patch_column, zero_index), (KT, KT, 2 * EMBED_SPAN)).reshape(KT * KT, 2 * EMBED_SPAN)
        usable = lax.dynamic_slice(padded_valid, (patch_line, patch_column), (KT, KT)).reshape(KT * KT)
        visibility_matrix = allowed_band & (usable[None, :] > 0)
        summary_line = summary_lookup_payload[patch_position]
        return local_attention(asking_lines, patch_lookups[:, :EMBED_SPAN], patch_lookups[:, EMBED_SPAN:], visibility_matrix, summary_line[:EMBED_SPAN], summary_line[EMBED_SPAN:], attention_branches, logit_factor)
    blended_channels = lax.map(single_patch, jnp.arange(SUMMARY_TALL * SUMMARY_BROAD, dtype=jnp.int32))
    blended_channels = blended_channels.reshape(SUMMARY_TALL, SUMMARY_BROAD, PATCH_SIDE, PATCH_SIDE, EMBED_SPAN).transpose(0, 2, 1, 3, 4).reshape(GRID_TALL * GRID_BROAD, EMBED_SPAN)
    tokens_new = grid_elements.reshape(GRID_TALL * GRID_BROAD, EMBED_SPAN).astype(jnp.float32) + jnp.dot(blended_channels, final_projection, preferred_element_type=jnp.float32)
    element_result = tokens_new.astype(jnp.bfloat16).reshape(GRID_TALL, GRID_BROAD, EMBED_SPAN)
    return (element_result, summary_result)
```

```python
import jax
import jax.numpy as jnp
from jax import lax
from jax.sharding import PartitionSpec as P

HEAD_DIM = 64
PATCH_SIDE = 16
RADIUS = 4


def with_halo(block, sides, width):
    for axis, dim in sides:
        count = lax.axis_size(axis)
        forward = [(i, i + 1) for i in range(count - 1)]
        backward = [(target, source) for source, target in forward]
        low = lax.ppermute(
            lax.slice_in_dim(block, block.shape[dim] - width, None, axis=dim), axis, forward
        )
        high = lax.ppermute(lax.slice_in_dim(block, 0, width, axis=dim), axis, backward)
        block = jnp.concatenate([low, block, high], axis=dim)
    return block


def gather_all(triple_projection, final_projection, summary_sequence):
    channels = triple_projection.shape[0]
    img, row, col = lax.axis_size("img"), lax.axis_size("row"), lax.axis_size("col")
    triple_t, final_t = triple_projection.T, final_projection.T
    pieces = img * col
    if triple_t.shape[0] % (8 * pieces) or final_t.shape[0] % (8 * pieces):
        return (
            lax.all_gather(triple_t, "row", axis=0, tiled=True),
            lax.all_gather(final_t, "row", axis=0, tiled=True),
            lax.all_gather(summary_sequence, ("row", "col"), axis=0, tiled=True),
        )
    mine = lax.axis_index("img") * col + lax.axis_index("col")
    triple_rows, final_rows = triple_t.shape[0] // pieces, final_t.shape[0] // pieces
    carrier_rows = summary_sequence.shape[0]
    spare = -carrier_rows % 8
    pack = jnp.concatenate(
        [
            lax.dynamic_slice_in_dim(triple_t, mine * triple_rows, triple_rows),
            lax.dynamic_slice_in_dim(final_t, mine * final_rows, final_rows),
            summary_sequence,
            jnp.zeros((spare, channels), summary_sequence.dtype),
        ]
    )
    whole = lax.all_gather(pack, ("row", "img", "col"), axis=0)
    triple_all = whole[:, :triple_rows].reshape(-1, channels)
    final_all = whole[:, triple_rows : triple_rows + final_rows].reshape(-1, channels)
    first = triple_rows + final_rows
    carriers = whole[:, first : first + carrier_rows].reshape(row, img, col * carrier_rows, channels)
    carriers = lax.dynamic_index_in_dim(carriers, lax.axis_index("img"), 1, keepdims=False)
    return triple_all, final_all, carriers.reshape(-1, channels)


def layer_normalise(payload_lines):
    payload_lines = payload_lines.astype(jnp.float32)
    center = payload_lines - jnp.mean(payload_lines, axis=-1, keepdims=True)
    spread = jnp.mean(center * center, axis=-1, keepdims=True)
    return center * lax.rsqrt(spread + 1e-05)


def summary_attention(asking_lines, lookup_lines, payload_lines, attention_branches, logit_factor):
    query_count = asking_lines.shape[0]
    key_count = lookup_lines.shape[0]
    asking_branches = asking_lines.reshape(query_count, attention_branches, -1)
    k_heads = lookup_lines.reshape(key_count, attention_branches, -1)
    v_heads = payload_lines.reshape(key_count, attention_branches, -1)
    scores = (
        jnp.einsum("qhd,khd->hqk", asking_branches, k_heads, preferred_element_type=jnp.float32)
        * logit_factor
    )
    logit_exponential = jnp.exp(scores)
    weights = (logit_exponential / jnp.sum(logit_exponential, axis=-1, keepdims=True)).astype(
        jnp.bfloat16
    )
    blended_channels = jnp.einsum(
        "hqk,khd->qhd", weights, v_heads, preferred_element_type=jnp.float32
    )
    return blended_channels.reshape(query_count, -1).astype(jnp.bfloat16)


def band_mask(window_side, tile_side, reach):
    query_pos = jnp.arange(window_side * window_side, dtype=jnp.int32)
    key_pos = jnp.arange(tile_side * tile_side, dtype=jnp.int32)
    row_step = key_pos[None, :] // tile_side - query_pos[:, None] // window_side
    col_step = key_pos[None, :] % tile_side - query_pos[:, None] % window_side
    return (row_step >= 0) & (row_step <= 2 * reach) & (col_step >= 0) & (col_step <= 2 * reach)


def local_attention(
    asking_lines,
    lookup_lines,
    payload_lines,
    visibility_matrix,
    summary_lookup,
    summary_payload,
    attention_branches,
    logit_factor,
):
    query_count = asking_lines.shape[0]
    key_count = lookup_lines.shape[0]
    asking_branches = asking_lines.reshape(query_count, attention_branches, -1)
    k_heads = lookup_lines.reshape(key_count, attention_branches, -1)
    v_heads = payload_lines.reshape(key_count, attention_branches, -1)
    summary_lookup_lines = summary_lookup.reshape(attention_branches, -1)
    summary_payload_lines = summary_payload.reshape(attention_branches, -1)
    scores = (
        jnp.einsum("qhd,khd->hqk", asking_branches, k_heads, preferred_element_type=jnp.float32)
        * logit_factor
    )
    summary_logits = (
        jnp.einsum(
            "zry,ry->rz", asking_branches, summary_lookup_lines, preferred_element_type=jnp.float32
        )
        * logit_factor
    )
    logit_exponential = jnp.where(visibility_matrix[None, :, :], jnp.exp(scores), 0.0)
    summary_exponential = jnp.exp(summary_logits)
    normaliser_total = jnp.sum(logit_exponential, axis=-1) + summary_exponential
    weights = (logit_exponential / normaliser_total[:, :, None]).astype(jnp.bfloat16)
    summary_attention_dist = (summary_exponential / normaliser_total).astype(jnp.bfloat16)
    blended_channels = jnp.einsum(
        "hqk,khd->qhd", weights, v_heads, preferred_element_type=jnp.float32
    )
    blended_channels = blended_channels + jnp.einsum(
        "qh,qv->hqv",
        summary_attention_dist,
        summary_payload_lines,
        preferred_element_type=jnp.float32,
    )
    return blended_channels.reshape(query_count, -1).astype(jnp.bfloat16)


def local(grid_elements, summary_vectors, triple_projection, final_projection, genuine_flags):
    tile_rows, tile_cols, channel_count = grid_elements.shape
    attention_branches = channel_count // HEAD_DIM
    logit_factor = HEAD_DIM ** (-0.5)
    block_rows = tile_rows // PATCH_SIDE
    block_cols = tile_cols // PATCH_SIDE
    tile_side = PATCH_SIDE + 2 * RADIUS
    summary_sequence = summary_vectors.reshape(-1, channel_count)
    padded_tokens, padded_valid = (
        with_halo(grid_elements, (("row", 0), ("col", 1)), RADIUS),
        with_halo(genuine_flags.astype(jnp.bfloat16), (("row", 0), ("col", 1)), RADIUS),
    )
    token_norm = layer_normalise(padded_tokens.reshape(-1, channel_count)).astype(jnp.bfloat16)
    summary_gain_vector = layer_normalise(summary_sequence).astype(jnp.bfloat16)
    triple_t, final_t, carriers = gather_all(triple_projection, final_projection, summary_sequence)
    matrix_section = triple_t.T
    joined_result = final_t.T
    token_part = jnp.dot(token_norm, matrix_section, preferred_element_type=jnp.float32).astype(
        jnp.bfloat16
    )
    summary_share = jnp.dot(
        summary_gain_vector, matrix_section[:, :channel_count], preferred_element_type=jnp.float32
    ).astype(jnp.bfloat16)
    summary_broadcast = jnp.dot(
        layer_normalise(carriers).astype(jnp.bfloat16),
        matrix_section[:, channel_count:],
        preferred_element_type=jnp.float32,
    ).astype(jnp.bfloat16)
    token_qkv = token_part
    blended_summaries = summary_attention(
        summary_share,
        summary_broadcast[:, :channel_count],
        summary_broadcast[:, channel_count:],
        attention_branches,
        logit_factor,
    )
    renewed_summaries = summary_sequence.astype(jnp.float32) + jnp.dot(
        blended_summaries, joined_result, preferred_element_type=jnp.float32
    )
    summary_result = renewed_summaries.astype(jnp.bfloat16).reshape(summary_vectors.shape)
    summary_lookup_payload = jnp.dot(
        layer_normalise(renewed_summaries).astype(jnp.bfloat16),
        matrix_section[:, channel_count:],
        preferred_element_type=jnp.float32,
    ).astype(jnp.bfloat16)
    whole_qkv = token_qkv.reshape(tile_rows + 2 * RADIUS, tile_cols + 2 * RADIUS, 3 * channel_count)
    padded_kv = whole_qkv[:, :, channel_count:]
    token_qkv = whole_qkv[RADIUS : RADIUS + tile_rows, RADIUS : RADIUS + tile_cols, :]
    allowed_band = band_mask(PATCH_SIDE, tile_side, RADIUS)
    zero_index = jnp.zeros((), jnp.int32)

    def single_patch(patch_position):
        patch_line = patch_position // block_cols * PATCH_SIDE
        patch_column = patch_position % block_cols * PATCH_SIDE
        asking_lines = lax.dynamic_slice(
            token_qkv,
            (patch_line, patch_column, zero_index),
            (PATCH_SIDE, PATCH_SIDE, channel_count),
        ).reshape(PATCH_SIDE * PATCH_SIDE, channel_count)
        patch_lookups = lax.dynamic_slice(
            padded_kv,
            (patch_line, patch_column, zero_index),
            (tile_side, tile_side, 2 * channel_count),
        ).reshape(tile_side * tile_side, 2 * channel_count)
        usable = lax.dynamic_slice(
            padded_valid, (patch_line, patch_column), (tile_side, tile_side)
        ).reshape(tile_side * tile_side)
        visibility_matrix = allowed_band & (usable[None, :] > 0.5)
        summary_line = summary_lookup_payload[patch_position]
        return local_attention(
            asking_lines,
            patch_lookups[:, :channel_count],
            patch_lookups[:, channel_count:],
            visibility_matrix,
            summary_line[:channel_count],
            summary_line[channel_count:],
            attention_branches,
            logit_factor,
        )

    blended_channels = lax.map(single_patch, jnp.arange(block_rows * block_cols, dtype=jnp.int32))
    blended_channels = (
        blended_channels.reshape(block_rows, block_cols, PATCH_SIDE, PATCH_SIDE, channel_count)
        .transpose(0, 2, 1, 3, 4)
        .reshape(tile_rows * tile_cols, channel_count)
    )
    tokens_new = grid_elements.reshape(-1, channel_count).astype(jnp.float32) + jnp.dot(
        blended_channels, joined_result, preferred_element_type=jnp.float32
    )
    element_result = tokens_new.astype(jnp.bfloat16).reshape(tile_rows, tile_cols, channel_count)
    return (element_result, summary_result)


def solution(mesh):
    placed = (
        P(("img", "row"), "col", None),
        P(("img", "row"), "col", None),
        P(None, "row"),
        P(None, "row"),
        P(("img", "row"), "col"),
    )
    return jax.shard_map(
        local,
        mesh=mesh,
        in_specs=placed,
        out_specs=(P(("img", "row"), "col", None), P(("img", "row"), "col", None)),
        check_vma=False,
    )
```

```python
import functools

import jax
import jax.numpy as jnp
from jax import lax
from jax.experimental import pallas as pl
from jax.experimental.pallas import tpu as pltpu
from jax.sharding import PartitionSpec as P

HEAD_DIM = 64
PATCH_SIDE = 16
RADIUS = 4
TILE = 2 * RADIUS
LANES = 128
GROUP = 256
INVALID = 100.0
HIDDEN = -1e30
VMEM_BYTES = 56 * 1024 * 1024


def nt(a, b):
    return lax.dot_general(a, b, (((1,), (1,)), ((), ())), preferred_element_type=jnp.float32)


def nn(a, b):
    return lax.dot_general(a, b, (((1,), (0,)), ((), ())), preferred_element_type=jnp.float32)


def layer_normalise(lines):
    center = lines - jnp.mean(lines, axis=-1, keepdims=True)
    spread = jnp.mean(center * center, axis=-1, keepdims=True)
    return center * lax.rsqrt(spread + 1e-05)


def shifted(block, axis, step, fill):
    count = lax.axis_size(axis)
    pairs = [(i, i + step) for i in range(count) if 0 <= i + step < count]
    got = lax.ppermute(block, axis, pairs)
    me = lax.axis_index(axis)
    edge = (me == 0) if step > 0 else (me == count - 1)
    return jnp.where(edge, jnp.asarray(fill, block.dtype), got)


def swapped(block, axis, bit):
    count = lax.axis_size(axis)
    return lax.ppermute(block, axis, [(i, i ^ bit) for i in range(count)])


def bits_of(count):
    bits, bit = [], count // 2
    while bit:
        bits.append(bit)
        bit //= 2
    return bits


def prepare_kernel(x_ref, mark_ref, top_ref, bottom_ref, left_ref, right_ref, xq_ref, xkv_ref, hide_ref, pad, flag_pad):
    rows, cols, _ = x_ref.shape
    wide_rows, wide_cols = rows + 2 * RADIUS, cols + 2 * RADIUS
    half = wide_rows // 2
    step = 2

    def own(i, _):
        at = pl.multiple_of(i * step, step)
        y = layer_normalise(x_ref[pl.ds(at, step)].astype(jnp.float32))
        for c in range(cols // TILE):
            piece = y[:, c * TILE : (c + 1) * TILE, :].reshape(step * TILE, -1)
            to = pl.multiple_of(c * rows * TILE + at * TILE, step * TILE)
            xq_ref[pl.ds(to, step * TILE), :] = piece.astype(jnp.bfloat16)
        pad[pl.ds(RADIUS + at, step), RADIUS : RADIUS + cols, :] = y
        flag_pad[pl.ds(RADIUS + at, step), RADIUS : RADIUS + cols, :] = mark_ref[pl.ds(at, step)].astype(jnp.float32)
        return 0

    lax.fori_loop(0, rows // step, own, 0)
    for ref, first in ((top_ref, 0), (bottom_ref, RADIUS + rows)):
        for i in range(0, RADIUS, step):
            lines = ref[i : i + step].astype(jnp.float32)
            pad[first + i : first + i + step, RADIUS : RADIUS + cols, :] = layer_normalise(lines)
            flag_pad[first + i : first + i + step, RADIUS : RADIUS + cols, :] = lines[:, :, :LANES]

    for ref, first in ((left_ref, 0), (right_ref, RADIUS + cols)):
        def side(i, _):
            lines = ref[pl.ds(i, 1)].astype(jnp.float32)
            y = layer_normalise(lines)
            for part in range(2):
                at = slice(part * RADIUS, (part + 1) * RADIUS)
                pad[pl.ds(part * half + i, 1), first : first + RADIUS, :] = y[:, at, :]
                flag_pad[pl.ds(part * half + i, 1), first : first + RADIUS, :] = lines[:, at, :LANES]
            return 0

        lax.fori_loop(0, half, side, 0)

    for c in range(wide_cols // TILE):
        def block(i, _):
            at = pl.multiple_of(i * step, step)
            to = pl.multiple_of(c * wide_rows * TILE + at * TILE, step * TILE)
            lines = pad[pl.ds(at, step), c * TILE : (c + 1) * TILE, :]
            xkv_ref[pl.ds(to, step * TILE), :] = lines.reshape(step * TILE, -1).astype(jnp.bfloat16)
            return 0

        lax.fori_loop(0, wide_rows // step, block, 0)

    first_lane = (lax.broadcasted_iota(jnp.int32, (8, LANES), 1) == 0).astype(jnp.bfloat16)
    spans = []
    for c in range(wide_cols // TILE):
        lines = flag_pad[:, c * TILE : (c + 1) * TILE, :].reshape(wide_rows * TILE, LANES)
        spans.append(jnp.where(nt(first_lane, lines.astype(jnp.bfloat16)) > INVALID / 2, HIDDEN, 0.0))
    tall = rows // TILE
    for c in range(cols // TILE):
        for r in range(tall):
            at = slice(r * TILE * TILE, r * TILE * TILE + 2 * TILE * TILE)
            hide_ref[c * tall + r] = jnp.concatenate([spans[c][:, at], spans[c + 1][:, at]], axis=1)


def block_kernel(offsets, place_ref, x_ref, xq_ref, xkv_ref, hide_ref, own_ref, *refs):
    packs = refs[: len(offsets)]
    out_ref, summary_ref, wt, wo, q_s, kv_s, mix_s, kce, vc_s = refs[len(offsets) :]
    rows, cols, channels = x_ref.shape
    groups = channels // GROUP
    heads = channels // HEAD_DIM
    heads_in = GROUP // HEAD_DIM
    wide_rows = rows + 2 * RADIUS
    factor = HEAD_DIM ** (-0.5)
    carriers_here = own_ref.shape[0]
    me = place_ref[0]
    shards = len(offsets)
    triple_rows, final_rows = wt.shape[0] // shards, wo.shape[0] // shards
    for off, pack in zip(offsets, packs):
        shard = me ^ off
        wt[pl.ds(pl.multiple_of(shard * triple_rows, 16), triple_rows), :] = pack[:triple_rows, :]
        wo[pl.ds(pl.multiple_of(shard * final_rows, 16), final_rows), :] = pack[triple_rows : triple_rows + final_rows, :]

    q_rows, kv_rows = xq_ref.shape[0], xkv_ref.shape[0]
    q_chunk, kv_chunk = q_rows // 4, kv_rows // 5

    def project_q(n, _):
        w = wt[pl.ds(pl.multiple_of(n * GROUP, GROUP), GROUP), :]
        for m in range(0, q_rows, q_chunk):
            q_s[n, m : m + q_chunk, :] = (nt(xq_ref[m : m + q_chunk, :], w) * factor).astype(jnp.bfloat16)
        return 0

    def project_kv(n, _):
        w = wt[pl.ds(pl.multiple_of(channels + n * GROUP, GROUP), GROUP), :]
        for m in range(0, kv_rows, kv_chunk):
            kv_s[n, m : m + kv_chunk, :] = nt(xkv_ref[m : m + kv_chunk, :], w).astype(jnp.bfloat16)
        return 0

    lax.fori_loop(0, groups, project_q, 0)
    lax.fori_loop(0, 2 * groups, project_kv, 0)

    first = triple_rows + final_rows
    carriers = jnp.concatenate([pack[first:, :].astype(jnp.float32) for pack in packs], axis=0)
    carriers = layer_normalise(carriers).astype(jnp.bfloat16)
    own = own_ref[...]
    own_norm = layer_normalise(own).astype(jnp.bfloat16)
    qc = (nt(own_norm, wt[:channels, :]) * factor).astype(jnp.bfloat16).astype(jnp.float32)
    kc = nt(carriers, wt[channels : 2 * channels, :]).astype(jnp.bfloat16)
    vc = nt(carriers, wt[2 * channels :, :]).astype(jnp.bfloat16)
    head_of = lax.broadcasted_iota(jnp.int32, (1, channels), 1) // HEAD_DIM
    stacked = jnp.concatenate([jnp.where(head_of == h, qc, 0.0) for h in range(heads)], axis=0)
    e = jnp.exp(nt(stacked.astype(jnp.bfloat16), kc))
    weights = (e / jnp.sum(e, axis=-1, keepdims=True)).astype(jnp.bfloat16)
    o = nn(weights, vc)
    mix = jnp.zeros((carriers_here, channels), jnp.float32)
    for h in range(heads):
        mix = jnp.where(head_of == h, o[h * carriers_here : (h + 1) * carriers_here, :], mix)
    renewed = own + nt(mix.astype(jnp.bfloat16), wo[...])
    summary_ref[...] = renewed
    fresh = nt(layer_normalise(renewed).astype(jnp.bfloat16), wt[channels:, :]).astype(jnp.bfloat16).astype(jnp.float32)
    vc_s[...] = fresh[:, channels:]
    same = (
        lax.broadcasted_iota(jnp.int32, (GROUP, GROUP), 0) // HEAD_DIM
        == lax.broadcasted_iota(jnp.int32, (GROUP, GROUP), 1) // HEAD_DIM
    )
    windows = kce.shape[0] // groups
    for w in range(windows):
        for g in range(groups):
            kce[w * groups + g] = jnp.where(same, fresh[w : w + 1, g * GROUP : (g + 1) * GROUP], 0.0).astype(jnp.bfloat16)

    queries, span = TILE * TILE, 2 * TILE * TILE
    qi = lax.broadcasted_iota(jnp.int32, (queries, 2 * span), 0)
    ki = lax.broadcasted_iota(jnp.int32, (queries, 2 * span), 1)
    row_step = (ki % span) // TILE - qi // TILE
    col_step = (ki // span) * TILE + ki % TILE - qi % TILE
    seen = (row_step >= 0) & (row_step <= 2 * RADIUS) & (col_step >= 0) & (col_step <= 2 * RADIUS)
    band = jnp.where(seen, 0.0, HIDDEN)
    group_head = lax.broadcasted_iota(jnp.int32, (1, GROUP), 1) // HEAD_DIM
    tall, broad = rows // TILE, cols // TILE
    per_side = PATCH_SIDE // TILE

    def tile(t, _):
        c, r = t // tall, t % tall
        q_at = pl.multiple_of(c * (rows * TILE) + r * queries, queries)
        k0 = pl.multiple_of(c * (wide_rows * TILE) + r * queries, queries)
        k1 = pl.multiple_of(k0 + wide_rows * TILE, queries)
        window = (r // per_side) * (broad // per_side) + c // per_side
        bias = band + hide_ref[t][0:1, :]
        for g in range(groups):
            q = q_s[g, pl.ds(q_at, queries), :]
            q32 = q.astype(jnp.float32)
            qq = jnp.concatenate(
                [jnp.where(group_head == h, q32, 0.0).astype(jnp.bfloat16) for h in range(heads_in)], axis=0
            )
            k = jnp.concatenate([kv_s[g, pl.ds(k0, span), :], kv_s[g, pl.ds(k1, span), :]], axis=0)
            v = jnp.concatenate(
                [kv_s[groups + g, pl.ds(k0, span), :], kv_s[groups + g, pl.ds(k1, span), :]], axis=0
            )
            p = jnp.exp(nt(qq, k).reshape(heads_in, queries, 2 * span) + bias[None])
            total = jnp.sum(p, axis=-1, keepdims=True)
            o = nn(p.reshape(heads_in * queries, 2 * span).astype(jnp.bfloat16), v)
            o = o.reshape(heads_in, queries, GROUP)
            kept, kept_total = o[0], total[0]
            for h in range(1, heads_in):
                kept = jnp.where(group_head == h, o[h], kept)
                kept_total = jnp.where(group_head == h, total[h], kept_total)
            pc = jnp.exp(nt(q, kce[window * groups + g]))
            v_new = vc_s[pl.ds(window, 1), g * GROUP : (g + 1) * GROUP]
            mixed = (kept + pc * v_new) / (kept_total + pc)
            mix_s[pl.ds(q_at, queries), g * GROUP : (g + 1) * GROUP] = mixed.astype(jnp.bfloat16)
        return 0

    lax.fori_loop(0, tall * broad, tile, 0)

    for pair in range(broad // 2):
        for g in range(groups):
            at = slice(g * GROUP, (g + 1) * GROUP)
            w = wo[at, :]
            parts = [
                nt(mix_s[b * rows * TILE : (b + 1) * rows * TILE, :], w).reshape(rows, TILE, GROUP)
                for b in (2 * pair, 2 * pair + 1)
            ]
            both = slice(2 * pair * TILE, 2 * (pair + 1) * TILE)
            y = jnp.concatenate(parts, axis=1) + x_ref[:, both, at].astype(jnp.float32)
            out_ref[:, both, at] = y.astype(jnp.bfloat16)


def local(grid_elements, summary_vectors, triple_projection, final_projection, genuine_flags):
    rows, cols, channels = grid_elements.shape
    wide_rows, wide_cols = rows + 2 * RADIUS, cols + 2 * RADIUS
    own = summary_vectors.reshape(-1, channels)

    carriers = own
    for bit in bits_of(lax.axis_size("col")):
        carriers = jnp.concatenate([carriers, swapped(carriers, "col", bit)], axis=0)
    pack = jnp.concatenate([triple_projection.T, final_projection.T, carriers], axis=0)

    marked = jnp.where(genuine_flags[:, :, None] > 0, grid_elements, jnp.asarray(INVALID, grid_elements.dtype))
    top = shifted(marked[rows - RADIUS :], "row", 1, INVALID)
    bottom = shifted(marked[:RADIUS], "row", -1, INVALID)

    packs, offsets = [pack], [0]
    for bit in bits_of(lax.axis_size("row")):
        packs = packs + [swapped(p, "row", bit) for p in packs]
        offsets = offsets + [o ^ bit for o in offsets]

    def edge(at):
        strip = jnp.concatenate([top[:, at], marked[:, at], bottom[:, at]], axis=0)
        return jnp.concatenate([strip[: wide_rows // 2], strip[wide_rows // 2 :]], axis=1)

    left = shifted(edge(slice(cols - RADIUS, None)), "col", 1, INVALID)
    right = shifted(edge(slice(0, RADIUS)), "col", -1, INVALID)

    mark = jnp.where(genuine_flags[:, :, None] > 0, 0.0, INVALID).astype(jnp.bfloat16)
    mark = jnp.broadcast_to(mark, (rows, cols, LANES))
    tiles = (rows // TILE) * (cols // TILE)
    keys = 4 * TILE * TILE
    vmem = pl.BlockSpec(memory_space=pltpu.VMEM)
    xq, xkv, hide = pl.pallas_call(
        prepare_kernel,
        out_shape=(
            jax.ShapeDtypeStruct((rows * cols, channels), jnp.bfloat16),
            jax.ShapeDtypeStruct((wide_rows * wide_cols, channels), jnp.bfloat16),
            jax.ShapeDtypeStruct((tiles, 8, keys), jnp.float32),
        ),
        in_specs=[vmem] * 6,
        out_specs=(vmem,) * 3,
        scratch_shapes=[
            pltpu.VMEM((wide_rows, wide_cols, channels), jnp.float32),
            pltpu.VMEM((wide_rows, wide_cols, LANES), jnp.float32),
        ],
        compiler_params=pltpu.CompilerParams(vmem_limit_bytes=VMEM_BYTES),
        cost_estimate=pl.CostEstimate(flops=20_000_000, bytes_accessed=8_000_000, transcendentals=3000),
        name="prepare",
    )(grid_elements, mark, top, bottom, left, right)

    groups = channels // GROUP
    own_lines = own.astype(jnp.float32)
    spare = -own.shape[0] % 8
    own_lines = jnp.concatenate([own_lines, jnp.zeros((spare, channels), jnp.float32)], axis=0)
    place = lax.axis_index("row").astype(jnp.int32).reshape(1)
    out, renewed = pl.pallas_call(
        functools.partial(block_kernel, offsets),
        out_shape=(
            jax.ShapeDtypeStruct(grid_elements.shape, jnp.bfloat16),
            jax.ShapeDtypeStruct(own_lines.shape, jnp.float32),
        ),
        in_specs=[pl.BlockSpec(memory_space=pltpu.SMEM)] + [vmem] * (5 + len(packs)),
        out_specs=(vmem,) * 2,
        scratch_shapes=[
            pltpu.VMEM((3 * channels, channels), jnp.bfloat16),
            pltpu.VMEM((channels, channels), jnp.bfloat16),
            pltpu.VMEM((groups, rows * cols, GROUP), jnp.bfloat16),
            pltpu.VMEM((2 * groups, wide_rows * wide_cols, GROUP), jnp.bfloat16),
            pltpu.VMEM((rows * cols, channels), jnp.bfloat16),
            pltpu.VMEM((own.shape[0] * groups, GROUP, GROUP), jnp.bfloat16),
            pltpu.VMEM((own_lines.shape[0], channels), jnp.float32),
        ],
        compiler_params=pltpu.CompilerParams(vmem_limit_bytes=VMEM_BYTES),
        cost_estimate=pl.CostEstimate(flops=10_000_000_000, bytes_accessed=12_000_000, transcendentals=4_000_000),
        name="block",
    )(place, grid_elements, xq, xkv, hide, own_lines, *packs)
    summary_result = renewed[: own.shape[0]].astype(jnp.bfloat16).reshape(summary_vectors.shape)
    return (out, summary_result)


def solution(mesh):
    placed = (
        P(("img", "row"), "col", None),
        P(("img", "row"), "col", None),
        P(None, "row"),
        P(None, "row"),
        P(("img", "row"), "col"),
    )
    return jax.shard_map(
        local,
        mesh=mesh,
        in_specs=placed,
        out_specs=(P(("img", "row"), "col", None), P(("img", "row"), "col", None)),
        check_vma=False,
    )
```

```python
import functools

import jax
import jax.numpy as jnp
from jax import lax
from jax.experimental import pallas as pl
from jax.experimental.pallas import tpu as pltpu
from jax.sharding import PartitionSpec as P

HEAD_DIM = 64
PATCH_SIDE = 16
RADIUS = 4
TILE = 2 * RADIUS
LANES = 128
GROUP = 256
INVALID = 100.0
HIDDEN = -1e30
VMEM_BYTES = 40 * 1024 * 1024


def nt(a, b):
    return lax.dot_general(a, b, (((1,), (1,)), ((), ())), preferred_element_type=jnp.float32)


def nn(a, b):
    return lax.dot_general(a, b, (((1,), (0,)), ((), ())), preferred_element_type=jnp.float32)


def layer_normalise(lines):
    center = lines - jnp.mean(lines, axis=-1, keepdims=True)
    spread = jnp.mean(center * center, axis=-1, keepdims=True)
    return center * lax.rsqrt(spread + 1e-05)


def shifted(block, axis, step, fill):
    count = lax.axis_size(axis)
    pairs = [(i, i + step) for i in range(count) if 0 <= i + step < count]
    got = lax.ppermute(block, axis, pairs)
    me = lax.axis_index(axis)
    edge = (me == 0) if step > 0 else (me == count - 1)
    return jnp.where(edge, jnp.asarray(fill, block.dtype), got)


def swapped(block, axis, bit):
    count = lax.axis_size(axis)
    return lax.ppermute(block, axis, [(i, i ^ bit) for i in range(count)])


def bits_of(count):
    bits, bit = [], count // 2
    while bit:
        bits.append(bit)
        bit //= 2
    return bits


def own_kernel(x_ref, xq_ref):
    rows, cols, _ = x_ref.shape
    step = 4

    def own(i, _):
        at = pl.multiple_of(i * step, step)
        y = layer_normalise(x_ref[pl.ds(at, step)].astype(jnp.float32))
        for c in range(cols // TILE):
            piece = y[:, c * TILE : (c + 1) * TILE, :].reshape(step * TILE, -1)
            to = pl.multiple_of(c * rows * TILE + at * TILE, step * TILE)
            xq_ref[pl.ds(to, step * TILE), :] = piece.astype(jnp.bfloat16)
        return 0

    lax.fori_loop(0, rows // step, own, 0)


def halo_kernel(xq_ref, mark_ref, top_ref, bottom_ref, left_ref, right_ref, xkv_ref, hide_ref, top_s, bottom_s, left_s, right_s, flag_s):
    rows, cols, _ = mark_ref.shape
    wide_rows, wide_cols = rows + 2 * RADIUS, cols + 2 * RADIUS
    half = wide_rows // 2
    step = 2
    for ref, out, size in ((top_ref, top_s, 2), (bottom_ref, bottom_s, 2), (left_ref, left_s, 5), (right_ref, right_s, 5)):
        for i in range(0, ref.shape[0], size):
            out[i : i + size] = layer_normalise(ref[i : i + size].astype(jnp.float32))

    def lines_of(ref):
        return ref.astype(jnp.float32)

    def merge(at, blocks, left, right, to_ref):
        low = lax.broadcasted_iota(jnp.int32, (1, TILE, 1), 1) < RADIUS
        before = left
        for c in range(len(blocks) + 1):
            after = jnp.roll(blocks[c], RADIUS, axis=1) if c < len(blocks) else right
            to = c * wide_rows * TILE + at * TILE
            to = pl.multiple_of(to, step * TILE) if not isinstance(to, int) else to
            lines = jnp.where(low, before, after).reshape(step * TILE, -1)
            to_ref[pl.ds(to, step * TILE), :] = lines.astype(jnp.bfloat16)
            before = after

    def sides(at, upper, left_ref, right_ref, lanes):
        if upper:
            at = at - half
            left, right = jnp.roll(lines_of(left_ref[pl.ds(at, step), :, lanes]), RADIUS, axis=1), lines_of(
                right_ref[pl.ds(at, step), :, lanes]
            )
        else:
            left, right = lines_of(left_ref[pl.ds(at, step), :, lanes]), jnp.roll(
                lines_of(right_ref[pl.ds(at, step), :, lanes]), RADIUS, axis=1
            )
        return left, right

    every, few = slice(None), slice(0, LANES)

    def band(at, ref, ref_s, first, upper):
        cut = [slice(c * TILE, (c + 1) * TILE) for c in range(cols // TILE)]
        merge(at, [ref_s[first : first + step, k, :] for k in cut], *sides(at, upper, left_s, right_s, every), xkv_ref)
        marks = ref[first : first + step, :, :LANES].astype(jnp.float32)
        merge(at, [marks[:, k, :] for k in cut], *sides(at, upper, left_ref, right_ref, few), flag_s)

    for i in range(0, RADIUS, step):
        band(i, top_ref, top_s, i, False)
        band(RADIUS + rows + i, bottom_ref, bottom_s, i, True)

    def middle(i, upper):
        at = pl.multiple_of(i * step, step)
        own = at - RADIUS
        blocks = []
        for c in range(cols // TILE):
            first = pl.multiple_of(c * rows * TILE + own * TILE, step * TILE)
            blocks.append(xq_ref[pl.ds(first, step * TILE), :].astype(jnp.float32).reshape(step, TILE, -1))
        merge(at, blocks, *sides(at, upper, left_s, right_s, every), xkv_ref)
        marks = mark_ref[pl.ds(own, step)].astype(jnp.float32)
        marks = [marks[:, c * TILE : (c + 1) * TILE, :] for c in range(cols // TILE)]
        merge(at, marks, *sides(at, upper, left_ref, right_ref, few), flag_s)
        return 0

    lax.fori_loop(RADIUS // step, half // step, lambda i, _: middle(i, False), 0)
    lax.fori_loop(half // step, (RADIUS + rows) // step, lambda i, _: middle(i, True), 0)

    first_lane = (lax.broadcasted_iota(jnp.int32, (8, LANES), 1) == 0).astype(jnp.bfloat16)
    spans = []
    for c in range(wide_cols // TILE):
        lines = flag_s[c * wide_rows * TILE : (c + 1) * wide_rows * TILE, :]
        spans.append(jnp.where(nt(first_lane, lines) > INVALID / 2, HIDDEN, 0.0))
    tall = rows // TILE
    for c in range(cols // TILE):
        for r in range(tall):
            at = slice(r * TILE * TILE, r * TILE * TILE + 2 * TILE * TILE)
            hide_ref[c * tall + r] = jnp.concatenate([spans[c][:, at], spans[c + 1][:, at]], axis=1)


def block_kernel(offsets, place_ref, hide_ref, own_ref, carriers_ref, x_hbm, xq_hbm, xkv_hbm, *refs):
    shards = len(offsets)
    triples, finals = refs[:shards], refs[shards : 2 * shards]
    out_hbm, summary_ref, x_ref, xq_ref, xkv_ref, out_ref, wt, wo, q_s, kv_s, mix_s, kce, vc_s, sems, out_sems = refs[2 * shards :]
    rows, cols, channels = x_ref.shape
    groups = channels // GROUP
    heads = channels // HEAD_DIM
    heads_in = GROUP // HEAD_DIM
    wide_rows = rows + 2 * RADIUS
    factor = HEAD_DIM ** (-0.5)
    carriers_here = own_ref.shape[0]
    me = place_ref[0]
    triple_rows, final_rows = wt.shape[0] // shards, wo.shape[0] // shards

    def coming(source, target, number):
        copy = pltpu.make_async_copy(source, target, sems.at[number])
        copy.start()
        return copy

    wt_copies, wo_copies = [], []
    for j, off in enumerate(offsets):
        to = pl.multiple_of((me ^ off) * triple_rows, 16)
        wt_copies.append(coming(triples[j], wt.at[pl.ds(to, triple_rows), :], j))
    xq_copy = coming(xq_hbm, xq_ref, 2 * shards)
    xkv_copy = coming(xkv_hbm, xkv_ref, 2 * shards + 1)
    for j, off in enumerate(offsets):
        to = pl.multiple_of((me ^ off) * final_rows, 16)
        wo_copies.append(coming(finals[j], wo.at[pl.ds(to, final_rows), :], shards + j))
    x_copy = coming(x_hbm, x_ref, 2 * shards + 2)

    q_rows, kv_rows = xq_ref.shape[0], xkv_ref.shape[0]
    q_chunk, kv_chunk = q_rows // 4, kv_rows // 5

    def project_q(n, _):
        w = wt[pl.ds(pl.multiple_of(n * GROUP, GROUP), GROUP), :]
        for m in range(0, q_rows, q_chunk):
            q_s[n, m : m + q_chunk, :] = (nt(xq_ref[m : m + q_chunk, :], w) * factor).astype(jnp.bfloat16)
        return 0

    def project_kv(n, _):
        w = wt[pl.ds(pl.multiple_of(channels + n * GROUP, GROUP), GROUP), :]
        for m in range(0, kv_rows, kv_chunk):
            kv_s[n, m : m + kv_chunk, :] = nt(xkv_ref[m : m + kv_chunk, :], w).astype(jnp.bfloat16)
        return 0

    for copy in wt_copies:
        copy.wait()
    xq_copy.wait()
    lax.fori_loop(0, groups, project_q, 0)
    xkv_copy.wait()
    lax.fori_loop(0, 2 * groups, project_kv, 0)

    for copy in wo_copies:
        copy.wait()
    carriers = layer_normalise(carriers_ref[...].astype(jnp.float32)).astype(jnp.bfloat16)
    own = own_ref[...]
    own_norm = layer_normalise(own).astype(jnp.bfloat16)
    qc = (nt(own_norm, wt[:channels, :]) * factor).astype(jnp.bfloat16).astype(jnp.float32)
    kc = nt(carriers, wt[channels : 2 * channels, :]).astype(jnp.bfloat16)
    vc = nt(carriers, wt[2 * channels :, :]).astype(jnp.bfloat16)
    head_of = lax.broadcasted_iota(jnp.int32, (1, channels), 1) // HEAD_DIM
    stacked = jnp.concatenate([jnp.where(head_of == h, qc, 0.0) for h in range(heads)], axis=0)
    e = jnp.exp(nt(stacked.astype(jnp.bfloat16), kc))
    weights = (e / jnp.sum(e, axis=-1, keepdims=True)).astype(jnp.bfloat16)
    o = nn(weights, vc)
    mix = jnp.zeros((carriers_here, channels), jnp.float32)
    for h in range(heads):
        mix = jnp.where(head_of == h, o[h * carriers_here : (h + 1) * carriers_here, :], mix)
    renewed = own + nt(mix.astype(jnp.bfloat16), wo[...])
    summary_ref[...] = renewed
    fresh = nt(layer_normalise(renewed).astype(jnp.bfloat16), wt[channels:, :]).astype(jnp.bfloat16).astype(jnp.float32)
    vc_s[...] = fresh[:, channels:]
    same = (
        lax.broadcasted_iota(jnp.int32, (GROUP, GROUP), 0) // HEAD_DIM
        == lax.broadcasted_iota(jnp.int32, (GROUP, GROUP), 1) // HEAD_DIM
    )
    windows = kce.shape[0] // groups
    for w in range(windows):
        for g in range(groups):
            kce[w * groups + g] = jnp.where(same, fresh[w : w + 1, g * GROUP : (g + 1) * GROUP], 0.0).astype(jnp.bfloat16)

    queries, span = TILE * TILE, 2 * TILE * TILE
    qi = lax.broadcasted_iota(jnp.int32, (queries, 2 * span), 0)
    ki = lax.broadcasted_iota(jnp.int32, (queries, 2 * span), 1)
    row_step = (ki % span) // TILE - qi // TILE
    col_step = (ki // span) * TILE + ki % TILE - qi % TILE
    seen = (row_step >= 0) & (row_step <= 2 * RADIUS) & (col_step >= 0) & (col_step <= 2 * RADIUS)
    band = jnp.where(seen, 0.0, HIDDEN)
    group_head = lax.broadcasted_iota(jnp.int32, (1, GROUP), 1) // HEAD_DIM
    tall, broad = rows // TILE, cols // TILE
    per_side = PATCH_SIDE // TILE

    def tile(t, _):
        c, r = t // tall, t % tall
        q_at = pl.multiple_of(c * (rows * TILE) + r * queries, queries)
        k0 = pl.multiple_of(c * (wide_rows * TILE) + r * queries, queries)
        k1 = pl.multiple_of(k0 + wide_rows * TILE, queries)
        window = (r // per_side) * (broad // per_side) + c // per_side
        bias = band + hide_ref[t][0:1, :]
        for g in range(groups):
            q = q_s[g, pl.ds(q_at, queries), :]
            q32 = q.astype(jnp.float32)
            qq = jnp.concatenate(
                [jnp.where(group_head == h, q32, 0.0).astype(jnp.bfloat16) for h in range(heads_in)], axis=0
            )
            k = jnp.concatenate([kv_s[g, pl.ds(k0, span), :], kv_s[g, pl.ds(k1, span), :]], axis=0)
            v = jnp.concatenate(
                [kv_s[groups + g, pl.ds(k0, span), :], kv_s[groups + g, pl.ds(k1, span), :]], axis=0
            )
            p = jnp.exp(nt(qq, k).reshape(heads_in, queries, 2 * span) + bias[None])
            total = jnp.sum(p, axis=-1, keepdims=True)
            o = nn(p.reshape(heads_in * queries, 2 * span).astype(jnp.bfloat16), v)
            o = o.reshape(heads_in, queries, GROUP)
            kept, kept_total = o[0], total[0]
            for h in range(1, heads_in):
                kept = jnp.where(group_head == h, o[h], kept)
                kept_total = jnp.where(group_head == h, total[h], kept_total)
            pc = jnp.exp(nt(q, kce[window * groups + g]))
            v_new = vc_s[pl.ds(window, 1), g * GROUP : (g + 1) * GROUP]
            mixed = (kept + pc * v_new) / (kept_total + pc)
            mix_s[pl.ds(q_at, queries), g * GROUP : (g + 1) * GROUP] = mixed.astype(jnp.bfloat16)
        return 0

    lax.fori_loop(0, tall * broad, tile, 0)

    x_copy.wait()
    going = []
    for pair in range(broad // 2):
        both = slice(2 * pair * TILE, 2 * (pair + 1) * TILE)
        for g in range(groups):
            at = slice(g * GROUP, (g + 1) * GROUP)
            w = wo[at, :]
            parts = [
                nt(mix_s[b * rows * TILE : (b + 1) * rows * TILE, :], w).reshape(rows, TILE, GROUP)
                for b in (2 * pair, 2 * pair + 1)
            ]
            y = jnp.concatenate(parts, axis=1) + x_ref[:, both, at].astype(jnp.float32)
            out_ref[pair, :, :, at] = y.astype(jnp.bfloat16)
        copy = pltpu.make_async_copy(out_ref.at[pair], out_hbm.at[:, both, :], out_sems.at[pair])
        copy.start()
        going.append(copy)
    for copy in going:
        copy.wait()


def local(grid_elements, summary_vectors, triple_projection, final_projection, genuine_flags):
    rows, cols, channels = grid_elements.shape
    wide_rows, wide_cols = rows + 2 * RADIUS, cols + 2 * RADIUS
    own = summary_vectors.reshape(-1, channels)

    triple_t, final_t = triple_projection.T, final_projection.T

    marked = jnp.where(genuine_flags[:, :, None] > 0, grid_elements, jnp.asarray(INVALID, grid_elements.dtype))
    top = shifted(marked[rows - RADIUS :], "row", 1, INVALID)
    bottom = shifted(marked[:RADIUS], "row", -1, INVALID)

    finals, triples, offsets = [final_t], [triple_t], [0]
    carriers = own
    for bit in bits_of(lax.axis_size("col")):
        carriers = jnp.concatenate([carriers, swapped(carriers, "col", bit)], axis=0)
    for bit in bits_of(lax.axis_size("row")):
        finals = finals + [swapped(p, "row", bit) for p in finals]
        triples = triples + [swapped(p, "row", bit) for p in triples]
        carriers = jnp.concatenate([carriers, swapped(carriers, "row", bit)], axis=0)
        offsets = offsets + [o ^ bit for o in offsets]

    def edge(at):
        strip = jnp.concatenate([top[:, at], marked[:, at], bottom[:, at]], axis=0)
        return jnp.concatenate([strip[: wide_rows // 2], strip[wide_rows // 2 :]], axis=1)

    left = shifted(edge(slice(cols - RADIUS, None)), "col", 1, INVALID)
    right = shifted(edge(slice(0, RADIUS)), "col", -1, INVALID)

    mark = jnp.where(genuine_flags[:, :, None] > 0, 0.0, INVALID).astype(jnp.bfloat16)
    mark = jnp.broadcast_to(mark, (rows, cols, LANES))
    tiles = (rows // TILE) * (cols // TILE)
    keys = 4 * TILE * TILE
    vmem = pl.BlockSpec(memory_space=pltpu.VMEM)
    anywhere = pl.BlockSpec(memory_space=pl.ANY)
    xq = pl.pallas_call(
        own_kernel,
        out_shape=jax.ShapeDtypeStruct((rows * cols, channels), jnp.bfloat16),
        in_specs=[vmem],
        out_specs=vmem,
        compiler_params=pltpu.CompilerParams(vmem_limit_bytes=16 * 1024 * 1024),
        cost_estimate=pl.CostEstimate(flops=10_000_000, bytes_accessed=3_000_000, transcendentals=1000),
        name="own_norm",
    )(grid_elements)
    xkv, hide = pl.pallas_call(
        halo_kernel,
        out_shape=(
            jax.ShapeDtypeStruct((wide_rows * wide_cols, channels), jnp.bfloat16),
            jax.ShapeDtypeStruct((tiles, 8, keys), jnp.float32),
        ),
        in_specs=[vmem] * 6,
        out_specs=(vmem,) * 2,
        scratch_shapes=[
            pltpu.VMEM(top.shape, jnp.float32),
            pltpu.VMEM(bottom.shape, jnp.float32),
            pltpu.VMEM(left.shape, jnp.float32),
            pltpu.VMEM(right.shape, jnp.float32),
            pltpu.VMEM((wide_rows * wide_cols, LANES), jnp.bfloat16),
        ],
        compiler_params=pltpu.CompilerParams(vmem_limit_bytes=24 * 1024 * 1024),
        cost_estimate=pl.CostEstimate(flops=10_000_000, bytes_accessed=6_000_000, transcendentals=1000),
        name="halo_norm",
    )(xq, mark, top, bottom, left, right)

    groups = channels // GROUP
    own_lines = own.astype(jnp.float32)
    spare = -own.shape[0] % 8
    own_lines = jnp.concatenate([own_lines, jnp.zeros((spare, channels), jnp.float32)], axis=0)
    place = lax.axis_index("row").astype(jnp.int32).reshape(1)
    shards = len(offsets)
    out, renewed = pl.pallas_call(
        functools.partial(block_kernel, offsets),
        out_shape=(
            jax.ShapeDtypeStruct(grid_elements.shape, jnp.bfloat16),
            jax.ShapeDtypeStruct(own_lines.shape, jnp.float32),
        ),
        in_specs=[pl.BlockSpec(memory_space=pltpu.SMEM)] + [vmem] * 3 + [anywhere] * (3 + 2 * shards),
        out_specs=(anywhere, vmem),
        scratch_shapes=[
            pltpu.VMEM(grid_elements.shape, jnp.bfloat16),
            pltpu.VMEM(xq.shape, jnp.bfloat16),
            pltpu.VMEM(xkv.shape, jnp.bfloat16),
            pltpu.VMEM((cols // (2 * TILE), rows, 2 * TILE, channels), jnp.bfloat16),
            pltpu.VMEM((3 * channels, channels), jnp.bfloat16),
            pltpu.VMEM((channels, channels), jnp.bfloat16),
            pltpu.VMEM((groups, rows * cols, GROUP), jnp.bfloat16),
            pltpu.VMEM((2 * groups, wide_rows * wide_cols, GROUP), jnp.bfloat16),
            pltpu.VMEM((rows * cols, channels), jnp.bfloat16),
            pltpu.VMEM((own.shape[0] * groups, GROUP, GROUP), jnp.bfloat16),
            pltpu.VMEM((own_lines.shape[0], channels), jnp.float32),
            pltpu.SemaphoreType.DMA((2 * shards + 3,)),
            pltpu.SemaphoreType.DMA((cols // (2 * TILE),)),
        ],
        compiler_params=pltpu.CompilerParams(vmem_limit_bytes=VMEM_BYTES),
        cost_estimate=pl.CostEstimate(flops=10_000_000_000, bytes_accessed=12_000_000, transcendentals=4_000_000),
        name="block",
    )(place, hide, own_lines, carriers, grid_elements, xq, xkv, *triples, *finals)
    summary_result = renewed[: own.shape[0]].astype(jnp.bfloat16).reshape(summary_vectors.shape)
    return (out, summary_result)


def solution(mesh):
    placed = (
        P(("img", "row"), "col", None),
        P(("img", "row"), "col", None),
        P(None, "row"),
        P(None, "row"),
        P(("img", "row"), "col"),
    )
    return jax.shard_map(
        local,
        mesh=mesh,
        in_specs=placed,
        out_specs=(P(("img", "row"), "col", None), P(("img", "row"), "col", None)),
        check_vma=False,
    )
```

```python
import functools

import jax
import jax.numpy as jnp
from jax import lax
from jax.experimental import pallas as pl
from jax.experimental.pallas import tpu as pltpu
from jax.sharding import PartitionSpec as P

HEAD_DIM = 64
PATCH_SIDE = 16
RADIUS = 4
TILE = 2 * RADIUS
LANES = 128
GROUP = 256
INVALID = 100.0
HIDDEN = -1e30
VMEM_BYTES = 40 * 1024 * 1024


def nt(a, b):
    return lax.dot_general(a, b, (((1,), (1,)), ((), ())), preferred_element_type=jnp.float32)


def nn(a, b):
    return lax.dot_general(a, b, (((1,), (0,)), ((), ())), preferred_element_type=jnp.float32)


def layer_normalise(lines):
    center = lines - jnp.mean(lines, axis=-1, keepdims=True)
    spread = jnp.mean(center * center, axis=-1, keepdims=True)
    return center * lax.rsqrt(spread + 1e-05)


def shifted(block, axis, step):
    count = lax.axis_size(axis)
    return lax.ppermute(block, axis, [(i, i + step) for i in range(count) if 0 <= i + step < count])


def swapped(block, axis, bit):
    count = lax.axis_size(axis)
    return lax.ppermute(block, axis, [(i, i ^ bit) for i in range(count)])


def after(block, *others):
    return lax.optimization_barrier((block, *others))[0]


def bits_of(count):
    bits, bit = [], count // 2
    while bit:
        bits.append(bit)
        bit //= 2
    return bits


def marked_lanes(lines, hidden):
    first = jnp.where(hidden, INVALID, lines[:, :, :LANES])
    return jnp.concatenate([first, lines[:, :, LANES:]], axis=2).astype(jnp.bfloat16)


def edge_kernel(flags_ref, x_ref, mark_ref, last_ref, first_ref, spread):
    rows, cols = flags_ref.shape
    row_at = lax.broadcasted_iota(jnp.int32, (cols, cols), 0)
    diagonal = row_at == lax.broadcasted_iota(jnp.int32, (cols, cols), 1)
    for r in range(rows):
        hidden = jnp.where(flags_ref[r : r + 1, :] > 0, 0.0, INVALID)
        spread[r * cols : (r + 1) * cols, :] = jnp.where(diagonal, hidden, 0.0).astype(jnp.bfloat16)
    marks = nn(spread[...], jnp.ones((cols, LANES), jnp.bfloat16)).reshape(rows, cols, LANES)
    mark_ref[...] = marks.astype(jnp.bfloat16)
    for ref, at in ((last_ref, slice(rows - RADIUS, rows)), (first_ref, slice(0, RADIUS))):
        ref[...] = marked_lanes(x_ref[at].astype(jnp.float32), marks[at] > INVALID / 2)


def strip_kernel(x_ref, mark_ref, top_ref, bottom_ref, last_ref, first_ref):
    rows, cols, channels = x_ref.shape
    middle = rows // 2
    low = lax.broadcasted_iota(jnp.int32, (1, TILE, 1), 1) < RADIUS
    for ref, columns, last in ((last_ref, slice(cols - TILE, cols), True), (first_ref, slice(0, TILE), False)):
        for lane in range(0, channels, LANES):
            lanes = slice(lane, lane + LANES)

            def own(part):
                lines = x_ref[part, columns, lanes].astype(jnp.float32)
                if lane == 0:
                    lines = jnp.where(mark_ref[part, columns, :].astype(jnp.float32) > INVALID / 2, INVALID, lines)
                return lines

            upper = jnp.concatenate([top_ref[:, columns, lanes].astype(jnp.float32), own(slice(0, middle))], axis=0)
            lower = jnp.concatenate([own(slice(middle, rows)), bottom_ref[:, columns, lanes].astype(jnp.float32)], axis=0)
            if last:
                upper = jnp.roll(upper, RADIUS, axis=1)
            else:
                lower = jnp.roll(lower, RADIUS, axis=1)
            ref[:, :, lanes] = jnp.where(low, upper, lower).astype(jnp.bfloat16)


def own_kernel(x_ref, xq_ref):
    rows, cols, _ = x_ref.shape
    step = 4

    def own(i, _):
        at = pl.multiple_of(i * step, step)
        y = layer_normalise(x_ref[pl.ds(at, step)].astype(jnp.float32))
        for c in range(cols // TILE):
            piece = y[:, c * TILE : (c + 1) * TILE, :].reshape(step * TILE, -1)
            to = pl.multiple_of(c * rows * TILE + at * TILE, step * TILE)
            xq_ref[pl.ds(to, step * TILE), :] = piece.astype(jnp.bfloat16)
        return 0

    lax.fori_loop(0, rows // step, own, 0)


def halo_kernel(border_ref, xq_ref, mark_ref, top_ref, bottom_ref, left_ref, right_ref, xkv_ref, hide_ref, top_s, bottom_s, left_s, right_s, flag_s):
    rows, cols, _ = mark_ref.shape
    wide_rows, wide_cols = rows + 2 * RADIUS, cols + 2 * RADIUS
    half = wide_rows // 2
    step = 2
    for ref, out, size in ((top_ref, top_s, 2), (bottom_ref, bottom_s, 2), (left_ref, left_s, 5), (right_ref, right_s, 5)):
        for i in range(0, ref.shape[0], size):
            out[i : i + size] = layer_normalise(ref[i : i + size].astype(jnp.float32))

    def lines_of(ref):
        return ref.astype(jnp.float32)

    def merge(at, blocks, left, right, to_ref):
        low = lax.broadcasted_iota(jnp.int32, (1, TILE, 1), 1) < RADIUS
        before = left
        for c in range(len(blocks) + 1):
            after = jnp.roll(blocks[c], RADIUS, axis=1) if c < len(blocks) else right
            to = c * wide_rows * TILE + at * TILE
            to = pl.multiple_of(to, step * TILE) if not isinstance(to, int) else to
            lines = jnp.where(low, before, after).reshape(step * TILE, -1)
            to_ref[pl.ds(to, step * TILE), :] = lines.astype(jnp.bfloat16)
            before = after

    def sides(at, upper, left_ref, right_ref, lanes):
        if upper:
            at = at - half
            left, right = jnp.roll(lines_of(left_ref[pl.ds(at, step), :, lanes]), RADIUS, axis=1), lines_of(
                right_ref[pl.ds(at, step), :, lanes]
            )
        else:
            left, right = lines_of(left_ref[pl.ds(at, step), :, lanes]), jnp.roll(
                lines_of(right_ref[pl.ds(at, step), :, lanes]), RADIUS, axis=1
            )
        return left, right

    every, few = slice(None), slice(0, LANES)

    def hide_if(border, lines):
        return jnp.where(border_ref[border] > 0, INVALID, lines)

    def mark_sides(at, upper):
        left, right = sides(at, upper, left_ref, right_ref, few)
        return hide_if(2, left), hide_if(3, right)

    def band(at, ref, ref_s, first, upper):
        cut = [slice(c * TILE, (c + 1) * TILE) for c in range(cols // TILE)]
        merge(at, [ref_s[first : first + step, k, :] for k in cut], *sides(at, upper, left_s, right_s, every), xkv_ref)
        marks = hide_if(int(upper), ref[first : first + step, :, :LANES].astype(jnp.float32))
        beside = [hide_if(int(upper), side) for side in mark_sides(at, upper)]
        merge(at, [marks[:, k, :] for k in cut], *beside, flag_s)

    for i in range(0, RADIUS, step):
        band(i, top_ref, top_s, i, False)
        band(RADIUS + rows + i, bottom_ref, bottom_s, i, True)

    def middle(i, upper):
        at = pl.multiple_of(i * step, step)
        own = at - RADIUS
        blocks = []
        for c in range(cols // TILE):
            first = pl.multiple_of(c * rows * TILE + own * TILE, step * TILE)
            blocks.append(xq_ref[pl.ds(first, step * TILE), :].astype(jnp.float32).reshape(step, TILE, -1))
        merge(at, blocks, *sides(at, upper, left_s, right_s, every), xkv_ref)
        marks = mark_ref[pl.ds(own, step)].astype(jnp.float32)
        marks = [marks[:, c * TILE : (c + 1) * TILE, :] for c in range(cols // TILE)]
        merge(at, marks, *mark_sides(at, upper), flag_s)
        return 0

    lax.fori_loop(RADIUS // step, half // step, lambda i, _: middle(i, False), 0)
    lax.fori_loop(half // step, (RADIUS + rows) // step, lambda i, _: middle(i, True), 0)

    first_lane = (lax.broadcasted_iota(jnp.int32, (8, LANES), 1) == 0).astype(jnp.bfloat16)
    spans = []
    for c in range(wide_cols // TILE):
        lines = flag_s[c * wide_rows * TILE : (c + 1) * wide_rows * TILE, :]
        spans.append(jnp.where(nt(first_lane, lines) > INVALID / 2, HIDDEN, 0.0))
    tall = rows // TILE
    for c in range(cols // TILE):
        for r in range(tall):
            at = slice(r * TILE * TILE, r * TILE * TILE + 2 * TILE * TILE)
            hide_ref[c * tall + r] = jnp.concatenate([spans[c][:, at], spans[c + 1][:, at]], axis=1)


def block_kernel(offsets, carrier_parts, place_ref, hide_ref, x_hbm, xq_hbm, xkv_hbm, *refs):
    shards = len(offsets)
    parts, refs = refs[:carrier_parts], refs[carrier_parts:]
    triples, finals = refs[:shards], refs[shards : 2 * shards]
    out_hbm, summary_ref, x_ref, xq_ref, xkv_ref, out_ref, wt, wo, q_s, kv_s, mix_s, kce, vc_s, sems, out_sems = refs[2 * shards :]
    rows, cols, channels = x_ref.shape
    groups = channels // GROUP
    heads = channels // HEAD_DIM
    heads_in = GROUP // HEAD_DIM
    wide_rows = rows + 2 * RADIUS
    factor = HEAD_DIM ** (-0.5)
    carriers_here = parts[0].shape[0]
    me = place_ref[0]
    triple_rows, final_rows = wt.shape[0] // shards, wo.shape[0] // shards

    def coming(source, target, number):
        copy = pltpu.make_async_copy(source, target, sems.at[number])
        copy.start()
        return copy

    wt_copies, wo_copies = [], []
    for j, off in enumerate(offsets):
        to = pl.multiple_of((me ^ off) * triple_rows, 16)
        wt_copies.append(coming(triples[j], wt.at[pl.ds(to, triple_rows), :], j))
    xq_copy = coming(xq_hbm, xq_ref, 2 * shards)
    xkv_copy = coming(xkv_hbm, xkv_ref, 2 * shards + 1)
    for j, off in enumerate(offsets):
        to = pl.multiple_of((me ^ off) * final_rows, 16)
        wo_copies.append(coming(finals[j], wo.at[pl.ds(to, final_rows), :], shards + j))
    x_copy = coming(x_hbm, x_ref, 2 * shards + 2)

    q_rows, kv_rows = xq_ref.shape[0], xkv_ref.shape[0]
    q_chunk, kv_chunk = q_rows // 4, kv_rows // 5

    def project_q(n, _):
        w = wt[pl.ds(pl.multiple_of(n * GROUP, GROUP), GROUP), :]
        for m in range(0, q_rows, q_chunk):
            q_s[n, m : m + q_chunk, :] = (nt(xq_ref[m : m + q_chunk, :], w) * factor).astype(jnp.bfloat16)
        return 0

    def project_kv(n, _):
        w = wt[pl.ds(pl.multiple_of(channels + n * GROUP, GROUP), GROUP), :]
        for m in range(0, kv_rows, kv_chunk):
            kv_s[n, m : m + kv_chunk, :] = nt(xkv_ref[m : m + kv_chunk, :], w).astype(jnp.bfloat16)
        return 0

    for copy in wt_copies:
        copy.wait()
    xq_copy.wait()
    lax.fori_loop(0, groups, project_q, 0)
    xkv_copy.wait()
    lax.fori_loop(0, 2 * groups, project_kv, 0)

    for copy in wo_copies:
        copy.wait()
    carriers = jnp.concatenate([part[...].astype(jnp.float32) for part in parts], axis=0)
    own = carriers[:carriers_here]
    carriers = layer_normalise(carriers).astype(jnp.bfloat16)
    own_norm = layer_normalise(own).astype(jnp.bfloat16)
    qc = (nt(own_norm, wt[:channels, :]) * factor).astype(jnp.bfloat16).astype(jnp.float32)
    kc = nt(carriers, wt[channels : 2 * channels, :]).astype(jnp.bfloat16)
    vc = nt(carriers, wt[2 * channels :, :]).astype(jnp.bfloat16)
    head_of = lax.broadcasted_iota(jnp.int32, (1, channels), 1) // HEAD_DIM
    stacked = jnp.concatenate([jnp.where(head_of == h, qc, 0.0) for h in range(heads)], axis=0)
    e = jnp.exp(nt(stacked.astype(jnp.bfloat16), kc))
    weights = (e / jnp.sum(e, axis=-1, keepdims=True)).astype(jnp.bfloat16)
    o = nn(weights, vc)
    mix = jnp.zeros((carriers_here, channels), jnp.float32)
    for h in range(heads):
        mix = jnp.where(head_of == h, o[h * carriers_here : (h + 1) * carriers_here, :], mix)
    renewed = own + nt(mix.astype(jnp.bfloat16), wo[...])
    per_row = summary_ref.shape[1]
    for i in range(summary_ref.shape[0]):
        summary_ref[i] = renewed[i * per_row : (i + 1) * per_row, :].astype(jnp.bfloat16)
    fresh = nt(layer_normalise(renewed).astype(jnp.bfloat16), wt[channels:, :]).astype(jnp.bfloat16).astype(jnp.float32)
    vc_s[...] = fresh[:, channels:]
    same = (
        lax.broadcasted_iota(jnp.int32, (GROUP, GROUP), 0) // HEAD_DIM
        == lax.broadcasted_iota(jnp.int32, (GROUP, GROUP), 1) // HEAD_DIM
    )
    windows = kce.shape[0] // groups
    for w in range(windows):
        for g in range(groups):
            kce[w * groups + g] = jnp.where(same, fresh[w : w + 1, g * GROUP : (g + 1) * GROUP], 0.0).astype(jnp.bfloat16)

    queries, span = TILE * TILE, 2 * TILE * TILE
    qi = lax.broadcasted_iota(jnp.int32, (queries, 2 * span), 0)
    ki = lax.broadcasted_iota(jnp.int32, (queries, 2 * span), 1)
    row_step = (ki % span) // TILE - qi // TILE
    col_step = (ki // span) * TILE + ki % TILE - qi % TILE
    seen = (row_step >= 0) & (row_step <= 2 * RADIUS) & (col_step >= 0) & (col_step <= 2 * RADIUS)
    band = jnp.where(seen, 0.0, HIDDEN)
    group_head = lax.broadcasted_iota(jnp.int32, (1, GROUP), 1) // HEAD_DIM
    tall, broad = rows // TILE, cols // TILE
    per_side = PATCH_SIDE // TILE

    def tile(t, _):
        c, r = t // tall, t % tall
        q_at = pl.multiple_of(c * (rows * TILE) + r * queries, queries)
        k0 = pl.multiple_of(c * (wide_rows * TILE) + r * queries, queries)
        k1 = pl.multiple_of(k0 + wide_rows * TILE, queries)
        window = (r // per_side) * (broad // per_side) + c // per_side
        bias = band + hide_ref[t][0:1, :]
        for g in range(groups):
            q = q_s[g, pl.ds(q_at, queries), :]
            q32 = q.astype(jnp.float32)
            qq = jnp.concatenate(
                [jnp.where(group_head == h, q32, 0.0).astype(jnp.bfloat16) for h in range(heads_in)], axis=0
            )
            k = jnp.concatenate([kv_s[g, pl.ds(k0, span), :], kv_s[g, pl.ds(k1, span), :]], axis=0)
            v = jnp.concatenate(
                [kv_s[groups + g, pl.ds(k0, span), :], kv_s[groups + g, pl.ds(k1, span), :]], axis=0
            )
            p = jnp.exp(nt(qq, k).reshape(heads_in, queries, 2 * span) + bias[None])
            total = jnp.sum(p, axis=-1, keepdims=True)
            o = nn(p.reshape(heads_in * queries, 2 * span).astype(jnp.bfloat16), v)
            o = o.reshape(heads_in, queries, GROUP)
            kept, kept_total = o[0], total[0]
            for h in range(1, heads_in):
                kept = jnp.where(group_head == h, o[h], kept)
                kept_total = jnp.where(group_head == h, total[h], kept_total)
            pc = jnp.exp(nt(q, kce[window * groups + g]))
            v_new = vc_s[pl.ds(window, 1), g * GROUP : (g + 1) * GROUP]
            mixed = (kept + pc * v_new) / (kept_total + pc)
            mix_s[pl.ds(q_at, queries), g * GROUP : (g + 1) * GROUP] = mixed.astype(jnp.bfloat16)
        return 0

    lax.fori_loop(0, tall * broad, tile, 0)

    x_copy.wait()
    going = []
    for pair in range(broad // 2):
        both = slice(2 * pair * TILE, 2 * (pair + 1) * TILE)
        for g in range(groups):
            at = slice(g * GROUP, (g + 1) * GROUP)
            w = wo[at, :]
            parts = [
                nt(mix_s[b * rows * TILE : (b + 1) * rows * TILE, :], w).reshape(rows, TILE, GROUP)
                for b in (2 * pair, 2 * pair + 1)
            ]
            y = jnp.concatenate(parts, axis=1) + x_ref[:, both, at].astype(jnp.float32)
            out_ref[pair, :, :, at] = y.astype(jnp.bfloat16)
        copy = pltpu.make_async_copy(out_ref.at[pair], out_hbm.at[:, both, :], out_sems.at[pair])
        copy.start()
        going.append(copy)
    for copy in going:
        copy.wait()


def local(grid_elements, summary_vectors, triple_projection, final_projection, genuine_flags):
    rows, cols, channels = grid_elements.shape
    wide_rows, wide_cols = rows + 2 * RADIUS, cols + 2 * RADIUS
    own = summary_vectors.reshape(-1, channels)

    triple_t, final_t = triple_projection.T, final_projection.T
    vmem = pl.BlockSpec(memory_space=pltpu.VMEM)
    anywhere = pl.BlockSpec(memory_space=pl.ANY)
    scalars = pl.BlockSpec(memory_space=pltpu.SMEM)
    small = pltpu.CompilerParams(vmem_limit_bytes=16 * 1024 * 1024)
    row_strip = jax.ShapeDtypeStruct((RADIUS, cols, channels), jnp.bfloat16)
    col_strip = jax.ShapeDtypeStruct((wide_rows // 2, 2 * RADIUS, channels), jnp.bfloat16)

    mark, last_rows, first_rows = pl.pallas_call(
        edge_kernel,
        out_shape=(jax.ShapeDtypeStruct((rows, cols, LANES), jnp.bfloat16), row_strip, row_strip),
        in_specs=[vmem] * 2,
        out_specs=(vmem,) * 3,
        scratch_shapes=[pltpu.VMEM((rows * cols, cols), jnp.bfloat16)],
        compiler_params=small,
        cost_estimate=pl.CostEstimate(flops=1_000_000, bytes_accessed=2_000_000, transcendentals=0),
        name="edge_rows",
    )(genuine_flags, grid_elements)
    top = shifted(last_rows, "row", 1)
    bottom = shifted(first_rows, "row", -1)

    row_bits = bits_of(lax.axis_size("row"))
    far, rest = row_bits[0], row_bits[1:]
    far_final = swapped(final_t, "row", far)
    far_triple = swapped(after(triple_t, top, bottom, far_final), "row", far)
    finals, triples, offsets = [final_t], [triple_t], [0]
    for bit in rest:
        finals = finals + [swapped(p, "row", bit) for p in finals]
        triples = triples + [swapped(p, "row", bit) for p in triples]
        offsets = offsets + [o ^ bit for o in offsets]
    parts, carriers = [], own
    for bit in bits_of(lax.axis_size("col")):
        got = swapped(carriers, "col", bit)
        carriers = jnp.concatenate([carriers, got], axis=0)
        parts = parts + [got] if parts else [carriers]

    last_cols, first_cols = pl.pallas_call(
        strip_kernel,
        out_shape=(col_strip, col_strip),
        in_specs=[vmem] * 4,
        out_specs=(vmem,) * 2,
        compiler_params=small,
        cost_estimate=pl.CostEstimate(flops=1_000_000, bytes_accessed=2_000_000, transcendentals=0),
        name="edge_columns",
    )(grid_elements, mark, top, bottom)
    left = shifted(last_cols, "col", 1)
    right = shifted(first_cols, "col", -1)

    tiles = (rows // TILE) * (cols // TILE)
    keys = 4 * TILE * TILE
    xq = pl.pallas_call(
        own_kernel,
        out_shape=jax.ShapeDtypeStruct((rows * cols, channels), jnp.bfloat16),
        in_specs=[vmem],
        out_specs=vmem,
        compiler_params=small,
        cost_estimate=pl.CostEstimate(flops=10_000_000, bytes_accessed=3_000_000, transcendentals=1000),
        name="own_norm",
    )(grid_elements)
    row_at, col_at = lax.axis_index("row"), lax.axis_index("col")
    borders = (row_at == 0, row_at == lax.axis_size("row") - 1, col_at == 0, col_at == lax.axis_size("col") - 1)
    borders = jnp.stack([border.astype(jnp.int32) for border in borders])
    xkv, hide = pl.pallas_call(
        halo_kernel,
        out_shape=(
            jax.ShapeDtypeStruct((wide_rows * wide_cols, channels), jnp.bfloat16),
            jax.ShapeDtypeStruct((tiles, 8, keys), jnp.float32),
        ),
        in_specs=[scalars] + [vmem] * 6,
        out_specs=(vmem,) * 2,
        scratch_shapes=[
            pltpu.VMEM(top.shape, jnp.float32),
            pltpu.VMEM(bottom.shape, jnp.float32),
            pltpu.VMEM(left.shape, jnp.float32),
            pltpu.VMEM(right.shape, jnp.float32),
            pltpu.VMEM((wide_rows * wide_cols, LANES), jnp.bfloat16),
        ],
        compiler_params=pltpu.CompilerParams(vmem_limit_bytes=24 * 1024 * 1024),
        cost_estimate=pl.CostEstimate(flops=10_000_000, bytes_accessed=6_000_000, transcendentals=1000),
        name="halo_norm",
    )(borders, xq, mark, top, bottom, left, right)

    far_finals = [far_final]
    for bit in rest:
        far_finals = far_finals + [swapped(p, "row", bit) for p in far_finals]
    far_triples = [after(far_triple, xkv, carriers, *far_finals)]
    for bit in rest:
        far_triples = far_triples + [swapped(p, "row", bit) for p in far_triples]
    carriers = after(carriers, far_triple)
    for bit in row_bits:
        got = swapped(carriers, "row", bit)
        carriers = jnp.concatenate([carriers, got], axis=0)
        parts = parts + [got]
    finals, triples = finals + far_finals, triples + far_triples
    offsets = offsets + [o ^ far for o in offsets]

    groups = channels // GROUP
    place = lax.axis_index("row").astype(jnp.int32).reshape(1)
    shards = len(offsets)
    out, summary_result = pl.pallas_call(
        functools.partial(block_kernel, offsets, len(parts)),
        out_shape=(
            jax.ShapeDtypeStruct(grid_elements.shape, jnp.bfloat16),
            jax.ShapeDtypeStruct(summary_vectors.shape, jnp.bfloat16),
        ),
        in_specs=[scalars, vmem] + [anywhere] * 3 + [vmem] * len(parts) + [anywhere] * (2 * shards),
        out_specs=(anywhere, vmem),
        scratch_shapes=[
            pltpu.VMEM(grid_elements.shape, jnp.bfloat16),
            pltpu.VMEM(xq.shape, jnp.bfloat16),
            pltpu.VMEM(xkv.shape, jnp.bfloat16),
            pltpu.VMEM((cols // (2 * TILE), rows, 2 * TILE, channels), jnp.bfloat16),
            pltpu.VMEM((3 * channels, channels), jnp.bfloat16),
            pltpu.VMEM((channels, channels), jnp.bfloat16),
            pltpu.VMEM((groups, rows * cols, GROUP), jnp.bfloat16),
            pltpu.VMEM((2 * groups, wide_rows * wide_cols, GROUP), jnp.bfloat16),
            pltpu.VMEM((rows * cols, channels), jnp.bfloat16),
            pltpu.VMEM((own.shape[0] * groups, GROUP, GROUP), jnp.bfloat16),
            pltpu.VMEM((parts[0].shape[0], channels), jnp.float32),
            pltpu.SemaphoreType.DMA((2 * shards + 3,)),
            pltpu.SemaphoreType.DMA((cols // (2 * TILE),)),
        ],
        compiler_params=pltpu.CompilerParams(vmem_limit_bytes=VMEM_BYTES),
        cost_estimate=pl.CostEstimate(flops=10_000_000_000, bytes_accessed=12_000_000, transcendentals=4_000_000),
        name="block",
    )(place, hide, grid_elements, xq, xkv, *parts, *triples, *finals)
    return (out, summary_result)


def solution(mesh):
    placed = (
        P(("img", "row"), "col", None),
        P(("img", "row"), "col", None),
        P(None, "row"),
        P(None, "row"),
        P(("img", "row"), "col"),
    )
    return jax.shard_map(
        local,
        mesh=mesh,
        in_specs=placed,
        out_specs=(P(("img", "row"), "col", None), P(("img", "row"), "col", None)),
        check_vma=False,
    )
```

```python
import functools

import jax
import jax.numpy as jnp
from jax import lax
from jax.experimental import pallas as pl
from jax.experimental.pallas import tpu as pltpu
from jax.sharding import PartitionSpec as P

HEAD_DIM = 64
PATCH_SIDE = 16
RADIUS = 4
TILE = 2 * RADIUS
LANES = 128
GROUP = 256
INVALID = 100.0
HIDDEN = -1e30
EVEN_ROW, EVEN_COL, ROW, STARTS = 4, 5, 6, 7
VMEM_BYTES = 24 * 1024 * 1024


def nt(a, b):
    return lax.dot_general(a, b, (((1,), (1,)), ((), ())), preferred_element_type=jnp.float32)


def nn(a, b):
    return lax.dot_general(a, b, (((1,), (0,)), ((), ())), preferred_element_type=jnp.float32)


def layer_normalise(lines):
    center = lines - jnp.mean(lines, axis=-1, keepdims=True)
    spread = jnp.mean(center * center, axis=-1, keepdims=True)
    return center * lax.rsqrt(spread + 1e-05)


def pair_swapped(even_block, odd_block, axis):
    count = lax.axis_size(axis)
    got = []
    for first, block in ((0, even_block), (1, odd_block)):
        pairs = [(i, i + 1) for i in range(first, count - 1, 2)]
        got.append(lax.ppermute(block, axis, pairs + [(b, a) for a, b in pairs]))
    return got


def swapped(block, axis, bit):
    count = lax.axis_size(axis)
    return lax.ppermute(block, axis, [(i, i ^ bit) for i in range(count)])


def after(block, *others):
    return lax.optimization_barrier((block, *others))[0]


def bits_of(count):
    bits, bit = [], count // 2
    while bit:
        bits.append(bit)
        bit //= 2
    return bits


def marked_lanes(lines, hidden):
    first = jnp.where(hidden, INVALID, lines[:, :, :LANES])
    return jnp.concatenate([first, lines[:, :, LANES:]], axis=2)


def edge_kernel(place_ref, flags_ref, x_ref, mark_ref, even_ref, odd_ref, spread):
    rows, cols = flags_ref.shape
    row_at = lax.broadcasted_iota(jnp.int32, (cols, cols), 0)
    diagonal = row_at == lax.broadcasted_iota(jnp.int32, (cols, cols), 1)
    for r in range(rows):
        hidden = jnp.where(flags_ref[r : r + 1, :] > 0, 0.0, INVALID)
        spread[r * cols : (r + 1) * cols, :] = jnp.where(diagonal, hidden, 0.0).astype(jnp.bfloat16)
    marks = nn(spread[...], jnp.ones((cols, LANES), jnp.bfloat16)).reshape(rows, cols, LANES)
    mark_ref[...] = marks.astype(jnp.bfloat16)
    first, last = [
        marked_lanes(x_ref[at].astype(jnp.float32), marks[at] > INVALID / 2)
        for at in (slice(0, RADIUS), slice(rows - RADIUS, rows))
    ]
    even = place_ref[EVEN_ROW] > 0
    even_ref[...] = jnp.where(even, last, first).astype(jnp.bfloat16)
    odd_ref[...] = jnp.where(even, first, last).astype(jnp.bfloat16)


def strip_kernel(place_ref, x_ref, mark_ref, even_rows_ref, odd_rows_ref, even_ref, odd_ref):
    rows, cols, channels = x_ref.shape
    middle = rows // 2
    low = lax.broadcasted_iota(jnp.int32, (1, TILE, 1), 1) < RADIUS
    even_row, even_col = place_ref[EVEN_ROW] > 0, place_ref[EVEN_COL] > 0
    for lane in range(0, channels, LANES):
        lanes = slice(lane, lane + LANES)
        strips = []
        for columns, last in ((slice(0, TILE), False), (slice(cols - TILE, cols), True)):

            def own(part):
                lines = x_ref[part, columns, lanes].astype(jnp.float32)
                if lane == 0:
                    lines = jnp.where(mark_ref[part, columns, :].astype(jnp.float32) > INVALID / 2, INVALID, lines)
                return lines

            even_rows = even_rows_ref[:, columns, lanes].astype(jnp.float32)
            odd_rows = odd_rows_ref[:, columns, lanes].astype(jnp.float32)
            top, bottom = jnp.where(even_row, odd_rows, even_rows), jnp.where(even_row, even_rows, odd_rows)
            upper = jnp.concatenate([top, own(slice(0, middle))], axis=0)
            lower = jnp.concatenate([own(slice(middle, rows)), bottom], axis=0)
            if last:
                upper = jnp.roll(upper, RADIUS, axis=1)
            else:
                lower = jnp.roll(lower, RADIUS, axis=1)
            strips.append(jnp.where(low, upper, lower))
        first, last = strips
        even_ref[:, :, lanes] = jnp.where(even_col, last, first).astype(jnp.bfloat16)
        odd_ref[:, :, lanes] = jnp.where(even_col, first, last).astype(jnp.bfloat16)


def own_kernel(x_ref, xq_ref):
    rows, cols, _ = x_ref.shape
    step = 4

    def own(i, _):
        at = pl.multiple_of(i * step, step)
        y = layer_normalise(x_ref[pl.ds(at, step)].astype(jnp.float32))
        for c in range(cols // TILE):
            piece = y[:, c * TILE : (c + 1) * TILE, :].reshape(step * TILE, -1)
            to = pl.multiple_of(c * rows * TILE + at * TILE, step * TILE)
            xq_ref[pl.ds(to, step * TILE), :] = piece.astype(jnp.bfloat16)
        return 0

    lax.fori_loop(0, rows // step, own, 0)


def halo_kernel(place_ref, xq_ref, mark_ref, even_rows_ref, odd_rows_ref, even_cols_ref, odd_cols_ref, xkv_ref, hide_ref, *scratch):
    rows, cols, _ = mark_ref.shape
    wide_rows, wide_cols = rows + 2 * RADIUS, cols + 2 * RADIUS
    half = wide_rows // 2
    step = 2
    top_s, bottom_s, left_s, right_s, top_ref, bottom_ref, left_ref, right_ref, flag_s = scratch
    for even, odd, low, high, low_flags, high_flags, parity, size in (
        (even_rows_ref, odd_rows_ref, top_s, bottom_s, top_ref, bottom_ref, EVEN_ROW, 2),
        (even_cols_ref, odd_cols_ref, left_s, right_s, left_ref, right_ref, EVEN_COL, 5),
    ):
        flip = place_ref[parity] > 0
        for i in range(0, even.shape[0], size):
            a, b = even[i : i + size].astype(jnp.float32), odd[i : i + size].astype(jnp.float32)
            for lines, out, flags in ((jnp.where(flip, b, a), low, low_flags), (jnp.where(flip, a, b), high, high_flags)):
                out[i : i + size] = layer_normalise(lines)
                flags[i : i + size] = lines[:, :, :LANES]

    def lines_of(ref):
        return ref.astype(jnp.float32)

    def merge(at, blocks, left, right, to_ref):
        low = lax.broadcasted_iota(jnp.int32, (1, TILE, 1), 1) < RADIUS
        before = left
        for c in range(len(blocks) + 1):
            after = jnp.roll(blocks[c], RADIUS, axis=1) if c < len(blocks) else right
            to = c * wide_rows * TILE + at * TILE
            to = pl.multiple_of(to, step * TILE) if not isinstance(to, int) else to
            lines = jnp.where(low, before, after).reshape(step * TILE, -1)
            to_ref[pl.ds(to, step * TILE), :] = lines.astype(jnp.bfloat16)
            before = after

    def sides(at, upper, left_ref, right_ref, lanes):
        if upper:
            at = at - half
            left, right = jnp.roll(lines_of(left_ref[pl.ds(at, step), :, lanes]), RADIUS, axis=1), lines_of(
                right_ref[pl.ds(at, step), :, lanes]
            )
        else:
            left, right = lines_of(left_ref[pl.ds(at, step), :, lanes]), jnp.roll(
                lines_of(right_ref[pl.ds(at, step), :, lanes]), RADIUS, axis=1
            )
        return left, right

    every, few = slice(None), slice(0, LANES)

    def hide_if(border, lines):
        return jnp.where(place_ref[border] > 0, INVALID, lines)

    def mark_sides(at, upper):
        left, right = sides(at, upper, left_ref, right_ref, few)
        return hide_if(2, left), hide_if(3, right)

    def band(at, ref, ref_s, first, upper):
        cut = [slice(c * TILE, (c + 1) * TILE) for c in range(cols // TILE)]
        merge(at, [ref_s[first : first + step, k, :] for k in cut], *sides(at, upper, left_s, right_s, every), xkv_ref)
        marks = hide_if(int(upper), ref[first : first + step])
        beside = [hide_if(int(upper), side) for side in mark_sides(at, upper)]
        merge(at, [marks[:, k, :] for k in cut], *beside, flag_s)

    for i in range(0, RADIUS, step):
        band(i, top_ref, top_s, i, False)
        band(RADIUS + rows + i, bottom_ref, bottom_s, i, True)

    def middle(i, upper):
        at = pl.multiple_of(i * step, step)
        own = at - RADIUS
        blocks = []
        for c in range(cols // TILE):
            first = pl.multiple_of(c * rows * TILE + own * TILE, step * TILE)
            blocks.append(xq_ref[pl.ds(first, step * TILE), :].astype(jnp.float32).reshape(step, TILE, -1))
        merge(at, blocks, *sides(at, upper, left_s, right_s, every), xkv_ref)
        marks = mark_ref[pl.ds(own, step)].astype(jnp.float32)
        marks = [marks[:, c * TILE : (c + 1) * TILE, :] for c in range(cols // TILE)]
        merge(at, marks, *mark_sides(at, upper), flag_s)
        return 0

    lax.fori_loop(RADIUS // step, half // step, lambda i, _: middle(i, False), 0)
    lax.fori_loop(half // step, (RADIUS + rows) // step, lambda i, _: middle(i, True), 0)

    first_lane = (lax.broadcasted_iota(jnp.int32, (8, LANES), 1) == 0).astype(jnp.bfloat16)
    spans = []
    for c in range(wide_cols // TILE):
        lines = flag_s[c * wide_rows * TILE : (c + 1) * wide_rows * TILE, :]
        spans.append(jnp.where(nt(first_lane, lines) > INVALID / 2, HIDDEN, 0.0))
    tall = rows // TILE
    for c in range(cols // TILE):
        for r in range(tall):
            at = slice(r * TILE * TILE, r * TILE * TILE + 2 * TILE * TILE)
            hide_ref[c * tall + r] = jnp.concatenate([spans[c][:, at], spans[c + 1][:, at]], axis=1)


def project_kernel(whole, pieces, triple_rows, place_ref, *refs):
    sources, refs = refs[: len(whole) + len(pieces)], refs[len(whole) + len(pieces) :]
    xq_ref, xkv_ref, q_s, kv_s, wt, sems = refs
    channels = wt.shape[1]
    groups = channels // GROUP
    factor = HEAD_DIM ** (-0.5)
    me = place_ref[ROW]
    copies = []
    for j, source in enumerate(sources):
        if j < len(whole):
            to = (me ^ whole[j]) * triple_rows
        else:
            off, start = pieces[j - len(whole)]
            to = (me ^ off) * triple_rows + place_ref[STARTS + start]
        to = pl.multiple_of(to, 16)
        copy = pltpu.make_async_copy(source, wt.at[pl.ds(to, source.shape[0]), :], sems.at[j])
        copy.start()
        copies.append(copy)
    for copy in copies:
        copy.wait()

    q_rows, kv_rows = xq_ref.shape[0], xkv_ref.shape[0]
    q_chunk, kv_chunk = q_rows // 4, kv_rows // 5

    def project_q(n, _):
        w = wt[pl.ds(pl.multiple_of(n * GROUP, GROUP), GROUP), :]
        for m in range(0, q_rows, q_chunk):
            q_s[n, m : m + q_chunk, :] = (nt(xq_ref[m : m + q_chunk, :], w) * factor).astype(jnp.bfloat16)
        return 0

    def project_kv(n, _):
        w = wt[pl.ds(pl.multiple_of(channels + n * GROUP, GROUP), GROUP), :]
        for m in range(0, kv_rows, kv_chunk):
            kv_s[n, m : m + kv_chunk, :] = nt(xkv_ref[m : m + kv_chunk, :], w).astype(jnp.bfloat16)
        return 0

    lax.fori_loop(0, groups, project_q, 0)
    lax.fori_loop(0, 2 * groups, project_kv, 0)


def carrier_kernel(offsets, carrier_parts, place_ref, wt, *refs):
    shards = len(offsets)
    parts, finals, refs = refs[:carrier_parts], refs[carrier_parts : carrier_parts + shards], refs[carrier_parts + shards :]
    summary_ref, wo, kce, vc_s, sems = refs
    channels = wt.shape[1]
    groups = channels // GROUP
    heads = channels // HEAD_DIM
    factor = HEAD_DIM ** (-0.5)
    carriers_here = parts[0].shape[0]
    final_rows = wo.shape[0] // shards
    copies = []
    for j, off in enumerate(offsets):
        to = pl.multiple_of((place_ref[ROW] ^ off) * final_rows, 16)
        copy = pltpu.make_async_copy(finals[j], wo.at[pl.ds(to, final_rows), :], sems.at[j])
        copy.start()
        copies.append(copy)
    carriers = jnp.concatenate([part[...].astype(jnp.float32) for part in parts], axis=0)
    own = carriers[:carriers_here]
    carriers = layer_normalise(carriers).astype(jnp.bfloat16)
    own_norm = layer_normalise(own).astype(jnp.bfloat16)
    qc = (nt(own_norm, wt[:channels, :]) * factor).astype(jnp.bfloat16).astype(jnp.float32)
    kc = nt(carriers, wt[channels : 2 * channels, :]).astype(jnp.bfloat16)
    vc = nt(carriers, wt[2 * channels :, :]).astype(jnp.bfloat16)
    head_of = lax.broadcasted_iota(jnp.int32, (1, channels), 1) // HEAD_DIM
    stacked = jnp.concatenate([jnp.where(head_of == h, qc, 0.0) for h in range(heads)], axis=0)
    e = jnp.exp(nt(stacked.astype(jnp.bfloat16), kc))
    weights = (e / jnp.sum(e, axis=-1, keepdims=True)).astype(jnp.bfloat16)
    o = nn(weights, vc)
    mix = jnp.zeros((carriers_here, channels), jnp.float32)
    for h in range(heads):
        mix = jnp.where(head_of == h, o[h * carriers_here : (h + 1) * carriers_here, :], mix)
    for copy in copies:
        copy.wait()
    renewed = own + nt(mix.astype(jnp.bfloat16), wo[...])
    per_row = summary_ref.shape[1]
    for i in range(summary_ref.shape[0]):
        summary_ref[i] = renewed[i * per_row : (i + 1) * per_row, :].astype(jnp.bfloat16)
    fresh = nt(layer_normalise(renewed).astype(jnp.bfloat16), wt[channels:, :]).astype(jnp.bfloat16).astype(jnp.float32)
    vc_s[...] = fresh[:, channels:]
    same = (
        lax.broadcasted_iota(jnp.int32, (GROUP, GROUP), 0) // HEAD_DIM
        == lax.broadcasted_iota(jnp.int32, (GROUP, GROUP), 1) // HEAD_DIM
    )
    windows = kce.shape[0] // groups
    for w in range(windows):
        for g in range(groups):
            kce[w * groups + g] = jnp.where(same, fresh[w : w + 1, g * GROUP : (g + 1) * GROUP], 0.0).astype(jnp.bfloat16)


def attend_kernel(x_ref, q_s, kv_s, hide_ref, kce, vc_s, wo, out_hbm, out_ref, mix_s, out_sems):
    rows, cols, channels = x_ref.shape
    groups = channels // GROUP
    heads_in = GROUP // HEAD_DIM
    wide_rows = rows + 2 * RADIUS
    queries, span = TILE * TILE, 2 * TILE * TILE
    qi = lax.broadcasted_iota(jnp.int32, (queries, 2 * span), 0)
    ki = lax.broadcasted_iota(jnp.int32, (queries, 2 * span), 1)
    row_step = (ki % span) // TILE - qi // TILE
    col_step = (ki // span) * TILE + ki % TILE - qi % TILE
    seen = (row_step >= 0) & (row_step <= 2 * RADIUS) & (col_step >= 0) & (col_step <= 2 * RADIUS)
    band = jnp.where(seen, 0.0, HIDDEN)
    group_head = lax.broadcasted_iota(jnp.int32, (1, GROUP), 1) // HEAD_DIM
    tall, broad = rows // TILE, cols // TILE
    per_side = PATCH_SIDE // TILE

    def tile(t, _):
        c, r = t // tall, t % tall
        q_at = pl.multiple_of(c * (rows * TILE) + r * queries, queries)
        k0 = pl.multiple_of(c * (wide_rows * TILE) + r * queries, queries)
        k1 = pl.multiple_of(k0 + wide_rows * TILE, queries)
        window = (r // per_side) * (broad // per_side) + c // per_side
        bias = band + hide_ref[t][0:1, :]
        for g in range(groups):
            q = q_s[g, pl.ds(q_at, queries), :]
            q32 = q.astype(jnp.float32)
            qq = jnp.concatenate(
                [jnp.where(group_head == h, q32, 0.0).astype(jnp.bfloat16) for h in range(heads_in)], axis=0
            )
            k = jnp.concatenate([kv_s[g, pl.ds(k0, span), :], kv_s[g, pl.ds(k1, span), :]], axis=0)
            v = jnp.concatenate(
                [kv_s[groups + g, pl.ds(k0, span), :], kv_s[groups + g, pl.ds(k1, span), :]], axis=0
            )
            p = jnp.exp(nt(qq, k).reshape(heads_in, queries, 2 * span) + bias[None])
            total = jnp.sum(p, axis=-1, keepdims=True)
            o = nn(p.reshape(heads_in * queries, 2 * span).astype(jnp.bfloat16), v)
            o = o.reshape(heads_in, queries, GROUP)
            kept, kept_total = o[0], total[0]
            for h in range(1, heads_in):
                kept = jnp.where(group_head == h, o[h], kept)
                kept_total = jnp.where(group_head == h, total[h], kept_total)
            pc = jnp.exp(nt(q, kce[window * groups + g]))
            v_new = vc_s[pl.ds(window, 1), g * GROUP : (g + 1) * GROUP]
            mixed = (kept + pc * v_new) / (kept_total + pc)
            mix_s[pl.ds(q_at, queries), g * GROUP : (g + 1) * GROUP] = mixed.astype(jnp.bfloat16)
        return 0

    lax.fori_loop(0, tall * broad, tile, 0)

    going = []
    for pair in range(broad // 2):
        both = slice(2 * pair * TILE, 2 * (pair + 1) * TILE)
        for g in range(groups):
            at = slice(g * GROUP, (g + 1) * GROUP)
            w = wo[at, :]
            parts = [
                nt(mix_s[b * rows * TILE : (b + 1) * rows * TILE, :], w).reshape(rows, TILE, GROUP)
                for b in (2 * pair, 2 * pair + 1)
            ]
            y = jnp.concatenate(parts, axis=1) + x_ref[:, both, at].astype(jnp.float32)
            out_ref[pair, :, :, at] = y.astype(jnp.bfloat16)
        copy = pltpu.make_async_copy(out_ref.at[pair], out_hbm.at[:, both, :], out_sems.at[pair])
        copy.start()
        going.append(copy)
    for copy in going:
        copy.wait()


def local(grid_elements, summary_vectors, triple_projection, final_projection, genuine_flags):
    rows, cols, channels = grid_elements.shape
    wide_rows, wide_cols = rows + 2 * RADIUS, cols + 2 * RADIUS
    own = summary_vectors.reshape(-1, channels)

    triple_t, final_t = triple_projection.T, final_projection.T
    vmem = pl.BlockSpec(memory_space=pltpu.VMEM)
    anywhere = pl.BlockSpec(memory_space=pl.ANY)
    scalars = pl.BlockSpec(memory_space=pltpu.SMEM)
    small = pltpu.CompilerParams(vmem_limit_bytes=16 * 1024 * 1024)
    row_strip = jax.ShapeDtypeStruct((RADIUS, cols, channels), jnp.bfloat16)
    col_strip = jax.ShapeDtypeStruct((wide_rows // 2, 2 * RADIUS, channels), jnp.bfloat16)

    row, col, img = lax.axis_size("row"), lax.axis_size("col"), lax.axis_size("img")
    row_at, col_at, img_at = lax.axis_index("row"), lax.axis_index("col"), lax.axis_index("img")
    row_bits = bits_of(row)
    far, rest = row_bits[0], row_bits[1:]
    relays = img if triple_t.shape[0] % (16 * (img + 1)) == 0 else 0
    piece_rows = triple_t.shape[0] // (relays + 1)
    starts = [(img_at - k) % img for k in range(relays)] + [jnp.int32(relays)]
    place = [row_at == 0, row_at == row - 1, col_at == 0, col_at == col - 1, row_at % 2 == 0, col_at % 2 == 0, row_at]
    place = jnp.stack([jnp.asarray(p).astype(jnp.int32) for p in place + [start * piece_rows for start in starts]])

    got = swapped(own, "row", far)
    carriers = jnp.concatenate([own, got], axis=0)
    parts = [carriers]
    far_pieces = []
    if relays:
        mine = lax.dynamic_slice_in_dim(triple_t, img_at * piece_rows, piece_rows)
        far_pieces.append(swapped(mine, "row", far))

    mark, even_rows, odd_rows = pl.pallas_call(
        edge_kernel,
        out_shape=(jax.ShapeDtypeStruct((rows, cols, LANES), jnp.bfloat16), row_strip, row_strip),
        in_specs=[scalars] + [vmem] * 2,
        out_specs=(vmem,) * 3,
        scratch_shapes=[pltpu.VMEM((rows * cols, cols), jnp.bfloat16)],
        compiler_params=small,
        cost_estimate=pl.CostEstimate(flops=1_000_000, bytes_accessed=2_000_000, transcendentals=0),
        name="edge_rows",
    )(place, genuine_flags, grid_elements)
    even_rows, odd_rows = pair_swapped(even_rows, odd_rows, "row")

    far_pieces.append(swapped(after(triple_t[relays * piece_rows :], even_rows, odd_rows), "row", far))
    far_final = swapped(after(final_t, even_rows, odd_rows), "row", far)
    if relays:
        first = after(far_pieces[0], even_rows, odd_rows)
        others = [lax.ppermute(first, "img", [(i, (i + k) % img) for i in range(img)]) for k in range(1, relays)]
        far_pieces = [first] + others + far_pieces[1:]

    even_cols, odd_cols = pl.pallas_call(
        strip_kernel,
        out_shape=(col_strip, col_strip),
        in_specs=[scalars] + [vmem] * 4,
        out_specs=(vmem,) * 2,
        compiler_params=small,
        cost_estimate=pl.CostEstimate(flops=1_000_000, bytes_accessed=2_000_000, transcendentals=0),
        name="edge_columns",
    )(place, grid_elements, mark, even_rows, odd_rows)
    even_cols, odd_cols = pair_swapped(even_cols, odd_cols, "col")

    finals, triples, offsets = [final_t], [triple_t], [0]
    for bit in rest:
        finals = finals + [swapped(p, "row", bit) for p in finals]
        triples = triples + [swapped(p, "row", bit) for p in triples]
        offsets = offsets + [o ^ bit for o in offsets]
    for axis, bits in (("col", bits_of(col)), ("row", rest)):
        for bit in bits:
            got = swapped(carriers, axis, bit)
            carriers = jnp.concatenate([carriers, got], axis=0)
            parts = parts + [got]

    tiles = (rows // TILE) * (cols // TILE)
    keys = 4 * TILE * TILE
    xq = pl.pallas_call(
        own_kernel,
        out_shape=jax.ShapeDtypeStruct((rows * cols, channels), jnp.bfloat16),
        in_specs=[vmem],
        out_specs=vmem,
        compiler_params=small,
        cost_estimate=pl.CostEstimate(flops=10_000_000, bytes_accessed=3_000_000, transcendentals=1000),
        name="own_norm",
    )(grid_elements)
    xkv, hide = pl.pallas_call(
        halo_kernel,
        out_shape=(
            jax.ShapeDtypeStruct((wide_rows * wide_cols, channels), jnp.bfloat16),
            jax.ShapeDtypeStruct((tiles, 8, keys), jnp.float32),
        ),
        in_specs=[scalars] + [vmem] * 6,
        out_specs=(vmem,) * 2,
        scratch_shapes=[
            *[pltpu.VMEM(shape.shape, jnp.float32) for shape in (row_strip, row_strip, col_strip, col_strip)],
            *[pltpu.VMEM((*shape.shape[:2], LANES), jnp.float32) for shape in (row_strip, row_strip, col_strip, col_strip)],
            pltpu.VMEM((wide_rows * wide_cols, LANES), jnp.bfloat16),
        ],
        compiler_params=pltpu.CompilerParams(vmem_limit_bytes=24 * 1024 * 1024),
        cost_estimate=pl.CostEstimate(flops=10_000_000, bytes_accessed=6_000_000, transcendentals=1000),
        name="halo_norm",
    )(place, xq, mark, even_rows, odd_rows, even_cols, odd_cols)

    far_finals, far_offsets = [far_final], [far]
    far_pieces = [[piece] for piece in far_pieces]
    for bit in rest:
        far_finals = far_finals + [swapped(p, "row", bit) for p in far_finals]
        far_pieces = [same + [swapped(p, "row", bit) for p in same] for same in far_pieces]
        far_offsets = far_offsets + [o ^ bit for o in far_offsets]

    groups = channels // GROUP
    numbered = [(off, number) for number in range(len(far_pieces)) for off in far_offsets]
    sources = triples + [piece for same in far_pieces for piece in same]
    q, kv, wt = pl.pallas_call(
        functools.partial(project_kernel, offsets, numbered, triple_t.shape[0]),
        out_shape=(
            jax.ShapeDtypeStruct((groups, rows * cols, GROUP), jnp.bfloat16),
            jax.ShapeDtypeStruct((2 * groups, wide_rows * wide_cols, GROUP), jnp.bfloat16),
            jax.ShapeDtypeStruct((3 * channels, channels), jnp.bfloat16),
        ),
        in_specs=[scalars] + [anywhere] * len(sources) + [vmem] * 2,
        out_specs=(vmem,) * 3,
        scratch_shapes=[pltpu.SemaphoreType.DMA((len(sources),))],
        compiler_params=pltpu.CompilerParams(vmem_limit_bytes=VMEM_BYTES),
        cost_estimate=pl.CostEstimate(flops=5_000_000_000, bytes_accessed=14_000_000, transcendentals=0),
        name="project",
    )(place, *sources, xq, xkv)

    finals, offsets = finals + far_finals, offsets + far_offsets
    carriers_here = parts[0].shape[0]
    summary_result, wo, kce, vc = pl.pallas_call(
        functools.partial(carrier_kernel, offsets, len(parts)),
        out_shape=(
            jax.ShapeDtypeStruct(summary_vectors.shape, jnp.bfloat16),
            jax.ShapeDtypeStruct((channels, channels), jnp.bfloat16),
            jax.ShapeDtypeStruct((own.shape[0] * groups, GROUP, GROUP), jnp.bfloat16),
            jax.ShapeDtypeStruct((carriers_here, channels), jnp.float32),
        ),
        in_specs=[scalars] + [vmem] * (1 + len(parts)) + [anywhere] * len(finals),
        out_specs=(vmem,) * 4,
        scratch_shapes=[pltpu.SemaphoreType.DMA((len(finals),))],
        compiler_params=pltpu.CompilerParams(vmem_limit_bytes=VMEM_BYTES),
        cost_estimate=pl.CostEstimate(flops=500_000_000, bytes_accessed=5_000_000, transcendentals=10_000),
        name="carriers",
    )(place, wt, *parts, *finals)

    out = pl.pallas_call(
        attend_kernel,
        out_shape=jax.ShapeDtypeStruct(grid_elements.shape, jnp.bfloat16),
        in_specs=[vmem] * 7,
        out_specs=anywhere,
        scratch_shapes=[
            pltpu.VMEM((cols // (2 * TILE), rows, 2 * TILE, channels), jnp.bfloat16),
            pltpu.VMEM((rows * cols, channels), jnp.bfloat16),
            pltpu.SemaphoreType.DMA((cols // (2 * TILE),)),
        ],
        compiler_params=pltpu.CompilerParams(vmem_limit_bytes=VMEM_BYTES),
        cost_estimate=pl.CostEstimate(flops=5_000_000_000, bytes_accessed=12_000_000, transcendentals=4_000_000),
        name="attend",
    )(grid_elements, q, kv, hide, kce, vc, wo)
    return (out, summary_result)


def solution(mesh):
    placed = (
        P(("img", "row"), "col", None),
        P(("img", "row"), "col", None),
        P(None, "row"),
        P(None, "row"),
        P(("img", "row"), "col"),
    )
    return jax.shard_map(
        local,
        mesh=mesh,
        in_specs=placed,
        out_specs=(P(("img", "row"), "col", None), P(("img", "row"), "col", None)),
        check_vma=False,
    )
```

```python
import functools

import jax
import jax.numpy as jnp
from jax import lax
from jax.experimental import pallas as pl
from jax.experimental.pallas import tpu as pltpu
from jax.sharding import PartitionSpec as P

HEAD_DIM = 64
PATCH_SIDE = 16
RADIUS = 4
TILE = 2 * RADIUS
LANES = 128
GROUP = 256
INVALID = 100.0
HIDDEN = -1e30
EVEN_ROW, EVEN_COL, ROW, HALF = 4, 5, 6, 7
VMEM_BYTES = 24 * 1024 * 1024


def nt(a, b):
    return lax.dot_general(a, b, (((1,), (1,)), ((), ())), preferred_element_type=jnp.float32)


def nn(a, b):
    return lax.dot_general(a, b, (((1,), (0,)), ((), ())), preferred_element_type=jnp.float32)


def layer_normalise(lines):
    center = lines - jnp.mean(lines, axis=-1, keepdims=True)
    spread = jnp.mean(center * center, axis=-1, keepdims=True)
    return center * lax.rsqrt(spread + 1e-05)


def pair_swapped(even_block, odd_block, axis):
    count = lax.axis_size(axis)
    got = []
    for first, block in ((0, even_block), (1, odd_block)):
        pairs = [(i, i + 1) for i in range(first, count - 1, 2)]
        got.append(lax.ppermute(block, axis, pairs + [(b, a) for a, b in pairs]))
    return got


def swapped(block, axis, bit):
    count = lax.axis_size(axis)
    return lax.ppermute(block, axis, [(i, i ^ bit) for i in range(count)])


def after(block, *others):
    return lax.optimization_barrier((block, *others))[0]


def bits_of(count):
    bits, bit = [], count // 2
    while bit:
        bits.append(bit)
        bit //= 2
    return bits


def marked_lanes(lines, hidden):
    first = jnp.where(hidden, INVALID, lines[:, :, :LANES])
    return jnp.concatenate([first, lines[:, :, LANES:]], axis=2)


def edge_kernel(place_ref, flags_hbm, x_hbm, mark_ref, even_ref, odd_ref, flags_ref, first_s, last_s, spread, sems):
    rows, cols = flags_ref.shape
    copies = [
        pltpu.make_async_copy(x_hbm.at[0:RADIUS], first_s, sems.at[0]),
        pltpu.make_async_copy(x_hbm.at[rows - RADIUS : rows], last_s, sems.at[1]),
    ]
    flags_copy = pltpu.make_async_copy(flags_hbm, flags_ref, sems.at[2])
    flags_copy.start()
    for copy in copies:
        copy.start()
    flags_copy.wait()
    row_at = lax.broadcasted_iota(jnp.int32, (cols, cols), 0)
    diagonal = row_at == lax.broadcasted_iota(jnp.int32, (cols, cols), 1)
    for r in range(rows):
        hidden = jnp.where(flags_ref[r : r + 1, :] > 0, 0.0, INVALID)
        spread[r * cols : (r + 1) * cols, :] = jnp.where(diagonal, hidden, 0.0).astype(jnp.bfloat16)
    marks = nn(spread[...], jnp.ones((cols, LANES), jnp.bfloat16)).reshape(rows, cols, LANES)
    mark_ref[...] = marks.astype(jnp.bfloat16)
    for copy in copies:
        copy.wait()
    first, last = [
        marked_lanes(ref[...].astype(jnp.float32), marks[at] > INVALID / 2)
        for ref, at in ((first_s, slice(0, RADIUS)), (last_s, slice(rows - RADIUS, rows)))
    ]
    even = place_ref[EVEN_ROW] > 0
    even_ref[...] = jnp.where(even, last, first).astype(jnp.bfloat16)
    odd_ref[...] = jnp.where(even, first, last).astype(jnp.bfloat16)


def strip_kernel(place_ref, x_ref, mark_ref, even_rows_ref, odd_rows_ref, even_ref, odd_ref):
    rows, cols, channels = x_ref.shape
    middle = rows // 2
    low = lax.broadcasted_iota(jnp.int32, (1, TILE, 1), 1) < RADIUS
    even_row, even_col = place_ref[EVEN_ROW] > 0, place_ref[EVEN_COL] > 0
    for lane in range(0, channels, LANES):
        lanes = slice(lane, lane + LANES)
        strips = []
        for columns, last in ((slice(0, TILE), False), (slice(cols - TILE, cols), True)):

            def own(part):
                lines = x_ref[part, columns, lanes].astype(jnp.float32)
                if lane == 0:
                    lines = jnp.where(mark_ref[part, columns, :].astype(jnp.float32) > INVALID / 2, INVALID, lines)
                return lines

            even_rows = even_rows_ref[:, columns, lanes].astype(jnp.float32)
            odd_rows = odd_rows_ref[:, columns, lanes].astype(jnp.float32)
            top, bottom = jnp.where(even_row, odd_rows, even_rows), jnp.where(even_row, even_rows, odd_rows)
            upper = jnp.concatenate([top, own(slice(0, middle))], axis=0)
            lower = jnp.concatenate([own(slice(middle, rows)), bottom], axis=0)
            if last:
                upper = jnp.roll(upper, RADIUS, axis=1)
            else:
                lower = jnp.roll(lower, RADIUS, axis=1)
            strips.append(jnp.where(low, upper, lower))
        first, last = strips
        even_ref[:, :, lanes] = jnp.where(even_col, last, first).astype(jnp.bfloat16)
        odd_ref[:, :, lanes] = jnp.where(even_col, first, last).astype(jnp.bfloat16)


def own_kernel(x_ref, xq_ref):
    rows, cols, _ = x_ref.shape
    step = 4

    def own(i, _):
        at = pl.multiple_of(i * step, step)
        y = layer_normalise(x_ref[pl.ds(at, step)].astype(jnp.float32))
        for c in range(cols // TILE):
            piece = y[:, c * TILE : (c + 1) * TILE, :].reshape(step * TILE, -1)
            to = pl.multiple_of(c * rows * TILE + at * TILE, step * TILE)
            xq_ref[pl.ds(to, step * TILE), :] = piece.astype(jnp.bfloat16)
        return 0

    lax.fori_loop(0, rows // step, own, 0)


def halo_kernel(place_ref, xq_ref, mark_ref, even_rows_ref, odd_rows_ref, even_cols_ref, odd_cols_ref, xkv_ref, hide_ref, *scratch):
    rows, cols, _ = mark_ref.shape
    wide_rows, wide_cols = rows + 2 * RADIUS, cols + 2 * RADIUS
    half = wide_rows // 2
    step = 2
    top_s, bottom_s, left_s, right_s, top_ref, bottom_ref, left_ref, right_ref, flag_s = scratch
    for even, odd, low, high, low_flags, high_flags, parity, size in (
        (even_rows_ref, odd_rows_ref, top_s, bottom_s, top_ref, bottom_ref, EVEN_ROW, 2),
        (even_cols_ref, odd_cols_ref, left_s, right_s, left_ref, right_ref, EVEN_COL, 5),
    ):
        flip = place_ref[parity] > 0
        for i in range(0, even.shape[0], size):
            a, b = even[i : i + size].astype(jnp.float32), odd[i : i + size].astype(jnp.float32)
            for lines, out, flags in ((jnp.where(flip, b, a), low, low_flags), (jnp.where(flip, a, b), high, high_flags)):
                out[i : i + size] = layer_normalise(lines)
                flags[i : i + size] = lines[:, :, :LANES]

    def lines_of(ref):
        return ref.astype(jnp.float32)

    def merge(at, blocks, left, right, to_ref):
        low = lax.broadcasted_iota(jnp.int32, (1, TILE, 1), 1) < RADIUS
        before = left
        for c in range(len(blocks) + 1):
            after = jnp.roll(blocks[c], RADIUS, axis=1) if c < len(blocks) else right
            to = c * wide_rows * TILE + at * TILE
            to = pl.multiple_of(to, step * TILE) if not isinstance(to, int) else to
            lines = jnp.where(low, before, after).reshape(step * TILE, -1)
            to_ref[pl.ds(to, step * TILE), :] = lines.astype(jnp.bfloat16)
            before = after

    def sides(at, upper, left_ref, right_ref, lanes):
        if upper:
            at = at - half
            left, right = jnp.roll(lines_of(left_ref[pl.ds(at, step), :, lanes]), RADIUS, axis=1), lines_of(
                right_ref[pl.ds(at, step), :, lanes]
            )
        else:
            left, right = lines_of(left_ref[pl.ds(at, step), :, lanes]), jnp.roll(
                lines_of(right_ref[pl.ds(at, step), :, lanes]), RADIUS, axis=1
            )
        return left, right

    every, few = slice(None), slice(0, LANES)

    def hide_if(border, lines):
        return jnp.where(place_ref[border] > 0, INVALID, lines)

    def mark_sides(at, upper):
        left, right = sides(at, upper, left_ref, right_ref, few)
        return hide_if(2, left), hide_if(3, right)

    def band(at, ref, ref_s, first, upper):
        cut = [slice(c * TILE, (c + 1) * TILE) for c in range(cols // TILE)]
        merge(at, [ref_s[first : first + step, k, :] for k in cut], *sides(at, upper, left_s, right_s, every), xkv_ref)
        marks = hide_if(int(upper), ref[first : first + step])
        beside = [hide_if(int(upper), side) for side in mark_sides(at, upper)]
        merge(at, [marks[:, k, :] for k in cut], *beside, flag_s)

    for i in range(0, RADIUS, step):
        band(i, top_ref, top_s, i, False)
        band(RADIUS + rows + i, bottom_ref, bottom_s, i, True)

    def middle(i, upper):
        at = pl.multiple_of(i * step, step)
        own = at - RADIUS
        blocks = []
        for c in range(cols // TILE):
            first = pl.multiple_of(c * rows * TILE + own * TILE, step * TILE)
            blocks.append(xq_ref[pl.ds(first, step * TILE), :].astype(jnp.float32).reshape(step, TILE, -1))
        merge(at, blocks, *sides(at, upper, left_s, right_s, every), xkv_ref)
        marks = mark_ref[pl.ds(own, step)].astype(jnp.float32)
        marks = [marks[:, c * TILE : (c + 1) * TILE, :] for c in range(cols // TILE)]
        merge(at, marks, *mark_sides(at, upper), flag_s)
        return 0

    lax.fori_loop(RADIUS // step, half // step, lambda i, _: middle(i, False), 0)
    lax.fori_loop(half // step, (RADIUS + rows) // step, lambda i, _: middle(i, True), 0)

    first_lane = (lax.broadcasted_iota(jnp.int32, (8, LANES), 1) == 0).astype(jnp.bfloat16)
    spans = []
    for c in range(wide_cols // TILE):
        lines = flag_s[c * wide_rows * TILE : (c + 1) * wide_rows * TILE, :]
        spans.append(jnp.where(nt(first_lane, lines) > INVALID / 2, HIDDEN, 0.0))
    tall = rows // TILE
    for c in range(cols // TILE):
        for r in range(tall):
            at = slice(r * TILE * TILE, r * TILE * TILE + 2 * TILE * TILE)
            hide_ref[c * tall + r] = jnp.concatenate([spans[c][:, at], spans[c + 1][:, at]], axis=1)


def column_chunks(channels, half):
    at, end = half * 3 * channels // 2, (half + 1) * 3 * channels // 2
    chunks = []
    while at < end:
        width = min(GROUP - at % GROUP, end - at)
        chunks.append((at, at // channels, at % channels // GROUP, at % GROUP, width))
        at += width
    return chunks


def project_half(half, base, wt, xq_ref, xkv_ref, put):
    channels = wt.shape[1]
    factor = HEAD_DIM ** (-0.5)
    whole = 0
    for at, section, group, lane, width in column_chunks(channels, half):
        w = wt[at - base : at - base + width, :]
        source = xq_ref if section == 0 else xkv_ref
        chunk = source.shape[0] // (2 if section == 0 else 4)
        for m in range(0, source.shape[0], chunk):
            y = nt(source[m : m + chunk, :], w)
            put(section, group, lane, width, whole, slice(m, m + chunk), (y * factor if section == 0 else y).astype(jnp.bfloat16))
        whole += width == GROUP


def early_kernel(offsets, place_ref, *refs):
    triples, refs = refs[: len(offsets)], refs[len(offsets) :]
    xq_ref, xkv_ref, whole_ref, part_ref, wt, sems = refs
    triple_rows = wt.shape[0] // len(offsets)
    copies = []
    for j, off in enumerate(offsets):
        to = pl.multiple_of(((place_ref[ROW] ^ off) % len(offsets)) * triple_rows, 16)
        copies.append(pltpu.make_async_copy(triples[j], wt.at[pl.ds(to, triple_rows), :], sems.at[j]))
        copies[-1].start()
    for copy in copies:
        copy.wait()

    def put(section, group, lane, width, number, lines, value):
        if width == GROUP:
            whole_ref[number, lines, :] = value
        else:
            part_ref[lines, :] = value

    for half in range(2):
        pl.when(place_ref[HALF] == half)(
            functools.partial(project_half, half, half * wt.shape[0], wt, xq_ref, xkv_ref, put)
        )


def late_kernel(offsets, place_ref, *refs):
    triples, refs = refs[: len(offsets)], refs[len(offsets) :]
    xq_ref, xkv_ref, whole_ref, part_ref, q_s, kv_s, wt, sems, early_sems = refs
    triple_rows = wt.shape[0] // len(offsets)
    channels = wt.shape[1]
    groups = channels // GROUP
    copies = []
    for j, off in reversed(list(enumerate(offsets))):
        to = pl.multiple_of((place_ref[ROW] ^ off) * triple_rows, 16)
        copies.append(pltpu.make_async_copy(triples[j], wt.at[pl.ds(to, triple_rows), :], sems.at[j]))
        copies[-1].start()

    def put(section, group, lane, width, number, lines, value):
        if section == 0:
            q_s[group, lines, :] = value
        else:
            kv_s[(section - 1) * groups + group, lines, lane : lane + width] = value

    def late(half):
        number, moves = 0, []
        for _, section, group, lane, width in column_chunks(channels, 1 - half):
            source = whole_ref.at[number] if width == GROUP else part_ref
            if section == 0:
                source, target = source.at[0 : q_s.shape[1], :], q_s.at[group]
            else:
                target = kv_s.at[(section - 1) * groups + group, :, lane : lane + width]
            move = pltpu.make_async_copy(source, target, early_sems.at[len(moves)])
            move.start()
            moves.append(move)
            number += width == GROUP
        project_half(half, 0, wt, xq_ref, xkv_ref, put)
        for move in moves:
            move.wait()

    for copy in copies:
        copy.wait()
    for half in range(2):
        pl.when(place_ref[HALF] != half)(functools.partial(late, half))


def carrier_kernel(offsets, carrier_parts, place_ref, wt, *refs):
    shards = len(offsets)
    parts, finals, refs = refs[:carrier_parts], refs[carrier_parts : carrier_parts + shards], refs[carrier_parts + shards :]
    summary_ref, wo, kce, vc_s, sems = refs
    channels = wt.shape[1]
    groups = channels // GROUP
    heads = channels // HEAD_DIM
    factor = HEAD_DIM ** (-0.5)
    carriers_here = parts[0].shape[0]
    final_rows = wo.shape[0] // shards
    copies = []
    for j, off in enumerate(offsets):
        to = pl.multiple_of((place_ref[ROW] ^ off) * final_rows, 16)
        copy = pltpu.make_async_copy(finals[j], wo.at[pl.ds(to, final_rows), :], sems.at[j])
        copy.start()
        copies.append(copy)
    carriers = jnp.concatenate([part[...].astype(jnp.float32) for part in parts], axis=0)
    own = carriers[:carriers_here]
    carriers = layer_normalise(carriers).astype(jnp.bfloat16)
    own_norm = layer_normalise(own).astype(jnp.bfloat16)
    qc = (nt(own_norm, wt[:channels, :]) * factor).astype(jnp.bfloat16).astype(jnp.float32)
    kc = nt(carriers, wt[channels : 2 * channels, :]).astype(jnp.bfloat16)
    vc = nt(carriers, wt[2 * channels :, :]).astype(jnp.bfloat16)
    head_of = lax.broadcasted_iota(jnp.int32, (1, channels), 1) // HEAD_DIM
    stacked = jnp.concatenate([jnp.where(head_of == h, qc, 0.0) for h in range(heads)], axis=0)
    e = jnp.exp(nt(stacked.astype(jnp.bfloat16), kc))
    weights = (e / jnp.sum(e, axis=-1, keepdims=True)).astype(jnp.bfloat16)
    o = nn(weights, vc)
    mix = jnp.zeros((carriers_here, channels), jnp.float32)
    for h in range(heads):
        mix = jnp.where(head_of == h, o[h * carriers_here : (h + 1) * carriers_here, :], mix)
    for copy in copies:
        copy.wait()
    renewed = own + nt(mix.astype(jnp.bfloat16), wo[...])
    per_row = summary_ref.shape[1]
    for i in range(summary_ref.shape[0]):
        summary_ref[i] = renewed[i * per_row : (i + 1) * per_row, :].astype(jnp.bfloat16)
    fresh = nt(layer_normalise(renewed).astype(jnp.bfloat16), wt[channels:, :]).astype(jnp.bfloat16).astype(jnp.float32)
    vc_s[...] = fresh[:, channels:]
    same = (
        lax.broadcasted_iota(jnp.int32, (GROUP, GROUP), 0) // HEAD_DIM
        == lax.broadcasted_iota(jnp.int32, (GROUP, GROUP), 1) // HEAD_DIM
    )
    windows = kce.shape[0] // groups
    for w in range(windows):
        for g in range(groups):
            kce[w * groups + g] = jnp.where(same, fresh[w : w + 1, g * GROUP : (g + 1) * GROUP], 0.0).astype(jnp.bfloat16)


def attend_kernel(x_ref, q_s, kv_s, hide_ref, kce, vc_s, wo, out_hbm, out_ref, mix_s, out_sems):
    rows, cols, channels = x_ref.shape
    groups = channels // GROUP
    heads_in = GROUP // HEAD_DIM
    wide_rows = rows + 2 * RADIUS
    queries, span = TILE * TILE, 2 * TILE * TILE
    qi = lax.broadcasted_iota(jnp.int32, (queries, 2 * span), 0)
    ki = lax.broadcasted_iota(jnp.int32, (queries, 2 * span), 1)
    row_step = (ki % span) // TILE - qi // TILE
    col_step = (ki // span) * TILE + ki % TILE - qi % TILE
    seen = (row_step >= 0) & (row_step <= 2 * RADIUS) & (col_step >= 0) & (col_step <= 2 * RADIUS)
    band = jnp.where(seen, 0.0, HIDDEN)
    group_head = lax.broadcasted_iota(jnp.int32, (1, GROUP), 1) // HEAD_DIM
    tall, broad = rows // TILE, cols // TILE
    per_side = PATCH_SIDE // TILE

    def tile(t, _):
        c, r = t // tall, t % tall
        q_at = pl.multiple_of(c * (rows * TILE) + r * queries, queries)
        k0 = pl.multiple_of(c * (wide_rows * TILE) + r * queries, queries)
        k1 = pl.multiple_of(k0 + wide_rows * TILE, queries)
        window = (r // per_side) * (broad // per_side) + c // per_side
        bias = band + hide_ref[t][0:1, :]
        for g in range(groups):
            q = q_s[g, pl.ds(q_at, queries), :]
            q32 = q.astype(jnp.float32)
            qq = jnp.concatenate(
                [jnp.where(group_head == h, q32, 0.0).astype(jnp.bfloat16) for h in range(heads_in)], axis=0
            )
            k = jnp.concatenate([kv_s[g, pl.ds(k0, span), :], kv_s[g, pl.ds(k1, span), :]], axis=0)
            v = jnp.concatenate(
                [kv_s[groups + g, pl.ds(k0, span), :], kv_s[groups + g, pl.ds(k1, span), :]], axis=0
            )
            p = jnp.exp(nt(qq, k).reshape(heads_in, queries, 2 * span) + bias[None])
            total = jnp.sum(p, axis=-1, keepdims=True)
            o = nn(p.reshape(heads_in * queries, 2 * span).astype(jnp.bfloat16), v)
            o = o.reshape(heads_in, queries, GROUP)
            kept, kept_total = o[0], total[0]
            for h in range(1, heads_in):
                kept = jnp.where(group_head == h, o[h], kept)
                kept_total = jnp.where(group_head == h, total[h], kept_total)
            pc = jnp.exp(nt(q, kce[window * groups + g]))
            v_new = vc_s[pl.ds(window, 1), g * GROUP : (g + 1) * GROUP]
            mixed = (kept + pc * v_new) / (kept_total + pc)
            mix_s[pl.ds(q_at, queries), g * GROUP : (g + 1) * GROUP] = mixed.astype(jnp.bfloat16)
        return 0

    lax.fori_loop(0, tall * broad, tile, 0)

    going = []
    for pair in range(broad // 2):
        both = slice(2 * pair * TILE, 2 * (pair + 1) * TILE)
        for g in range(groups):
            at = slice(g * GROUP, (g + 1) * GROUP)
            w = wo[at, :]
            parts = [
                nt(mix_s[b * rows * TILE : (b + 1) * rows * TILE, :], w).reshape(rows, TILE, GROUP)
                for b in (2 * pair, 2 * pair + 1)
            ]
            y = jnp.concatenate(parts, axis=1) + x_ref[:, both, at].astype(jnp.float32)
            out_ref[pair, :, :, at] = y.astype(jnp.bfloat16)
        copy = pltpu.make_async_copy(out_ref.at[pair], out_hbm.at[:, both, :], out_sems.at[pair])
        copy.start()
        going.append(copy)
    for copy in going:
        copy.wait()


def local(grid_elements, summary_vectors, triple_projection, final_projection, genuine_flags):
    rows, cols, channels = grid_elements.shape
    wide_rows, wide_cols = rows + 2 * RADIUS, cols + 2 * RADIUS
    own = summary_vectors.reshape(-1, channels)

    triple_t, final_t = triple_projection.T, final_projection.T
    vmem = pl.BlockSpec(memory_space=pltpu.VMEM)
    anywhere = pl.BlockSpec(memory_space=pl.ANY)
    scalars = pl.BlockSpec(memory_space=pltpu.SMEM)
    hbm = pl.BlockSpec(memory_space=pltpu.HBM)
    small = pltpu.CompilerParams(vmem_limit_bytes=16 * 1024 * 1024)
    row_strip = jax.ShapeDtypeStruct((RADIUS, cols, channels), jnp.bfloat16)
    col_strip = jax.ShapeDtypeStruct((wide_rows // 2, 2 * RADIUS, channels), jnp.bfloat16)

    row, col = lax.axis_size("row"), lax.axis_size("col")
    row_at, col_at = lax.axis_index("row"), lax.axis_index("col")
    row_bits = bits_of(row)
    far, rest = row_bits[0], row_bits[1:]
    place = [row_at == 0, row_at == row - 1, col_at == 0, col_at == col - 1, row_at % 2 == 0, col_at % 2 == 0]
    place = jnp.stack([jnp.asarray(p).astype(jnp.int32) for p in place + [row_at, row_at // far]])

    far_final = swapped(final_t, "row", far)

    mark, even_rows, odd_rows = pl.pallas_call(
        edge_kernel,
        out_shape=(
            jax.ShapeDtypeStruct((rows, cols, LANES), jnp.bfloat16),
            row_strip,
            row_strip,
        ),
        in_specs=[scalars, hbm, hbm],
        out_specs=(vmem,) * 3,
        scratch_shapes=[
            pltpu.VMEM((rows, cols), jnp.int32),
            pltpu.VMEM(row_strip.shape, jnp.bfloat16),
            pltpu.VMEM(row_strip.shape, jnp.bfloat16),
            pltpu.VMEM((rows * cols, cols), jnp.bfloat16),
            pltpu.SemaphoreType.DMA((3,)),
        ],
        compiler_params=small,
        cost_estimate=pl.CostEstimate(flops=1_000_000, bytes_accessed=1_000_000, transcendentals=0),
        name="edge_rows",
    )(place, *(pltpu.with_memory_space_constraint(a, pltpu.HBM) for a in (genuine_flags, grid_elements)))
    even_rows, odd_rows = pair_swapped(even_rows, odd_rows, "row")

    far_triple = swapped(after(triple_t, even_rows, odd_rows, far_final), "row", far)

    even_cols, odd_cols = pl.pallas_call(
        strip_kernel,
        out_shape=(col_strip, col_strip),
        in_specs=[scalars] + [vmem] * 4,
        out_specs=(vmem,) * 2,
        compiler_params=small,
        cost_estimate=pl.CostEstimate(flops=1_000_000, bytes_accessed=1_000_000, transcendentals=0),
        name="edge_columns",
    )(place, grid_elements, mark, even_rows, odd_rows)
    even_cols, odd_cols = pair_swapped(even_cols, odd_cols, "col")

    finals, triples, offsets = [final_t], [triple_t], [0]
    for bit in rest:
        finals = finals + [swapped(p, "row", bit) for p in finals]
        triples = triples + [swapped(p, "row", bit) for p in triples]
        offsets = offsets + [o ^ bit for o in offsets]
    parts, carriers = [], after(own, even_cols, odd_cols)
    for bit in bits_of(col):
        got = swapped(carriers, "col", bit)
        carriers = jnp.concatenate([carriers, got], axis=0)
        parts = parts + [got] if parts else [carriers]

    tiles = (rows // TILE) * (cols // TILE)
    keys = 4 * TILE * TILE
    xq = pl.pallas_call(
        own_kernel,
        out_shape=jax.ShapeDtypeStruct((rows * cols, channels), jnp.bfloat16),
        in_specs=[vmem],
        out_specs=vmem,
        compiler_params=small,
        cost_estimate=pl.CostEstimate(flops=1_000_000, bytes_accessed=1_000_000, transcendentals=0),
        name="own_norm",
    )(grid_elements)
    xkv, hide = pl.pallas_call(
        halo_kernel,
        out_shape=(
            jax.ShapeDtypeStruct((wide_rows * wide_cols, channels), jnp.bfloat16),
            jax.ShapeDtypeStruct((tiles, 8, keys), jnp.float32),
        ),
        in_specs=[scalars] + [vmem] * 6,
        out_specs=(vmem,) * 2,
        scratch_shapes=[
            *[pltpu.VMEM(shape.shape, jnp.float32) for shape in (row_strip, row_strip, col_strip, col_strip)],
            *[pltpu.VMEM((*shape.shape[:2], LANES), jnp.float32) for shape in (row_strip, row_strip, col_strip, col_strip)],
            pltpu.VMEM((wide_rows * wide_cols, LANES), jnp.bfloat16),
        ],
        compiler_params=pltpu.CompilerParams(vmem_limit_bytes=24 * 1024 * 1024),
        cost_estimate=pl.CostEstimate(flops=1_000_000, bytes_accessed=1_000_000, transcendentals=0),
        name="halo_norm",
    )(place, xq, mark, even_rows, odd_rows, even_cols, odd_cols)

    groups = channels // GROUP
    project = dict(
        compiler_params=pltpu.CompilerParams(vmem_limit_bytes=VMEM_BYTES),
        cost_estimate=pl.CostEstimate(flops=1_000_000, bytes_accessed=1_000_000, transcendentals=0),
    )
    early = pl.pallas_call(
        functools.partial(early_kernel, offsets),
        out_shape=(
            jax.ShapeDtypeStruct((3 * groups // 2, wide_rows * wide_cols, GROUP), jnp.bfloat16),
            jax.ShapeDtypeStruct((wide_rows * wide_cols, GROUP // 2), jnp.bfloat16),
        ),
        in_specs=[scalars] + [anywhere] * len(triples) + [vmem] * 2,
        out_specs=(vmem,) * 2,
        scratch_shapes=[
            pltpu.VMEM((3 * channels // 2, channels), jnp.bfloat16),
            pltpu.SemaphoreType.DMA((len(triples),)),
        ],
        name="project_early",
        **project,
    )(place, *triples, xq, after(xkv, carriers))

    far_finals, far_triples = [far_final], [after(far_triple, *early)]
    carriers = after(carriers, far_triple)
    for bit in row_bits:
        got = swapped(carriers, "row", bit)
        carriers = jnp.concatenate([carriers, got], axis=0)
        parts = parts + [got]
    for bit in rest:
        far_finals = far_finals + [swapped(p, "row", bit) for p in far_finals]
        far_triples = far_triples + [swapped(p, "row", bit) for p in far_triples]
    finals, triples = finals + far_finals, triples + far_triples
    offsets = offsets + [o ^ far for o in offsets]

    q, kv, wt = pl.pallas_call(
        functools.partial(late_kernel, offsets),
        out_shape=(
            jax.ShapeDtypeStruct((groups, rows * cols, GROUP), jnp.bfloat16),
            jax.ShapeDtypeStruct((2 * groups, wide_rows * wide_cols, GROUP), jnp.bfloat16),
            jax.ShapeDtypeStruct((3 * channels, channels), jnp.bfloat16),
        ),
        in_specs=[scalars] + [anywhere] * len(triples) + [vmem] * 2 + [anywhere] * 2,
        out_specs=(vmem,) * 3,
        scratch_shapes=[
            pltpu.SemaphoreType.DMA((len(triples),)),
            pltpu.SemaphoreType.DMA((3 * groups // 2 + 1,)),
        ],
        name="project_late",
        **project,
    )(place, *triples, xq, xkv, *early)

    carriers_here = parts[0].shape[0]
    summary_result, wo, kce, vc = pl.pallas_call(
        functools.partial(carrier_kernel, offsets, len(parts)),
        out_shape=(
            jax.ShapeDtypeStruct(summary_vectors.shape, jnp.bfloat16),
            jax.ShapeDtypeStruct((channels, channels), jnp.bfloat16),
            jax.ShapeDtypeStruct((own.shape[0] * groups, GROUP, GROUP), jnp.bfloat16),
            jax.ShapeDtypeStruct((carriers_here, channels), jnp.float32),
        ),
        in_specs=[scalars] + [vmem] * (1 + len(parts)) + [anywhere] * len(finals),
        out_specs=(vmem,) * 4,
        scratch_shapes=[pltpu.SemaphoreType.DMA((len(finals),))],
        compiler_params=pltpu.CompilerParams(vmem_limit_bytes=VMEM_BYTES),
        cost_estimate=pl.CostEstimate(flops=500_000_000, bytes_accessed=5_000_000, transcendentals=10_000),
        name="carriers",
    )(place, wt, *parts, *finals)

    out = pl.pallas_call(
        attend_kernel,
        out_shape=jax.ShapeDtypeStruct(grid_elements.shape, jnp.bfloat16),
        in_specs=[vmem] * 7,
        out_specs=anywhere,
        scratch_shapes=[
            pltpu.VMEM((cols // (2 * TILE), rows, 2 * TILE, channels), jnp.bfloat16),
            pltpu.VMEM((rows * cols, channels), jnp.bfloat16),
            pltpu.SemaphoreType.DMA((cols // (2 * TILE),)),
        ],
        compiler_params=pltpu.CompilerParams(vmem_limit_bytes=VMEM_BYTES),
        cost_estimate=pl.CostEstimate(flops=5_000_000_000, bytes_accessed=12_000_000, transcendentals=4_000_000),
        name="attend",
    )(grid_elements, q, kv, hide, kce, vc, wo)
    return (out, summary_result)


def solution(mesh):
    placed = (
        P(("img", "row"), "col", None),
        P(("img", "row"), "col", None),
        P(None, "row"),
        P(None, "row"),
        P(("img", "row"), "col"),
    )
    return jax.shard_map(
        local,
        mesh=mesh,
        in_specs=placed,
        out_specs=(P(("img", "row"), "col", None), P(("img", "row"), "col", None)),
        check_vma=False,
    )
```

```python
import functools

import jax
import jax.numpy as jnp
from jax import lax
from jax.experimental import pallas as pl
from jax.experimental.pallas import tpu as pltpu
from jax.sharding import PartitionSpec as P

HEAD_DIM = 64
PATCH_SIDE = 16
RADIUS = 4
TILE = 2 * RADIUS
LANES = 128
GROUP = 256
INVALID = 100.0
HIDDEN = -1e30
EVEN_ROW, EVEN_COL, ROW, STARTS = 4, 5, 6, 7
VMEM_BYTES = 24 * 1024 * 1024


def nt(a, b):
    return lax.dot_general(a, b, (((1,), (1,)), ((), ())), preferred_element_type=jnp.float32)


def nn(a, b):
    return lax.dot_general(a, b, (((1,), (0,)), ((), ())), preferred_element_type=jnp.float32)


def layer_normalise(lines):
    center = lines - jnp.mean(lines, axis=-1, keepdims=True)
    spread = jnp.mean(center * center, axis=-1, keepdims=True)
    return center * lax.rsqrt(spread + 1e-05)


def pair_swapped(even_block, odd_block, axis):
    count = lax.axis_size(axis)
    got = []
    for first, block in ((0, even_block), (1, odd_block)):
        pairs = [(i, i + 1) for i in range(first, count - 1, 2)]
        got.append(lax.ppermute(block, axis, pairs + [(b, a) for a, b in pairs]))
    return got


def swapped(block, axis, bit):
    count = lax.axis_size(axis)
    return lax.ppermute(block, axis, [(i, i ^ bit) for i in range(count)])


def after(block, *others):
    return lax.optimization_barrier((block, *others))[0]


def bits_of(count):
    bits, bit = [], count // 2
    while bit:
        bits.append(bit)
        bit //= 2
    return bits


def marked_lanes(lines, hidden):
    first = jnp.where(hidden, INVALID, lines[:, :, :LANES])
    return jnp.concatenate([first, lines[:, :, LANES:]], axis=2)


def edge_kernel(piece_rows, place_ref, flags_hbm, x_hbm, triple_hbm, mark_ref, even_ref, odd_ref, mine_ref, last_ref, *scratch):
    flags_ref, first_s, last_s, spread, sems = scratch
    rows, cols = flags_ref.shape
    own_start = pl.multiple_of(place_ref[STARTS], 16)
    last_start = triple_hbm.shape[0] - last_ref.shape[0]
    copies = [
        pltpu.make_async_copy(x_hbm.at[0:RADIUS], first_s, sems.at[0]),
        pltpu.make_async_copy(x_hbm.at[rows - RADIUS : rows], last_s, sems.at[1]),
        pltpu.make_async_copy(triple_hbm.at[pl.ds(own_start, piece_rows), :], mine_ref, sems.at[2]),
        pltpu.make_async_copy(triple_hbm.at[last_start:, :], last_ref, sems.at[3]),
    ]
    flags_copy = pltpu.make_async_copy(flags_hbm, flags_ref, sems.at[4])
    flags_copy.start()
    for copy in copies:
        copy.start()
    flags_copy.wait()
    row_at = lax.broadcasted_iota(jnp.int32, (cols, cols), 0)
    diagonal = row_at == lax.broadcasted_iota(jnp.int32, (cols, cols), 1)
    for r in range(rows):
        hidden = jnp.where(flags_ref[r : r + 1, :] > 0, 0.0, INVALID)
        spread[r * cols : (r + 1) * cols, :] = jnp.where(diagonal, hidden, 0.0).astype(jnp.bfloat16)
    marks = nn(spread[...], jnp.ones((cols, LANES), jnp.bfloat16)).reshape(rows, cols, LANES)
    mark_ref[...] = marks.astype(jnp.bfloat16)
    for copy in copies:
        copy.wait()
    first, last = [
        marked_lanes(ref[...].astype(jnp.float32), marks[at] > INVALID / 2)
        for ref, at in ((first_s, slice(0, RADIUS)), (last_s, slice(rows - RADIUS, rows)))
    ]
    even = place_ref[EVEN_ROW] > 0
    even_ref[...] = jnp.where(even, last, first).astype(jnp.bfloat16)
    odd_ref[...] = jnp.where(even, first, last).astype(jnp.bfloat16)


def strip_kernel(place_ref, x_ref, mark_ref, even_rows_ref, odd_rows_ref, even_ref, odd_ref):
    rows, cols, channels = x_ref.shape
    middle = rows // 2
    low = lax.broadcasted_iota(jnp.int32, (1, TILE, 1), 1) < RADIUS
    even_row, even_col = place_ref[EVEN_ROW] > 0, place_ref[EVEN_COL] > 0
    for lane in range(0, channels, LANES):
        lanes = slice(lane, lane + LANES)
        strips = []
        for columns, last in ((slice(0, TILE), False), (slice(cols - TILE, cols), True)):

            def own(part):
                lines = x_ref[part, columns, lanes].astype(jnp.float32)
                if lane == 0:
                    lines = jnp.where(mark_ref[part, columns, :].astype(jnp.float32) > INVALID / 2, INVALID, lines)
                return lines

            even_rows = even_rows_ref[:, columns, lanes].astype(jnp.float32)
            odd_rows = odd_rows_ref[:, columns, lanes].astype(jnp.float32)
            top, bottom = jnp.where(even_row, odd_rows, even_rows), jnp.where(even_row, even_rows, odd_rows)
            upper = jnp.concatenate([top, own(slice(0, middle))], axis=0)
            lower = jnp.concatenate([own(slice(middle, rows)), bottom], axis=0)
            if last:
                upper = jnp.roll(upper, RADIUS, axis=1)
            else:
                lower = jnp.roll(lower, RADIUS, axis=1)
            strips.append(jnp.where(low, upper, lower))
        first, last = strips
        even_ref[:, :, lanes] = jnp.where(even_col, last, first).astype(jnp.bfloat16)
        odd_ref[:, :, lanes] = jnp.where(even_col, first, last).astype(jnp.bfloat16)


def own_kernel(x_ref, xq_ref):
    rows, cols, _ = x_ref.shape
    step = 4

    def own(i, _):
        at = pl.multiple_of(i * step, step)
        y = layer_normalise(x_ref[pl.ds(at, step)].astype(jnp.float32))
        for c in range(cols // TILE):
            piece = y[:, c * TILE : (c + 1) * TILE, :].reshape(step * TILE, -1)
            to = pl.multiple_of(c * rows * TILE + at * TILE, step * TILE)
            xq_ref[pl.ds(to, step * TILE), :] = piece.astype(jnp.bfloat16)
        return 0

    lax.fori_loop(0, rows // step, own, 0)


def halo_kernel(place_ref, xq_ref, mark_ref, even_rows_ref, odd_rows_ref, even_cols_ref, odd_cols_ref, xkv_ref, hide_ref, *scratch):
    rows, cols, _ = mark_ref.shape
    wide_rows, wide_cols = rows + 2 * RADIUS, cols + 2 * RADIUS
    half = wide_rows // 2
    step = 2
    top_s, bottom_s, left_s, right_s, top_ref, bottom_ref, left_ref, right_ref, flag_s = scratch
    for even, odd, low, high, low_flags, high_flags, parity, size in (
        (even_rows_ref, odd_rows_ref, top_s, bottom_s, top_ref, bottom_ref, EVEN_ROW, 2),
        (even_cols_ref, odd_cols_ref, left_s, right_s, left_ref, right_ref, EVEN_COL, 5),
    ):
        flip = place_ref[parity] > 0
        for i in range(0, even.shape[0], size):
            a, b = even[i : i + size].astype(jnp.float32), odd[i : i + size].astype(jnp.float32)
            for lines, out, flags in ((jnp.where(flip, b, a), low, low_flags), (jnp.where(flip, a, b), high, high_flags)):
                out[i : i + size] = layer_normalise(lines)
                flags[i : i + size] = lines[:, :, :LANES]

    def lines_of(ref):
        return ref.astype(jnp.float32)

    def merge(at, blocks, left, right, to_ref):
        low = lax.broadcasted_iota(jnp.int32, (1, TILE, 1), 1) < RADIUS
        before = left
        for c in range(len(blocks) + 1):
            after = jnp.roll(blocks[c], RADIUS, axis=1) if c < len(blocks) else right
            to = c * wide_rows * TILE + at * TILE
            to = pl.multiple_of(to, step * TILE) if not isinstance(to, int) else to
            lines = jnp.where(low, before, after).reshape(step * TILE, -1)
            to_ref[pl.ds(to, step * TILE), :] = lines.astype(jnp.bfloat16)
            before = after

    def sides(at, upper, left_ref, right_ref, lanes):
        if upper:
            at = at - half
            left, right = jnp.roll(lines_of(left_ref[pl.ds(at, step), :, lanes]), RADIUS, axis=1), lines_of(
                right_ref[pl.ds(at, step), :, lanes]
            )
        else:
            left, right = lines_of(left_ref[pl.ds(at, step), :, lanes]), jnp.roll(
                lines_of(right_ref[pl.ds(at, step), :, lanes]), RADIUS, axis=1
            )
        return left, right

    every, few = slice(None), slice(0, LANES)

    def hide_if(border, lines):
        return jnp.where(place_ref[border] > 0, INVALID, lines)

    def mark_sides(at, upper):
        left, right = sides(at, upper, left_ref, right_ref, few)
        return hide_if(2, left), hide_if(3, right)

    def band(at, ref, ref_s, first, upper):
        cut = [slice(c * TILE, (c + 1) * TILE) for c in range(cols // TILE)]
        merge(at, [ref_s[first : first + step, k, :] for k in cut], *sides(at, upper, left_s, right_s, every), xkv_ref)
        marks = hide_if(int(upper), ref[first : first + step])
        beside = [hide_if(int(upper), side) for side in mark_sides(at, upper)]
        merge(at, [marks[:, k, :] for k in cut], *beside, flag_s)

    for i in range(0, RADIUS, step):
        band(i, top_ref, top_s, i, False)
        band(RADIUS + rows + i, bottom_ref, bottom_s, i, True)

    def middle(i, upper):
        at = pl.multiple_of(i * step, step)
        own = at - RADIUS
        blocks = []
        for c in range(cols // TILE):
            first = pl.multiple_of(c * rows * TILE + own * TILE, step * TILE)
            blocks.append(xq_ref[pl.ds(first, step * TILE), :].astype(jnp.float32).reshape(step, TILE, -1))
        merge(at, blocks, *sides(at, upper, left_s, right_s, every), xkv_ref)
        marks = mark_ref[pl.ds(own, step)].astype(jnp.float32)
        marks = [marks[:, c * TILE : (c + 1) * TILE, :] for c in range(cols // TILE)]
        merge(at, marks, *mark_sides(at, upper), flag_s)
        return 0

    lax.fori_loop(RADIUS // step, half // step, lambda i, _: middle(i, False), 0)
    lax.fori_loop(half // step, (RADIUS + rows) // step, lambda i, _: middle(i, True), 0)

    first_lane = (lax.broadcasted_iota(jnp.int32, (8, LANES), 1) == 0).astype(jnp.bfloat16)
    spans = []
    for c in range(wide_cols // TILE):
        lines = flag_s[c * wide_rows * TILE : (c + 1) * wide_rows * TILE, :]
        spans.append(jnp.where(nt(first_lane, lines) > INVALID / 2, HIDDEN, 0.0))
    tall = rows // TILE
    for c in range(cols // TILE):
        for r in range(tall):
            at = slice(r * TILE * TILE, r * TILE * TILE + 2 * TILE * TILE)
            hide_ref[c * tall + r] = jnp.concatenate([spans[c][:, at], spans[c + 1][:, at]], axis=1)


def project_kernel(whole, pieces, triple_rows, place_ref, *refs):
    sources, refs = refs[: len(whole) + len(pieces)], refs[len(whole) + len(pieces) :]
    xq_ref, xkv_ref, q_s, kv_s, wt, sems = refs
    channels = wt.shape[1]
    groups = channels // GROUP
    factor = HEAD_DIM ** (-0.5)
    me = place_ref[ROW]
    copies = []
    for j, source in enumerate(sources):
        if j < len(whole):
            to = (me ^ whole[j]) * triple_rows
        else:
            off, start = pieces[j - len(whole)]
            to = (me ^ off) * triple_rows + place_ref[STARTS + start]
        to = pl.multiple_of(to, 16)
        copy = pltpu.make_async_copy(source, wt.at[pl.ds(to, source.shape[0]), :], sems.at[j])
        copy.start()
        copies.append(copy)
    for copy in copies:
        copy.wait()

    q_rows, kv_rows = xq_ref.shape[0], xkv_ref.shape[0]
    q_chunk, kv_chunk = q_rows // 2, kv_rows // 4

    def project_q(n, _):
        w = wt[pl.ds(pl.multiple_of(n * GROUP, GROUP), GROUP), :]
        for m in range(0, q_rows, q_chunk):
            q_s[n, m : m + q_chunk, :] = (nt(xq_ref[m : m + q_chunk, :], w) * factor).astype(jnp.bfloat16)
        return 0

    def project_kv(n, _):
        w = wt[pl.ds(pl.multiple_of(channels + n * GROUP, GROUP), GROUP), :]
        for m in range(0, kv_rows, kv_chunk):
            kv_s[n, m : m + kv_chunk, :] = nt(xkv_ref[m : m + kv_chunk, :], w).astype(jnp.bfloat16)
        return 0

    lax.fori_loop(0, groups, project_q, 0)
    lax.fori_loop(0, 2 * groups, project_kv, 0)


def carrier_kernel(offsets, place_ref, wt, own_ref, carriers_ref, *refs):
    shards = len(offsets)
    finals, refs = refs[:shards], refs[shards:]
    summary_ref, wo, kce, vc_s, own_s, carriers_s, sems = refs
    channels = wt.shape[1]
    groups = channels // GROUP
    heads = channels // HEAD_DIM
    factor = HEAD_DIM ** (-0.5)
    carriers_here = own_s.shape[0]
    final_rows = wo.shape[0] // shards
    copies = []
    for j, off in enumerate(offsets):
        to = pl.multiple_of((place_ref[ROW] ^ off) * final_rows, 16)
        copy = pltpu.make_async_copy(finals[j], wo.at[pl.ds(to, final_rows), :], sems.at[j])
        copy.start()
        copies.append(copy)
    own_s[...] = jnp.zeros_like(own_s)
    per_row = own_ref.shape[1]
    for i in range(own_ref.shape[0]):
        own_s[i * per_row : (i + 1) * per_row, :] = own_ref[i].astype(jnp.float32)
    per_device = carriers_ref.shape[1]
    for i in range(carriers_ref.shape[0]):
        carriers_s[i * per_device : (i + 1) * per_device, :] = carriers_ref[i].astype(jnp.float32)
    own = own_s[...]
    carriers = layer_normalise(carriers_s[...]).astype(jnp.bfloat16)
    own_norm = layer_normalise(own).astype(jnp.bfloat16)
    qc = (nt(own_norm, wt[:channels, :]) * factor).astype(jnp.bfloat16).astype(jnp.float32)
    kc = nt(carriers, wt[channels : 2 * channels, :]).astype(jnp.bfloat16)
    vc = nt(carriers, wt[2 * channels :, :]).astype(jnp.bfloat16)
    head_of = lax.broadcasted_iota(jnp.int32, (1, channels), 1) // HEAD_DIM
    stacked = jnp.concatenate([jnp.where(head_of == h, qc, 0.0) for h in range(heads)], axis=0)
    e = jnp.exp(nt(stacked.astype(jnp.bfloat16), kc))
    weights = (e / jnp.sum(e, axis=-1, keepdims=True)).astype(jnp.bfloat16)
    o = nn(weights, vc)
    mix = jnp.zeros((carriers_here, channels), jnp.float32)
    for h in range(heads):
        mix = jnp.where(head_of == h, o[h * carriers_here : (h + 1) * carriers_here, :], mix)
    for copy in copies:
        copy.wait()
    renewed = own + nt(mix.astype(jnp.bfloat16), wo[...])
    for i in range(summary_ref.shape[0]):
        summary_ref[i] = renewed[i * per_row : (i + 1) * per_row, :].astype(jnp.bfloat16)
    fresh = nt(layer_normalise(renewed).astype(jnp.bfloat16), wt[channels:, :]).astype(jnp.bfloat16).astype(jnp.float32)
    vc_s[...] = fresh[:, channels:]
    same = (
        lax.broadcasted_iota(jnp.int32, (GROUP, GROUP), 0) // HEAD_DIM
        == lax.broadcasted_iota(jnp.int32, (GROUP, GROUP), 1) // HEAD_DIM
    )
    windows = own_ref.shape[0] * per_row
    for w in range(windows):
        for g in range(groups):
            kce[w * groups + g] = jnp.where(same, fresh[w : w + 1, g * GROUP : (g + 1) * GROUP], 0.0).astype(jnp.bfloat16)


def attend_kernel(x_ref, q_s, kv_s, hide_ref, kce, vc_s, wo, out_hbm, out_ref, mix_s, out_sems):
    rows, cols, channels = x_ref.shape
    groups = channels // GROUP
    heads_in = GROUP // HEAD_DIM
    wide_rows = rows + 2 * RADIUS
    queries, span = TILE * TILE, 2 * TILE * TILE
    qi = lax.broadcasted_iota(jnp.int32, (queries, 2 * span), 0)
    ki = lax.broadcasted_iota(jnp.int32, (queries, 2 * span), 1)
    row_step = (ki % span) // TILE - qi // TILE
    col_step = (ki // span) * TILE + ki % TILE - qi % TILE
    seen = (row_step >= 0) & (row_step <= 2 * RADIUS) & (col_step >= 0) & (col_step <= 2 * RADIUS)
    band = jnp.where(seen, 0.0, HIDDEN)
    group_head = lax.broadcasted_iota(jnp.int32, (1, GROUP), 1) // HEAD_DIM
    tall, broad = rows // TILE, cols // TILE
    per_side = PATCH_SIDE // TILE

    def tile(t, _):
        c, r = t // tall, t % tall
        q_at = pl.multiple_of(c * (rows * TILE) + r * queries, queries)
        k0 = pl.multiple_of(c * (wide_rows * TILE) + r * queries, queries)
        k1 = pl.multiple_of(k0 + wide_rows * TILE, queries)
        window = (r // per_side) * (broad // per_side) + c // per_side
        bias = band + hide_ref[t][0:1, :]
        for g in range(groups):
            q = q_s[g, pl.ds(q_at, queries), :]
            q32 = q.astype(jnp.float32)
            qq = jnp.concatenate(
                [jnp.where(group_head == h, q32, 0.0).astype(jnp.bfloat16) for h in range(heads_in)], axis=0
            )
            k = jnp.concatenate([kv_s[g, pl.ds(k0, span), :], kv_s[g, pl.ds(k1, span), :]], axis=0)
            v = jnp.concatenate(
                [kv_s[groups + g, pl.ds(k0, span), :], kv_s[groups + g, pl.ds(k1, span), :]], axis=0
            )
            p = jnp.exp(nt(qq, k).reshape(heads_in, queries, 2 * span) + bias[None])
            total = jnp.sum(p, axis=-1, keepdims=True)
            o = nn(p.reshape(heads_in * queries, 2 * span).astype(jnp.bfloat16), v)
            o = o.reshape(heads_in, queries, GROUP)
            kept, kept_total = o[0], total[0]
            for h in range(1, heads_in):
                kept = jnp.where(group_head == h, o[h], kept)
                kept_total = jnp.where(group_head == h, total[h], kept_total)
            pc = jnp.exp(nt(q, kce[window * groups + g]))
            v_new = vc_s[pl.ds(window, 1), g * GROUP : (g + 1) * GROUP]
            mixed = (kept + pc * v_new) / (kept_total + pc)
            mix_s[pl.ds(q_at, queries), g * GROUP : (g + 1) * GROUP] = mixed.astype(jnp.bfloat16)
        return 0

    lax.fori_loop(0, tall * broad, tile, 0)

    going = []
    for pair in range(broad // 2):
        both = slice(2 * pair * TILE, 2 * (pair + 1) * TILE)
        for g in range(groups):
            at = slice(g * GROUP, (g + 1) * GROUP)
            w = wo[at, :]
            parts = [
                nt(mix_s[b * rows * TILE : (b + 1) * rows * TILE, :], w).reshape(rows, TILE, GROUP)
                for b in (2 * pair, 2 * pair + 1)
            ]
            y = jnp.concatenate(parts, axis=1) + x_ref[:, both, at].astype(jnp.float32)
            out_ref[pair, :, :, at] = y.astype(jnp.bfloat16)
        copy = pltpu.make_async_copy(out_ref.at[pair], out_hbm.at[:, both, :], out_sems.at[pair])
        copy.start()
        going.append(copy)
    for copy in going:
        copy.wait()


def local(grid_elements, summary_vectors, triple_projection, final_projection, genuine_flags):
    rows, cols, channels = grid_elements.shape
    wide_rows, wide_cols = rows + 2 * RADIUS, cols + 2 * RADIUS
    own = summary_vectors.reshape(-1, channels)

    triple_t, final_t = triple_projection.T, final_projection.T
    vmem = pl.BlockSpec(memory_space=pltpu.VMEM)
    anywhere = pl.BlockSpec(memory_space=pl.ANY)
    scalars = pl.BlockSpec(memory_space=pltpu.SMEM)
    hbm = pl.BlockSpec(memory_space=pltpu.HBM)
    small = pltpu.CompilerParams(vmem_limit_bytes=16 * 1024 * 1024)
    row_strip = jax.ShapeDtypeStruct((RADIUS, cols, channels), jnp.bfloat16)
    col_strip = jax.ShapeDtypeStruct((wide_rows // 2, 2 * RADIUS, channels), jnp.bfloat16)

    row, col, img = lax.axis_size("row"), lax.axis_size("col"), lax.axis_size("img")
    row_at, col_at, img_at = lax.axis_index("row"), lax.axis_index("col"), lax.axis_index("img")
    row_bits = bits_of(row)
    far, rest = row_bits[0], row_bits[1:]
    relays = img if triple_t.shape[0] % (16 * (img + 1)) == 0 else 0
    piece_rows = triple_t.shape[0] // (relays + 1)
    starts = [(img_at - k) % img for k in range(relays)] + [jnp.int32(relays)]
    place = [row_at == 0, row_at == row - 1, col_at == 0, col_at == col - 1, row_at % 2 == 0, col_at % 2 == 0, row_at]
    place = jnp.stack([jnp.asarray(p).astype(jnp.int32) for p in place + [start * piece_rows for start in starts]])

    everyone = jnp.broadcast_to(own[None], (row * col, *own.shape))
    carriers = lax.all_to_all(everyone, ("row", "col"), 0, 0)
    place = after(place, carriers)

    mark, even_rows, odd_rows, mine, last = pl.pallas_call(
        functools.partial(edge_kernel, piece_rows),
        out_shape=(
            jax.ShapeDtypeStruct((rows, cols, LANES), jnp.bfloat16),
            row_strip,
            row_strip,
            jax.ShapeDtypeStruct((piece_rows, channels), jnp.bfloat16),
            jax.ShapeDtypeStruct((triple_t.shape[0] - relays * piece_rows, channels), jnp.bfloat16),
        ),
        in_specs=[scalars, hbm, hbm, hbm],
        out_specs=(vmem,) * 5,
        scratch_shapes=[
            pltpu.VMEM((rows, cols), jnp.int32),
            pltpu.VMEM(row_strip.shape, jnp.bfloat16),
            pltpu.VMEM(row_strip.shape, jnp.bfloat16),
            pltpu.VMEM((rows * cols, cols), jnp.bfloat16),
            pltpu.SemaphoreType.DMA((5,)),
        ],
        compiler_params=small,
        cost_estimate=pl.CostEstimate(flops=1_000_000, bytes_accessed=2_000_000, transcendentals=0),
        name="edge_rows",
    )(place, *(pltpu.with_memory_space_constraint(a, pltpu.HBM) for a in (genuine_flags, grid_elements, triple_t)))
    even_rows, odd_rows = pair_swapped(even_rows, odd_rows, "row")

    far_pieces = []
    if relays:
        first = swapped(after(mine, even_rows, odd_rows), "row", far)
    far_last = swapped(after(last, even_rows, odd_rows), "row", far)

    even_cols, odd_cols = pl.pallas_call(
        strip_kernel,
        out_shape=(col_strip, col_strip),
        in_specs=[scalars] + [vmem] * 4,
        out_specs=(vmem,) * 2,
        compiler_params=small,
        cost_estimate=pl.CostEstimate(flops=1_000_000, bytes_accessed=2_000_000, transcendentals=0),
        name="edge_columns",
    )(place, grid_elements, mark, even_rows, odd_rows)
    even_cols, odd_cols = pair_swapped(even_cols, odd_cols, "col")
    if relays:
        first = after(first, even_cols, odd_cols)
        others = [lax.ppermute(first, "img", [(i, (i + k) % img) for i in range(img)]) for k in range(1, relays)]
        far_pieces = [first] + others
    far_pieces.append(far_last)

    finals, triples, offsets = [final_t], [triple_t], [0]
    for bit in rest:
        finals = finals + [swapped(p, "row", bit) for p in finals]
        triples = triples + [swapped(p, "row", bit) for p in triples]
        offsets = offsets + [o ^ bit for o in offsets]
    tiles = (rows // TILE) * (cols // TILE)
    keys = 4 * TILE * TILE
    xq = pl.pallas_call(
        own_kernel,
        out_shape=jax.ShapeDtypeStruct((rows * cols, channels), jnp.bfloat16),
        in_specs=[vmem],
        out_specs=vmem,
        compiler_params=small,
        cost_estimate=pl.CostEstimate(flops=10_000_000, bytes_accessed=3_000_000, transcendentals=1000),
        name="own_norm",
    )(grid_elements)
    xkv, hide = pl.pallas_call(
        halo_kernel,
        out_shape=(
            jax.ShapeDtypeStruct((wide_rows * wide_cols, channels), jnp.bfloat16),
            jax.ShapeDtypeStruct((tiles, 8, keys), jnp.float32),
        ),
        in_specs=[scalars] + [vmem] * 6,
        out_specs=(vmem,) * 2,
        scratch_shapes=[
            *[pltpu.VMEM(shape.shape, jnp.float32) for shape in (row_strip, row_strip, col_strip, col_strip)],
            *[pltpu.VMEM((*shape.shape[:2], LANES), jnp.float32) for shape in (row_strip, row_strip, col_strip, col_strip)],
            pltpu.VMEM((wide_rows * wide_cols, LANES), jnp.bfloat16),
        ],
        compiler_params=pltpu.CompilerParams(vmem_limit_bytes=24 * 1024 * 1024),
        cost_estimate=pl.CostEstimate(flops=10_000_000, bytes_accessed=6_000_000, transcendentals=1000),
        name="halo_norm",
    )(place, xq, mark, even_rows, odd_rows, even_cols, odd_cols)

    far_final = swapped(after(final_t, xkv, far_last), "row", far)

    far_offsets = [far]
    far_pieces = [[after(piece, xkv)] for piece in far_pieces]
    for bit in rest:
        far_pieces = [same + [swapped(p, "row", bit) for p in same] for same in far_pieces]
        far_offsets = far_offsets + [o ^ bit for o in far_offsets]

    groups = channels // GROUP
    numbered = [(off, number) for number in range(len(far_pieces)) for off in far_offsets]
    sources = triples + [piece for same in far_pieces for piece in same]
    q, kv, wt = pl.pallas_call(
        functools.partial(project_kernel, offsets, numbered, triple_t.shape[0]),
        out_shape=(
            jax.ShapeDtypeStruct((groups, rows * cols, GROUP), jnp.bfloat16),
            jax.ShapeDtypeStruct((2 * groups, wide_rows * wide_cols, GROUP), jnp.bfloat16),
            jax.ShapeDtypeStruct((3 * channels, channels), jnp.bfloat16),
        ),
        in_specs=[scalars] + [anywhere] * len(sources) + [vmem] * 2,
        out_specs=(vmem,) * 3,
        scratch_shapes=[pltpu.SemaphoreType.DMA((len(sources),))],
        compiler_params=pltpu.CompilerParams(vmem_limit_bytes=VMEM_BYTES),
        cost_estimate=pl.CostEstimate(flops=5_000_000_000, bytes_accessed=14_000_000, transcendentals=0),
        name="project",
    )(place, *sources, xq, xkv)

    far_finals = [after(far_final, q)]
    for bit in rest:
        far_finals = far_finals + [swapped(p, "row", bit) for p in far_finals]
    finals, offsets = finals + far_finals, offsets + far_offsets
    carriers_here = own.shape[0] + -own.shape[0] % 8
    summary_result, wo, kce, vc = pl.pallas_call(
        functools.partial(carrier_kernel, offsets),
        out_shape=(
            jax.ShapeDtypeStruct(summary_vectors.shape, jnp.bfloat16),
            jax.ShapeDtypeStruct((channels, channels), jnp.bfloat16),
            jax.ShapeDtypeStruct((own.shape[0] * groups, GROUP, GROUP), jnp.bfloat16),
            jax.ShapeDtypeStruct((carriers_here, channels), jnp.float32),
        ),
        in_specs=[scalars] + [vmem] * 3 + [anywhere] * len(finals),
        out_specs=(vmem,) * 4,
        scratch_shapes=[
            pltpu.VMEM((carriers_here, channels), jnp.float32),
            pltpu.VMEM((row * col * own.shape[0], channels), jnp.float32),
            pltpu.SemaphoreType.DMA((len(finals),)),
        ],
        compiler_params=pltpu.CompilerParams(vmem_limit_bytes=VMEM_BYTES),
        cost_estimate=pl.CostEstimate(flops=500_000_000, bytes_accessed=5_000_000, transcendentals=10_000),
        name="carriers",
    )(place, wt, summary_vectors, carriers, *finals)

    out = pl.pallas_call(
        attend_kernel,
        out_shape=jax.ShapeDtypeStruct(grid_elements.shape, jnp.bfloat16),
        in_specs=[vmem] * 7,
        out_specs=anywhere,
        scratch_shapes=[
            pltpu.VMEM((cols // (2 * TILE), rows, 2 * TILE, channels), jnp.bfloat16),
            pltpu.VMEM((rows * cols, channels), jnp.bfloat16),
            pltpu.SemaphoreType.DMA((cols // (2 * TILE),)),
        ],
        compiler_params=pltpu.CompilerParams(vmem_limit_bytes=VMEM_BYTES),
        cost_estimate=pl.CostEstimate(flops=5_000_000_000, bytes_accessed=12_000_000, transcendentals=4_000_000),
        name="attend",
    )(grid_elements, q, kv, hide, kce, vc, wo)
    return (out, summary_result)


def solution(mesh):
    placed = (
        P(("img", "row"), "col", None),
        P(("img", "row"), "col", None),
        P(None, "row"),
        P(None, "row"),
        P(("img", "row"), "col"),
    )
    return jax.shard_map(
        local,
        mesh=mesh,
        in_specs=placed,
        out_specs=(P(("img", "row"), "col", None), P(("img", "row"), "col", None)),
        check_vma=False,
    )
```

```python
import functools

import jax
import jax.numpy as jnp
from jax import lax
from jax.experimental import pallas as pl
from jax.experimental.pallas import tpu as pltpu
from jax.sharding import PartitionSpec as P

HEAD_DIM = 64
PATCH_SIDE = 16
RADIUS = 4
TILE = 2 * RADIUS
LANES = 128
GROUP = 256
INVALID = 100.0
HIDDEN = -1e30
EVEN_ROW, EVEN_COL, ROW, STARTS = 4, 5, 6, 7
VMEM_BYTES = 24 * 1024 * 1024


def nt(a, b):
    return lax.dot_general(a, b, (((1,), (1,)), ((), ())), preferred_element_type=jnp.float32)


def nn(a, b):
    return lax.dot_general(a, b, (((1,), (0,)), ((), ())), preferred_element_type=jnp.float32)


def layer_normalise(lines):
    center = lines - jnp.mean(lines, axis=-1, keepdims=True)
    spread = jnp.mean(center * center, axis=-1, keepdims=True)
    return center * lax.rsqrt(spread + 1e-05)


def pair_swapped(even_block, odd_block, axis):
    count = lax.axis_size(axis)
    got = []
    for first, block in ((0, even_block), (1, odd_block)):
        pairs = [(i, i + 1) for i in range(first, count - 1, 2)]
        got.append(lax.ppermute(block, axis, pairs + [(b, a) for a, b in pairs]))
    return got


def swapped(block, axis, bit):
    count = lax.axis_size(axis)
    return lax.ppermute(block, axis, [(i, i ^ bit) for i in range(count)])


def after(block, *others):
    return lax.optimization_barrier((block, *others))[0]


def bits_of(count):
    bits, bit = [], count // 2
    while bit:
        bits.append(bit)
        bit //= 2
    return bits


def marked_lanes(lines, hidden):
    first = jnp.where(hidden, INVALID, lines[:, :, :LANES])
    return jnp.concatenate([first, lines[:, :, LANES:]], axis=2)


def edge_kernel(piece_rows, place_ref, flags_hbm, x_hbm, triple_hbm, mark_ref, *refs):
    even_rows_ref, odd_rows_ref, even_cols_ref, odd_cols_ref, mine_ref, last_ref, flags_ref, x_ref, spread, sems = refs
    rows, cols, channels = x_ref.shape
    middle = rows // 2
    own_start = pl.multiple_of(place_ref[STARTS], 16)
    last_start = triple_hbm.shape[0] - last_ref.shape[0]
    copies = [
        pltpu.make_async_copy(flags_hbm, flags_ref, sems.at[0]),
        pltpu.make_async_copy(x_hbm, x_ref, sems.at[1]),
        pltpu.make_async_copy(triple_hbm.at[pl.ds(own_start, piece_rows), :], mine_ref, sems.at[2]),
        pltpu.make_async_copy(triple_hbm.at[last_start:, :], last_ref, sems.at[3]),
    ]
    for copy in copies:
        copy.start()
    copies[0].wait()
    row_at = lax.broadcasted_iota(jnp.int32, (cols, cols), 0)
    diagonal = row_at == lax.broadcasted_iota(jnp.int32, (cols, cols), 1)
    for r in range(rows):
        hidden = jnp.where(flags_ref[r : r + 1, :] > 0, 0.0, INVALID)
        spread[r * cols : (r + 1) * cols, :] = jnp.where(diagonal, hidden, 0.0).astype(jnp.bfloat16)
    marks = nn(spread[...], jnp.ones((cols, LANES), jnp.bfloat16)).reshape(rows, cols, LANES)
    mark_ref[...] = marks.astype(jnp.bfloat16)
    copies[1].wait()
    first, last = [
        marked_lanes(x_ref[at].astype(jnp.float32), marks[at] > INVALID / 2)
        for at in (slice(0, RADIUS), slice(rows - RADIUS, rows))
    ]
    even = place_ref[EVEN_ROW] > 0
    even_rows_ref[...] = jnp.where(even, last, first).astype(jnp.bfloat16)
    odd_rows_ref[...] = jnp.where(even, first, last).astype(jnp.bfloat16)
    even = place_ref[EVEN_COL] > 0
    low = lax.broadcasted_iota(jnp.int32, (1, TILE, 1), 1) < RADIUS
    for lane in range(0, channels, LANES):
        lanes = slice(lane, lane + LANES)
        strips = []
        for columns in (slice(0, TILE), slice(cols - TILE, cols)):
            halves = []
            for part in (slice(0, middle), slice(middle, rows)):
                lines = x_ref[part, columns, lanes].astype(jnp.float32)
                halves.append(jnp.where(marks[part, columns, :] > INVALID / 2, INVALID, lines) if lane == 0 else lines)
            strips.append(halves)
        (first_up, first_down), (last_up, last_down) = strips
        first = jnp.where(low, first_up, jnp.roll(first_down, RADIUS, axis=1))
        last = jnp.where(low, jnp.roll(last_up, RADIUS, axis=1), last_down)
        even_cols_ref[:, :, lanes] = jnp.where(even, last, first).astype(jnp.bfloat16)
        odd_cols_ref[:, :, lanes] = jnp.where(even, first, last).astype(jnp.bfloat16)
    for copy in copies[2:]:
        copy.wait()


def corner_kernel(place_ref, even_rows_ref, odd_rows_ref, even_ref, odd_ref):
    cols = even_rows_ref.shape[1]
    low = lax.broadcasted_iota(jnp.int32, (1, TILE, 1), 1) < RADIUS
    flip = place_ref[EVEN_ROW] > 0
    even_rows, odd_rows = even_rows_ref[...].astype(jnp.float32), odd_rows_ref[...].astype(jnp.float32)
    top, bottom = jnp.where(flip, odd_rows, even_rows), jnp.where(flip, even_rows, odd_rows)
    first = jnp.where(low, top[:, :TILE, :], jnp.roll(bottom[:, :TILE, :], RADIUS, axis=1))
    last = jnp.where(low, jnp.roll(top[:, cols - TILE :, :], RADIUS, axis=1), bottom[:, cols - TILE :, :])
    even = place_ref[EVEN_COL] > 0
    even_ref[...] = jnp.where(even, last, first).astype(jnp.bfloat16)
    odd_ref[...] = jnp.where(even, first, last).astype(jnp.bfloat16)


def own_kernel(x_ref, xq_ref):
    rows, cols, _ = x_ref.shape
    step = 4

    def own(i, _):
        at = pl.multiple_of(i * step, step)
        y = layer_normalise(x_ref[pl.ds(at, step)].astype(jnp.float32))
        for c in range(cols // TILE):
            piece = y[:, c * TILE : (c + 1) * TILE, :].reshape(step * TILE, -1)
            to = pl.multiple_of(c * rows * TILE + at * TILE, step * TILE)
            xq_ref[pl.ds(to, step * TILE), :] = piece.astype(jnp.bfloat16)
        return 0

    lax.fori_loop(0, rows // step, own, 0)


def halo_kernel(place_ref, xq_ref, mark_ref, *refs):
    even_rows_ref, odd_rows_ref, even_cols_ref, odd_cols_ref, even_corners_ref, odd_corners_ref, xkv_ref, hide_ref = refs[:8]
    scratch = refs[8:]
    rows, cols, _ = mark_ref.shape
    wide_rows, wide_cols = rows + 2 * RADIUS, cols + 2 * RADIUS
    half = wide_rows // 2
    step = 2
    top_s, bottom_s, left_s, right_s, left_corner_s, right_corner_s = scratch[:6]
    top_ref, bottom_ref, left_ref, right_ref, left_corner_ref, right_corner_ref, flag_s = scratch[6:]
    for even, odd, low, high, low_flags, high_flags, parity, size in (
        (even_rows_ref, odd_rows_ref, top_s, bottom_s, top_ref, bottom_ref, EVEN_ROW, 2),
        (even_cols_ref, odd_cols_ref, left_s, right_s, left_ref, right_ref, EVEN_COL, 4),
        (even_corners_ref, odd_corners_ref, left_corner_s, right_corner_s, left_corner_ref, right_corner_ref, EVEN_COL, 4),
    ):
        flip = place_ref[parity] > 0
        for i in range(0, even.shape[0], size):
            a, b = even[i : i + size].astype(jnp.float32), odd[i : i + size].astype(jnp.float32)
            for lines, out, flags in ((jnp.where(flip, b, a), low, low_flags), (jnp.where(flip, a, b), high, high_flags)):
                out[i : i + size] = layer_normalise(lines)
                flags[i : i + size] = lines[:, :, :LANES]

    def lines_of(ref):
        return ref.astype(jnp.float32)

    def merge(at, blocks, left, right, to_ref):
        low = lax.broadcasted_iota(jnp.int32, (1, TILE, 1), 1) < RADIUS
        before = left
        for c in range(len(blocks) + 1):
            after = jnp.roll(blocks[c], RADIUS, axis=1) if c < len(blocks) else right
            to = c * wide_rows * TILE + at * TILE
            to = pl.multiple_of(to, step * TILE) if not isinstance(to, int) else to
            lines = jnp.where(low, before, after).reshape(step * TILE, -1)
            to_ref[pl.ds(to, step * TILE), :] = lines.astype(jnp.bfloat16)
            before = after

    def sides(at, upper, left_ref, right_ref):
        left, right = lines_of(left_ref[pl.ds(at, step)]), lines_of(right_ref[pl.ds(at, step)])
        if upper:
            return jnp.roll(left, RADIUS, axis=1), right
        return left, jnp.roll(right, RADIUS, axis=1)

    def hide_if(border, lines):
        return jnp.where(place_ref[border] > 0, INVALID, lines)

    def band(at, ref, ref_s, first, upper):
        cut = [slice(c * TILE, (c + 1) * TILE) for c in range(cols // TILE)]
        lines = ref_s[first : first + step]
        merge(at, [lines[:, k, :] for k in cut], *sides(first, upper, left_corner_s, right_corner_s), xkv_ref)
        marks = hide_if(int(upper), ref[first : first + step])
        left, right = sides(first, upper, left_corner_ref, right_corner_ref)
        left, right = hide_if(int(upper), hide_if(2, left)), hide_if(int(upper), hide_if(3, right))
        merge(at, [marks[:, k, :] for k in cut], left, right, flag_s)

    for i in range(0, RADIUS, step):
        band(i, top_ref, top_s, i, False)
        band(RADIUS + rows + i, bottom_ref, bottom_s, i, True)

    def middle(i, upper):
        at = pl.multiple_of(i * step, step)
        own = at - RADIUS
        blocks = []
        for c in range(cols // TILE):
            first = pl.multiple_of(c * rows * TILE + own * TILE, step * TILE)
            blocks.append(xq_ref[pl.ds(first, step * TILE), :].astype(jnp.float32).reshape(step, TILE, -1))
        strip_at = own - (rows // 2 if upper else 0)
        merge(at, blocks, *sides(strip_at, upper, left_s, right_s), xkv_ref)
        marks = mark_ref[pl.ds(own, step)].astype(jnp.float32)
        marks = [marks[:, c * TILE : (c + 1) * TILE, :] for c in range(cols // TILE)]
        left, right = sides(strip_at, upper, left_ref, right_ref)
        merge(at, marks, hide_if(2, left), hide_if(3, right), flag_s)
        return 0

    lax.fori_loop(RADIUS // step, half // step, lambda i, _: middle(i, False), 0)
    lax.fori_loop(half // step, (RADIUS + rows) // step, lambda i, _: middle(i, True), 0)

    first_lane = (lax.broadcasted_iota(jnp.int32, (8, LANES), 1) == 0).astype(jnp.bfloat16)
    spans = []
    for c in range(wide_cols // TILE):
        lines = flag_s[c * wide_rows * TILE : (c + 1) * wide_rows * TILE, :]
        spans.append(jnp.where(nt(first_lane, lines) > INVALID / 2, HIDDEN, 0.0))
    tall = rows // TILE
    for c in range(cols // TILE):
        for r in range(tall):
            at = slice(r * TILE * TILE, r * TILE * TILE + 2 * TILE * TILE)
            hide_ref[c * tall + r] = jnp.concatenate([spans[c][:, at], spans[c + 1][:, at]], axis=1)


def project_kernel(whole, pieces, triple_rows, place_ref, *refs):
    sources, refs = refs[: len(whole) + len(pieces)], refs[len(whole) + len(pieces) :]
    xq_ref, xkv_ref, q_s, kv_s, wt, sems = refs
    channels = wt.shape[1]
    groups = channels // GROUP
    factor = HEAD_DIM ** (-0.5)
    me = place_ref[ROW]
    copies = []
    for j, source in enumerate(sources):
        if j < len(whole):
            to = (me ^ whole[j]) * triple_rows
        else:
            off, start = pieces[j - len(whole)]
            to = (me ^ off) * triple_rows + place_ref[STARTS + start]
        to = pl.multiple_of(to, 16)
        copy = pltpu.make_async_copy(source, wt.at[pl.ds(to, source.shape[0]), :], sems.at[j])
        copy.start()
        copies.append(copy)
    for copy in copies:
        copy.wait()

    q_rows, kv_rows = xq_ref.shape[0], xkv_ref.shape[0]
    q_chunk, kv_chunk = q_rows // 2, kv_rows // 4

    def project_q(n, _):
        w = wt[pl.ds(pl.multiple_of(n * GROUP, GROUP), GROUP), :]
        for m in range(0, q_rows, q_chunk):
            q_s[n, m : m + q_chunk, :] = (nt(xq_ref[m : m + q_chunk, :], w) * factor).astype(jnp.bfloat16)
        return 0

    def project_kv(n, _):
        w = wt[pl.ds(pl.multiple_of(channels + n * GROUP, GROUP), GROUP), :]
        for m in range(0, kv_rows, kv_chunk):
            kv_s[n, m : m + kv_chunk, :] = nt(xkv_ref[m : m + kv_chunk, :], w).astype(jnp.bfloat16)
        return 0

    lax.fori_loop(0, groups, project_q, 0)
    lax.fori_loop(0, 2 * groups, project_kv, 0)


def carrier_kernel(offsets, carrier_parts, place_ref, wt, *refs):
    shards = len(offsets)
    parts, finals, refs = refs[:carrier_parts], refs[carrier_parts : carrier_parts + shards], refs[carrier_parts + shards :]
    summary_ref, wo, kce, vc_s, sems = refs
    per_row = summary_ref.shape[1]
    channels = wt.shape[1]
    groups = channels // GROUP
    heads = channels // HEAD_DIM
    factor = HEAD_DIM ** (-0.5)
    carriers_here = parts[0].shape[0]
    final_rows = wo.shape[0] // shards
    copies = []
    for j, off in enumerate(offsets):
        to = pl.multiple_of((place_ref[ROW] ^ off) * final_rows, 16)
        copy = pltpu.make_async_copy(finals[j], wo.at[pl.ds(to, final_rows), :], sems.at[j])
        copy.start()
        copies.append(copy)
    carriers = jnp.concatenate([part[...].astype(jnp.float32) for part in parts], axis=0)
    own = carriers[:carriers_here]
    carriers = layer_normalise(carriers).astype(jnp.bfloat16)
    own_norm = layer_normalise(own).astype(jnp.bfloat16)
    qc = (nt(own_norm, wt[:channels, :]) * factor).astype(jnp.bfloat16).astype(jnp.float32)
    kc = nt(carriers, wt[channels : 2 * channels, :]).astype(jnp.bfloat16)
    vc = nt(carriers, wt[2 * channels :, :]).astype(jnp.bfloat16)
    head_of = lax.broadcasted_iota(jnp.int32, (1, channels), 1) // HEAD_DIM
    stacked = jnp.concatenate([jnp.where(head_of == h, qc, 0.0) for h in range(heads)], axis=0)
    e = jnp.exp(nt(stacked.astype(jnp.bfloat16), kc))
    weights = (e / jnp.sum(e, axis=-1, keepdims=True)).astype(jnp.bfloat16)
    o = nn(weights, vc)
    mix = jnp.zeros((carriers_here, channels), jnp.float32)
    for h in range(heads):
        mix = jnp.where(head_of == h, o[h * carriers_here : (h + 1) * carriers_here, :], mix)
    for copy in copies:
        copy.wait()
    renewed = own + nt(mix.astype(jnp.bfloat16), wo[...])
    for i in range(summary_ref.shape[0]):
        summary_ref[i] = renewed[i * per_row : (i + 1) * per_row, :].astype(jnp.bfloat16)
    fresh = nt(layer_normalise(renewed).astype(jnp.bfloat16), wt[channels:, :]).astype(jnp.bfloat16).astype(jnp.float32)
    vc_s[...] = fresh[:, channels:]
    same = (
        lax.broadcasted_iota(jnp.int32, (GROUP, GROUP), 0) // HEAD_DIM
        == lax.broadcasted_iota(jnp.int32, (GROUP, GROUP), 1) // HEAD_DIM
    )
    windows = kce.shape[0] // groups
    for w in range(windows):
        for g in range(groups):
            kce[w * groups + g] = jnp.where(same, fresh[w : w + 1, g * GROUP : (g + 1) * GROUP], 0.0).astype(jnp.bfloat16)


def attend_kernel(x_ref, q_s, kv_s, hide_ref, kce, vc_s, wo, out_hbm, out_ref, mix_s, out_sems):
    rows, cols, channels = x_ref.shape
    groups = channels // GROUP
    heads_in = GROUP // HEAD_DIM
    wide_rows = rows + 2 * RADIUS
    queries, span = TILE * TILE, 2 * TILE * TILE
    qi = lax.broadcasted_iota(jnp.int32, (queries, 2 * span), 0)
    ki = lax.broadcasted_iota(jnp.int32, (queries, 2 * span), 1)
    row_step = (ki % span) // TILE - qi // TILE
    col_step = (ki // span) * TILE + ki % TILE - qi % TILE
    seen = (row_step >= 0) & (row_step <= 2 * RADIUS) & (col_step >= 0) & (col_step <= 2 * RADIUS)
    band = jnp.where(seen, 0.0, HIDDEN)
    group_head = lax.broadcasted_iota(jnp.int32, (1, GROUP), 1) // HEAD_DIM
    tall, broad = rows // TILE, cols // TILE
    per_side = PATCH_SIDE // TILE

    def tile(t, _):
        c, r = t // tall, t % tall
        q_at = pl.multiple_of(c * (rows * TILE) + r * queries, queries)
        k0 = pl.multiple_of(c * (wide_rows * TILE) + r * queries, queries)
        k1 = pl.multiple_of(k0 + wide_rows * TILE, queries)
        window = (r // per_side) * (broad // per_side) + c // per_side
        bias = band + hide_ref[t][0:1, :]
        for g in range(groups):
            q = q_s[g, pl.ds(q_at, queries), :]
            q32 = q.astype(jnp.float32)
            qq = jnp.concatenate(
                [jnp.where(group_head == h, q32, 0.0).astype(jnp.bfloat16) for h in range(heads_in)], axis=0
            )
            k = jnp.concatenate([kv_s[g, pl.ds(k0, span), :], kv_s[g, pl.ds(k1, span), :]], axis=0)
            v = jnp.concatenate(
                [kv_s[groups + g, pl.ds(k0, span), :], kv_s[groups + g, pl.ds(k1, span), :]], axis=0
            )
            p = jnp.exp(nt(qq, k).reshape(heads_in, queries, 2 * span) + bias[None])
            total = jnp.sum(p, axis=-1, keepdims=True)
            o = nn(p.reshape(heads_in * queries, 2 * span).astype(jnp.bfloat16), v)
            o = o.reshape(heads_in, queries, GROUP)
            kept, kept_total = o[0], total[0]
            for h in range(1, heads_in):
                kept = jnp.where(group_head == h, o[h], kept)
                kept_total = jnp.where(group_head == h, total[h], kept_total)
            pc = jnp.exp(nt(q, kce[window * groups + g]))
            v_new = vc_s[pl.ds(window, 1), g * GROUP : (g + 1) * GROUP]
            mixed = (kept + pc * v_new) / (kept_total + pc)
            mix_s[pl.ds(q_at, queries), g * GROUP : (g + 1) * GROUP] = mixed.astype(jnp.bfloat16)
        return 0

    lax.fori_loop(0, tall * broad, tile, 0)

    going = []
    for pair in range(broad // 2):
        both = slice(2 * pair * TILE, 2 * (pair + 1) * TILE)
        for g in range(groups):
            at = slice(g * GROUP, (g + 1) * GROUP)
            w = wo[at, :]
            parts = [
                nt(mix_s[b * rows * TILE : (b + 1) * rows * TILE, :], w).reshape(rows, TILE, GROUP)
                for b in (2 * pair, 2 * pair + 1)
            ]
            y = jnp.concatenate(parts, axis=1) + x_ref[:, both, at].astype(jnp.float32)
            out_ref[pair, :, :, at] = y.astype(jnp.bfloat16)
        copy = pltpu.make_async_copy(out_ref.at[pair], out_hbm.at[:, both, :], out_sems.at[pair])
        copy.start()
        going.append(copy)
    for copy in going:
        copy.wait()


def local(grid_elements, summary_vectors, triple_projection, final_projection, genuine_flags):
    rows, cols, channels = grid_elements.shape
    wide_rows, wide_cols = rows + 2 * RADIUS, cols + 2 * RADIUS
    own = summary_vectors.reshape(-1, channels)

    triple_t, final_t = triple_projection.T, final_projection.T
    vmem = pl.BlockSpec(memory_space=pltpu.VMEM)
    anywhere = pl.BlockSpec(memory_space=pl.ANY)
    scalars = pl.BlockSpec(memory_space=pltpu.SMEM)
    hbm = pl.BlockSpec(memory_space=pltpu.HBM)
    small = pltpu.CompilerParams(vmem_limit_bytes=16 * 1024 * 1024)
    row_strip = jax.ShapeDtypeStruct((RADIUS, cols, channels), jnp.bfloat16)
    col_strip = jax.ShapeDtypeStruct((rows // 2, TILE, channels), jnp.bfloat16)
    corner = jax.ShapeDtypeStruct((RADIUS, TILE, channels), jnp.bfloat16)

    row, col, img = lax.axis_size("row"), lax.axis_size("col"), lax.axis_size("img")
    row_at, col_at, img_at = lax.axis_index("row"), lax.axis_index("col"), lax.axis_index("img")
    row_bits = bits_of(row)
    far, rest = row_bits[0], row_bits[1:]
    relays = img if triple_t.shape[0] % (16 * (img + 1)) == 0 else 0
    piece_rows = triple_t.shape[0] // (relays + 1)
    starts = [(img_at - k) % img for k in range(relays)] + [jnp.int32(relays)]
    place = [row_at == 0, row_at == row - 1, col_at == 0, col_at == col - 1, row_at % 2 == 0, col_at % 2 == 0, row_at]
    place = jnp.stack([jnp.asarray(p).astype(jnp.int32) for p in place + [start * piece_rows for start in starts]])

    mark, even_rows, odd_rows, even_cols, odd_cols, mine, last = pl.pallas_call(
        functools.partial(edge_kernel, piece_rows),
        out_shape=(
            jax.ShapeDtypeStruct((rows, cols, LANES), jnp.bfloat16),
            row_strip,
            row_strip,
            col_strip,
            col_strip,
            jax.ShapeDtypeStruct((piece_rows, channels), jnp.bfloat16),
            jax.ShapeDtypeStruct((triple_t.shape[0] - relays * piece_rows, channels), jnp.bfloat16),
        ),
        in_specs=[scalars, hbm, hbm, hbm],
        out_specs=(vmem,) * 7,
        scratch_shapes=[
            pltpu.VMEM((rows, cols), jnp.int32),
            pltpu.VMEM(grid_elements.shape, jnp.bfloat16),
            pltpu.VMEM((rows * cols, cols), jnp.bfloat16),
            pltpu.SemaphoreType.DMA((4,)),
        ],
        compiler_params=small,
        cost_estimate=pl.CostEstimate(flops=1_000_000, bytes_accessed=2_000_000, transcendentals=0),
        name="edge_rows",
    )(place, *(pltpu.with_memory_space_constraint(a, pltpu.HBM) for a in (genuine_flags, grid_elements, triple_t)))
    even_rows, odd_rows = pair_swapped(even_rows, odd_rows, "row")
    even_cols, odd_cols = pair_swapped(even_cols, odd_cols, "col")

    got = swapped(own, "row", far)
    carriers = jnp.concatenate([own, got], axis=0)
    parts = [carriers]
    far_pieces = []
    if relays:
        first = swapped(after(mine, even_rows, odd_rows, got), "row", far)
    far_last = swapped(after(last, even_rows, odd_rows), "row", far)

    even_corners, odd_corners = pl.pallas_call(
        corner_kernel,
        out_shape=(corner, corner),
        in_specs=[scalars] + [vmem] * 2,
        out_specs=(vmem,) * 2,
        compiler_params=small,
        cost_estimate=pl.CostEstimate(flops=1_000_000, bytes_accessed=1_000_000, transcendentals=0),
        name="corners",
    )(place, even_rows, after(odd_rows, even_cols, odd_cols))
    even_corners, odd_corners = pair_swapped(even_corners, odd_corners, "col")
    if relays:
        first = after(first, even_cols, odd_cols)
        others = [lax.ppermute(first, "img", [(i, (i + k) % img) for i in range(img)]) for k in range(1, relays)]
        far_pieces = [first] + others
    far_pieces.append(far_last)

    finals, triples, offsets = [final_t], [triple_t], [0]
    for bit in rest:
        finals = finals + [swapped(p, "row", bit) for p in finals]
        triples = triples + [swapped(p, "row", bit) for p in triples]
        offsets = offsets + [o ^ bit for o in offsets]
    carriers = after(carriers, even_corners, odd_corners)
    for bit in bits_of(col):
        got = swapped(carriers, "col", bit)
        carriers = jnp.concatenate([carriers, got], axis=0)
        parts = parts + [got]
    tiles = (rows // TILE) * (cols // TILE)
    keys = 4 * TILE * TILE
    xq = pl.pallas_call(
        own_kernel,
        out_shape=jax.ShapeDtypeStruct((rows * cols, channels), jnp.bfloat16),
        in_specs=[vmem],
        out_specs=vmem,
        compiler_params=small,
        cost_estimate=pl.CostEstimate(flops=10_000_000, bytes_accessed=3_000_000, transcendentals=1000),
        name="own_norm",
    )(grid_elements)
    strips = [row_strip] * 2 + [col_strip] * 2 + [corner] * 2
    xkv, hide = pl.pallas_call(
        halo_kernel,
        out_shape=(
            jax.ShapeDtypeStruct((wide_rows * wide_cols, channels), jnp.bfloat16),
            jax.ShapeDtypeStruct((tiles, 8, keys), jnp.float32),
        ),
        in_specs=[scalars] + [vmem] * 8,
        out_specs=(vmem,) * 2,
        scratch_shapes=[
            *[pltpu.VMEM(shape.shape, jnp.float32) for shape in strips],
            *[pltpu.VMEM((*shape.shape[:2], LANES), jnp.float32) for shape in strips],
            pltpu.VMEM((wide_rows * wide_cols, LANES), jnp.bfloat16),
        ],
        compiler_params=pltpu.CompilerParams(vmem_limit_bytes=24 * 1024 * 1024),
        cost_estimate=pl.CostEstimate(flops=10_000_000, bytes_accessed=6_000_000, transcendentals=1000),
        name="halo_norm",
    )(place, xq, mark, even_rows, odd_rows, even_cols, odd_cols, even_corners, odd_corners)

    far_final = swapped(after(final_t, xkv, far_last), "row", far)

    far_offsets = [far]
    far_pieces = [[after(piece, xkv, carriers)] for piece in far_pieces]
    for bit in rest:
        got = swapped(carriers, "row", bit)
        carriers = jnp.concatenate([carriers, got], axis=0)
        parts = parts + [got]
    for bit in rest:
        far_pieces = [same + [swapped(p, "row", bit) for p in same] for same in far_pieces]
        far_offsets = far_offsets + [o ^ bit for o in far_offsets]

    groups = channels // GROUP
    numbered = [(off, number) for number in range(len(far_pieces)) for off in far_offsets]
    sources = triples + [piece for same in far_pieces for piece in same]
    q, kv, wt = pl.pallas_call(
        functools.partial(project_kernel, offsets, numbered, triple_t.shape[0]),
        out_shape=(
            jax.ShapeDtypeStruct((groups, rows * cols, GROUP), jnp.bfloat16),
            jax.ShapeDtypeStruct((2 * groups, wide_rows * wide_cols, GROUP), jnp.bfloat16),
            jax.ShapeDtypeStruct((3 * channels, channels), jnp.bfloat16),
        ),
        in_specs=[scalars] + [anywhere] * len(sources) + [vmem] * 2,
        out_specs=(vmem,) * 3,
        scratch_shapes=[pltpu.SemaphoreType.DMA((len(sources),))],
        compiler_params=pltpu.CompilerParams(vmem_limit_bytes=VMEM_BYTES),
        cost_estimate=pl.CostEstimate(flops=5_000_000_000, bytes_accessed=14_000_000, transcendentals=0),
        name="project",
    )(place, *sources, xq, xkv)

    far_finals = [after(far_final, q)]
    for bit in rest:
        far_finals = far_finals + [swapped(p, "row", bit) for p in far_finals]
    finals, offsets = finals + far_finals, offsets + far_offsets
    carriers_here = parts[0].shape[0]
    summary_result, wo, kce, vc = pl.pallas_call(
        functools.partial(carrier_kernel, offsets, len(parts)),
        out_shape=(
            jax.ShapeDtypeStruct(summary_vectors.shape, jnp.bfloat16),
            jax.ShapeDtypeStruct((channels, channels), jnp.bfloat16),
            jax.ShapeDtypeStruct((own.shape[0] * groups, GROUP, GROUP), jnp.bfloat16),
            jax.ShapeDtypeStruct((carriers_here, channels), jnp.float32),
        ),
        in_specs=[scalars] + [vmem] * (1 + len(parts)) + [anywhere] * len(finals),
        out_specs=(vmem,) * 4,
        scratch_shapes=[pltpu.SemaphoreType.DMA((len(finals),))],
        compiler_params=pltpu.CompilerParams(vmem_limit_bytes=VMEM_BYTES),
        cost_estimate=pl.CostEstimate(flops=500_000_000, bytes_accessed=5_000_000, transcendentals=10_000),
        name="carriers",
    )(place, wt, *parts, *finals)

    out = pl.pallas_call(
        attend_kernel,
        out_shape=jax.ShapeDtypeStruct(grid_elements.shape, jnp.bfloat16),
        in_specs=[vmem] * 7,
        out_specs=anywhere,
        scratch_shapes=[
            pltpu.VMEM((cols // (2 * TILE), rows, 2 * TILE, channels), jnp.bfloat16),
            pltpu.VMEM((rows * cols, channels), jnp.bfloat16),
            pltpu.SemaphoreType.DMA((cols // (2 * TILE),)),
        ],
        compiler_params=pltpu.CompilerParams(vmem_limit_bytes=VMEM_BYTES),
        cost_estimate=pl.CostEstimate(flops=5_000_000_000, bytes_accessed=12_000_000, transcendentals=4_000_000),
        name="attend",
    )(grid_elements, q, kv, hide, kce, vc, wo)
    return (out, summary_result)


def solution(mesh):
    placed = (
        P(("img", "row"), "col", None),
        P(("img", "row"), "col", None),
        P(None, "row"),
        P(None, "row"),
        P(("img", "row"), "col"),
    )
    return jax.shard_map(
        local,
        mesh=mesh,
        in_specs=placed,
        out_specs=(P(("img", "row"), "col", None), P(("img", "row"), "col", None)),
        check_vma=False,
    )
```

```python
import functools

import jax
import jax.numpy as jnp
from jax import lax
from jax.experimental import pallas as pl
from jax.experimental.pallas import tpu as pltpu
from jax.sharding import PartitionSpec as P

HEAD_DIM = 64
PATCH_SIDE = 16
RADIUS = 4
TILE = 2 * RADIUS
LANES = 128
GROUP = 256
INVALID = 100.0
HIDDEN = -1e30
EVEN_ROW, EVEN_COL, ROW, STARTS = 4, 5, 6, 7
VMEM_BYTES = 24 * 1024 * 1024


def nt(a, b):
    return lax.dot_general(a, b, (((1,), (1,)), ((), ())), preferred_element_type=jnp.float32)


def nn(a, b):
    return lax.dot_general(a, b, (((1,), (0,)), ((), ())), preferred_element_type=jnp.float32)


def layer_normalise(lines):
    center = lines - jnp.mean(lines, axis=-1, keepdims=True)
    spread = jnp.mean(center * center, axis=-1, keepdims=True)
    return center * lax.rsqrt(spread + 1e-05)


def pair_swapped(even_block, odd_block, axis):
    count = lax.axis_size(axis)
    got = []
    for first, block in ((0, even_block), (1, odd_block)):
        pairs = [(i, i + 1) for i in range(first, count - 1, 2)]
        got.append(lax.ppermute(block, axis, pairs + [(b, a) for a, b in pairs]))
    return got


def swapped(block, axis, bit):
    count = lax.axis_size(axis)
    return lax.ppermute(block, axis, [(i, i ^ bit) for i in range(count)])


def after(block, *others):
    return lax.optimization_barrier((block, *others))[0]


def bits_of(count):
    bits, bit = [], count // 2
    while bit:
        bits.append(bit)
        bit //= 2
    return bits


def marked_lanes(lines, hidden):
    first = jnp.where(hidden, INVALID, lines[:, :, :LANES])
    return jnp.concatenate([first, lines[:, :, LANES:]], axis=2)


def edge_kernel(piece_rows, place_ref, flags_hbm, x_hbm, triple_hbm, mark_ref, even_ref, odd_ref, mine_ref, last_ref, *scratch):
    flags_ref, first_s, last_s, spread, sems = scratch
    rows, cols = flags_ref.shape
    own_start = pl.multiple_of(place_ref[STARTS], 16)
    last_start = triple_hbm.shape[0] - last_ref.shape[0]
    copies = [
        pltpu.make_async_copy(x_hbm.at[0:RADIUS], first_s, sems.at[0]),
        pltpu.make_async_copy(x_hbm.at[rows - RADIUS : rows], last_s, sems.at[1]),
        pltpu.make_async_copy(triple_hbm.at[pl.ds(own_start, piece_rows), :], mine_ref, sems.at[2]),
        pltpu.make_async_copy(triple_hbm.at[last_start:, :], last_ref, sems.at[3]),
    ]
    flags_copy = pltpu.make_async_copy(flags_hbm, flags_ref, sems.at[4])
    flags_copy.start()
    for copy in copies:
        copy.start()
    flags_copy.wait()
    row_at = lax.broadcasted_iota(jnp.int32, (cols, cols), 0)
    diagonal = row_at == lax.broadcasted_iota(jnp.int32, (cols, cols), 1)
    for r in range(rows):
        hidden = jnp.where(flags_ref[r : r + 1, :] > 0, 0.0, INVALID)
        spread[r * cols : (r + 1) * cols, :] = jnp.where(diagonal, hidden, 0.0).astype(jnp.bfloat16)
    marks = nn(spread[...], jnp.ones((cols, LANES), jnp.bfloat16)).reshape(rows, cols, LANES)
    mark_ref[...] = marks.astype(jnp.bfloat16)
    for copy in copies:
        copy.wait()
    first, last = [
        marked_lanes(ref[...].astype(jnp.float32), marks[at] > INVALID / 2)
        for ref, at in ((first_s, slice(0, RADIUS)), (last_s, slice(rows - RADIUS, rows)))
    ]
    even = place_ref[EVEN_ROW] > 0
    even_ref[...] = jnp.where(even, last, first).astype(jnp.bfloat16)
    odd_ref[...] = jnp.where(even, first, last).astype(jnp.bfloat16)


def strip_kernel(place_ref, x_ref, mark_ref, even_rows_ref, odd_rows_ref, carriers_ref, even_ref, odd_ref, carriers_s):
    per_row = carriers_ref.shape[1]
    carriers_s[...] = jnp.zeros_like(carriers_s)
    for i in range(carriers_ref.shape[0]):
        carriers_s[i * per_row : (i + 1) * per_row, :] = carriers_ref[i].astype(jnp.float32)
    for i in range(carriers_s.shape[0] // TILE):
        even_ref[odd_ref.shape[0] + i] = carriers_s[i * TILE : (i + 1) * TILE, :].astype(jnp.bfloat16)
    rows, cols, channels = x_ref.shape
    middle = rows // 2
    low = lax.broadcasted_iota(jnp.int32, (1, TILE, 1), 1) < RADIUS
    even_row, even_col = place_ref[EVEN_ROW] > 0, place_ref[EVEN_COL] > 0
    for lane in range(0, channels, LANES):
        lanes = slice(lane, lane + LANES)
        strips = []
        for columns, last in ((slice(0, TILE), False), (slice(cols - TILE, cols), True)):

            def own(part):
                lines = x_ref[part, columns, lanes].astype(jnp.float32)
                if lane == 0:
                    lines = jnp.where(mark_ref[part, columns, :].astype(jnp.float32) > INVALID / 2, INVALID, lines)
                return lines

            even_rows = even_rows_ref[:, columns, lanes].astype(jnp.float32)
            odd_rows = odd_rows_ref[:, columns, lanes].astype(jnp.float32)
            top, bottom = jnp.where(even_row, odd_rows, even_rows), jnp.where(even_row, even_rows, odd_rows)
            upper = jnp.concatenate([top, own(slice(0, middle))], axis=0)
            lower = jnp.concatenate([own(slice(middle, rows)), bottom], axis=0)
            if last:
                upper = jnp.roll(upper, RADIUS, axis=1)
            else:
                lower = jnp.roll(lower, RADIUS, axis=1)
            strips.append(jnp.where(low, upper, lower))
        first, last = strips
        even_ref[: odd_ref.shape[0], :, lanes] = jnp.where(even_col, last, first).astype(jnp.bfloat16)
        odd_ref[:, :, lanes] = jnp.where(even_col, first, last).astype(jnp.bfloat16)


def own_kernel(x_ref, xq_ref):
    rows, cols, _ = x_ref.shape
    step = 4

    def own(i, _):
        at = pl.multiple_of(i * step, step)
        y = layer_normalise(x_ref[pl.ds(at, step)].astype(jnp.float32))
        for c in range(cols // TILE):
            piece = y[:, c * TILE : (c + 1) * TILE, :].reshape(step * TILE, -1)
            to = pl.multiple_of(c * rows * TILE + at * TILE, step * TILE)
            xq_ref[pl.ds(to, step * TILE), :] = piece.astype(jnp.bfloat16)
        return 0

    lax.fori_loop(0, rows // step, own, 0)


def halo_kernel(place_ref, xq_ref, mark_ref, even_rows_ref, odd_rows_ref, even_cols_ref, odd_cols_ref, xkv_ref, hide_ref, *scratch):
    rows, cols, _ = mark_ref.shape
    wide_rows, wide_cols = rows + 2 * RADIUS, cols + 2 * RADIUS
    half = wide_rows // 2
    step = 2
    top_s, bottom_s, left_s, right_s, top_ref, bottom_ref, left_ref, right_ref, flag_s = scratch
    for even, odd, low, high, low_flags, high_flags, parity, size in (
        (even_rows_ref, odd_rows_ref, top_s, bottom_s, top_ref, bottom_ref, EVEN_ROW, 2),
        (even_cols_ref, odd_cols_ref, left_s, right_s, left_ref, right_ref, EVEN_COL, 5),
    ):
        flip = place_ref[parity] > 0
        for i in range(0, odd.shape[0], size):
            a, b = even[i : i + size].astype(jnp.float32), odd[i : i + size].astype(jnp.float32)
            for lines, out, flags in ((jnp.where(flip, b, a), low, low_flags), (jnp.where(flip, a, b), high, high_flags)):
                out[i : i + size] = layer_normalise(lines)
                flags[i : i + size] = lines[:, :, :LANES]

    def lines_of(ref):
        return ref.astype(jnp.float32)

    def merge(at, blocks, left, right, to_ref):
        low = lax.broadcasted_iota(jnp.int32, (1, TILE, 1), 1) < RADIUS
        before = left
        for c in range(len(blocks) + 1):
            after = jnp.roll(blocks[c], RADIUS, axis=1) if c < len(blocks) else right
            to = c * wide_rows * TILE + at * TILE
            to = pl.multiple_of(to, step * TILE) if not isinstance(to, int) else to
            lines = jnp.where(low, before, after).reshape(step * TILE, -1)
            to_ref[pl.ds(to, step * TILE), :] = lines.astype(jnp.bfloat16)
            before = after

    def sides(at, upper, left_ref, right_ref, lanes):
        if upper:
            at = at - half
            left, right = jnp.roll(lines_of(left_ref[pl.ds(at, step), :, lanes]), RADIUS, axis=1), lines_of(
                right_ref[pl.ds(at, step), :, lanes]
            )
        else:
            left, right = lines_of(left_ref[pl.ds(at, step), :, lanes]), jnp.roll(
                lines_of(right_ref[pl.ds(at, step), :, lanes]), RADIUS, axis=1
            )
        return left, right

    every, few = slice(None), slice(0, LANES)

    def hide_if(border, lines):
        return jnp.where(place_ref[border] > 0, INVALID, lines)

    def mark_sides(at, upper):
        left, right = sides(at, upper, left_ref, right_ref, few)
        return hide_if(2, left), hide_if(3, right)

    def band(at, ref, ref_s, first, upper):
        cut = [slice(c * TILE, (c + 1) * TILE) for c in range(cols // TILE)]
        merge(at, [ref_s[first : first + step, k, :] for k in cut], *sides(at, upper, left_s, right_s, every), xkv_ref)
        marks = hide_if(int(upper), ref[first : first + step])
        beside = [hide_if(int(upper), side) for side in mark_sides(at, upper)]
        merge(at, [marks[:, k, :] for k in cut], *beside, flag_s)

    for i in range(0, RADIUS, step):
        band(i, top_ref, top_s, i, False)
        band(RADIUS + rows + i, bottom_ref, bottom_s, i, True)

    def middle(i, upper):
        at = pl.multiple_of(i * step, step)
        own = at - RADIUS
        blocks = []
        for c in range(cols // TILE):
            first = pl.multiple_of(c * rows * TILE + own * TILE, step * TILE)
            blocks.append(xq_ref[pl.ds(first, step * TILE), :].astype(jnp.float32).reshape(step, TILE, -1))
        merge(at, blocks, *sides(at, upper, left_s, right_s, every), xkv_ref)
        marks = mark_ref[pl.ds(own, step)].astype(jnp.float32)
        marks = [marks[:, c * TILE : (c + 1) * TILE, :] for c in range(cols // TILE)]
        merge(at, marks, *mark_sides(at, upper), flag_s)
        return 0

    lax.fori_loop(RADIUS // step, half // step, lambda i, _: middle(i, False), 0)
    lax.fori_loop(half // step, (RADIUS + rows) // step, lambda i, _: middle(i, True), 0)

    first_lane = (lax.broadcasted_iota(jnp.int32, (8, LANES), 1) == 0).astype(jnp.bfloat16)
    spans = []
    for c in range(wide_cols // TILE):
        lines = flag_s[c * wide_rows * TILE : (c + 1) * wide_rows * TILE, :]
        spans.append(jnp.where(nt(first_lane, lines) > INVALID / 2, HIDDEN, 0.0))
    tall = rows // TILE
    for c in range(cols // TILE):
        for r in range(tall):
            at = slice(r * TILE * TILE, r * TILE * TILE + 2 * TILE * TILE)
            hide_ref[c * tall + r] = jnp.concatenate([spans[c][:, at], spans[c + 1][:, at]], axis=1)


def project_kernel(whole, pieces, triple_rows, place_ref, *refs):
    sources, refs = refs[: len(whole) + len(pieces)], refs[len(whole) + len(pieces) :]
    xq_ref, xkv_ref, q_s, kv_s, wt, sems = refs
    channels = wt.shape[1]
    groups = channels // GROUP
    factor = HEAD_DIM ** (-0.5)
    me = place_ref[ROW]
    copies = []
    for j, source in enumerate(sources):
        if j < len(whole):
            to = (me ^ whole[j]) * triple_rows
        else:
            off, start = pieces[j - len(whole)]
            to = (me ^ off) * triple_rows + place_ref[STARTS + start]
        to = pl.multiple_of(to, 16)
        copy = pltpu.make_async_copy(source, wt.at[pl.ds(to, source.shape[0]), :], sems.at[j])
        copy.start()
        copies.append(copy)
    for copy in copies:
        copy.wait()

    q_rows, kv_rows = xq_ref.shape[0], xkv_ref.shape[0]
    q_chunk, kv_chunk = q_rows // 2, kv_rows // 4

    def project_q(n, _):
        w = wt[pl.ds(pl.multiple_of(n * GROUP, GROUP), GROUP), :]
        for m in range(0, q_rows, q_chunk):
            q_s[n, m : m + q_chunk, :] = (nt(xq_ref[m : m + q_chunk, :], w) * factor).astype(jnp.bfloat16)
        return 0

    def project_kv(n, _):
        w = wt[pl.ds(pl.multiple_of(channels + n * GROUP, GROUP), GROUP), :]
        for m in range(0, kv_rows, kv_chunk):
            kv_s[n, m : m + kv_chunk, :] = nt(xkv_ref[m : m + kv_chunk, :], w).astype(jnp.bfloat16)
        return 0

    lax.fori_loop(0, groups, project_q, 0)
    lax.fori_loop(0, 2 * groups, project_kv, 0)


def carrier_kernel(offsets, place_ref, wt, *refs):
    shards = len(offsets)
    finals, refs = refs[:shards], refs[shards:]
    summary_ref, wo, kce, vc_s, carriers_s, sems = refs
    per_row = summary_ref.shape[1]
    channels = wt.shape[1]
    groups = channels // GROUP
    heads = channels // HEAD_DIM
    factor = HEAD_DIM ** (-0.5)
    carriers_here = vc_s.shape[0]
    final_rows = wo.shape[0] // shards
    copies = []
    for j, off in enumerate(offsets):
        to = pl.multiple_of((place_ref[ROW] ^ off) * final_rows, 16)
        copy = pltpu.make_async_copy(finals[j].at[0:final_rows, :], wo.at[pl.ds(to, final_rows), :], sems.at[j])
        copy.start()
        copies.append(copy)
    coming = []
    sent = carriers_s.shape[0] // shards
    for j in range(shards):
        source = finals[j].at[final_rows : final_rows + sent, :]
        copy = pltpu.make_async_copy(source, carriers_s.at[j * sent : (j + 1) * sent, :], sems.at[shards + j])
        copy.start()
        coming.append(copy)
    for copy in coming:
        copy.wait()
    carriers = carriers_s[...].astype(jnp.float32)
    own = carriers[:carriers_here]
    carriers = layer_normalise(carriers).astype(jnp.bfloat16)
    own_norm = layer_normalise(own).astype(jnp.bfloat16)
    qc = (nt(own_norm, wt[:channels, :]) * factor).astype(jnp.bfloat16).astype(jnp.float32)
    kc = nt(carriers, wt[channels : 2 * channels, :]).astype(jnp.bfloat16)
    vc = nt(carriers, wt[2 * channels :, :]).astype(jnp.bfloat16)
    head_of = lax.broadcasted_iota(jnp.int32, (1, channels), 1) // HEAD_DIM
    stacked = jnp.concatenate([jnp.where(head_of == h, qc, 0.0) for h in range(heads)], axis=0)
    e = jnp.exp(nt(stacked.astype(jnp.bfloat16), kc))
    weights = (e / jnp.sum(e, axis=-1, keepdims=True)).astype(jnp.bfloat16)
    o = nn(weights, vc)
    mix = jnp.zeros((carriers_here, channels), jnp.float32)
    for h in range(heads):
        mix = jnp.where(head_of == h, o[h * carriers_here : (h + 1) * carriers_here, :], mix)
    for copy in copies:
        copy.wait()
    renewed = own + nt(mix.astype(jnp.bfloat16), wo[...])
    for i in range(summary_ref.shape[0]):
        summary_ref[i] = renewed[i * per_row : (i + 1) * per_row, :].astype(jnp.bfloat16)
    fresh = nt(layer_normalise(renewed).astype(jnp.bfloat16), wt[channels:, :]).astype(jnp.bfloat16).astype(jnp.float32)
    vc_s[...] = fresh[:, channels:]
    same = (
        lax.broadcasted_iota(jnp.int32, (GROUP, GROUP), 0) // HEAD_DIM
        == lax.broadcasted_iota(jnp.int32, (GROUP, GROUP), 1) // HEAD_DIM
    )
    windows = kce.shape[0] // groups
    for w in range(windows):
        for g in range(groups):
            kce[w * groups + g] = jnp.where(same, fresh[w : w + 1, g * GROUP : (g + 1) * GROUP], 0.0).astype(jnp.bfloat16)


def attend_kernel(x_ref, q_s, kv_s, hide_ref, kce, vc_s, wo, out_hbm, out_ref, mix_s, out_sems):
    rows, cols, channels = x_ref.shape
    groups = channels // GROUP
    heads_in = GROUP // HEAD_DIM
    wide_rows = rows + 2 * RADIUS
    queries, span = TILE * TILE, 2 * TILE * TILE
    qi = lax.broadcasted_iota(jnp.int32, (queries, 2 * span), 0)
    ki = lax.broadcasted_iota(jnp.int32, (queries, 2 * span), 1)
    row_step = (ki % span) // TILE - qi // TILE
    col_step = (ki // span) * TILE + ki % TILE - qi % TILE
    seen = (row_step >= 0) & (row_step <= 2 * RADIUS) & (col_step >= 0) & (col_step <= 2 * RADIUS)
    band = jnp.where(seen, 0.0, HIDDEN)
    group_head = lax.broadcasted_iota(jnp.int32, (1, GROUP), 1) // HEAD_DIM
    tall, broad = rows // TILE, cols // TILE
    per_side = PATCH_SIDE // TILE

    def tile(t, _):
        c, r = t // tall, t % tall
        q_at = pl.multiple_of(c * (rows * TILE) + r * queries, queries)
        k0 = pl.multiple_of(c * (wide_rows * TILE) + r * queries, queries)
        k1 = pl.multiple_of(k0 + wide_rows * TILE, queries)
        window = (r // per_side) * (broad // per_side) + c // per_side
        bias = band + hide_ref[t][0:1, :]
        for g in range(groups):
            q = q_s[g, pl.ds(q_at, queries), :]
            q32 = q.astype(jnp.float32)
            qq = jnp.concatenate(
                [jnp.where(group_head == h, q32, 0.0).astype(jnp.bfloat16) for h in range(heads_in)], axis=0
            )
            k = jnp.concatenate([kv_s[g, pl.ds(k0, span), :], kv_s[g, pl.ds(k1, span), :]], axis=0)
            v = jnp.concatenate(
                [kv_s[groups + g, pl.ds(k0, span), :], kv_s[groups + g, pl.ds(k1, span), :]], axis=0
            )
            p = jnp.exp(nt(qq, k).reshape(heads_in, queries, 2 * span) + bias[None])
            total = jnp.sum(p, axis=-1, keepdims=True)
            o = nn(p.reshape(heads_in * queries, 2 * span).astype(jnp.bfloat16), v)
            o = o.reshape(heads_in, queries, GROUP)
            kept, kept_total = o[0], total[0]
            for h in range(1, heads_in):
                kept = jnp.where(group_head == h, o[h], kept)
                kept_total = jnp.where(group_head == h, total[h], kept_total)
            pc = jnp.exp(nt(q, kce[window * groups + g]))
            v_new = vc_s[pl.ds(window, 1), g * GROUP : (g + 1) * GROUP]
            mixed = (kept + pc * v_new) / (kept_total + pc)
            mix_s[pl.ds(q_at, queries), g * GROUP : (g + 1) * GROUP] = mixed.astype(jnp.bfloat16)
        return 0

    lax.fori_loop(0, tall * broad, tile, 0)

    going = []
    for pair in range(broad // 2):
        both = slice(2 * pair * TILE, 2 * (pair + 1) * TILE)
        for g in range(groups):
            at = slice(g * GROUP, (g + 1) * GROUP)
            w = wo[at, :]
            parts = [
                nt(mix_s[b * rows * TILE : (b + 1) * rows * TILE, :], w).reshape(rows, TILE, GROUP)
                for b in (2 * pair, 2 * pair + 1)
            ]
            y = jnp.concatenate(parts, axis=1) + x_ref[:, both, at].astype(jnp.float32)
            out_ref[pair, :, :, at] = y.astype(jnp.bfloat16)
        copy = pltpu.make_async_copy(out_ref.at[pair], out_hbm.at[:, both, :], out_sems.at[pair])
        copy.start()
        going.append(copy)
    for copy in going:
        copy.wait()


def local(grid_elements, summary_vectors, triple_projection, final_projection, genuine_flags):
    rows, cols, channels = grid_elements.shape
    wide_rows, wide_cols = rows + 2 * RADIUS, cols + 2 * RADIUS
    own = summary_vectors.reshape(-1, channels)

    triple_t, final_t = triple_projection.T, final_projection.T
    vmem = pl.BlockSpec(memory_space=pltpu.VMEM)
    anywhere = pl.BlockSpec(memory_space=pl.ANY)
    scalars = pl.BlockSpec(memory_space=pltpu.SMEM)
    hbm = pl.BlockSpec(memory_space=pltpu.HBM)
    small = pltpu.CompilerParams(vmem_limit_bytes=16 * 1024 * 1024)
    row_strip = jax.ShapeDtypeStruct((RADIUS, cols, channels), jnp.bfloat16)
    col_strip = jax.ShapeDtypeStruct((wide_rows // 2, 2 * RADIUS, channels), jnp.bfloat16)

    row, col, img = lax.axis_size("row"), lax.axis_size("col"), lax.axis_size("img")
    row_at, col_at, img_at = lax.axis_index("row"), lax.axis_index("col"), lax.axis_index("img")
    row_bits = bits_of(row)
    far, rest = row_bits[0], row_bits[1:]
    relays = img if triple_t.shape[0] % (16 * (img + 1)) == 0 else 0
    piece_rows = triple_t.shape[0] // (relays + 1)
    starts = [(img_at - k) % img for k in range(relays)] + [jnp.int32(relays)]
    place = [row_at == 0, row_at == row - 1, col_at == 0, col_at == col - 1, row_at % 2 == 0, col_at % 2 == 0, row_at]
    place = jnp.stack([jnp.asarray(p).astype(jnp.int32) for p in place + [start * piece_rows for start in starts]])

    mark, even_rows, odd_rows, mine, last = pl.pallas_call(
        functools.partial(edge_kernel, piece_rows),
        out_shape=(
            jax.ShapeDtypeStruct((rows, cols, LANES), jnp.bfloat16),
            row_strip,
            row_strip,
            jax.ShapeDtypeStruct((piece_rows, channels), jnp.bfloat16),
            jax.ShapeDtypeStruct((triple_t.shape[0] - relays * piece_rows, channels), jnp.bfloat16),
        ),
        in_specs=[scalars, hbm, hbm, hbm],
        out_specs=(vmem,) * 5,
        scratch_shapes=[
            pltpu.VMEM((rows, cols), jnp.int32),
            pltpu.VMEM(row_strip.shape, jnp.bfloat16),
            pltpu.VMEM(row_strip.shape, jnp.bfloat16),
            pltpu.VMEM((rows * cols, cols), jnp.bfloat16),
            pltpu.SemaphoreType.DMA((5,)),
        ],
        compiler_params=small,
        cost_estimate=pl.CostEstimate(flops=1_000_000, bytes_accessed=2_000_000, transcendentals=0),
        name="edge_rows",
    )(place, *(pltpu.with_memory_space_constraint(a, pltpu.HBM) for a in (genuine_flags, grid_elements, triple_t)))
    even_rows, odd_rows = pair_swapped(even_rows, odd_rows, "row")

    far_pieces = []
    if relays:
        first = swapped(after(mine, even_rows, odd_rows), "row", far)
    far_last = swapped(after(last, even_rows, odd_rows), "row", far)

    carrier_tiles = -(-own.shape[0] // TILE)
    even_cols, odd_cols = pl.pallas_call(
        strip_kernel,
        out_shape=(jax.ShapeDtypeStruct((col_strip.shape[0] + carrier_tiles, *col_strip.shape[1:]), jnp.bfloat16), col_strip),
        in_specs=[scalars] + [vmem] * 5,
        out_specs=(vmem,) * 2,
        scratch_shapes=[pltpu.VMEM((carrier_tiles * TILE, channels), jnp.float32)],
        compiler_params=small,
        cost_estimate=pl.CostEstimate(flops=1_000_000, bytes_accessed=2_000_000, transcendentals=0),
        name="edge_columns",
    )(place, grid_elements, mark, even_rows, odd_rows, summary_vectors)
    even_cols, odd_cols = pair_swapped(even_cols, odd_cols, "col")
    carriers = even_cols[col_strip.shape[0] :].reshape(-1, channels)[: own.shape[0]]
    carriers = jnp.concatenate([own, carriers], axis=0)
    for bit in bits_of(col)[:-1]:
        carriers = jnp.concatenate([carriers, swapped(carriers, "col", bit)], axis=0)
    if relays:
        first = after(first, even_cols, odd_cols)
        others = [lax.ppermute(first, "img", [(i, (i + k) % img) for i in range(img)]) for k in range(1, relays)]
        far_pieces = [first] + others
    far_pieces.append(far_last)

    final_pack = jnp.concatenate([final_t, carriers], axis=0)
    finals, triples, offsets = [final_pack], [triple_t], [0]
    for bit in rest:
        finals = finals + [swapped(p, "row", bit) for p in finals]
        triples = triples + [swapped(p, "row", bit) for p in triples]
        offsets = offsets + [o ^ bit for o in offsets]
    tiles = (rows // TILE) * (cols // TILE)
    keys = 4 * TILE * TILE
    xq = pl.pallas_call(
        own_kernel,
        out_shape=jax.ShapeDtypeStruct((rows * cols, channels), jnp.bfloat16),
        in_specs=[vmem],
        out_specs=vmem,
        compiler_params=small,
        cost_estimate=pl.CostEstimate(flops=10_000_000, bytes_accessed=3_000_000, transcendentals=1000),
        name="own_norm",
    )(grid_elements)
    xkv, hide = pl.pallas_call(
        halo_kernel,
        out_shape=(
            jax.ShapeDtypeStruct((wide_rows * wide_cols, channels), jnp.bfloat16),
            jax.ShapeDtypeStruct((tiles, 8, keys), jnp.float32),
        ),
        in_specs=[scalars] + [vmem] * 6,
        out_specs=(vmem,) * 2,
        scratch_shapes=[
            *[pltpu.VMEM(shape.shape, jnp.float32) for shape in (row_strip, row_strip, col_strip, col_strip)],
            *[pltpu.VMEM((*shape.shape[:2], LANES), jnp.float32) for shape in (row_strip, row_strip, col_strip, col_strip)],
            pltpu.VMEM((wide_rows * wide_cols, LANES), jnp.bfloat16),
        ],
        compiler_params=pltpu.CompilerParams(vmem_limit_bytes=24 * 1024 * 1024),
        cost_estimate=pl.CostEstimate(flops=10_000_000, bytes_accessed=6_000_000, transcendentals=1000),
        name="halo_norm",
    )(place, xq, mark, even_rows, odd_rows, even_cols, odd_cols)

    far_final = swapped(after(final_pack, xkv, far_last), "row", far)

    far_offsets = [far]
    far_pieces = [[after(piece, xkv)] for piece in far_pieces]
    for bit in rest:
        far_pieces = [same + [swapped(p, "row", bit) for p in same] for same in far_pieces]
        far_offsets = far_offsets + [o ^ bit for o in far_offsets]

    groups = channels // GROUP
    numbered = [(off, number) for number in range(len(far_pieces)) for off in far_offsets]
    sources = triples + [piece for same in far_pieces for piece in same]
    q, kv, wt = pl.pallas_call(
        functools.partial(project_kernel, offsets, numbered, triple_t.shape[0]),
        out_shape=(
            jax.ShapeDtypeStruct((groups, rows * cols, GROUP), jnp.bfloat16),
            jax.ShapeDtypeStruct((2 * groups, wide_rows * wide_cols, GROUP), jnp.bfloat16),
            jax.ShapeDtypeStruct((3 * channels, channels), jnp.bfloat16),
        ),
        in_specs=[scalars] + [anywhere] * len(sources) + [vmem] * 2,
        out_specs=(vmem,) * 3,
        scratch_shapes=[pltpu.SemaphoreType.DMA((len(sources),))],
        compiler_params=pltpu.CompilerParams(vmem_limit_bytes=VMEM_BYTES),
        cost_estimate=pl.CostEstimate(flops=5_000_000_000, bytes_accessed=14_000_000, transcendentals=0),
        name="project",
    )(place, *sources, xq, xkv)

    far_finals = [after(far_final, q)]
    for bit in rest:
        far_finals = far_finals + [swapped(p, "row", bit) for p in far_finals]
    finals, offsets = finals + far_finals, offsets + far_offsets
    carriers_here = carrier_tiles * TILE
    summary_result, wo, kce, vc = pl.pallas_call(
        functools.partial(carrier_kernel, offsets),
        out_shape=(
            jax.ShapeDtypeStruct(summary_vectors.shape, jnp.bfloat16),
            jax.ShapeDtypeStruct((channels, channels), jnp.bfloat16),
            jax.ShapeDtypeStruct((own.shape[0] * groups, GROUP, GROUP), jnp.bfloat16),
            jax.ShapeDtypeStruct((carriers_here, channels), jnp.float32),
        ),
        in_specs=[scalars, vmem] + [anywhere] * len(finals),
        out_specs=(vmem,) * 4,
        scratch_shapes=[
            pltpu.VMEM((row * col * own.shape[0], channels), jnp.bfloat16),
            pltpu.SemaphoreType.DMA((2 * len(finals),)),
        ],
        compiler_params=pltpu.CompilerParams(vmem_limit_bytes=VMEM_BYTES),
        cost_estimate=pl.CostEstimate(flops=500_000_000, bytes_accessed=5_000_000, transcendentals=10_000),
        name="carriers",
    )(place, wt, *finals)

    out = pl.pallas_call(
        attend_kernel,
        out_shape=jax.ShapeDtypeStruct(grid_elements.shape, jnp.bfloat16),
        in_specs=[vmem] * 7,
        out_specs=anywhere,
        scratch_shapes=[
            pltpu.VMEM((cols // (2 * TILE), rows, 2 * TILE, channels), jnp.bfloat16),
            pltpu.VMEM((rows * cols, channels), jnp.bfloat16),
            pltpu.SemaphoreType.DMA((cols // (2 * TILE),)),
        ],
        compiler_params=pltpu.CompilerParams(vmem_limit_bytes=VMEM_BYTES),
        cost_estimate=pl.CostEstimate(flops=5_000_000_000, bytes_accessed=12_000_000, transcendentals=4_000_000),
        name="attend",
    )(grid_elements, q, kv, hide, kce, vc, wo)
    return (out, summary_result)


def solution(mesh):
    placed = (
        P(("img", "row"), "col", None),
        P(("img", "row"), "col", None),
        P(None, "row"),
        P(None, "row"),
        P(("img", "row"), "col"),
    )
    return jax.shard_map(
        local,
        mesh=mesh,
        in_specs=placed,
        out_specs=(P(("img", "row"), "col", None), P(("img", "row"), "col", None)),
        check_vma=False,
    )
```

```python
import functools

import jax
import jax.numpy as jnp
from jax import lax
from jax.experimental import pallas as pl
from jax.experimental.pallas import tpu as pltpu
from jax.sharding import PartitionSpec as P

HEAD_DIM = 64
PATCH_SIDE = 16
RADIUS = 4
TILE = 2 * RADIUS
LANES = 128
GROUP = 256
INVALID = 100.0
HIDDEN = -1e30
EVEN_ROW, EVEN_COL, ROW, STARTS = 4, 5, 6, 7
VMEM_BYTES = 24 * 1024 * 1024


def nt(a, b):
    return lax.dot_general(a, b, (((1,), (1,)), ((), ())), preferred_element_type=jnp.float32)


def nn(a, b):
    return lax.dot_general(a, b, (((1,), (0,)), ((), ())), preferred_element_type=jnp.float32)


def layer_normalise(lines):
    center = lines - jnp.mean(lines, axis=-1, keepdims=True)
    spread = jnp.mean(center * center, axis=-1, keepdims=True)
    return center * lax.rsqrt(spread + 1e-05)


def pair_swapped(even_block, odd_block, axis):
    count = lax.axis_size(axis)
    got = []
    for first, block in ((0, even_block), (1, odd_block)):
        pairs = [(i, i + 1) for i in range(first, count - 1, 2)]
        got.append(lax.ppermute(block, axis, pairs + [(b, a) for a, b in pairs]))
    return got


def swapped(block, axis, bit):
    count = lax.axis_size(axis)
    return lax.ppermute(block, axis, [(i, i ^ bit) for i in range(count)])


def after(block, *others):
    return lax.optimization_barrier((block, *others))[0]


def bits_of(count):
    bits, bit = [], count // 2
    while bit:
        bits.append(bit)
        bit //= 2
    return bits


def marked_lanes(lines, hidden):
    first = jnp.where(hidden, INVALID, lines[:, :, :LANES])
    return jnp.concatenate([first, lines[:, :, LANES:]], axis=2)


def edge_kernel(piece_rows, place_ref, flags_hbm, x_hbm, triple_hbm, mark_ref, even_ref, odd_ref, mine_ref, last_ref, *scratch):
    flags_ref, first_s, last_s, spread, sems = scratch
    rows, cols = flags_ref.shape
    own_start = pl.multiple_of(place_ref[STARTS], 16)
    last_start = triple_hbm.shape[0] - last_ref.shape[0]
    copies = [
        pltpu.make_async_copy(x_hbm.at[0:RADIUS], first_s, sems.at[0]),
        pltpu.make_async_copy(x_hbm.at[rows - RADIUS : rows], last_s, sems.at[1]),
        pltpu.make_async_copy(triple_hbm.at[pl.ds(own_start, piece_rows), :], mine_ref, sems.at[2]),
        pltpu.make_async_copy(triple_hbm.at[last_start:, :], last_ref, sems.at[3]),
    ]
    flags_copy = pltpu.make_async_copy(flags_hbm, flags_ref, sems.at[4])
    flags_copy.start()
    for copy in copies:
        copy.start()
    flags_copy.wait()
    row_at = lax.broadcasted_iota(jnp.int32, (cols, cols), 0)
    diagonal = row_at == lax.broadcasted_iota(jnp.int32, (cols, cols), 1)
    for r in range(rows):
        hidden = jnp.where(flags_ref[r : r + 1, :] > 0, 0.0, INVALID)
        spread[r * cols : (r + 1) * cols, :] = jnp.where(diagonal, hidden, 0.0).astype(jnp.bfloat16)
    marks = nn(spread[...], jnp.ones((cols, LANES), jnp.bfloat16)).reshape(rows, cols, LANES)
    mark_ref[...] = marks.astype(jnp.bfloat16)
    for copy in copies:
        copy.wait()
    first, last = [
        marked_lanes(ref[...].astype(jnp.float32), marks[at] > INVALID / 2)
        for ref, at in ((first_s, slice(0, RADIUS)), (last_s, slice(rows - RADIUS, rows)))
    ]
    even = place_ref[EVEN_ROW] > 0
    even_ref[...] = jnp.where(even, last, first).astype(jnp.bfloat16)
    odd_ref[...] = jnp.where(even, first, last).astype(jnp.bfloat16)


def strip_kernel(place_ref, x_ref, mark_ref, even_rows_ref, odd_rows_ref, carriers_ref, even_ref, odd_ref, carriers_s):
    per_row = carriers_ref.shape[1]
    carriers_s[...] = jnp.zeros_like(carriers_s)
    for i in range(carriers_ref.shape[0]):
        carriers_s[i * per_row : (i + 1) * per_row, :] = carriers_ref[i].astype(jnp.float32)
    for i in range(carriers_s.shape[0] // TILE):
        even_ref[odd_ref.shape[0] + i] = carriers_s[i * TILE : (i + 1) * TILE, :].astype(jnp.bfloat16)
    rows, cols, channels = x_ref.shape
    middle = rows // 2
    low = lax.broadcasted_iota(jnp.int32, (1, TILE, 1), 1) < RADIUS
    even_row, even_col = place_ref[EVEN_ROW] > 0, place_ref[EVEN_COL] > 0
    for lane in range(0, channels, LANES):
        lanes = slice(lane, lane + LANES)
        strips = []
        for columns, last in ((slice(0, TILE), False), (slice(cols - TILE, cols), True)):

            def own(part):
                lines = x_ref[part, columns, lanes].astype(jnp.float32)
                if lane == 0:
                    lines = jnp.where(mark_ref[part, columns, :].astype(jnp.float32) > INVALID / 2, INVALID, lines)
                return lines

            even_rows = even_rows_ref[:, columns, lanes].astype(jnp.float32)
            odd_rows = odd_rows_ref[:, columns, lanes].astype(jnp.float32)
            top, bottom = jnp.where(even_row, odd_rows, even_rows), jnp.where(even_row, even_rows, odd_rows)
            upper = jnp.concatenate([top, own(slice(0, middle))], axis=0)
            lower = jnp.concatenate([own(slice(middle, rows)), bottom], axis=0)
            if last:
                upper = jnp.roll(upper, RADIUS, axis=1)
            else:
                lower = jnp.roll(lower, RADIUS, axis=1)
            strips.append(jnp.where(low, upper, lower))
        first, last = strips
        even_ref[: odd_ref.shape[0], :, lanes] = jnp.where(even_col, last, first).astype(jnp.bfloat16)
        odd_ref[:, :, lanes] = jnp.where(even_col, first, last).astype(jnp.bfloat16)


def own_kernel(x_ref, xq_ref):
    rows, cols, _ = x_ref.shape
    step = 4

    def own(i, _):
        at = pl.multiple_of(i * step, step)
        y = layer_normalise(x_ref[pl.ds(at, step)].astype(jnp.float32))
        for c in range(cols // TILE):
            piece = y[:, c * TILE : (c + 1) * TILE, :].reshape(step * TILE, -1)
            to = pl.multiple_of(c * rows * TILE + at * TILE, step * TILE)
            xq_ref[pl.ds(to, step * TILE), :] = piece.astype(jnp.bfloat16)
        return 0

    lax.fori_loop(0, rows // step, own, 0)


def halo_kernel(place_ref, xq_ref, mark_ref, even_rows_ref, odd_rows_ref, even_cols_ref, odd_cols_ref, xkv_ref, hide_ref, *scratch):
    rows, cols, _ = mark_ref.shape
    wide_rows, wide_cols = rows + 2 * RADIUS, cols + 2 * RADIUS
    half = wide_rows // 2
    step = 2
    top_s, bottom_s, left_s, right_s, top_ref, bottom_ref, left_ref, right_ref, flag_s = scratch
    for even, odd, low, high, low_flags, high_flags, parity, size in (
        (even_rows_ref, odd_rows_ref, top_s, bottom_s, top_ref, bottom_ref, EVEN_ROW, 2),
        (even_cols_ref, odd_cols_ref, left_s, right_s, left_ref, right_ref, EVEN_COL, 5),
    ):
        flip = place_ref[parity] > 0
        for i in range(0, odd.shape[0], size):
            a, b = even[i : i + size].astype(jnp.float32), odd[i : i + size].astype(jnp.float32)
            for lines, out, flags in ((jnp.where(flip, b, a), low, low_flags), (jnp.where(flip, a, b), high, high_flags)):
                out[i : i + size] = layer_normalise(lines)
                flags[i : i + size] = lines[:, :, :LANES]

    def lines_of(ref):
        return ref.astype(jnp.float32)

    def merge(at, blocks, left, right, to_ref):
        low = lax.broadcasted_iota(jnp.int32, (1, TILE, 1), 1) < RADIUS
        before = left
        for c in range(len(blocks) + 1):
            after = jnp.roll(blocks[c], RADIUS, axis=1) if c < len(blocks) else right
            to = c * wide_rows * TILE + at * TILE
            to = pl.multiple_of(to, step * TILE) if not isinstance(to, int) else to
            lines = jnp.where(low, before, after).reshape(step * TILE, -1)
            to_ref[pl.ds(to, step * TILE), :] = lines.astype(jnp.bfloat16)
            before = after

    def sides(at, upper, left_ref, right_ref, lanes):
        if upper:
            at = at - half
            left, right = jnp.roll(lines_of(left_ref[pl.ds(at, step), :, lanes]), RADIUS, axis=1), lines_of(
                right_ref[pl.ds(at, step), :, lanes]
            )
        else:
            left, right = lines_of(left_ref[pl.ds(at, step), :, lanes]), jnp.roll(
                lines_of(right_ref[pl.ds(at, step), :, lanes]), RADIUS, axis=1
            )
        return left, right

    every, few = slice(None), slice(0, LANES)

    def hide_if(border, lines):
        return jnp.where(place_ref[border] > 0, INVALID, lines)

    def mark_sides(at, upper):
        left, right = sides(at, upper, left_ref, right_ref, few)
        return hide_if(2, left), hide_if(3, right)

    def band(at, ref, ref_s, first, upper):
        cut = [slice(c * TILE, (c + 1) * TILE) for c in range(cols // TILE)]
        merge(at, [ref_s[first : first + step, k, :] for k in cut], *sides(at, upper, left_s, right_s, every), xkv_ref)
        marks = hide_if(int(upper), ref[first : first + step])
        beside = [hide_if(int(upper), side) for side in mark_sides(at, upper)]
        merge(at, [marks[:, k, :] for k in cut], *beside, flag_s)

    for i in range(0, RADIUS, step):
        band(i, top_ref, top_s, i, False)
        band(RADIUS + rows + i, bottom_ref, bottom_s, i, True)

    def middle(i, upper):
        at = pl.multiple_of(i * step, step)
        own = at - RADIUS
        blocks = []
        for c in range(cols // TILE):
            first = pl.multiple_of(c * rows * TILE + own * TILE, step * TILE)
            blocks.append(xq_ref[pl.ds(first, step * TILE), :].astype(jnp.float32).reshape(step, TILE, -1))
        merge(at, blocks, *sides(at, upper, left_s, right_s, every), xkv_ref)
        marks = mark_ref[pl.ds(own, step)].astype(jnp.float32)
        marks = [marks[:, c * TILE : (c + 1) * TILE, :] for c in range(cols // TILE)]
        merge(at, marks, *mark_sides(at, upper), flag_s)
        return 0

    lax.fori_loop(RADIUS // step, half // step, lambda i, _: middle(i, False), 0)
    lax.fori_loop(half // step, (RADIUS + rows) // step, lambda i, _: middle(i, True), 0)

    first_lane = (lax.broadcasted_iota(jnp.int32, (8, LANES), 1) == 0).astype(jnp.bfloat16)
    spans = []
    for c in range(wide_cols // TILE):
        lines = flag_s[c * wide_rows * TILE : (c + 1) * wide_rows * TILE, :]
        spans.append(jnp.where(nt(first_lane, lines) > INVALID / 2, HIDDEN, 0.0))
    tall = rows // TILE
    for c in range(cols // TILE):
        for r in range(tall):
            at = slice(r * TILE * TILE, r * TILE * TILE + 2 * TILE * TILE)
            hide_ref[c * tall + r] = jnp.concatenate([spans[c][:, at], spans[c + 1][:, at]], axis=1)


def project_kernel(whole, pieces, triple_rows, place_ref, *refs):
    sources, refs = refs[: len(whole) + len(pieces)], refs[len(whole) + len(pieces) :]
    xq_ref, xkv_ref, q_s, kv_s, wt, sems = refs
    channels = wt.shape[1]
    groups = channels // GROUP
    factor = HEAD_DIM ** (-0.5)
    me = place_ref[ROW]
    copies = []
    for j, source in enumerate(sources):
        if j < len(whole):
            to = (me ^ whole[j]) * triple_rows
        else:
            off, start = pieces[j - len(whole)]
            to = (me ^ off) * triple_rows + place_ref[STARTS + start]
        to = pl.multiple_of(to, 16)
        copy = pltpu.make_async_copy(source, wt.at[pl.ds(to, source.shape[0]), :], sems.at[j])
        copy.start()
        copies.append(copy)
    for copy in copies:
        copy.wait()

    q_rows, kv_rows = xq_ref.shape[0], xkv_ref.shape[0]
    q_chunk, kv_chunk = q_rows // 2, kv_rows // 4

    def project_q(n, _):
        w = wt[pl.ds(pl.multiple_of(n * GROUP, GROUP), GROUP), :]
        for m in range(0, q_rows, q_chunk):
            q_s[n, m : m + q_chunk, :] = (nt(xq_ref[m : m + q_chunk, :], w) * factor).astype(jnp.bfloat16)
        return 0

    def project_kv(n, _):
        w = wt[pl.ds(pl.multiple_of(channels + n * GROUP, GROUP), GROUP), :]
        for m in range(0, kv_rows, kv_chunk):
            kv_s[n, m : m + kv_chunk, :] = nt(xkv_ref[m : m + kv_chunk, :], w).astype(jnp.bfloat16)
        return 0

    lax.fori_loop(0, groups, project_q, 0)
    lax.fori_loop(0, 2 * groups, project_kv, 0)


def carrier_kernel(offsets, place_ref, wt, *refs):
    shards = len(offsets)
    finals, refs = refs[:shards], refs[shards:]
    summary_ref, wo, kce, vc_s, carriers_s, sems = refs
    per_row = summary_ref.shape[1]
    channels = wt.shape[1]
    groups = channels // GROUP
    heads = channels // HEAD_DIM
    factor = HEAD_DIM ** (-0.5)
    carriers_here = vc_s.shape[0]
    final_rows = wo.shape[0] // shards
    copies = []
    for j, off in enumerate(offsets):
        to = pl.multiple_of((place_ref[ROW] ^ off) * final_rows, 16)
        copy = pltpu.make_async_copy(finals[j].at[0:final_rows, :], wo.at[pl.ds(to, final_rows), :], sems.at[j])
        copy.start()
        copies.append(copy)
    coming = []
    sent = carriers_s.shape[0] // shards
    for j in range(shards):
        source = finals[j].at[final_rows : final_rows + sent, :]
        copy = pltpu.make_async_copy(source, carriers_s.at[j * sent : (j + 1) * sent, :], sems.at[shards + j])
        copy.start()
        coming.append(copy)
    for copy in coming:
        copy.wait()
    carriers = carriers_s[...].astype(jnp.float32)
    own = carriers[:carriers_here]
    carriers = layer_normalise(carriers).astype(jnp.bfloat16)
    own_norm = layer_normalise(own).astype(jnp.bfloat16)
    qc = (nt(own_norm, wt[:channels, :]) * factor).astype(jnp.bfloat16).astype(jnp.float32)
    kc = nt(carriers, wt[channels : 2 * channels, :]).astype(jnp.bfloat16)
    vc = nt(carriers, wt[2 * channels :, :]).astype(jnp.bfloat16)
    head_of = lax.broadcasted_iota(jnp.int32, (1, channels), 1) // HEAD_DIM
    stacked = jnp.concatenate([jnp.where(head_of == h, qc, 0.0) for h in range(heads)], axis=0)
    e = jnp.exp(nt(stacked.astype(jnp.bfloat16), kc))
    weights = (e / jnp.sum(e, axis=-1, keepdims=True)).astype(jnp.bfloat16)
    o = nn(weights, vc)
    mix = jnp.zeros((carriers_here, channels), jnp.float32)
    for h in range(heads):
        mix = jnp.where(head_of == h, o[h * carriers_here : (h + 1) * carriers_here, :], mix)
    for copy in copies:
        copy.wait()
    renewed = own + nt(mix.astype(jnp.bfloat16), wo[...])
    for i in range(summary_ref.shape[0]):
        summary_ref[i] = renewed[i * per_row : (i + 1) * per_row, :].astype(jnp.bfloat16)
    fresh = nt(layer_normalise(renewed).astype(jnp.bfloat16), wt[channels:, :]).astype(jnp.bfloat16).astype(jnp.float32)
    vc_s[...] = fresh[:, channels:]
    same = (
        lax.broadcasted_iota(jnp.int32, (GROUP, GROUP), 0) // HEAD_DIM
        == lax.broadcasted_iota(jnp.int32, (GROUP, GROUP), 1) // HEAD_DIM
    )
    windows = kce.shape[0] // groups
    for w in range(windows):
        for g in range(groups):
            kce[w * groups + g] = jnp.where(same, fresh[w : w + 1, g * GROUP : (g + 1) * GROUP], 0.0).astype(jnp.bfloat16)


def attend_kernel(x_ref, q_s, kv_s, hide_ref, kce, vc_s, wo, out_hbm, out_ref, mix_s, out_sems):
    rows, cols, channels = x_ref.shape
    groups = channels // GROUP
    heads_in = GROUP // HEAD_DIM
    wide_rows = rows + 2 * RADIUS
    queries, span = TILE * TILE, 2 * TILE * TILE
    qi = lax.broadcasted_iota(jnp.int32, (queries, 2 * span), 0)
    ki = lax.broadcasted_iota(jnp.int32, (queries, 2 * span), 1)
    row_step = (ki % span) // TILE - qi // TILE
    col_step = (ki // span) * TILE + ki % TILE - qi % TILE
    seen = (row_step >= 0) & (row_step <= 2 * RADIUS) & (col_step >= 0) & (col_step <= 2 * RADIUS)
    band = jnp.where(seen, 0.0, HIDDEN)
    group_head = lax.broadcasted_iota(jnp.int32, (1, GROUP), 1) // HEAD_DIM
    tall, broad = rows // TILE, cols // TILE
    per_side = PATCH_SIDE // TILE

    def tile(t, _):
        c, r = t // tall, t % tall
        q_at = pl.multiple_of(c * (rows * TILE) + r * queries, queries)
        k0 = pl.multiple_of(c * (wide_rows * TILE) + r * queries, queries)
        k1 = pl.multiple_of(k0 + wide_rows * TILE, queries)
        window = (r // per_side) * (broad // per_side) + c // per_side
        bias = band + hide_ref[t][0:1, :]
        for g in range(groups):
            q = q_s[g, pl.ds(q_at, queries), :]
            q32 = q.astype(jnp.float32)
            qq = jnp.concatenate(
                [jnp.where(group_head == h, q32, 0.0).astype(jnp.bfloat16) for h in range(heads_in)], axis=0
            )
            k = jnp.concatenate([kv_s[g, pl.ds(k0, span), :], kv_s[g, pl.ds(k1, span), :]], axis=0)
            v = jnp.concatenate(
                [kv_s[groups + g, pl.ds(k0, span), :], kv_s[groups + g, pl.ds(k1, span), :]], axis=0
            )
            p = jnp.exp(nt(qq, k).reshape(heads_in, queries, 2 * span) + bias[None])
            total = jnp.sum(p, axis=-1, keepdims=True)
            o = nn(p.reshape(heads_in * queries, 2 * span).astype(jnp.bfloat16), v)
            o = o.reshape(heads_in, queries, GROUP)
            kept, kept_total = o[0], total[0]
            for h in range(1, heads_in):
                kept = jnp.where(group_head == h, o[h], kept)
                kept_total = jnp.where(group_head == h, total[h], kept_total)
            pc = jnp.exp(nt(q, kce[window * groups + g]))
            v_new = vc_s[pl.ds(window, 1), g * GROUP : (g + 1) * GROUP]
            mixed = (kept + pc * v_new) / (kept_total + pc)
            mix_s[pl.ds(q_at, queries), g * GROUP : (g + 1) * GROUP] = mixed.astype(jnp.bfloat16)
        return 0

    lax.fori_loop(0, tall * broad, tile, 0)

    going = []
    for pair in range(broad // 2):
        both = slice(2 * pair * TILE, 2 * (pair + 1) * TILE)
        for g in range(groups):
            at = slice(g * GROUP, (g + 1) * GROUP)
            w = wo[at, :]
            parts = [
                nt(mix_s[b * rows * TILE : (b + 1) * rows * TILE, :], w).reshape(rows, TILE, GROUP)
                for b in (2 * pair, 2 * pair + 1)
            ]
            y = jnp.concatenate(parts, axis=1) + x_ref[:, both, at].astype(jnp.float32)
            out_ref[pair, :, :, at] = y.astype(jnp.bfloat16)
        copy = pltpu.make_async_copy(out_ref.at[pair], out_hbm.at[:, both, :], out_sems.at[pair])
        copy.start()
        going.append(copy)
    for copy in going:
        copy.wait()


def local(grid_elements, summary_vectors, triple_projection, final_projection, genuine_flags):
    rows, cols, channels = grid_elements.shape
    wide_rows, wide_cols = rows + 2 * RADIUS, cols + 2 * RADIUS
    own = summary_vectors.reshape(-1, channels)

    triple_t, final_t = triple_projection.T, final_projection.T
    vmem = pl.BlockSpec(memory_space=pltpu.VMEM)
    anywhere = pl.BlockSpec(memory_space=pl.ANY)
    scalars = pl.BlockSpec(memory_space=pltpu.SMEM)
    hbm = pl.BlockSpec(memory_space=pltpu.HBM)
    small = pltpu.CompilerParams(vmem_limit_bytes=16 * 1024 * 1024)
    row_strip = jax.ShapeDtypeStruct((RADIUS, cols, channels), jnp.bfloat16)
    col_strip = jax.ShapeDtypeStruct((wide_rows // 2, 2 * RADIUS, channels), jnp.bfloat16)

    row, col, img = lax.axis_size("row"), lax.axis_size("col"), lax.axis_size("img")
    row_at, col_at, img_at = lax.axis_index("row"), lax.axis_index("col"), lax.axis_index("img")
    row_bits = bits_of(row)
    far, rest = row_bits[0], row_bits[1:]
    relays = img if triple_t.shape[0] % (16 * (img + 1)) == 0 else 0
    piece_rows = triple_t.shape[0] // (relays + 1)
    starts = [(img_at - k) % img for k in range(relays)] + [jnp.int32(relays)]
    place = [row_at == 0, row_at == row - 1, col_at == 0, col_at == col - 1, row_at % 2 == 0, col_at % 2 == 0, row_at]
    place = jnp.stack([jnp.asarray(p).astype(jnp.int32) for p in place + [start * piece_rows for start in starts]])

    mark, even_rows, odd_rows, mine, last = pl.pallas_call(
        functools.partial(edge_kernel, piece_rows),
        out_shape=(
            jax.ShapeDtypeStruct((rows, cols, LANES), jnp.bfloat16),
            row_strip,
            row_strip,
            jax.ShapeDtypeStruct((piece_rows, channels), jnp.bfloat16),
            jax.ShapeDtypeStruct((triple_t.shape[0] - relays * piece_rows, channels), jnp.bfloat16),
        ),
        in_specs=[scalars, hbm, hbm, hbm],
        out_specs=(vmem,) * 5,
        scratch_shapes=[
            pltpu.VMEM((rows, cols), jnp.int32),
            pltpu.VMEM(row_strip.shape, jnp.bfloat16),
            pltpu.VMEM(row_strip.shape, jnp.bfloat16),
            pltpu.VMEM((rows * cols, cols), jnp.bfloat16),
            pltpu.SemaphoreType.DMA((5,)),
        ],
        compiler_params=small,
        cost_estimate=pl.CostEstimate(flops=1_000_000, bytes_accessed=2_000_000, transcendentals=0),
        name="edge_rows",
    )(place, *(pltpu.with_memory_space_constraint(a, pltpu.HBM) for a in (genuine_flags, grid_elements, triple_t)))
    even_rows, odd_rows = pair_swapped(even_rows, odd_rows, "row")

    far_pieces = []
    if relays:
        first = swapped(mine, "row", far)
    far_last = swapped(after(last, even_rows, odd_rows), "row", far)

    carrier_tiles = -(-own.shape[0] // TILE)
    even_cols, odd_cols = pl.pallas_call(
        strip_kernel,
        out_shape=(jax.ShapeDtypeStruct((col_strip.shape[0] + carrier_tiles, *col_strip.shape[1:]), jnp.bfloat16), col_strip),
        in_specs=[scalars] + [vmem] * 5,
        out_specs=(vmem,) * 2,
        scratch_shapes=[pltpu.VMEM((carrier_tiles * TILE, channels), jnp.float32)],
        compiler_params=small,
        cost_estimate=pl.CostEstimate(flops=1_000_000, bytes_accessed=2_000_000, transcendentals=0),
        name="edge_columns",
    )(place, grid_elements, mark, even_rows, odd_rows, summary_vectors)
    even_cols, odd_cols = pair_swapped(even_cols, odd_cols, "col")
    carriers = even_cols[col_strip.shape[0] :].reshape(-1, channels)[: own.shape[0]]
    carriers = jnp.concatenate([own, carriers], axis=0)
    for bit in bits_of(col)[:-1]:
        got = swapped(carriers, "col", bit)
        carriers = jnp.concatenate([carriers, got], axis=0)
    if relays:
        first = after(first, even_cols, odd_cols)
        others = [lax.ppermute(first, "img", [(i, (i + k) % img) for i in range(img)]) for k in range(1, relays)]
        far_pieces = [first] + others
    far_pieces.append(far_last)

    final_pack = jnp.concatenate([final_t, carriers], axis=0)
    finals, triples, offsets = [final_pack], [triple_t], [0]
    for bit in rest:
        finals = finals + [swapped(p, "row", bit) for p in finals]
        triples = triples + [swapped(p, "row", bit) for p in triples]
        offsets = offsets + [o ^ bit for o in offsets]
    tiles = (rows // TILE) * (cols // TILE)
    keys = 4 * TILE * TILE
    xq = pl.pallas_call(
        own_kernel,
        out_shape=jax.ShapeDtypeStruct((rows * cols, channels), jnp.bfloat16),
        in_specs=[vmem],
        out_specs=vmem,
        compiler_params=small,
        cost_estimate=pl.CostEstimate(flops=10_000_000, bytes_accessed=3_000_000, transcendentals=1000),
        name="own_norm",
    )(grid_elements)
    xkv, hide = pl.pallas_call(
        halo_kernel,
        out_shape=(
            jax.ShapeDtypeStruct((wide_rows * wide_cols, channels), jnp.bfloat16),
            jax.ShapeDtypeStruct((tiles, 8, keys), jnp.float32),
        ),
        in_specs=[scalars] + [vmem] * 6,
        out_specs=(vmem,) * 2,
        scratch_shapes=[
            *[pltpu.VMEM(shape.shape, jnp.float32) for shape in (row_strip, row_strip, col_strip, col_strip)],
            *[pltpu.VMEM((*shape.shape[:2], LANES), jnp.float32) for shape in (row_strip, row_strip, col_strip, col_strip)],
            pltpu.VMEM((wide_rows * wide_cols, LANES), jnp.bfloat16),
        ],
        compiler_params=pltpu.CompilerParams(vmem_limit_bytes=24 * 1024 * 1024),
        cost_estimate=pl.CostEstimate(flops=10_000_000, bytes_accessed=6_000_000, transcendentals=1000),
        name="halo_norm",
    )(place, after(xq, got), mark, even_rows, odd_rows, even_cols, odd_cols)

    far_final = swapped(after(final_pack, far_last), "row", far)

    far_offsets = [far]
    far_pieces = [[after(piece, xkv)] for piece in far_pieces]
    for bit in rest:
        far_pieces = [same + [swapped(p, "row", bit) for p in same] for same in far_pieces]
        far_offsets = far_offsets + [o ^ bit for o in far_offsets]

    groups = channels // GROUP
    numbered = [(off, number) for number in range(len(far_pieces)) for off in far_offsets]
    sources = triples + [piece for same in far_pieces for piece in same]
    q, kv, wt = pl.pallas_call(
        functools.partial(project_kernel, offsets, numbered, triple_t.shape[0]),
        out_shape=(
            jax.ShapeDtypeStruct((groups, rows * cols, GROUP), jnp.bfloat16),
            jax.ShapeDtypeStruct((2 * groups, wide_rows * wide_cols, GROUP), jnp.bfloat16),
            jax.ShapeDtypeStruct((3 * channels, channels), jnp.bfloat16),
        ),
        in_specs=[scalars] + [anywhere] * len(sources) + [vmem] * 2,
        out_specs=(vmem,) * 3,
        scratch_shapes=[pltpu.SemaphoreType.DMA((len(sources),))],
        compiler_params=pltpu.CompilerParams(vmem_limit_bytes=VMEM_BYTES),
        cost_estimate=pl.CostEstimate(flops=5_000_000_000, bytes_accessed=14_000_000, transcendentals=0),
        name="project",
    )(place, *sources, xq, xkv)

    far_finals = [after(far_final, q)]
    for bit in rest:
        far_finals = far_finals + [swapped(p, "row", bit) for p in far_finals]
    finals, offsets = finals + far_finals, offsets + far_offsets
    carriers_here = carrier_tiles * TILE
    summary_result, wo, kce, vc = pl.pallas_call(
        functools.partial(carrier_kernel, offsets),
        out_shape=(
            jax.ShapeDtypeStruct(summary_vectors.shape, jnp.bfloat16),
            jax.ShapeDtypeStruct((channels, channels), jnp.bfloat16),
            jax.ShapeDtypeStruct((own.shape[0] * groups, GROUP, GROUP), jnp.bfloat16),
            jax.ShapeDtypeStruct((carriers_here, channels), jnp.float32),
        ),
        in_specs=[scalars, vmem] + [anywhere] * len(finals),
        out_specs=(vmem,) * 4,
        scratch_shapes=[
            pltpu.VMEM((row * col * own.shape[0], channels), jnp.bfloat16),
            pltpu.SemaphoreType.DMA((2 * len(finals),)),
        ],
        compiler_params=pltpu.CompilerParams(vmem_limit_bytes=VMEM_BYTES),
        cost_estimate=pl.CostEstimate(flops=500_000_000, bytes_accessed=5_000_000, transcendentals=10_000),
        name="carriers",
    )(place, wt, *finals)

    out = pl.pallas_call(
        attend_kernel,
        out_shape=jax.ShapeDtypeStruct(grid_elements.shape, jnp.bfloat16),
        in_specs=[vmem] * 7,
        out_specs=anywhere,
        scratch_shapes=[
            pltpu.VMEM((cols // (2 * TILE), rows, 2 * TILE, channels), jnp.bfloat16),
            pltpu.VMEM((rows * cols, channels), jnp.bfloat16),
            pltpu.SemaphoreType.DMA((cols // (2 * TILE),)),
        ],
        compiler_params=pltpu.CompilerParams(vmem_limit_bytes=VMEM_BYTES),
        cost_estimate=pl.CostEstimate(flops=5_000_000_000, bytes_accessed=12_000_000, transcendentals=4_000_000),
        name="attend",
    )(grid_elements, q, kv, hide, kce, vc, wo)
    return (out, summary_result)


def solution(mesh):
    placed = (
        P(("img", "row"), "col", None),
        P(("img", "row"), "col", None),
        P(None, "row"),
        P(None, "row"),
        P(("img", "row"), "col"),
    )
    return jax.shard_map(
        local,
        mesh=mesh,
        in_specs=placed,
        out_specs=(P(("img", "row"), "col", None), P(("img", "row"), "col", None)),
        check_vma=False,
    )
```

```python
import functools

import jax
import jax.numpy as jnp
from jax import lax
from jax.experimental import pallas as pl
from jax.experimental.pallas import tpu as pltpu
from jax.sharding import PartitionSpec as P

HEAD_DIM = 64
PATCH_SIDE = 16
RADIUS = 4
TILE = 2 * RADIUS
LANES = 128
GROUP = 256
INVALID = 100.0
HIDDEN = -1e30
LOG2_E = 1.4426950408889634
EVEN_ROW, EVEN_COL, ROW, STARTS = 4, 5, 6, 7
VMEM_BYTES = 26 * 1024 * 1024


def nt(a, b):
    return lax.dot_general(a, b, (((1,), (1,)), ((), ())), preferred_element_type=jnp.float32)


def nn(a, b):
    return lax.dot_general(a, b, (((1,), (0,)), ((), ())), preferred_element_type=jnp.float32)


def layer_normalise(lines):
    center = lines - jnp.mean(lines, axis=-1, keepdims=True)
    spread = jnp.mean(center * center, axis=-1, keepdims=True)
    return center * lax.rsqrt(spread + 1e-05)


def pair_swapped(even_block, odd_block, axis):
    count = lax.axis_size(axis)
    got = []
    for first, block in ((0, even_block), (1, odd_block)):
        pairs = [(i, i + 1) for i in range(first, count - 1, 2)]
        got.append(lax.ppermute(block, axis, pairs + [(b, a) for a, b in pairs]))
    return got


def swapped(block, axis, bit):
    count = lax.axis_size(axis)
    return lax.ppermute(block, axis, [(i, i ^ bit) for i in range(count)])


def after(block, *others):
    return lax.optimization_barrier((block, *others))[0]


def bits_of(count):
    bits, bit = [], count // 2
    while bit:
        bits.append(bit)
        bit //= 2
    return bits


def marked_lanes(lines, hidden):
    first = jnp.where(hidden, INVALID, lines[:, :, :LANES])
    return jnp.concatenate([first, lines[:, :, LANES:]], axis=2)


def edge_kernel(piece_rows, place_ref, flags_hbm, x_hbm, triple_hbm, mark_ref, even_ref, odd_ref, mine_ref, last_ref, *scratch):
    flags_ref, first_s, last_s, spread, sems = scratch
    rows, cols = flags_ref.shape
    own_start = pl.multiple_of(place_ref[STARTS], 16)
    last_start = triple_hbm.shape[0] - last_ref.shape[0]
    copies = [
        pltpu.make_async_copy(x_hbm.at[0:RADIUS], first_s, sems.at[0]),
        pltpu.make_async_copy(x_hbm.at[rows - RADIUS : rows], last_s, sems.at[1]),
        pltpu.make_async_copy(triple_hbm.at[pl.ds(own_start, piece_rows), :], mine_ref, sems.at[2]),
        pltpu.make_async_copy(triple_hbm.at[last_start:, :], last_ref, sems.at[3]),
    ]
    flags_copy = pltpu.make_async_copy(flags_hbm, flags_ref, sems.at[4])
    flags_copy.start()
    for copy in copies:
        copy.start()
    flags_copy.wait()
    row_at = lax.broadcasted_iota(jnp.int32, (cols, cols), 0)
    diagonal = row_at == lax.broadcasted_iota(jnp.int32, (cols, cols), 1)
    for r in range(rows):
        hidden = jnp.where(flags_ref[r : r + 1, :] > 0, 0.0, INVALID)
        spread[r * cols : (r + 1) * cols, :] = jnp.where(diagonal, hidden, 0.0).astype(jnp.bfloat16)
    marks = nn(spread[...], jnp.ones((cols, LANES), jnp.bfloat16)).reshape(rows, cols, LANES)
    mark_ref[...] = marks.astype(jnp.bfloat16)
    for copy in copies:
        copy.wait()
    first, last = [
        marked_lanes(ref[...].astype(jnp.float32), marks[at] > INVALID / 2)
        for ref, at in ((first_s, slice(0, RADIUS)), (last_s, slice(rows - RADIUS, rows)))
    ]
    even = place_ref[EVEN_ROW] > 0
    even_ref[...] = jnp.where(even, last, first).astype(jnp.bfloat16)
    odd_ref[...] = jnp.where(even, first, last).astype(jnp.bfloat16)


def strip_kernel(place_ref, x_ref, mark_ref, even_rows_ref, odd_rows_ref, carriers_ref, even_ref, odd_ref, carriers_s):
    per_row = carriers_ref.shape[1]
    carriers_s[...] = jnp.zeros_like(carriers_s)
    for i in range(carriers_ref.shape[0]):
        carriers_s[i * per_row : (i + 1) * per_row, :] = carriers_ref[i].astype(jnp.float32)
    for i in range(carriers_s.shape[0] // TILE):
        even_ref[odd_ref.shape[0] + i] = carriers_s[i * TILE : (i + 1) * TILE, :].astype(jnp.bfloat16)
    rows, cols, channels = x_ref.shape
    middle = rows // 2
    low = lax.broadcasted_iota(jnp.int32, (1, TILE, 1), 1) < RADIUS
    even_row, even_col = place_ref[EVEN_ROW] > 0, place_ref[EVEN_COL] > 0
    for lane in range(0, channels, LANES):
        lanes = slice(lane, lane + LANES)
        strips = []
        for columns, last in ((slice(0, TILE), False), (slice(cols - TILE, cols), True)):

            def own(part):
                lines = x_ref[part, columns, lanes].astype(jnp.float32)
                if lane == 0:
                    lines = jnp.where(mark_ref[part, columns, :].astype(jnp.float32) > INVALID / 2, INVALID, lines)
                return lines

            even_rows = even_rows_ref[:, columns, lanes].astype(jnp.float32)
            odd_rows = odd_rows_ref[:, columns, lanes].astype(jnp.float32)
            top, bottom = jnp.where(even_row, odd_rows, even_rows), jnp.where(even_row, even_rows, odd_rows)
            upper = jnp.concatenate([top, own(slice(0, middle))], axis=0)
            lower = jnp.concatenate([own(slice(middle, rows)), bottom], axis=0)
            if last:
                upper = jnp.roll(upper, RADIUS, axis=1)
            else:
                lower = jnp.roll(lower, RADIUS, axis=1)
            strips.append(jnp.where(low, upper, lower))
        first, last = strips
        even_ref[: odd_ref.shape[0], :, lanes] = jnp.where(even_col, last, first).astype(jnp.bfloat16)
        odd_ref[:, :, lanes] = jnp.where(even_col, first, last).astype(jnp.bfloat16)


def own_kernel(x_ref, xq_ref):
    rows, cols, _ = x_ref.shape
    step = 4

    def own(i, _):
        at = pl.multiple_of(i * step, step)
        y = layer_normalise(x_ref[pl.ds(at, step)].astype(jnp.float32))
        for c in range(cols // TILE):
            piece = y[:, c * TILE : (c + 1) * TILE, :].reshape(step * TILE, -1)
            to = pl.multiple_of(c * rows * TILE + at * TILE, step * TILE)
            xq_ref[pl.ds(to, step * TILE), :] = piece.astype(jnp.bfloat16)
        return 0

    lax.fori_loop(0, rows // step, own, 0)


def halo_kernel(place_ref, xq_ref, mark_ref, even_rows_ref, odd_rows_ref, even_cols_ref, odd_cols_ref, xkv_ref, hide_ref, *scratch):
    rows, cols, _ = mark_ref.shape
    wide_rows, wide_cols = rows + 2 * RADIUS, cols + 2 * RADIUS
    half = wide_rows // 2
    step = 2
    top_s, bottom_s, left_s, right_s, top_ref, bottom_ref, left_ref, right_ref, flag_s = scratch
    for even, odd, low, high, low_flags, high_flags, parity, size in (
        (even_rows_ref, odd_rows_ref, top_s, bottom_s, top_ref, bottom_ref, EVEN_ROW, 2),
        (even_cols_ref, odd_cols_ref, left_s, right_s, left_ref, right_ref, EVEN_COL, 5),
    ):
        flip = place_ref[parity] > 0
        for i in range(0, odd.shape[0], size):
            a, b = even[i : i + size].astype(jnp.float32), odd[i : i + size].astype(jnp.float32)
            for lines, out, flags in ((jnp.where(flip, b, a), low, low_flags), (jnp.where(flip, a, b), high, high_flags)):
                out[i : i + size] = layer_normalise(lines)
                flags[i : i + size] = lines[:, :, :LANES]

    def lines_of(ref):
        return ref.astype(jnp.float32)

    def merge(at, blocks, left, right, to_ref):
        low = lax.broadcasted_iota(jnp.int32, (1, TILE, 1), 1) < RADIUS
        before = left
        for c in range(len(blocks) + 1):
            after = jnp.roll(blocks[c], RADIUS, axis=1) if c < len(blocks) else right
            to = c * wide_rows * TILE + at * TILE
            to = pl.multiple_of(to, step * TILE) if not isinstance(to, int) else to
            lines = jnp.where(low, before, after).reshape(step * TILE, -1)
            to_ref[pl.ds(to, step * TILE), :] = lines.astype(jnp.bfloat16)
            before = after

    def sides(at, upper, left_ref, right_ref, lanes):
        if upper:
            at = at - half
            left, right = jnp.roll(lines_of(left_ref[pl.ds(at, step), :, lanes]), RADIUS, axis=1), lines_of(
                right_ref[pl.ds(at, step), :, lanes]
            )
        else:
            left, right = lines_of(left_ref[pl.ds(at, step), :, lanes]), jnp.roll(
                lines_of(right_ref[pl.ds(at, step), :, lanes]), RADIUS, axis=1
            )
        return left, right

    every, few = slice(None), slice(0, LANES)

    def hide_if(border, lines):
        return jnp.where(place_ref[border] > 0, INVALID, lines)

    def mark_sides(at, upper):
        left, right = sides(at, upper, left_ref, right_ref, few)
        return hide_if(2, left), hide_if(3, right)

    def band(at, ref, ref_s, first, upper):
        cut = [slice(c * TILE, (c + 1) * TILE) for c in range(cols // TILE)]
        merge(at, [ref_s[first : first + step, k, :] for k in cut], *sides(at, upper, left_s, right_s, every), xkv_ref)
        marks = hide_if(int(upper), ref[first : first + step])
        beside = [hide_if(int(upper), side) for side in mark_sides(at, upper)]
        merge(at, [marks[:, k, :] for k in cut], *beside, flag_s)

    for i in range(0, RADIUS, step):
        band(i, top_ref, top_s, i, False)
        band(RADIUS + rows + i, bottom_ref, bottom_s, i, True)

    def middle(i, upper):
        at = pl.multiple_of(i * step, step)
        own = at - RADIUS
        blocks = []
        for c in range(cols // TILE):
            first = pl.multiple_of(c * rows * TILE + own * TILE, step * TILE)
            blocks.append(xq_ref[pl.ds(first, step * TILE), :].astype(jnp.float32).reshape(step, TILE, -1))
        merge(at, blocks, *sides(at, upper, left_s, right_s, every), xkv_ref)
        marks = mark_ref[pl.ds(own, step)].astype(jnp.float32)
        marks = [marks[:, c * TILE : (c + 1) * TILE, :] for c in range(cols // TILE)]
        merge(at, marks, *mark_sides(at, upper), flag_s)
        return 0

    lax.fori_loop(RADIUS // step, half // step, lambda i, _: middle(i, False), 0)
    lax.fori_loop(half // step, (RADIUS + rows) // step, lambda i, _: middle(i, True), 0)

    first_lane = (lax.broadcasted_iota(jnp.int32, (8, LANES), 1) == 0).astype(jnp.bfloat16)
    spans = []
    for c in range(wide_cols // TILE):
        lines = flag_s[c * wide_rows * TILE : (c + 1) * wide_rows * TILE, :]
        spans.append(jnp.where(nt(first_lane, lines) > INVALID / 2, HIDDEN, 0.0))
    tall = rows // TILE
    for c in range(cols // TILE):
        for r in range(tall):
            at = slice(r * TILE * TILE, r * TILE * TILE + 2 * TILE * TILE)
            hide_ref[c * tall + r] = jnp.concatenate([spans[c][:, at], spans[c + 1][:, at]], axis=1)


def project_kernel(whole, pieces, triple_rows, place_ref, *refs):
    sources, refs = refs[: len(whole) + len(pieces)], refs[len(whole) + len(pieces) :]
    xq_ref, xkv_ref, q_s, k_s, v_s, wt, sems = refs
    channels = wt.shape[1]
    groups = channels // GROUP
    factor = HEAD_DIM ** (-0.5) * LOG2_E
    me = place_ref[ROW]
    copies = []
    for j, source in enumerate(sources):
        if j < len(whole):
            to = (me ^ whole[j]) * triple_rows
        else:
            off, start = pieces[j - len(whole)]
            to = (me ^ off) * triple_rows + place_ref[STARTS + start]
        to = pl.multiple_of(to, 16)
        copy = pltpu.make_async_copy(source, wt.at[pl.ds(to, source.shape[0]), :], sems.at[j])
        copy.start()
        copies.append(copy)
    for copy in copies:
        copy.wait()

    q_rows, kv_rows = xq_ref.shape[0], xkv_ref.shape[0]
    q_chunk, kv_chunk = q_rows // 2, kv_rows // 4

    def project_q(n, _):
        w = wt[pl.ds(pl.multiple_of(n * GROUP, GROUP), GROUP), :]
        for m in range(0, q_rows, q_chunk):
            q_s[n, m : m + q_chunk, :] = (nt(xq_ref[m : m + q_chunk, :], w) * factor).astype(jnp.bfloat16)
        return 0

    def project_k(n, _):
        w = wt[pl.ds(pl.multiple_of(channels + n * GROUP, GROUP), GROUP), :]
        for m in range(0, kv_rows, kv_chunk):
            k_s[n, m : m + kv_chunk, :] = nt(xkv_ref[m : m + kv_chunk, :], w).astype(jnp.bfloat16)
        return 0

    def project_v(n, _):
        w = wt[pl.ds(pl.multiple_of(2 * channels + n * GROUP, GROUP), GROUP), :]
        for m in range(0, kv_rows, kv_chunk):
            y = nt(xkv_ref[m : m + kv_chunk, :], w).astype(jnp.bfloat16)
            for j in range(GROUP // LANES):
                v_s[GROUP // LANES * n + j, m : m + kv_chunk, :LANES] = y[:, j * LANES : (j + 1) * LANES]
                v_s[GROUP // LANES * n + j, m : m + kv_chunk, LANES:] = jnp.ones((kv_chunk, LANES), jnp.bfloat16)
        return 0

    lax.fori_loop(0, groups, project_q, 0)
    lax.fori_loop(0, groups, project_k, 0)
    lax.fori_loop(0, groups, project_v, 0)


def carrier_kernel(offsets, place_ref, wt, *refs):
    shards = len(offsets)
    finals, refs = refs[:shards], refs[shards:]
    summary_ref, wo, kce, vc_s, carriers_s, sems = refs
    per_row = summary_ref.shape[1]
    channels = wt.shape[1]
    groups = channels // GROUP
    heads = channels // HEAD_DIM
    factor = HEAD_DIM ** (-0.5)
    carriers_here = vc_s.shape[0]
    final_rows = wo.shape[0] // shards
    copies = []
    for j, off in enumerate(offsets):
        to = pl.multiple_of((place_ref[ROW] ^ off) * final_rows, 16)
        copy = pltpu.make_async_copy(finals[j].at[0:final_rows, :], wo.at[pl.ds(to, final_rows), :], sems.at[j])
        copy.start()
        copies.append(copy)
    coming = []
    sent = carriers_s.shape[0] // shards
    for j in range(shards):
        source = finals[j].at[final_rows : final_rows + sent, :]
        copy = pltpu.make_async_copy(source, carriers_s.at[j * sent : (j + 1) * sent, :], sems.at[shards + j])
        copy.start()
        coming.append(copy)
    for copy in coming:
        copy.wait()
    carriers = carriers_s[...].astype(jnp.float32)
    own = carriers[:carriers_here]
    carriers = layer_normalise(carriers).astype(jnp.bfloat16)
    own_norm = layer_normalise(own).astype(jnp.bfloat16)
    qc = (nt(own_norm, wt[:channels, :]) * factor).astype(jnp.bfloat16).astype(jnp.float32)
    kc = nt(carriers, wt[channels : 2 * channels, :]).astype(jnp.bfloat16)
    vc = nt(carriers, wt[2 * channels :, :]).astype(jnp.bfloat16)
    head_of = lax.broadcasted_iota(jnp.int32, (1, channels), 1) // HEAD_DIM
    stacked = jnp.concatenate([jnp.where(head_of == h, qc, 0.0) for h in range(heads)], axis=0)
    e = jnp.exp(nt(stacked.astype(jnp.bfloat16), kc))
    weights = (e / jnp.sum(e, axis=-1, keepdims=True)).astype(jnp.bfloat16)
    o = nn(weights, vc)
    mix = jnp.zeros((carriers_here, channels), jnp.float32)
    for h in range(heads):
        mix = jnp.where(head_of == h, o[h * carriers_here : (h + 1) * carriers_here, :], mix)
    for copy in copies:
        copy.wait()
    renewed = own + nt(mix.astype(jnp.bfloat16), wo[...])
    for i in range(summary_ref.shape[0]):
        summary_ref[i] = renewed[i * per_row : (i + 1) * per_row, :].astype(jnp.bfloat16)
    fresh = nt(layer_normalise(renewed).astype(jnp.bfloat16), wt[channels:, :]).astype(jnp.bfloat16).astype(jnp.float32)
    vc_s[...] = fresh[:, channels:]
    same = (
        lax.broadcasted_iota(jnp.int32, (GROUP, GROUP), 0) // HEAD_DIM
        == lax.broadcasted_iota(jnp.int32, (GROUP, GROUP), 1) // HEAD_DIM
    )
    windows = kce.shape[0] // groups
    for w in range(windows):
        for g in range(groups):
            kce[w * groups + g] = jnp.where(same, fresh[w : w + 1, g * GROUP : (g + 1) * GROUP], 0.0).astype(jnp.bfloat16)


def attend_kernel(x_ref, q_s, k_s, v_s, hide_ref, kce, vc_s, wo, out_hbm, out_ref, mix_s, out_sems):
    rows, cols, channels = x_ref.shape
    groups = channels // GROUP
    heads_in = GROUP // HEAD_DIM
    wide_rows = rows + 2 * RADIUS
    queries, span = TILE * TILE, 2 * TILE * TILE
    qi = lax.broadcasted_iota(jnp.int32, (queries, 2 * span), 0)
    ki = lax.broadcasted_iota(jnp.int32, (queries, 2 * span), 1)
    row_step = (ki % span) // TILE - qi // TILE
    col_step = (ki // span) * TILE + ki % TILE - qi % TILE
    seen = (row_step >= 0) & (row_step <= 2 * RADIUS) & (col_step >= 0) & (col_step <= 2 * RADIUS)
    band = jnp.where(seen, 0.0, HIDDEN)
    group_head = lax.broadcasted_iota(jnp.int32, (1, GROUP), 1) // HEAD_DIM
    only = [jnp.where(group_head == h, 1.0, 0.0).astype(jnp.bfloat16) for h in range(heads_in)]
    pair_head = lax.broadcasted_iota(jnp.int32, (1, LANES), 1) // HEAD_DIM
    pairs, in_pair = GROUP // LANES, LANES // HEAD_DIM
    tall, broad = rows // TILE, cols // TILE
    per_side = PATCH_SIDE // TILE

    def tile(t, _):
        c, r = t // tall, t % tall
        q_at = pl.multiple_of(c * (rows * TILE) + r * queries, queries)
        k0 = pl.multiple_of(c * (wide_rows * TILE) + r * queries, queries)
        k1 = pl.multiple_of(k0 + wide_rows * TILE, queries)
        window = (r // per_side) * (broad // per_side) + c // per_side
        bias = band + hide_ref[t][0:1, :]
        for g in range(groups):
            q = q_s[g, pl.ds(q_at, queries), :]
            qq = jnp.concatenate([q * mask for mask in only], axis=0)
            k = jnp.concatenate([k_s[g, pl.ds(k0, span), :], k_s[g, pl.ds(k1, span), :]], axis=0)
            p = jnp.exp2(nt(qq, k).reshape(heads_in, queries, 2 * span) + bias[None])
            p = p.reshape(heads_in * queries, 2 * span).astype(jnp.bfloat16)
            pc = jnp.exp2(nt(q, kce[window * groups + g]))
            v_new = vc_s[pl.ds(window, 1), g * GROUP : (g + 1) * GROUP]
            for j in range(pairs):
                v = jnp.concatenate(
                    [v_s[pairs * g + j, pl.ds(k0, span), :], v_s[pairs * g + j, pl.ds(k1, span), :]], axis=0
                )
                o = nn(p[j * in_pair * queries : (j + 1) * in_pair * queries, :], v)
                kept = o[:queries]
                for h in range(1, in_pair):
                    mine = o[h * queries : (h + 1) * queries]
                    kept = jnp.where(jnp.concatenate([pair_head] * 2, axis=1) == h, mine, kept)
                new = pc[:, j * LANES : (j + 1) * LANES]
                at = slice(g * GROUP + j * LANES, g * GROUP + (j + 1) * LANES)
                mixed = (kept[:, :LANES] + new * v_new[:, j * LANES : (j + 1) * LANES]) / (kept[:, LANES:] + new)
                mix_s[pl.ds(q_at, queries), at] = mixed.astype(jnp.bfloat16)
        return 0

    lax.fori_loop(0, tall * broad, tile, 0, unroll=2)

    going = []
    for pair in range(broad // 2):
        both = slice(2 * pair * TILE, 2 * (pair + 1) * TILE)
        for g in range(groups):
            at = slice(g * GROUP, (g + 1) * GROUP)
            w = wo[at, :]
            parts = [
                nt(mix_s[b * rows * TILE : (b + 1) * rows * TILE, :], w).reshape(rows, TILE, GROUP)
                for b in (2 * pair, 2 * pair + 1)
            ]
            y = jnp.concatenate(parts, axis=1) + x_ref[:, both, at].astype(jnp.float32)
            out_ref[pair, :, :, at] = y.astype(jnp.bfloat16)
        copy = pltpu.make_async_copy(out_ref.at[pair], out_hbm.at[:, both, :], out_sems.at[pair])
        copy.start()
        going.append(copy)
    for copy in going:
        copy.wait()


def local(grid_elements, summary_vectors, triple_projection, final_projection, genuine_flags):
    rows, cols, channels = grid_elements.shape
    wide_rows, wide_cols = rows + 2 * RADIUS, cols + 2 * RADIUS
    own = summary_vectors.reshape(-1, channels)

    triple_t, final_t = triple_projection.T, final_projection.T
    vmem = pl.BlockSpec(memory_space=pltpu.VMEM)
    anywhere = pl.BlockSpec(memory_space=pl.ANY)
    scalars = pl.BlockSpec(memory_space=pltpu.SMEM)
    hbm = pl.BlockSpec(memory_space=pltpu.HBM)
    small = pltpu.CompilerParams(vmem_limit_bytes=16 * 1024 * 1024)
    row_strip = jax.ShapeDtypeStruct((RADIUS, cols, channels), jnp.bfloat16)
    col_strip = jax.ShapeDtypeStruct((wide_rows // 2, 2 * RADIUS, channels), jnp.bfloat16)

    row, col, img = lax.axis_size("row"), lax.axis_size("col"), lax.axis_size("img")
    row_at, col_at, img_at = lax.axis_index("row"), lax.axis_index("col"), lax.axis_index("img")
    row_bits = bits_of(row)
    far, rest = row_bits[0], row_bits[1:]
    relays = img if triple_t.shape[0] % (16 * (img + 1)) == 0 else 0
    piece_rows = triple_t.shape[0] // (relays + 1)
    starts = [(img_at - k) % img for k in range(relays)] + [jnp.int32(relays)]
    place = [row_at == 0, row_at == row - 1, col_at == 0, col_at == col - 1, row_at % 2 == 0, col_at % 2 == 0, row_at]
    place = jnp.stack([jnp.asarray(p).astype(jnp.int32) for p in place + [start * piece_rows for start in starts]])

    mark, even_rows, odd_rows, mine, last = pl.pallas_call(
        functools.partial(edge_kernel, piece_rows),
        out_shape=(
            jax.ShapeDtypeStruct((rows, cols, LANES), jnp.bfloat16),
            row_strip,
            row_strip,
            jax.ShapeDtypeStruct((piece_rows, channels), jnp.bfloat16),
            jax.ShapeDtypeStruct((triple_t.shape[0] - relays * piece_rows, channels), jnp.bfloat16),
        ),
        in_specs=[scalars, hbm, hbm, hbm],
        out_specs=(vmem,) * 5,
        scratch_shapes=[
            pltpu.VMEM((rows, cols), jnp.int32),
            pltpu.VMEM(row_strip.shape, jnp.bfloat16),
            pltpu.VMEM(row_strip.shape, jnp.bfloat16),
            pltpu.VMEM((rows * cols, cols), jnp.bfloat16),
            pltpu.SemaphoreType.DMA((5,)),
        ],
        compiler_params=small,
        cost_estimate=pl.CostEstimate(flops=1_000_000, bytes_accessed=2_000_000, transcendentals=0),
        name="edge_rows",
    )(place, *(pltpu.with_memory_space_constraint(a, pltpu.HBM) for a in (genuine_flags, grid_elements, triple_t)))
    even_rows, odd_rows = pair_swapped(even_rows, odd_rows, "row")

    far_pieces = []
    if relays:
        first = swapped(mine, "row", far)
    far_last = swapped(after(last, even_rows, odd_rows), "row", far)

    carrier_tiles = -(-own.shape[0] // TILE)
    even_cols, odd_cols = pl.pallas_call(
        strip_kernel,
        out_shape=(jax.ShapeDtypeStruct((col_strip.shape[0] + carrier_tiles, *col_strip.shape[1:]), jnp.bfloat16), col_strip),
        in_specs=[scalars] + [vmem] * 5,
        out_specs=(vmem,) * 2,
        scratch_shapes=[pltpu.VMEM((carrier_tiles * TILE, channels), jnp.float32)],
        compiler_params=small,
        cost_estimate=pl.CostEstimate(flops=1_000_000, bytes_accessed=2_000_000, transcendentals=0),
        name="edge_columns",
    )(place, grid_elements, mark, even_rows, odd_rows, summary_vectors)
    even_cols, odd_cols = pair_swapped(even_cols, odd_cols, "col")
    carriers = even_cols[col_strip.shape[0] :].reshape(-1, channels)[: own.shape[0]]
    carriers = jnp.concatenate([own, carriers], axis=0)
    for bit in bits_of(col)[:-1]:
        got = swapped(carriers, "col", bit)
        carriers = jnp.concatenate([carriers, got], axis=0)
    if relays:
        first = after(first, even_cols, odd_cols)
        others = [lax.ppermute(first, "img", [(i, (i + k) % img) for i in range(img)]) for k in range(1, relays)]
        far_pieces = [first] + others
    far_pieces.append(far_last)

    final_pack = jnp.concatenate([final_t, carriers], axis=0)
    finals, triples, offsets = [final_pack], [triple_t], [0]
    for bit in rest:
        finals = finals + [swapped(p, "row", bit) for p in finals]
        triples = triples + [swapped(p, "row", bit) for p in triples]
        offsets = offsets + [o ^ bit for o in offsets]
    tiles = (rows // TILE) * (cols // TILE)
    keys = 4 * TILE * TILE
    xq = pl.pallas_call(
        own_kernel,
        out_shape=jax.ShapeDtypeStruct((rows * cols, channels), jnp.bfloat16),
        in_specs=[vmem],
        out_specs=vmem,
        compiler_params=small,
        cost_estimate=pl.CostEstimate(flops=10_000_000, bytes_accessed=3_000_000, transcendentals=1000),
        name="own_norm",
    )(grid_elements)
    xkv, hide = pl.pallas_call(
        halo_kernel,
        out_shape=(
            jax.ShapeDtypeStruct((wide_rows * wide_cols, channels), jnp.bfloat16),
            jax.ShapeDtypeStruct((tiles, 8, keys), jnp.float32),
        ),
        in_specs=[scalars] + [vmem] * 6,
        out_specs=(vmem,) * 2,
        scratch_shapes=[
            *[pltpu.VMEM(shape.shape, jnp.float32) for shape in (row_strip, row_strip, col_strip, col_strip)],
            *[pltpu.VMEM((*shape.shape[:2], LANES), jnp.float32) for shape in (row_strip, row_strip, col_strip, col_strip)],
            pltpu.VMEM((wide_rows * wide_cols, LANES), jnp.bfloat16),
        ],
        compiler_params=pltpu.CompilerParams(vmem_limit_bytes=24 * 1024 * 1024),
        cost_estimate=pl.CostEstimate(flops=10_000_000, bytes_accessed=6_000_000, transcendentals=1000),
        name="halo_norm",
    )(place, after(xq, got), mark, even_rows, odd_rows, even_cols, odd_cols)

    far_final = swapped(final_pack, "row", far)

    far_offsets = [far]
    far_pieces = [[after(piece, xkv)] for piece in far_pieces]
    for bit in rest:
        far_pieces = [same + [swapped(p, "row", bit) for p in same] for same in far_pieces]
        far_offsets = far_offsets + [o ^ bit for o in far_offsets]

    groups = channels // GROUP
    numbered = [(off, number) for number in range(len(far_pieces)) for off in far_offsets]
    sources = triples + [piece for same in far_pieces for piece in same]
    q, k, v, wt = pl.pallas_call(
        functools.partial(project_kernel, offsets, numbered, triple_t.shape[0]),
        out_shape=(
            jax.ShapeDtypeStruct((groups, rows * cols, GROUP), jnp.bfloat16),
            jax.ShapeDtypeStruct((groups, wide_rows * wide_cols, GROUP), jnp.bfloat16),
            jax.ShapeDtypeStruct((channels // LANES, wide_rows * wide_cols, 2 * LANES), jnp.bfloat16),
            jax.ShapeDtypeStruct((3 * channels, channels), jnp.bfloat16),
        ),
        in_specs=[scalars] + [anywhere] * len(sources) + [vmem] * 2,
        out_specs=(vmem,) * 4,
        scratch_shapes=[pltpu.SemaphoreType.DMA((len(sources),))],
        compiler_params=pltpu.CompilerParams(vmem_limit_bytes=VMEM_BYTES),
        cost_estimate=pl.CostEstimate(flops=5_000_000_000, bytes_accessed=14_000_000, transcendentals=0),
        name="project",
    )(place, *sources, xq, xkv)

    far_finals = [after(far_final, q)]
    for bit in rest:
        far_finals = far_finals + [swapped(p, "row", bit) for p in far_finals]
    finals, offsets = finals + far_finals, offsets + far_offsets
    carriers_here = carrier_tiles * TILE
    summary_result, wo, kce, vc = pl.pallas_call(
        functools.partial(carrier_kernel, offsets),
        out_shape=(
            jax.ShapeDtypeStruct(summary_vectors.shape, jnp.bfloat16),
            jax.ShapeDtypeStruct((channels, channels), jnp.bfloat16),
            jax.ShapeDtypeStruct((own.shape[0] * groups, GROUP, GROUP), jnp.bfloat16),
            jax.ShapeDtypeStruct((carriers_here, channels), jnp.float32),
        ),
        in_specs=[scalars, vmem] + [anywhere] * len(finals),
        out_specs=(vmem,) * 4,
        scratch_shapes=[
            pltpu.VMEM((row * col * own.shape[0], channels), jnp.bfloat16),
            pltpu.SemaphoreType.DMA((2 * len(finals),)),
        ],
        compiler_params=pltpu.CompilerParams(vmem_limit_bytes=VMEM_BYTES),
        cost_estimate=pl.CostEstimate(flops=500_000_000, bytes_accessed=5_000_000, transcendentals=10_000),
        name="carriers",
    )(place, wt, *finals)

    out = pl.pallas_call(
        attend_kernel,
        out_shape=jax.ShapeDtypeStruct(grid_elements.shape, jnp.bfloat16),
        in_specs=[vmem] * 8,
        out_specs=anywhere,
        scratch_shapes=[
            pltpu.VMEM((cols // (2 * TILE), rows, 2 * TILE, channels), jnp.bfloat16),
            pltpu.VMEM((rows * cols, channels), jnp.bfloat16),
            pltpu.SemaphoreType.DMA((cols // (2 * TILE),)),
        ],
        compiler_params=pltpu.CompilerParams(vmem_limit_bytes=VMEM_BYTES),
        cost_estimate=pl.CostEstimate(flops=5_000_000_000, bytes_accessed=12_000_000, transcendentals=4_000_000),
        name="attend",
    )(grid_elements, q, k, v, hide, kce, vc, wo)
    return (out, summary_result)


def solution(mesh):
    placed = (
        P(("img", "row"), "col", None),
        P(("img", "row"), "col", None),
        P(None, "row"),
        P(None, "row"),
        P(("img", "row"), "col"),
    )
    return jax.shard_map(
        local,
        mesh=mesh,
        in_specs=placed,
        out_specs=(P(("img", "row"), "col", None), P(("img", "row"), "col", None)),
        check_vma=False,
    )
```

```python
import functools

import jax
import jax.numpy as jnp
from jax import lax
from jax.experimental import pallas as pl
from jax.experimental.pallas import tpu as pltpu
from jax.sharding import PartitionSpec as P

HEAD_DIM = 64
PATCH_SIDE = 16
RADIUS = 4
TILE = 2 * RADIUS
LANES = 128
GROUP = 256
INVALID = 100.0
HIDDEN = -1e30
LOG2_E = 1.4426950408889634
EVEN_ROW, EVEN_COL, ROW, STARTS = 4, 5, 6, 7
VMEM_BYTES = 26 * 1024 * 1024


def nt(a, b):
    return lax.dot_general(a, b, (((1,), (1,)), ((), ())), preferred_element_type=jnp.float32)


def nn(a, b):
    return lax.dot_general(a, b, (((1,), (0,)), ((), ())), preferred_element_type=jnp.float32)


def layer_normalise(lines):
    center = lines - jnp.mean(lines, axis=-1, keepdims=True)
    spread = jnp.mean(center * center, axis=-1, keepdims=True)
    return center * lax.rsqrt(spread + 1e-05)


def pair_swapped(even_block, odd_block, axis):
    count = lax.axis_size(axis)
    got = []
    for first, block in ((0, even_block), (1, odd_block)):
        pairs = [(i, i + 1) for i in range(first, count - 1, 2)]
        got.append(lax.ppermute(block, axis, pairs + [(b, a) for a, b in pairs]))
    return got


def swapped(block, axis, bit):
    count = lax.axis_size(axis)
    return lax.ppermute(block, axis, [(i, i ^ bit) for i in range(count)])


def after(block, *others):
    return lax.optimization_barrier((block, *others))[0]


def bits_of(count):
    bits, bit = [], count // 2
    while bit:
        bits.append(bit)
        bit //= 2
    return bits


def marked_lanes(lines, hidden):
    first = jnp.where(hidden, INVALID, lines[:, :, :LANES])
    return jnp.concatenate([first, lines[:, :, LANES:]], axis=2)


def edge_kernel(piece_rows, place_ref, flags_hbm, x_hbm, triple_hbm, mark_ref, even_ref, odd_ref, mine_ref, last_ref, *scratch):
    flags_ref, first_s, last_s, spread, sems = scratch
    rows, cols = flags_ref.shape
    own_start = pl.multiple_of(place_ref[STARTS], 16)
    last_start = triple_hbm.shape[0] - last_ref.shape[0]
    copies = [
        pltpu.make_async_copy(x_hbm.at[0:RADIUS], first_s, sems.at[0]),
        pltpu.make_async_copy(x_hbm.at[rows - RADIUS : rows], last_s, sems.at[1]),
        pltpu.make_async_copy(triple_hbm.at[pl.ds(own_start, piece_rows), :], mine_ref, sems.at[2]),
        pltpu.make_async_copy(triple_hbm.at[last_start:, :], last_ref, sems.at[3]),
    ]
    flags_copy = pltpu.make_async_copy(flags_hbm, flags_ref, sems.at[4])
    flags_copy.start()
    for copy in copies:
        copy.start()
    flags_copy.wait()
    row_at = lax.broadcasted_iota(jnp.int32, (cols, cols), 0)
    diagonal = row_at == lax.broadcasted_iota(jnp.int32, (cols, cols), 1)
    for r in range(rows):
        hidden = jnp.where(flags_ref[r : r + 1, :] > 0, 0.0, INVALID)
        spread[r * cols : (r + 1) * cols, :] = jnp.where(diagonal, hidden, 0.0).astype(jnp.bfloat16)
    marks = nn(spread[...], jnp.ones((cols, LANES), jnp.bfloat16)).reshape(rows, cols, LANES)
    mark_ref[...] = marks.astype(jnp.bfloat16)
    for copy in copies:
        copy.wait()
    first, last = [
        marked_lanes(ref[...].astype(jnp.float32), marks[at] > INVALID / 2)
        for ref, at in ((first_s, slice(0, RADIUS)), (last_s, slice(rows - RADIUS, rows)))
    ]
    even = place_ref[EVEN_ROW] > 0
    even_ref[...] = jnp.where(even, last, first).astype(jnp.bfloat16)
    odd_ref[...] = jnp.where(even, first, last).astype(jnp.bfloat16)


def strip_kernel(place_ref, x_ref, mark_ref, even_rows_ref, odd_rows_ref, carriers_ref, even_ref, odd_ref, carriers_s):
    per_row = carriers_ref.shape[1]
    carriers_s[...] = jnp.zeros_like(carriers_s)
    for i in range(carriers_ref.shape[0]):
        carriers_s[i * per_row : (i + 1) * per_row, :] = carriers_ref[i].astype(jnp.float32)
    for i in range(carriers_s.shape[0] // TILE):
        even_ref[odd_ref.shape[0] + i] = carriers_s[i * TILE : (i + 1) * TILE, :].astype(jnp.bfloat16)
    rows, cols, channels = x_ref.shape
    middle = rows // 2
    low = lax.broadcasted_iota(jnp.int32, (1, TILE, 1), 1) < RADIUS
    even_row, even_col = place_ref[EVEN_ROW] > 0, place_ref[EVEN_COL] > 0
    for lane in range(0, channels, LANES):
        lanes = slice(lane, lane + LANES)
        strips = []
        for columns, last in ((slice(0, TILE), False), (slice(cols - TILE, cols), True)):

            def own(part):
                lines = x_ref[part, columns, lanes].astype(jnp.float32)
                if lane == 0:
                    lines = jnp.where(mark_ref[part, columns, :].astype(jnp.float32) > INVALID / 2, INVALID, lines)
                return lines

            even_rows = even_rows_ref[:, columns, lanes].astype(jnp.float32)
            odd_rows = odd_rows_ref[:, columns, lanes].astype(jnp.float32)
            top, bottom = jnp.where(even_row, odd_rows, even_rows), jnp.where(even_row, even_rows, odd_rows)
            upper = jnp.concatenate([top, own(slice(0, middle))], axis=0)
            lower = jnp.concatenate([own(slice(middle, rows)), bottom], axis=0)
            if last:
                upper = jnp.roll(upper, RADIUS, axis=1)
            else:
                lower = jnp.roll(lower, RADIUS, axis=1)
            strips.append(jnp.where(low, upper, lower))
        first, last = strips
        even_ref[: odd_ref.shape[0], :, lanes] = jnp.where(even_col, last, first).astype(jnp.bfloat16)
        odd_ref[:, :, lanes] = jnp.where(even_col, first, last).astype(jnp.bfloat16)


def own_kernel(x_ref, xq_ref):
    rows, cols, _ = x_ref.shape
    step = 4

    def own(i, _):
        at = pl.multiple_of(i * step, step)
        y = layer_normalise(x_ref[pl.ds(at, step)].astype(jnp.float32))
        for c in range(cols // TILE):
            piece = y[:, c * TILE : (c + 1) * TILE, :].reshape(step * TILE, -1)
            to = pl.multiple_of(c * rows * TILE + at * TILE, step * TILE)
            xq_ref[pl.ds(to, step * TILE), :] = piece.astype(jnp.bfloat16)
        return 0

    lax.fori_loop(0, rows // step, own, 0)


def halo_kernel(place_ref, xq_ref, mark_ref, even_rows_ref, odd_rows_ref, even_cols_ref, odd_cols_ref, xkv_ref, hide_ref, *scratch):
    rows, cols, _ = mark_ref.shape
    wide_rows, wide_cols = rows + 2 * RADIUS, cols + 2 * RADIUS
    half = wide_rows // 2
    step = 2
    top_s, bottom_s, left_s, right_s, top_ref, bottom_ref, left_ref, right_ref, flag_s = scratch
    for even, odd, low, high, low_flags, high_flags, parity, size in (
        (even_rows_ref, odd_rows_ref, top_s, bottom_s, top_ref, bottom_ref, EVEN_ROW, 2),
        (even_cols_ref, odd_cols_ref, left_s, right_s, left_ref, right_ref, EVEN_COL, 5),
    ):
        flip = place_ref[parity] > 0
        for i in range(0, odd.shape[0], size):
            a, b = even[i : i + size].astype(jnp.float32), odd[i : i + size].astype(jnp.float32)
            for lines, out, flags in ((jnp.where(flip, b, a), low, low_flags), (jnp.where(flip, a, b), high, high_flags)):
                out[i : i + size] = layer_normalise(lines)
                flags[i : i + size] = lines[:, :, :LANES]

    def lines_of(ref):
        return ref.astype(jnp.float32)

    def merge(at, blocks, left, right, to_ref):
        low = lax.broadcasted_iota(jnp.int32, (1, TILE, 1), 1) < RADIUS
        before = left
        for c in range(len(blocks) + 1):
            after = jnp.roll(blocks[c], RADIUS, axis=1) if c < len(blocks) else right
            to = c * wide_rows * TILE + at * TILE
            to = pl.multiple_of(to, step * TILE) if not isinstance(to, int) else to
            lines = jnp.where(low, before, after).reshape(step * TILE, -1)
            to_ref[pl.ds(to, step * TILE), :] = lines.astype(jnp.bfloat16)
            before = after

    def sides(at, upper, left_ref, right_ref, lanes):
        if upper:
            at = at - half
            left, right = jnp.roll(lines_of(left_ref[pl.ds(at, step), :, lanes]), RADIUS, axis=1), lines_of(
                right_ref[pl.ds(at, step), :, lanes]
            )
        else:
            left, right = lines_of(left_ref[pl.ds(at, step), :, lanes]), jnp.roll(
                lines_of(right_ref[pl.ds(at, step), :, lanes]), RADIUS, axis=1
            )
        return left, right

    every, few = slice(None), slice(0, LANES)

    def hide_if(border, lines):
        return jnp.where(place_ref[border] > 0, INVALID, lines)

    def mark_sides(at, upper):
        left, right = sides(at, upper, left_ref, right_ref, few)
        return hide_if(2, left), hide_if(3, right)

    def band(at, ref, ref_s, first, upper):
        cut = [slice(c * TILE, (c + 1) * TILE) for c in range(cols // TILE)]
        merge(at, [ref_s[first : first + step, k, :] for k in cut], *sides(at, upper, left_s, right_s, every), xkv_ref)
        marks = hide_if(int(upper), ref[first : first + step])
        beside = [hide_if(int(upper), side) for side in mark_sides(at, upper)]
        merge(at, [marks[:, k, :] for k in cut], *beside, flag_s)

    for i in range(0, RADIUS, step):
        band(i, top_ref, top_s, i, False)
        band(RADIUS + rows + i, bottom_ref, bottom_s, i, True)

    def middle(i, upper):
        at = pl.multiple_of(i * step, step)
        own = at - RADIUS
        blocks = []
        for c in range(cols // TILE):
            first = pl.multiple_of(c * rows * TILE + own * TILE, step * TILE)
            blocks.append(xq_ref[pl.ds(first, step * TILE), :].astype(jnp.float32).reshape(step, TILE, -1))
        merge(at, blocks, *sides(at, upper, left_s, right_s, every), xkv_ref)
        marks = mark_ref[pl.ds(own, step)].astype(jnp.float32)
        marks = [marks[:, c * TILE : (c + 1) * TILE, :] for c in range(cols // TILE)]
        merge(at, marks, *mark_sides(at, upper), flag_s)
        return 0

    lax.fori_loop(RADIUS // step, half // step, lambda i, _: middle(i, False), 0)
    lax.fori_loop(half // step, (RADIUS + rows) // step, lambda i, _: middle(i, True), 0)

    first_lane = (lax.broadcasted_iota(jnp.int32, (8, LANES), 1) == 0).astype(jnp.bfloat16)
    spans = []
    for c in range(wide_cols // TILE):
        lines = flag_s[c * wide_rows * TILE : (c + 1) * wide_rows * TILE, :]
        spans.append(jnp.where(nt(first_lane, lines) > INVALID / 2, HIDDEN, 0.0))
    tall = rows // TILE
    for c in range(cols // TILE):
        for r in range(tall):
            at = slice(r * TILE * TILE, r * TILE * TILE + 2 * TILE * TILE)
            hide_ref[c * tall + r] = jnp.concatenate([spans[c][:, at], spans[c + 1][:, at]], axis=1)


def project_kernel(whole, pieces, triple_rows, place_ref, *refs):
    sources, refs = refs[: len(whole) + len(pieces)], refs[len(whole) + len(pieces) :]
    xq_ref, xkv_ref, q_s, k_s, v_s, wt, sems = refs
    channels = wt.shape[1]
    groups = channels // GROUP
    factor = HEAD_DIM ** (-0.5) * LOG2_E
    me = place_ref[ROW]
    copies = []
    for j, source in enumerate(sources):
        if j < len(whole):
            to = (me ^ whole[j]) * triple_rows
        else:
            off, start = pieces[j - len(whole)]
            to = (me ^ off) * triple_rows + place_ref[STARTS + start]
        to = pl.multiple_of(to, 16)
        copy = pltpu.make_async_copy(source, wt.at[pl.ds(to, source.shape[0]), :], sems.at[j])
        copy.start()
        copies.append(copy)
    for copy in copies:
        copy.wait()

    q_rows, kv_rows = xq_ref.shape[0], xkv_ref.shape[0]
    q_chunk, kv_chunk = q_rows // 2, kv_rows // 4

    def project_q(n, _):
        w = wt[pl.ds(pl.multiple_of(n * GROUP, GROUP), GROUP), :]
        for m in range(0, q_rows, q_chunk):
            q_s[n, m : m + q_chunk, :] = (nt(xq_ref[m : m + q_chunk, :], w) * factor).astype(jnp.bfloat16)
        return 0

    def project_k(n, _):
        w = wt[pl.ds(pl.multiple_of(channels + n * GROUP, GROUP), GROUP), :]
        for m in range(0, kv_rows, kv_chunk):
            k_s[n, m : m + kv_chunk, :] = nt(xkv_ref[m : m + kv_chunk, :], w).astype(jnp.bfloat16)
        return 0

    def project_v(n, _):
        w = wt[pl.ds(pl.multiple_of(2 * channels + n * GROUP, GROUP), GROUP), :]
        for m in range(0, kv_rows, kv_chunk):
            y = nt(xkv_ref[m : m + kv_chunk, :], w).astype(jnp.bfloat16)
            for j in range(GROUP // LANES):
                v_s[GROUP // LANES * n + j, m : m + kv_chunk, :LANES] = y[:, j * LANES : (j + 1) * LANES]
                v_s[GROUP // LANES * n + j, m : m + kv_chunk, LANES:] = jnp.ones((kv_chunk, LANES), jnp.bfloat16)
        return 0

    lax.fori_loop(0, groups, project_q, 0)
    lax.fori_loop(0, groups, project_k, 0)
    lax.fori_loop(0, groups, project_v, 0)


def carrier_kernel(offsets, place_ref, wt, *refs):
    shards = len(offsets)
    finals, refs = refs[:shards], refs[shards:]
    summary_ref, wo, kce, vc_s, carriers_s, sems = refs
    per_row = summary_ref.shape[1]
    channels = wt.shape[1]
    groups = channels // GROUP
    heads = channels // HEAD_DIM
    factor = HEAD_DIM ** (-0.5)
    carriers_here = vc_s.shape[0]
    final_rows = wo.shape[0] // shards
    copies = []
    for j, off in enumerate(offsets):
        to = pl.multiple_of((place_ref[ROW] ^ off) * final_rows, 16)
        copy = pltpu.make_async_copy(finals[j].at[0:final_rows, :], wo.at[pl.ds(to, final_rows), :], sems.at[j])
        copy.start()
        copies.append(copy)
    coming = []
    sent = carriers_s.shape[0] // shards
    for j in range(shards):
        source = finals[j].at[final_rows : final_rows + sent, :]
        copy = pltpu.make_async_copy(source, carriers_s.at[j * sent : (j + 1) * sent, :], sems.at[shards + j])
        copy.start()
        coming.append(copy)
    for copy in coming:
        copy.wait()
    carriers = carriers_s[...].astype(jnp.float32)
    own = carriers[:carriers_here]
    carriers = layer_normalise(carriers).astype(jnp.bfloat16)
    own_norm = layer_normalise(own).astype(jnp.bfloat16)
    qc = (nt(own_norm, wt[:channels, :]) * factor).astype(jnp.bfloat16).astype(jnp.float32)
    kc = nt(carriers, wt[channels : 2 * channels, :]).astype(jnp.bfloat16)
    vc = nt(carriers, wt[2 * channels :, :]).astype(jnp.bfloat16)
    head_of = lax.broadcasted_iota(jnp.int32, (1, channels), 1) // HEAD_DIM
    stacked = jnp.concatenate([jnp.where(head_of == h, qc, 0.0) for h in range(heads)], axis=0)
    e = jnp.exp(nt(stacked.astype(jnp.bfloat16), kc))
    weights = (e / jnp.sum(e, axis=-1, keepdims=True)).astype(jnp.bfloat16)
    o = nn(weights, vc)
    mix = jnp.zeros((carriers_here, channels), jnp.float32)
    for h in range(heads):
        mix = jnp.where(head_of == h, o[h * carriers_here : (h + 1) * carriers_here, :], mix)
    for copy in copies:
        copy.wait()
    renewed = own + nt(mix.astype(jnp.bfloat16), wo[...])
    for i in range(summary_ref.shape[0]):
        summary_ref[i] = renewed[i * per_row : (i + 1) * per_row, :].astype(jnp.bfloat16)
    fresh = nt(layer_normalise(renewed).astype(jnp.bfloat16), wt[channels:, :]).astype(jnp.bfloat16).astype(jnp.float32)
    vc_s[...] = fresh[:, channels:]
    same = (
        lax.broadcasted_iota(jnp.int32, (GROUP, GROUP), 0) // HEAD_DIM
        == lax.broadcasted_iota(jnp.int32, (GROUP, GROUP), 1) // HEAD_DIM
    )
    windows = kce.shape[0] // groups
    for w in range(windows):
        for g in range(groups):
            kce[w * groups + g] = jnp.where(same, fresh[w : w + 1, g * GROUP : (g + 1) * GROUP], 0.0).astype(jnp.bfloat16)


def attend_kernel(tall, broad, q_s, k_s, v_s, hide_ref, kce, vc_s, mix_s, pc_s, even_s, odd_s):
    groups, tiles = q_s.shape[0], hide_ref.shape[0]
    heads_in = GROUP // HEAD_DIM
    queries, span = TILE * TILE, 2 * TILE * TILE
    side = PATCH_SIDE // TILE
    wide = (tall + 1) * queries
    qi = lax.broadcasted_iota(jnp.int32, (queries, 2 * span), 0)
    ki = lax.broadcasted_iota(jnp.int32, (queries, 2 * span), 1)
    row_step = (ki % span) // TILE - qi // TILE
    col_step = (ki // span) * TILE + ki % TILE - qi % TILE
    seen = (row_step >= 0) & (row_step <= 2 * RADIUS) & (col_step >= 0) & (col_step <= 2 * RADIUS)
    band = jnp.where(seen, 0.0, HIDDEN)
    group_head = lax.broadcasted_iota(jnp.int32, (1, GROUP), 1) // HEAD_DIM
    only = [jnp.where(group_head == h, 1.0, 0.0).astype(jnp.bfloat16) for h in range(heads_in)]
    pairs, in_pair = GROUP // LANES, LANES // HEAD_DIM
    pair_head = lax.broadcasted_iota(jnp.int32, (1, 2 * LANES), 1) % LANES // HEAD_DIM

    for c in range(broad):
        for w in range(tall // side):
            at = slice((c * tall + w * side) * queries, (c * tall + (w + 1) * side) * queries)
            window = w * (broad // side) + c // side
            for g in range(groups):
                pc_s[at, g * GROUP : (g + 1) * GROUP] = jnp.exp2(nt(q_s[g, at, :], kce[window * groups + g]))

    def keys_at(t):
        k0 = pl.multiple_of(t // tall * wide + t % tall * queries, queries)
        return k0, pl.multiple_of(k0 + wide, queries)

    def scores(t, ref):
        q_at = pl.multiple_of(t * queries, queries)
        k0, k1 = keys_at(t)
        for g in range(groups):
            q = q_s[g, pl.ds(q_at, queries), :]
            qq = jnp.concatenate([q * mask for mask in only], axis=0)
            k = jnp.concatenate([k_s[g, pl.ds(k0, span), :], k_s[g, pl.ds(k1, span), :]], axis=0)
            ref[g] = nt(qq, k)

    def finish(t, ref):
        q_at = pl.multiple_of(t * queries, queries)
        k0, k1 = keys_at(t)
        window = t % tall // side * (broad // side) + t // tall // side
        bias = band + hide_ref[t][0:1, :]
        for g in range(groups):
            p = jnp.exp2(ref[g].reshape(heads_in, queries, 2 * span) + bias[None])
            p = p.reshape(heads_in * queries, 2 * span).astype(jnp.bfloat16)
            v_new = vc_s[pl.ds(window, 1), g * GROUP : (g + 1) * GROUP]
            for j in range(pairs):
                at = slice(g * GROUP + j * LANES, g * GROUP + (j + 1) * LANES)
                v = jnp.concatenate(
                    [v_s[pairs * g + j, pl.ds(k0, span), :], v_s[pairs * g + j, pl.ds(k1, span), :]], axis=0
                )
                o = nn(p[j * in_pair * queries : (j + 1) * in_pair * queries, :], v)
                kept = o[:queries]
                for h in range(1, in_pair):
                    kept = jnp.where(pair_head == h, o[h * queries : (h + 1) * queries], kept)
                new = pc_s[pl.ds(q_at, queries), at]
                mixed = (kept[:, :LANES] + new * v_new[:, j * LANES : (j + 1) * LANES]) / (kept[:, LANES:] + new)
                mix_s[pl.ds(q_at, queries), at] = mixed.astype(jnp.bfloat16)

    scores(0, even_s)

    def two(i, _):
        t = 2 * i
        scores(t + 1, odd_s)
        finish(t, even_s)
        scores(jnp.minimum(t + 2, tiles - 1), even_s)
        finish(t + 1, odd_s)
        return 0

    lax.fori_loop(0, tiles // 2, two, 0)


def out_kernel(x_ref, mix_s, wo, out_hbm, out_ref, out_sems):
    rows, cols, channels = x_ref.shape
    going = []
    for pair in range(cols // (2 * TILE)):
        both = slice(2 * pair * TILE, 2 * (pair + 1) * TILE)
        for g in range(channels // GROUP):
            at = slice(g * GROUP, (g + 1) * GROUP)
            w = wo[at, :]
            parts = [
                nt(mix_s[b * rows * TILE : (b + 1) * rows * TILE, :], w).reshape(rows, TILE, GROUP)
                for b in (2 * pair, 2 * pair + 1)
            ]
            y = jnp.concatenate(parts, axis=1) + x_ref[:, both, at].astype(jnp.float32)
            out_ref[pair, :, :, at] = y.astype(jnp.bfloat16)
        copy = pltpu.make_async_copy(out_ref.at[pair], out_hbm.at[:, both, :], out_sems.at[pair])
        copy.start()
        going.append(copy)
    for copy in going:
        copy.wait()


def local(grid_elements, summary_vectors, triple_projection, final_projection, genuine_flags):
    rows, cols, channels = grid_elements.shape
    wide_rows, wide_cols = rows + 2 * RADIUS, cols + 2 * RADIUS
    own = summary_vectors.reshape(-1, channels)

    triple_t, final_t = triple_projection.T, final_projection.T
    vmem = pl.BlockSpec(memory_space=pltpu.VMEM)
    anywhere = pl.BlockSpec(memory_space=pl.ANY)
    scalars = pl.BlockSpec(memory_space=pltpu.SMEM)
    hbm = pl.BlockSpec(memory_space=pltpu.HBM)
    small = pltpu.CompilerParams(vmem_limit_bytes=16 * 1024 * 1024)
    row_strip = jax.ShapeDtypeStruct((RADIUS, cols, channels), jnp.bfloat16)
    col_strip = jax.ShapeDtypeStruct((wide_rows // 2, 2 * RADIUS, channels), jnp.bfloat16)

    row, col, img = lax.axis_size("row"), lax.axis_size("col"), lax.axis_size("img")
    row_at, col_at, img_at = lax.axis_index("row"), lax.axis_index("col"), lax.axis_index("img")
    row_bits = bits_of(row)
    far, rest = row_bits[0], row_bits[1:]
    relays = img if triple_t.shape[0] % (16 * (img + 1)) == 0 else 0
    piece_rows = triple_t.shape[0] // (relays + 1)
    starts = [(img_at - k) % img for k in range(relays)] + [jnp.int32(relays)]
    place = [row_at == 0, row_at == row - 1, col_at == 0, col_at == col - 1, row_at % 2 == 0, col_at % 2 == 0, row_at]
    place = jnp.stack([jnp.asarray(p).astype(jnp.int32) for p in place + [start * piece_rows for start in starts]])

    mark, even_rows, odd_rows, mine, last = pl.pallas_call(
        functools.partial(edge_kernel, piece_rows),
        out_shape=(
            jax.ShapeDtypeStruct((rows, cols, LANES), jnp.bfloat16),
            row_strip,
            row_strip,
            jax.ShapeDtypeStruct((piece_rows, channels), jnp.bfloat16),
            jax.ShapeDtypeStruct((triple_t.shape[0] - relays * piece_rows, channels), jnp.bfloat16),
        ),
        in_specs=[scalars, hbm, hbm, hbm],
        out_specs=(vmem,) * 5,
        scratch_shapes=[
            pltpu.VMEM((rows, cols), jnp.int32),
            pltpu.VMEM(row_strip.shape, jnp.bfloat16),
            pltpu.VMEM(row_strip.shape, jnp.bfloat16),
            pltpu.VMEM((rows * cols, cols), jnp.bfloat16),
            pltpu.SemaphoreType.DMA((5,)),
        ],
        compiler_params=small,
        cost_estimate=pl.CostEstimate(flops=1_000_000, bytes_accessed=2_000_000, transcendentals=0),
        name="edge_rows",
    )(place, *(pltpu.with_memory_space_constraint(a, pltpu.HBM) for a in (genuine_flags, grid_elements, triple_t)))
    even_rows, odd_rows = pair_swapped(even_rows, odd_rows, "row")

    far_pieces = []
    if relays:
        first = swapped(mine, "row", far)
    far_last = swapped(after(last, even_rows, odd_rows), "row", far)

    carrier_tiles = -(-own.shape[0] // TILE)
    even_cols, odd_cols = pl.pallas_call(
        strip_kernel,
        out_shape=(jax.ShapeDtypeStruct((col_strip.shape[0] + carrier_tiles, *col_strip.shape[1:]), jnp.bfloat16), col_strip),
        in_specs=[scalars] + [vmem] * 5,
        out_specs=(vmem,) * 2,
        scratch_shapes=[pltpu.VMEM((carrier_tiles * TILE, channels), jnp.float32)],
        compiler_params=small,
        cost_estimate=pl.CostEstimate(flops=1_000_000, bytes_accessed=2_000_000, transcendentals=0),
        name="edge_columns",
    )(place, grid_elements, mark, even_rows, odd_rows, summary_vectors)
    even_cols, odd_cols = pair_swapped(even_cols, odd_cols, "col")
    carriers = even_cols[col_strip.shape[0] :].reshape(-1, channels)[: own.shape[0]]
    carriers = jnp.concatenate([own, carriers], axis=0)
    for bit in bits_of(col)[:-1]:
        got = swapped(carriers, "col", bit)
        carriers = jnp.concatenate([carriers, got], axis=0)
    if relays:
        first = after(first, even_cols, odd_cols)
        others = [lax.ppermute(first, "img", [(i, (i + k) % img) for i in range(img)]) for k in range(1, relays)]
        far_pieces = [first] + others
    far_pieces.append(far_last)

    final_pack = jnp.concatenate([final_t, carriers], axis=0)
    finals, triples, offsets = [final_pack], [triple_t], [0]
    for bit in rest:
        finals = finals + [swapped(p, "row", bit) for p in finals]
        triples = triples + [swapped(p, "row", bit) for p in triples]
        offsets = offsets + [o ^ bit for o in offsets]
    tiles = (rows // TILE) * (cols // TILE)
    keys = 4 * TILE * TILE
    xq = pl.pallas_call(
        own_kernel,
        out_shape=jax.ShapeDtypeStruct((rows * cols, channels), jnp.bfloat16),
        in_specs=[vmem],
        out_specs=vmem,
        compiler_params=small,
        cost_estimate=pl.CostEstimate(flops=10_000_000, bytes_accessed=3_000_000, transcendentals=1000),
        name="own_norm",
    )(grid_elements)
    xkv, hide = pl.pallas_call(
        halo_kernel,
        out_shape=(
            jax.ShapeDtypeStruct((wide_rows * wide_cols, channels), jnp.bfloat16),
            jax.ShapeDtypeStruct((tiles, 8, keys), jnp.float32),
        ),
        in_specs=[scalars] + [vmem] * 6,
        out_specs=(vmem,) * 2,
        scratch_shapes=[
            *[pltpu.VMEM(shape.shape, jnp.float32) for shape in (row_strip, row_strip, col_strip, col_strip)],
            *[pltpu.VMEM((*shape.shape[:2], LANES), jnp.float32) for shape in (row_strip, row_strip, col_strip, col_strip)],
            pltpu.VMEM((wide_rows * wide_cols, LANES), jnp.bfloat16),
        ],
        compiler_params=pltpu.CompilerParams(vmem_limit_bytes=24 * 1024 * 1024),
        cost_estimate=pl.CostEstimate(flops=10_000_000, bytes_accessed=6_000_000, transcendentals=1000),
        name="halo_norm",
    )(place, after(xq, got), mark, even_rows, odd_rows, even_cols, odd_cols)

    far_final = swapped(final_pack, "row", far)

    far_offsets = [far]
    far_pieces = [[after(piece, xkv)] for piece in far_pieces]
    for bit in rest:
        far_pieces = [same + [swapped(p, "row", bit) for p in same] for same in far_pieces]
        far_offsets = far_offsets + [o ^ bit for o in far_offsets]

    groups = channels // GROUP
    numbered = [(off, number) for number in range(len(far_pieces)) for off in far_offsets]
    sources = triples + [piece for same in far_pieces for piece in same]
    q, k, v, wt = pl.pallas_call(
        functools.partial(project_kernel, offsets, numbered, triple_t.shape[0]),
        out_shape=(
            jax.ShapeDtypeStruct((groups, rows * cols, GROUP), jnp.bfloat16),
            jax.ShapeDtypeStruct((groups, wide_rows * wide_cols, GROUP), jnp.bfloat16),
            jax.ShapeDtypeStruct((channels // LANES, wide_rows * wide_cols, 2 * LANES), jnp.bfloat16),
            jax.ShapeDtypeStruct((3 * channels, channels), jnp.bfloat16),
        ),
        in_specs=[scalars] + [anywhere] * len(sources) + [vmem] * 2,
        out_specs=(vmem,) * 4,
        scratch_shapes=[pltpu.SemaphoreType.DMA((len(sources),))],
        compiler_params=pltpu.CompilerParams(vmem_limit_bytes=VMEM_BYTES),
        cost_estimate=pl.CostEstimate(flops=5_000_000_000, bytes_accessed=14_000_000, transcendentals=0),
        name="project",
    )(place, *sources, xq, xkv)

    far_finals = [after(far_final, q)]
    for bit in rest:
        far_finals = far_finals + [swapped(p, "row", bit) for p in far_finals]
    finals, offsets = finals + far_finals, offsets + far_offsets
    carriers_here = carrier_tiles * TILE
    summary_result, wo, kce, vc = pl.pallas_call(
        functools.partial(carrier_kernel, offsets),
        out_shape=(
            jax.ShapeDtypeStruct(summary_vectors.shape, jnp.bfloat16),
            jax.ShapeDtypeStruct((channels, channels), jnp.bfloat16),
            jax.ShapeDtypeStruct((own.shape[0] * groups, GROUP, GROUP), jnp.bfloat16),
            jax.ShapeDtypeStruct((carriers_here, channels), jnp.float32),
        ),
        in_specs=[scalars, vmem] + [anywhere] * len(finals),
        out_specs=(vmem,) * 4,
        scratch_shapes=[
            pltpu.VMEM((row * col * own.shape[0], channels), jnp.bfloat16),
            pltpu.SemaphoreType.DMA((2 * len(finals),)),
        ],
        compiler_params=pltpu.CompilerParams(vmem_limit_bytes=VMEM_BYTES),
        cost_estimate=pl.CostEstimate(flops=500_000_000, bytes_accessed=5_000_000, transcendentals=10_000),
        name="carriers",
    )(place, wt, *finals)

    scores = (groups, GROUP // HEAD_DIM * TILE * TILE, keys)
    mix = pl.pallas_call(
        functools.partial(attend_kernel, rows // TILE, cols // TILE),
        out_shape=jax.ShapeDtypeStruct((rows * cols, channels), jnp.bfloat16),
        in_specs=[vmem] * 6,
        out_specs=vmem,
        scratch_shapes=[
            pltpu.VMEM((rows * cols, channels), jnp.float32),
            pltpu.VMEM(scores, jnp.float32),
            pltpu.VMEM(scores, jnp.float32),
        ],
        compiler_params=pltpu.CompilerParams(vmem_limit_bytes=VMEM_BYTES),
        cost_estimate=pl.CostEstimate(flops=4_000_000_000, bytes_accessed=12_000_000, transcendentals=4_000_000),
        name="attend",
    )(q, k, v, hide, kce, vc)

    out = pl.pallas_call(
        out_kernel,
        out_shape=jax.ShapeDtypeStruct(grid_elements.shape, jnp.bfloat16),
        in_specs=[vmem] * 3,
        out_specs=anywhere,
        scratch_shapes=[
            pltpu.VMEM((cols // (2 * TILE), rows, 2 * TILE, channels), jnp.bfloat16),
            pltpu.SemaphoreType.DMA((cols // (2 * TILE),)),
        ],
        compiler_params=pltpu.CompilerParams(vmem_limit_bytes=VMEM_BYTES),
        cost_estimate=pl.CostEstimate(flops=1_200_000_000, bytes_accessed=6_000_000, transcendentals=0),
        name="out",
    )(grid_elements, mix, wo)
    return (out, summary_result)


def solution(mesh):
    placed = (
        P(("img", "row"), "col", None),
        P(("img", "row"), "col", None),
        P(None, "row"),
        P(None, "row"),
        P(("img", "row"), "col"),
    )
    return jax.shard_map(
        local,
        mesh=mesh,
        in_specs=placed,
        out_specs=(P(("img", "row"), "col", None), P(("img", "row"), "col", None)),
        check_vma=False,
    )
```

```python
import functools

import jax
import jax.numpy as jnp
from jax import lax
from jax.experimental import pallas as pl
from jax.experimental.pallas import tpu as pltpu
from jax.sharding import PartitionSpec as P

HEAD_DIM = 64
PATCH_SIDE = 16
RADIUS = 4
TILE = 2 * RADIUS
LANES = 128
GROUP = 256
INVALID = 100.0
HIDDEN = -1e30
LOG2_E = 1.4426950408889634
EVEN_ROW, EVEN_COL, ROW, STARTS = 4, 5, 6, 7
VMEM_BYTES = 26 * 1024 * 1024


def nt(a, b):
    return lax.dot_general(a, b, (((1,), (1,)), ((), ())), preferred_element_type=jnp.float32)


def nn(a, b):
    return lax.dot_general(a, b, (((1,), (0,)), ((), ())), preferred_element_type=jnp.float32)


def layer_normalise(lines):
    center = lines - jnp.mean(lines, axis=-1, keepdims=True)
    spread = jnp.mean(center * center, axis=-1, keepdims=True)
    return center * lax.rsqrt(spread + 1e-05)


def pair_swapped(even_block, odd_block, axis):
    count = lax.axis_size(axis)
    got = []
    for first, block in ((0, even_block), (1, odd_block)):
        pairs = [(i, i + 1) for i in range(first, count - 1, 2)]
        got.append(lax.ppermute(block, axis, pairs + [(b, a) for a, b in pairs]))
    return got


def swapped(block, axis, bit):
    count = lax.axis_size(axis)
    return lax.ppermute(block, axis, [(i, i ^ bit) for i in range(count)])


def after(block, *others):
    return lax.optimization_barrier((block, *others))[0]


def bits_of(count):
    bits, bit = [], count // 2
    while bit:
        bits.append(bit)
        bit //= 2
    return bits


def marked_lanes(lines, hidden):
    first = jnp.where(hidden, INVALID, lines[:, :, :LANES])
    return jnp.concatenate([first, lines[:, :, LANES:]], axis=2)


def edge_kernel(piece_rows, place_ref, flags_hbm, x_hbm, triple_hbm, mark_ref, even_ref, odd_ref, mine_ref, last_ref, x_ref, *scratch):
    flags_ref, spread, sems = scratch
    rows, cols = flags_ref.shape
    own_start = pl.multiple_of(place_ref[STARTS], 16)
    last_start = triple_hbm.shape[0] - last_ref.shape[0]
    copies = [
        pltpu.make_async_copy(x_hbm, x_ref, sems.at[0]),
        pltpu.make_async_copy(triple_hbm.at[pl.ds(own_start, piece_rows), :], mine_ref, sems.at[1]),
        pltpu.make_async_copy(triple_hbm.at[last_start:, :], last_ref, sems.at[2]),
    ]
    flags_copy = pltpu.make_async_copy(flags_hbm, flags_ref, sems.at[3])
    flags_copy.start()
    for copy in copies:
        copy.start()
    flags_copy.wait()
    row_at = lax.broadcasted_iota(jnp.int32, (cols, cols), 0)
    diagonal = row_at == lax.broadcasted_iota(jnp.int32, (cols, cols), 1)
    for r in range(rows):
        hidden = jnp.where(flags_ref[r : r + 1, :] > 0, 0.0, INVALID)
        spread[r * cols : (r + 1) * cols, :] = jnp.where(diagonal, hidden, 0.0).astype(jnp.bfloat16)
    marks = nn(spread[...], jnp.ones((cols, LANES), jnp.bfloat16)).reshape(rows, cols, LANES)
    mark_ref[...] = marks.astype(jnp.bfloat16)
    for copy in copies:
        copy.wait()
    first, last = [
        marked_lanes(x_ref[at].astype(jnp.float32), marks[at] > INVALID / 2)
        for at in (slice(0, RADIUS), slice(rows - RADIUS, rows))
    ]
    even = place_ref[EVEN_ROW] > 0
    even_ref[...] = jnp.where(even, last, first).astype(jnp.bfloat16)
    odd_ref[...] = jnp.where(even, first, last).astype(jnp.bfloat16)


def strip_kernel(place_ref, x_ref, mark_ref, even_rows_ref, odd_rows_ref, carriers_ref, even_ref, odd_ref, carriers_s):
    per_row = carriers_ref.shape[1]
    carriers_s[...] = jnp.zeros_like(carriers_s)
    for i in range(carriers_ref.shape[0]):
        carriers_s[i * per_row : (i + 1) * per_row, :] = carriers_ref[i].astype(jnp.float32)
    for i in range(carriers_s.shape[0] // TILE):
        even_ref[odd_ref.shape[0] + i] = carriers_s[i * TILE : (i + 1) * TILE, :].astype(jnp.bfloat16)
    rows, cols, channels = x_ref.shape
    middle = rows // 2
    low = lax.broadcasted_iota(jnp.int32, (1, TILE, 1), 1) < RADIUS
    even_row, even_col = place_ref[EVEN_ROW] > 0, place_ref[EVEN_COL] > 0
    for lane in range(0, channels, LANES):
        lanes = slice(lane, lane + LANES)
        strips = []
        for columns, last in ((slice(0, TILE), False), (slice(cols - TILE, cols), True)):

            def own(part):
                lines = x_ref[part, columns, lanes].astype(jnp.float32)
                if lane == 0:
                    lines = jnp.where(mark_ref[part, columns, :].astype(jnp.float32) > INVALID / 2, INVALID, lines)
                return lines

            even_rows = even_rows_ref[:, columns, lanes].astype(jnp.float32)
            odd_rows = odd_rows_ref[:, columns, lanes].astype(jnp.float32)
            top, bottom = jnp.where(even_row, odd_rows, even_rows), jnp.where(even_row, even_rows, odd_rows)
            upper = jnp.concatenate([top, own(slice(0, middle))], axis=0)
            lower = jnp.concatenate([own(slice(middle, rows)), bottom], axis=0)
            if last:
                upper = jnp.roll(upper, RADIUS, axis=1)
            else:
                lower = jnp.roll(lower, RADIUS, axis=1)
            strips.append(jnp.where(low, upper, lower))
        first, last = strips
        even_ref[: odd_ref.shape[0], :, lanes] = jnp.where(even_col, last, first).astype(jnp.bfloat16)
        odd_ref[:, :, lanes] = jnp.where(even_col, first, last).astype(jnp.bfloat16)


def own_kernel(x_ref, xq_ref):
    rows, cols, _ = x_ref.shape
    step = 4

    def own(i, _):
        at = pl.multiple_of(i * step, step)
        y = layer_normalise(x_ref[pl.ds(at, step)].astype(jnp.float32))
        for c in range(cols // TILE):
            piece = y[:, c * TILE : (c + 1) * TILE, :].reshape(step * TILE, -1)
            to = pl.multiple_of(c * rows * TILE + at * TILE, step * TILE)
            xq_ref[pl.ds(to, step * TILE), :] = piece.astype(jnp.bfloat16)
        return 0

    lax.fori_loop(0, rows // step, own, 0)


def halo_kernel(place_ref, xq_ref, mark_ref, even_rows_ref, odd_rows_ref, even_cols_ref, odd_cols_ref, xkv_ref, hide_ref, *scratch):
    rows, cols, _ = mark_ref.shape
    wide_rows, wide_cols = rows + 2 * RADIUS, cols + 2 * RADIUS
    half = wide_rows // 2
    step = 2
    top_s, bottom_s, left_s, right_s, top_ref, bottom_ref, left_ref, right_ref, flag_s = scratch
    for even, odd, low, high, low_flags, high_flags, parity, size in (
        (even_rows_ref, odd_rows_ref, top_s, bottom_s, top_ref, bottom_ref, EVEN_ROW, 2),
        (even_cols_ref, odd_cols_ref, left_s, right_s, left_ref, right_ref, EVEN_COL, 5),
    ):
        flip = place_ref[parity] > 0
        for i in range(0, odd.shape[0], size):
            a, b = even[i : i + size].astype(jnp.float32), odd[i : i + size].astype(jnp.float32)
            for lines, out, flags in ((jnp.where(flip, b, a), low, low_flags), (jnp.where(flip, a, b), high, high_flags)):
                out[i : i + size] = layer_normalise(lines)
                flags[i : i + size] = lines[:, :, :LANES]

    def lines_of(ref):
        return ref.astype(jnp.float32)

    def merge(at, blocks, left, right, to_ref):
        low = lax.broadcasted_iota(jnp.int32, (1, TILE, 1), 1) < RADIUS
        before = left
        for c in range(len(blocks) + 1):
            after = jnp.roll(blocks[c], RADIUS, axis=1) if c < len(blocks) else right
            to = c * wide_rows * TILE + at * TILE
            to = pl.multiple_of(to, step * TILE) if not isinstance(to, int) else to
            lines = jnp.where(low, before, after).reshape(step * TILE, -1)
            to_ref[pl.ds(to, step * TILE), :] = lines.astype(jnp.bfloat16)
            before = after

    def sides(at, upper, left_ref, right_ref, lanes):
        if upper:
            at = at - half
            left, right = jnp.roll(lines_of(left_ref[pl.ds(at, step), :, lanes]), RADIUS, axis=1), lines_of(
                right_ref[pl.ds(at, step), :, lanes]
            )
        else:
            left, right = lines_of(left_ref[pl.ds(at, step), :, lanes]), jnp.roll(
                lines_of(right_ref[pl.ds(at, step), :, lanes]), RADIUS, axis=1
            )
        return left, right

    every, few = slice(None), slice(0, LANES)

    def hide_if(border, lines):
        return jnp.where(place_ref[border] > 0, INVALID, lines)

    def mark_sides(at, upper):
        left, right = sides(at, upper, left_ref, right_ref, few)
        return hide_if(2, left), hide_if(3, right)

    def band(at, ref, ref_s, first, upper):
        cut = [slice(c * TILE, (c + 1) * TILE) for c in range(cols // TILE)]
        merge(at, [ref_s[first : first + step, k, :] for k in cut], *sides(at, upper, left_s, right_s, every), xkv_ref)
        marks = hide_if(int(upper), ref[first : first + step])
        beside = [hide_if(int(upper), side) for side in mark_sides(at, upper)]
        merge(at, [marks[:, k, :] for k in cut], *beside, flag_s)

    for i in range(0, RADIUS, step):
        band(i, top_ref, top_s, i, False)
        band(RADIUS + rows + i, bottom_ref, bottom_s, i, True)

    def middle(i, upper):
        at = pl.multiple_of(i * step, step)
        own = at - RADIUS
        blocks = []
        for c in range(cols // TILE):
            first = pl.multiple_of(c * rows * TILE + own * TILE, step * TILE)
            blocks.append(xq_ref[pl.ds(first, step * TILE), :].astype(jnp.float32).reshape(step, TILE, -1))
        merge(at, blocks, *sides(at, upper, left_s, right_s, every), xkv_ref)
        marks = mark_ref[pl.ds(own, step)].astype(jnp.float32)
        marks = [marks[:, c * TILE : (c + 1) * TILE, :] for c in range(cols // TILE)]
        merge(at, marks, *mark_sides(at, upper), flag_s)
        return 0

    lax.fori_loop(RADIUS // step, half // step, lambda i, _: middle(i, False), 0)
    lax.fori_loop(half // step, (RADIUS + rows) // step, lambda i, _: middle(i, True), 0)

    first_lane = (lax.broadcasted_iota(jnp.int32, (8, LANES), 1) == 0).astype(jnp.bfloat16)
    spans = []
    for c in range(wide_cols // TILE):
        lines = flag_s[c * wide_rows * TILE : (c + 1) * wide_rows * TILE, :]
        spans.append(jnp.where(nt(first_lane, lines) > INVALID / 2, HIDDEN, 0.0))
    tall = rows // TILE
    for c in range(cols // TILE):
        for r in range(tall):
            at = slice(r * TILE * TILE, r * TILE * TILE + 2 * TILE * TILE)
            hide_ref[c * tall + r] = jnp.concatenate([spans[c][:, at], spans[c + 1][:, at]], axis=1)


def project_kernel(whole, pieces, triple_rows, place_ref, *refs):
    sources, refs = refs[: len(whole) + len(pieces)], refs[len(whole) + len(pieces) :]
    xq_ref, xkv_ref, q_s, k_s, v_s, wt, sems = refs
    channels = wt.shape[1]
    groups = channels // GROUP
    factor = HEAD_DIM ** (-0.5) * LOG2_E
    me = place_ref[ROW]
    copies = []
    for j, source in enumerate(sources):
        if j < len(whole):
            to = (me ^ whole[j]) * triple_rows
        else:
            off, start = pieces[j - len(whole)]
            to = (me ^ off) * triple_rows + place_ref[STARTS + start]
        to = pl.multiple_of(to, 16)
        copy = pltpu.make_async_copy(source, wt.at[pl.ds(to, source.shape[0]), :], sems.at[j])
        copy.start()
        copies.append(copy)
    for copy in copies:
        copy.wait()

    q_rows, kv_rows = xq_ref.shape[0], xkv_ref.shape[0]
    q_chunk, kv_chunk = q_rows, kv_rows

    def project_q(n, _):
        w = wt[pl.ds(pl.multiple_of(n * GROUP, GROUP), GROUP), :]
        for m in range(0, q_rows, q_chunk):
            q_s[n, m : m + q_chunk, :] = (nt(xq_ref[m : m + q_chunk, :], w) * factor).astype(jnp.bfloat16)
        return 0

    def project_k(n, _):
        w = wt[pl.ds(pl.multiple_of(channels + n * GROUP, GROUP), GROUP), :]
        for m in range(0, kv_rows, kv_chunk):
            k_s[n, m : m + kv_chunk, :] = nt(xkv_ref[m : m + kv_chunk, :], w).astype(jnp.bfloat16)
        return 0

    def project_v(n, _):
        w = wt[pl.ds(pl.multiple_of(2 * channels + n * GROUP, GROUP), GROUP), :]
        for m in range(0, kv_rows, kv_chunk):
            v_s[n, m : m + kv_chunk, :] = nt(xkv_ref[m : m + kv_chunk, :], w).astype(jnp.bfloat16)
        return 0

    lax.fori_loop(0, groups, project_q, 0)
    lax.fori_loop(0, groups, project_k, 0)
    lax.fori_loop(0, groups, project_v, 0)


def carrier_kernel(offsets, place_ref, wt, *refs):
    shards = len(offsets)
    finals, refs = refs[:shards], refs[shards:]
    summary_ref, wo, kce, vc_s, carriers_s, sems = refs
    per_row = summary_ref.shape[1]
    channels = wt.shape[1]
    groups = channels // GROUP
    heads = channels // HEAD_DIM
    factor = HEAD_DIM ** (-0.5)
    carriers_here = vc_s.shape[0]
    final_rows = wo.shape[0] // shards
    copies = []
    for j, off in enumerate(offsets):
        to = pl.multiple_of((place_ref[ROW] ^ off) * final_rows, 16)
        copy = pltpu.make_async_copy(finals[j].at[0:final_rows, :], wo.at[pl.ds(to, final_rows), :], sems.at[j])
        copy.start()
        copies.append(copy)
    coming = []
    sent = carriers_s.shape[0] // shards
    for j in range(shards):
        source = finals[j].at[final_rows : final_rows + sent, :]
        copy = pltpu.make_async_copy(source, carriers_s.at[j * sent : (j + 1) * sent, :], sems.at[shards + j])
        copy.start()
        coming.append(copy)
    for copy in coming:
        copy.wait()
    carriers = carriers_s[...].astype(jnp.float32)
    own = carriers[:carriers_here]
    carriers = layer_normalise(carriers).astype(jnp.bfloat16)
    own_norm = layer_normalise(own).astype(jnp.bfloat16)
    qc = (nt(own_norm, wt[:channels, :]) * factor).astype(jnp.bfloat16).astype(jnp.float32)
    kc = nt(carriers, wt[channels : 2 * channels, :]).astype(jnp.bfloat16)
    vc = nt(carriers, wt[2 * channels :, :]).astype(jnp.bfloat16)
    head_of = lax.broadcasted_iota(jnp.int32, (1, channels), 1) // HEAD_DIM
    stacked = jnp.concatenate([jnp.where(head_of == h, qc, 0.0) for h in range(heads)], axis=0)
    e = jnp.exp(nt(stacked.astype(jnp.bfloat16), kc))
    weights = (e / jnp.sum(e, axis=-1, keepdims=True)).astype(jnp.bfloat16)
    o = nn(weights, vc)
    mix = jnp.zeros((carriers_here, channels), jnp.float32)
    for h in range(heads):
        mix = jnp.where(head_of == h, o[h * carriers_here : (h + 1) * carriers_here, :], mix)
    for copy in copies:
        copy.wait()
    renewed = own + nt(mix.astype(jnp.bfloat16), wo[...])
    for i in range(summary_ref.shape[0]):
        summary_ref[i] = renewed[i * per_row : (i + 1) * per_row, :].astype(jnp.bfloat16)
    fresh = nt(layer_normalise(renewed).astype(jnp.bfloat16), wt[channels:, :]).astype(jnp.bfloat16).astype(jnp.float32)
    vc_s[...] = fresh[:, channels:]
    same = (
        lax.broadcasted_iota(jnp.int32, (GROUP, GROUP), 0) // HEAD_DIM
        == lax.broadcasted_iota(jnp.int32, (GROUP, GROUP), 1) // HEAD_DIM
    )
    windows = kce.shape[0] // groups
    for w in range(windows):
        for g in range(groups):
            kce[w * groups + g] = jnp.where(same, fresh[w : w + 1, g * GROUP : (g + 1) * GROUP], 0.0).astype(jnp.bfloat16)


def attend_kernel(tall, broad, q_s, k_s, v_s, hide_ref, kce, vc_s, mix_s, pc_s, even_s, odd_s):
    groups, tiles = q_s.shape[0], hide_ref.shape[0]
    heads_in = GROUP // HEAD_DIM
    queries, span = TILE * TILE, 2 * TILE * TILE
    side = PATCH_SIDE // TILE
    wide = (tall + 1) * queries
    qi = lax.broadcasted_iota(jnp.int32, (queries, 2 * span), 0)
    ki = lax.broadcasted_iota(jnp.int32, (queries, 2 * span), 1)
    row_step = (ki % span) // TILE - qi // TILE
    col_step = (ki // span) * TILE + ki % TILE - qi % TILE
    seen = (row_step >= 0) & (row_step <= 2 * RADIUS) & (col_step >= 0) & (col_step <= 2 * RADIUS)
    band = jnp.where(seen, 0.0, HIDDEN)
    group_head = lax.broadcasted_iota(jnp.int32, (1, GROUP), 1) // HEAD_DIM
    only = [jnp.where(group_head == h, 1.0, 0.0).astype(jnp.bfloat16) for h in range(heads_in)]
    in_pair = LANES // HEAD_DIM
    pair_head = lax.broadcasted_iota(jnp.int32, (1, LANES), 1) // HEAD_DIM

    for c in range(broad):
        for w in range(tall // side):
            at = slice((c * tall + w * side) * queries, (c * tall + (w + 1) * side) * queries)
            window = w * (broad // side) + c // side
            for g in range(groups):
                pc_s[at, g * GROUP : (g + 1) * GROUP] = jnp.exp2(nt(q_s[g, at, :], kce[window * groups + g]))

    def keys_at(t):
        k0 = pl.multiple_of(t // tall * wide + t % tall * queries, queries)
        return k0, pl.multiple_of(k0 + wide, queries)

    def scores(t, ref):
        q_at = pl.multiple_of(t * queries, queries)
        k0, k1 = keys_at(t)
        for g in range(groups):
            q = q_s[g, pl.ds(q_at, queries), :]
            qq = jnp.concatenate([q * mask for mask in only], axis=0)
            k = jnp.concatenate([k_s[g, pl.ds(k0, span), :], k_s[g, pl.ds(k1, span), :]], axis=0)
            ref[g] = nt(qq, k)

    def finish(t, ref):
        q_at = pl.multiple_of(t * queries, queries)
        k0, k1 = keys_at(t)
        window = t % tall // side * (broad // side) + t // tall // side
        bias = band + hide_ref[t][0:1, :]
        for g in range(groups):
            p = jnp.exp2(ref[g].reshape(heads_in, queries, 2 * span) + bias[None])
            total = jnp.sum(p, axis=-1, keepdims=True)
            v = jnp.concatenate([v_s[g, pl.ds(k0, span), :], v_s[g, pl.ds(k1, span), :]], axis=0)
            o = nn(p.reshape(heads_in * queries, 2 * span).astype(jnp.bfloat16), v).reshape(heads_in, queries, GROUP)
            v_new = vc_s[pl.ds(window, 1), g * GROUP : (g + 1) * GROUP]
            for j in range(GROUP // LANES):
                lanes = slice(j * LANES, (j + 1) * LANES)
                at = slice(g * GROUP + j * LANES, g * GROUP + (j + 1) * LANES)
                kept, kept_total = o[j * in_pair, :, lanes], total[j * in_pair]
                for h in range(1, in_pair):
                    kept = jnp.where(pair_head == h, o[j * in_pair + h, :, lanes], kept)
                    kept_total = jnp.where(pair_head == h, total[j * in_pair + h], kept_total)
                new = pc_s[pl.ds(q_at, queries), at]
                mixed = (kept + new * v_new[:, lanes]) / (kept_total + new)
                mix_s[pl.ds(q_at, queries), at] = mixed.astype(jnp.bfloat16)

    scores(0, even_s)

    def two(i, _):
        t = 2 * i
        scores(t + 1, odd_s)
        finish(t, even_s)
        scores(jnp.minimum(t + 2, tiles - 1), even_s)
        finish(t + 1, odd_s)
        return 0

    lax.fori_loop(0, tiles // 2, two, 0)


def out_kernel(x_ref, mix_s, wo, out_hbm, out_ref, out_sems):
    rows, cols, channels = x_ref.shape
    going = []
    for pair in range(cols // (2 * TILE)):
        both = slice(2 * pair * TILE, 2 * (pair + 1) * TILE)
        for g in range(channels // GROUP):
            at = slice(g * GROUP, (g + 1) * GROUP)
            w = wo[at, :]
            y = nt(mix_s[2 * pair * rows * TILE : 2 * (pair + 1) * rows * TILE, :], w).reshape(2, rows, TILE, GROUP)
            y = jnp.concatenate([y[0], y[1]], axis=1) + x_ref[:, both, at].astype(jnp.float32)
            out_ref[pair, :, :, at] = y.astype(jnp.bfloat16)
        copy = pltpu.make_async_copy(out_ref.at[pair], out_hbm.at[:, both, :], out_sems.at[pair])
        copy.start()
        going.append(copy)
    for copy in going:
        copy.wait()


def local(grid_elements, summary_vectors, triple_projection, final_projection, genuine_flags):
    rows, cols, channels = grid_elements.shape
    wide_rows, wide_cols = rows + 2 * RADIUS, cols + 2 * RADIUS
    own = summary_vectors.reshape(-1, channels)

    triple_t, final_t = triple_projection.T, final_projection.T
    vmem = pl.BlockSpec(memory_space=pltpu.VMEM)
    anywhere = pl.BlockSpec(memory_space=pl.ANY)
    scalars = pl.BlockSpec(memory_space=pltpu.SMEM)
    hbm = pl.BlockSpec(memory_space=pltpu.HBM)
    small = pltpu.CompilerParams(vmem_limit_bytes=16 * 1024 * 1024)
    row_strip = jax.ShapeDtypeStruct((RADIUS, cols, channels), jnp.bfloat16)
    col_strip = jax.ShapeDtypeStruct((wide_rows // 2, 2 * RADIUS, channels), jnp.bfloat16)

    row, col, img = lax.axis_size("row"), lax.axis_size("col"), lax.axis_size("img")
    row_at, col_at, img_at = lax.axis_index("row"), lax.axis_index("col"), lax.axis_index("img")
    row_bits = bits_of(row)
    far, rest = row_bits[0], row_bits[1:]
    relays = img if triple_t.shape[0] % (16 * (img + 1)) == 0 else 0
    piece_rows = triple_t.shape[0] // (relays + 1)
    starts = [(img_at - k) % img for k in range(relays)] + [jnp.int32(relays)]
    place = [row_at == 0, row_at == row - 1, col_at == 0, col_at == col - 1, row_at % 2 == 0, col_at % 2 == 0, row_at]
    place = jnp.stack([jnp.asarray(p).astype(jnp.int32) for p in place + [start * piece_rows for start in starts]])

    mark, even_rows, odd_rows, mine, last, x = pl.pallas_call(
        functools.partial(edge_kernel, piece_rows),
        out_shape=(
            jax.ShapeDtypeStruct((rows, cols, LANES), jnp.bfloat16),
            row_strip,
            row_strip,
            jax.ShapeDtypeStruct((piece_rows, channels), jnp.bfloat16),
            jax.ShapeDtypeStruct((triple_t.shape[0] - relays * piece_rows, channels), jnp.bfloat16),
            jax.ShapeDtypeStruct(grid_elements.shape, jnp.bfloat16),
        ),
        in_specs=[scalars, hbm, hbm, hbm],
        out_specs=(vmem,) * 6,
        scratch_shapes=[
            pltpu.VMEM((rows, cols), jnp.int32),
            pltpu.VMEM((rows * cols, cols), jnp.bfloat16),
            pltpu.SemaphoreType.DMA((4,)),
        ],
        compiler_params=small,
        cost_estimate=pl.CostEstimate(flops=1_000_000, bytes_accessed=2_000_000, transcendentals=0),
        name="edge_rows",
    )(place, *(pltpu.with_memory_space_constraint(a, pltpu.HBM) for a in (genuine_flags, grid_elements, triple_t)))
    even_rows, odd_rows = pair_swapped(even_rows, odd_rows, "row")

    far_pieces = []
    if relays:
        first = swapped(mine, "row", far)
    far_last = swapped(after(last, even_rows, odd_rows), "row", far)

    carrier_tiles = -(-own.shape[0] // TILE)
    even_cols, odd_cols = pl.pallas_call(
        strip_kernel,
        out_shape=(jax.ShapeDtypeStruct((col_strip.shape[0] + carrier_tiles, *col_strip.shape[1:]), jnp.bfloat16), col_strip),
        in_specs=[scalars] + [vmem] * 5,
        out_specs=(vmem,) * 2,
        scratch_shapes=[pltpu.VMEM((carrier_tiles * TILE, channels), jnp.float32)],
        compiler_params=small,
        cost_estimate=pl.CostEstimate(flops=1_000_000, bytes_accessed=2_000_000, transcendentals=0),
        name="edge_columns",
    )(place, x, mark, even_rows, odd_rows, summary_vectors)
    even_cols, odd_cols = pair_swapped(even_cols, odd_cols, "col")
    carriers = even_cols[col_strip.shape[0] :].reshape(-1, channels)[: own.shape[0]]
    carriers = jnp.concatenate([own, carriers], axis=0)
    for bit in bits_of(col)[:-1]:
        got = swapped(carriers, "col", bit)
        carriers = jnp.concatenate([carriers, got], axis=0)
    if relays:
        first = after(first, even_cols, odd_cols)
        others = [lax.ppermute(first, "img", [(i, (i + k) % img) for i in range(img)]) for k in range(1, relays)]
        far_pieces = [first] + others
    far_pieces.append(far_last)

    final_pack = jnp.concatenate([final_t, carriers], axis=0)
    finals, triples, offsets = [final_pack], [triple_t], [0]
    for bit in rest:
        finals = finals + [swapped(p, "row", bit) for p in finals]
        triples = triples + [swapped(p, "row", bit) for p in triples]
        offsets = offsets + [o ^ bit for o in offsets]
    tiles = (rows // TILE) * (cols // TILE)
    keys = 4 * TILE * TILE
    xq = pl.pallas_call(
        own_kernel,
        out_shape=jax.ShapeDtypeStruct((rows * cols, channels), jnp.bfloat16),
        in_specs=[vmem],
        out_specs=vmem,
        compiler_params=small,
        cost_estimate=pl.CostEstimate(flops=10_000_000, bytes_accessed=3_000_000, transcendentals=1000),
        name="own_norm",
    )(x)
    xkv, hide = pl.pallas_call(
        halo_kernel,
        out_shape=(
            jax.ShapeDtypeStruct((wide_rows * wide_cols, channels), jnp.bfloat16),
            jax.ShapeDtypeStruct((tiles, 8, keys), jnp.float32),
        ),
        in_specs=[scalars] + [vmem] * 6,
        out_specs=(vmem,) * 2,
        scratch_shapes=[
            *[pltpu.VMEM(shape.shape, jnp.float32) for shape in (row_strip, row_strip, col_strip, col_strip)],
            *[pltpu.VMEM((*shape.shape[:2], LANES), jnp.float32) for shape in (row_strip, row_strip, col_strip, col_strip)],
            pltpu.VMEM((wide_rows * wide_cols, LANES), jnp.bfloat16),
        ],
        compiler_params=pltpu.CompilerParams(vmem_limit_bytes=24 * 1024 * 1024),
        cost_estimate=pl.CostEstimate(flops=10_000_000, bytes_accessed=6_000_000, transcendentals=1000),
        name="halo_norm",
    )(place, after(xq, got), mark, even_rows, odd_rows, even_cols, odd_cols)

    far_final = swapped(final_pack, "row", far)

    far_offsets = [far]
    far_pieces = [[after(piece, xkv)] for piece in far_pieces]
    for bit in rest:
        far_pieces = [same + [swapped(p, "row", bit) for p in same] for same in far_pieces]
        far_offsets = far_offsets + [o ^ bit for o in far_offsets]

    groups = channels // GROUP
    numbered = [(off, number) for number in range(len(far_pieces)) for off in far_offsets]
    sources = triples + [piece for same in far_pieces for piece in same]
    q, k, v, wt = pl.pallas_call(
        functools.partial(project_kernel, offsets, numbered, triple_t.shape[0]),
        out_shape=(
            jax.ShapeDtypeStruct((groups, rows * cols, GROUP), jnp.bfloat16),
            jax.ShapeDtypeStruct((groups, wide_rows * wide_cols, GROUP), jnp.bfloat16),
            jax.ShapeDtypeStruct((groups, wide_rows * wide_cols, GROUP), jnp.bfloat16),
            jax.ShapeDtypeStruct((3 * channels, channels), jnp.bfloat16),
        ),
        in_specs=[scalars] + [anywhere] * len(sources) + [vmem] * 2,
        out_specs=(vmem,) * 4,
        scratch_shapes=[pltpu.SemaphoreType.DMA((len(sources),))],
        compiler_params=pltpu.CompilerParams(vmem_limit_bytes=VMEM_BYTES),
        cost_estimate=pl.CostEstimate(flops=5_000_000_000, bytes_accessed=14_000_000, transcendentals=0),
        name="project",
    )(place, *sources, xq, xkv)

    far_finals = [after(far_final, q)]
    for bit in rest:
        far_finals = far_finals + [swapped(p, "row", bit) for p in far_finals]
    finals, offsets = finals + far_finals, offsets + far_offsets
    carriers_here = carrier_tiles * TILE
    summary_result, wo, kce, vc = pl.pallas_call(
        functools.partial(carrier_kernel, offsets),
        out_shape=(
            jax.ShapeDtypeStruct(summary_vectors.shape, jnp.bfloat16),
            jax.ShapeDtypeStruct((channels, channels), jnp.bfloat16),
            jax.ShapeDtypeStruct((own.shape[0] * groups, GROUP, GROUP), jnp.bfloat16),
            jax.ShapeDtypeStruct((carriers_here, channels), jnp.float32),
        ),
        in_specs=[scalars, vmem] + [anywhere] * len(finals),
        out_specs=(vmem,) * 4,
        scratch_shapes=[
            pltpu.VMEM((row * col * own.shape[0], channels), jnp.bfloat16),
            pltpu.SemaphoreType.DMA((2 * len(finals),)),
        ],
        compiler_params=pltpu.CompilerParams(vmem_limit_bytes=VMEM_BYTES),
        cost_estimate=pl.CostEstimate(flops=500_000_000, bytes_accessed=5_000_000, transcendentals=10_000),
        name="carriers",
    )(place, wt, *finals)

    scores = (groups, GROUP // HEAD_DIM * TILE * TILE, keys)
    mix = pl.pallas_call(
        functools.partial(attend_kernel, rows // TILE, cols // TILE),
        out_shape=jax.ShapeDtypeStruct((rows * cols, channels), jnp.bfloat16),
        in_specs=[vmem] * 6,
        out_specs=vmem,
        scratch_shapes=[
            pltpu.VMEM((rows * cols, channels), jnp.float32),
            pltpu.VMEM(scores, jnp.float32),
            pltpu.VMEM(scores, jnp.float32),
        ],
        compiler_params=pltpu.CompilerParams(vmem_limit_bytes=VMEM_BYTES),
        cost_estimate=pl.CostEstimate(flops=4_000_000_000, bytes_accessed=12_000_000, transcendentals=4_000_000),
        name="attend",
    )(q, k, v, hide, kce, vc)

    out = pl.pallas_call(
        out_kernel,
        out_shape=jax.ShapeDtypeStruct(grid_elements.shape, jnp.bfloat16),
        in_specs=[vmem] * 3,
        out_specs=anywhere,
        scratch_shapes=[
            pltpu.VMEM((cols // (2 * TILE), rows, 2 * TILE, channels), jnp.bfloat16),
            pltpu.SemaphoreType.DMA((cols // (2 * TILE),)),
        ],
        compiler_params=pltpu.CompilerParams(vmem_limit_bytes=VMEM_BYTES),
        cost_estimate=pl.CostEstimate(flops=1_200_000_000, bytes_accessed=6_000_000, transcendentals=0),
        name="out",
    )(x, mix, wo)
    return (out, summary_result)


def solution(mesh):
    placed = (
        P(("img", "row"), "col", None),
        P(("img", "row"), "col", None),
        P(None, "row"),
        P(None, "row"),
        P(("img", "row"), "col"),
    )
    return jax.shard_map(
        local,
        mesh=mesh,
        in_specs=placed,
        out_specs=(P(("img", "row"), "col", None), P(("img", "row"), "col", None)),
        check_vma=False,
    )
```

```python
import functools

import jax
import jax.numpy as jnp
from jax import lax
from jax.experimental import pallas as pl
from jax.experimental.pallas import tpu as pltpu
from jax.sharding import PartitionSpec as P

HEAD_DIM = 64
PATCH_SIDE = 16
RADIUS = 4
TILE = 2 * RADIUS
LANES = 128
GROUP = 256
INVALID = 100.0
HIDDEN = -1e30
LOG2_E = 1.4426950408889634
EVEN_ROW, EVEN_COL, ROW, STARTS = 4, 5, 6, 7
VMEM_BYTES = 26 * 1024 * 1024


def nt(a, b):
    return lax.dot_general(a, b, (((1,), (1,)), ((), ())), preferred_element_type=jnp.float32)


def nn(a, b):
    return lax.dot_general(a, b, (((1,), (0,)), ((), ())), preferred_element_type=jnp.float32)


def layer_normalise(lines):
    center = lines - jnp.mean(lines, axis=-1, keepdims=True)
    spread = jnp.mean(center * center, axis=-1, keepdims=True)
    return center * lax.rsqrt(spread + 1e-05)


def pair_swapped(even_block, odd_block, axis):
    count = lax.axis_size(axis)
    got = []
    for first, block in ((0, even_block), (1, odd_block)):
        pairs = [(i, i + 1) for i in range(first, count - 1, 2)]
        got.append(lax.ppermute(block, axis, pairs + [(b, a) for a, b in pairs]))
    return got


def swapped(block, axis, bit):
    count = lax.axis_size(axis)
    return lax.ppermute(block, axis, [(i, i ^ bit) for i in range(count)])


def after(block, *others):
    return lax.optimization_barrier((block, *others))[0]


def bits_of(count):
    bits, bit = [], count // 2
    while bit:
        bits.append(bit)
        bit //= 2
    return bits


def marked_lanes(lines, hidden):
    first = jnp.where(hidden, INVALID, lines[:, :, :LANES])
    return jnp.concatenate([first, lines[:, :, LANES:]], axis=2)


def edge_kernel(place_ref, flags_hbm, x_hbm, mark_ref, even_ref, odd_ref, x_ref, *scratch):
    flags_ref, spread, sems = scratch
    rows, cols = flags_ref.shape
    flags_copy = pltpu.make_async_copy(flags_hbm, flags_ref, sems.at[0])
    x_copy = pltpu.make_async_copy(x_hbm, x_ref, sems.at[1])
    flags_copy.start()
    x_copy.start()
    flags_copy.wait()
    row_at = lax.broadcasted_iota(jnp.int32, (cols, cols), 0)
    diagonal = row_at == lax.broadcasted_iota(jnp.int32, (cols, cols), 1)
    for r in range(rows):
        hidden = jnp.where(flags_ref[r : r + 1, :] > 0, 0.0, INVALID)
        spread[r * cols : (r + 1) * cols, :] = jnp.where(diagonal, hidden, 0.0).astype(jnp.bfloat16)
    marks = nn(spread[...], jnp.ones((cols, LANES), jnp.bfloat16)).reshape(rows, cols, LANES)
    mark_ref[...] = marks.astype(jnp.bfloat16)
    x_copy.wait()
    first, last = [
        marked_lanes(x_ref[at].astype(jnp.float32), marks[at] > INVALID / 2)
        for at in (slice(0, RADIUS), slice(rows - RADIUS, rows))
    ]
    even = place_ref[EVEN_ROW] > 0
    even_ref[...] = jnp.where(even, last, first).astype(jnp.bfloat16)
    odd_ref[...] = jnp.where(even, first, last).astype(jnp.bfloat16)


def piece_kernel(place_ref, triple_hbm, mine_hbm, last_hbm, sems):
    start = pl.multiple_of(place_ref[STARTS], 16)
    last = triple_hbm.shape[0] - last_hbm.shape[0]
    copies = [
        pltpu.make_async_copy(triple_hbm.at[pl.ds(start, mine_hbm.shape[0]), :], mine_hbm, sems.at[0]),
        pltpu.make_async_copy(triple_hbm.at[last:, :], last_hbm, sems.at[1]),
    ]
    for copy in copies:
        copy.start()
    for copy in copies:
        copy.wait()


def strip_kernel(place_ref, x_ref, mark_ref, even_rows_ref, odd_rows_ref, carriers_ref, even_ref, odd_ref, carriers_s):
    per_row = carriers_ref.shape[1]
    carriers_s[...] = jnp.zeros_like(carriers_s)
    for i in range(carriers_ref.shape[0]):
        carriers_s[i * per_row : (i + 1) * per_row, :] = carriers_ref[i].astype(jnp.float32)
    for i in range(carriers_s.shape[0] // TILE):
        even_ref[odd_ref.shape[0] + i] = carriers_s[i * TILE : (i + 1) * TILE, :].astype(jnp.bfloat16)
    rows, cols, channels = x_ref.shape
    middle = rows // 2
    low = lax.broadcasted_iota(jnp.int32, (1, TILE, 1), 1) < RADIUS
    even_row, even_col = place_ref[EVEN_ROW] > 0, place_ref[EVEN_COL] > 0
    for lane in range(0, channels, LANES):
        lanes = slice(lane, lane + LANES)
        strips = []
        for columns, last in ((slice(0, TILE), False), (slice(cols - TILE, cols), True)):

            def own(part):
                lines = x_ref[part, columns, lanes].astype(jnp.float32)
                if lane == 0:
                    lines = jnp.where(mark_ref[part, columns, :].astype(jnp.float32) > INVALID / 2, INVALID, lines)
                return lines

            even_rows = even_rows_ref[:, columns, lanes].astype(jnp.float32)
            odd_rows = odd_rows_ref[:, columns, lanes].astype(jnp.float32)
            top, bottom = jnp.where(even_row, odd_rows, even_rows), jnp.where(even_row, even_rows, odd_rows)
            upper = jnp.concatenate([top, own(slice(0, middle))], axis=0)
            lower = jnp.concatenate([own(slice(middle, rows)), bottom], axis=0)
            if last:
                upper = jnp.roll(upper, RADIUS, axis=1)
            else:
                lower = jnp.roll(lower, RADIUS, axis=1)
            strips.append(jnp.where(low, upper, lower))
        first, last = strips
        even_ref[: odd_ref.shape[0], :, lanes] = jnp.where(even_col, last, first).astype(jnp.bfloat16)
        odd_ref[:, :, lanes] = jnp.where(even_col, first, last).astype(jnp.bfloat16)


def own_kernel(x_ref, xq_ref):
    rows, cols, _ = x_ref.shape
    step = 4

    def own(i, _):
        at = pl.multiple_of(i * step, step)
        y = layer_normalise(x_ref[pl.ds(at, step)].astype(jnp.float32))
        for c in range(cols // TILE):
            piece = y[:, c * TILE : (c + 1) * TILE, :].reshape(step * TILE, -1)
            to = pl.multiple_of(c * rows * TILE + at * TILE, step * TILE)
            xq_ref[pl.ds(to, step * TILE), :] = piece.astype(jnp.bfloat16)
        return 0

    lax.fori_loop(0, rows // step, own, 0)


def halo_kernel(place_ref, xq_ref, mark_ref, even_rows_ref, odd_rows_ref, even_cols_ref, odd_cols_ref, xkv_ref, hide_ref, *scratch):
    rows, cols, _ = mark_ref.shape
    wide_rows, wide_cols = rows + 2 * RADIUS, cols + 2 * RADIUS
    half = wide_rows // 2
    step = 2
    top_s, bottom_s, left_s, right_s, top_ref, bottom_ref, left_ref, right_ref, flag_s = scratch
    for even, odd, low, high, low_flags, high_flags, parity, size in (
        (even_rows_ref, odd_rows_ref, top_s, bottom_s, top_ref, bottom_ref, EVEN_ROW, 2),
        (even_cols_ref, odd_cols_ref, left_s, right_s, left_ref, right_ref, EVEN_COL, 5),
    ):
        flip = place_ref[parity] > 0
        for i in range(0, odd.shape[0], size):
            a, b = even[i : i + size].astype(jnp.float32), odd[i : i + size].astype(jnp.float32)
            for lines, out, flags in ((jnp.where(flip, b, a), low, low_flags), (jnp.where(flip, a, b), high, high_flags)):
                out[i : i + size] = layer_normalise(lines)
                flags[i : i + size] = lines[:, :, :LANES]

    def lines_of(ref):
        return ref.astype(jnp.float32)

    def merge(at, blocks, left, right, to_ref):
        low = lax.broadcasted_iota(jnp.int32, (1, TILE, 1), 1) < RADIUS
        before = left
        for c in range(len(blocks) + 1):
            after = jnp.roll(blocks[c], RADIUS, axis=1) if c < len(blocks) else right
            to = c * wide_rows * TILE + at * TILE
            to = pl.multiple_of(to, step * TILE) if not isinstance(to, int) else to
            lines = jnp.where(low, before, after).reshape(step * TILE, -1)
            to_ref[pl.ds(to, step * TILE), :] = lines.astype(jnp.bfloat16)
            before = after

    def sides(at, upper, left_ref, right_ref, lanes):
        if upper:
            at = at - half
            left, right = jnp.roll(lines_of(left_ref[pl.ds(at, step), :, lanes]), RADIUS, axis=1), lines_of(
                right_ref[pl.ds(at, step), :, lanes]
            )
        else:
            left, right = lines_of(left_ref[pl.ds(at, step), :, lanes]), jnp.roll(
                lines_of(right_ref[pl.ds(at, step), :, lanes]), RADIUS, axis=1
            )
        return left, right

    every, few = slice(None), slice(0, LANES)

    def hide_if(border, lines):
        return jnp.where(place_ref[border] > 0, INVALID, lines)

    def mark_sides(at, upper):
        left, right = sides(at, upper, left_ref, right_ref, few)
        return hide_if(2, left), hide_if(3, right)

    def band(at, ref, ref_s, first, upper):
        cut = [slice(c * TILE, (c + 1) * TILE) for c in range(cols // TILE)]
        merge(at, [ref_s[first : first + step, k, :] for k in cut], *sides(at, upper, left_s, right_s, every), xkv_ref)
        marks = hide_if(int(upper), ref[first : first + step])
        beside = [hide_if(int(upper), side) for side in mark_sides(at, upper)]
        merge(at, [marks[:, k, :] for k in cut], *beside, flag_s)

    for i in range(0, RADIUS, step):
        band(i, top_ref, top_s, i, False)
        band(RADIUS + rows + i, bottom_ref, bottom_s, i, True)

    def middle(i, upper):
        at = pl.multiple_of(i * step, step)
        own = at - RADIUS
        blocks = []
        for c in range(cols // TILE):
            first = pl.multiple_of(c * rows * TILE + own * TILE, step * TILE)
            blocks.append(xq_ref[pl.ds(first, step * TILE), :].astype(jnp.float32).reshape(step, TILE, -1))
        merge(at, blocks, *sides(at, upper, left_s, right_s, every), xkv_ref)
        marks = mark_ref[pl.ds(own, step)].astype(jnp.float32)
        marks = [marks[:, c * TILE : (c + 1) * TILE, :] for c in range(cols // TILE)]
        merge(at, marks, *mark_sides(at, upper), flag_s)
        return 0

    lax.fori_loop(RADIUS // step, half // step, lambda i, _: middle(i, False), 0)
    lax.fori_loop(half // step, (RADIUS + rows) // step, lambda i, _: middle(i, True), 0)

    first_lane = (lax.broadcasted_iota(jnp.int32, (8, LANES), 1) == 0).astype(jnp.bfloat16)
    spans = []
    for c in range(wide_cols // TILE):
        lines = flag_s[c * wide_rows * TILE : (c + 1) * wide_rows * TILE, :]
        spans.append(jnp.where(nt(first_lane, lines) > INVALID / 2, HIDDEN, 0.0))
    tall = rows // TILE
    for c in range(cols // TILE):
        for r in range(tall):
            at = slice(r * TILE * TILE, r * TILE * TILE + 2 * TILE * TILE)
            hide_ref[c * tall + r] = jnp.concatenate([spans[c][:, at], spans[c + 1][:, at]], axis=1)


def project_kernel(whole, pieces, triple_rows, place_ref, *refs):
    sources, refs = refs[: len(whole) + len(pieces)], refs[len(whole) + len(pieces) :]
    xq_ref, xkv_ref, q_s, k_s, v_s, wt, sems = refs
    channels = wt.shape[1]
    groups = channels // GROUP
    factor = HEAD_DIM ** (-0.5) * LOG2_E
    me = place_ref[ROW]
    copies = []
    for j, source in enumerate(sources):
        if j < len(whole):
            to = (me ^ whole[j]) * triple_rows
        else:
            off, start = pieces[j - len(whole)]
            to = (me ^ off) * triple_rows + place_ref[STARTS + start]
        to = pl.multiple_of(to, 16)
        copy = pltpu.make_async_copy(source, wt.at[pl.ds(to, source.shape[0]), :], sems.at[j])
        copy.start()
        copies.append(copy)
    for copy in copies:
        copy.wait()

    q_rows, kv_rows = xq_ref.shape[0], xkv_ref.shape[0]
    q_chunk, kv_chunk = q_rows // 2, kv_rows // 4

    def project_q(n, _):
        w = wt[pl.ds(pl.multiple_of(n * GROUP, GROUP), GROUP), :]
        for m in range(0, q_rows, q_chunk):
            q_s[n, m : m + q_chunk, :] = (nt(xq_ref[m : m + q_chunk, :], w) * factor).astype(jnp.bfloat16)
        return 0

    def project_k(n, _):
        w = wt[pl.ds(pl.multiple_of(channels + n * GROUP, GROUP), GROUP), :]
        for m in range(0, kv_rows, kv_chunk):
            k_s[n, m : m + kv_chunk, :] = nt(xkv_ref[m : m + kv_chunk, :], w).astype(jnp.bfloat16)
        return 0

    def project_v(n, _):
        w = wt[pl.ds(pl.multiple_of(2 * channels + n * GROUP, GROUP), GROUP), :]
        for m in range(0, kv_rows, kv_chunk):
            v_s[n, m : m + kv_chunk, :] = nt(xkv_ref[m : m + kv_chunk, :], w).astype(jnp.bfloat16)
        return 0

    lax.fori_loop(0, groups, project_q, 0)
    lax.fori_loop(0, groups, project_k, 0)
    lax.fori_loop(0, groups, project_v, 0)


def carrier_kernel(offsets, place_ref, wt, *refs):
    shards = len(offsets)
    finals, refs = refs[:shards], refs[shards:]
    summary_ref, wo, kce, vc_s, carriers_s, sems = refs
    per_row = summary_ref.shape[1]
    channels = wt.shape[1]
    groups = channels // GROUP
    heads = channels // HEAD_DIM
    factor = HEAD_DIM ** (-0.5)
    carriers_here = vc_s.shape[0]
    final_rows = wo.shape[0] // shards
    copies = []
    for j, off in enumerate(offsets):
        to = pl.multiple_of((place_ref[ROW] ^ off) * final_rows, 16)
        copy = pltpu.make_async_copy(finals[j].at[0:final_rows, :], wo.at[pl.ds(to, final_rows), :], sems.at[j])
        copy.start()
        copies.append(copy)
    coming = []
    sent = carriers_s.shape[0] // shards
    for j in range(shards):
        source = finals[j].at[final_rows : final_rows + sent, :]
        copy = pltpu.make_async_copy(source, carriers_s.at[j * sent : (j + 1) * sent, :], sems.at[shards + j])
        copy.start()
        coming.append(copy)
    for copy in coming:
        copy.wait()
    carriers = carriers_s[...].astype(jnp.float32)
    own = carriers[:carriers_here]
    carriers = layer_normalise(carriers).astype(jnp.bfloat16)
    own_norm = layer_normalise(own).astype(jnp.bfloat16)
    qc = (nt(own_norm, wt[:channels, :]) * factor).astype(jnp.bfloat16).astype(jnp.float32)
    kc = nt(carriers, wt[channels : 2 * channels, :]).astype(jnp.bfloat16)
    vc = nt(carriers, wt[2 * channels :, :]).astype(jnp.bfloat16)
    head_of = lax.broadcasted_iota(jnp.int32, (1, channels), 1) // HEAD_DIM
    stacked = jnp.concatenate([jnp.where(head_of == h, qc, 0.0) for h in range(heads)], axis=0)
    e = jnp.exp(nt(stacked.astype(jnp.bfloat16), kc))
    weights = (e / jnp.sum(e, axis=-1, keepdims=True)).astype(jnp.bfloat16)
    o = nn(weights, vc)
    mix = jnp.zeros((carriers_here, channels), jnp.float32)
    for h in range(heads):
        mix = jnp.where(head_of == h, o[h * carriers_here : (h + 1) * carriers_here, :], mix)
    for copy in copies:
        copy.wait()
    renewed = own + nt(mix.astype(jnp.bfloat16), wo[...])
    for i in range(summary_ref.shape[0]):
        summary_ref[i] = renewed[i * per_row : (i + 1) * per_row, :].astype(jnp.bfloat16)
    fresh = nt(layer_normalise(renewed).astype(jnp.bfloat16), wt[channels:, :]).astype(jnp.bfloat16).astype(jnp.float32)
    vc_s[...] = fresh[:, channels:]
    same = (
        lax.broadcasted_iota(jnp.int32, (GROUP, GROUP), 0) // HEAD_DIM
        == lax.broadcasted_iota(jnp.int32, (GROUP, GROUP), 1) // HEAD_DIM
    )
    windows = kce.shape[0] // groups
    for w in range(windows):
        for g in range(groups):
            kce[w * groups + g] = jnp.where(same, fresh[w : w + 1, g * GROUP : (g + 1) * GROUP], 0.0).astype(jnp.bfloat16)


def attend_kernel(tall, broad, q_s, k_s, v_s, hide_ref, kce, vc_s, mix_s, pc_s, even_s, odd_s):
    groups, tiles = q_s.shape[0], hide_ref.shape[0]
    heads_in = GROUP // HEAD_DIM
    queries, span = TILE * TILE, 2 * TILE * TILE
    side = PATCH_SIDE // TILE
    wide = (tall + 1) * queries
    qi = lax.broadcasted_iota(jnp.int32, (queries, 2 * span), 0)
    ki = lax.broadcasted_iota(jnp.int32, (queries, 2 * span), 1)
    row_step = (ki % span) // TILE - qi // TILE
    col_step = (ki // span) * TILE + ki % TILE - qi % TILE
    seen = (row_step >= 0) & (row_step <= 2 * RADIUS) & (col_step >= 0) & (col_step <= 2 * RADIUS)
    band = jnp.where(seen, 0.0, HIDDEN)
    group_head = lax.broadcasted_iota(jnp.int32, (1, GROUP), 1) // HEAD_DIM
    only = [jnp.where(group_head == h, 1.0, 0.0).astype(jnp.bfloat16) for h in range(heads_in)]
    in_pair = LANES // HEAD_DIM
    pair_head = lax.broadcasted_iota(jnp.int32, (1, LANES), 1) // HEAD_DIM

    for c in range(broad):
        for w in range(tall // side):
            at = slice((c * tall + w * side) * queries, (c * tall + (w + 1) * side) * queries)
            window = w * (broad // side) + c // side
            for g in range(groups):
                pc_s[at, g * GROUP : (g + 1) * GROUP] = jnp.exp2(nt(q_s[g, at, :], kce[window * groups + g]))

    def keys_at(t):
        k0 = pl.multiple_of(t // tall * wide + t % tall * queries, queries)
        return k0, pl.multiple_of(k0 + wide, queries)

    def scores(t, ref):
        q_at = pl.multiple_of(t * queries, queries)
        k0, k1 = keys_at(t)
        for g in range(groups):
            q = q_s[g, pl.ds(q_at, queries), :]
            qq = jnp.concatenate([q * mask for mask in only], axis=0)
            k = jnp.concatenate([k_s[g, pl.ds(k0, span), :], k_s[g, pl.ds(k1, span), :]], axis=0)
            ref[g] = nt(qq, k)

    def finish(t, ref):
        q_at = pl.multiple_of(t * queries, queries)
        k0, k1 = keys_at(t)
        window = t % tall // side * (broad // side) + t // tall // side
        bias = band + hide_ref[t][0:1, :]
        for g in range(groups):
            p = jnp.exp2(ref[g].reshape(heads_in, queries, 2 * span) + bias[None])
            total = jnp.sum(p, axis=-1, keepdims=True)
            v = jnp.concatenate([v_s[g, pl.ds(k0, span), :], v_s[g, pl.ds(k1, span), :]], axis=0)
            o = nn(p.reshape(heads_in * queries, 2 * span).astype(jnp.bfloat16), v).reshape(heads_in, queries, GROUP)
            v_new = vc_s[pl.ds(window, 1), g * GROUP : (g + 1) * GROUP]
            for j in range(GROUP // LANES):
                lanes = slice(j * LANES, (j + 1) * LANES)
                at = slice(g * GROUP + j * LANES, g * GROUP + (j + 1) * LANES)
                kept, kept_total = o[j * in_pair, :, lanes], total[j * in_pair]
                for h in range(1, in_pair):
                    kept = jnp.where(pair_head == h, o[j * in_pair + h, :, lanes], kept)
                    kept_total = jnp.where(pair_head == h, total[j * in_pair + h], kept_total)
                new = pc_s[pl.ds(q_at, queries), at]
                mixed = (kept + new * v_new[:, lanes]) / (kept_total + new)
                mix_s[pl.ds(q_at, queries), at] = mixed.astype(jnp.bfloat16)

    scores(0, even_s)

    def two(i, _):
        t = 2 * i
        scores(t + 1, odd_s)
        finish(t, even_s)
        scores(jnp.minimum(t + 2, tiles - 1), even_s)
        finish(t + 1, odd_s)
        return 0

    lax.fori_loop(0, tiles // 2, two, 0)


def out_kernel(x_ref, mix_s, wo, out_hbm, out_ref, out_sems):
    rows, cols, channels = x_ref.shape
    going = []
    for pair in range(cols // (2 * TILE)):
        both = slice(2 * pair * TILE, 2 * (pair + 1) * TILE)
        for g in range(channels // GROUP):
            at = slice(g * GROUP, (g + 1) * GROUP)
            w = wo[at, :]
            y = nt(mix_s[2 * pair * rows * TILE : 2 * (pair + 1) * rows * TILE, :], w).reshape(2, rows, TILE, GROUP)
            y = jnp.concatenate([y[0], y[1]], axis=1) + x_ref[:, both, at].astype(jnp.float32)
            out_ref[pair, :, :, at] = y.astype(jnp.bfloat16)
        copy = pltpu.make_async_copy(out_ref.at[pair], out_hbm.at[:, both, :], out_sems.at[pair])
        copy.start()
        going.append(copy)
    for copy in going:
        copy.wait()


def local(grid_elements, summary_vectors, triple_projection, final_projection, genuine_flags):
    rows, cols, channels = grid_elements.shape
    wide_rows, wide_cols = rows + 2 * RADIUS, cols + 2 * RADIUS
    own = summary_vectors.reshape(-1, channels)

    triple_t, final_t = triple_projection.T, final_projection.T
    vmem = pl.BlockSpec(memory_space=pltpu.VMEM)
    anywhere = pl.BlockSpec(memory_space=pl.ANY)
    scalars = pl.BlockSpec(memory_space=pltpu.SMEM)
    hbm = pl.BlockSpec(memory_space=pltpu.HBM)
    small = pltpu.CompilerParams(vmem_limit_bytes=8 * 1024 * 1024)
    row_strip = jax.ShapeDtypeStruct((RADIUS, cols, channels), jnp.bfloat16)
    col_strip = jax.ShapeDtypeStruct((wide_rows // 2, 2 * RADIUS, channels), jnp.bfloat16)

    row, col, img = lax.axis_size("row"), lax.axis_size("col"), lax.axis_size("img")
    row_at, col_at, img_at = lax.axis_index("row"), lax.axis_index("col"), lax.axis_index("img")
    row_bits = bits_of(row)
    far, rest = row_bits[0], row_bits[1:]
    relays = img if triple_t.shape[0] % (16 * (img + 1)) == 0 else 0
    piece_rows = triple_t.shape[0] // (relays + 1)
    starts = [(img_at - k) % img for k in range(relays)] + [jnp.int32(relays)]
    place = [row_at == 0, row_at == row - 1, col_at == 0, col_at == col - 1, row_at % 2 == 0, col_at % 2 == 0, row_at]
    place = jnp.stack([jnp.asarray(p).astype(jnp.int32) for p in place + [start * piece_rows for start in starts]])

    mark, even_rows, odd_rows, x = pl.pallas_call(
        edge_kernel,
        out_shape=(
            pltpu.VMEM((rows, cols, LANES), jnp.bfloat16),
            pltpu.VMEM(row_strip.shape, jnp.bfloat16),
            pltpu.VMEM(row_strip.shape, jnp.bfloat16),
            pltpu.VMEM(grid_elements.shape, jnp.bfloat16),
        ),
        in_specs=[scalars, hbm, hbm],
        out_specs=(vmem,) * 4,
        scratch_shapes=[
            pltpu.VMEM((rows, cols), jnp.int32),
            pltpu.VMEM((rows * cols, cols), jnp.bfloat16),
            pltpu.SemaphoreType.DMA((2,)),
        ],
        compiler_params=small,
        cost_estimate=pl.CostEstimate(flops=1_000_000, bytes_accessed=1_000_000, transcendentals=0),
        name="edge_rows",
    )(place, *(pltpu.with_memory_space_constraint(a, pltpu.HBM) for a in (genuine_flags, grid_elements)))
    mine, last = pl.pallas_call(
        piece_kernel,
        out_shape=(
            pltpu.HBM((piece_rows, channels), jnp.bfloat16),
            pltpu.HBM((triple_t.shape[0] - relays * piece_rows, channels), jnp.bfloat16),
        ),
        in_specs=[scalars, hbm],
        out_specs=(hbm, hbm),
        scratch_shapes=[pltpu.SemaphoreType.DMA((2,))],
        compiler_params=small,
        cost_estimate=pl.CostEstimate(flops=1_000_000, bytes_accessed=1_000_000, transcendentals=0),
        name="pieces",
    )(place, pltpu.with_memory_space_constraint(after(triple_t, even_rows), pltpu.HBM))
    xq = pl.pallas_call(
        own_kernel,
        out_shape=pltpu.VMEM((rows * cols, channels), jnp.bfloat16),
        in_specs=[vmem],
        out_specs=vmem,
        compiler_params=small,
        cost_estimate=pl.CostEstimate(flops=1_000_000, bytes_accessed=1_000_000, transcendentals=0),
        name="own_norm",
    )(x)
    even_rows, odd_rows = pair_swapped(even_rows, odd_rows, "row")

    far_pieces = []
    if relays:
        first = swapped(mine, "row", far)
    far_last = swapped(after(last, even_rows, odd_rows), "row", far)

    carrier_tiles = -(-own.shape[0] // TILE)
    even_cols, odd_cols = pl.pallas_call(
        strip_kernel,
        out_shape=(
            pltpu.VMEM((col_strip.shape[0] + carrier_tiles, *col_strip.shape[1:]), jnp.bfloat16),
            pltpu.VMEM(col_strip.shape, jnp.bfloat16),
        ),
        in_specs=[scalars] + [vmem] * 5,
        out_specs=(vmem,) * 2,
        scratch_shapes=[pltpu.VMEM((carrier_tiles * TILE, channels), jnp.float32)],
        compiler_params=small,
        cost_estimate=pl.CostEstimate(flops=1_000_000, bytes_accessed=2_000_000, transcendentals=0),
        name="edge_columns",
    )(place, x, after(mark, xq), even_rows, odd_rows, summary_vectors)
    even_cols, odd_cols = pair_swapped(even_cols, odd_cols, "col")
    carriers = even_cols[col_strip.shape[0] :].reshape(-1, channels)[: own.shape[0]]
    carriers = jnp.concatenate([own, carriers], axis=0)
    for bit in bits_of(col)[:-1]:
        got = swapped(carriers, "col", bit)
        carriers = jnp.concatenate([carriers, got], axis=0)
    if relays:
        first = after(first, even_cols, odd_cols)
        others = [lax.ppermute(first, "img", [(i, (i + k) % img) for i in range(img)]) for k in range(1, relays)]
        far_pieces = [first] + others
    far_pieces.append(far_last)

    final_pack = jnp.concatenate([final_t, carriers], axis=0)
    finals, triples, offsets = [final_pack], [triple_t], [0]
    for bit in rest:
        finals = finals + [swapped(p, "row", bit) for p in finals]
        triples = triples + [swapped(p, "row", bit) for p in triples]
        offsets = offsets + [o ^ bit for o in offsets]
    tiles = (rows // TILE) * (cols // TILE)
    keys = 4 * TILE * TILE
    xkv, hide = pl.pallas_call(
        halo_kernel,
        out_shape=(
            pltpu.VMEM((wide_rows * wide_cols, channels), jnp.bfloat16),
            pltpu.VMEM((tiles, 8, keys), jnp.float32),
        ),
        in_specs=[scalars] + [vmem] * 6,
        out_specs=(vmem,) * 2,
        scratch_shapes=[
            *[pltpu.VMEM(shape.shape, jnp.float32) for shape in (row_strip, row_strip, col_strip, col_strip)],
            *[pltpu.VMEM((*shape.shape[:2], LANES), jnp.float32) for shape in (row_strip, row_strip, col_strip, col_strip)],
            pltpu.VMEM((wide_rows * wide_cols, LANES), jnp.bfloat16),
        ],
        compiler_params=pltpu.CompilerParams(vmem_limit_bytes=12 * 1024 * 1024),
        cost_estimate=pl.CostEstimate(flops=10_000_000, bytes_accessed=6_000_000, transcendentals=1000),
        name="halo_norm",
    )(place, after(xq, got), mark, even_rows, odd_rows, even_cols, odd_cols)

    far_final = swapped(final_pack, "row", far)

    far_offsets = [far]
    far_pieces = [[after(piece, xkv)] for piece in far_pieces]
    for bit in rest:
        far_pieces = [same + [swapped(p, "row", bit) for p in same] for same in far_pieces]
        far_offsets = far_offsets + [o ^ bit for o in far_offsets]

    groups = channels // GROUP
    numbered = [(off, number) for number in range(len(far_pieces)) for off in far_offsets]
    sources = triples + [piece for same in far_pieces for piece in same]
    q, k, v, wt = pl.pallas_call(
        functools.partial(project_kernel, offsets, numbered, triple_t.shape[0]),
        out_shape=(
            jax.ShapeDtypeStruct((groups, rows * cols, GROUP), jnp.bfloat16),
            jax.ShapeDtypeStruct((groups, wide_rows * wide_cols, GROUP), jnp.bfloat16),
            jax.ShapeDtypeStruct((groups, wide_rows * wide_cols, GROUP), jnp.bfloat16),
            jax.ShapeDtypeStruct((3 * channels, channels), jnp.bfloat16),
        ),
        in_specs=[scalars] + [anywhere] * len(sources) + [vmem] * 2,
        out_specs=(vmem,) * 4,
        scratch_shapes=[pltpu.SemaphoreType.DMA((len(sources),))],
        compiler_params=pltpu.CompilerParams(vmem_limit_bytes=VMEM_BYTES),
        cost_estimate=pl.CostEstimate(flops=5_000_000_000, bytes_accessed=14_000_000, transcendentals=0),
        name="project",
    )(place, *sources, xq, xkv)

    far_finals = [after(far_final, q)]
    for bit in rest:
        far_finals = far_finals + [swapped(p, "row", bit) for p in far_finals]
    finals, offsets = finals + far_finals, offsets + far_offsets
    carriers_here = carrier_tiles * TILE
    summary_result, wo, kce, vc = pl.pallas_call(
        functools.partial(carrier_kernel, offsets),
        out_shape=(
            jax.ShapeDtypeStruct(summary_vectors.shape, jnp.bfloat16),
            jax.ShapeDtypeStruct((channels, channels), jnp.bfloat16),
            jax.ShapeDtypeStruct((own.shape[0] * groups, GROUP, GROUP), jnp.bfloat16),
            jax.ShapeDtypeStruct((carriers_here, channels), jnp.float32),
        ),
        in_specs=[scalars, vmem] + [anywhere] * len(finals),
        out_specs=(vmem,) * 4,
        scratch_shapes=[
            pltpu.VMEM((row * col * own.shape[0], channels), jnp.bfloat16),
            pltpu.SemaphoreType.DMA((2 * len(finals),)),
        ],
        compiler_params=pltpu.CompilerParams(vmem_limit_bytes=VMEM_BYTES),
        cost_estimate=pl.CostEstimate(flops=500_000_000, bytes_accessed=5_000_000, transcendentals=10_000),
        name="carriers",
    )(place, wt, *finals)

    scores = (groups, GROUP // HEAD_DIM * TILE * TILE, keys)
    mix = pl.pallas_call(
        functools.partial(attend_kernel, rows // TILE, cols // TILE),
        out_shape=jax.ShapeDtypeStruct((rows * cols, channels), jnp.bfloat16),
        in_specs=[vmem] * 6,
        out_specs=vmem,
        scratch_shapes=[
            pltpu.VMEM((rows * cols, channels), jnp.float32),
            pltpu.VMEM(scores, jnp.float32),
            pltpu.VMEM(scores, jnp.float32),
        ],
        compiler_params=pltpu.CompilerParams(vmem_limit_bytes=VMEM_BYTES),
        cost_estimate=pl.CostEstimate(flops=4_000_000_000, bytes_accessed=12_000_000, transcendentals=4_000_000),
        name="attend",
    )(q, k, v, hide, kce, vc)

    out = pl.pallas_call(
        out_kernel,
        out_shape=jax.ShapeDtypeStruct(grid_elements.shape, jnp.bfloat16),
        in_specs=[vmem] * 3,
        out_specs=anywhere,
        scratch_shapes=[
            pltpu.VMEM((cols // (2 * TILE), rows, 2 * TILE, channels), jnp.bfloat16),
            pltpu.SemaphoreType.DMA((cols // (2 * TILE),)),
        ],
        compiler_params=pltpu.CompilerParams(vmem_limit_bytes=VMEM_BYTES),
        cost_estimate=pl.CostEstimate(flops=1_200_000_000, bytes_accessed=6_000_000, transcendentals=0),
        name="out",
    )(x, mix, wo)
    return (out, summary_result)


def solution(mesh):
    placed = (
        P(("img", "row"), "col", None),
        P(("img", "row"), "col", None),
        P(None, "row"),
        P(None, "row"),
        P(("img", "row"), "col"),
    )
    return jax.shard_map(
        local,
        mesh=mesh,
        in_specs=placed,
        out_specs=(P(("img", "row"), "col", None), P(("img", "row"), "col", None)),
        check_vma=False,
    )
```

```python
import functools

import jax
import jax.numpy as jnp
from jax import lax
from jax.experimental import pallas as pl
from jax.experimental.pallas import tpu as pltpu
from jax.sharding import PartitionSpec as P

HEAD_DIM = 64
PATCH_SIDE = 16
RADIUS = 4
TILE = 2 * RADIUS
LANES = 128
GROUP = 256
INVALID = 100.0
HIDDEN = -1e30
LOG2_E = 1.4426950408889634
EVEN_ROW, EVEN_COL, ROW, STARTS = 4, 5, 6, 7
VMEM_BYTES = 26 * 1024 * 1024


def nt(a, b):
    return lax.dot_general(a, b, (((1,), (1,)), ((), ())), preferred_element_type=jnp.float32)


def nn(a, b):
    return lax.dot_general(a, b, (((1,), (0,)), ((), ())), preferred_element_type=jnp.float32)


def layer_normalise(lines):
    center = lines - jnp.mean(lines, axis=-1, keepdims=True)
    spread = jnp.mean(center * center, axis=-1, keepdims=True)
    return center * lax.rsqrt(spread + 1e-05)


def pair_swapped(even_block, odd_block, axis):
    count = lax.axis_size(axis)
    got = []
    for first, block in ((0, even_block), (1, odd_block)):
        pairs = [(i, i + 1) for i in range(first, count - 1, 2)]
        got.append(lax.ppermute(block, axis, pairs + [(b, a) for a, b in pairs]))
    return got


def swapped(block, axis, bit):
    count = lax.axis_size(axis)
    return lax.ppermute(block, axis, [(i, i ^ bit) for i in range(count)])


def after(block, *others):
    return lax.optimization_barrier((block, *others))[0]


def bits_of(count):
    bits, bit = [], count // 2
    while bit:
        bits.append(bit)
        bit //= 2
    return bits


def marked_lanes(lines, hidden):
    first = jnp.where(hidden, INVALID, lines[:, :, :LANES])
    return jnp.concatenate([first, lines[:, :, LANES:]], axis=2)


def edge_kernel(place_ref, flags_hbm, x_hbm, mark_ref, even_ref, odd_ref, x_ref, *scratch):
    flags_ref, spread, sems = scratch
    rows, cols = flags_ref.shape
    flags_copy = pltpu.make_async_copy(flags_hbm, flags_ref, sems.at[0])
    x_copy = pltpu.make_async_copy(x_hbm, x_ref, sems.at[1])
    flags_copy.start()
    x_copy.start()
    flags_copy.wait()
    row_at = lax.broadcasted_iota(jnp.int32, (cols, cols), 0)
    diagonal = row_at == lax.broadcasted_iota(jnp.int32, (cols, cols), 1)
    for r in range(rows):
        hidden = jnp.where(flags_ref[r : r + 1, :] > 0, 0.0, INVALID)
        spread[r * cols : (r + 1) * cols, :] = jnp.where(diagonal, hidden, 0.0).astype(jnp.bfloat16)
    marks = nn(spread[...], jnp.ones((cols, LANES), jnp.bfloat16)).reshape(rows, cols, LANES)
    mark_ref[...] = marks.astype(jnp.bfloat16)
    x_copy.wait()
    first, last = [
        marked_lanes(x_ref[at].astype(jnp.float32), marks[at] > INVALID / 2)
        for at in (slice(0, RADIUS), slice(rows - RADIUS, rows))
    ]
    even = place_ref[EVEN_ROW] > 0
    even_ref[...] = jnp.where(even, last, first).astype(jnp.bfloat16)
    odd_ref[...] = jnp.where(even, first, last).astype(jnp.bfloat16)


def piece_kernel(place_ref, triple_hbm, mine_ref, last_ref, sems):
    start = pl.multiple_of(place_ref[STARTS], 16)
    last = triple_hbm.shape[0] - last_ref.shape[0]
    copies = [
        pltpu.make_async_copy(triple_hbm.at[pl.ds(start, mine_ref.shape[0]), :], mine_ref, sems.at[0]),
        pltpu.make_async_copy(triple_hbm.at[last:, :], last_ref, sems.at[1]),
    ]
    for copy in copies:
        copy.start()
    for copy in copies:
        copy.wait()


def strip_kernel(place_ref, x_ref, mark_ref, even_rows_ref, odd_rows_ref, carriers_ref, even_ref, odd_ref, carriers_s):
    per_row = carriers_ref.shape[1]
    carriers_s[...] = jnp.zeros_like(carriers_s)
    for i in range(carriers_ref.shape[0]):
        carriers_s[i * per_row : (i + 1) * per_row, :] = carriers_ref[i].astype(jnp.float32)
    for i in range(carriers_s.shape[0] // TILE):
        even_ref[odd_ref.shape[0] + i] = carriers_s[i * TILE : (i + 1) * TILE, :].astype(jnp.bfloat16)
    rows, cols, channels = x_ref.shape
    middle = rows // 2
    low = lax.broadcasted_iota(jnp.int32, (1, TILE, 1), 1) < RADIUS
    even_row, even_col = place_ref[EVEN_ROW] > 0, place_ref[EVEN_COL] > 0
    for lane in range(0, channels, LANES):
        lanes = slice(lane, lane + LANES)
        strips = []
        for columns, last in ((slice(0, TILE), False), (slice(cols - TILE, cols), True)):

            def own(part):
                lines = x_ref[part, columns, lanes].astype(jnp.float32)
                if lane == 0:
                    lines = jnp.where(mark_ref[part, columns, :].astype(jnp.float32) > INVALID / 2, INVALID, lines)
                return lines

            even_rows = even_rows_ref[:, columns, lanes].astype(jnp.float32)
            odd_rows = odd_rows_ref[:, columns, lanes].astype(jnp.float32)
            top, bottom = jnp.where(even_row, odd_rows, even_rows), jnp.where(even_row, even_rows, odd_rows)
            upper = jnp.concatenate([top, own(slice(0, middle))], axis=0)
            lower = jnp.concatenate([own(slice(middle, rows)), bottom], axis=0)
            if last:
                upper = jnp.roll(upper, RADIUS, axis=1)
            else:
                lower = jnp.roll(lower, RADIUS, axis=1)
            strips.append(jnp.where(low, upper, lower))
        first, last = strips
        even_ref[: odd_ref.shape[0], :, lanes] = jnp.where(even_col, last, first).astype(jnp.bfloat16)
        odd_ref[:, :, lanes] = jnp.where(even_col, first, last).astype(jnp.bfloat16)


def carrier_pair_kernel(own_ref, got_hbm, out_ref, got_s, pair_s, sem):
    per_row, here = own_ref.shape[1], own_ref.shape[0] * own_ref.shape[1]
    tiles = got_s.shape[0]
    copy = pltpu.make_async_copy(got_hbm.at[got_hbm.shape[0] - tiles :], got_s, sem)
    copy.start()
    for i in range(own_ref.shape[0]):
        pair_s[i * per_row : (i + 1) * per_row, :] = own_ref[i].astype(jnp.float32)
    copy.wait()
    pair_s[here:, :] = got_s[...].astype(jnp.float32).reshape(tiles * TILE, -1)[:here]
    out_ref[...] = pair_s[...].astype(jnp.bfloat16)


def pack_kernel(final_hbm, *refs):
    parts, (out_ref, sem) = refs[:-2], refs[-2:]
    rows = final_hbm.shape[0]
    copy = pltpu.make_async_copy(final_hbm, out_ref.at[0:rows, :], sem)
    copy.start()
    carriers = jnp.concatenate([part[...].astype(jnp.float32) for part in parts], axis=0)
    out_ref[rows:, :] = carriers.astype(jnp.bfloat16)
    copy.wait()


def own_kernel(x_ref, xq_ref):
    rows, cols, _ = x_ref.shape
    step = 4

    def own(i, _):
        at = pl.multiple_of(i * step, step)
        y = layer_normalise(x_ref[pl.ds(at, step)].astype(jnp.float32))
        for c in range(cols // TILE):
            piece = y[:, c * TILE : (c + 1) * TILE, :].reshape(step * TILE, -1)
            to = pl.multiple_of(c * rows * TILE + at * TILE, step * TILE)
            xq_ref[pl.ds(to, step * TILE), :] = piece.astype(jnp.bfloat16)
        return 0

    lax.fori_loop(0, rows // step, own, 0)


def halo_kernel(place_ref, xq_ref, mark_ref, even_rows_ref, odd_rows_ref, even_cols_ref, odd_cols_ref, xkv_ref, hide_ref, *scratch):
    rows, cols, _ = mark_ref.shape
    wide_rows, wide_cols = rows + 2 * RADIUS, cols + 2 * RADIUS
    half = wide_rows // 2
    step = 2
    top_s, bottom_s, left_s, right_s, top_ref, bottom_ref, left_ref, right_ref, flag_s = scratch
    for even, odd, low, high, low_flags, high_flags, parity, size in (
        (even_rows_ref, odd_rows_ref, top_s, bottom_s, top_ref, bottom_ref, EVEN_ROW, 2),
        (even_cols_ref, odd_cols_ref, left_s, right_s, left_ref, right_ref, EVEN_COL, 5),
    ):
        flip = place_ref[parity] > 0
        for i in range(0, odd.shape[0], size):
            a, b = even[i : i + size].astype(jnp.float32), odd[i : i + size].astype(jnp.float32)
            for lines, out, flags in ((jnp.where(flip, b, a), low, low_flags), (jnp.where(flip, a, b), high, high_flags)):
                out[i : i + size] = layer_normalise(lines)
                flags[i : i + size] = lines[:, :, :LANES]

    def lines_of(ref):
        return ref.astype(jnp.float32)

    def merge(at, blocks, left, right, to_ref):
        low = lax.broadcasted_iota(jnp.int32, (1, TILE, 1), 1) < RADIUS
        before = left
        for c in range(len(blocks) + 1):
            after = jnp.roll(blocks[c], RADIUS, axis=1) if c < len(blocks) else right
            to = c * wide_rows * TILE + at * TILE
            to = pl.multiple_of(to, step * TILE) if not isinstance(to, int) else to
            lines = jnp.where(low, before, after).reshape(step * TILE, -1)
            to_ref[pl.ds(to, step * TILE), :] = lines.astype(jnp.bfloat16)
            before = after

    def sides(at, upper, left_ref, right_ref, lanes):
        if upper:
            at = at - half
            left, right = jnp.roll(lines_of(left_ref[pl.ds(at, step), :, lanes]), RADIUS, axis=1), lines_of(
                right_ref[pl.ds(at, step), :, lanes]
            )
        else:
            left, right = lines_of(left_ref[pl.ds(at, step), :, lanes]), jnp.roll(
                lines_of(right_ref[pl.ds(at, step), :, lanes]), RADIUS, axis=1
            )
        return left, right

    every, few = slice(None), slice(0, LANES)

    def hide_if(border, lines):
        return jnp.where(place_ref[border] > 0, INVALID, lines)

    def mark_sides(at, upper):
        left, right = sides(at, upper, left_ref, right_ref, few)
        return hide_if(2, left), hide_if(3, right)

    def band(at, ref, ref_s, first, upper):
        cut = [slice(c * TILE, (c + 1) * TILE) for c in range(cols // TILE)]
        merge(at, [ref_s[first : first + step, k, :] for k in cut], *sides(at, upper, left_s, right_s, every), xkv_ref)
        marks = hide_if(int(upper), ref[first : first + step])
        beside = [hide_if(int(upper), side) for side in mark_sides(at, upper)]
        merge(at, [marks[:, k, :] for k in cut], *beside, flag_s)

    for i in range(0, RADIUS, step):
        band(i, top_ref, top_s, i, False)
        band(RADIUS + rows + i, bottom_ref, bottom_s, i, True)

    def middle(i, upper):
        at = pl.multiple_of(i * step, step)
        own = at - RADIUS
        blocks = []
        for c in range(cols // TILE):
            first = pl.multiple_of(c * rows * TILE + own * TILE, step * TILE)
            blocks.append(xq_ref[pl.ds(first, step * TILE), :].astype(jnp.float32).reshape(step, TILE, -1))
        merge(at, blocks, *sides(at, upper, left_s, right_s, every), xkv_ref)
        marks = mark_ref[pl.ds(own, step)].astype(jnp.float32)
        marks = [marks[:, c * TILE : (c + 1) * TILE, :] for c in range(cols // TILE)]
        merge(at, marks, *mark_sides(at, upper), flag_s)
        return 0

    lax.fori_loop(RADIUS // step, half // step, lambda i, _: middle(i, False), 0)
    lax.fori_loop(half // step, (RADIUS + rows) // step, lambda i, _: middle(i, True), 0)

    first_lane = (lax.broadcasted_iota(jnp.int32, (8, LANES), 1) == 0).astype(jnp.bfloat16)
    spans = []
    for c in range(wide_cols // TILE):
        lines = flag_s[c * wide_rows * TILE : (c + 1) * wide_rows * TILE, :]
        spans.append(jnp.where(nt(first_lane, lines) > INVALID / 2, HIDDEN, 0.0))
    tall = rows // TILE
    for c in range(cols // TILE):
        for r in range(tall):
            at = slice(r * TILE * TILE, r * TILE * TILE + 2 * TILE * TILE)
            hide_ref[c * tall + r] = jnp.concatenate([spans[c][:, at], spans[c + 1][:, at]], axis=1)


def project_kernel(whole, pieces, triple_rows, place_ref, *refs):
    sources, refs = refs[: len(whole) + len(pieces)], refs[len(whole) + len(pieces) :]
    xq_ref, xkv_ref, q_s, k_s, v_s, wt, sems = refs
    channels = wt.shape[1]
    groups = channels // GROUP
    factor = HEAD_DIM ** (-0.5) * LOG2_E
    me = place_ref[ROW]
    copies = []
    for j, source in enumerate(sources):
        if j < len(whole):
            to = (me ^ whole[j]) * triple_rows
        else:
            off, start = pieces[j - len(whole)]
            to = (me ^ off) * triple_rows + place_ref[STARTS + start]
        to = pl.multiple_of(to, 16)
        copy = pltpu.make_async_copy(source, wt.at[pl.ds(to, source.shape[0]), :], sems.at[j])
        copy.start()
        copies.append(copy)
    for copy in copies:
        copy.wait()

    q_rows, kv_rows = xq_ref.shape[0], xkv_ref.shape[0]
    q_chunk, kv_chunk = q_rows // 2, kv_rows // 4

    def project_q(n, _):
        w = wt[pl.ds(pl.multiple_of(n * GROUP, GROUP), GROUP), :]
        for m in range(0, q_rows, q_chunk):
            q_s[n, m : m + q_chunk, :] = (nt(xq_ref[m : m + q_chunk, :], w) * factor).astype(jnp.bfloat16)
        return 0

    def project_k(n, _):
        w = wt[pl.ds(pl.multiple_of(channels + n * GROUP, GROUP), GROUP), :]
        for m in range(0, kv_rows, kv_chunk):
            k_s[n, m : m + kv_chunk, :] = nt(xkv_ref[m : m + kv_chunk, :], w).astype(jnp.bfloat16)
        return 0

    def project_v(n, _):
        w = wt[pl.ds(pl.multiple_of(2 * channels + n * GROUP, GROUP), GROUP), :]
        for m in range(0, kv_rows, kv_chunk):
            v_s[n, m : m + kv_chunk, :] = nt(xkv_ref[m : m + kv_chunk, :], w).astype(jnp.bfloat16)
        return 0

    lax.fori_loop(0, groups, project_q, 0)
    lax.fori_loop(0, groups, project_k, 0)
    lax.fori_loop(0, groups, project_v, 0)


def carrier_kernel(offsets, place_ref, wt, *refs):
    shards = len(offsets)
    finals, refs = refs[:shards], refs[shards:]
    summary_ref, wo, kce, vc_s, carriers_s, sems = refs
    per_row = summary_ref.shape[1]
    channels = wt.shape[1]
    groups = channels // GROUP
    heads = channels // HEAD_DIM
    factor = HEAD_DIM ** (-0.5)
    carriers_here = vc_s.shape[0]
    final_rows = wo.shape[0] // shards
    copies = []
    for j, off in enumerate(offsets):
        to = pl.multiple_of((place_ref[ROW] ^ off) * final_rows, 16)
        copy = pltpu.make_async_copy(finals[j].at[0:final_rows, :], wo.at[pl.ds(to, final_rows), :], sems.at[j])
        copy.start()
        copies.append(copy)
    coming = []
    sent = carriers_s.shape[0] // shards
    for j in range(shards):
        source = finals[j].at[final_rows : final_rows + sent, :]
        copy = pltpu.make_async_copy(source, carriers_s.at[j * sent : (j + 1) * sent, :], sems.at[shards + j])
        copy.start()
        coming.append(copy)
    for copy in coming:
        copy.wait()
    carriers = carriers_s[...].astype(jnp.float32)
    own = carriers[:carriers_here]
    carriers = layer_normalise(carriers).astype(jnp.bfloat16)
    own_norm = layer_normalise(own).astype(jnp.bfloat16)
    qc = (nt(own_norm, wt[:channels, :]) * factor).astype(jnp.bfloat16).astype(jnp.float32)
    kc = nt(carriers, wt[channels : 2 * channels, :]).astype(jnp.bfloat16)
    vc = nt(carriers, wt[2 * channels :, :]).astype(jnp.bfloat16)
    head_of = lax.broadcasted_iota(jnp.int32, (1, channels), 1) // HEAD_DIM
    stacked = jnp.concatenate([jnp.where(head_of == h, qc, 0.0) for h in range(heads)], axis=0)
    e = jnp.exp(nt(stacked.astype(jnp.bfloat16), kc))
    weights = (e / jnp.sum(e, axis=-1, keepdims=True)).astype(jnp.bfloat16)
    o = nn(weights, vc)
    mix = jnp.zeros((carriers_here, channels), jnp.float32)
    for h in range(heads):
        mix = jnp.where(head_of == h, o[h * carriers_here : (h + 1) * carriers_here, :], mix)
    for copy in copies:
        copy.wait()
    renewed = own + nt(mix.astype(jnp.bfloat16), wo[...])
    for i in range(summary_ref.shape[0]):
        summary_ref[i] = renewed[i * per_row : (i + 1) * per_row, :].astype(jnp.bfloat16)
    fresh = nt(layer_normalise(renewed).astype(jnp.bfloat16), wt[channels:, :]).astype(jnp.bfloat16).astype(jnp.float32)
    vc_s[...] = fresh[:, channels:]
    same = (
        lax.broadcasted_iota(jnp.int32, (GROUP, GROUP), 0) // HEAD_DIM
        == lax.broadcasted_iota(jnp.int32, (GROUP, GROUP), 1) // HEAD_DIM
    )
    windows = kce.shape[0] // groups
    for w in range(windows):
        for g in range(groups):
            kce[w * groups + g] = jnp.where(same, fresh[w : w + 1, g * GROUP : (g + 1) * GROUP], 0.0).astype(jnp.bfloat16)


def attend_kernel(tall, broad, q_s, k_s, v_s, hide_ref, kce, vc_s, mix_s, pc_s, even_s, odd_s):
    groups, tiles = q_s.shape[0], hide_ref.shape[0]
    heads_in = GROUP // HEAD_DIM
    queries, span = TILE * TILE, 2 * TILE * TILE
    side = PATCH_SIDE // TILE
    wide = (tall + 1) * queries
    qi = lax.broadcasted_iota(jnp.int32, (queries, 2 * span), 0)
    ki = lax.broadcasted_iota(jnp.int32, (queries, 2 * span), 1)
    row_step = (ki % span) // TILE - qi // TILE
    col_step = (ki // span) * TILE + ki % TILE - qi % TILE
    seen = (row_step >= 0) & (row_step <= 2 * RADIUS) & (col_step >= 0) & (col_step <= 2 * RADIUS)
    band = jnp.where(seen, 0.0, HIDDEN)
    group_head = lax.broadcasted_iota(jnp.int32, (1, GROUP), 1) // HEAD_DIM
    only = [jnp.where(group_head == h, 1.0, 0.0).astype(jnp.bfloat16) for h in range(heads_in)]
    in_pair = LANES // HEAD_DIM
    pair_head = lax.broadcasted_iota(jnp.int32, (1, LANES), 1) // HEAD_DIM

    for c in range(broad):
        for w in range(tall // side):
            at = slice((c * tall + w * side) * queries, (c * tall + (w + 1) * side) * queries)
            window = w * (broad // side) + c // side
            for g in range(groups):
                pc_s[at, g * GROUP : (g + 1) * GROUP] = jnp.exp2(nt(q_s[g, at, :], kce[window * groups + g]))

    def keys_at(t):
        k0 = pl.multiple_of(t // tall * wide + t % tall * queries, queries)
        return k0, pl.multiple_of(k0 + wide, queries)

    def scores(t, ref):
        q_at = pl.multiple_of(t * queries, queries)
        k0, k1 = keys_at(t)
        for g in range(groups):
            q = q_s[g, pl.ds(q_at, queries), :]
            qq = jnp.concatenate([q * mask for mask in only], axis=0)
            k = jnp.concatenate([k_s[g, pl.ds(k0, span), :], k_s[g, pl.ds(k1, span), :]], axis=0)
            ref[g] = nt(qq, k)

    def finish(t, ref):
        q_at = pl.multiple_of(t * queries, queries)
        k0, k1 = keys_at(t)
        window = t % tall // side * (broad // side) + t // tall // side
        bias = band + hide_ref[t][0:1, :]
        for g in range(groups):
            p = jnp.exp2(ref[g].reshape(heads_in, queries, 2 * span) + bias[None])
            total = jnp.sum(p, axis=-1, keepdims=True)
            v = jnp.concatenate([v_s[g, pl.ds(k0, span), :], v_s[g, pl.ds(k1, span), :]], axis=0)
            o = nn(p.reshape(heads_in * queries, 2 * span).astype(jnp.bfloat16), v).reshape(heads_in, queries, GROUP)
            v_new = vc_s[pl.ds(window, 1), g * GROUP : (g + 1) * GROUP]
            for j in range(GROUP // LANES):
                lanes = slice(j * LANES, (j + 1) * LANES)
                at = slice(g * GROUP + j * LANES, g * GROUP + (j + 1) * LANES)
                kept, kept_total = o[j * in_pair, :, lanes], total[j * in_pair]
                for h in range(1, in_pair):
                    kept = jnp.where(pair_head == h, o[j * in_pair + h, :, lanes], kept)
                    kept_total = jnp.where(pair_head == h, total[j * in_pair + h], kept_total)
                new = pc_s[pl.ds(q_at, queries), at]
                mixed = (kept + new * v_new[:, lanes]) / (kept_total + new)
                mix_s[pl.ds(q_at, queries), at] = mixed.astype(jnp.bfloat16)

    scores(0, even_s)

    def two(i, _):
        t = 2 * i
        scores(t + 1, odd_s)
        finish(t, even_s)
        scores(jnp.minimum(t + 2, tiles - 1), even_s)
        finish(t + 1, odd_s)
        return 0

    lax.fori_loop(0, tiles // 2, two, 0)


def out_kernel(x_ref, mix_s, wo, out_hbm, out_ref, out_sems):
    rows, cols, channels = x_ref.shape
    going = []
    for pair in range(cols // (2 * TILE)):
        both = slice(2 * pair * TILE, 2 * (pair + 1) * TILE)
        for g in range(channels // GROUP):
            at = slice(g * GROUP, (g + 1) * GROUP)
            w = wo[at, :]
            y = nt(mix_s[2 * pair * rows * TILE : 2 * (pair + 1) * rows * TILE, :], w).reshape(2, rows, TILE, GROUP)
            y = jnp.concatenate([y[0], y[1]], axis=1) + x_ref[:, both, at].astype(jnp.float32)
            out_ref[pair, :, :, at] = y.astype(jnp.bfloat16)
        copy = pltpu.make_async_copy(out_ref.at[pair], out_hbm.at[:, both, :], out_sems.at[pair])
        copy.start()
        going.append(copy)
    for copy in going:
        copy.wait()


def local(grid_elements, summary_vectors, triple_projection, final_projection, genuine_flags):
    rows, cols, channels = grid_elements.shape
    wide_rows, wide_cols = rows + 2 * RADIUS, cols + 2 * RADIUS

    triple_t, final_t = triple_projection.T, final_projection.T
    vmem = pl.BlockSpec(memory_space=pltpu.VMEM)
    anywhere = pl.BlockSpec(memory_space=pl.ANY)
    scalars = pl.BlockSpec(memory_space=pltpu.SMEM)
    hbm = pl.BlockSpec(memory_space=pltpu.HBM)
    small = pltpu.CompilerParams(vmem_limit_bytes=8 * 1024 * 1024)
    row_strip = jax.ShapeDtypeStruct((RADIUS, cols, channels), jnp.bfloat16)
    col_strip = jax.ShapeDtypeStruct((wide_rows // 2, 2 * RADIUS, channels), jnp.bfloat16)

    row, col, img = lax.axis_size("row"), lax.axis_size("col"), lax.axis_size("img")
    row_at, col_at, img_at = lax.axis_index("row"), lax.axis_index("col"), lax.axis_index("img")
    row_bits = bits_of(row)
    far, rest = row_bits[0], row_bits[1:]
    relays = img if triple_t.shape[0] % (16 * (img + 1)) == 0 else 0
    piece_rows = triple_t.shape[0] // (relays + 1)
    starts = [(img_at - k) % img for k in range(relays)] + [jnp.int32(relays)]
    place = [row_at == 0, row_at == row - 1, col_at == 0, col_at == col - 1, row_at % 2 == 0, col_at % 2 == 0, row_at]
    place = jnp.stack([jnp.asarray(p).astype(jnp.int32) for p in place + [start * piece_rows for start in starts]])

    mark, even_rows, odd_rows, x = pl.pallas_call(
        edge_kernel,
        out_shape=(
            pltpu.VMEM((rows, cols, LANES), jnp.bfloat16),
            pltpu.VMEM(row_strip.shape, jnp.bfloat16),
            pltpu.VMEM(row_strip.shape, jnp.bfloat16),
            pltpu.VMEM(grid_elements.shape, jnp.bfloat16),
        ),
        in_specs=[scalars, hbm, hbm],
        out_specs=(vmem,) * 4,
        scratch_shapes=[
            pltpu.VMEM((rows, cols), jnp.int32),
            pltpu.VMEM((rows * cols, cols), jnp.bfloat16),
            pltpu.SemaphoreType.DMA((2,)),
        ],
        compiler_params=small,
        cost_estimate=pl.CostEstimate(flops=1_000_000, bytes_accessed=1_000_000, transcendentals=0),
        name="edge_rows",
    )(place, *(pltpu.with_memory_space_constraint(a, pltpu.HBM) for a in (genuine_flags, grid_elements)))
    mine, last = pl.pallas_call(
        piece_kernel,
        out_shape=(
            pltpu.VMEM((piece_rows, channels), jnp.bfloat16),
            pltpu.VMEM((triple_t.shape[0] - relays * piece_rows, channels), jnp.bfloat16),
        ),
        in_specs=[scalars, hbm],
        out_specs=(vmem, vmem),
        scratch_shapes=[pltpu.SemaphoreType.DMA((2,))],
        compiler_params=small,
        cost_estimate=pl.CostEstimate(flops=1_000_000, bytes_accessed=1_000_000, transcendentals=0),
        name="pieces",
    )(place, pltpu.with_memory_space_constraint(after(triple_t, even_rows), pltpu.HBM))
    xq = pl.pallas_call(
        own_kernel,
        out_shape=pltpu.VMEM((rows * cols, channels), jnp.bfloat16),
        in_specs=[vmem],
        out_specs=vmem,
        compiler_params=small,
        cost_estimate=pl.CostEstimate(flops=1_000_000, bytes_accessed=1_000_000, transcendentals=0),
        name="own_norm",
    )(x)
    even_rows, odd_rows = pair_swapped(even_rows, odd_rows, "row")

    far_pieces = []
    if relays:
        first = swapped(mine, "row", far)
    far_last = swapped(after(last, even_rows, odd_rows), "row", far)

    own_rows = summary_vectors.shape[0] * summary_vectors.shape[1]
    carrier_tiles = -(-own_rows // TILE)
    even_cols, odd_cols = pl.pallas_call(
        strip_kernel,
        out_shape=(
            pltpu.VMEM((col_strip.shape[0] + carrier_tiles, *col_strip.shape[1:]), jnp.bfloat16),
            pltpu.VMEM(col_strip.shape, jnp.bfloat16),
        ),
        in_specs=[scalars] + [vmem] * 5,
        out_specs=(vmem,) * 2,
        scratch_shapes=[pltpu.VMEM((carrier_tiles * TILE, channels), jnp.float32)],
        compiler_params=small,
        cost_estimate=pl.CostEstimate(flops=1_000_000, bytes_accessed=2_000_000, transcendentals=0),
        name="edge_columns",
    )(place, x, after(mark, xq), even_rows, odd_rows, summary_vectors)
    even_cols, odd_cols = pair_swapped(even_cols, odd_cols, "col")
    carriers = pl.pallas_call(
        carrier_pair_kernel,
        out_shape=pltpu.VMEM((2 * own_rows, channels), jnp.bfloat16),
        in_specs=[vmem, anywhere],
        out_specs=vmem,
        scratch_shapes=[
            pltpu.VMEM((carrier_tiles, TILE, channels), jnp.bfloat16),
            pltpu.VMEM((2 * own_rows, channels), jnp.float32),
            pltpu.SemaphoreType.DMA,
        ],
        compiler_params=small,
        cost_estimate=pl.CostEstimate(flops=1_000, bytes_accessed=1_000, transcendentals=0),
        name="carrier_pair",
    )(summary_vectors, even_cols)
    parts = [carriers]
    for bit in bits_of(col)[:-1]:
        carriers = carriers if len(parts) == 1 else jnp.concatenate(parts, axis=0)
        got = swapped(carriers, "col", bit)
        parts.append(got)
    if relays:
        first = after(first, even_cols, odd_cols)
        others = [lax.ppermute(first, "img", [(i, (i + k) % img) for i in range(img)]) for k in range(1, relays)]
        far_pieces = [first] + others
    far_pieces.append(far_last)

    final_pack = pl.pallas_call(
        pack_kernel,
        out_shape=pltpu.VMEM((final_t.shape[0] + col * own_rows, channels), jnp.bfloat16),
        in_specs=[hbm] + [vmem] * len(parts),
        out_specs=vmem,
        scratch_shapes=[pltpu.SemaphoreType.DMA],
        compiler_params=small,
        cost_estimate=pl.CostEstimate(flops=1_000, bytes_accessed=1_000, transcendentals=0),
        name="final_pack",
    )(pltpu.with_memory_space_constraint(final_t, pltpu.HBM), *parts)
    finals, triples, offsets = [final_pack], [triple_t], [0]
    for bit in rest:
        finals = finals + [swapped(p, "row", bit) for p in finals]
        triples = triples + [swapped(p, "row", bit) for p in triples]
        offsets = offsets + [o ^ bit for o in offsets]
    tiles = (rows // TILE) * (cols // TILE)
    keys = 4 * TILE * TILE
    xkv, hide = pl.pallas_call(
        halo_kernel,
        out_shape=(
            pltpu.VMEM((wide_rows * wide_cols, channels), jnp.bfloat16),
            pltpu.VMEM((tiles, 8, keys), jnp.float32),
        ),
        in_specs=[scalars] + [vmem] * 6,
        out_specs=(vmem,) * 2,
        scratch_shapes=[
            *[pltpu.VMEM(shape.shape, jnp.float32) for shape in (row_strip, row_strip, col_strip, col_strip)],
            *[pltpu.VMEM((*shape.shape[:2], LANES), jnp.float32) for shape in (row_strip, row_strip, col_strip, col_strip)],
            pltpu.VMEM((wide_rows * wide_cols, LANES), jnp.bfloat16),
        ],
        compiler_params=pltpu.CompilerParams(vmem_limit_bytes=12 * 1024 * 1024),
        cost_estimate=pl.CostEstimate(flops=10_000_000, bytes_accessed=6_000_000, transcendentals=1000),
        name="halo_norm",
    )(place, after(xq, got), mark, even_rows, odd_rows, even_cols, odd_cols)

    far_final = swapped(final_pack, "row", far)

    far_offsets = [far]
    far_pieces = [[after(piece, xkv)] for piece in far_pieces]
    for bit in rest:
        far_pieces = [same + [swapped(p, "row", bit) for p in same] for same in far_pieces]
        far_offsets = far_offsets + [o ^ bit for o in far_offsets]

    groups = channels // GROUP
    numbered = [(off, number) for number in range(len(far_pieces)) for off in far_offsets]
    sources = triples + [piece for same in far_pieces for piece in same]
    q, k, v, wt = pl.pallas_call(
        functools.partial(project_kernel, offsets, numbered, triple_t.shape[0]),
        out_shape=(
            jax.ShapeDtypeStruct((groups, rows * cols, GROUP), jnp.bfloat16),
            jax.ShapeDtypeStruct((groups, wide_rows * wide_cols, GROUP), jnp.bfloat16),
            jax.ShapeDtypeStruct((groups, wide_rows * wide_cols, GROUP), jnp.bfloat16),
            jax.ShapeDtypeStruct((3 * channels, channels), jnp.bfloat16),
        ),
        in_specs=[scalars] + [anywhere] * len(sources) + [vmem] * 2,
        out_specs=(vmem,) * 4,
        scratch_shapes=[pltpu.SemaphoreType.DMA((len(sources),))],
        compiler_params=pltpu.CompilerParams(vmem_limit_bytes=VMEM_BYTES),
        cost_estimate=pl.CostEstimate(flops=5_000_000_000, bytes_accessed=14_000_000, transcendentals=0),
        name="project",
    )(place, *sources, xq, xkv)

    far_finals = [after(far_final, q)]
    for bit in rest:
        far_finals = far_finals + [swapped(p, "row", bit) for p in far_finals]
    finals, offsets = finals + far_finals, offsets + far_offsets
    carriers_here = carrier_tiles * TILE
    summary_result, wo, kce, vc = pl.pallas_call(
        functools.partial(carrier_kernel, offsets),
        out_shape=(
            jax.ShapeDtypeStruct(summary_vectors.shape, jnp.bfloat16),
            jax.ShapeDtypeStruct((channels, channels), jnp.bfloat16),
            jax.ShapeDtypeStruct((own_rows * groups, GROUP, GROUP), jnp.bfloat16),
            jax.ShapeDtypeStruct((carriers_here, channels), jnp.float32),
        ),
        in_specs=[scalars, vmem] + [anywhere] * len(finals),
        out_specs=(vmem,) * 4,
        scratch_shapes=[
            pltpu.VMEM((row * col * own_rows, channels), jnp.bfloat16),
            pltpu.SemaphoreType.DMA((2 * len(finals),)),
        ],
        compiler_params=pltpu.CompilerParams(vmem_limit_bytes=VMEM_BYTES),
        cost_estimate=pl.CostEstimate(flops=500_000_000, bytes_accessed=5_000_000, transcendentals=10_000),
        name="carriers",
    )(place, wt, *finals)

    scores = (groups, GROUP // HEAD_DIM * TILE * TILE, keys)
    mix = pl.pallas_call(
        functools.partial(attend_kernel, rows // TILE, cols // TILE),
        out_shape=jax.ShapeDtypeStruct((rows * cols, channels), jnp.bfloat16),
        in_specs=[vmem] * 6,
        out_specs=vmem,
        scratch_shapes=[
            pltpu.VMEM((rows * cols, channels), jnp.float32),
            pltpu.VMEM(scores, jnp.float32),
            pltpu.VMEM(scores, jnp.float32),
        ],
        compiler_params=pltpu.CompilerParams(vmem_limit_bytes=VMEM_BYTES),
        cost_estimate=pl.CostEstimate(flops=4_000_000_000, bytes_accessed=12_000_000, transcendentals=4_000_000),
        name="attend",
    )(q, k, v, hide, kce, vc)

    out = pl.pallas_call(
        out_kernel,
        out_shape=jax.ShapeDtypeStruct(grid_elements.shape, jnp.bfloat16),
        in_specs=[vmem] * 3,
        out_specs=anywhere,
        scratch_shapes=[
            pltpu.VMEM((cols // (2 * TILE), rows, 2 * TILE, channels), jnp.bfloat16),
            pltpu.SemaphoreType.DMA((cols // (2 * TILE),)),
        ],
        compiler_params=pltpu.CompilerParams(vmem_limit_bytes=VMEM_BYTES),
        cost_estimate=pl.CostEstimate(flops=1_200_000_000, bytes_accessed=6_000_000, transcendentals=0),
        name="out",
    )(x, mix, wo)
    return (out, summary_result)


def solution(mesh):
    placed = (
        P(("img", "row"), "col", None),
        P(("img", "row"), "col", None),
        P(None, "row"),
        P(None, "row"),
        P(("img", "row"), "col"),
    )
    return jax.shard_map(
        local,
        mesh=mesh,
        in_specs=placed,
        out_specs=(P(("img", "row"), "col", None), P(("img", "row"), "col", None)),
        check_vma=False,
    )
```

```python
import functools

import jax
import jax.numpy as jnp
from jax import lax
from jax.experimental import pallas as pl
from jax.experimental.pallas import tpu as pltpu
from jax.sharding import PartitionSpec as P

HEAD_DIM = 64
PATCH_SIDE = 16
RADIUS = 4
TILE = 2 * RADIUS
LANES = 128
GROUP = 256
INVALID = 100.0
HIDDEN = -1e30
LOG2_E = 1.4426950408889634
EVEN_ROW, EVEN_COL, ROW, STARTS = 4, 5, 6, 7
VMEM_BYTES = 26 * 1024 * 1024


def nt(a, b):
    return lax.dot_general(a, b, (((1,), (1,)), ((), ())), preferred_element_type=jnp.float32)


def nn(a, b):
    return lax.dot_general(a, b, (((1,), (0,)), ((), ())), preferred_element_type=jnp.float32)


def layer_normalise(lines):
    center = lines - jnp.mean(lines, axis=-1, keepdims=True)
    spread = jnp.mean(center * center, axis=-1, keepdims=True)
    return center * lax.rsqrt(spread + 1e-05)


def pair_swapped(even_block, odd_block, axis):
    count = lax.axis_size(axis)
    got = []
    for first, block in ((0, even_block), (1, odd_block)):
        pairs = [(i, i + 1) for i in range(first, count - 1, 2)]
        got.append(lax.ppermute(block, axis, pairs + [(b, a) for a, b in pairs]))
    return got


def swapped(block, axis, bit):
    count = lax.axis_size(axis)
    return lax.ppermute(block, axis, [(i, i ^ bit) for i in range(count)])


def after(block, *others):
    return lax.optimization_barrier((block, *others))[0]


def bits_of(count):
    bits, bit = [], count // 2
    while bit:
        bits.append(bit)
        bit //= 2
    return bits


def marked_lanes(lines, hidden):
    first = jnp.where(hidden, INVALID, lines[:, :, :LANES])
    return jnp.concatenate([first, lines[:, :, LANES:]], axis=2)


def edge_kernel(place_ref, flags_hbm, x_hbm, carriers_ref, mark_ref, *refs):
    even_rows_ref, odd_rows_ref, even_cols_ref, odd_cols_ref, x_ref, flags_ref, spread, carriers_s, sems = refs
    rows, cols, channels = x_ref.shape
    middle = rows // 2
    flags_copy = pltpu.make_async_copy(flags_hbm, flags_ref, sems.at[0])
    x_copy = pltpu.make_async_copy(x_hbm, x_ref, sems.at[1])
    flags_copy.start()
    x_copy.start()
    per_row = carriers_ref.shape[1]
    carriers_s[...] = jnp.zeros_like(carriers_s)
    for i in range(carriers_ref.shape[0]):
        carriers_s[i * per_row : (i + 1) * per_row, :] = carriers_ref[i].astype(jnp.float32)
    for i in range(carriers_s.shape[0] // TILE):
        even_cols_ref[middle + i] = carriers_s[i * TILE : (i + 1) * TILE, :].astype(jnp.bfloat16)
    flags_copy.wait()
    row_at = lax.broadcasted_iota(jnp.int32, (cols, cols), 0)
    diagonal = row_at == lax.broadcasted_iota(jnp.int32, (cols, cols), 1)
    for r in range(rows):
        hidden = jnp.where(flags_ref[r : r + 1, :] > 0, 0.0, INVALID)
        spread[r * cols : (r + 1) * cols, :] = jnp.where(diagonal, hidden, 0.0).astype(jnp.bfloat16)
    marks = nn(spread[...], jnp.ones((cols, LANES), jnp.bfloat16)).reshape(rows, cols, LANES)
    mark_ref[...] = marks.astype(jnp.bfloat16)
    x_copy.wait()
    first, last = [
        marked_lanes(x_ref[at].astype(jnp.float32), marks[at] > INVALID / 2)
        for at in (slice(0, RADIUS), slice(rows - RADIUS, rows))
    ]
    even = place_ref[EVEN_ROW] > 0
    even_rows_ref[...] = jnp.where(even, last, first).astype(jnp.bfloat16)
    odd_rows_ref[...] = jnp.where(even, first, last).astype(jnp.bfloat16)
    even = place_ref[EVEN_COL] > 0
    low = lax.broadcasted_iota(jnp.int32, (1, TILE, 1), 1) < RADIUS
    for lane in range(0, channels, LANES):
        lanes = slice(lane, lane + LANES)
        strips = []
        for columns in (slice(0, TILE), slice(cols - TILE, cols)):
            halves = []
            for part in (slice(0, middle), slice(middle, rows)):
                lines = x_ref[part, columns, lanes].astype(jnp.float32)
                halves.append(jnp.where(marks[part, columns, :] > INVALID / 2, INVALID, lines) if lane == 0 else lines)
            strips.append(halves)
        (first_up, first_down), (last_up, last_down) = strips
        first = jnp.where(low, first_up, jnp.roll(first_down, RADIUS, axis=1))
        last = jnp.where(low, jnp.roll(last_up, RADIUS, axis=1), last_down)
        even_cols_ref[:middle, :, lanes] = jnp.where(even, last, first).astype(jnp.bfloat16)
        odd_cols_ref[:, :, lanes] = jnp.where(even, first, last).astype(jnp.bfloat16)


def piece_kernel(place_ref, triple_hbm, mine_ref, last_ref, sems):
    start = pl.multiple_of(place_ref[STARTS], 16)
    last = triple_hbm.shape[0] - last_ref.shape[0]
    copies = [
        pltpu.make_async_copy(triple_hbm.at[pl.ds(start, mine_ref.shape[0]), :], mine_ref, sems.at[0]),
        pltpu.make_async_copy(triple_hbm.at[last:, :], last_ref, sems.at[1]),
    ]
    for copy in copies:
        copy.start()
    for copy in copies:
        copy.wait()


def corner_kernel(place_ref, even_rows_ref, odd_rows_ref, even_ref, odd_ref):
    cols = even_rows_ref.shape[1]
    low = lax.broadcasted_iota(jnp.int32, (1, TILE, 1), 1) < RADIUS
    flip = place_ref[EVEN_ROW] > 0
    even_rows, odd_rows = even_rows_ref[...].astype(jnp.float32), odd_rows_ref[...].astype(jnp.float32)
    top, bottom = jnp.where(flip, odd_rows, even_rows), jnp.where(flip, even_rows, odd_rows)
    first = jnp.where(low, top[:, :TILE, :], jnp.roll(bottom[:, :TILE, :], RADIUS, axis=1))
    last = jnp.where(low, jnp.roll(top[:, cols - TILE :, :], RADIUS, axis=1), bottom[:, cols - TILE :, :])
    even = place_ref[EVEN_COL] > 0
    even_ref[...] = jnp.where(even, last, first).astype(jnp.bfloat16)
    odd_ref[...] = jnp.where(even, first, last).astype(jnp.bfloat16)


def carrier_pair_kernel(own_ref, got_hbm, out_ref, got_s, pair_s, sem):
    per_row, here = own_ref.shape[1], own_ref.shape[0] * own_ref.shape[1]
    tiles = got_s.shape[0]
    copy = pltpu.make_async_copy(got_hbm.at[got_hbm.shape[0] - tiles :], got_s, sem)
    copy.start()
    for i in range(own_ref.shape[0]):
        pair_s[i * per_row : (i + 1) * per_row, :] = own_ref[i].astype(jnp.float32)
    copy.wait()
    pair_s[here:, :] = got_s[...].astype(jnp.float32).reshape(tiles * TILE, -1)[:here]
    out_ref[...] = pair_s[...].astype(jnp.bfloat16)


def pack_kernel(final_ref, *refs):
    parts, out_ref = refs[:-1], refs[-1]
    rows = final_ref.shape[0]
    out_ref[:rows, :] = final_ref[...]
    carriers = jnp.concatenate([part[...].astype(jnp.float32) for part in parts], axis=0)
    out_ref[rows:, :] = carriers.astype(jnp.bfloat16)


def own_kernel(x_ref, xq_ref):
    rows, cols, _ = x_ref.shape
    step = 4

    def own(i, _):
        at = pl.multiple_of(i * step, step)
        y = layer_normalise(x_ref[pl.ds(at, step)].astype(jnp.float32))
        for c in range(cols // TILE):
            piece = y[:, c * TILE : (c + 1) * TILE, :].reshape(step * TILE, -1)
            to = pl.multiple_of(c * rows * TILE + at * TILE, step * TILE)
            xq_ref[pl.ds(to, step * TILE), :] = piece.astype(jnp.bfloat16)
        return 0

    lax.fori_loop(0, rows // step, own, 0)


def halo_kernel(place_ref, xq_ref, mark_ref, *refs):
    even_rows_ref, odd_rows_ref, even_cols_ref, odd_cols_ref, even_corners_ref, odd_corners_ref, xkv_ref, hide_ref = refs[:8]
    scratch = refs[8:]
    rows, cols, _ = mark_ref.shape
    wide_rows, wide_cols = rows + 2 * RADIUS, cols + 2 * RADIUS
    half = wide_rows // 2
    step = 2
    top_s, bottom_s, left_s, right_s, left_corner_s, right_corner_s = scratch[:6]
    top_ref, bottom_ref, left_ref, right_ref, left_corner_ref, right_corner_ref, flag_s = scratch[6:]
    for even, odd, low, high, low_flags, high_flags, parity, size in (
        (even_rows_ref, odd_rows_ref, top_s, bottom_s, top_ref, bottom_ref, EVEN_ROW, 2),
        (even_cols_ref, odd_cols_ref, left_s, right_s, left_ref, right_ref, EVEN_COL, 4),
        (even_corners_ref, odd_corners_ref, left_corner_s, right_corner_s, left_corner_ref, right_corner_ref, EVEN_COL, 4),
    ):
        flip = place_ref[parity] > 0
        for i in range(0, odd.shape[0], size):
            a, b = even[i : i + size].astype(jnp.float32), odd[i : i + size].astype(jnp.float32)
            for lines, out, flags in ((jnp.where(flip, b, a), low, low_flags), (jnp.where(flip, a, b), high, high_flags)):
                out[i : i + size] = layer_normalise(lines)
                flags[i : i + size] = lines[:, :, :LANES]

    def lines_of(ref):
        return ref.astype(jnp.float32)

    def merge(at, blocks, left, right, to_ref):
        low = lax.broadcasted_iota(jnp.int32, (1, TILE, 1), 1) < RADIUS
        before = left
        for c in range(len(blocks) + 1):
            after = jnp.roll(blocks[c], RADIUS, axis=1) if c < len(blocks) else right
            to = c * wide_rows * TILE + at * TILE
            to = pl.multiple_of(to, step * TILE) if not isinstance(to, int) else to
            lines = jnp.where(low, before, after).reshape(step * TILE, -1)
            to_ref[pl.ds(to, step * TILE), :] = lines.astype(jnp.bfloat16)
            before = after

    def sides(at, upper, left_ref, right_ref):
        left, right = lines_of(left_ref[pl.ds(at, step)]), lines_of(right_ref[pl.ds(at, step)])
        if upper:
            return jnp.roll(left, RADIUS, axis=1), right
        return left, jnp.roll(right, RADIUS, axis=1)

    def hide_if(border, lines):
        return jnp.where(place_ref[border] > 0, INVALID, lines)

    def band(at, ref, ref_s, first, upper):
        cut = [slice(c * TILE, (c + 1) * TILE) for c in range(cols // TILE)]
        lines = ref_s[first : first + step]
        merge(at, [lines[:, k, :] for k in cut], *sides(first, upper, left_corner_s, right_corner_s), xkv_ref)
        marks = hide_if(int(upper), ref[first : first + step])
        left, right = sides(first, upper, left_corner_ref, right_corner_ref)
        left, right = hide_if(int(upper), hide_if(2, left)), hide_if(int(upper), hide_if(3, right))
        merge(at, [marks[:, k, :] for k in cut], left, right, flag_s)

    for i in range(0, RADIUS, step):
        band(i, top_ref, top_s, i, False)
        band(RADIUS + rows + i, bottom_ref, bottom_s, i, True)

    def middle(i, upper):
        at = pl.multiple_of(i * step, step)
        own = at - RADIUS
        blocks = []
        for c in range(cols // TILE):
            first = pl.multiple_of(c * rows * TILE + own * TILE, step * TILE)
            blocks.append(xq_ref[pl.ds(first, step * TILE), :].astype(jnp.float32).reshape(step, TILE, -1))
        strip_at = own - (rows // 2 if upper else 0)
        merge(at, blocks, *sides(strip_at, upper, left_s, right_s), xkv_ref)
        marks = mark_ref[pl.ds(own, step)].astype(jnp.float32)
        marks = [marks[:, c * TILE : (c + 1) * TILE, :] for c in range(cols // TILE)]
        left, right = sides(strip_at, upper, left_ref, right_ref)
        merge(at, marks, hide_if(2, left), hide_if(3, right), flag_s)
        return 0

    lax.fori_loop(RADIUS // step, half // step, lambda i, _: middle(i, False), 0)
    lax.fori_loop(half // step, (RADIUS + rows) // step, lambda i, _: middle(i, True), 0)

    first_lane = (lax.broadcasted_iota(jnp.int32, (8, LANES), 1) == 0).astype(jnp.bfloat16)
    spans = []
    for c in range(wide_cols // TILE):
        lines = flag_s[c * wide_rows * TILE : (c + 1) * wide_rows * TILE, :]
        spans.append(jnp.where(nt(first_lane, lines) > INVALID / 2, HIDDEN, 0.0))
    tall = rows // TILE
    for c in range(cols // TILE):
        for r in range(tall):
            at = slice(r * TILE * TILE, r * TILE * TILE + 2 * TILE * TILE)
            hide_ref[c * tall + r] = jnp.concatenate([spans[c][:, at], spans[c + 1][:, at]], axis=1)


def project_kernel(whole, pieces, triple_rows, place_ref, *refs):
    sources, refs = refs[: len(whole) + len(pieces)], refs[len(whole) + len(pieces) :]
    xq_ref, xkv_ref, q_s, k_s, v_s, wt, sems = refs
    channels = wt.shape[1]
    groups = channels // GROUP
    factor = HEAD_DIM ** (-0.5) * LOG2_E
    me = place_ref[ROW]
    copies = []
    for j, source in enumerate(sources):
        if j < len(whole):
            to = (me ^ whole[j]) * triple_rows
        else:
            off, start = pieces[j - len(whole)]
            to = (me ^ off) * triple_rows + place_ref[STARTS + start]
        to = pl.multiple_of(to, 16)
        copy = pltpu.make_async_copy(source, wt.at[pl.ds(to, source.shape[0]), :], sems.at[j])
        copy.start()
        copies.append(copy)
    for copy in copies:
        copy.wait()

    q_rows, kv_rows = xq_ref.shape[0], xkv_ref.shape[0]
    q_chunk, kv_chunk = q_rows // 2, kv_rows // 4

    def project_q(n, _):
        w = wt[pl.ds(pl.multiple_of(n * GROUP, GROUP), GROUP), :]
        for m in range(0, q_rows, q_chunk):
            q_s[n, m : m + q_chunk, :] = (nt(xq_ref[m : m + q_chunk, :], w) * factor).astype(jnp.bfloat16)
        return 0

    def project_k(n, _):
        w = wt[pl.ds(pl.multiple_of(channels + n * GROUP, GROUP), GROUP), :]
        for m in range(0, kv_rows, kv_chunk):
            k_s[n, m : m + kv_chunk, :] = nt(xkv_ref[m : m + kv_chunk, :], w).astype(jnp.bfloat16)
        return 0

    def project_v(n, _):
        w = wt[pl.ds(pl.multiple_of(2 * channels + n * GROUP, GROUP), GROUP), :]
        for m in range(0, kv_rows, kv_chunk):
            v_s[n, m : m + kv_chunk, :] = nt(xkv_ref[m : m + kv_chunk, :], w).astype(jnp.bfloat16)
        return 0

    lax.fori_loop(0, groups, project_q, 0)
    lax.fori_loop(0, groups, project_k, 0)
    lax.fori_loop(0, groups, project_v, 0)


def carrier_kernel(offsets, place_ref, wt, *refs):
    shards = len(offsets)
    finals, refs = refs[:shards], refs[shards:]
    summary_ref, wo, kce, vc_s, carriers_s, sems = refs
    per_row = summary_ref.shape[1]
    channels = wt.shape[1]
    groups = channels // GROUP
    heads = channels // HEAD_DIM
    factor = HEAD_DIM ** (-0.5)
    carriers_here = vc_s.shape[0]
    final_rows = wo.shape[0] // shards
    copies = []
    for j, off in enumerate(offsets):
        to = pl.multiple_of((place_ref[ROW] ^ off) * final_rows, 16)
        copy = pltpu.make_async_copy(finals[j].at[0:final_rows, :], wo.at[pl.ds(to, final_rows), :], sems.at[j])
        copy.start()
        copies.append(copy)
    coming = []
    sent = carriers_s.shape[0] // shards
    for j in range(shards):
        source = finals[j].at[final_rows : final_rows + sent, :]
        copy = pltpu.make_async_copy(source, carriers_s.at[j * sent : (j + 1) * sent, :], sems.at[shards + j])
        copy.start()
        coming.append(copy)
    for copy in coming:
        copy.wait()
    carriers = carriers_s[...].astype(jnp.float32)
    own = carriers[:carriers_here]
    carriers = layer_normalise(carriers).astype(jnp.bfloat16)
    own_norm = layer_normalise(own).astype(jnp.bfloat16)
    qc = (nt(own_norm, wt[:channels, :]) * factor).astype(jnp.bfloat16).astype(jnp.float32)
    kc = nt(carriers, wt[channels : 2 * channels, :]).astype(jnp.bfloat16)
    vc = nt(carriers, wt[2 * channels :, :]).astype(jnp.bfloat16)
    head_of = lax.broadcasted_iota(jnp.int32, (1, channels), 1) // HEAD_DIM
    stacked = jnp.concatenate([jnp.where(head_of == h, qc, 0.0) for h in range(heads)], axis=0)
    e = jnp.exp(nt(stacked.astype(jnp.bfloat16), kc))
    weights = (e / jnp.sum(e, axis=-1, keepdims=True)).astype(jnp.bfloat16)
    o = nn(weights, vc)
    mix = jnp.zeros((carriers_here, channels), jnp.float32)
    for h in range(heads):
        mix = jnp.where(head_of == h, o[h * carriers_here : (h + 1) * carriers_here, :], mix)
    for copy in copies:
        copy.wait()
    renewed = own + nt(mix.astype(jnp.bfloat16), wo[...])
    for i in range(summary_ref.shape[0]):
        summary_ref[i] = renewed[i * per_row : (i + 1) * per_row, :].astype(jnp.bfloat16)
    fresh = nt(layer_normalise(renewed).astype(jnp.bfloat16), wt[channels:, :]).astype(jnp.bfloat16).astype(jnp.float32)
    vc_s[...] = fresh[:, channels:]
    same = (
        lax.broadcasted_iota(jnp.int32, (GROUP, GROUP), 0) // HEAD_DIM
        == lax.broadcasted_iota(jnp.int32, (GROUP, GROUP), 1) // HEAD_DIM
    )
    windows = kce.shape[0] // groups
    for w in range(windows):
        for g in range(groups):
            kce[w * groups + g] = jnp.where(same, fresh[w : w + 1, g * GROUP : (g + 1) * GROUP], 0.0).astype(jnp.bfloat16)


def attend_kernel(tall, broad, q_s, k_s, v_s, hide_ref, kce, vc_s, mix_s, pc_s, even_s, odd_s):
    groups, tiles = q_s.shape[0], hide_ref.shape[0]
    heads_in = GROUP // HEAD_DIM
    queries, span = TILE * TILE, 2 * TILE * TILE
    side = PATCH_SIDE // TILE
    wide = (tall + 1) * queries
    qi = lax.broadcasted_iota(jnp.int32, (queries, 2 * span), 0)
    ki = lax.broadcasted_iota(jnp.int32, (queries, 2 * span), 1)
    row_step = (ki % span) // TILE - qi // TILE
    col_step = (ki // span) * TILE + ki % TILE - qi % TILE
    seen = (row_step >= 0) & (row_step <= 2 * RADIUS) & (col_step >= 0) & (col_step <= 2 * RADIUS)
    band = jnp.where(seen, 0.0, HIDDEN)
    group_head = lax.broadcasted_iota(jnp.int32, (1, GROUP), 1) // HEAD_DIM
    only = [jnp.where(group_head == h, 1.0, 0.0).astype(jnp.bfloat16) for h in range(heads_in)]
    in_pair = LANES // HEAD_DIM
    pair_head = lax.broadcasted_iota(jnp.int32, (1, LANES), 1) // HEAD_DIM

    for c in range(broad):
        for w in range(tall // side):
            at = slice((c * tall + w * side) * queries, (c * tall + (w + 1) * side) * queries)
            window = w * (broad // side) + c // side
            for g in range(groups):
                pc_s[at, g * GROUP : (g + 1) * GROUP] = jnp.exp2(nt(q_s[g, at, :], kce[window * groups + g]))

    def keys_at(t):
        k0 = pl.multiple_of(t // tall * wide + t % tall * queries, queries)
        return k0, pl.multiple_of(k0 + wide, queries)

    def scores(t, ref):
        q_at = pl.multiple_of(t * queries, queries)
        k0, k1 = keys_at(t)
        for g in range(groups):
            q = q_s[g, pl.ds(q_at, queries), :]
            qq = jnp.concatenate([q * mask for mask in only], axis=0)
            k = jnp.concatenate([k_s[g, pl.ds(k0, span), :], k_s[g, pl.ds(k1, span), :]], axis=0)
            ref[g] = nt(qq, k)

    def finish(t, ref):
        q_at = pl.multiple_of(t * queries, queries)
        k0, k1 = keys_at(t)
        window = t % tall // side * (broad // side) + t // tall // side
        bias = band + hide_ref[t][0:1, :]
        for g in range(groups):
            p = jnp.exp2(ref[g].reshape(heads_in, queries, 2 * span) + bias[None])
            total = jnp.sum(p, axis=-1, keepdims=True)
            v = jnp.concatenate([v_s[g, pl.ds(k0, span), :], v_s[g, pl.ds(k1, span), :]], axis=0)
            o = nn(p.reshape(heads_in * queries, 2 * span).astype(jnp.bfloat16), v).reshape(heads_in, queries, GROUP)
            v_new = vc_s[pl.ds(window, 1), g * GROUP : (g + 1) * GROUP]
            for j in range(GROUP // LANES):
                lanes = slice(j * LANES, (j + 1) * LANES)
                at = slice(g * GROUP + j * LANES, g * GROUP + (j + 1) * LANES)
                kept, kept_total = o[j * in_pair, :, lanes], total[j * in_pair]
                for h in range(1, in_pair):
                    kept = jnp.where(pair_head == h, o[j * in_pair + h, :, lanes], kept)
                    kept_total = jnp.where(pair_head == h, total[j * in_pair + h], kept_total)
                new = pc_s[pl.ds(q_at, queries), at]
                mixed = (kept + new * v_new[:, lanes]) / (kept_total + new)
                mix_s[pl.ds(q_at, queries), at] = mixed.astype(jnp.bfloat16)

    scores(0, even_s)

    def two(i, _):
        t = 2 * i
        scores(t + 1, odd_s)
        finish(t, even_s)
        scores(jnp.minimum(t + 2, tiles - 1), even_s)
        finish(t + 1, odd_s)
        return 0

    lax.fori_loop(0, tiles // 2, two, 0)


def out_kernel(x_ref, mix_s, wo, out_hbm, out_ref, out_sems):
    rows, cols, channels = x_ref.shape
    going = []
    for pair in range(cols // (2 * TILE)):
        both = slice(2 * pair * TILE, 2 * (pair + 1) * TILE)
        for g in range(channels // GROUP):
            at = slice(g * GROUP, (g + 1) * GROUP)
            w = wo[at, :]
            y = nt(mix_s[2 * pair * rows * TILE : 2 * (pair + 1) * rows * TILE, :], w).reshape(2, rows, TILE, GROUP)
            y = jnp.concatenate([y[0], y[1]], axis=1) + x_ref[:, both, at].astype(jnp.float32)
            out_ref[pair, :, :, at] = y.astype(jnp.bfloat16)
        copy = pltpu.make_async_copy(out_ref.at[pair], out_hbm.at[:, both, :], out_sems.at[pair])
        copy.start()
        going.append(copy)
    for copy in going:
        copy.wait()


def local(grid_elements, summary_vectors, triple_projection, final_projection, genuine_flags):
    rows, cols, channels = grid_elements.shape
    wide_rows, wide_cols = rows + 2 * RADIUS, cols + 2 * RADIUS

    triple_t, final_t = triple_projection.T, final_projection.T
    vmem = pl.BlockSpec(memory_space=pltpu.VMEM)
    anywhere = pl.BlockSpec(memory_space=pl.ANY)
    scalars = pl.BlockSpec(memory_space=pltpu.SMEM)
    hbm = pl.BlockSpec(memory_space=pltpu.HBM)
    small = pltpu.CompilerParams(vmem_limit_bytes=8 * 1024 * 1024)
    row_strip = jax.ShapeDtypeStruct((RADIUS, cols, channels), jnp.bfloat16)
    col_strip = jax.ShapeDtypeStruct((rows // 2, TILE, channels), jnp.bfloat16)
    corner = jax.ShapeDtypeStruct((RADIUS, TILE, channels), jnp.bfloat16)
    own_rows = summary_vectors.shape[0] * summary_vectors.shape[1]
    carrier_tiles = -(-own_rows // TILE)

    row, col, img = lax.axis_size("row"), lax.axis_size("col"), lax.axis_size("img")
    row_at, col_at, img_at = lax.axis_index("row"), lax.axis_index("col"), lax.axis_index("img")
    row_bits = bits_of(row)
    far, rest = row_bits[0], row_bits[1:]
    relays = img if triple_t.shape[0] % (16 * (img + 1)) == 0 else 0
    piece_rows = triple_t.shape[0] // (relays + 1)
    starts = [(img_at - k) % img for k in range(relays)] + [jnp.int32(relays)]
    place = [row_at == 0, row_at == row - 1, col_at == 0, col_at == col - 1, row_at % 2 == 0, col_at % 2 == 0, row_at]
    place = jnp.stack([jnp.asarray(p).astype(jnp.int32) for p in place + [start * piece_rows for start in starts]])

    mark, even_rows, odd_rows, even_cols, odd_cols, x = pl.pallas_call(
        edge_kernel,
        out_shape=(
            pltpu.VMEM((rows, cols, LANES), jnp.bfloat16),
            pltpu.VMEM(row_strip.shape, jnp.bfloat16),
            pltpu.VMEM(row_strip.shape, jnp.bfloat16),
            pltpu.VMEM((col_strip.shape[0] + carrier_tiles, *col_strip.shape[1:]), jnp.bfloat16),
            pltpu.VMEM(col_strip.shape, jnp.bfloat16),
            pltpu.VMEM(grid_elements.shape, jnp.bfloat16),
        ),
        in_specs=[scalars, hbm, hbm, vmem],
        out_specs=(vmem,) * 6,
        scratch_shapes=[
            pltpu.VMEM((rows, cols), jnp.int32),
            pltpu.VMEM((rows * cols, cols), jnp.bfloat16),
            pltpu.VMEM((carrier_tiles * TILE, channels), jnp.float32),
            pltpu.SemaphoreType.DMA((2,)),
        ],
        compiler_params=small,
        cost_estimate=pl.CostEstimate(flops=1_000_000, bytes_accessed=1_000_000, transcendentals=0),
        name="edge_rows",
    )(place, *(pltpu.with_memory_space_constraint(a, pltpu.HBM) for a in (genuine_flags, grid_elements)), summary_vectors)
    mine, last = pl.pallas_call(
        piece_kernel,
        out_shape=(
            pltpu.VMEM((piece_rows, channels), jnp.bfloat16),
            pltpu.VMEM((triple_t.shape[0] - relays * piece_rows, channels), jnp.bfloat16),
        ),
        in_specs=[scalars, hbm],
        out_specs=(vmem, vmem),
        scratch_shapes=[pltpu.SemaphoreType.DMA((2,))],
        compiler_params=small,
        cost_estimate=pl.CostEstimate(flops=1_000_000, bytes_accessed=1_000_000, transcendentals=0),
        name="pieces",
    )(place, pltpu.with_memory_space_constraint(after(triple_t, even_rows), pltpu.HBM))
    xq = pl.pallas_call(
        own_kernel,
        out_shape=pltpu.VMEM((rows * cols, channels), jnp.bfloat16),
        in_specs=[vmem],
        out_specs=vmem,
        compiler_params=small,
        cost_estimate=pl.CostEstimate(flops=1_000_000, bytes_accessed=1_000_000, transcendentals=0),
        name="own_norm",
    )(x)
    even_rows, odd_rows = pair_swapped(even_rows, odd_rows, "row")
    even_cols, odd_cols = pair_swapped(even_cols, odd_cols, "col")

    far_pieces = []
    if relays:
        first = swapped(mine, "row", far)
    far_last = swapped(after(last, even_rows, odd_rows), "row", far)

    even_corners, odd_corners = pl.pallas_call(
        corner_kernel,
        out_shape=(pltpu.VMEM(corner.shape, jnp.bfloat16),) * 2,
        in_specs=[scalars] + [vmem] * 2,
        out_specs=(vmem,) * 2,
        compiler_params=small,
        cost_estimate=pl.CostEstimate(flops=1_000_000, bytes_accessed=1_000_000, transcendentals=0),
        name="corners",
    )(place, after(even_rows, xq), after(odd_rows, even_cols, odd_cols))
    even_corners, odd_corners = pair_swapped(even_corners, odd_corners, "col")

    carriers = pl.pallas_call(
        carrier_pair_kernel,
        out_shape=pltpu.VMEM((2 * own_rows, channels), jnp.bfloat16),
        in_specs=[vmem, anywhere],
        out_specs=vmem,
        scratch_shapes=[
            pltpu.VMEM((carrier_tiles, TILE, channels), jnp.bfloat16),
            pltpu.VMEM((2 * own_rows, channels), jnp.float32),
            pltpu.SemaphoreType.DMA,
        ],
        compiler_params=small,
        cost_estimate=pl.CostEstimate(flops=1_000, bytes_accessed=1_000, transcendentals=0),
        name="carrier_pair",
    )(summary_vectors, even_cols)
    parts = [carriers]
    for bit in bits_of(col)[:-1]:
        carriers = carriers if len(parts) == 1 else jnp.concatenate(parts, axis=0)
        got = swapped(carriers, "col", 2 * bit - 1)
        parts.append(got)
    if relays:
        first = after(first, even_cols, odd_cols)
        others = [lax.ppermute(first, "img", [(i, (i + k) % img) for i in range(img)]) for k in range(1, relays)]
        far_pieces = [first] + others
    far_pieces.append(far_last)

    final_pack = pl.pallas_call(
        pack_kernel,
        out_shape=pltpu.VMEM((final_t.shape[0] + col * own_rows, channels), jnp.bfloat16),
        in_specs=[vmem] * (1 + len(parts)),
        out_specs=vmem,
        compiler_params=small,
        cost_estimate=pl.CostEstimate(flops=1_000, bytes_accessed=1_000, transcendentals=0),
        name="final_pack",
    )(final_t, *parts)
    finals, triples, offsets = [final_pack], [after(triple_t, even_cols, odd_cols, even_rows, odd_rows, xq)], [0]
    for bit in rest:
        finals = finals + [swapped(p, "row", bit) for p in finals]
        triples = triples + [swapped(p, "row", bit) for p in triples]
        offsets = offsets + [o ^ bit for o in offsets]
    tiles = (rows // TILE) * (cols // TILE)
    keys = 4 * TILE * TILE
    strips = [row_strip] * 2 + [col_strip] * 2 + [corner] * 2
    xkv, hide = pl.pallas_call(
        halo_kernel,
        out_shape=(
            pltpu.VMEM((wide_rows * wide_cols, channels), jnp.bfloat16),
            pltpu.VMEM((tiles, 8, keys), jnp.float32),
        ),
        in_specs=[scalars] + [vmem] * 8,
        out_specs=(vmem,) * 2,
        scratch_shapes=[
            *[pltpu.VMEM(shape.shape, jnp.float32) for shape in strips],
            *[pltpu.VMEM((*shape.shape[:2], LANES), jnp.float32) for shape in strips],
            pltpu.VMEM((wide_rows * wide_cols, LANES), jnp.bfloat16),
        ],
        compiler_params=pltpu.CompilerParams(vmem_limit_bytes=12 * 1024 * 1024),
        cost_estimate=pl.CostEstimate(flops=10_000_000, bytes_accessed=6_000_000, transcendentals=1000),
        name="halo_norm",
    )(place, after(xq, got), mark, even_rows, odd_rows, even_cols, odd_cols, even_corners, odd_corners)

    far_final = swapped(final_pack, "row", far)

    far_offsets = [far]
    far_pieces = [[after(piece, xkv)] for piece in far_pieces]
    for bit in rest:
        far_pieces = [same + [swapped(p, "row", bit) for p in same] for same in far_pieces]
        far_offsets = far_offsets + [o ^ bit for o in far_offsets]

    groups = channels // GROUP
    numbered = [(off, number) for number in range(len(far_pieces)) for off in far_offsets]
    sources = triples + [piece for same in far_pieces for piece in same]
    q, k, v, wt = pl.pallas_call(
        functools.partial(project_kernel, offsets, numbered, triple_t.shape[0]),
        out_shape=(
            jax.ShapeDtypeStruct((groups, rows * cols, GROUP), jnp.bfloat16),
            jax.ShapeDtypeStruct((groups, wide_rows * wide_cols, GROUP), jnp.bfloat16),
            jax.ShapeDtypeStruct((groups, wide_rows * wide_cols, GROUP), jnp.bfloat16),
            jax.ShapeDtypeStruct((3 * channels, channels), jnp.bfloat16),
        ),
        in_specs=[scalars] + [anywhere] * len(sources) + [vmem] * 2,
        out_specs=(vmem,) * 4,
        scratch_shapes=[pltpu.SemaphoreType.DMA((len(sources),))],
        compiler_params=pltpu.CompilerParams(vmem_limit_bytes=VMEM_BYTES),
        cost_estimate=pl.CostEstimate(flops=5_000_000_000, bytes_accessed=14_000_000, transcendentals=0),
        name="project",
    )(place, *sources, xq, xkv)

    far_finals = [after(far_final, q)]
    for bit in rest:
        far_finals = far_finals + [swapped(p, "row", bit) for p in far_finals]
    finals, offsets = finals + far_finals, offsets + far_offsets
    carriers_here = carrier_tiles * TILE
    summary_result, wo, kce, vc = pl.pallas_call(
        functools.partial(carrier_kernel, offsets),
        out_shape=(
            jax.ShapeDtypeStruct(summary_vectors.shape, jnp.bfloat16),
            jax.ShapeDtypeStruct((channels, channels), jnp.bfloat16),
            jax.ShapeDtypeStruct((own_rows * groups, GROUP, GROUP), jnp.bfloat16),
            jax.ShapeDtypeStruct((carriers_here, channels), jnp.float32),
        ),
        in_specs=[scalars, vmem] + [anywhere] * len(finals),
        out_specs=(vmem,) * 4,
        scratch_shapes=[
            pltpu.VMEM((row * col * own_rows, channels), jnp.bfloat16),
            pltpu.SemaphoreType.DMA((2 * len(finals),)),
        ],
        compiler_params=pltpu.CompilerParams(vmem_limit_bytes=VMEM_BYTES),
        cost_estimate=pl.CostEstimate(flops=500_000_000, bytes_accessed=5_000_000, transcendentals=10_000),
        name="carriers",
    )(place, wt, *finals)

    scores = (groups, GROUP // HEAD_DIM * TILE * TILE, keys)
    mix = pl.pallas_call(
        functools.partial(attend_kernel, rows // TILE, cols // TILE),
        out_shape=jax.ShapeDtypeStruct((rows * cols, channels), jnp.bfloat16),
        in_specs=[vmem] * 6,
        out_specs=vmem,
        scratch_shapes=[
            pltpu.VMEM((rows * cols, channels), jnp.float32),
            pltpu.VMEM(scores, jnp.float32),
            pltpu.VMEM(scores, jnp.float32),
        ],
        compiler_params=pltpu.CompilerParams(vmem_limit_bytes=VMEM_BYTES),
        cost_estimate=pl.CostEstimate(flops=4_000_000_000, bytes_accessed=12_000_000, transcendentals=4_000_000),
        name="attend",
    )(q, k, v, hide, kce, vc)

    out = pl.pallas_call(
        out_kernel,
        out_shape=jax.ShapeDtypeStruct(grid_elements.shape, jnp.bfloat16),
        in_specs=[vmem] * 3,
        out_specs=anywhere,
        scratch_shapes=[
            pltpu.VMEM((cols // (2 * TILE), rows, 2 * TILE, channels), jnp.bfloat16),
            pltpu.SemaphoreType.DMA((cols // (2 * TILE),)),
        ],
        compiler_params=pltpu.CompilerParams(vmem_limit_bytes=VMEM_BYTES),
        cost_estimate=pl.CostEstimate(flops=1_200_000_000, bytes_accessed=6_000_000, transcendentals=0),
        name="out",
    )(x, mix, wo)
    return (out, summary_result)


def solution(mesh):
    placed = (
        P(("img", "row"), "col", None),
        P(("img", "row"), "col", None),
        P(None, "row"),
        P(None, "row"),
        P(("img", "row"), "col"),
    )
    return jax.shard_map(
        local,
        mesh=mesh,
        in_specs=placed,
        out_specs=(P(("img", "row"), "col", None), P(("img", "row"), "col", None)),
        check_vma=False,
    )
```

```python
import functools

import jax
import jax.numpy as jnp
from jax import lax
from jax.experimental import pallas as pl
from jax.experimental.pallas import tpu as pltpu
from jax.sharding import PartitionSpec as P

HEAD_DIM = 64
PATCH_SIDE = 16
RADIUS = 4
TILE = 2 * RADIUS
LANES = 128
GROUP = 256
INVALID = 100.0
HIDDEN = -1e30
LOG2_E = 1.4426950408889634
EVEN_ROW, EVEN_COL, ROW, STARTS = 4, 5, 6, 7
VMEM_BYTES = 26 * 1024 * 1024


def nt(a, b):
    return lax.dot_general(a, b, (((1,), (1,)), ((), ())), preferred_element_type=jnp.float32)


def nn(a, b):
    return lax.dot_general(a, b, (((1,), (0,)), ((), ())), preferred_element_type=jnp.float32)


def layer_normalise(lines):
    center = lines - jnp.mean(lines, axis=-1, keepdims=True)
    spread = jnp.mean(center * center, axis=-1, keepdims=True)
    return center * lax.rsqrt(spread + 1e-05)


def pair_swapped(even_block, odd_block, axis):
    count = lax.axis_size(axis)
    got = []
    for first, block in ((0, even_block), (1, odd_block)):
        pairs = [(i, i + 1) for i in range(first, count - 1, 2)]
        got.append(lax.ppermute(block, axis, pairs + [(b, a) for a, b in pairs]))
    return got


def swapped(block, axis, bit):
    count = lax.axis_size(axis)
    return lax.ppermute(block, axis, [(i, i ^ bit) for i in range(count)])


def after(block, *others):
    return lax.optimization_barrier((block, *others))[0]


def bits_of(count):
    bits, bit = [], count // 2
    while bit:
        bits.append(bit)
        bit //= 2
    return bits


def marked_lanes(lines, hidden):
    first = jnp.where(hidden, INVALID, lines[:, :, :LANES])
    return jnp.concatenate([first, lines[:, :, LANES:]], axis=2)


def edge_kernel(place_ref, flags_hbm, x_hbm, carriers_ref, mark_ref, *refs):
    even_rows_ref, odd_rows_ref, even_cols_ref, odd_cols_ref, x_ref, flags_ref, spread, carriers_s, sems = refs
    rows, cols, channels = x_ref.shape
    middle = rows // 2
    flags_copy = pltpu.make_async_copy(flags_hbm, flags_ref, sems.at[0])
    x_copy = pltpu.make_async_copy(x_hbm, x_ref, sems.at[1])
    flags_copy.start()
    x_copy.start()
    per_row = carriers_ref.shape[1]
    carriers_s[...] = jnp.zeros_like(carriers_s)
    for i in range(carriers_ref.shape[0]):
        carriers_s[i * per_row : (i + 1) * per_row, :] = carriers_ref[i].astype(jnp.float32)
    for i in range(carriers_s.shape[0] // TILE):
        even_cols_ref[middle + i] = carriers_s[i * TILE : (i + 1) * TILE, :].astype(jnp.bfloat16)
    flags_copy.wait()
    row_at = lax.broadcasted_iota(jnp.int32, (cols, cols), 0)
    diagonal = row_at == lax.broadcasted_iota(jnp.int32, (cols, cols), 1)
    for r in range(rows):
        hidden = jnp.where(flags_ref[r : r + 1, :] > 0, 0.0, INVALID)
        spread[r * cols : (r + 1) * cols, :] = jnp.where(diagonal, hidden, 0.0).astype(jnp.bfloat16)
    marks = nn(spread[...], jnp.ones((cols, LANES), jnp.bfloat16)).reshape(rows, cols, LANES)
    mark_ref[...] = marks.astype(jnp.bfloat16)
    x_copy.wait()
    first, last = [
        marked_lanes(x_ref[at].astype(jnp.float32), marks[at] > INVALID / 2)
        for at in (slice(0, RADIUS), slice(rows - RADIUS, rows))
    ]
    even = place_ref[EVEN_ROW] > 0
    even_rows_ref[...] = jnp.where(even, last, first).astype(jnp.bfloat16)
    odd_rows_ref[...] = jnp.where(even, first, last).astype(jnp.bfloat16)
    even = place_ref[EVEN_COL] > 0
    low = lax.broadcasted_iota(jnp.int32, (1, TILE, 1), 1) < RADIUS
    for lane in range(0, channels, LANES):
        lanes = slice(lane, lane + LANES)
        strips = []
        for columns in (slice(0, TILE), slice(cols - TILE, cols)):
            halves = []
            for part in (slice(0, middle), slice(middle, rows)):
                lines = x_ref[part, columns, lanes].astype(jnp.float32)
                halves.append(jnp.where(marks[part, columns, :] > INVALID / 2, INVALID, lines) if lane == 0 else lines)
            strips.append(halves)
        (first_up, first_down), (last_up, last_down) = strips
        first = jnp.where(low, first_up, jnp.roll(first_down, RADIUS, axis=1))
        last = jnp.where(low, jnp.roll(last_up, RADIUS, axis=1), last_down)
        even_cols_ref[:middle, :, lanes] = jnp.where(even, last, first).astype(jnp.bfloat16)
        odd_cols_ref[:, :, lanes] = jnp.where(even, first, last).astype(jnp.bfloat16)


def piece_kernel(place_ref, triple_hbm, mine_ref, last_ref, sems):
    start = pl.multiple_of(place_ref[STARTS], 16)
    last = triple_hbm.shape[0] - last_ref.shape[0]
    copies = [
        pltpu.make_async_copy(triple_hbm.at[pl.ds(start, mine_ref.shape[0]), :], mine_ref, sems.at[0]),
        pltpu.make_async_copy(triple_hbm.at[last:, :], last_ref, sems.at[1]),
    ]
    for copy in copies:
        copy.start()
    for copy in copies:
        copy.wait()


def corner_kernel(place_ref, even_rows_ref, odd_rows_ref, even_ref, odd_ref):
    cols = even_rows_ref.shape[1]
    low = lax.broadcasted_iota(jnp.int32, (1, TILE, 1), 1) < RADIUS
    flip = place_ref[EVEN_ROW] > 0
    even_rows, odd_rows = even_rows_ref[...].astype(jnp.float32), odd_rows_ref[...].astype(jnp.float32)
    top, bottom = jnp.where(flip, odd_rows, even_rows), jnp.where(flip, even_rows, odd_rows)
    first = jnp.where(low, top[:, :TILE, :], jnp.roll(bottom[:, :TILE, :], RADIUS, axis=1))
    last = jnp.where(low, jnp.roll(top[:, cols - TILE :, :], RADIUS, axis=1), bottom[:, cols - TILE :, :])
    even = place_ref[EVEN_COL] > 0
    even_ref[...] = jnp.where(even, last, first).astype(jnp.bfloat16)
    odd_ref[...] = jnp.where(even, first, last).astype(jnp.bfloat16)


def carrier_pair_kernel(own_ref, got_hbm, out_ref, got_s, pair_s, sem):
    per_row, here = own_ref.shape[1], own_ref.shape[0] * own_ref.shape[1]
    tiles = got_s.shape[0]
    copy = pltpu.make_async_copy(got_hbm.at[got_hbm.shape[0] - tiles :], got_s, sem)
    copy.start()
    for i in range(own_ref.shape[0]):
        pair_s[i * per_row : (i + 1) * per_row, :] = own_ref[i].astype(jnp.float32)
    copy.wait()
    pair_s[here:, :] = got_s[...].astype(jnp.float32).reshape(tiles * TILE, -1)[:here]
    out_ref[...] = pair_s[...].astype(jnp.bfloat16)


def pack_kernel(final_ref, *refs):
    parts, out_ref = refs[:-1], refs[-1]
    rows = final_ref.shape[0]
    out_ref[:rows, :] = final_ref[...]
    carriers = jnp.concatenate([part[...].astype(jnp.float32) for part in parts], axis=0)
    out_ref[rows:, :] = carriers.astype(jnp.bfloat16)


def own_kernel(x_ref, xq_ref):
    rows, cols, _ = x_ref.shape
    step = 4

    def own(i, _):
        at = pl.multiple_of(i * step, step)
        y = layer_normalise(x_ref[pl.ds(at, step)].astype(jnp.float32))
        for c in range(cols // TILE):
            piece = y[:, c * TILE : (c + 1) * TILE, :].reshape(step * TILE, -1)
            to = pl.multiple_of(c * rows * TILE + at * TILE, step * TILE)
            xq_ref[pl.ds(to, step * TILE), :] = piece.astype(jnp.bfloat16)
        return 0

    lax.fori_loop(0, rows // step, own, 0)


def halo_kernel(place_ref, xq_ref, mark_ref, *refs):
    even_rows_ref, odd_rows_ref, even_cols_ref, odd_cols_ref, even_corners_ref, odd_corners_ref, xkv_ref, hide_ref = refs[:8]
    scratch = refs[8:]
    rows, cols, _ = mark_ref.shape
    wide_rows, wide_cols = rows + 2 * RADIUS, cols + 2 * RADIUS
    half = wide_rows // 2
    step = 2
    top_s, bottom_s, left_s, right_s, left_corner_s, right_corner_s = scratch[:6]
    top_ref, bottom_ref, left_ref, right_ref, left_corner_ref, right_corner_ref, flag_s = scratch[6:]
    for even, odd, low, high, low_flags, high_flags, parity, size in (
        (even_rows_ref, odd_rows_ref, top_s, bottom_s, top_ref, bottom_ref, EVEN_ROW, 2),
        (even_cols_ref, odd_cols_ref, left_s, right_s, left_ref, right_ref, EVEN_COL, 4),
        (even_corners_ref, odd_corners_ref, left_corner_s, right_corner_s, left_corner_ref, right_corner_ref, EVEN_COL, 4),
    ):
        flip = place_ref[parity] > 0
        for i in range(0, odd.shape[0], size):
            a, b = even[i : i + size].astype(jnp.float32), odd[i : i + size].astype(jnp.float32)
            for lines, out, flags in ((jnp.where(flip, b, a), low, low_flags), (jnp.where(flip, a, b), high, high_flags)):
                out[i : i + size] = layer_normalise(lines)
                flags[i : i + size] = lines[:, :, :LANES]

    def lines_of(ref):
        return ref.astype(jnp.float32)

    def merge(at, blocks, left, right, to_ref):
        low = lax.broadcasted_iota(jnp.int32, (1, TILE, 1), 1) < RADIUS
        before = left
        for c in range(len(blocks) + 1):
            after = jnp.roll(blocks[c], RADIUS, axis=1) if c < len(blocks) else right
            to = c * wide_rows * TILE + at * TILE
            to = pl.multiple_of(to, step * TILE) if not isinstance(to, int) else to
            lines = jnp.where(low, before, after).reshape(step * TILE, -1)
            to_ref[pl.ds(to, step * TILE), :] = lines.astype(jnp.bfloat16)
            before = after

    def sides(at, upper, left_ref, right_ref):
        left, right = lines_of(left_ref[pl.ds(at, step)]), lines_of(right_ref[pl.ds(at, step)])
        if upper:
            return jnp.roll(left, RADIUS, axis=1), right
        return left, jnp.roll(right, RADIUS, axis=1)

    def hide_if(border, lines):
        return jnp.where(place_ref[border] > 0, INVALID, lines)

    def band(at, ref, ref_s, first, upper):
        cut = [slice(c * TILE, (c + 1) * TILE) for c in range(cols // TILE)]
        lines = ref_s[first : first + step]
        merge(at, [lines[:, k, :] for k in cut], *sides(first, upper, left_corner_s, right_corner_s), xkv_ref)
        marks = hide_if(int(upper), ref[first : first + step])
        left, right = sides(first, upper, left_corner_ref, right_corner_ref)
        left, right = hide_if(int(upper), hide_if(2, left)), hide_if(int(upper), hide_if(3, right))
        merge(at, [marks[:, k, :] for k in cut], left, right, flag_s)

    for i in range(0, RADIUS, step):
        band(i, top_ref, top_s, i, False)
        band(RADIUS + rows + i, bottom_ref, bottom_s, i, True)

    def middle(i, upper):
        at = pl.multiple_of(i * step, step)
        own = at - RADIUS
        blocks = []
        for c in range(cols // TILE):
            first = pl.multiple_of(c * rows * TILE + own * TILE, step * TILE)
            blocks.append(xq_ref[pl.ds(first, step * TILE), :].astype(jnp.float32).reshape(step, TILE, -1))
        strip_at = own - (rows // 2 if upper else 0)
        merge(at, blocks, *sides(strip_at, upper, left_s, right_s), xkv_ref)
        marks = mark_ref[pl.ds(own, step)].astype(jnp.float32)
        marks = [marks[:, c * TILE : (c + 1) * TILE, :] for c in range(cols // TILE)]
        left, right = sides(strip_at, upper, left_ref, right_ref)
        merge(at, marks, hide_if(2, left), hide_if(3, right), flag_s)
        return 0

    lax.fori_loop(RADIUS // step, half // step, lambda i, _: middle(i, False), 0)
    lax.fori_loop(half // step, (RADIUS + rows) // step, lambda i, _: middle(i, True), 0)

    first_lane = (lax.broadcasted_iota(jnp.int32, (8, LANES), 1) == 0).astype(jnp.bfloat16)
    spans = []
    for c in range(wide_cols // TILE):
        lines = flag_s[c * wide_rows * TILE : (c + 1) * wide_rows * TILE, :]
        spans.append(jnp.where(nt(first_lane, lines) > INVALID / 2, HIDDEN, 0.0))
    tall = rows // TILE
    for c in range(cols // TILE):
        for r in range(tall):
            at = slice(r * TILE * TILE, r * TILE * TILE + 2 * TILE * TILE)
            hide_ref[c * tall + r] = jnp.concatenate([spans[c][:, at], spans[c + 1][:, at]], axis=1)


def project_kernel(whole, pieces, triple_rows, place_ref, *refs):
    sources, refs = refs[: len(whole) + len(pieces)], refs[len(whole) + len(pieces) :]
    xq_ref, xkv_ref, q_s, k_s, v_s, wt, sems = refs
    channels = wt.shape[1]
    groups = channels // GROUP
    factor = HEAD_DIM ** (-0.5) * LOG2_E
    me = place_ref[ROW]
    copies = []
    for j, source in enumerate(sources):
        if j < len(whole):
            to = (me ^ whole[j]) * triple_rows
        else:
            off, start = pieces[j - len(whole)]
            to = (me ^ off) * triple_rows + place_ref[STARTS + start]
        to = pl.multiple_of(to, 16)
        copy = pltpu.make_async_copy(source, wt.at[pl.ds(to, source.shape[0]), :], sems.at[j])
        copy.start()
        copies.append(copy)
    for copy in copies:
        copy.wait()

    q_rows, kv_rows = xq_ref.shape[0], xkv_ref.shape[0]
    q_chunk, kv_chunk = q_rows // 2, kv_rows // 4

    def project_q(n, _):
        w = wt[pl.ds(pl.multiple_of(n * GROUP, GROUP), GROUP), :]
        for m in range(0, q_rows, q_chunk):
            q_s[n, m : m + q_chunk, :] = (nt(xq_ref[m : m + q_chunk, :], w) * factor).astype(jnp.bfloat16)
        return 0

    def project_k(n, _):
        w = wt[pl.ds(pl.multiple_of(channels + n * GROUP, GROUP), GROUP), :]
        for m in range(0, kv_rows, kv_chunk):
            k_s[n, m : m + kv_chunk, :] = nt(xkv_ref[m : m + kv_chunk, :], w).astype(jnp.bfloat16)
        return 0

    def project_v(n, _):
        w = wt[pl.ds(pl.multiple_of(2 * channels + n * GROUP, GROUP), GROUP), :]
        for m in range(0, kv_rows, kv_chunk):
            v_s[n, m : m + kv_chunk, :] = nt(xkv_ref[m : m + kv_chunk, :], w).astype(jnp.bfloat16)
        return 0

    lax.fori_loop(0, groups, project_q, 0)
    lax.fori_loop(0, groups, project_k, 0)
    lax.fori_loop(0, groups, project_v, 0)


def carrier_kernel(offsets, place_ref, wt, *refs):
    shards = len(offsets)
    finals, refs = refs[:shards], refs[shards:]
    summary_ref, wo, kce, vc_s, carriers_s, sems = refs
    per_row = summary_ref.shape[1]
    channels = wt.shape[1]
    groups = channels // GROUP
    heads = channels // HEAD_DIM
    factor = HEAD_DIM ** (-0.5)
    carriers_here = vc_s.shape[0]
    final_rows = wo.shape[0] // shards
    copies = []
    for j, off in enumerate(offsets):
        to = pl.multiple_of((place_ref[ROW] ^ off) * final_rows, 16)
        copy = pltpu.make_async_copy(finals[j].at[0:final_rows, :], wo.at[pl.ds(to, final_rows), :], sems.at[j])
        copy.start()
        copies.append(copy)
    coming = []
    sent = carriers_s.shape[0] // shards
    for j in range(shards):
        source = finals[j].at[final_rows : final_rows + sent, :]
        copy = pltpu.make_async_copy(source, carriers_s.at[j * sent : (j + 1) * sent, :], sems.at[shards + j])
        copy.start()
        coming.append(copy)
    for copy in coming:
        copy.wait()
    carriers = carriers_s[...].astype(jnp.float32)
    own = carriers[:carriers_here]
    carriers = layer_normalise(carriers).astype(jnp.bfloat16)
    own_norm = layer_normalise(own).astype(jnp.bfloat16)
    qc = (nt(own_norm, wt[:channels, :]) * factor).astype(jnp.bfloat16).astype(jnp.float32)
    kc = nt(carriers, wt[channels : 2 * channels, :]).astype(jnp.bfloat16)
    vc = nt(carriers, wt[2 * channels :, :]).astype(jnp.bfloat16)
    head_of = lax.broadcasted_iota(jnp.int32, (1, channels), 1) // HEAD_DIM
    stacked = jnp.concatenate([jnp.where(head_of == h, qc, 0.0) for h in range(heads)], axis=0)
    e = jnp.exp(nt(stacked.astype(jnp.bfloat16), kc))
    weights = (e / jnp.sum(e, axis=-1, keepdims=True)).astype(jnp.bfloat16)
    o = nn(weights, vc)
    mix = jnp.zeros((carriers_here, channels), jnp.float32)
    for h in range(heads):
        mix = jnp.where(head_of == h, o[h * carriers_here : (h + 1) * carriers_here, :], mix)
    for copy in copies:
        copy.wait()
    renewed = own + nt(mix.astype(jnp.bfloat16), wo[...])
    for i in range(summary_ref.shape[0]):
        summary_ref[i] = renewed[i * per_row : (i + 1) * per_row, :].astype(jnp.bfloat16)
    fresh = nt(layer_normalise(renewed).astype(jnp.bfloat16), wt[channels:, :]).astype(jnp.bfloat16).astype(jnp.float32)
    vc_s[...] = fresh[:, channels:]
    same = (
        lax.broadcasted_iota(jnp.int32, (GROUP, GROUP), 0) // HEAD_DIM
        == lax.broadcasted_iota(jnp.int32, (GROUP, GROUP), 1) // HEAD_DIM
    )
    windows = kce.shape[0] // groups
    for w in range(windows):
        for g in range(groups):
            kce[w * groups + g] = jnp.where(same, fresh[w : w + 1, g * GROUP : (g + 1) * GROUP], 0.0).astype(jnp.bfloat16)


def attend_kernel(tall, broad, q_s, k_s, v_s, hide_ref, kce, vc_s, mix_s, pc_s, even_s, odd_s):
    groups, tiles = q_s.shape[0], hide_ref.shape[0]
    heads_in = GROUP // HEAD_DIM
    queries, span = TILE * TILE, 2 * TILE * TILE
    side = PATCH_SIDE // TILE
    wide = (tall + 1) * queries
    qi = lax.broadcasted_iota(jnp.int32, (queries, 2 * span), 0)
    ki = lax.broadcasted_iota(jnp.int32, (queries, 2 * span), 1)
    row_step = (ki % span) // TILE - qi // TILE
    col_step = (ki // span) * TILE + ki % TILE - qi % TILE
    seen = (row_step >= 0) & (row_step <= 2 * RADIUS) & (col_step >= 0) & (col_step <= 2 * RADIUS)
    band = jnp.where(seen, 0.0, HIDDEN)
    group_head = lax.broadcasted_iota(jnp.int32, (1, GROUP), 1) // HEAD_DIM
    only = [jnp.where(group_head == h, 1.0, 0.0).astype(jnp.bfloat16) for h in range(heads_in)]
    in_pair = LANES // HEAD_DIM
    pair_head = lax.broadcasted_iota(jnp.int32, (1, LANES), 1) // HEAD_DIM

    for c in range(broad):
        for w in range(tall // side):
            at = slice((c * tall + w * side) * queries, (c * tall + (w + 1) * side) * queries)
            window = w * (broad // side) + c // side
            for g in range(groups):
                pc_s[at, g * GROUP : (g + 1) * GROUP] = jnp.exp2(nt(q_s[g, at, :], kce[window * groups + g]))

    def keys_at(t):
        k0 = pl.multiple_of(t // tall * wide + t % tall * queries, queries)
        return k0, pl.multiple_of(k0 + wide, queries)

    def scores(t, ref):
        q_at = pl.multiple_of(t * queries, queries)
        k0, k1 = keys_at(t)
        for g in range(groups):
            q = q_s[g, pl.ds(q_at, queries), :]
            qq = jnp.concatenate([q * mask for mask in only], axis=0)
            k = jnp.concatenate([k_s[g, pl.ds(k0, span), :], k_s[g, pl.ds(k1, span), :]], axis=0)
            ref[g] = nt(qq, k)

    def finish(t, ref):
        q_at = pl.multiple_of(t * queries, queries)
        k0, k1 = keys_at(t)
        window = t % tall // side * (broad // side) + t // tall // side
        bias = band + hide_ref[t][0:1, :]
        for g in range(groups):
            p = jnp.exp2(ref[g].reshape(heads_in, queries, 2 * span) + bias[None])
            total = jnp.sum(p, axis=-1, keepdims=True)
            v = jnp.concatenate([v_s[g, pl.ds(k0, span), :], v_s[g, pl.ds(k1, span), :]], axis=0)
            o = nn(p.reshape(heads_in * queries, 2 * span).astype(jnp.bfloat16), v).reshape(heads_in, queries, GROUP)
            v_new = vc_s[pl.ds(window, 1), g * GROUP : (g + 1) * GROUP]
            for j in range(GROUP // LANES):
                lanes = slice(j * LANES, (j + 1) * LANES)
                at = slice(g * GROUP + j * LANES, g * GROUP + (j + 1) * LANES)
                kept, kept_total = o[j * in_pair, :, lanes], total[j * in_pair]
                for h in range(1, in_pair):
                    kept = jnp.where(pair_head == h, o[j * in_pair + h, :, lanes], kept)
                    kept_total = jnp.where(pair_head == h, total[j * in_pair + h], kept_total)
                new = pc_s[pl.ds(q_at, queries), at]
                mixed = (kept + new * v_new[:, lanes]) / (kept_total + new)
                mix_s[pl.ds(q_at, queries), at] = mixed.astype(jnp.bfloat16)

    scores(0, even_s)

    def two(i, _):
        t = 2 * i
        scores(t + 1, odd_s)
        finish(t, even_s)
        scores(jnp.minimum(t + 2, tiles - 1), even_s)
        finish(t + 1, odd_s)
        return 0

    lax.fori_loop(0, tiles // 2, two, 0)


def out_kernel(x_ref, mix_s, wo, out_hbm, out_ref, out_sems):
    rows, cols, channels = x_ref.shape
    going = []
    for pair in range(cols // (2 * TILE)):
        both = slice(2 * pair * TILE, 2 * (pair + 1) * TILE)
        for g in range(channels // GROUP):
            at = slice(g * GROUP, (g + 1) * GROUP)
            w = wo[at, :]
            y = nt(mix_s[2 * pair * rows * TILE : 2 * (pair + 1) * rows * TILE, :], w).reshape(2, rows, TILE, GROUP)
            y = jnp.concatenate([y[0], y[1]], axis=1) + x_ref[:, both, at].astype(jnp.float32)
            out_ref[pair, :, :, at] = y.astype(jnp.bfloat16)
        copy = pltpu.make_async_copy(out_ref.at[pair], out_hbm.at[:, both, :], out_sems.at[pair])
        copy.start()
        going.append(copy)
    for copy in going:
        copy.wait()


def local(grid_elements, summary_vectors, triple_projection, final_projection, genuine_flags):
    rows, cols, channels = grid_elements.shape
    wide_rows, wide_cols = rows + 2 * RADIUS, cols + 2 * RADIUS

    triple_t, final_t = triple_projection.T, final_projection.T
    vmem = pl.BlockSpec(memory_space=pltpu.VMEM)
    anywhere = pl.BlockSpec(memory_space=pl.ANY)
    scalars = pl.BlockSpec(memory_space=pltpu.SMEM)
    hbm = pl.BlockSpec(memory_space=pltpu.HBM)
    small = pltpu.CompilerParams(vmem_limit_bytes=8 * 1024 * 1024)
    row_strip = jax.ShapeDtypeStruct((RADIUS, cols, channels), jnp.bfloat16)
    col_strip = jax.ShapeDtypeStruct((rows // 2, TILE, channels), jnp.bfloat16)
    corner = jax.ShapeDtypeStruct((RADIUS, TILE, channels), jnp.bfloat16)
    own_rows = summary_vectors.shape[0] * summary_vectors.shape[1]
    carrier_tiles = -(-own_rows // TILE)

    row, col, img = lax.axis_size("row"), lax.axis_size("col"), lax.axis_size("img")
    row_at, col_at, img_at = lax.axis_index("row"), lax.axis_index("col"), lax.axis_index("img")
    row_bits = bits_of(row)
    far, rest = row_bits[0], row_bits[1:]
    relays = img if triple_t.shape[0] % (16 * (img + 1)) == 0 else 0
    piece_rows = triple_t.shape[0] // (relays + 1)
    starts = [(img_at - k) % img for k in range(relays)] + [jnp.int32(relays)]
    place = [row_at == 0, row_at == row - 1, col_at == 0, col_at == col - 1, row_at % 2 == 0, col_at % 2 == 0, row_at]
    place = jnp.stack([jnp.asarray(p).astype(jnp.int32) for p in place + [start * piece_rows for start in starts]])

    mine, last = pl.pallas_call(
        piece_kernel,
        out_shape=(
            pltpu.VMEM((piece_rows, channels), jnp.bfloat16),
            pltpu.VMEM((triple_t.shape[0] - relays * piece_rows, channels), jnp.bfloat16),
        ),
        in_specs=[scalars, hbm],
        out_specs=(vmem, vmem),
        scratch_shapes=[pltpu.SemaphoreType.DMA((2,))],
        compiler_params=small,
        cost_estimate=pl.CostEstimate(flops=1_000_000, bytes_accessed=1_000_000, transcendentals=0),
        name="pieces",
    )(place, pltpu.with_memory_space_constraint(triple_t, pltpu.HBM))
    place = after(place, mine)

    mark, even_rows, odd_rows, even_cols, odd_cols, x = pl.pallas_call(
        edge_kernel,
        out_shape=(
            pltpu.VMEM((rows, cols, LANES), jnp.bfloat16),
            pltpu.VMEM(row_strip.shape, jnp.bfloat16),
            pltpu.VMEM(row_strip.shape, jnp.bfloat16),
            pltpu.VMEM((col_strip.shape[0] + carrier_tiles, *col_strip.shape[1:]), jnp.bfloat16),
            pltpu.VMEM(col_strip.shape, jnp.bfloat16),
            pltpu.VMEM(grid_elements.shape, jnp.bfloat16),
        ),
        in_specs=[scalars, hbm, hbm, vmem],
        out_specs=(vmem,) * 6,
        scratch_shapes=[
            pltpu.VMEM((rows, cols), jnp.int32),
            pltpu.VMEM((rows * cols, cols), jnp.bfloat16),
            pltpu.VMEM((carrier_tiles * TILE, channels), jnp.float32),
            pltpu.SemaphoreType.DMA((2,)),
        ],
        compiler_params=small,
        cost_estimate=pl.CostEstimate(flops=1_000_000, bytes_accessed=1_000_000, transcendentals=0),
        name="edge_rows",
    )(place, *(pltpu.with_memory_space_constraint(a, pltpu.HBM) for a in (genuine_flags, grid_elements)), summary_vectors)
    xq = pl.pallas_call(
        own_kernel,
        out_shape=pltpu.VMEM((rows * cols, channels), jnp.bfloat16),
        in_specs=[vmem],
        out_specs=vmem,
        compiler_params=small,
        cost_estimate=pl.CostEstimate(flops=1_000_000, bytes_accessed=1_000_000, transcendentals=0),
        name="own_norm",
    )(x)
    even_rows, odd_rows = pair_swapped(even_rows, odd_rows, "row")
    even_cols, odd_cols = pair_swapped(even_cols, odd_cols, "col")

    far_pieces = []
    if relays:
        first = swapped(mine, "row", far)
    far_last = swapped(after(last, even_rows, odd_rows), "row", far)

    even_corners, odd_corners = pl.pallas_call(
        corner_kernel,
        out_shape=(pltpu.VMEM(corner.shape, jnp.bfloat16),) * 2,
        in_specs=[scalars] + [vmem] * 2,
        out_specs=(vmem,) * 2,
        compiler_params=small,
        cost_estimate=pl.CostEstimate(flops=1_000_000, bytes_accessed=1_000_000, transcendentals=0),
        name="corners",
    )(place, after(even_rows, xq), after(odd_rows, even_cols, odd_cols))
    even_corners, odd_corners = pair_swapped(even_corners, odd_corners, "col")

    carriers = pl.pallas_call(
        carrier_pair_kernel,
        out_shape=pltpu.VMEM((2 * own_rows, channels), jnp.bfloat16),
        in_specs=[vmem, anywhere],
        out_specs=vmem,
        scratch_shapes=[
            pltpu.VMEM((carrier_tiles, TILE, channels), jnp.bfloat16),
            pltpu.VMEM((2 * own_rows, channels), jnp.float32),
            pltpu.SemaphoreType.DMA,
        ],
        compiler_params=small,
        cost_estimate=pl.CostEstimate(flops=1_000, bytes_accessed=1_000, transcendentals=0),
        name="carrier_pair",
    )(summary_vectors, even_cols)
    parts = [carriers]
    for bit in bits_of(col)[:-1]:
        carriers = carriers if len(parts) == 1 else jnp.concatenate(parts, axis=0)
        got = swapped(carriers, "col", 2 * bit - 1)
        parts.append(got)
    if relays:
        others = [lax.ppermute(first, "img", [(i, (i + k) % img) for i in range(img)]) for k in range(1, relays)]
        far_pieces = [first] + others
    far_pieces.append(far_last)

    final_pack = pl.pallas_call(
        pack_kernel,
        out_shape=pltpu.VMEM((final_t.shape[0] + col * own_rows, channels), jnp.bfloat16),
        in_specs=[vmem] * (1 + len(parts)),
        out_specs=vmem,
        compiler_params=small,
        cost_estimate=pl.CostEstimate(flops=1_000, bytes_accessed=1_000, transcendentals=0),
        name="final_pack",
    )(final_t, *parts)
    finals, triples, offsets = [final_pack], [after(triple_t, even_cols, odd_cols, even_rows, odd_rows, xq, first)], [0]
    for bit in rest:
        finals = finals + [swapped(p, "row", bit) for p in finals]
        triples = triples + [swapped(p, "row", bit) for p in triples]
        offsets = offsets + [o ^ bit for o in offsets]
    tiles = (rows // TILE) * (cols // TILE)
    keys = 4 * TILE * TILE
    strips = [row_strip] * 2 + [col_strip] * 2 + [corner] * 2
    xkv, hide = pl.pallas_call(
        halo_kernel,
        out_shape=(
            pltpu.VMEM((wide_rows * wide_cols, channels), jnp.bfloat16),
            pltpu.VMEM((tiles, 8, keys), jnp.float32),
        ),
        in_specs=[scalars] + [vmem] * 8,
        out_specs=(vmem,) * 2,
        scratch_shapes=[
            *[pltpu.VMEM(shape.shape, jnp.float32) for shape in strips],
            *[pltpu.VMEM((*shape.shape[:2], LANES), jnp.float32) for shape in strips],
            pltpu.VMEM((wide_rows * wide_cols, LANES), jnp.bfloat16),
        ],
        compiler_params=pltpu.CompilerParams(vmem_limit_bytes=12 * 1024 * 1024),
        cost_estimate=pl.CostEstimate(flops=10_000_000, bytes_accessed=6_000_000, transcendentals=1000),
        name="halo_norm",
    )(place, after(xq, got), mark, even_rows, odd_rows, even_cols, odd_cols, even_corners, odd_corners)

    far_final = swapped(final_pack, "row", far)

    far_offsets = [far]
    far_pieces = [[after(piece, xkv)] for piece in far_pieces]
    for bit in rest:
        far_pieces = [same + [swapped(p, "row", bit) for p in same] for same in far_pieces]
        far_offsets = far_offsets + [o ^ bit for o in far_offsets]

    groups = channels // GROUP
    numbered = [(off, number) for number in range(len(far_pieces)) for off in far_offsets]
    sources = triples + [piece for same in far_pieces for piece in same]
    q, k, v, wt = pl.pallas_call(
        functools.partial(project_kernel, offsets, numbered, triple_t.shape[0]),
        out_shape=(
            jax.ShapeDtypeStruct((groups, rows * cols, GROUP), jnp.bfloat16),
            jax.ShapeDtypeStruct((groups, wide_rows * wide_cols, GROUP), jnp.bfloat16),
            jax.ShapeDtypeStruct((groups, wide_rows * wide_cols, GROUP), jnp.bfloat16),
            jax.ShapeDtypeStruct((3 * channels, channels), jnp.bfloat16),
        ),
        in_specs=[scalars] + [anywhere] * len(sources) + [vmem] * 2,
        out_specs=(vmem,) * 4,
        scratch_shapes=[pltpu.SemaphoreType.DMA((len(sources),))],
        compiler_params=pltpu.CompilerParams(vmem_limit_bytes=VMEM_BYTES),
        cost_estimate=pl.CostEstimate(flops=5_000_000_000, bytes_accessed=14_000_000, transcendentals=0),
        name="project",
    )(place, *sources, xq, xkv)

    far_finals = [after(far_final, q)]
    for bit in rest:
        far_finals = far_finals + [swapped(p, "row", bit) for p in far_finals]
    finals, offsets = finals + far_finals, offsets + far_offsets
    carriers_here = carrier_tiles * TILE
    summary_result, wo, kce, vc = pl.pallas_call(
        functools.partial(carrier_kernel, offsets),
        out_shape=(
            jax.ShapeDtypeStruct(summary_vectors.shape, jnp.bfloat16),
            jax.ShapeDtypeStruct((channels, channels), jnp.bfloat16),
            jax.ShapeDtypeStruct((own_rows * groups, GROUP, GROUP), jnp.bfloat16),
            jax.ShapeDtypeStruct((carriers_here, channels), jnp.float32),
        ),
        in_specs=[scalars, vmem] + [anywhere] * len(finals),
        out_specs=(vmem,) * 4,
        scratch_shapes=[
            pltpu.VMEM((row * col * own_rows, channels), jnp.bfloat16),
            pltpu.SemaphoreType.DMA((2 * len(finals),)),
        ],
        compiler_params=pltpu.CompilerParams(vmem_limit_bytes=VMEM_BYTES),
        cost_estimate=pl.CostEstimate(flops=500_000_000, bytes_accessed=5_000_000, transcendentals=10_000),
        name="carriers",
    )(place, wt, *finals)

    scores = (groups, GROUP // HEAD_DIM * TILE * TILE, keys)
    mix = pl.pallas_call(
        functools.partial(attend_kernel, rows // TILE, cols // TILE),
        out_shape=jax.ShapeDtypeStruct((rows * cols, channels), jnp.bfloat16),
        in_specs=[vmem] * 6,
        out_specs=vmem,
        scratch_shapes=[
            pltpu.VMEM((rows * cols, channels), jnp.float32),
            pltpu.VMEM(scores, jnp.float32),
            pltpu.VMEM(scores, jnp.float32),
        ],
        compiler_params=pltpu.CompilerParams(vmem_limit_bytes=VMEM_BYTES),
        cost_estimate=pl.CostEstimate(flops=4_000_000_000, bytes_accessed=12_000_000, transcendentals=4_000_000),
        name="attend",
    )(q, k, v, hide, kce, vc)

    out = pl.pallas_call(
        out_kernel,
        out_shape=jax.ShapeDtypeStruct(grid_elements.shape, jnp.bfloat16),
        in_specs=[vmem] * 3,
        out_specs=anywhere,
        scratch_shapes=[
            pltpu.VMEM((cols // (2 * TILE), rows, 2 * TILE, channels), jnp.bfloat16),
            pltpu.SemaphoreType.DMA((cols // (2 * TILE),)),
        ],
        compiler_params=pltpu.CompilerParams(vmem_limit_bytes=VMEM_BYTES),
        cost_estimate=pl.CostEstimate(flops=1_200_000_000, bytes_accessed=6_000_000, transcendentals=0),
        name="out",
    )(x, mix, wo)
    return (out, summary_result)


def solution(mesh):
    placed = (
        P(("img", "row"), "col", None),
        P(("img", "row"), "col", None),
        P(None, "row"),
        P(None, "row"),
        P(("img", "row"), "col"),
    )
    return jax.shard_map(
        local,
        mesh=mesh,
        in_specs=placed,
        out_specs=(P(("img", "row"), "col", None), P(("img", "row"), "col", None)),
        check_vma=False,
    )
```

```python
import functools

import jax
import jax.numpy as jnp
from jax import lax
from jax.experimental import pallas as pl
from jax.experimental.pallas import tpu as pltpu
from jax.sharding import PartitionSpec as P

HEAD_DIM = 64
PATCH_SIDE = 16
RADIUS = 4
TILE = 2 * RADIUS
LANES = 128
GROUP = 256
INVALID = 100.0
HIDDEN = -1e30
LOG2_E = 1.4426950408889634
EVEN_ROW, EVEN_COL, ROW, STARTS = 4, 5, 6, 7
VMEM_BYTES = 26 * 1024 * 1024


def nt(a, b):
    return lax.dot_general(a, b, (((1,), (1,)), ((), ())), preferred_element_type=jnp.float32)


def nn(a, b):
    return lax.dot_general(a, b, (((1,), (0,)), ((), ())), preferred_element_type=jnp.float32)


def layer_normalise(lines):
    center = lines - jnp.mean(lines, axis=-1, keepdims=True)
    spread = jnp.mean(center * center, axis=-1, keepdims=True)
    return center * lax.rsqrt(spread + 1e-05)


def pair_swapped(even_block, odd_block, axis):
    count = lax.axis_size(axis)
    got = []
    for first, block in ((0, even_block), (1, odd_block)):
        pairs = [(i, i + 1) for i in range(first, count - 1, 2)]
        got.append(lax.ppermute(block, axis, pairs + [(b, a) for a, b in pairs]))
    return got


def swapped(block, axis, bit):
    count = lax.axis_size(axis)
    return lax.ppermute(block, axis, [(i, i ^ bit) for i in range(count)])


def after(block, *others):
    return lax.optimization_barrier((block, *others))[0]


def bits_of(count):
    bits, bit = [], count // 2
    while bit:
        bits.append(bit)
        bit //= 2
    return bits


def marked_lanes(lines, hidden):
    first = jnp.where(hidden, INVALID, lines[:, :, :LANES])
    return jnp.concatenate([first, lines[:, :, LANES:]], axis=2)


def edge_kernel(place_ref, flags_hbm, x_hbm, carriers_ref, mark_ref, *refs):
    even_rows_ref, odd_rows_ref, even_cols_ref, odd_cols_ref, x_ref, flags_ref, spread, carriers_s, sems = refs
    rows, cols, channels = x_ref.shape
    middle = rows // 2
    flags_copy = pltpu.make_async_copy(flags_hbm, flags_ref, sems.at[0])
    x_copy = pltpu.make_async_copy(x_hbm, x_ref, sems.at[1])
    flags_copy.start()
    x_copy.start()
    per_row = carriers_ref.shape[1]
    carriers_s[...] = jnp.zeros_like(carriers_s)
    for i in range(carriers_ref.shape[0]):
        carriers_s[i * per_row : (i + 1) * per_row, :] = carriers_ref[i].astype(jnp.float32)
    for i in range(carriers_s.shape[0] // TILE):
        even_cols_ref[middle + i] = carriers_s[i * TILE : (i + 1) * TILE, :].astype(jnp.bfloat16)
    flags_copy.wait()
    row_at = lax.broadcasted_iota(jnp.int32, (cols, cols), 0)
    diagonal = row_at == lax.broadcasted_iota(jnp.int32, (cols, cols), 1)
    for r in range(rows):
        hidden = jnp.where(flags_ref[r : r + 1, :] > 0, 0.0, INVALID)
        spread[r * cols : (r + 1) * cols, :] = jnp.where(diagonal, hidden, 0.0).astype(jnp.bfloat16)
    marks = nn(spread[...], jnp.ones((cols, LANES), jnp.bfloat16)).reshape(rows, cols, LANES)
    mark_ref[...] = marks.astype(jnp.bfloat16)
    x_copy.wait()
    first, last = [
        marked_lanes(x_ref[at].astype(jnp.float32), marks[at] > INVALID / 2)
        for at in (slice(0, RADIUS), slice(rows - RADIUS, rows))
    ]
    even = place_ref[EVEN_ROW] > 0
    even_rows_ref[...] = jnp.where(even, last, first).astype(jnp.bfloat16)
    odd_rows_ref[...] = jnp.where(even, first, last).astype(jnp.bfloat16)
    even = place_ref[EVEN_COL] > 0
    low = lax.broadcasted_iota(jnp.int32, (1, TILE, 1), 1) < RADIUS
    for lane in range(0, channels, LANES):
        lanes = slice(lane, lane + LANES)
        strips = []
        for columns in (slice(0, TILE), slice(cols - TILE, cols)):
            halves = []
            for part in (slice(0, middle), slice(middle, rows)):
                lines = x_ref[part, columns, lanes].astype(jnp.float32)
                halves.append(jnp.where(marks[part, columns, :] > INVALID / 2, INVALID, lines) if lane == 0 else lines)
            strips.append(halves)
        (first_up, first_down), (last_up, last_down) = strips
        first = jnp.where(low, first_up, jnp.roll(first_down, RADIUS, axis=1))
        last = jnp.where(low, jnp.roll(last_up, RADIUS, axis=1), last_down)
        even_cols_ref[:middle, :, lanes] = jnp.where(even, last, first).astype(jnp.bfloat16)
        odd_cols_ref[:, :, lanes] = jnp.where(even, first, last).astype(jnp.bfloat16)


def piece_kernel(place_ref, triple_hbm, mine_ref, last_ref, sems):
    start = pl.multiple_of(place_ref[STARTS], 16)
    last = triple_hbm.shape[0] - last_ref.shape[0]
    copies = [
        pltpu.make_async_copy(triple_hbm.at[pl.ds(start, mine_ref.shape[0]), :], mine_ref, sems.at[0]),
        pltpu.make_async_copy(triple_hbm.at[last:, :], last_ref, sems.at[1]),
    ]
    for copy in copies:
        copy.start()
    for copy in copies:
        copy.wait()


def corner_kernel(place_ref, even_rows_ref, odd_rows_ref, even_ref, odd_ref):
    cols = even_rows_ref.shape[1]
    low = lax.broadcasted_iota(jnp.int32, (1, TILE, 1), 1) < RADIUS
    flip = place_ref[EVEN_ROW] > 0
    even_rows, odd_rows = even_rows_ref[...].astype(jnp.float32), odd_rows_ref[...].astype(jnp.float32)
    top, bottom = jnp.where(flip, odd_rows, even_rows), jnp.where(flip, even_rows, odd_rows)
    first = jnp.where(low, top[:, :TILE, :], jnp.roll(bottom[:, :TILE, :], RADIUS, axis=1))
    last = jnp.where(low, jnp.roll(top[:, cols - TILE :, :], RADIUS, axis=1), bottom[:, cols - TILE :, :])
    even = place_ref[EVEN_COL] > 0
    even_ref[...] = jnp.where(even, last, first).astype(jnp.bfloat16)
    odd_ref[...] = jnp.where(even, first, last).astype(jnp.bfloat16)


def carrier_pair_kernel(own_ref, got_hbm, out_ref, got_s, pair_s, sem):
    per_row, here = own_ref.shape[1], own_ref.shape[0] * own_ref.shape[1]
    tiles = got_s.shape[0]
    copy = pltpu.make_async_copy(got_hbm.at[got_hbm.shape[0] - tiles :], got_s, sem)
    copy.start()
    for i in range(own_ref.shape[0]):
        pair_s[i * per_row : (i + 1) * per_row, :] = own_ref[i].astype(jnp.float32)
    copy.wait()
    pair_s[here:, :] = got_s[...].astype(jnp.float32).reshape(tiles * TILE, -1)[:here]
    out_ref[...] = pair_s[...].astype(jnp.bfloat16)


def pack_kernel(final_ref, *refs):
    parts, out_ref = refs[:-1], refs[-1]
    rows = final_ref.shape[0]
    out_ref[:rows, :] = final_ref[...]
    carriers = jnp.concatenate([part[...].astype(jnp.float32) for part in parts], axis=0)
    out_ref[rows:, :] = carriers.astype(jnp.bfloat16)


def own_kernel(x_ref, xq_ref):
    rows, cols, _ = x_ref.shape
    step = 4

    def own(i, _):
        at = pl.multiple_of(i * step, step)
        y = layer_normalise(x_ref[pl.ds(at, step)].astype(jnp.float32))
        for c in range(cols // TILE):
            piece = y[:, c * TILE : (c + 1) * TILE, :].reshape(step * TILE, -1)
            to = pl.multiple_of(c * rows * TILE + at * TILE, step * TILE)
            xq_ref[pl.ds(to, step * TILE), :] = piece.astype(jnp.bfloat16)
        return 0

    lax.fori_loop(0, rows // step, own, 0)


def halo_kernel(place_ref, xq_ref, mark_ref, *refs):
    even_rows_ref, odd_rows_ref, even_cols_ref, odd_cols_ref, even_corners_ref, odd_corners_ref, xkv_ref, hide_ref = refs[:8]
    scratch = refs[8:]
    rows, cols, _ = mark_ref.shape
    wide_rows, wide_cols = rows + 2 * RADIUS, cols + 2 * RADIUS
    half = wide_rows // 2
    step = 2
    top_s, bottom_s, left_s, right_s, left_corner_s, right_corner_s = scratch[:6]
    top_ref, bottom_ref, left_ref, right_ref, left_corner_ref, right_corner_ref, flag_s = scratch[6:]
    for even, odd, low, high, low_flags, high_flags, parity, size in (
        (even_rows_ref, odd_rows_ref, top_s, bottom_s, top_ref, bottom_ref, EVEN_ROW, 2),
        (even_cols_ref, odd_cols_ref, left_s, right_s, left_ref, right_ref, EVEN_COL, 4),
        (even_corners_ref, odd_corners_ref, left_corner_s, right_corner_s, left_corner_ref, right_corner_ref, EVEN_COL, 4),
    ):
        flip = place_ref[parity] > 0
        for i in range(0, odd.shape[0], size):
            a, b = even[i : i + size].astype(jnp.float32), odd[i : i + size].astype(jnp.float32)
            for lines, out, flags in ((jnp.where(flip, b, a), low, low_flags), (jnp.where(flip, a, b), high, high_flags)):
                out[i : i + size] = layer_normalise(lines)
                flags[i : i + size] = lines[:, :, :LANES]

    def lines_of(ref):
        return ref.astype(jnp.float32)

    def merge(at, blocks, left, right, to_ref):
        low = lax.broadcasted_iota(jnp.int32, (1, TILE, 1), 1) < RADIUS
        before = left
        for c in range(len(blocks) + 1):
            after = jnp.roll(blocks[c], RADIUS, axis=1) if c < len(blocks) else right
            to = c * wide_rows * TILE + at * TILE
            to = pl.multiple_of(to, step * TILE) if not isinstance(to, int) else to
            lines = jnp.where(low, before, after).reshape(step * TILE, -1)
            to_ref[pl.ds(to, step * TILE), :] = lines.astype(jnp.bfloat16)
            before = after

    def sides(at, upper, left_ref, right_ref):
        left, right = lines_of(left_ref[pl.ds(at, step)]), lines_of(right_ref[pl.ds(at, step)])
        if upper:
            return jnp.roll(left, RADIUS, axis=1), right
        return left, jnp.roll(right, RADIUS, axis=1)

    def hide_if(border, lines):
        return jnp.where(place_ref[border] > 0, INVALID, lines)

    def band(at, ref, ref_s, first, upper):
        cut = [slice(c * TILE, (c + 1) * TILE) for c in range(cols // TILE)]
        lines = ref_s[first : first + step]
        merge(at, [lines[:, k, :] for k in cut], *sides(first, upper, left_corner_s, right_corner_s), xkv_ref)
        marks = hide_if(int(upper), ref[first : first + step])
        left, right = sides(first, upper, left_corner_ref, right_corner_ref)
        left, right = hide_if(int(upper), hide_if(2, left)), hide_if(int(upper), hide_if(3, right))
        merge(at, [marks[:, k, :] for k in cut], left, right, flag_s)

    for i in range(0, RADIUS, step):
        band(i, top_ref, top_s, i, False)
        band(RADIUS + rows + i, bottom_ref, bottom_s, i, True)

    def middle(i, upper):
        at = pl.multiple_of(i * step, step)
        own = at - RADIUS
        blocks = []
        for c in range(cols // TILE):
            first = pl.multiple_of(c * rows * TILE + own * TILE, step * TILE)
            blocks.append(xq_ref[pl.ds(first, step * TILE), :].astype(jnp.float32).reshape(step, TILE, -1))
        strip_at = own - (rows // 2 if upper else 0)
        merge(at, blocks, *sides(strip_at, upper, left_s, right_s), xkv_ref)
        marks = mark_ref[pl.ds(own, step)].astype(jnp.float32)
        marks = [marks[:, c * TILE : (c + 1) * TILE, :] for c in range(cols // TILE)]
        left, right = sides(strip_at, upper, left_ref, right_ref)
        merge(at, marks, hide_if(2, left), hide_if(3, right), flag_s)
        return 0

    lax.fori_loop(RADIUS // step, half // step, lambda i, _: middle(i, False), 0)
    lax.fori_loop(half // step, (RADIUS + rows) // step, lambda i, _: middle(i, True), 0)

    first_lane = (lax.broadcasted_iota(jnp.int32, (8, LANES), 1) == 0).astype(jnp.bfloat16)
    spans = []
    for c in range(wide_cols // TILE):
        lines = flag_s[c * wide_rows * TILE : (c + 1) * wide_rows * TILE, :]
        spans.append(jnp.where(nt(first_lane, lines) > INVALID / 2, HIDDEN, 0.0))
    tall = rows // TILE
    for c in range(cols // TILE):
        for r in range(tall):
            at = slice(r * TILE * TILE, r * TILE * TILE + 2 * TILE * TILE)
            hide_ref[c * tall + r] = jnp.concatenate([spans[c][:, at], spans[c + 1][:, at]], axis=1)


def project_kernel(whole, pieces, triple_rows, place_ref, *refs):
    sources, refs = refs[: len(whole) + len(pieces)], refs[len(whole) + len(pieces) :]
    xq_ref, xkv_ref, q_s, k_s, v_s, wt, sems = refs
    channels = wt.shape[1]
    groups = channels // GROUP
    factor = HEAD_DIM ** (-0.5) * LOG2_E
    me = place_ref[ROW]
    copies = []
    for j, source in enumerate(sources):
        if j < len(whole):
            to = (me ^ whole[j]) * triple_rows
        else:
            off, start = pieces[j - len(whole)]
            to = (me ^ off) * triple_rows + place_ref[STARTS + start]
        to = pl.multiple_of(to, 16)
        copy = pltpu.make_async_copy(source, wt.at[pl.ds(to, source.shape[0]), :], sems.at[j])
        copy.start()
        copies.append(copy)
    for copy in copies:
        copy.wait()

    q_rows, kv_rows = xq_ref.shape[0], xkv_ref.shape[0]
    q_chunk, kv_chunk = q_rows // 2, kv_rows // 4

    def project_q(n, _):
        w = wt[pl.ds(pl.multiple_of(n * GROUP, GROUP), GROUP), :]
        for m in range(0, q_rows, q_chunk):
            q_s[n, m : m + q_chunk, :] = (nt(xq_ref[m : m + q_chunk, :], w) * factor).astype(jnp.bfloat16)
        return 0

    def project_k(n, _):
        w = wt[pl.ds(pl.multiple_of(channels + n * GROUP, GROUP), GROUP), :]
        for m in range(0, kv_rows, kv_chunk):
            k_s[n, m : m + kv_chunk, :] = nt(xkv_ref[m : m + kv_chunk, :], w).astype(jnp.bfloat16)
        return 0

    def project_v(n, _):
        w = wt[pl.ds(pl.multiple_of(2 * channels + n * GROUP, GROUP), GROUP), :]
        for m in range(0, kv_rows, kv_chunk):
            v_s[n, m : m + kv_chunk, :] = nt(xkv_ref[m : m + kv_chunk, :], w).astype(jnp.bfloat16)
        return 0

    lax.fori_loop(0, groups, project_q, 0)
    lax.fori_loop(0, groups, project_k, 0)
    lax.fori_loop(0, groups, project_v, 0)


def carrier_kernel(offsets, place_ref, wt, *refs):
    shards = len(offsets)
    finals, refs = refs[:shards], refs[shards:]
    summary_ref, wo, kce, vc_s, carriers_s, sems = refs
    per_row = summary_ref.shape[1]
    channels = wt.shape[1]
    groups = channels // GROUP
    heads = channels // HEAD_DIM
    factor = HEAD_DIM ** (-0.5)
    carriers_here = vc_s.shape[0]
    final_rows = wo.shape[0] // shards
    copies = []
    for j, off in enumerate(offsets):
        to = pl.multiple_of((place_ref[ROW] ^ off) * final_rows, 16)
        copy = pltpu.make_async_copy(finals[j].at[0:final_rows, :], wo.at[pl.ds(to, final_rows), :], sems.at[j])
        copy.start()
        copies.append(copy)
    coming = []
    sent = carriers_s.shape[0] // shards
    for j in range(shards):
        source = finals[j].at[final_rows : final_rows + sent, :]
        copy = pltpu.make_async_copy(source, carriers_s.at[j * sent : (j + 1) * sent, :], sems.at[shards + j])
        copy.start()
        coming.append(copy)
    for copy in coming:
        copy.wait()
    carriers = carriers_s[...].astype(jnp.float32)
    own = carriers[:carriers_here]
    carriers = layer_normalise(carriers).astype(jnp.bfloat16)
    own_norm = layer_normalise(own).astype(jnp.bfloat16)
    qc = (nt(own_norm, wt[:channels, :]) * factor).astype(jnp.bfloat16).astype(jnp.float32)
    kc = nt(carriers, wt[channels : 2 * channels, :]).astype(jnp.bfloat16)
    vc = nt(carriers, wt[2 * channels :, :]).astype(jnp.bfloat16)
    head_of = lax.broadcasted_iota(jnp.int32, (1, channels), 1) // HEAD_DIM
    stacked = jnp.concatenate([jnp.where(head_of == h, qc, 0.0) for h in range(heads)], axis=0)
    e = jnp.exp(nt(stacked.astype(jnp.bfloat16), kc))
    weights = (e / jnp.sum(e, axis=-1, keepdims=True)).astype(jnp.bfloat16)
    o = nn(weights, vc)
    mix = jnp.zeros((carriers_here, channels), jnp.float32)
    for h in range(heads):
        mix = jnp.where(head_of == h, o[h * carriers_here : (h + 1) * carriers_here, :], mix)
    for copy in copies:
        copy.wait()
    renewed = own + nt(mix.astype(jnp.bfloat16), wo[...])
    for i in range(summary_ref.shape[0]):
        summary_ref[i] = renewed[i * per_row : (i + 1) * per_row, :].astype(jnp.bfloat16)
    fresh = nt(layer_normalise(renewed).astype(jnp.bfloat16), wt[channels:, :]).astype(jnp.bfloat16).astype(jnp.float32)
    vc_s[...] = fresh[:, channels:]
    same = (
        lax.broadcasted_iota(jnp.int32, (GROUP, GROUP), 0) // HEAD_DIM
        == lax.broadcasted_iota(jnp.int32, (GROUP, GROUP), 1) // HEAD_DIM
    )
    windows = kce.shape[0] // groups
    for w in range(windows):
        for g in range(groups):
            kce[w * groups + g] = jnp.where(same, fresh[w : w + 1, g * GROUP : (g + 1) * GROUP], 0.0).astype(jnp.bfloat16)


def attend_kernel(tall, broad, q_s, k_s, v_s, hide_ref, kce, vc_s, mix_s, pc_s, even_s, odd_s):
    groups, tiles = q_s.shape[0], hide_ref.shape[0]
    heads_in = GROUP // HEAD_DIM
    queries, span = TILE * TILE, 2 * TILE * TILE
    side = PATCH_SIDE // TILE
    wide = (tall + 1) * queries
    qi = lax.broadcasted_iota(jnp.int32, (queries, 2 * span), 0)
    ki = lax.broadcasted_iota(jnp.int32, (queries, 2 * span), 1)
    row_step = (ki % span) // TILE - qi // TILE
    col_step = (ki // span) * TILE + ki % TILE - qi % TILE
    seen = (row_step >= 0) & (row_step <= 2 * RADIUS) & (col_step >= 0) & (col_step <= 2 * RADIUS)
    band = jnp.where(seen, 0.0, HIDDEN)
    group_head = lax.broadcasted_iota(jnp.int32, (1, GROUP), 1) // HEAD_DIM
    only = [jnp.where(group_head == h, 1.0, 0.0).astype(jnp.bfloat16) for h in range(heads_in)]
    in_pair = LANES // HEAD_DIM
    pair_head = lax.broadcasted_iota(jnp.int32, (1, LANES), 1) // HEAD_DIM

    for c in range(broad):
        for w in range(tall // side):
            at = slice((c * tall + w * side) * queries, (c * tall + (w + 1) * side) * queries)
            window = w * (broad // side) + c // side
            for g in range(groups):
                pc_s[at, g * GROUP : (g + 1) * GROUP] = jnp.exp2(nt(q_s[g, at, :], kce[window * groups + g]))

    def keys_at(t):
        k0 = pl.multiple_of(t // tall * wide + t % tall * queries, queries)
        return k0, pl.multiple_of(k0 + wide, queries)

    def scores(t, ref):
        q_at = pl.multiple_of(t * queries, queries)
        k0, k1 = keys_at(t)
        for g in range(groups):
            q = q_s[g, pl.ds(q_at, queries), :]
            qq = jnp.concatenate([q * mask for mask in only], axis=0)
            k = jnp.concatenate([k_s[g, pl.ds(k0, span), :], k_s[g, pl.ds(k1, span), :]], axis=0)
            ref[g] = nt(qq, k)

    def finish(t, ref):
        q_at = pl.multiple_of(t * queries, queries)
        k0, k1 = keys_at(t)
        window = t % tall // side * (broad // side) + t // tall // side
        bias = band + hide_ref[t][0:1, :]
        for g in range(groups):
            p = jnp.exp2(ref[g].reshape(heads_in, queries, 2 * span) + bias[None])
            total = jnp.sum(p, axis=-1, keepdims=True)
            v = jnp.concatenate([v_s[g, pl.ds(k0, span), :], v_s[g, pl.ds(k1, span), :]], axis=0)
            o = nn(p.reshape(heads_in * queries, 2 * span).astype(jnp.bfloat16), v).reshape(heads_in, queries, GROUP)
            v_new = vc_s[pl.ds(window, 1), g * GROUP : (g + 1) * GROUP]
            for j in range(GROUP // LANES):
                lanes = slice(j * LANES, (j + 1) * LANES)
                at = slice(g * GROUP + j * LANES, g * GROUP + (j + 1) * LANES)
                kept, kept_total = o[j * in_pair, :, lanes], total[j * in_pair]
                for h in range(1, in_pair):
                    kept = jnp.where(pair_head == h, o[j * in_pair + h, :, lanes], kept)
                    kept_total = jnp.where(pair_head == h, total[j * in_pair + h], kept_total)
                new = pc_s[pl.ds(q_at, queries), at]
                mixed = (kept + new * v_new[:, lanes]) / (kept_total + new)
                mix_s[pl.ds(q_at, queries), at] = mixed.astype(jnp.bfloat16)

    scores(0, even_s)

    def two(i, _):
        t = 2 * i
        scores(t + 1, odd_s)
        finish(t, even_s)
        scores(jnp.minimum(t + 2, tiles - 1), even_s)
        finish(t + 1, odd_s)
        return 0

    lax.fori_loop(0, tiles // 2, two, 0)


def out_kernel(x_ref, mix_s, wo, out_hbm, out_ref, out_sems):
    rows, cols, channels = x_ref.shape
    going = []
    for pair in range(cols // (2 * TILE)):
        both = slice(2 * pair * TILE, 2 * (pair + 1) * TILE)
        for g in range(channels // GROUP):
            at = slice(g * GROUP, (g + 1) * GROUP)
            w = wo[at, :]
            y = nt(mix_s[2 * pair * rows * TILE : 2 * (pair + 1) * rows * TILE, :], w).reshape(2, rows, TILE, GROUP)
            y = jnp.concatenate([y[0], y[1]], axis=1) + x_ref[:, both, at].astype(jnp.float32)
            out_ref[pair, :, :, at] = y.astype(jnp.bfloat16)
        copy = pltpu.make_async_copy(out_ref.at[pair], out_hbm.at[:, both, :], out_sems.at[pair])
        copy.start()
        going.append(copy)
    for copy in going:
        copy.wait()


def local(grid_elements, summary_vectors, triple_projection, final_projection, genuine_flags):
    rows, cols, channels = grid_elements.shape
    wide_rows, wide_cols = rows + 2 * RADIUS, cols + 2 * RADIUS

    triple_t, final_t = triple_projection.T, final_projection.T
    vmem = pl.BlockSpec(memory_space=pltpu.VMEM)
    anywhere = pl.BlockSpec(memory_space=pl.ANY)
    scalars = pl.BlockSpec(memory_space=pltpu.SMEM)
    hbm = pl.BlockSpec(memory_space=pltpu.HBM)
    small = pltpu.CompilerParams(vmem_limit_bytes=8 * 1024 * 1024)
    row_strip = jax.ShapeDtypeStruct((RADIUS, cols, channels), jnp.bfloat16)
    col_strip = jax.ShapeDtypeStruct((rows // 2, TILE, channels), jnp.bfloat16)
    corner = jax.ShapeDtypeStruct((RADIUS, TILE, channels), jnp.bfloat16)
    own_rows = summary_vectors.shape[0] * summary_vectors.shape[1]
    carrier_tiles = -(-own_rows // TILE)

    row, col, img = lax.axis_size("row"), lax.axis_size("col"), lax.axis_size("img")
    row_at, col_at, img_at = lax.axis_index("row"), lax.axis_index("col"), lax.axis_index("img")
    row_bits = bits_of(row)
    far, rest = row_bits[0], row_bits[1:]
    piece_rows = triple_t.shape[0] * 5 // (8 * img) // 16 * 16
    relays = img if piece_rows else 0
    starts = [(img_at - k) % img for k in range(relays)] + [jnp.int32(relays)]
    place = [row_at == 0, row_at == row - 1, col_at == 0, col_at == col - 1, row_at % 2 == 0, col_at % 2 == 0, row_at]
    place = jnp.stack([jnp.asarray(p).astype(jnp.int32) for p in place + [start * piece_rows for start in starts]])

    mine, last = pl.pallas_call(
        piece_kernel,
        out_shape=(
            pltpu.VMEM((max(piece_rows, 16), channels), jnp.bfloat16),
            pltpu.VMEM((triple_t.shape[0] - relays * piece_rows, channels), jnp.bfloat16),
        ),
        in_specs=[scalars, hbm],
        out_specs=(vmem, vmem),
        scratch_shapes=[pltpu.SemaphoreType.DMA((2,))],
        compiler_params=small,
        cost_estimate=pl.CostEstimate(flops=1_000_000, bytes_accessed=1_000_000, transcendentals=0),
        name="pieces",
    )(place, pltpu.with_memory_space_constraint(triple_t, pltpu.HBM))
    place = after(place, mine)

    mark, even_rows, odd_rows, even_cols, odd_cols, x = pl.pallas_call(
        edge_kernel,
        out_shape=(
            pltpu.VMEM((rows, cols, LANES), jnp.bfloat16),
            pltpu.VMEM(row_strip.shape, jnp.bfloat16),
            pltpu.VMEM(row_strip.shape, jnp.bfloat16),
            pltpu.VMEM((col_strip.shape[0] + carrier_tiles, *col_strip.shape[1:]), jnp.bfloat16),
            pltpu.VMEM(col_strip.shape, jnp.bfloat16),
            pltpu.VMEM(grid_elements.shape, jnp.bfloat16),
        ),
        in_specs=[scalars, hbm, hbm, vmem],
        out_specs=(vmem,) * 6,
        scratch_shapes=[
            pltpu.VMEM((rows, cols), jnp.int32),
            pltpu.VMEM((rows * cols, cols), jnp.bfloat16),
            pltpu.VMEM((carrier_tiles * TILE, channels), jnp.float32),
            pltpu.SemaphoreType.DMA((2,)),
        ],
        compiler_params=small,
        cost_estimate=pl.CostEstimate(flops=1_000_000, bytes_accessed=1_000_000, transcendentals=0),
        name="edge_rows",
    )(place, *(pltpu.with_memory_space_constraint(a, pltpu.HBM) for a in (genuine_flags, grid_elements)), summary_vectors)
    xq = pl.pallas_call(
        own_kernel,
        out_shape=pltpu.VMEM((rows * cols, channels), jnp.bfloat16),
        in_specs=[vmem],
        out_specs=vmem,
        compiler_params=small,
        cost_estimate=pl.CostEstimate(flops=1_000_000, bytes_accessed=1_000_000, transcendentals=0),
        name="own_norm",
    )(x)
    even_rows, odd_rows = pair_swapped(even_rows, odd_rows, "row")
    even_cols, odd_cols = pair_swapped(even_cols, odd_cols, "col")

    far_pieces = []
    if relays:
        first = swapped(mine, "row", far)
    far_last = swapped(after(last, even_rows, odd_rows, first), "row", far)

    even_corners, odd_corners = pl.pallas_call(
        corner_kernel,
        out_shape=(pltpu.VMEM(corner.shape, jnp.bfloat16),) * 2,
        in_specs=[scalars] + [vmem] * 2,
        out_specs=(vmem,) * 2,
        compiler_params=small,
        cost_estimate=pl.CostEstimate(flops=1_000_000, bytes_accessed=1_000_000, transcendentals=0),
        name="corners",
    )(place, after(even_rows, xq, first), after(odd_rows, even_cols, odd_cols))
    even_corners, odd_corners = pair_swapped(even_corners, odd_corners, "col")

    carriers = pl.pallas_call(
        carrier_pair_kernel,
        out_shape=pltpu.VMEM((2 * own_rows, channels), jnp.bfloat16),
        in_specs=[vmem, anywhere],
        out_specs=vmem,
        scratch_shapes=[
            pltpu.VMEM((carrier_tiles, TILE, channels), jnp.bfloat16),
            pltpu.VMEM((2 * own_rows, channels), jnp.float32),
            pltpu.SemaphoreType.DMA,
        ],
        compiler_params=small,
        cost_estimate=pl.CostEstimate(flops=1_000, bytes_accessed=1_000, transcendentals=0),
        name="carrier_pair",
    )(summary_vectors, even_cols)
    parts = [carriers]
    for bit in bits_of(col)[:-1]:
        carriers = carriers if len(parts) == 1 else jnp.concatenate(parts, axis=0)
        got = swapped(carriers, "col", 2 * bit - 1)
        parts.append(got)

    if relays:
        first = after(first, even_corners, odd_corners, got)
        others = [lax.ppermute(first, "img", [(i, (i + k) % img) for i in range(img)]) for k in range(1, relays)]
        far_pieces = [first] + others
    far_pieces.append(far_last)

    final_pack = pl.pallas_call(
        pack_kernel,
        out_shape=pltpu.VMEM((final_t.shape[0] + col * own_rows, channels), jnp.bfloat16),
        in_specs=[vmem] * (1 + len(parts)),
        out_specs=vmem,
        compiler_params=small,
        cost_estimate=pl.CostEstimate(flops=1_000, bytes_accessed=1_000, transcendentals=0),
        name="final_pack",
    )(final_t, *parts)
    finals, triples, offsets = [final_pack], [after(triple_t, even_cols, odd_cols, even_rows, odd_rows, xq, first)], [0]
    for bit in rest:
        finals = finals + [swapped(p, "row", bit) for p in finals]
        triples = triples + [swapped(p, "row", bit) for p in triples]
        offsets = offsets + [o ^ bit for o in offsets]
    tiles = (rows // TILE) * (cols // TILE)
    keys = 4 * TILE * TILE
    strips = [row_strip] * 2 + [col_strip] * 2 + [corner] * 2
    xkv, hide = pl.pallas_call(
        halo_kernel,
        out_shape=(
            pltpu.VMEM((wide_rows * wide_cols, channels), jnp.bfloat16),
            pltpu.VMEM((tiles, 8, keys), jnp.float32),
        ),
        in_specs=[scalars] + [vmem] * 8,
        out_specs=(vmem,) * 2,
        scratch_shapes=[
            *[pltpu.VMEM(shape.shape, jnp.float32) for shape in strips],
            *[pltpu.VMEM((*shape.shape[:2], LANES), jnp.float32) for shape in strips],
            pltpu.VMEM((wide_rows * wide_cols, LANES), jnp.bfloat16),
        ],
        compiler_params=pltpu.CompilerParams(vmem_limit_bytes=12 * 1024 * 1024),
        cost_estimate=pl.CostEstimate(flops=10_000_000, bytes_accessed=6_000_000, transcendentals=1000),
        name="halo_norm",
    )(place, after(xq, got), mark, even_rows, odd_rows, even_cols, odd_cols, even_corners, odd_corners)

    far_final = swapped(final_pack, "row", far)

    far_offsets = [far]
    far_pieces = [[after(piece, xkv)] for piece in far_pieces]
    for bit in rest:
        far_pieces = [same + [swapped(p, "row", bit) for p in same] for same in far_pieces]
        far_offsets = far_offsets + [o ^ bit for o in far_offsets]

    groups = channels // GROUP
    numbered = [(off, number) for number in range(len(far_pieces)) for off in far_offsets]
    sources = triples + [piece for same in far_pieces for piece in same]
    q, k, v, wt = pl.pallas_call(
        functools.partial(project_kernel, offsets, numbered, triple_t.shape[0]),
        out_shape=(
            jax.ShapeDtypeStruct((groups, rows * cols, GROUP), jnp.bfloat16),
            jax.ShapeDtypeStruct((groups, wide_rows * wide_cols, GROUP), jnp.bfloat16),
            jax.ShapeDtypeStruct((groups, wide_rows * wide_cols, GROUP), jnp.bfloat16),
            jax.ShapeDtypeStruct((3 * channels, channels), jnp.bfloat16),
        ),
        in_specs=[scalars] + [anywhere] * len(sources) + [vmem] * 2,
        out_specs=(vmem,) * 4,
        scratch_shapes=[pltpu.SemaphoreType.DMA((len(sources),))],
        compiler_params=pltpu.CompilerParams(vmem_limit_bytes=VMEM_BYTES),
        cost_estimate=pl.CostEstimate(flops=5_000_000_000, bytes_accessed=14_000_000, transcendentals=0),
        name="project",
    )(place, *sources, xq, xkv)

    far_finals = [after(far_final, q)]
    for bit in rest:
        far_finals = far_finals + [swapped(p, "row", bit) for p in far_finals]
    finals, offsets = finals + far_finals, offsets + far_offsets
    carriers_here = carrier_tiles * TILE
    summary_result, wo, kce, vc = pl.pallas_call(
        functools.partial(carrier_kernel, offsets),
        out_shape=(
            jax.ShapeDtypeStruct(summary_vectors.shape, jnp.bfloat16),
            jax.ShapeDtypeStruct((channels, channels), jnp.bfloat16),
            jax.ShapeDtypeStruct((own_rows * groups, GROUP, GROUP), jnp.bfloat16),
            jax.ShapeDtypeStruct((carriers_here, channels), jnp.float32),
        ),
        in_specs=[scalars, vmem] + [anywhere] * len(finals),
        out_specs=(vmem,) * 4,
        scratch_shapes=[
            pltpu.VMEM((row * col * own_rows, channels), jnp.bfloat16),
            pltpu.SemaphoreType.DMA((2 * len(finals),)),
        ],
        compiler_params=pltpu.CompilerParams(vmem_limit_bytes=VMEM_BYTES),
        cost_estimate=pl.CostEstimate(flops=500_000_000, bytes_accessed=5_000_000, transcendentals=10_000),
        name="carriers",
    )(place, wt, *finals)

    scores = (groups, GROUP // HEAD_DIM * TILE * TILE, keys)
    mix = pl.pallas_call(
        functools.partial(attend_kernel, rows // TILE, cols // TILE),
        out_shape=jax.ShapeDtypeStruct((rows * cols, channels), jnp.bfloat16),
        in_specs=[vmem] * 6,
        out_specs=vmem,
        scratch_shapes=[
            pltpu.VMEM((rows * cols, channels), jnp.float32),
            pltpu.VMEM(scores, jnp.float32),
            pltpu.VMEM(scores, jnp.float32),
        ],
        compiler_params=pltpu.CompilerParams(vmem_limit_bytes=VMEM_BYTES),
        cost_estimate=pl.CostEstimate(flops=4_000_000_000, bytes_accessed=12_000_000, transcendentals=4_000_000),
        name="attend",
    )(q, k, v, hide, kce, vc)

    out = pl.pallas_call(
        out_kernel,
        out_shape=jax.ShapeDtypeStruct(grid_elements.shape, jnp.bfloat16),
        in_specs=[vmem] * 3,
        out_specs=anywhere,
        scratch_shapes=[
            pltpu.VMEM((cols // (2 * TILE), rows, 2 * TILE, channels), jnp.bfloat16),
            pltpu.SemaphoreType.DMA((cols // (2 * TILE),)),
        ],
        compiler_params=pltpu.CompilerParams(vmem_limit_bytes=VMEM_BYTES),
        cost_estimate=pl.CostEstimate(flops=1_200_000_000, bytes_accessed=6_000_000, transcendentals=0),
        name="out",
    )(x, mix, wo)
    return (out, summary_result)


def solution(mesh):
    placed = (
        P(("img", "row"), "col", None),
        P(("img", "row"), "col", None),
        P(None, "row"),
        P(None, "row"),
        P(("img", "row"), "col"),
    )
    return jax.shard_map(
        local,
        mesh=mesh,
        in_specs=placed,
        out_specs=(P(("img", "row"), "col", None), P(("img", "row"), "col", None)),
        check_vma=False,
    )
```

```python
import functools

import jax
import jax.numpy as jnp
from jax import lax
from jax.experimental import pallas as pl
from jax.experimental.pallas import tpu as pltpu
from jax.sharding import PartitionSpec as P

HEAD_DIM = 64
PATCH_SIDE = 16
RADIUS = 4
TILE = 2 * RADIUS
LANES = 128
GROUP = 256
INVALID = 100.0
HIDDEN = -1e30
LOG2_E = 1.4426950408889634
EVEN_ROW, EVEN_COL, ROW, STARTS = 4, 5, 6, 7
VMEM_BYTES = 26 * 1024 * 1024


def nt(a, b):
    return lax.dot_general(a, b, (((1,), (1,)), ((), ())), preferred_element_type=jnp.float32)


def nn(a, b):
    return lax.dot_general(a, b, (((1,), (0,)), ((), ())), preferred_element_type=jnp.float32)


def layer_normalise(lines):
    center = lines - jnp.mean(lines, axis=-1, keepdims=True)
    spread = jnp.mean(center * center, axis=-1, keepdims=True)
    return center * lax.rsqrt(spread + 1e-05)


def pair_swapped(even_block, odd_block, axis):
    count = lax.axis_size(axis)
    got = []
    for first, block in ((0, even_block), (1, odd_block)):
        pairs = [(i, i + 1) for i in range(first, count - 1, 2)]
        got.append(lax.ppermute(block, axis, pairs + [(b, a) for a, b in pairs]))
    return got


def swapped(block, axis, bit):
    count = lax.axis_size(axis)
    return lax.ppermute(block, axis, [(i, i ^ bit) for i in range(count)])


def after(block, *others):
    return lax.optimization_barrier((block, *others))[0]


def bits_of(count):
    bits, bit = [], count // 2
    while bit:
        bits.append(bit)
        bit //= 2
    return bits


def marked_lanes(lines, hidden):
    first = jnp.where(hidden, INVALID, lines[:, :, :LANES])
    return jnp.concatenate([first, lines[:, :, LANES:]], axis=2)


def edge_kernel(place_ref, flags_hbm, x_hbm, mark_ref, even_ref, odd_ref, x_ref, *scratch):
    flags_ref, spread, sems = scratch
    rows, cols = flags_ref.shape
    flags_copy = pltpu.make_async_copy(flags_hbm, flags_ref, sems.at[0])
    x_copy = pltpu.make_async_copy(x_hbm, x_ref, sems.at[1])
    flags_copy.start()
    x_copy.start()
    flags_copy.wait()
    row_at = lax.broadcasted_iota(jnp.int32, (cols, cols), 0)
    diagonal = row_at == lax.broadcasted_iota(jnp.int32, (cols, cols), 1)
    for r in range(rows):
        hidden = jnp.where(flags_ref[r : r + 1, :] > 0, 0.0, INVALID)
        spread[r * cols : (r + 1) * cols, :] = jnp.where(diagonal, hidden, 0.0).astype(jnp.bfloat16)
    marks = nn(spread[...], jnp.ones((cols, LANES), jnp.bfloat16)).reshape(rows, cols, LANES)
    mark_ref[...] = marks.astype(jnp.bfloat16)
    x_copy.wait()
    first, last = [
        marked_lanes(x_ref[at].astype(jnp.float32), marks[at] > INVALID / 2)
        for at in (slice(0, RADIUS), slice(rows - RADIUS, rows))
    ]
    even = place_ref[EVEN_ROW] > 0
    even_ref[...] = jnp.where(even, last, first).astype(jnp.bfloat16)
    odd_ref[...] = jnp.where(even, first, last).astype(jnp.bfloat16)


def piece_kernel(place_ref, triple_hbm, mine_ref, last_ref, sems):
    start = pl.multiple_of(place_ref[STARTS], 16)
    last = triple_hbm.shape[0] - last_ref.shape[0]
    copies = [
        pltpu.make_async_copy(triple_hbm.at[pl.ds(start, mine_ref.shape[0]), :], mine_ref, sems.at[0]),
        pltpu.make_async_copy(triple_hbm.at[last:, :], last_ref, sems.at[1]),
    ]
    for copy in copies:
        copy.start()
    for copy in copies:
        copy.wait()


def strip_kernel(place_ref, x_ref, mark_ref, even_rows_ref, odd_rows_ref, carriers_ref, even_ref, odd_ref, carriers_s):
    per_row = carriers_ref.shape[1]
    carriers_s[...] = jnp.zeros_like(carriers_s)
    for i in range(carriers_ref.shape[0]):
        carriers_s[i * per_row : (i + 1) * per_row, :] = carriers_ref[i].astype(jnp.float32)
    for i in range(carriers_s.shape[0] // TILE):
        even_ref[odd_ref.shape[0] + i] = carriers_s[i * TILE : (i + 1) * TILE, :].astype(jnp.bfloat16)
    rows, cols, channels = x_ref.shape
    middle = rows // 2
    low = lax.broadcasted_iota(jnp.int32, (1, TILE, 1), 1) < RADIUS
    even_row, even_col = place_ref[EVEN_ROW] > 0, place_ref[EVEN_COL] > 0
    for lane in range(0, channels, LANES):
        lanes = slice(lane, lane + LANES)
        strips = []
        for columns, last in ((slice(0, TILE), False), (slice(cols - TILE, cols), True)):

            def own(part):
                lines = x_ref[part, columns, lanes].astype(jnp.float32)
                if lane == 0:
                    lines = jnp.where(mark_ref[part, columns, :].astype(jnp.float32) > INVALID / 2, INVALID, lines)
                return lines

            even_rows = even_rows_ref[:, columns, lanes].astype(jnp.float32)
            odd_rows = odd_rows_ref[:, columns, lanes].astype(jnp.float32)
            top, bottom = jnp.where(even_row, odd_rows, even_rows), jnp.where(even_row, even_rows, odd_rows)
            upper = jnp.concatenate([top, own(slice(0, middle))], axis=0)
            lower = jnp.concatenate([own(slice(middle, rows)), bottom], axis=0)
            if last:
                upper = jnp.roll(upper, RADIUS, axis=1)
            else:
                lower = jnp.roll(lower, RADIUS, axis=1)
            strips.append(jnp.where(low, upper, lower))
        first, last = strips
        even_ref[: odd_ref.shape[0], :, lanes] = jnp.where(even_col, last, first).astype(jnp.bfloat16)
        odd_ref[:, :, lanes] = jnp.where(even_col, first, last).astype(jnp.bfloat16)


def carrier_pair_kernel(own_ref, got_hbm, out_ref, got_s, pair_s, sem):
    per_row, here = own_ref.shape[1], own_ref.shape[0] * own_ref.shape[1]
    tiles = got_s.shape[0]
    copy = pltpu.make_async_copy(got_hbm.at[got_hbm.shape[0] - tiles :], got_s, sem)
    copy.start()
    for i in range(own_ref.shape[0]):
        pair_s[i * per_row : (i + 1) * per_row, :] = own_ref[i].astype(jnp.float32)
    copy.wait()
    pair_s[here:, :] = got_s[...].astype(jnp.float32).reshape(tiles * TILE, -1)[:here]
    out_ref[...] = pair_s[...].astype(jnp.bfloat16)


def pack_kernel(final_ref, *refs):
    parts, out_ref = refs[:-1], refs[-1]
    rows = final_ref.shape[0]
    out_ref[:rows, :] = final_ref[...]
    carriers = jnp.concatenate([part[...].astype(jnp.float32) for part in parts], axis=0)
    out_ref[rows:, :] = carriers.astype(jnp.bfloat16)


def own_kernel(x_ref, xq_ref):
    rows, cols, _ = x_ref.shape
    step = 4

    def own(i, _):
        at = pl.multiple_of(i * step, step)
        y = layer_normalise(x_ref[pl.ds(at, step)].astype(jnp.float32))
        for c in range(cols // TILE):
            piece = y[:, c * TILE : (c + 1) * TILE, :].reshape(step * TILE, -1)
            to = pl.multiple_of(c * rows * TILE + at * TILE, step * TILE)
            xq_ref[pl.ds(to, step * TILE), :] = piece.astype(jnp.bfloat16)
        return 0

    lax.fori_loop(0, rows // step, own, 0)


def halo_kernel(place_ref, xq_ref, mark_ref, even_rows_ref, odd_rows_ref, even_cols_ref, odd_cols_ref, xkv_ref, hide_ref, *scratch):
    rows, cols, _ = mark_ref.shape
    wide_rows, wide_cols = rows + 2 * RADIUS, cols + 2 * RADIUS
    half = wide_rows // 2
    step = 2
    top_s, bottom_s, left_s, right_s, top_ref, bottom_ref, left_ref, right_ref, flag_s = scratch
    for even, odd, low, high, low_flags, high_flags, parity, size in (
        (even_rows_ref, odd_rows_ref, top_s, bottom_s, top_ref, bottom_ref, EVEN_ROW, 2),
        (even_cols_ref, odd_cols_ref, left_s, right_s, left_ref, right_ref, EVEN_COL, 5),
    ):
        flip = place_ref[parity] > 0
        for i in range(0, odd.shape[0], size):
            a, b = even[i : i + size].astype(jnp.float32), odd[i : i + size].astype(jnp.float32)
            for lines, out, flags in ((jnp.where(flip, b, a), low, low_flags), (jnp.where(flip, a, b), high, high_flags)):
                out[i : i + size] = layer_normalise(lines)
                flags[i : i + size] = lines[:, :, :LANES]

    def lines_of(ref):
        return ref.astype(jnp.float32)

    def merge(at, blocks, left, right, to_ref):
        low = lax.broadcasted_iota(jnp.int32, (1, TILE, 1), 1) < RADIUS
        before = left
        for c in range(len(blocks) + 1):
            after = jnp.roll(blocks[c], RADIUS, axis=1) if c < len(blocks) else right
            to = c * wide_rows * TILE + at * TILE
            to = pl.multiple_of(to, step * TILE) if not isinstance(to, int) else to
            lines = jnp.where(low, before, after).reshape(step * TILE, -1)
            to_ref[pl.ds(to, step * TILE), :] = lines.astype(jnp.bfloat16)
            before = after

    def sides(at, upper, left_ref, right_ref, lanes):
        if upper:
            at = at - half
            left, right = jnp.roll(lines_of(left_ref[pl.ds(at, step), :, lanes]), RADIUS, axis=1), lines_of(
                right_ref[pl.ds(at, step), :, lanes]
            )
        else:
            left, right = lines_of(left_ref[pl.ds(at, step), :, lanes]), jnp.roll(
                lines_of(right_ref[pl.ds(at, step), :, lanes]), RADIUS, axis=1
            )
        return left, right

    every, few = slice(None), slice(0, LANES)

    def hide_if(border, lines):
        return jnp.where(place_ref[border] > 0, INVALID, lines)

    def mark_sides(at, upper):
        left, right = sides(at, upper, left_ref, right_ref, few)
        return hide_if(2, left), hide_if(3, right)

    def band(at, ref, ref_s, first, upper):
        cut = [slice(c * TILE, (c + 1) * TILE) for c in range(cols // TILE)]
        merge(at, [ref_s[first : first + step, k, :] for k in cut], *sides(at, upper, left_s, right_s, every), xkv_ref)
        marks = hide_if(int(upper), ref[first : first + step])
        beside = [hide_if(int(upper), side) for side in mark_sides(at, upper)]
        merge(at, [marks[:, k, :] for k in cut], *beside, flag_s)

    for i in range(0, RADIUS, step):
        band(i, top_ref, top_s, i, False)
        band(RADIUS + rows + i, bottom_ref, bottom_s, i, True)

    def middle(i, upper):
        at = pl.multiple_of(i * step, step)
        own = at - RADIUS
        blocks = []
        for c in range(cols // TILE):
            first = pl.multiple_of(c * rows * TILE + own * TILE, step * TILE)
            blocks.append(xq_ref[pl.ds(first, step * TILE), :].astype(jnp.float32).reshape(step, TILE, -1))
        merge(at, blocks, *sides(at, upper, left_s, right_s, every), xkv_ref)
        marks = mark_ref[pl.ds(own, step)].astype(jnp.float32)
        marks = [marks[:, c * TILE : (c + 1) * TILE, :] for c in range(cols // TILE)]
        merge(at, marks, *mark_sides(at, upper), flag_s)
        return 0

    lax.fori_loop(RADIUS // step, half // step, lambda i, _: middle(i, False), 0)
    lax.fori_loop(half // step, (RADIUS + rows) // step, lambda i, _: middle(i, True), 0)

    first_lane = (lax.broadcasted_iota(jnp.int32, (8, LANES), 1) == 0).astype(jnp.bfloat16)
    spans = []
    for c in range(wide_cols // TILE):
        lines = flag_s[c * wide_rows * TILE : (c + 1) * wide_rows * TILE, :]
        spans.append(jnp.where(nt(first_lane, lines) > INVALID / 2, HIDDEN, 0.0))
    tall = rows // TILE
    for c in range(cols // TILE):
        for r in range(tall):
            at = slice(r * TILE * TILE, r * TILE * TILE + 2 * TILE * TILE)
            hide_ref[c * tall + r] = jnp.concatenate([spans[c][:, at], spans[c + 1][:, at]], axis=1)


def project_kernel(whole, pieces, triple_rows, place_ref, *refs):
    sources, refs = refs[: len(whole) + len(pieces)], refs[len(whole) + len(pieces) :]
    xq_ref, xkv_ref, q_s, k_s, wt, sems = refs
    channels = wt.shape[1]
    groups = channels // GROUP
    factor = HEAD_DIM ** (-0.5) * LOG2_E
    me = place_ref[ROW]
    copies = []
    for j, source in enumerate(sources):
        if j < len(whole):
            to = (me ^ whole[j]) * triple_rows
        else:
            off, start = pieces[j - len(whole)]
            to = (me ^ off) * triple_rows + place_ref[STARTS + start]
        to = pl.multiple_of(to, 16)
        copy = pltpu.make_async_copy(source, wt.at[pl.ds(to, source.shape[0]), :], sems.at[j])
        copy.start()
        copies.append(copy)
    for copy in copies:
        copy.wait()

    q_rows, kv_rows = xq_ref.shape[0], xkv_ref.shape[0]
    q_chunk, kv_chunk = q_rows // 2, kv_rows // 4

    def project_q(n, _):
        w = wt[pl.ds(pl.multiple_of(n * GROUP, GROUP), GROUP), :]
        for m in range(0, q_rows, q_chunk):
            q_s[n, m : m + q_chunk, :] = (nt(xq_ref[m : m + q_chunk, :], w) * factor).astype(jnp.bfloat16)
        return 0

    def project_k(n, _):
        w = wt[pl.ds(pl.multiple_of(channels + n * GROUP, GROUP), GROUP), :]
        for m in range(0, kv_rows, kv_chunk):
            k_s[n, m : m + kv_chunk, :] = nt(xkv_ref[m : m + kv_chunk, :], w).astype(jnp.bfloat16)
        return 0

    lax.fori_loop(0, groups, project_q, 0)
    lax.fori_loop(0, groups, project_k, 0)


def value_kernel(wt, xkv_ref, v_s):
    channels = wt.shape[1]
    chunk = xkv_ref.shape[0] // 4

    def project_v(n, _):
        w = wt[pl.ds(pl.multiple_of(2 * channels + n * GROUP, GROUP), GROUP), :]
        for m in range(0, xkv_ref.shape[0], chunk):
            v_s[n, m : m + chunk, :] = nt(xkv_ref[m : m + chunk, :], w).astype(jnp.bfloat16)
        return 0

    lax.fori_loop(0, channels // GROUP, project_v, 0)


def carrier_kernel(offsets, place_ref, wt, *refs):
    shards = len(offsets)
    finals, refs = refs[:shards], refs[shards:]
    summary_ref, wo, kce, vc_s, carriers_s, sems = refs
    per_row = summary_ref.shape[1]
    channels = wt.shape[1]
    groups = channels // GROUP
    heads = channels // HEAD_DIM
    factor = HEAD_DIM ** (-0.5)
    carriers_here = vc_s.shape[0]
    final_rows = wo.shape[0] // shards
    copies = []
    for j, off in enumerate(offsets):
        to = pl.multiple_of((place_ref[ROW] ^ off) * final_rows, 16)
        copy = pltpu.make_async_copy(finals[j].at[0:final_rows, :], wo.at[pl.ds(to, final_rows), :], sems.at[j])
        copy.start()
        copies.append(copy)
    coming = []
    sent = carriers_s.shape[0] // shards
    for j in range(shards):
        source = finals[j].at[final_rows : final_rows + sent, :]
        copy = pltpu.make_async_copy(source, carriers_s.at[j * sent : (j + 1) * sent, :], sems.at[shards + j])
        copy.start()
        coming.append(copy)
    for copy in coming:
        copy.wait()
    carriers = carriers_s[...].astype(jnp.float32)
    own = carriers[:carriers_here]
    carriers = layer_normalise(carriers).astype(jnp.bfloat16)
    own_norm = layer_normalise(own).astype(jnp.bfloat16)
    qc = (nt(own_norm, wt[:channels, :]) * factor).astype(jnp.bfloat16).astype(jnp.float32)
    kc = nt(carriers, wt[channels : 2 * channels, :]).astype(jnp.bfloat16)
    vc = nt(carriers, wt[2 * channels :, :]).astype(jnp.bfloat16)
    head_of = lax.broadcasted_iota(jnp.int32, (1, channels), 1) // HEAD_DIM
    stacked = jnp.concatenate([jnp.where(head_of == h, qc, 0.0) for h in range(heads)], axis=0)
    e = jnp.exp(nt(stacked.astype(jnp.bfloat16), kc))
    weights = (e / jnp.sum(e, axis=-1, keepdims=True)).astype(jnp.bfloat16)
    o = nn(weights, vc)
    mix = jnp.zeros((carriers_here, channels), jnp.float32)
    for h in range(heads):
        mix = jnp.where(head_of == h, o[h * carriers_here : (h + 1) * carriers_here, :], mix)
    for copy in copies:
        copy.wait()
    renewed = own + nt(mix.astype(jnp.bfloat16), wo[...])
    for i in range(summary_ref.shape[0]):
        summary_ref[i] = renewed[i * per_row : (i + 1) * per_row, :].astype(jnp.bfloat16)
    fresh = nt(layer_normalise(renewed).astype(jnp.bfloat16), wt[channels:, :]).astype(jnp.bfloat16).astype(jnp.float32)
    vc_s[...] = fresh[:, channels:]
    same = (
        lax.broadcasted_iota(jnp.int32, (GROUP, GROUP), 0) // HEAD_DIM
        == lax.broadcasted_iota(jnp.int32, (GROUP, GROUP), 1) // HEAD_DIM
    )
    windows = kce.shape[0] // groups
    for w in range(windows):
        for g in range(groups):
            kce[w * groups + g] = jnp.where(same, fresh[w : w + 1, g * GROUP : (g + 1) * GROUP], 0.0).astype(jnp.bfloat16)


def attend_kernel(tall, broad, q_s, k_s, v_s, hide_ref, kce, vc_s, mix_s, pc_s, even_s, odd_s):
    groups, tiles = q_s.shape[0], hide_ref.shape[0]
    heads_in = GROUP // HEAD_DIM
    queries, span = TILE * TILE, 2 * TILE * TILE
    side = PATCH_SIDE // TILE
    wide = (tall + 1) * queries
    qi = lax.broadcasted_iota(jnp.int32, (queries, 2 * span), 0)
    ki = lax.broadcasted_iota(jnp.int32, (queries, 2 * span), 1)
    row_step = (ki % span) // TILE - qi // TILE
    col_step = (ki // span) * TILE + ki % TILE - qi % TILE
    seen = (row_step >= 0) & (row_step <= 2 * RADIUS) & (col_step >= 0) & (col_step <= 2 * RADIUS)
    band = jnp.where(seen, 0.0, HIDDEN)
    group_head = lax.broadcasted_iota(jnp.int32, (1, GROUP), 1) // HEAD_DIM
    only = [jnp.where(group_head == h, 1.0, 0.0).astype(jnp.bfloat16) for h in range(heads_in)]
    in_pair = LANES // HEAD_DIM
    pair_head = lax.broadcasted_iota(jnp.int32, (1, LANES), 1) // HEAD_DIM

    for c in range(broad):
        for w in range(tall // side):
            at = slice((c * tall + w * side) * queries, (c * tall + (w + 1) * side) * queries)
            window = w * (broad // side) + c // side
            for g in range(groups):
                pc_s[at, g * GROUP : (g + 1) * GROUP] = jnp.exp2(nt(q_s[g, at, :], kce[window * groups + g]))

    def keys_at(t):
        k0 = pl.multiple_of(t // tall * wide + t % tall * queries, queries)
        return k0, pl.multiple_of(k0 + wide, queries)

    def scores(t, ref):
        q_at = pl.multiple_of(t * queries, queries)
        k0, k1 = keys_at(t)
        for g in range(groups):
            q = q_s[g, pl.ds(q_at, queries), :]
            qq = jnp.concatenate([q * mask for mask in only], axis=0)
            k = jnp.concatenate([k_s[g, pl.ds(k0, span), :], k_s[g, pl.ds(k1, span), :]], axis=0)
            ref[g] = nt(qq, k)

    def finish(t, ref):
        q_at = pl.multiple_of(t * queries, queries)
        k0, k1 = keys_at(t)
        window = t % tall // side * (broad // side) + t // tall // side
        bias = band + hide_ref[t][0:1, :]
        for g in range(groups):
            p = jnp.exp2(ref[g].reshape(heads_in, queries, 2 * span) + bias[None])
            total = jnp.sum(p, axis=-1, keepdims=True)
            v = jnp.concatenate([v_s[g, pl.ds(k0, span), :], v_s[g, pl.ds(k1, span), :]], axis=0)
            o = nn(p.reshape(heads_in * queries, 2 * span).astype(jnp.bfloat16), v).reshape(heads_in, queries, GROUP)
            v_new = vc_s[pl.ds(window, 1), g * GROUP : (g + 1) * GROUP]
            for j in range(GROUP // LANES):
                lanes = slice(j * LANES, (j + 1) * LANES)
                at = slice(g * GROUP + j * LANES, g * GROUP + (j + 1) * LANES)
                kept, kept_total = o[j * in_pair, :, lanes], total[j * in_pair]
                for h in range(1, in_pair):
                    kept = jnp.where(pair_head == h, o[j * in_pair + h, :, lanes], kept)
                    kept_total = jnp.where(pair_head == h, total[j * in_pair + h], kept_total)
                new = pc_s[pl.ds(q_at, queries), at]
                mixed = (kept + new * v_new[:, lanes]) / (kept_total + new)
                mix_s[pl.ds(q_at, queries), at] = mixed.astype(jnp.bfloat16)

    scores(0, even_s)

    def two(i, _):
        t = 2 * i
        scores(t + 1, odd_s)
        finish(t, even_s)
        scores(jnp.minimum(t + 2, tiles - 1), even_s)
        finish(t + 1, odd_s)
        return 0

    lax.fori_loop(0, tiles // 2, two, 0)


def out_kernel(x_ref, mix_s, wo, out_hbm, out_ref, out_sems):
    rows, cols, channels = x_ref.shape
    going = []
    for pair in range(cols // (2 * TILE)):
        both = slice(2 * pair * TILE, 2 * (pair + 1) * TILE)
        for g in range(channels // GROUP):
            at = slice(g * GROUP, (g + 1) * GROUP)
            w = wo[at, :]
            y = nt(mix_s[2 * pair * rows * TILE : 2 * (pair + 1) * rows * TILE, :], w).reshape(2, rows, TILE, GROUP)
            y = jnp.concatenate([y[0], y[1]], axis=1) + x_ref[:, both, at].astype(jnp.float32)
            out_ref[pair, :, :, at] = y.astype(jnp.bfloat16)
        copy = pltpu.make_async_copy(out_ref.at[pair], out_hbm.at[:, both, :], out_sems.at[pair])
        copy.start()
        going.append(copy)
    for copy in going:
        copy.wait()


def local(grid_elements, summary_vectors, triple_projection, final_projection, genuine_flags):
    rows, cols, channels = grid_elements.shape
    wide_rows, wide_cols = rows + 2 * RADIUS, cols + 2 * RADIUS

    triple_t, final_t = triple_projection.T, final_projection.T
    vmem = pl.BlockSpec(memory_space=pltpu.VMEM)
    anywhere = pl.BlockSpec(memory_space=pl.ANY)
    scalars = pl.BlockSpec(memory_space=pltpu.SMEM)
    hbm = pl.BlockSpec(memory_space=pltpu.HBM)
    small = pltpu.CompilerParams(vmem_limit_bytes=8 * 1024 * 1024)
    row_strip = jax.ShapeDtypeStruct((RADIUS, cols, channels), jnp.bfloat16)
    col_strip = jax.ShapeDtypeStruct((wide_rows // 2, 2 * RADIUS, channels), jnp.bfloat16)

    row, col, img = lax.axis_size("row"), lax.axis_size("col"), lax.axis_size("img")
    row_at, col_at, img_at = lax.axis_index("row"), lax.axis_index("col"), lax.axis_index("img")
    row_bits = bits_of(row)
    far, rest = row_bits[0], row_bits[1:]
    piece_rows = triple_t.shape[0] // (1 + img) // 16 * 16
    relays = img if piece_rows else 0
    starts = [(img_at - k) % img for k in range(relays)] + [jnp.int32(relays)]
    place = [row_at == 0, row_at == row - 1, col_at == 0, col_at == col - 1, row_at % 2 == 0, col_at % 2 == 0, row_at]
    place = jnp.stack([jnp.asarray(p).astype(jnp.int32) for p in place + [start * piece_rows for start in starts]])

    mark, even_rows, odd_rows, x = pl.pallas_call(
        edge_kernel,
        out_shape=(
            pltpu.VMEM((rows, cols, LANES), jnp.bfloat16),
            pltpu.VMEM(row_strip.shape, jnp.bfloat16),
            pltpu.VMEM(row_strip.shape, jnp.bfloat16),
            pltpu.VMEM(grid_elements.shape, jnp.bfloat16),
        ),
        in_specs=[scalars, hbm, hbm],
        out_specs=(vmem,) * 4,
        scratch_shapes=[
            pltpu.VMEM((rows, cols), jnp.int32),
            pltpu.VMEM((rows * cols, cols), jnp.bfloat16),
            pltpu.SemaphoreType.DMA((2,)),
        ],
        compiler_params=small,
        cost_estimate=pl.CostEstimate(flops=1_000_000, bytes_accessed=1_000_000, transcendentals=0),
        name="edge_rows",
    )(place, *(pltpu.with_memory_space_constraint(a, pltpu.HBM) for a in (genuine_flags, grid_elements)))
    mine, last = pl.pallas_call(
        piece_kernel,
        out_shape=(
            pltpu.VMEM((max(piece_rows, 16), channels), jnp.bfloat16),
            pltpu.VMEM((triple_t.shape[0] - relays * piece_rows, channels), jnp.bfloat16),
        ),
        in_specs=[scalars, hbm],
        out_specs=(vmem, vmem),
        scratch_shapes=[pltpu.SemaphoreType.DMA((2,))],
        compiler_params=small,
        cost_estimate=pl.CostEstimate(flops=1_000_000, bytes_accessed=1_000_000, transcendentals=0),
        name="pieces",
    )(place, pltpu.with_memory_space_constraint(after(triple_t, even_rows), pltpu.HBM))
    xq = pl.pallas_call(
        own_kernel,
        out_shape=pltpu.VMEM((rows * cols, channels), jnp.bfloat16),
        in_specs=[vmem],
        out_specs=vmem,
        compiler_params=small,
        cost_estimate=pl.CostEstimate(flops=1_000_000, bytes_accessed=1_000_000, transcendentals=0),
        name="own_norm",
    )(x)
    even_rows, odd_rows = pair_swapped(even_rows, odd_rows, "row")

    far_pieces = []
    if relays:
        first = swapped(mine, "row", far)
    far_last = swapped(after(last, even_rows, odd_rows), "row", far)

    own_rows = summary_vectors.shape[0] * summary_vectors.shape[1]
    carrier_tiles = -(-own_rows // TILE)
    even_cols, odd_cols = pl.pallas_call(
        strip_kernel,
        out_shape=(
            pltpu.VMEM((col_strip.shape[0] + carrier_tiles, *col_strip.shape[1:]), jnp.bfloat16),
            pltpu.VMEM(col_strip.shape, jnp.bfloat16),
        ),
        in_specs=[scalars] + [vmem] * 5,
        out_specs=(vmem,) * 2,
        scratch_shapes=[pltpu.VMEM((carrier_tiles * TILE, channels), jnp.float32)],
        compiler_params=small,
        cost_estimate=pl.CostEstimate(flops=1_000_000, bytes_accessed=2_000_000, transcendentals=0),
        name="edge_columns",
    )(place, x, after(mark, xq), even_rows, odd_rows, summary_vectors)
    even_cols, odd_cols = pair_swapped(even_cols, odd_cols, "col")
    carriers = pl.pallas_call(
        carrier_pair_kernel,
        out_shape=pltpu.VMEM((2 * own_rows, channels), jnp.bfloat16),
        in_specs=[vmem, anywhere],
        out_specs=vmem,
        scratch_shapes=[
            pltpu.VMEM((carrier_tiles, TILE, channels), jnp.bfloat16),
            pltpu.VMEM((2 * own_rows, channels), jnp.float32),
            pltpu.SemaphoreType.DMA,
        ],
        compiler_params=small,
        cost_estimate=pl.CostEstimate(flops=1_000, bytes_accessed=1_000, transcendentals=0),
        name="carrier_pair",
    )(summary_vectors, even_cols)
    parts = [carriers]
    for bit in bits_of(col)[:-1]:
        carriers = carriers if len(parts) == 1 else jnp.concatenate(parts, axis=0)
        got = swapped(carriers, "col", 2 * bit - 1)
        parts.append(got)
    if relays:
        first = after(first, even_cols, odd_cols, parts[0])
        others = [lax.ppermute(first, "img", [(i, (i + k) % img) for i in range(img)]) for k in range(1, relays)]
        far_pieces = [first] + others
    far_pieces.append(far_last)

    final_pack = pl.pallas_call(
        pack_kernel,
        out_shape=pltpu.VMEM((final_t.shape[0] + col * own_rows, channels), jnp.bfloat16),
        in_specs=[vmem] * (1 + len(parts)),
        out_specs=vmem,
        compiler_params=small,
        cost_estimate=pl.CostEstimate(flops=1_000, bytes_accessed=1_000, transcendentals=0),
        name="final_pack",
    )(final_t, *parts)
    finals, triples, offsets = [final_pack], [triple_t], [0]
    for bit in rest:
        finals = finals + [swapped(p, "row", bit) for p in finals]
        triples = triples + [swapped(p, "row", bit) for p in triples]
        offsets = offsets + [o ^ bit for o in offsets]
    tiles = (rows // TILE) * (cols // TILE)
    keys = 4 * TILE * TILE
    xkv, hide = pl.pallas_call(
        halo_kernel,
        out_shape=(
            pltpu.VMEM((wide_rows * wide_cols, channels), jnp.bfloat16),
            pltpu.VMEM((tiles, 8, keys), jnp.float32),
        ),
        in_specs=[scalars] + [vmem] * 6,
        out_specs=(vmem,) * 2,
        scratch_shapes=[
            *[pltpu.VMEM(shape.shape, jnp.float32) for shape in (row_strip, row_strip, col_strip, col_strip)],
            *[pltpu.VMEM((*shape.shape[:2], LANES), jnp.float32) for shape in (row_strip, row_strip, col_strip, col_strip)],
            pltpu.VMEM((wide_rows * wide_cols, LANES), jnp.bfloat16),
        ],
        compiler_params=pltpu.CompilerParams(vmem_limit_bytes=12 * 1024 * 1024),
        cost_estimate=pl.CostEstimate(flops=10_000_000, bytes_accessed=6_000_000, transcendentals=1000),
        name="halo_norm",
    )(place, after(xq, got), mark, even_rows, odd_rows, even_cols, odd_cols)

    far_final = swapped(final_pack, "row", far)

    far_offsets = [far]
    far_pieces = [[after(piece, xkv)] for piece in far_pieces]
    for bit in rest:
        far_pieces = [same + [swapped(p, "row", bit) for p in same] for same in far_pieces]
        far_offsets = far_offsets + [o ^ bit for o in far_offsets]

    groups = channels // GROUP
    numbered = [(off, number) for number in range(len(far_pieces)) for off in far_offsets]
    sources = triples + [piece for same in far_pieces for piece in same]
    q, k, wt = pl.pallas_call(
        functools.partial(project_kernel, offsets, numbered, triple_t.shape[0]),
        out_shape=(
            jax.ShapeDtypeStruct((groups, rows * cols, GROUP), jnp.bfloat16),
            jax.ShapeDtypeStruct((groups, wide_rows * wide_cols, GROUP), jnp.bfloat16),
            jax.ShapeDtypeStruct((3 * channels, channels), jnp.bfloat16),
        ),
        in_specs=[scalars] + [anywhere] * len(sources) + [vmem] * 2,
        out_specs=(vmem,) * 3,
        scratch_shapes=[pltpu.SemaphoreType.DMA((len(sources),))],
        compiler_params=pltpu.CompilerParams(vmem_limit_bytes=VMEM_BYTES),
        cost_estimate=pl.CostEstimate(flops=1_000_000, bytes_accessed=1_000_000, transcendentals=0),
        name="project",
    )(place, *sources, xq, xkv)

    v = pl.pallas_call(
        value_kernel,
        out_shape=jax.ShapeDtypeStruct((groups, wide_rows * wide_cols, GROUP), jnp.bfloat16),
        in_specs=[vmem] * 2,
        out_specs=vmem,
        compiler_params=pltpu.CompilerParams(vmem_limit_bytes=VMEM_BYTES),
        cost_estimate=pl.CostEstimate(flops=3_000_000_000, bytes_accessed=7_000_000, transcendentals=0),
        name="values",
    )(wt, xkv)

    far_finals = [after(far_final, q)]
    for bit in rest:
        far_finals = far_finals + [swapped(p, "row", bit) for p in far_finals]
    finals, offsets = finals + far_finals, offsets + far_offsets
    carriers_here = carrier_tiles * TILE
    summary_result, wo, kce, vc = pl.pallas_call(
        functools.partial(carrier_kernel, offsets),
        out_shape=(
            jax.ShapeDtypeStruct(summary_vectors.shape, jnp.bfloat16),
            jax.ShapeDtypeStruct((channels, channels), jnp.bfloat16),
            jax.ShapeDtypeStruct((own_rows * groups, GROUP, GROUP), jnp.bfloat16),
            jax.ShapeDtypeStruct((carriers_here, channels), jnp.float32),
        ),
        in_specs=[scalars, vmem] + [anywhere] * len(finals),
        out_specs=(vmem,) * 4,
        scratch_shapes=[
            pltpu.VMEM((row * col * own_rows, channels), jnp.bfloat16),
            pltpu.SemaphoreType.DMA((2 * len(finals),)),
        ],
        compiler_params=pltpu.CompilerParams(vmem_limit_bytes=VMEM_BYTES),
        cost_estimate=pl.CostEstimate(flops=500_000_000, bytes_accessed=5_000_000, transcendentals=10_000),
        name="carriers",
    )(place, wt, *finals)

    scores = (groups, GROUP // HEAD_DIM * TILE * TILE, keys)
    mix = pl.pallas_call(
        functools.partial(attend_kernel, rows // TILE, cols // TILE),
        out_shape=jax.ShapeDtypeStruct((rows * cols, channels), jnp.bfloat16),
        in_specs=[vmem] * 6,
        out_specs=vmem,
        scratch_shapes=[
            pltpu.VMEM((rows * cols, channels), jnp.float32),
            pltpu.VMEM(scores, jnp.float32),
            pltpu.VMEM(scores, jnp.float32),
        ],
        compiler_params=pltpu.CompilerParams(vmem_limit_bytes=VMEM_BYTES),
        cost_estimate=pl.CostEstimate(flops=4_000_000_000, bytes_accessed=12_000_000, transcendentals=4_000_000),
        name="attend",
    )(q, k, v, hide, kce, vc)

    out = pl.pallas_call(
        out_kernel,
        out_shape=jax.ShapeDtypeStruct(grid_elements.shape, jnp.bfloat16),
        in_specs=[vmem] * 3,
        out_specs=anywhere,
        scratch_shapes=[
            pltpu.VMEM((cols // (2 * TILE), rows, 2 * TILE, channels), jnp.bfloat16),
            pltpu.SemaphoreType.DMA((cols // (2 * TILE),)),
        ],
        compiler_params=pltpu.CompilerParams(vmem_limit_bytes=VMEM_BYTES),
        cost_estimate=pl.CostEstimate(flops=1_200_000_000, bytes_accessed=6_000_000, transcendentals=0),
        name="out",
    )(x, mix, wo)
    return (out, summary_result)


def solution(mesh):
    placed = (
        P(("img", "row"), "col", None),
        P(("img", "row"), "col", None),
        P(None, "row"),
        P(None, "row"),
        P(("img", "row"), "col"),
    )
    return jax.shard_map(
        local,
        mesh=mesh,
        in_specs=placed,
        out_specs=(P(("img", "row"), "col", None), P(("img", "row"), "col", None)),
        check_vma=False,
    )
```

```python
import functools

import jax
import jax.numpy as jnp
from jax import lax
from jax.experimental import pallas as pl
from jax.experimental.pallas import tpu as pltpu
from jax.sharding import PartitionSpec as P

HEAD_DIM = 64
PATCH_SIDE = 16
RADIUS = 4
TILE = 2 * RADIUS
LANES = 128
GROUP = 256
INVALID = 100.0
HIDDEN = -1e30
LOG2_E = 1.4426950408889634
EVEN_ROW, EVEN_COL, ROW, HALF, STARTS = 4, 5, 6, 7, 8
VMEM_BYTES = 26 * 1024 * 1024


def nt(a, b):
    return lax.dot_general(a, b, (((1,), (1,)), ((), ())), preferred_element_type=jnp.float32)


def nn(a, b):
    return lax.dot_general(a, b, (((1,), (0,)), ((), ())), preferred_element_type=jnp.float32)


def layer_normalise(lines):
    center = lines - jnp.mean(lines, axis=-1, keepdims=True)
    spread = jnp.mean(center * center, axis=-1, keepdims=True)
    return center * lax.rsqrt(spread + 1e-05)


def pair_swapped(even_block, odd_block, axis):
    count = lax.axis_size(axis)
    got = []
    for first, block in ((0, even_block), (1, odd_block)):
        pairs = [(i, i + 1) for i in range(first, count - 1, 2)]
        got.append(lax.ppermute(block, axis, pairs + [(b, a) for a, b in pairs]))
    return got


def swapped(block, axis, bit):
    count = lax.axis_size(axis)
    return lax.ppermute(block, axis, [(i, i ^ bit) for i in range(count)])


def after(block, *others):
    return lax.optimization_barrier((block, *others))[0]


def bits_of(count):
    bits, bit = [], count // 2
    while bit:
        bits.append(bit)
        bit //= 2
    return bits


def marked_lanes(lines, hidden):
    first = jnp.where(hidden, INVALID, lines[:, :, :LANES])
    return jnp.concatenate([first, lines[:, :, LANES:]], axis=2)


def edge_kernel(place_ref, flags_hbm, x_hbm, mark_ref, even_ref, odd_ref, x_ref, *scratch):
    flags_ref, spread, sems = scratch
    rows, cols = flags_ref.shape
    flags_copy = pltpu.make_async_copy(flags_hbm, flags_ref, sems.at[0])
    x_copy = pltpu.make_async_copy(x_hbm, x_ref, sems.at[1])
    flags_copy.start()
    x_copy.start()
    flags_copy.wait()
    row_at = lax.broadcasted_iota(jnp.int32, (cols, cols), 0)
    diagonal = row_at == lax.broadcasted_iota(jnp.int32, (cols, cols), 1)
    for r in range(rows):
        hidden = jnp.where(flags_ref[r : r + 1, :] > 0, 0.0, INVALID)
        spread[r * cols : (r + 1) * cols, :] = jnp.where(diagonal, hidden, 0.0).astype(jnp.bfloat16)
    marks = nn(spread[...], jnp.ones((cols, LANES), jnp.bfloat16)).reshape(rows, cols, LANES)
    mark_ref[...] = marks.astype(jnp.bfloat16)
    x_copy.wait()
    first, last = [
        marked_lanes(x_ref[at].astype(jnp.float32), marks[at] > INVALID / 2)
        for at in (slice(0, RADIUS), slice(rows - RADIUS, rows))
    ]
    even = place_ref[EVEN_ROW] > 0
    even_ref[...] = jnp.where(even, last, first).astype(jnp.bfloat16)
    odd_ref[...] = jnp.where(even, first, last).astype(jnp.bfloat16)


def piece_kernel(place_ref, triple_hbm, mine_ref, last_ref, sems):
    start = pl.multiple_of(place_ref[STARTS], 16)
    last = triple_hbm.shape[0] - last_ref.shape[0]
    copies = [
        pltpu.make_async_copy(triple_hbm.at[pl.ds(start, mine_ref.shape[0]), :], mine_ref, sems.at[0]),
        pltpu.make_async_copy(triple_hbm.at[last:, :], last_ref, sems.at[1]),
    ]
    for copy in copies:
        copy.start()
    for copy in copies:
        copy.wait()


def strip_kernel(place_ref, x_ref, mark_ref, even_rows_ref, odd_rows_ref, carriers_ref, even_ref, odd_ref, carriers_s):
    per_row = carriers_ref.shape[1]
    carriers_s[...] = jnp.zeros_like(carriers_s)
    for i in range(carriers_ref.shape[0]):
        carriers_s[i * per_row : (i + 1) * per_row, :] = carriers_ref[i].astype(jnp.float32)
    for i in range(carriers_s.shape[0] // TILE):
        even_ref[odd_ref.shape[0] + i] = carriers_s[i * TILE : (i + 1) * TILE, :].astype(jnp.bfloat16)
    rows, cols, channels = x_ref.shape
    middle = rows // 2
    low = lax.broadcasted_iota(jnp.int32, (1, TILE, 1), 1) < RADIUS
    even_row, even_col = place_ref[EVEN_ROW] > 0, place_ref[EVEN_COL] > 0
    for lane in range(0, channels, LANES):
        lanes = slice(lane, lane + LANES)
        strips = []
        for columns, last in ((slice(0, TILE), False), (slice(cols - TILE, cols), True)):

            def own(part):
                lines = x_ref[part, columns, lanes].astype(jnp.float32)
                if lane == 0:
                    lines = jnp.where(mark_ref[part, columns, :].astype(jnp.float32) > INVALID / 2, INVALID, lines)
                return lines

            even_rows = even_rows_ref[:, columns, lanes].astype(jnp.float32)
            odd_rows = odd_rows_ref[:, columns, lanes].astype(jnp.float32)
            top, bottom = jnp.where(even_row, odd_rows, even_rows), jnp.where(even_row, even_rows, odd_rows)
            upper = jnp.concatenate([top, own(slice(0, middle))], axis=0)
            lower = jnp.concatenate([own(slice(middle, rows)), bottom], axis=0)
            if last:
                upper = jnp.roll(upper, RADIUS, axis=1)
            else:
                lower = jnp.roll(lower, RADIUS, axis=1)
            strips.append(jnp.where(low, upper, lower))
        first, last = strips
        even_ref[: odd_ref.shape[0], :, lanes] = jnp.where(even_col, last, first).astype(jnp.bfloat16)
        odd_ref[:, :, lanes] = jnp.where(even_col, first, last).astype(jnp.bfloat16)


def carrier_pair_kernel(own_ref, got_hbm, out_ref, got_s, pair_s, sem):
    per_row, here = own_ref.shape[1], own_ref.shape[0] * own_ref.shape[1]
    tiles = got_s.shape[0]
    copy = pltpu.make_async_copy(got_hbm.at[got_hbm.shape[0] - tiles :], got_s, sem)
    copy.start()
    for i in range(own_ref.shape[0]):
        pair_s[i * per_row : (i + 1) * per_row, :] = own_ref[i].astype(jnp.float32)
    copy.wait()
    pair_s[here:, :] = got_s[...].astype(jnp.float32).reshape(tiles * TILE, -1)[:here]
    out_ref[...] = pair_s[...].astype(jnp.bfloat16)


def pack_kernel(final_ref, *refs):
    parts, out_ref = refs[:-1], refs[-1]
    rows = final_ref.shape[0]
    out_ref[:rows, :] = final_ref[...]
    carriers = jnp.concatenate([part[...].astype(jnp.float32) for part in parts], axis=0)
    out_ref[rows:, :] = carriers.astype(jnp.bfloat16)


def own_kernel(x_ref, xq_ref):
    rows, cols, _ = x_ref.shape
    step = 4

    def own(i, _):
        at = pl.multiple_of(i * step, step)
        y = layer_normalise(x_ref[pl.ds(at, step)].astype(jnp.float32))
        for c in range(cols // TILE):
            piece = y[:, c * TILE : (c + 1) * TILE, :].reshape(step * TILE, -1)
            to = pl.multiple_of(c * rows * TILE + at * TILE, step * TILE)
            xq_ref[pl.ds(to, step * TILE), :] = piece.astype(jnp.bfloat16)
        return 0

    lax.fori_loop(0, rows // step, own, 0)


def columns_of(lines):
    return [lines[:, c : c + TILE, :] for c in range(0, lines.shape[1], TILE)]


def tile_of(xq_ref, column, rows, at, step):
    first = pl.multiple_of(column * rows * TILE + at * TILE, step * TILE)
    return xq_ref[pl.ds(first, step * TILE), :].astype(jnp.float32).reshape(step, TILE, -1)


def store_lines(ref, block, wide_rows, at, lines):
    size = lines.shape[0] * TILE
    to = block * wide_rows * TILE + at * TILE
    to = to if isinstance(to, int) else pl.multiple_of(to, size)
    ref[pl.ds(to, size), :] = lines.reshape(size, -1).astype(jnp.bfloat16)


def middle_kernel(place_ref, xq_ref, even_rows_ref, odd_rows_ref, mid_ref, top_s, bottom_s):
    cols = even_rows_ref.shape[1]
    rows, step = xq_ref.shape[0] // cols, 2
    wide_rows = rows + 2 * RADIUS
    flip = place_ref[EVEN_ROW] > 0
    for i in range(0, RADIUS, step):
        a, b = even_rows_ref[i : i + step].astype(jnp.float32), odd_rows_ref[i : i + step].astype(jnp.float32)
        top_s[i : i + step] = layer_normalise(jnp.where(flip, b, a))
        bottom_s[i : i + step] = layer_normalise(jnp.where(flip, a, b))
    low = lax.broadcasted_iota(jnp.int32, (1, TILE, 1), 1) < RADIUS

    def merge(at, blocks):
        moved = [jnp.roll(block, RADIUS, axis=1) for block in blocks]
        for c in range(1, len(blocks)):
            store_lines(mid_ref, c - 1, wide_rows, at, jnp.where(low, moved[c - 1], moved[c]))

    for i in range(0, RADIUS, step):
        merge(i, columns_of(top_s[i : i + step]))
        merge(RADIUS + rows + i, columns_of(bottom_s[i : i + step]))

    def middle(i, _):
        at = pl.multiple_of(i * step, step)
        merge(RADIUS + at, [tile_of(xq_ref, c, rows, at, step) for c in range(cols // TILE)])
        return 0

    lax.fori_loop(0, rows // step, middle, 0)


def outer_kernel(place_ref, xq_ref, mark_ref, even_rows_ref, odd_rows_ref, even_cols_ref, odd_cols_ref, outer_ref, hide_ref, *scratch):
    rows, cols, _ = mark_ref.shape
    wide_rows, wide_cols = rows + 2 * RADIUS, cols + 2 * RADIUS
    half = wide_rows // 2
    step = 2
    top_s, bottom_s, left_s, right_s, top_ref, bottom_ref, left_ref, right_ref, flag_s = scratch
    flip = place_ref[EVEN_ROW] > 0
    a, b = even_rows_ref[...].astype(jnp.float32), odd_rows_ref[...].astype(jnp.float32)
    for lines, out, flags in ((jnp.where(flip, b, a), top_s, top_ref), (jnp.where(flip, a, b), bottom_s, bottom_ref)):
        ends = jnp.concatenate([lines[:, :TILE, :], lines[:, cols - TILE :, :]], axis=1)
        out[...] = layer_normalise(ends)
        flags[...] = lines[:, :, :LANES]
    flip = place_ref[EVEN_COL] > 0
    size = 5
    for i in range(0, odd_cols_ref.shape[0], size):
        a, b = even_cols_ref[i : i + size].astype(jnp.float32), odd_cols_ref[i : i + size].astype(jnp.float32)
        for lines, out, flags in ((jnp.where(flip, b, a), left_s, left_ref), (jnp.where(flip, a, b), right_s, right_ref)):
            out[i : i + size] = layer_normalise(lines)
            flags[i : i + size] = lines[:, :, :LANES]
    low = lax.broadcasted_iota(jnp.int32, (1, TILE, 1), 1) < RADIUS

    def lines_of(ref):
        return ref.astype(jnp.float32)

    def merge(at, blocks, left, right, to_ref):
        moved = [left] + [jnp.roll(block, RADIUS, axis=1) for block in blocks] + [right]
        for c in range(len(blocks) + 1):
            store_lines(to_ref, c, wide_rows, at, jnp.where(low, moved[c], moved[c + 1]))

    def merge_ends(at, first, last, left, right):
        store_lines(outer_ref, 0, wide_rows, at, jnp.where(low, left, jnp.roll(first, RADIUS, axis=1)))
        store_lines(outer_ref, 1, wide_rows, at, jnp.where(low, jnp.roll(last, RADIUS, axis=1), right))

    def sides(at, upper, left_ref, right_ref, lanes):
        if upper:
            at = at - half
            left, right = jnp.roll(lines_of(left_ref[pl.ds(at, step), :, lanes]), RADIUS, axis=1), lines_of(
                right_ref[pl.ds(at, step), :, lanes]
            )
        else:
            left, right = lines_of(left_ref[pl.ds(at, step), :, lanes]), jnp.roll(
                lines_of(right_ref[pl.ds(at, step), :, lanes]), RADIUS, axis=1
            )
        return left, right

    every, few = slice(None), slice(0, LANES)

    def hide_if(border, lines):
        return jnp.where(place_ref[border] > 0, INVALID, lines)

    def mark_sides(at, upper):
        left, right = sides(at, upper, left_ref, right_ref, few)
        return hide_if(2, left), hide_if(3, right)

    def band(at, ref, ref_s, first, upper):
        merge_ends(at, *columns_of(ref_s[first : first + step]), *sides(at, upper, left_s, right_s, every))
        marks = hide_if(int(upper), ref[first : first + step])
        beside = [hide_if(int(upper), side) for side in mark_sides(at, upper)]
        merge(at, columns_of(marks), *beside, flag_s)

    for i in range(0, RADIUS, step):
        band(i, top_ref, top_s, i, False)
        band(RADIUS + rows + i, bottom_ref, bottom_s, i, True)

    def middle(i, upper):
        at = pl.multiple_of(i * step, step)
        own = at - RADIUS
        ends = [tile_of(xq_ref, c, rows, own, step) for c in (0, cols // TILE - 1)]
        merge_ends(at, *ends, *sides(at, upper, left_s, right_s, every))
        merge(at, columns_of(mark_ref[pl.ds(own, step)].astype(jnp.float32)), *mark_sides(at, upper), flag_s)
        return 0

    lax.fori_loop(RADIUS // step, half // step, lambda i, _: middle(i, False), 0)
    lax.fori_loop(half // step, (RADIUS + rows) // step, lambda i, _: middle(i, True), 0)

    first_lane = (lax.broadcasted_iota(jnp.int32, (8, LANES), 1) == 0).astype(jnp.bfloat16)
    spans = []
    for c in range(wide_cols // TILE):
        lines = flag_s[c * wide_rows * TILE : (c + 1) * wide_rows * TILE, :]
        spans.append(jnp.where(nt(first_lane, lines) > INVALID / 2, HIDDEN, 0.0))
    tall = rows // TILE
    for c in range(cols // TILE):
        for r in range(tall):
            at = slice(r * TILE * TILE, r * TILE * TILE + 2 * TILE * TILE)
            hide_ref[c * tall + r] = jnp.concatenate([spans[c][:, at], spans[c + 1][:, at]], axis=1)


def column_chunks(channels, half):
    at, end = half * 3 * channels // 2, (half + 1) * 3 * channels // 2
    chunks = []
    while at < end:
        width = min(GROUP - at % GROUP, end - at)
        chunks.append((at, at // channels, at % channels // GROUP, at % GROUP, width))
        at += width
    return chunks


def numbered_chunks(channels, half):
    number, chunks = 0, []
    for chunk in column_chunks(channels, half):
        chunks.append((number, *chunk))
        number += chunk[-1] == GROUP
    return chunks


def project_lines(source, w, parts, factor, put):
    size = source.shape[0] // parts
    for m in range(0, source.shape[0], size):
        y = nt(source[m : m + size, :], w)
        put(slice(m, m + size), (y if factor == 1 else y * factor).astype(jnp.bfloat16))


QUERY_FACTOR = HEAD_DIM ** (-0.5) * LOG2_E


def early_kernel(offsets, place_ref, *refs):
    triples, refs = refs[: len(offsets)], refs[len(offsets) :]
    xq_ref, mid_ref, whole_ref, part_ref, near, sems = refs
    channels = near.shape[1]
    triple_rows = near.shape[0] // len(offsets)
    copies = []
    for j, off in enumerate(offsets):
        to = pl.multiple_of(((place_ref[ROW] ^ off) % len(offsets)) * triple_rows, 16)
        copies.append(pltpu.make_async_copy(triples[j], near.at[pl.ds(to, triple_rows), :], sems.at[j]))
        copies[-1].start()
    for copy in copies:
        copy.wait()

    def run(half):
        for number, at, section, _, _, width in numbered_chunks(channels, half):
            w = near[at - half * near.shape[0] : at - half * near.shape[0] + width, :]

            def put(lines, value, number=number, width=width):
                if width == GROUP:
                    whole_ref[number, lines, :] = value
                else:
                    part_ref[lines, :] = value

            if section == 0:
                project_lines(xq_ref, w, 2, QUERY_FACTOR, put)
            else:
                project_lines(mid_ref, w, 2, 1, put)

    for half in range(2):
        pl.when(place_ref[HALF] == half)(functools.partial(run, half))


def project_rest(half, sections, channels, near_at, far_at, sources, take, put):
    xq_ref, mid_ref, outer_ref = sources
    edge, mid = outer_ref.shape[0] // 2, mid_ref.shape[0]
    for number, at, section, group, lane, width in numbered_chunks(channels, half):
        if section in sections and section > 0:
            w = near_at(at, width)
            for first, to in ((0, 0), (edge, edge + mid)):
                put(section, group, lane, width, slice(to, to + edge), nt(outer_ref[first : first + edge, :], w).astype(jnp.bfloat16))
    take()
    for at, section, group, lane, width in column_chunks(channels, 1 - half):
        if section not in sections:
            continue
        w = far_at(at, width)
        if section == 0:
            project_lines(xq_ref, w, 2, QUERY_FACTOR, functools.partial(put, section, group, lane, width))
            continue
        for first, to in ((0, 0), (edge, edge + mid)):
            put(section, group, lane, width, slice(to, to + edge), nt(outer_ref[first : first + edge, :], w).astype(jnp.bfloat16))

        def put_mid(lines, value, section=section, group=group, lane=lane, width=width):
            put(section, group, lane, width, slice(edge + lines.start, edge + lines.stop), value)

        project_lines(mid_ref, w, 2, 1, put_mid)


def late_kernel(pieces, triple_rows, place_ref, *refs):
    sources, refs = refs[: len(pieces)], refs[len(pieces) :]
    near, whole_ref, part_ref, xq_ref, mid_ref, outer_ref, q_s, k_s, wt, sems, early_sems, near_sem = refs
    channels = wt.shape[1]
    edge, mid = outer_ref.shape[0] // 2, mid_ref.shape[0]
    coming = []
    for j, (off, start) in enumerate(pieces):
        to = pl.multiple_of((place_ref[ROW] ^ off) * triple_rows + place_ref[STARTS + start], 16)
        coming.append(pltpu.make_async_copy(sources[j], wt.at[pl.ds(to, sources[j].shape[0]), :], sems.at[j]))
        coming[-1].start()
    to = pl.multiple_of(place_ref[HALF] * near.shape[0], 16)
    near_copy = pltpu.make_async_copy(near, wt.at[pl.ds(to, near.shape[0]), :], near_sem)
    near_copy.start()

    def put(section, group, lane, width, lines, value):
        if section == 0:
            q_s[group, lines, :] = value
        else:
            k_s[group, lines, lane : lane + width] = value

    def take():
        for copy in coming:
            copy.wait()

    def run(half):
        moves = []
        for number, at, section, group, lane, width in numbered_chunks(channels, half):
            if section == 0:
                move = (whole_ref.at[number], q_s.at[group])
            elif section == 1 and width == GROUP:
                move = (whole_ref.at[number, 0:mid, :], k_s.at[group, edge : edge + mid, :])
            elif section == 1:
                move = (part_ref, k_s.at[group, edge : edge + mid, lane : lane + width])
            else:
                continue
            moves.append(pltpu.make_async_copy(*move, early_sems.at[len(moves)]))
            moves[-1].start()
        base = half * near.shape[0]
        project_rest(
            half, (0, 1), channels, lambda at, width: near[at - base : at - base + width, :], lambda at, width: wt[at : at + width, :],
            (xq_ref, mid_ref, outer_ref), take, put,
        )
        for move in moves:
            move.wait()

    for half in range(2):
        pl.when(place_ref[HALF] == half)(functools.partial(run, half))
    near_copy.wait()


def value_kernel(place_ref, wt, whole_ref, mid_ref, outer_ref, v_s, early_sems):
    channels = wt.shape[1]
    edge, mid = outer_ref.shape[0] // 2, mid_ref.shape[0]

    def put(section, group, lane, width, lines, value):
        v_s[group, lines, lane : lane + width] = value

    def run(half):
        moves = []
        for number, at, section, group, lane, width in numbered_chunks(channels, half):
            if section == 2:
                target = v_s.at[group, edge : edge + mid, :]
                moves.append(pltpu.make_async_copy(whole_ref.at[number, 0:mid, :], target, early_sems.at[len(moves)]))
                moves[-1].start()
        weights = lambda at, width: wt[at : at + width, :]
        project_rest(half, (2,), channels, weights, weights, (None, mid_ref, outer_ref), lambda: None, put)
        for move in moves:
            move.wait()

    for half in range(2):
        pl.when(place_ref[HALF] == half)(functools.partial(run, half))


def carrier_kernel(offsets, place_ref, wt, *refs):
    shards = len(offsets)
    finals, refs = refs[:shards], refs[shards:]
    summary_ref, wo, kce, vc_s, carriers_s, sems = refs
    per_row = summary_ref.shape[1]
    channels = wt.shape[1]
    groups = channels // GROUP
    heads = channels // HEAD_DIM
    factor = HEAD_DIM ** (-0.5)
    carriers_here = vc_s.shape[0]
    final_rows = wo.shape[0] // shards
    copies = []
    for j, off in enumerate(offsets):
        to = pl.multiple_of((place_ref[ROW] ^ off) * final_rows, 16)
        copy = pltpu.make_async_copy(finals[j].at[0:final_rows, :], wo.at[pl.ds(to, final_rows), :], sems.at[j])
        copy.start()
        copies.append(copy)
    coming = []
    sent = carriers_s.shape[0] // shards
    for j in range(shards):
        source = finals[j].at[final_rows : final_rows + sent, :]
        copy = pltpu.make_async_copy(source, carriers_s.at[j * sent : (j + 1) * sent, :], sems.at[shards + j])
        copy.start()
        coming.append(copy)
    for copy in coming:
        copy.wait()
    carriers = carriers_s[...].astype(jnp.float32)
    own = carriers[:carriers_here]
    carriers = layer_normalise(carriers).astype(jnp.bfloat16)
    own_norm = layer_normalise(own).astype(jnp.bfloat16)
    qc = (nt(own_norm, wt[:channels, :]) * factor).astype(jnp.bfloat16).astype(jnp.float32)
    kc = nt(carriers, wt[channels : 2 * channels, :]).astype(jnp.bfloat16)
    vc = nt(carriers, wt[2 * channels :, :]).astype(jnp.bfloat16)
    head_of = lax.broadcasted_iota(jnp.int32, (1, channels), 1) // HEAD_DIM
    stacked = jnp.concatenate([jnp.where(head_of == h, qc, 0.0) for h in range(heads)], axis=0)
    e = jnp.exp(nt(stacked.astype(jnp.bfloat16), kc))
    weights = (e / jnp.sum(e, axis=-1, keepdims=True)).astype(jnp.bfloat16)
    o = nn(weights, vc)
    mix = jnp.zeros((carriers_here, channels), jnp.float32)
    for h in range(heads):
        mix = jnp.where(head_of == h, o[h * carriers_here : (h + 1) * carriers_here, :], mix)
    for copy in copies:
        copy.wait()
    renewed = own + nt(mix.astype(jnp.bfloat16), wo[...])
    for i in range(summary_ref.shape[0]):
        summary_ref[i] = renewed[i * per_row : (i + 1) * per_row, :].astype(jnp.bfloat16)
    fresh = nt(layer_normalise(renewed).astype(jnp.bfloat16), wt[channels:, :]).astype(jnp.bfloat16).astype(jnp.float32)
    vc_s[...] = fresh[:, channels:]
    same = (
        lax.broadcasted_iota(jnp.int32, (GROUP, GROUP), 0) // HEAD_DIM
        == lax.broadcasted_iota(jnp.int32, (GROUP, GROUP), 1) // HEAD_DIM
    )
    windows = kce.shape[0] // groups
    for w in range(windows):
        for g in range(groups):
            kce[w * groups + g] = jnp.where(same, fresh[w : w + 1, g * GROUP : (g + 1) * GROUP], 0.0).astype(jnp.bfloat16)


def attend_kernel(tall, broad, q_s, k_s, v_s, hide_ref, kce, vc_s, mix_s, pc_s, even_s, odd_s):
    groups, tiles = q_s.shape[0], hide_ref.shape[0]
    heads_in = GROUP // HEAD_DIM
    queries, span = TILE * TILE, 2 * TILE * TILE
    side = PATCH_SIDE // TILE
    wide = (tall + 1) * queries
    qi = lax.broadcasted_iota(jnp.int32, (queries, 2 * span), 0)
    ki = lax.broadcasted_iota(jnp.int32, (queries, 2 * span), 1)
    row_step = (ki % span) // TILE - qi // TILE
    col_step = (ki // span) * TILE + ki % TILE - qi % TILE
    seen = (row_step >= 0) & (row_step <= 2 * RADIUS) & (col_step >= 0) & (col_step <= 2 * RADIUS)
    band = jnp.where(seen, 0.0, HIDDEN)
    group_head = lax.broadcasted_iota(jnp.int32, (1, GROUP), 1) // HEAD_DIM
    only = [jnp.where(group_head == h, 1.0, 0.0).astype(jnp.bfloat16) for h in range(heads_in)]
    in_pair = LANES // HEAD_DIM
    pair_head = lax.broadcasted_iota(jnp.int32, (1, LANES), 1) // HEAD_DIM

    for c in range(broad):
        for w in range(tall // side):
            at = slice((c * tall + w * side) * queries, (c * tall + (w + 1) * side) * queries)
            window = w * (broad // side) + c // side
            for g in range(groups):
                pc_s[at, g * GROUP : (g + 1) * GROUP] = jnp.exp2(nt(q_s[g, at, :], kce[window * groups + g]))

    def keys_at(t):
        k0 = pl.multiple_of(t // tall * wide + t % tall * queries, queries)
        return k0, pl.multiple_of(k0 + wide, queries)

    def scores(t, ref):
        q_at = pl.multiple_of(t * queries, queries)
        k0, k1 = keys_at(t)
        for g in range(groups):
            q = q_s[g, pl.ds(q_at, queries), :]
            qq = jnp.concatenate([q * mask for mask in only], axis=0)
            k = jnp.concatenate([k_s[g, pl.ds(k0, span), :], k_s[g, pl.ds(k1, span), :]], axis=0)
            ref[g] = nt(qq, k)

    def finish(t, ref):
        q_at = pl.multiple_of(t * queries, queries)
        k0, k1 = keys_at(t)
        window = t % tall // side * (broad // side) + t // tall // side
        bias = band + hide_ref[t][0:1, :]
        for g in range(groups):
            p = jnp.exp2(ref[g].reshape(heads_in, queries, 2 * span) + bias[None])
            total = jnp.sum(p, axis=-1, keepdims=True)
            v = jnp.concatenate([v_s[g, pl.ds(k0, span), :], v_s[g, pl.ds(k1, span), :]], axis=0)
            o = nn(p.reshape(heads_in * queries, 2 * span).astype(jnp.bfloat16), v).reshape(heads_in, queries, GROUP)
            v_new = vc_s[pl.ds(window, 1), g * GROUP : (g + 1) * GROUP]
            for j in range(GROUP // LANES):
                lanes = slice(j * LANES, (j + 1) * LANES)
                at = slice(g * GROUP + j * LANES, g * GROUP + (j + 1) * LANES)
                kept, kept_total = o[j * in_pair, :, lanes], total[j * in_pair]
                for h in range(1, in_pair):
                    kept = jnp.where(pair_head == h, o[j * in_pair + h, :, lanes], kept)
                    kept_total = jnp.where(pair_head == h, total[j * in_pair + h], kept_total)
                new = pc_s[pl.ds(q_at, queries), at]
                mixed = (kept + new * v_new[:, lanes]) / (kept_total + new)
                mix_s[pl.ds(q_at, queries), at] = mixed.astype(jnp.bfloat16)

    scores(0, even_s)

    def two(i, _):
        t = 2 * i
        scores(t + 1, odd_s)
        finish(t, even_s)
        scores(jnp.minimum(t + 2, tiles - 1), even_s)
        finish(t + 1, odd_s)
        return 0

    lax.fori_loop(0, tiles // 2, two, 0)


def out_kernel(x_ref, mix_s, wo, out_hbm, out_ref, out_sems):
    rows, cols, channels = x_ref.shape
    going = []
    for pair in range(cols // (2 * TILE)):
        both = slice(2 * pair * TILE, 2 * (pair + 1) * TILE)
        for g in range(channels // GROUP):
            at = slice(g * GROUP, (g + 1) * GROUP)
            w = wo[at, :]
            y = nt(mix_s[2 * pair * rows * TILE : 2 * (pair + 1) * rows * TILE, :], w).reshape(2, rows, TILE, GROUP)
            y = jnp.concatenate([y[0], y[1]], axis=1) + x_ref[:, both, at].astype(jnp.float32)
            out_ref[pair, :, :, at] = y.astype(jnp.bfloat16)
        copy = pltpu.make_async_copy(out_ref.at[pair], out_hbm.at[:, both, :], out_sems.at[pair])
        copy.start()
        going.append(copy)
    for copy in going:
        copy.wait()


def local(grid_elements, summary_vectors, triple_projection, final_projection, genuine_flags):
    rows, cols, channels = grid_elements.shape
    wide_rows, wide_cols = rows + 2 * RADIUS, cols + 2 * RADIUS

    triple_t, final_t = triple_projection.T, final_projection.T
    vmem = pl.BlockSpec(memory_space=pltpu.VMEM)
    anywhere = pl.BlockSpec(memory_space=pl.ANY)
    scalars = pl.BlockSpec(memory_space=pltpu.SMEM)
    hbm = pl.BlockSpec(memory_space=pltpu.HBM)
    small = pltpu.CompilerParams(vmem_limit_bytes=8 * 1024 * 1024)
    row_strip = jax.ShapeDtypeStruct((RADIUS, cols, channels), jnp.bfloat16)
    col_strip = jax.ShapeDtypeStruct((wide_rows // 2, 2 * RADIUS, channels), jnp.bfloat16)

    row, col, img = lax.axis_size("row"), lax.axis_size("col"), lax.axis_size("img")
    row_at, col_at, img_at = lax.axis_index("row"), lax.axis_index("col"), lax.axis_index("img")
    row_bits = bits_of(row)
    far, rest = row_bits[0], row_bits[1:]
    piece_rows = triple_t.shape[0] // (1 + img) // 16 * 16
    relays = img if piece_rows else 0
    starts = [(img_at - k) % img for k in range(relays)] + [jnp.int32(relays)]
    place = [row_at == 0, row_at == row - 1, col_at == 0, col_at == col - 1, row_at % 2 == 0, col_at % 2 == 0, row_at, row_at // far]
    place = jnp.stack([jnp.asarray(p).astype(jnp.int32) for p in place + [start * piece_rows for start in starts]])

    mark, even_rows, odd_rows, x = pl.pallas_call(
        edge_kernel,
        out_shape=(
            pltpu.VMEM((rows, cols, LANES), jnp.bfloat16),
            pltpu.VMEM(row_strip.shape, jnp.bfloat16),
            pltpu.VMEM(row_strip.shape, jnp.bfloat16),
            pltpu.VMEM(grid_elements.shape, jnp.bfloat16),
        ),
        in_specs=[scalars, hbm, hbm],
        out_specs=(vmem,) * 4,
        scratch_shapes=[
            pltpu.VMEM((rows, cols), jnp.int32),
            pltpu.VMEM((rows * cols, cols), jnp.bfloat16),
            pltpu.SemaphoreType.DMA((2,)),
        ],
        compiler_params=small,
        cost_estimate=pl.CostEstimate(flops=1_000_000, bytes_accessed=1_000_000, transcendentals=0),
        name="edge_rows",
    )(place, *(pltpu.with_memory_space_constraint(a, pltpu.HBM) for a in (genuine_flags, grid_elements)))
    mine, last = pl.pallas_call(
        piece_kernel,
        out_shape=(
            pltpu.VMEM((max(piece_rows, 16), channels), jnp.bfloat16),
            pltpu.VMEM((triple_t.shape[0] - relays * piece_rows, channels), jnp.bfloat16),
        ),
        in_specs=[scalars, hbm],
        out_specs=(vmem, vmem),
        scratch_shapes=[pltpu.SemaphoreType.DMA((2,))],
        compiler_params=small,
        cost_estimate=pl.CostEstimate(flops=1_000_000, bytes_accessed=1_000_000, transcendentals=0),
        name="pieces",
    )(place, pltpu.with_memory_space_constraint(after(triple_t, even_rows), pltpu.HBM))
    xq = pl.pallas_call(
        own_kernel,
        out_shape=pltpu.VMEM((rows * cols, channels), jnp.bfloat16),
        in_specs=[vmem],
        out_specs=vmem,
        compiler_params=small,
        cost_estimate=pl.CostEstimate(flops=1_000_000, bytes_accessed=1_000_000, transcendentals=0),
        name="own_norm",
    )(x)
    even_rows, odd_rows = pair_swapped(even_rows, odd_rows, "row")

    far_pieces = []
    if relays:
        first = swapped(mine, "row", far)
    far_last = swapped(after(last, even_rows, odd_rows), "row", far)

    own_rows = summary_vectors.shape[0] * summary_vectors.shape[1]
    carrier_tiles = -(-own_rows // TILE)
    even_cols, odd_cols = pl.pallas_call(
        strip_kernel,
        out_shape=(
            pltpu.VMEM((col_strip.shape[0] + carrier_tiles, *col_strip.shape[1:]), jnp.bfloat16),
            pltpu.VMEM(col_strip.shape, jnp.bfloat16),
        ),
        in_specs=[scalars] + [vmem] * 5,
        out_specs=(vmem,) * 2,
        scratch_shapes=[pltpu.VMEM((carrier_tiles * TILE, channels), jnp.float32)],
        compiler_params=small,
        cost_estimate=pl.CostEstimate(flops=1_000_000, bytes_accessed=2_000_000, transcendentals=0),
        name="edge_columns",
    )(place, x, after(mark, xq), even_rows, odd_rows, summary_vectors)
    even_cols, odd_cols = pair_swapped(even_cols, odd_cols, "col")
    groups = channels // GROUP
    triples, offsets = [triple_t], [0]
    for bit in rest:
        triples = triples + [swapped(p, "row", bit) for p in triples]
        offsets = offsets + [o ^ bit for o in offsets]
    mid = pl.pallas_call(
        middle_kernel,
        out_shape=pltpu.VMEM(((wide_cols // TILE - 2) * wide_rows * TILE, channels), jnp.bfloat16),
        in_specs=[scalars] + [vmem] * 3,
        out_specs=vmem,
        scratch_shapes=[pltpu.VMEM(row_strip.shape, jnp.float32)] * 2,
        compiler_params=small,
        cost_estimate=pl.CostEstimate(flops=1_000_000, bytes_accessed=1_000_000, transcendentals=0),
        name="middle_blocks",
    )(place, xq, even_rows, odd_rows)
    whole, part, near = pl.pallas_call(
        functools.partial(early_kernel, offsets),
        out_shape=(
            pltpu.VMEM((3 * groups // 2, rows * cols, GROUP), jnp.bfloat16),
            pltpu.VMEM((mid.shape[0], GROUP // 2), jnp.bfloat16),
            pltpu.VMEM((3 * channels // 2, channels), jnp.bfloat16),
        ),
        in_specs=[scalars] + [anywhere] * len(triples) + [vmem] * 2,
        out_specs=(vmem,) * 3,
        scratch_shapes=[pltpu.SemaphoreType.DMA((len(triples),))],
        compiler_params=pltpu.CompilerParams(vmem_limit_bytes=16 * 1024 * 1024),
        cost_estimate=pl.CostEstimate(flops=1_000_000, bytes_accessed=1_000_000, transcendentals=0),
        name="project_early",
    )(place, *triples, xq, mid)

    carriers = pl.pallas_call(
        carrier_pair_kernel,
        out_shape=pltpu.VMEM((2 * own_rows, channels), jnp.bfloat16),
        in_specs=[vmem, anywhere],
        out_specs=vmem,
        scratch_shapes=[
            pltpu.VMEM((carrier_tiles, TILE, channels), jnp.bfloat16),
            pltpu.VMEM((2 * own_rows, channels), jnp.float32),
            pltpu.SemaphoreType.DMA,
        ],
        compiler_params=small,
        cost_estimate=pl.CostEstimate(flops=1_000, bytes_accessed=1_000, transcendentals=0),
        name="carrier_pair",
    )(summary_vectors, after(even_cols, near))
    parts = [carriers]
    for bit in bits_of(col)[:-1]:
        carriers = carriers if len(parts) == 1 else jnp.concatenate(parts, axis=0)
        got = swapped(carriers, "col", 2 * bit - 1)
        parts.append(got)
    if relays:
        first = after(first, even_cols, odd_cols, parts[0])
        others = [lax.ppermute(first, "img", [(i, (i + k) % img) for i in range(img)]) for k in range(1, relays)]
        far_pieces = [first] + others
    far_pieces.append(far_last)

    final_pack = pl.pallas_call(
        pack_kernel,
        out_shape=pltpu.VMEM((final_t.shape[0] + col * own_rows, channels), jnp.bfloat16),
        in_specs=[vmem] * (1 + len(parts)),
        out_specs=vmem,
        compiler_params=small,
        cost_estimate=pl.CostEstimate(flops=1_000, bytes_accessed=1_000, transcendentals=0),
        name="final_pack",
    )(final_t, *parts)
    finals = [final_pack]
    for bit in rest:
        finals = finals + [swapped(p, "row", bit) for p in finals]
    tiles = (rows // TILE) * (cols // TILE)
    keys = 4 * TILE * TILE
    outer, hide = pl.pallas_call(
        outer_kernel,
        out_shape=(
            pltpu.VMEM((2 * wide_rows * TILE, channels), jnp.bfloat16),
            pltpu.VMEM((tiles, 8, keys), jnp.float32),
        ),
        in_specs=[scalars] + [vmem] * 6,
        out_specs=(vmem,) * 2,
        scratch_shapes=[
            *[pltpu.VMEM((RADIUS, 2 * TILE, channels), jnp.float32)] * 2,
            *[pltpu.VMEM(col_strip.shape, jnp.float32)] * 2,
            *[pltpu.VMEM((*shape.shape[:2], LANES), jnp.float32) for shape in (row_strip, row_strip, col_strip, col_strip)],
            pltpu.VMEM((wide_rows * wide_cols, LANES), jnp.bfloat16),
        ],
        compiler_params=pltpu.CompilerParams(vmem_limit_bytes=12 * 1024 * 1024),
        cost_estimate=pl.CostEstimate(flops=10_000_000, bytes_accessed=6_000_000, transcendentals=1000),
        name="outer_blocks",
    )(place, after(xq, got), mark, even_rows, odd_rows, even_cols, odd_cols)

    far_final = swapped(final_pack, "row", far)

    far_offsets = [far]
    far_pieces = [[after(piece, outer)] for piece in far_pieces]
    for bit in rest:
        far_pieces = [same + [swapped(p, "row", bit) for p in same] for same in far_pieces]
        far_offsets = far_offsets + [o ^ bit for o in far_offsets]

    numbered = [(off, number) for number in range(len(far_pieces)) for off in far_offsets]
    sources = [piece for same in far_pieces for piece in same]
    q, k, wt = pl.pallas_call(
        functools.partial(late_kernel, numbered, triple_t.shape[0]),
        out_shape=(
            jax.ShapeDtypeStruct((groups, rows * cols, GROUP), jnp.bfloat16),
            jax.ShapeDtypeStruct((groups, wide_rows * wide_cols, GROUP), jnp.bfloat16),
            jax.ShapeDtypeStruct((3 * channels, channels), jnp.bfloat16),
        ),
        in_specs=[scalars] + [anywhere] * len(sources) + [vmem] * 6,
        out_specs=(vmem,) * 3,
        scratch_shapes=[
            pltpu.SemaphoreType.DMA((len(sources),)),
            pltpu.SemaphoreType.DMA((3 * groups,)),
            pltpu.SemaphoreType.DMA,
        ],
        compiler_params=pltpu.CompilerParams(vmem_limit_bytes=VMEM_BYTES),
        cost_estimate=pl.CostEstimate(flops=1_000_000, bytes_accessed=1_000_000, transcendentals=0),
        name="project_late",
    )(place, *sources, near, whole, part, xq, mid, outer)

    v = pl.pallas_call(
        value_kernel,
        out_shape=jax.ShapeDtypeStruct((groups, wide_rows * wide_cols, GROUP), jnp.bfloat16),
        in_specs=[scalars] + [vmem] * 4,
        out_specs=vmem,
        scratch_shapes=[pltpu.SemaphoreType.DMA((groups,))],
        compiler_params=pltpu.CompilerParams(vmem_limit_bytes=VMEM_BYTES),
        cost_estimate=pl.CostEstimate(flops=3_000_000_000, bytes_accessed=7_000_000, transcendentals=0),
        name="values",
    )(place, wt, whole, mid, outer)

    far_finals = [after(far_final, q)]
    for bit in rest:
        far_finals = far_finals + [swapped(p, "row", bit) for p in far_finals]
    finals, offsets = finals + far_finals, offsets + far_offsets
    carriers_here = carrier_tiles * TILE
    summary_result, wo, kce, vc = pl.pallas_call(
        functools.partial(carrier_kernel, offsets),
        out_shape=(
            jax.ShapeDtypeStruct(summary_vectors.shape, jnp.bfloat16),
            jax.ShapeDtypeStruct((channels, channels), jnp.bfloat16),
            jax.ShapeDtypeStruct((own_rows * groups, GROUP, GROUP), jnp.bfloat16),
            jax.ShapeDtypeStruct((carriers_here, channels), jnp.float32),
        ),
        in_specs=[scalars, vmem] + [anywhere] * len(finals),
        out_specs=(vmem,) * 4,
        scratch_shapes=[
            pltpu.VMEM((row * col * own_rows, channels), jnp.bfloat16),
            pltpu.SemaphoreType.DMA((2 * len(finals),)),
        ],
        compiler_params=pltpu.CompilerParams(vmem_limit_bytes=VMEM_BYTES),
        cost_estimate=pl.CostEstimate(flops=500_000_000, bytes_accessed=5_000_000, transcendentals=10_000),
        name="carriers",
    )(place, wt, *finals)

    scores = (groups, GROUP // HEAD_DIM * TILE * TILE, keys)
    mix = pl.pallas_call(
        functools.partial(attend_kernel, rows // TILE, cols // TILE),
        out_shape=jax.ShapeDtypeStruct((rows * cols, channels), jnp.bfloat16),
        in_specs=[vmem] * 6,
        out_specs=vmem,
        scratch_shapes=[
            pltpu.VMEM((rows * cols, channels), jnp.float32),
            pltpu.VMEM(scores, jnp.float32),
            pltpu.VMEM(scores, jnp.float32),
        ],
        compiler_params=pltpu.CompilerParams(vmem_limit_bytes=VMEM_BYTES),
        cost_estimate=pl.CostEstimate(flops=4_000_000_000, bytes_accessed=12_000_000, transcendentals=4_000_000),
        name="attend",
    )(q, k, v, hide, kce, vc)

    out = pl.pallas_call(
        out_kernel,
        out_shape=jax.ShapeDtypeStruct(grid_elements.shape, jnp.bfloat16),
        in_specs=[vmem] * 3,
        out_specs=anywhere,
        scratch_shapes=[
            pltpu.VMEM((cols // (2 * TILE), rows, 2 * TILE, channels), jnp.bfloat16),
            pltpu.SemaphoreType.DMA((cols // (2 * TILE),)),
        ],
        compiler_params=pltpu.CompilerParams(vmem_limit_bytes=VMEM_BYTES),
        cost_estimate=pl.CostEstimate(flops=1_200_000_000, bytes_accessed=6_000_000, transcendentals=0),
        name="out",
    )(x, mix, wo)
    return (out, summary_result)


def solution(mesh):
    placed = (
        P(("img", "row"), "col", None),
        P(("img", "row"), "col", None),
        P(None, "row"),
        P(None, "row"),
        P(("img", "row"), "col"),
    )
    return jax.shard_map(
        local,
        mesh=mesh,
        in_specs=placed,
        out_specs=(P(("img", "row"), "col", None), P(("img", "row"), "col", None)),
        check_vma=False,
    )
```

```python
import functools

import jax
import jax.numpy as jnp
from jax import lax
from jax.experimental import pallas as pl
from jax.experimental.pallas import tpu as pltpu
from jax.sharding import PartitionSpec as P

HEAD_DIM = 64
PATCH_SIDE = 16
RADIUS = 4
TILE = 2 * RADIUS
LANES = 128
GROUP = 256
INVALID = 100.0
HIDDEN = -1e30
LOG2_E = 1.4426950408889634
EVEN_ROW, EVEN_COL, ROW, HALF, STARTS = 4, 5, 6, 7, 8
VMEM_BYTES = 26 * 1024 * 1024


def nt(a, b):
    return lax.dot_general(a, b, (((1,), (1,)), ((), ())), preferred_element_type=jnp.float32)


def nn(a, b):
    return lax.dot_general(a, b, (((1,), (0,)), ((), ())), preferred_element_type=jnp.float32)


def layer_normalise(lines):
    center = lines - jnp.mean(lines, axis=-1, keepdims=True)
    spread = jnp.mean(center * center, axis=-1, keepdims=True)
    return center * lax.rsqrt(spread + 1e-05)


def pair_swapped(even_block, odd_block, axis):
    count = lax.axis_size(axis)
    got = []
    for first, block in ((0, even_block), (1, odd_block)):
        pairs = [(i, i + 1) for i in range(first, count - 1, 2)]
        got.append(lax.ppermute(block, axis, pairs + [(b, a) for a, b in pairs]))
    return got


def swapped(block, axis, bit):
    count = lax.axis_size(axis)
    return lax.ppermute(block, axis, [(i, i ^ bit) for i in range(count)])


def after(block, *others):
    return lax.optimization_barrier((block, *others))[0]


def bits_of(count):
    bits, bit = [], count // 2
    while bit:
        bits.append(bit)
        bit //= 2
    return bits


def marked_lanes(lines, hidden):
    first = jnp.where(hidden, INVALID, lines[:, :, :LANES])
    return jnp.concatenate([first, lines[:, :, LANES:]], axis=2)


def edge_kernel(place_ref, flags_hbm, x_hbm, mark_ref, even_ref, odd_ref, x_ref, *scratch):
    flags_ref, spread, sems = scratch
    rows, cols = flags_ref.shape
    flags_copy = pltpu.make_async_copy(flags_hbm, flags_ref, sems.at[0])
    x_copy = pltpu.make_async_copy(x_hbm, x_ref, sems.at[1])
    flags_copy.start()
    x_copy.start()
    flags_copy.wait()
    row_at = lax.broadcasted_iota(jnp.int32, (cols, cols), 0)
    diagonal = row_at == lax.broadcasted_iota(jnp.int32, (cols, cols), 1)
    for r in range(rows):
        hidden = jnp.where(flags_ref[r : r + 1, :] > 0, 0.0, INVALID)
        spread[r * cols : (r + 1) * cols, :] = jnp.where(diagonal, hidden, 0.0).astype(jnp.bfloat16)
    marks = nn(spread[...], jnp.ones((cols, LANES), jnp.bfloat16)).reshape(rows, cols, LANES)
    mark_ref[...] = marks.astype(jnp.bfloat16)
    x_copy.wait()
    first, last = [
        marked_lanes(x_ref[at].astype(jnp.float32), marks[at] > INVALID / 2)
        for at in (slice(0, RADIUS), slice(rows - RADIUS, rows))
    ]
    even = place_ref[EVEN_ROW] > 0
    even_ref[...] = jnp.where(even, last, first).astype(jnp.bfloat16)
    odd_ref[...] = jnp.where(even, first, last).astype(jnp.bfloat16)


def piece_kernel(place_ref, triple_hbm, mine_ref, last_ref, sems):
    start = pl.multiple_of(place_ref[STARTS], 16)
    last = triple_hbm.shape[0] - last_ref.shape[0]
    copies = [
        pltpu.make_async_copy(triple_hbm.at[pl.ds(start, mine_ref.shape[0]), :], mine_ref, sems.at[0]),
        pltpu.make_async_copy(triple_hbm.at[last:, :], last_ref, sems.at[1]),
    ]
    for copy in copies:
        copy.start()
    for copy in copies:
        copy.wait()


def strip_kernel(place_ref, x_ref, mark_ref, even_rows_ref, odd_rows_ref, carriers_ref, even_ref, odd_ref, carriers_s):
    per_row = carriers_ref.shape[1]
    carriers_s[...] = jnp.zeros_like(carriers_s)
    for i in range(carriers_ref.shape[0]):
        carriers_s[i * per_row : (i + 1) * per_row, :] = carriers_ref[i].astype(jnp.float32)
    for i in range(carriers_s.shape[0] // TILE):
        even_ref[odd_ref.shape[0] + i] = carriers_s[i * TILE : (i + 1) * TILE, :].astype(jnp.bfloat16)
    rows, cols, channels = x_ref.shape
    middle = rows // 2
    low = lax.broadcasted_iota(jnp.int32, (1, TILE, 1), 1) < RADIUS
    even_row, even_col = place_ref[EVEN_ROW] > 0, place_ref[EVEN_COL] > 0
    for lane in range(0, channels, LANES):
        lanes = slice(lane, lane + LANES)
        strips = []
        for columns, last in ((slice(0, TILE), False), (slice(cols - TILE, cols), True)):

            def own(part):
                lines = x_ref[part, columns, lanes].astype(jnp.float32)
                if lane == 0:
                    lines = jnp.where(mark_ref[part, columns, :].astype(jnp.float32) > INVALID / 2, INVALID, lines)
                return lines

            even_rows = even_rows_ref[:, columns, lanes].astype(jnp.float32)
            odd_rows = odd_rows_ref[:, columns, lanes].astype(jnp.float32)
            top, bottom = jnp.where(even_row, odd_rows, even_rows), jnp.where(even_row, even_rows, odd_rows)
            upper = jnp.concatenate([top, own(slice(0, middle))], axis=0)
            lower = jnp.concatenate([own(slice(middle, rows)), bottom], axis=0)
            if last:
                upper = jnp.roll(upper, RADIUS, axis=1)
            else:
                lower = jnp.roll(lower, RADIUS, axis=1)
            strips.append(jnp.where(low, upper, lower))
        first, last = strips
        even_ref[: odd_ref.shape[0], :, lanes] = jnp.where(even_col, last, first).astype(jnp.bfloat16)
        odd_ref[:, :, lanes] = jnp.where(even_col, first, last).astype(jnp.bfloat16)


def carrier_pair_kernel(own_ref, got_hbm, out_ref, got_s, pair_s, sem):
    per_row, here = own_ref.shape[1], own_ref.shape[0] * own_ref.shape[1]
    tiles = got_s.shape[0]
    copy = pltpu.make_async_copy(got_hbm.at[got_hbm.shape[0] - tiles :], got_s, sem)
    copy.start()
    for i in range(own_ref.shape[0]):
        pair_s[i * per_row : (i + 1) * per_row, :] = own_ref[i].astype(jnp.float32)
    copy.wait()
    pair_s[here:, :] = got_s[...].astype(jnp.float32).reshape(tiles * TILE, -1)[:here]
    out_ref[...] = pair_s[...].astype(jnp.bfloat16)


def pack_kernel(final_ref, *refs):
    parts, out_ref = refs[:-1], refs[-1]
    rows = final_ref.shape[0]
    out_ref[:rows, :] = final_ref[...]
    carriers = jnp.concatenate([part[...].astype(jnp.float32) for part in parts], axis=0)
    out_ref[rows:, :] = carriers.astype(jnp.bfloat16)


def own_kernel(x_ref, xq_ref):
    rows, cols, _ = x_ref.shape
    step = 4

    def own(i, _):
        at = pl.multiple_of(i * step, step)
        y = layer_normalise(x_ref[pl.ds(at, step)].astype(jnp.float32))
        for c in range(cols // TILE):
            piece = y[:, c * TILE : (c + 1) * TILE, :].reshape(step * TILE, -1)
            to = pl.multiple_of(c * rows * TILE + at * TILE, step * TILE)
            xq_ref[pl.ds(to, step * TILE), :] = piece.astype(jnp.bfloat16)
        return 0

    lax.fori_loop(0, rows // step, own, 0)


def columns_of(lines):
    return [lines[:, c : c + TILE, :] for c in range(0, lines.shape[1], TILE)]


def tile_of(xq_ref, column, rows, at, step):
    first = pl.multiple_of(column * rows * TILE + at * TILE, step * TILE)
    return xq_ref[pl.ds(first, step * TILE), :].astype(jnp.float32).reshape(step, TILE, -1)


def store_lines(ref, block, wide_rows, at, lines):
    size = lines.shape[0] * TILE
    to = block * wide_rows * TILE + at * TILE
    to = to if isinstance(to, int) else pl.multiple_of(to, size)
    ref[pl.ds(to, size), :] = lines.reshape(size, -1).astype(jnp.bfloat16)


def middle_kernel(place_ref, xq_ref, even_rows_ref, odd_rows_ref, mid_ref, top_s, bottom_s):
    cols = even_rows_ref.shape[1]
    rows, step = xq_ref.shape[0] // cols, 2
    wide_rows = rows + 2 * RADIUS
    flip = place_ref[EVEN_ROW] > 0
    for i in range(0, RADIUS, step):
        a, b = even_rows_ref[i : i + step].astype(jnp.float32), odd_rows_ref[i : i + step].astype(jnp.float32)
        top_s[i : i + step] = layer_normalise(jnp.where(flip, b, a))
        bottom_s[i : i + step] = layer_normalise(jnp.where(flip, a, b))
    low = lax.broadcasted_iota(jnp.int32, (1, TILE, 1), 1) < RADIUS

    def merge(at, blocks):
        moved = [jnp.roll(block, RADIUS, axis=1) for block in blocks]
        for c in range(1, len(blocks)):
            store_lines(mid_ref, c - 1, wide_rows, at, jnp.where(low, moved[c - 1], moved[c]))

    for i in range(0, RADIUS, step):
        merge(i, columns_of(top_s[i : i + step]))
        merge(RADIUS + rows + i, columns_of(bottom_s[i : i + step]))

    def middle(i, _):
        at = pl.multiple_of(i * step, step)
        merge(RADIUS + at, [tile_of(xq_ref, c, rows, at, step) for c in range(cols // TILE)])
        return 0

    lax.fori_loop(0, rows // step, middle, 0)


def outer_kernel(place_ref, xq_ref, mark_ref, even_rows_ref, odd_rows_ref, even_cols_ref, odd_cols_ref, outer_ref, hide_ref, *scratch):
    rows, cols, _ = mark_ref.shape
    wide_rows, wide_cols = rows + 2 * RADIUS, cols + 2 * RADIUS
    half = wide_rows // 2
    step = 2
    top_s, bottom_s, left_s, right_s, top_ref, bottom_ref, left_ref, right_ref, flag_s = scratch
    flip = place_ref[EVEN_ROW] > 0
    a, b = even_rows_ref[...].astype(jnp.float32), odd_rows_ref[...].astype(jnp.float32)
    for lines, out, flags in ((jnp.where(flip, b, a), top_s, top_ref), (jnp.where(flip, a, b), bottom_s, bottom_ref)):
        ends = jnp.concatenate([lines[:, :TILE, :], lines[:, cols - TILE :, :]], axis=1)
        out[...] = layer_normalise(ends)
        flags[...] = lines[:, :, :LANES]
    flip = place_ref[EVEN_COL] > 0
    size = 5
    for i in range(0, odd_cols_ref.shape[0], size):
        a, b = even_cols_ref[i : i + size].astype(jnp.float32), odd_cols_ref[i : i + size].astype(jnp.float32)
        for lines, out, flags in ((jnp.where(flip, b, a), left_s, left_ref), (jnp.where(flip, a, b), right_s, right_ref)):
            out[i : i + size] = layer_normalise(lines)
            flags[i : i + size] = lines[:, :, :LANES]
    low = lax.broadcasted_iota(jnp.int32, (1, TILE, 1), 1) < RADIUS

    def lines_of(ref):
        return ref.astype(jnp.float32)

    def merge(at, blocks, left, right, to_ref):
        moved = [left] + [jnp.roll(block, RADIUS, axis=1) for block in blocks] + [right]
        for c in range(len(blocks) + 1):
            store_lines(to_ref, c, wide_rows, at, jnp.where(low, moved[c], moved[c + 1]))

    def merge_ends(at, first, last, left, right):
        store_lines(outer_ref, 0, wide_rows, at, jnp.where(low, left, jnp.roll(first, RADIUS, axis=1)))
        store_lines(outer_ref, 1, wide_rows, at, jnp.where(low, jnp.roll(last, RADIUS, axis=1), right))

    def sides(at, upper, left_ref, right_ref, lanes):
        if upper:
            at = at - half
            left, right = jnp.roll(lines_of(left_ref[pl.ds(at, step), :, lanes]), RADIUS, axis=1), lines_of(
                right_ref[pl.ds(at, step), :, lanes]
            )
        else:
            left, right = lines_of(left_ref[pl.ds(at, step), :, lanes]), jnp.roll(
                lines_of(right_ref[pl.ds(at, step), :, lanes]), RADIUS, axis=1
            )
        return left, right

    every, few = slice(None), slice(0, LANES)

    def hide_if(border, lines):
        return jnp.where(place_ref[border] > 0, INVALID, lines)

    def mark_sides(at, upper):
        left, right = sides(at, upper, left_ref, right_ref, few)
        return hide_if(2, left), hide_if(3, right)

    def band(at, ref, ref_s, first, upper):
        merge_ends(at, *columns_of(ref_s[first : first + step]), *sides(at, upper, left_s, right_s, every))
        marks = hide_if(int(upper), ref[first : first + step])
        beside = [hide_if(int(upper), side) for side in mark_sides(at, upper)]
        merge(at, columns_of(marks), *beside, flag_s)

    for i in range(0, RADIUS, step):
        band(i, top_ref, top_s, i, False)
        band(RADIUS + rows + i, bottom_ref, bottom_s, i, True)

    def middle(i, upper):
        at = pl.multiple_of(i * step, step)
        own = at - RADIUS
        ends = [tile_of(xq_ref, c, rows, own, step) for c in (0, cols // TILE - 1)]
        merge_ends(at, *ends, *sides(at, upper, left_s, right_s, every))
        merge(at, columns_of(mark_ref[pl.ds(own, step)].astype(jnp.float32)), *mark_sides(at, upper), flag_s)
        return 0

    lax.fori_loop(RADIUS // step, half // step, lambda i, _: middle(i, False), 0)
    lax.fori_loop(half // step, (RADIUS + rows) // step, lambda i, _: middle(i, True), 0)

    first_lane = (lax.broadcasted_iota(jnp.int32, (8, LANES), 1) == 0).astype(jnp.bfloat16)
    spans = []
    for c in range(wide_cols // TILE):
        lines = flag_s[c * wide_rows * TILE : (c + 1) * wide_rows * TILE, :]
        spans.append(jnp.where(nt(first_lane, lines) > INVALID / 2, HIDDEN, 0.0))
    tall = rows // TILE
    for c in range(cols // TILE):
        for r in range(tall):
            at = slice(r * TILE * TILE, r * TILE * TILE + 2 * TILE * TILE)
            hide_ref[c * tall + r] = jnp.concatenate([spans[c][:, at], spans[c + 1][:, at]], axis=1)


def column_chunks(channels, half):
    at, end = half * 3 * channels // 2, (half + 1) * 3 * channels // 2
    chunks = []
    while at < end:
        width = min(GROUP - at % GROUP, end - at)
        chunks.append((at, at // channels, at % channels // GROUP, at % GROUP, width))
        at += width
    return chunks


def numbered_chunks(channels, half):
    number, chunks = 0, []
    for chunk in column_chunks(channels, half):
        chunks.append((number, *chunk))
        number += chunk[-1] == GROUP
    return chunks


def project_lines(source, w, parts, factor, put):
    size = source.shape[0] // parts
    for m in range(0, source.shape[0], size):
        y = nt(source[m : m + size, :], w)
        put(slice(m, m + size), (y if factor == 1 else y * factor).astype(jnp.bfloat16))


QUERY_FACTOR = HEAD_DIM ** (-0.5) * LOG2_E


def early_kernel(offsets, place_ref, *refs):
    triples, refs = refs[: len(offsets)], refs[len(offsets) :]
    xq_ref, mid_ref, whole_ref, part_ref, near = refs
    channels = near.shape[1]
    triple_rows = near.shape[0] // len(offsets)
    for j, off in enumerate(offsets):
        to = pl.multiple_of(((place_ref[ROW] ^ off) % len(offsets)) * triple_rows, 16)
        near[pl.ds(to, triple_rows), :] = triples[j][...]

    def run(half):
        for number, at, section, _, _, width in numbered_chunks(channels, half):
            w = near[at - half * near.shape[0] : at - half * near.shape[0] + width, :]

            def put(lines, value, number=number, width=width):
                if width == GROUP:
                    whole_ref[number, lines, :] = value
                else:
                    part_ref[lines, :] = value

            if section == 0:
                project_lines(xq_ref, w, 2, QUERY_FACTOR, put)
            else:
                project_lines(mid_ref, w, 2, 1, put)

    for half in range(2):
        pl.when(place_ref[HALF] == half)(functools.partial(run, half))


def project_rest(half, sections, channels, near_at, far_at, sources, put):
    xq_ref, mid_ref, outer_ref = sources
    edge, mid = outer_ref.shape[0] // 2, mid_ref.shape[0]
    for number, at, section, group, lane, width in numbered_chunks(channels, half):
        if section in sections and section > 0:
            w = near_at(at, width)
            for first, to in ((0, 0), (edge, edge + mid)):
                put(section, group, lane, width, slice(to, to + edge), nt(outer_ref[first : first + edge, :], w).astype(jnp.bfloat16))
    for at, section, group, lane, width in column_chunks(channels, 1 - half):
        if section not in sections:
            continue
        w = far_at(at, width)
        if section == 0:
            project_lines(xq_ref, w, 2, QUERY_FACTOR, functools.partial(put, section, group, lane, width))
            continue
        for first, to in ((0, 0), (edge, edge + mid)):
            put(section, group, lane, width, slice(to, to + edge), nt(outer_ref[first : first + edge, :], w).astype(jnp.bfloat16))

        def put_mid(lines, value, section=section, group=group, lane=lane, width=width):
            put(section, group, lane, width, slice(edge + lines.start, edge + lines.stop), value)

        project_lines(mid_ref, w, 2, 1, put_mid)


def late_kernel(pieces, triple_rows, place_ref, *refs):
    sources, refs = refs[: len(pieces)], refs[len(pieces) :]
    near, whole_ref, part_ref, xq_ref, mid_ref, outer_ref, q_s, k_s, wt, near_sem = refs
    channels = wt.shape[1]
    edge, mid = outer_ref.shape[0] // 2, mid_ref.shape[0]
    for j, (off, start) in enumerate(pieces):
        to = pl.multiple_of((place_ref[ROW] ^ off) * triple_rows + place_ref[STARTS + start], 16)
        wt[pl.ds(to, sources[j].shape[0]), :] = sources[j][...]
    to = pl.multiple_of(place_ref[HALF] * near.shape[0], 16)
    near_copy = pltpu.make_async_copy(near, wt.at[pl.ds(to, near.shape[0]), :], near_sem)
    near_copy.start()

    def put(section, group, lane, width, lines, value):
        if section == 0:
            q_s[group, lines, :] = value
        else:
            k_s[group, lines, lane : lane + width] = value

    def run(half):
        for number, at, section, group, lane, width in numbered_chunks(channels, half):
            if section == 0:
                q_s[group] = whole_ref[number]
            elif section == 1 and width == GROUP:
                k_s[group, edge : edge + mid, :] = whole_ref[number, :mid, :]
            elif section == 1:
                k_s[group, edge : edge + mid, lane : lane + width] = part_ref[...]
        base = half * near.shape[0]
        project_rest(
            half, (0, 1), channels, lambda at, width: near[at - base : at - base + width, :], lambda at, width: wt[at : at + width, :],
            (xq_ref, mid_ref, outer_ref), put,
        )

    for half in range(2):
        pl.when(place_ref[HALF] == half)(functools.partial(run, half))
    near_copy.wait()


def value_kernel(place_ref, wt, whole_ref, mid_ref, outer_ref, v_s):
    channels = wt.shape[1]
    edge, mid = outer_ref.shape[0] // 2, mid_ref.shape[0]

    def put(section, group, lane, width, lines, value):
        v_s[group, lines, lane : lane + width] = value

    def run(half):
        for number, at, section, group, lane, width in numbered_chunks(channels, half):
            if section == 2:
                v_s[group, edge : edge + mid, :] = whole_ref[number, :mid, :]
        weights = lambda at, width: wt[at : at + width, :]
        project_rest(half, (2,), channels, weights, weights, (None, mid_ref, outer_ref), put)

    for half in range(2):
        pl.when(place_ref[HALF] == half)(functools.partial(run, half))


def carrier_kernel(offsets, place_ref, wt, *refs):
    shards = len(offsets)
    finals, refs = refs[:shards], refs[shards:]
    summary_ref, wo, kce, vc_s = refs
    per_row = summary_ref.shape[1]
    channels = wt.shape[1]
    groups = channels // GROUP
    heads = channels // HEAD_DIM
    factor = HEAD_DIM ** (-0.5)
    carriers_here = vc_s.shape[0]
    final_rows = wo.shape[0] // shards
    for j, off in enumerate(offsets):
        to = pl.multiple_of((place_ref[ROW] ^ off) * final_rows, 16)
        wo[pl.ds(to, final_rows), :] = finals[j][:final_rows, :]
    carriers = jnp.concatenate([final[final_rows:, :].astype(jnp.float32) for final in finals], axis=0)
    own = carriers[:carriers_here]
    carriers = layer_normalise(carriers).astype(jnp.bfloat16)
    own_norm = layer_normalise(own).astype(jnp.bfloat16)
    qc = (nt(own_norm, wt[:channels, :]) * factor).astype(jnp.bfloat16).astype(jnp.float32)
    kc = nt(carriers, wt[channels : 2 * channels, :]).astype(jnp.bfloat16)
    vc = nt(carriers, wt[2 * channels :, :]).astype(jnp.bfloat16)
    head_of = lax.broadcasted_iota(jnp.int32, (1, channels), 1) // HEAD_DIM
    stacked = jnp.concatenate([jnp.where(head_of == h, qc, 0.0) for h in range(heads)], axis=0)
    e = jnp.exp(nt(stacked.astype(jnp.bfloat16), kc))
    weights = (e / jnp.sum(e, axis=-1, keepdims=True)).astype(jnp.bfloat16)
    o = nn(weights, vc)
    mix = jnp.zeros((carriers_here, channels), jnp.float32)
    for h in range(heads):
        mix = jnp.where(head_of == h, o[h * carriers_here : (h + 1) * carriers_here, :], mix)
    renewed = own + nt(mix.astype(jnp.bfloat16), wo[...])
    for i in range(summary_ref.shape[0]):
        summary_ref[i] = renewed[i * per_row : (i + 1) * per_row, :].astype(jnp.bfloat16)
    fresh = nt(layer_normalise(renewed).astype(jnp.bfloat16), wt[channels:, :]).astype(jnp.bfloat16).astype(jnp.float32)
    vc_s[...] = fresh[:, channels:]
    same = (
        lax.broadcasted_iota(jnp.int32, (GROUP, GROUP), 0) // HEAD_DIM
        == lax.broadcasted_iota(jnp.int32, (GROUP, GROUP), 1) // HEAD_DIM
    )
    windows = kce.shape[0] // groups
    for w in range(windows):
        for g in range(groups):
            kce[w * groups + g] = jnp.where(same, fresh[w : w + 1, g * GROUP : (g + 1) * GROUP], 0.0).astype(jnp.bfloat16)


def attend_kernel(tall, broad, q_s, k_s, v_s, hide_ref, kce, vc_s, mix_s, pc_s, even_s, odd_s):
    groups, tiles = q_s.shape[0], hide_ref.shape[0]
    heads_in = GROUP // HEAD_DIM
    queries, span = TILE * TILE, 2 * TILE * TILE
    side = PATCH_SIDE // TILE
    wide = (tall + 1) * queries
    qi = lax.broadcasted_iota(jnp.int32, (queries, 2 * span), 0)
    ki = lax.broadcasted_iota(jnp.int32, (queries, 2 * span), 1)
    row_step = (ki % span) // TILE - qi // TILE
    col_step = (ki // span) * TILE + ki % TILE - qi % TILE
    seen = (row_step >= 0) & (row_step <= 2 * RADIUS) & (col_step >= 0) & (col_step <= 2 * RADIUS)
    band = jnp.where(seen, 0.0, HIDDEN)
    group_head = lax.broadcasted_iota(jnp.int32, (1, GROUP), 1) // HEAD_DIM
    only = [jnp.where(group_head == h, 1.0, 0.0).astype(jnp.bfloat16) for h in range(heads_in)]
    in_pair = LANES // HEAD_DIM
    pair_head = lax.broadcasted_iota(jnp.int32, (1, LANES), 1) // HEAD_DIM

    for c in range(broad):
        for w in range(tall // side):
            at = slice((c * tall + w * side) * queries, (c * tall + (w + 1) * side) * queries)
            window = w * (broad // side) + c // side
            for g in range(groups):
                pc_s[at, g * GROUP : (g + 1) * GROUP] = jnp.exp2(nt(q_s[g, at, :], kce[window * groups + g]))

    def keys_at(t):
        k0 = pl.multiple_of(t // tall * wide + t % tall * queries, queries)
        return k0, pl.multiple_of(k0 + wide, queries)

    def scores(t, ref):
        q_at = pl.multiple_of(t * queries, queries)
        k0, k1 = keys_at(t)
        for g in range(groups):
            q = q_s[g, pl.ds(q_at, queries), :]
            qq = jnp.concatenate([q * mask for mask in only], axis=0)
            k = jnp.concatenate([k_s[g, pl.ds(k0, span), :], k_s[g, pl.ds(k1, span), :]], axis=0)
            ref[g] = nt(qq, k)

    def finish(t, ref):
        q_at = pl.multiple_of(t * queries, queries)
        k0, k1 = keys_at(t)
        window = t % tall // side * (broad // side) + t // tall // side
        bias = band + hide_ref[t][0:1, :]
        for g in range(groups):
            p = jnp.exp2(ref[g].reshape(heads_in, queries, 2 * span) + bias[None])
            total = jnp.sum(p, axis=-1, keepdims=True)
            v = jnp.concatenate([v_s[g, pl.ds(k0, span), :], v_s[g, pl.ds(k1, span), :]], axis=0)
            o = nn(p.reshape(heads_in * queries, 2 * span).astype(jnp.bfloat16), v).reshape(heads_in, queries, GROUP)
            v_new = vc_s[pl.ds(window, 1), g * GROUP : (g + 1) * GROUP]
            for j in range(GROUP // LANES):
                lanes = slice(j * LANES, (j + 1) * LANES)
                at = slice(g * GROUP + j * LANES, g * GROUP + (j + 1) * LANES)
                kept, kept_total = o[j * in_pair, :, lanes], total[j * in_pair]
                for h in range(1, in_pair):
                    kept = jnp.where(pair_head == h, o[j * in_pair + h, :, lanes], kept)
                    kept_total = jnp.where(pair_head == h, total[j * in_pair + h], kept_total)
                new = pc_s[pl.ds(q_at, queries), at]
                mixed = (kept + new * v_new[:, lanes]) / (kept_total + new)
                mix_s[pl.ds(q_at, queries), at] = mixed.astype(jnp.bfloat16)

    scores(0, even_s)

    def two(i, _):
        t = 2 * i
        scores(t + 1, odd_s)
        finish(t, even_s)
        scores(jnp.minimum(t + 2, tiles - 1), even_s)
        finish(t + 1, odd_s)
        return 0

    lax.fori_loop(0, tiles // 2, two, 0)


def out_kernel(x_ref, mix_s, wo, out_hbm, out_ref, out_sems):
    rows, cols, channels = x_ref.shape
    going = []
    for pair in range(cols // (2 * TILE)):
        both = slice(2 * pair * TILE, 2 * (pair + 1) * TILE)
        for g in range(channels // GROUP):
            at = slice(g * GROUP, (g + 1) * GROUP)
            w = wo[at, :]
            y = nt(mix_s[2 * pair * rows * TILE : 2 * (pair + 1) * rows * TILE, :], w).reshape(2, rows, TILE, GROUP)
            y = jnp.concatenate([y[0], y[1]], axis=1) + x_ref[:, both, at].astype(jnp.float32)
            out_ref[pair, :, :, at] = y.astype(jnp.bfloat16)
        copy = pltpu.make_async_copy(out_ref.at[pair], out_hbm.at[:, both, :], out_sems.at[pair])
        copy.start()
        going.append(copy)
    for copy in going:
        copy.wait()


def local(grid_elements, summary_vectors, triple_projection, final_projection, genuine_flags):
    rows, cols, channels = grid_elements.shape
    wide_rows, wide_cols = rows + 2 * RADIUS, cols + 2 * RADIUS

    triple_t, final_t = triple_projection.T, final_projection.T
    vmem = pl.BlockSpec(memory_space=pltpu.VMEM)
    anywhere = pl.BlockSpec(memory_space=pl.ANY)
    scalars = pl.BlockSpec(memory_space=pltpu.SMEM)
    hbm = pl.BlockSpec(memory_space=pltpu.HBM)
    small = pltpu.CompilerParams(vmem_limit_bytes=8 * 1024 * 1024)
    row_strip = jax.ShapeDtypeStruct((RADIUS, cols, channels), jnp.bfloat16)
    col_strip = jax.ShapeDtypeStruct((wide_rows // 2, 2 * RADIUS, channels), jnp.bfloat16)

    row, col, img = lax.axis_size("row"), lax.axis_size("col"), lax.axis_size("img")
    row_at, col_at, img_at = lax.axis_index("row"), lax.axis_index("col"), lax.axis_index("img")
    row_bits = bits_of(row)
    far, rest = row_bits[0], row_bits[1:]
    piece_rows = triple_t.shape[0] * 5 // (8 * img) // 16 * 16
    relays = img if piece_rows else 0
    starts = [(img_at - k) % img for k in range(relays)] + [jnp.int32(relays)]
    place = [row_at == 0, row_at == row - 1, col_at == 0, col_at == col - 1, row_at % 2 == 0, col_at % 2 == 0, row_at, row_at // far]
    place = jnp.stack([jnp.asarray(p).astype(jnp.int32) for p in place + [start * piece_rows for start in starts]])

    mark, even_rows, odd_rows, x = pl.pallas_call(
        edge_kernel,
        out_shape=(
            pltpu.VMEM((rows, cols, LANES), jnp.bfloat16),
            pltpu.VMEM(row_strip.shape, jnp.bfloat16),
            pltpu.VMEM(row_strip.shape, jnp.bfloat16),
            pltpu.VMEM(grid_elements.shape, jnp.bfloat16),
        ),
        in_specs=[scalars, hbm, hbm],
        out_specs=(vmem,) * 4,
        scratch_shapes=[
            pltpu.VMEM((rows, cols), jnp.int32),
            pltpu.VMEM((rows * cols, cols), jnp.bfloat16),
            pltpu.SemaphoreType.DMA((2,)),
        ],
        compiler_params=small,
        cost_estimate=pl.CostEstimate(flops=1_000_000, bytes_accessed=1_000_000, transcendentals=0),
        name="edge_rows",
    )(place, *(pltpu.with_memory_space_constraint(a, pltpu.HBM) for a in (genuine_flags, grid_elements)))
    mine, last = pl.pallas_call(
        piece_kernel,
        out_shape=(
            pltpu.VMEM((max(piece_rows, 16), channels), jnp.bfloat16),
            pltpu.VMEM((triple_t.shape[0] - relays * piece_rows, channels), jnp.bfloat16),
        ),
        in_specs=[scalars, hbm],
        out_specs=(vmem, vmem),
        scratch_shapes=[pltpu.SemaphoreType.DMA((2,))],
        compiler_params=small,
        cost_estimate=pl.CostEstimate(flops=1_000_000, bytes_accessed=1_000_000, transcendentals=0),
        name="pieces",
    )(place, pltpu.with_memory_space_constraint(after(triple_t, even_rows), pltpu.HBM))
    xq = pl.pallas_call(
        own_kernel,
        out_shape=pltpu.VMEM((rows * cols, channels), jnp.bfloat16),
        in_specs=[vmem],
        out_specs=vmem,
        compiler_params=small,
        cost_estimate=pl.CostEstimate(flops=1_000_000, bytes_accessed=1_000_000, transcendentals=0),
        name="own_norm",
    )(x)
    even_rows, odd_rows = pair_swapped(even_rows, odd_rows, "row")

    far_pieces = []
    if relays:
        first = swapped(mine, "row", far)
    far_last = swapped(after(last, even_rows, odd_rows), "row", far)

    own_rows = summary_vectors.shape[0] * summary_vectors.shape[1]
    carrier_tiles = -(-own_rows // TILE)
    even_cols, odd_cols = pl.pallas_call(
        strip_kernel,
        out_shape=(
            pltpu.VMEM((col_strip.shape[0] + carrier_tiles, *col_strip.shape[1:]), jnp.bfloat16),
            pltpu.VMEM(col_strip.shape, jnp.bfloat16),
        ),
        in_specs=[scalars] + [vmem] * 5,
        out_specs=(vmem,) * 2,
        scratch_shapes=[pltpu.VMEM((carrier_tiles * TILE, channels), jnp.float32)],
        compiler_params=small,
        cost_estimate=pl.CostEstimate(flops=1_000_000, bytes_accessed=2_000_000, transcendentals=0),
        name="edge_columns",
    )(place, x, after(mark, xq), even_rows, odd_rows, summary_vectors)
    even_cols, odd_cols = pair_swapped(even_cols, odd_cols, "col")
    groups = channels // GROUP
    triples, offsets = [triple_t], [0]
    for bit in rest:
        triples = triples + [swapped(p, "row", bit) for p in triples]
        offsets = offsets + [o ^ bit for o in offsets]
    mid = pl.pallas_call(
        middle_kernel,
        out_shape=pltpu.VMEM(((wide_cols // TILE - 2) * wide_rows * TILE, channels), jnp.bfloat16),
        in_specs=[scalars] + [vmem] * 3,
        out_specs=vmem,
        scratch_shapes=[pltpu.VMEM(row_strip.shape, jnp.float32)] * 2,
        compiler_params=small,
        cost_estimate=pl.CostEstimate(flops=1_000_000, bytes_accessed=1_000_000, transcendentals=0),
        name="middle_blocks",
    )(place, xq, even_rows, odd_rows)
    whole, part, near = pl.pallas_call(
        functools.partial(early_kernel, offsets),
        out_shape=(
            pltpu.VMEM((3 * groups // 2, rows * cols, GROUP), jnp.bfloat16),
            pltpu.VMEM((mid.shape[0], GROUP // 2), jnp.bfloat16),
            pltpu.VMEM((3 * channels // 2, channels), jnp.bfloat16),
        ),
        in_specs=[scalars] + [vmem] * (len(triples) + 2),
        out_specs=(vmem,) * 3,
        compiler_params=pltpu.CompilerParams(vmem_limit_bytes=16 * 1024 * 1024),
        cost_estimate=pl.CostEstimate(flops=1_000_000, bytes_accessed=1_000_000, transcendentals=0),
        name="project_early",
    )(place, *triples, xq, mid)

    carriers = pl.pallas_call(
        carrier_pair_kernel,
        out_shape=pltpu.VMEM((2 * own_rows, channels), jnp.bfloat16),
        in_specs=[vmem, anywhere],
        out_specs=vmem,
        scratch_shapes=[
            pltpu.VMEM((carrier_tiles, TILE, channels), jnp.bfloat16),
            pltpu.VMEM((2 * own_rows, channels), jnp.float32),
            pltpu.SemaphoreType.DMA,
        ],
        compiler_params=small,
        cost_estimate=pl.CostEstimate(flops=1_000, bytes_accessed=1_000, transcendentals=0),
        name="carrier_pair",
    )(summary_vectors, after(even_cols, near))
    parts = [carriers]
    for bit in bits_of(col)[:-1]:
        carriers = carriers if len(parts) == 1 else jnp.concatenate(parts, axis=0)
        got = swapped(carriers, "col", 2 * bit - 1)
        parts.append(got)
    if relays:
        first = after(first, even_cols, odd_cols, parts[0])
        others = [lax.ppermute(first, "img", [(i, (i + k) % img) for i in range(img)]) for k in range(1, relays)]
        far_pieces = [first] + others
    far_pieces.append(far_last)

    tiles = (rows // TILE) * (cols // TILE)
    keys = 4 * TILE * TILE
    outer, hide = pl.pallas_call(
        outer_kernel,
        out_shape=(
            pltpu.VMEM((2 * wide_rows * TILE, channels), jnp.bfloat16),
            pltpu.VMEM((tiles, 8, keys), jnp.float32),
        ),
        in_specs=[scalars] + [vmem] * 6,
        out_specs=(vmem,) * 2,
        scratch_shapes=[
            *[pltpu.VMEM((RADIUS, 2 * TILE, channels), jnp.float32)] * 2,
            *[pltpu.VMEM(col_strip.shape, jnp.float32)] * 2,
            *[pltpu.VMEM((*shape.shape[:2], LANES), jnp.float32) for shape in (row_strip, row_strip, col_strip, col_strip)],
            pltpu.VMEM((wide_rows * wide_cols, LANES), jnp.bfloat16),
        ],
        compiler_params=pltpu.CompilerParams(vmem_limit_bytes=12 * 1024 * 1024),
        cost_estimate=pl.CostEstimate(flops=10_000_000, bytes_accessed=6_000_000, transcendentals=1000),
        name="outer_blocks",
    )(place, xq, mark, even_rows, odd_rows, even_cols, odd_cols)

    final_pack = pl.pallas_call(
        pack_kernel,
        out_shape=pltpu.VMEM((final_t.shape[0] + col * own_rows, channels), jnp.bfloat16),
        in_specs=[vmem] * (1 + len(parts)),
        out_specs=vmem,
        compiler_params=small,
        cost_estimate=pl.CostEstimate(flops=1_000, bytes_accessed=1_000, transcendentals=0),
        name="final_pack",
    )(final_t, *parts[:-1], after(parts[-1], outer))
    finals = [final_pack]
    for bit in rest:
        finals = finals + [swapped(p, "row", bit) for p in finals]

    far_final = swapped(final_pack, "row", far)

    far_offsets = [far]
    far_pieces = [[after(piece, outer, got)] for piece in far_pieces]
    for bit in rest:
        far_pieces = [same + [swapped(p, "row", bit) for p in same] for same in far_pieces]
        far_offsets = far_offsets + [o ^ bit for o in far_offsets]

    numbered = [(off, number) for number in range(len(far_pieces)) for off in far_offsets]
    sources = [piece for same in far_pieces for piece in same]
    q, k, wt = pl.pallas_call(
        functools.partial(late_kernel, numbered, triple_t.shape[0]),
        out_shape=(
            jax.ShapeDtypeStruct((groups, rows * cols, GROUP), jnp.bfloat16),
            jax.ShapeDtypeStruct((groups, wide_rows * wide_cols, GROUP), jnp.bfloat16),
            jax.ShapeDtypeStruct((3 * channels, channels), jnp.bfloat16),
        ),
        in_specs=[scalars] + [vmem] * (len(sources) + 6),
        out_specs=(vmem,) * 3,
        scratch_shapes=[pltpu.SemaphoreType.DMA],
        compiler_params=pltpu.CompilerParams(vmem_limit_bytes=VMEM_BYTES),
        cost_estimate=pl.CostEstimate(flops=1_000_000, bytes_accessed=1_000_000, transcendentals=0),
        name="project_late",
    )(place, *sources, near, whole, part, xq, mid, outer)

    v = pl.pallas_call(
        value_kernel,
        out_shape=jax.ShapeDtypeStruct((groups, wide_rows * wide_cols, GROUP), jnp.bfloat16),
        in_specs=[scalars] + [vmem] * 4,
        out_specs=vmem,
        compiler_params=pltpu.CompilerParams(vmem_limit_bytes=VMEM_BYTES),
        cost_estimate=pl.CostEstimate(flops=3_000_000_000, bytes_accessed=7_000_000, transcendentals=0),
        name="values",
    )(place, wt, whole, mid, outer)

    far_finals = [after(far_final, q)]
    for bit in rest:
        far_finals = far_finals + [swapped(p, "row", bit) for p in far_finals]
    finals, offsets = finals + far_finals, offsets + far_offsets
    carriers_here = carrier_tiles * TILE
    summary_result, wo, kce, vc = pl.pallas_call(
        functools.partial(carrier_kernel, offsets),
        out_shape=(
            jax.ShapeDtypeStruct(summary_vectors.shape, jnp.bfloat16),
            jax.ShapeDtypeStruct((channels, channels), jnp.bfloat16),
            jax.ShapeDtypeStruct((own_rows * groups, GROUP, GROUP), jnp.bfloat16),
            jax.ShapeDtypeStruct((carriers_here, channels), jnp.float32),
        ),
        in_specs=[scalars] + [vmem] * (1 + len(finals)),
        out_specs=(vmem,) * 4,
        compiler_params=pltpu.CompilerParams(vmem_limit_bytes=VMEM_BYTES),
        cost_estimate=pl.CostEstimate(flops=500_000_000, bytes_accessed=5_000_000, transcendentals=10_000),
        name="carriers",
    )(place, wt, *finals)

    scores = (groups, GROUP // HEAD_DIM * TILE * TILE, keys)
    mix = pl.pallas_call(
        functools.partial(attend_kernel, rows // TILE, cols // TILE),
        out_shape=jax.ShapeDtypeStruct((rows * cols, channels), jnp.bfloat16),
        in_specs=[vmem] * 6,
        out_specs=vmem,
        scratch_shapes=[
            pltpu.VMEM((rows * cols, channels), jnp.float32),
            pltpu.VMEM(scores, jnp.float32),
            pltpu.VMEM(scores, jnp.float32),
        ],
        compiler_params=pltpu.CompilerParams(vmem_limit_bytes=VMEM_BYTES),
        cost_estimate=pl.CostEstimate(flops=4_000_000_000, bytes_accessed=12_000_000, transcendentals=4_000_000),
        name="attend",
    )(q, k, v, hide, kce, vc)

    out = pl.pallas_call(
        out_kernel,
        out_shape=jax.ShapeDtypeStruct(grid_elements.shape, jnp.bfloat16),
        in_specs=[vmem] * 3,
        out_specs=anywhere,
        scratch_shapes=[
            pltpu.VMEM((cols // (2 * TILE), rows, 2 * TILE, channels), jnp.bfloat16),
            pltpu.SemaphoreType.DMA((cols // (2 * TILE),)),
        ],
        compiler_params=pltpu.CompilerParams(vmem_limit_bytes=VMEM_BYTES),
        cost_estimate=pl.CostEstimate(flops=1_200_000_000, bytes_accessed=6_000_000, transcendentals=0),
        name="out",
    )(x, mix, wo)
    return (out, summary_result)


def solution(mesh):
    placed = (
        P(("img", "row"), "col", None),
        P(("img", "row"), "col", None),
        P(None, "row"),
        P(None, "row"),
        P(("img", "row"), "col"),
    )
    return jax.shard_map(
        local,
        mesh=mesh,
        in_specs=placed,
        out_specs=(P(("img", "row"), "col", None), P(("img", "row"), "col", None)),
        check_vma=False,
    )
```

```python
import functools

import jax
import jax.numpy as jnp
from jax import lax
from jax.experimental import pallas as pl
from jax.experimental.pallas import tpu as pltpu
from jax.sharding import PartitionSpec as P

HEAD_DIM = 64
PATCH_SIDE = 16
RADIUS = 4
TILE = 2 * RADIUS
LANES = 128
GROUP = 256
INVALID = 100.0
HIDDEN = -1e30
LOG2_E = 1.4426950408889634
EVEN_ROW, EVEN_COL, ROW, HALF, STARTS = 4, 5, 6, 7, 8
VMEM_BYTES = 26 * 1024 * 1024


def nt(a, b):
    return lax.dot_general(a, b, (((1,), (1,)), ((), ())), preferred_element_type=jnp.float32)


def nn(a, b):
    return lax.dot_general(a, b, (((1,), (0,)), ((), ())), preferred_element_type=jnp.float32)


def layer_normalise(lines):
    center = lines - jnp.mean(lines, axis=-1, keepdims=True)
    spread = jnp.mean(center * center, axis=-1, keepdims=True)
    return center * lax.rsqrt(spread + 1e-05)


def pair_swapped(even_block, odd_block, axis):
    count = lax.axis_size(axis)
    got = []
    for first, block in ((0, even_block), (1, odd_block)):
        pairs = [(i, i + 1) for i in range(first, count - 1, 2)]
        got.append(lax.ppermute(block, axis, pairs + [(b, a) for a, b in pairs]))
    return got


def swapped(block, axis, bit):
    count = lax.axis_size(axis)
    return lax.ppermute(block, axis, [(i, i ^ bit) for i in range(count)])


def after(block, *others):
    return lax.optimization_barrier((block, *others))[0]


def bits_of(count):
    bits, bit = [], count // 2
    while bit:
        bits.append(bit)
        bit //= 2
    return bits


def marked_lanes(lines, hidden):
    first = jnp.where(hidden, INVALID, lines[:, :, :LANES])
    return jnp.concatenate([first, lines[:, :, LANES:]], axis=2)


def edge_kernel(place_ref, flags_hbm, x_hbm, mark_ref, even_ref, odd_ref, x_ref, *scratch):
    flags_ref, spread, sems = scratch
    rows, cols = flags_ref.shape
    flags_copy = pltpu.make_async_copy(flags_hbm, flags_ref, sems.at[0])
    x_copy = pltpu.make_async_copy(x_hbm, x_ref, sems.at[1])
    flags_copy.start()
    x_copy.start()
    flags_copy.wait()
    row_at = lax.broadcasted_iota(jnp.int32, (cols, cols), 0)
    diagonal = row_at == lax.broadcasted_iota(jnp.int32, (cols, cols), 1)
    for r in range(rows):
        hidden = jnp.where(flags_ref[r : r + 1, :] > 0, 0.0, INVALID)
        spread[r * cols : (r + 1) * cols, :] = jnp.where(diagonal, hidden, 0.0).astype(jnp.bfloat16)
    marks = nn(spread[...], jnp.ones((cols, LANES), jnp.bfloat16)).reshape(rows, cols, LANES)
    mark_ref[...] = marks.astype(jnp.bfloat16)
    x_copy.wait()
    first, last = [
        marked_lanes(x_ref[at].astype(jnp.float32), marks[at] > INVALID / 2)
        for at in (slice(0, RADIUS), slice(rows - RADIUS, rows))
    ]
    even = place_ref[EVEN_ROW] > 0
    even_ref[...] = jnp.where(even, last, first).astype(jnp.bfloat16)
    odd_ref[...] = jnp.where(even, first, last).astype(jnp.bfloat16)


def piece_kernel(place_ref, triple_hbm, mine_ref, last_ref, sems):
    start = pl.multiple_of(place_ref[STARTS], 16)
    last = triple_hbm.shape[0] - last_ref.shape[0]
    copies = [
        pltpu.make_async_copy(triple_hbm.at[pl.ds(start, mine_ref.shape[0]), :], mine_ref, sems.at[0]),
        pltpu.make_async_copy(triple_hbm.at[last:, :], last_ref, sems.at[1]),
    ]
    for copy in copies:
        copy.start()
    for copy in copies:
        copy.wait()


def strip_kernel(place_ref, x_ref, mark_ref, even_rows_ref, odd_rows_ref, carriers_ref, even_ref, odd_ref, carriers_s):
    per_row = carriers_ref.shape[1]
    carriers_s[...] = jnp.zeros_like(carriers_s)
    for i in range(carriers_ref.shape[0]):
        carriers_s[i * per_row : (i + 1) * per_row, :] = carriers_ref[i].astype(jnp.float32)
    for i in range(carriers_s.shape[0] // TILE):
        even_ref[odd_ref.shape[0] + i] = carriers_s[i * TILE : (i + 1) * TILE, :].astype(jnp.bfloat16)
    rows, cols, channels = x_ref.shape
    middle = rows // 2
    low = lax.broadcasted_iota(jnp.int32, (1, TILE, 1), 1) < RADIUS
    even_row, even_col = place_ref[EVEN_ROW] > 0, place_ref[EVEN_COL] > 0
    for lane in range(0, channels, LANES):
        lanes = slice(lane, lane + LANES)
        strips = []
        for columns, last in ((slice(0, TILE), False), (slice(cols - TILE, cols), True)):

            def own(part):
                lines = x_ref[part, columns, lanes].astype(jnp.float32)
                if lane == 0:
                    lines = jnp.where(mark_ref[part, columns, :].astype(jnp.float32) > INVALID / 2, INVALID, lines)
                return lines

            even_rows = even_rows_ref[:, columns, lanes].astype(jnp.float32)
            odd_rows = odd_rows_ref[:, columns, lanes].astype(jnp.float32)
            top, bottom = jnp.where(even_row, odd_rows, even_rows), jnp.where(even_row, even_rows, odd_rows)
            upper = jnp.concatenate([top, own(slice(0, middle))], axis=0)
            lower = jnp.concatenate([own(slice(middle, rows)), bottom], axis=0)
            if last:
                upper = jnp.roll(upper, RADIUS, axis=1)
            else:
                lower = jnp.roll(lower, RADIUS, axis=1)
            strips.append(jnp.where(low, upper, lower))
        first, last = strips
        even_ref[: odd_ref.shape[0], :, lanes] = jnp.where(even_col, last, first).astype(jnp.bfloat16)
        odd_ref[:, :, lanes] = jnp.where(even_col, first, last).astype(jnp.bfloat16)


def carrier_pair_kernel(own_ref, got_hbm, out_ref, got_s, pair_s, sem):
    per_row, here = own_ref.shape[1], own_ref.shape[0] * own_ref.shape[1]
    tiles = got_s.shape[0]
    copy = pltpu.make_async_copy(got_hbm.at[got_hbm.shape[0] - tiles :], got_s, sem)
    copy.start()
    for i in range(own_ref.shape[0]):
        pair_s[i * per_row : (i + 1) * per_row, :] = own_ref[i].astype(jnp.float32)
    copy.wait()
    pair_s[here:, :] = got_s[...].astype(jnp.float32).reshape(tiles * TILE, -1)[:here]
    out_ref[...] = pair_s[...].astype(jnp.bfloat16)


def join_kernel(*refs):
    parts, out_ref = refs[:-1], refs[-1]
    out_ref[...] = jnp.concatenate([part[...].astype(jnp.float32) for part in parts], axis=0).astype(jnp.bfloat16)


def own_kernel(x_ref, xq_ref):
    rows, cols, _ = x_ref.shape
    step = 4

    def own(i, _):
        at = pl.multiple_of(i * step, step)
        y = layer_normalise(x_ref[pl.ds(at, step)].astype(jnp.float32))
        for c in range(cols // TILE):
            piece = y[:, c * TILE : (c + 1) * TILE, :].reshape(step * TILE, -1)
            to = pl.multiple_of(c * rows * TILE + at * TILE, step * TILE)
            xq_ref[pl.ds(to, step * TILE), :] = piece.astype(jnp.bfloat16)
        return 0

    lax.fori_loop(0, rows // step, own, 0)


def columns_of(lines):
    return [lines[:, c : c + TILE, :] for c in range(0, lines.shape[1], TILE)]


def tile_of(xq_ref, column, rows, at, step):
    first = pl.multiple_of(column * rows * TILE + at * TILE, step * TILE)
    return xq_ref[pl.ds(first, step * TILE), :].astype(jnp.float32).reshape(step, TILE, -1)


def store_lines(ref, block, wide_rows, at, lines):
    size = lines.shape[0] * TILE
    to = block * wide_rows * TILE + at * TILE
    to = to if isinstance(to, int) else pl.multiple_of(to, size)
    ref[pl.ds(to, size), :] = lines.reshape(size, -1).astype(jnp.bfloat16)


def middle_kernel(place_ref, xq_ref, even_rows_ref, odd_rows_ref, mid_ref, top_s, bottom_s):
    cols = even_rows_ref.shape[1]
    rows, step = xq_ref.shape[0] // cols, 2
    wide_rows = rows + 2 * RADIUS
    flip = place_ref[EVEN_ROW] > 0
    for i in range(0, RADIUS, step):
        a, b = even_rows_ref[i : i + step].astype(jnp.float32), odd_rows_ref[i : i + step].astype(jnp.float32)
        top_s[i : i + step] = layer_normalise(jnp.where(flip, b, a))
        bottom_s[i : i + step] = layer_normalise(jnp.where(flip, a, b))
    low = lax.broadcasted_iota(jnp.int32, (1, TILE, 1), 1) < RADIUS

    def merge(at, blocks):
        moved = [jnp.roll(block, RADIUS, axis=1) for block in blocks]
        for c in range(1, len(blocks)):
            store_lines(mid_ref, c - 1, wide_rows, at, jnp.where(low, moved[c - 1], moved[c]))

    for i in range(0, RADIUS, step):
        merge(i, columns_of(top_s[i : i + step]))
        merge(RADIUS + rows + i, columns_of(bottom_s[i : i + step]))

    def middle(i, _):
        at = pl.multiple_of(i * step, step)
        merge(RADIUS + at, [tile_of(xq_ref, c, rows, at, step) for c in range(cols // TILE)])
        return 0

    lax.fori_loop(0, rows // step, middle, 0)


def outer_kernel(place_ref, xq_ref, mark_ref, even_rows_ref, odd_rows_ref, even_cols_ref, odd_cols_ref, outer_ref, hide_ref, *scratch):
    rows, cols, _ = mark_ref.shape
    wide_rows, wide_cols = rows + 2 * RADIUS, cols + 2 * RADIUS
    half = wide_rows // 2
    step = 2
    top_s, bottom_s, left_s, right_s, top_ref, bottom_ref, left_ref, right_ref, flag_s = scratch
    flip = place_ref[EVEN_ROW] > 0
    a, b = even_rows_ref[...].astype(jnp.float32), odd_rows_ref[...].astype(jnp.float32)
    for lines, out, flags in ((jnp.where(flip, b, a), top_s, top_ref), (jnp.where(flip, a, b), bottom_s, bottom_ref)):
        ends = jnp.concatenate([lines[:, :TILE, :], lines[:, cols - TILE :, :]], axis=1)
        out[...] = layer_normalise(ends)
        flags[...] = lines[:, :, :LANES]
    flip = place_ref[EVEN_COL] > 0
    size = 5
    for i in range(0, odd_cols_ref.shape[0], size):
        a, b = even_cols_ref[i : i + size].astype(jnp.float32), odd_cols_ref[i : i + size].astype(jnp.float32)
        for lines, out, flags in ((jnp.where(flip, b, a), left_s, left_ref), (jnp.where(flip, a, b), right_s, right_ref)):
            out[i : i + size] = layer_normalise(lines)
            flags[i : i + size] = lines[:, :, :LANES]
    low = lax.broadcasted_iota(jnp.int32, (1, TILE, 1), 1) < RADIUS

    def lines_of(ref):
        return ref.astype(jnp.float32)

    def merge(at, blocks, left, right, to_ref):
        moved = [left] + [jnp.roll(block, RADIUS, axis=1) for block in blocks] + [right]
        for c in range(len(blocks) + 1):
            store_lines(to_ref, c, wide_rows, at, jnp.where(low, moved[c], moved[c + 1]))

    def merge_ends(at, first, last, left, right):
        store_lines(outer_ref, 0, wide_rows, at, jnp.where(low, left, jnp.roll(first, RADIUS, axis=1)))
        store_lines(outer_ref, 1, wide_rows, at, jnp.where(low, jnp.roll(last, RADIUS, axis=1), right))

    def sides(at, upper, left_ref, right_ref, lanes):
        if upper:
            at = at - half
            left, right = jnp.roll(lines_of(left_ref[pl.ds(at, step), :, lanes]), RADIUS, axis=1), lines_of(
                right_ref[pl.ds(at, step), :, lanes]
            )
        else:
            left, right = lines_of(left_ref[pl.ds(at, step), :, lanes]), jnp.roll(
                lines_of(right_ref[pl.ds(at, step), :, lanes]), RADIUS, axis=1
            )
        return left, right

    every, few = slice(None), slice(0, LANES)

    def hide_if(border, lines):
        return jnp.where(place_ref[border] > 0, INVALID, lines)

    def mark_sides(at, upper):
        left, right = sides(at, upper, left_ref, right_ref, few)
        return hide_if(2, left), hide_if(3, right)

    def band(at, ref, ref_s, first, upper):
        merge_ends(at, *columns_of(ref_s[first : first + step]), *sides(at, upper, left_s, right_s, every))
        marks = hide_if(int(upper), ref[first : first + step])
        beside = [hide_if(int(upper), side) for side in mark_sides(at, upper)]
        merge(at, columns_of(marks), *beside, flag_s)

    for i in range(0, RADIUS, step):
        band(i, top_ref, top_s, i, False)
        band(RADIUS + rows + i, bottom_ref, bottom_s, i, True)

    def middle(i, upper):
        at = pl.multiple_of(i * step, step)
        own = at - RADIUS
        ends = [tile_of(xq_ref, c, rows, own, step) for c in (0, cols // TILE - 1)]
        merge_ends(at, *ends, *sides(at, upper, left_s, right_s, every))
        merge(at, columns_of(mark_ref[pl.ds(own, step)].astype(jnp.float32)), *mark_sides(at, upper), flag_s)
        return 0

    lax.fori_loop(RADIUS // step, half // step, lambda i, _: middle(i, False), 0)
    lax.fori_loop(half // step, (RADIUS + rows) // step, lambda i, _: middle(i, True), 0)

    first_lane = (lax.broadcasted_iota(jnp.int32, (8, LANES), 1) == 0).astype(jnp.bfloat16)
    spans = []
    for c in range(wide_cols // TILE):
        lines = flag_s[c * wide_rows * TILE : (c + 1) * wide_rows * TILE, :]
        spans.append(jnp.where(nt(first_lane, lines) > INVALID / 2, HIDDEN, 0.0))
    tall = rows // TILE
    for c in range(cols // TILE):
        for r in range(tall):
            at = slice(r * TILE * TILE, r * TILE * TILE + 2 * TILE * TILE)
            hide_ref[c * tall + r] = jnp.concatenate([spans[c][:, at], spans[c + 1][:, at]], axis=1)


def column_chunks(channels, half):
    at, end = half * 3 * channels // 2, (half + 1) * 3 * channels // 2
    chunks = []
    while at < end:
        width = min(GROUP - at % GROUP, end - at)
        chunks.append((at, at // channels, at % channels // GROUP, at % GROUP, width))
        at += width
    return chunks


def numbered_chunks(channels, half):
    number, chunks = 0, []
    for chunk in column_chunks(channels, half):
        chunks.append((number, *chunk))
        number += chunk[-1] == GROUP
    return chunks


def project_lines(source, w, parts, factor, put):
    size = source.shape[0] // parts
    for m in range(0, source.shape[0], size):
        y = nt(source[m : m + size, :], w)
        put(slice(m, m + size), (y if factor == 1 else y * factor).astype(jnp.bfloat16))


QUERY_FACTOR = HEAD_DIM ** (-0.5) * LOG2_E


def early_kernel(offsets, place_ref, *refs):
    triples, refs = refs[: len(offsets)], refs[len(offsets) :]
    xq_ref, mid_ref, whole_ref, part_ref, near = refs
    channels = near.shape[1]
    triple_rows = near.shape[0] // len(offsets)
    for j, off in enumerate(offsets):
        to = pl.multiple_of(((place_ref[ROW] ^ off) % len(offsets)) * triple_rows, 16)
        near[pl.ds(to, triple_rows), :] = triples[j][...]

    def run(half):
        for number, at, section, _, _, width in numbered_chunks(channels, half):
            w = near[at - half * near.shape[0] : at - half * near.shape[0] + width, :]

            def put(lines, value, number=number, width=width):
                if width == GROUP:
                    whole_ref[number, lines, :] = value
                else:
                    part_ref[lines, :] = value

            if section == 0:
                project_lines(xq_ref, w, 2, QUERY_FACTOR, put)
            else:
                project_lines(mid_ref, w, 2, 1, put)

    for half in range(2):
        pl.when(place_ref[HALF] == half)(functools.partial(run, half))


def project_rest(half, sections, channels, near_at, far_at, sources, put):
    xq_ref, mid_ref, outer_ref = sources
    edge, mid = outer_ref.shape[0] // 2, mid_ref.shape[0]
    for number, at, section, group, lane, width in numbered_chunks(channels, half):
        if section in sections and section > 0:
            w = near_at(at, width)
            for first, to in ((0, 0), (edge, edge + mid)):
                put(section, group, lane, width, slice(to, to + edge), nt(outer_ref[first : first + edge, :], w).astype(jnp.bfloat16))
    for at, section, group, lane, width in column_chunks(channels, 1 - half):
        if section not in sections:
            continue
        w = far_at(at, width)
        if section == 0:
            project_lines(xq_ref, w, 2, QUERY_FACTOR, functools.partial(put, section, group, lane, width))
            continue
        for first, to in ((0, 0), (edge, edge + mid)):
            put(section, group, lane, width, slice(to, to + edge), nt(outer_ref[first : first + edge, :], w).astype(jnp.bfloat16))

        def put_mid(lines, value, section=section, group=group, lane=lane, width=width):
            put(section, group, lane, width, slice(edge + lines.start, edge + lines.stop), value)

        project_lines(mid_ref, w, 2, 1, put_mid)


def late_kernel(pieces, triple_rows, place_ref, *refs):
    sources, refs = refs[: len(pieces)], refs[len(pieces) :]
    near, whole_ref, part_ref, xq_ref, mid_ref, outer_ref, q_s, k_s, wt, near_sem = refs
    channels = wt.shape[1]
    edge, mid = outer_ref.shape[0] // 2, mid_ref.shape[0]
    for j, (off, start) in enumerate(pieces):
        to = pl.multiple_of((place_ref[ROW] ^ off) * triple_rows + place_ref[STARTS + start], 16)
        wt[pl.ds(to, sources[j].shape[0]), :] = sources[j][...]
    to = pl.multiple_of(place_ref[HALF] * near.shape[0], 16)
    near_copy = pltpu.make_async_copy(near, wt.at[pl.ds(to, near.shape[0]), :], near_sem)
    near_copy.start()

    def put(section, group, lane, width, lines, value):
        if section == 0:
            q_s[group, lines, :] = value
        else:
            k_s[group, lines, lane : lane + width] = value

    def run(half):
        for number, at, section, group, lane, width in numbered_chunks(channels, half):
            if section == 0:
                q_s[group] = whole_ref[number]
            elif section == 1 and width == GROUP:
                k_s[group, edge : edge + mid, :] = whole_ref[number, :mid, :]
            elif section == 1:
                k_s[group, edge : edge + mid, lane : lane + width] = part_ref[...]
        base = half * near.shape[0]
        project_rest(
            half, (0, 1), channels, lambda at, width: near[at - base : at - base + width, :], lambda at, width: wt[at : at + width, :],
            (xq_ref, mid_ref, outer_ref), put,
        )

    for half in range(2):
        pl.when(place_ref[HALF] == half)(functools.partial(run, half))
    near_copy.wait()


def value_kernel(place_ref, wt, whole_ref, mid_ref, outer_ref, v_s):
    channels = wt.shape[1]
    edge, mid = outer_ref.shape[0] // 2, mid_ref.shape[0]

    def put(section, group, lane, width, lines, value):
        v_s[group, lines, lane : lane + width] = value

    def run(half):
        for number, at, section, group, lane, width in numbered_chunks(channels, half):
            if section == 2:
                v_s[group, edge : edge + mid, :] = whole_ref[number, :mid, :]
        weights = lambda at, width: wt[at : at + width, :]
        project_rest(half, (2,), channels, weights, weights, (None, mid_ref, outer_ref), put)

    for half in range(2):
        pl.when(place_ref[HALF] == half)(functools.partial(run, half))


def carrier_kernel(offsets, place_ref, wt, *refs):
    shards = len(offsets)
    parts, finals, refs = refs[:shards], refs[shards : 2 * shards], refs[2 * shards :]
    summary_ref, wo, kce, vc_s = refs
    per_row = summary_ref.shape[1]
    channels = wt.shape[1]
    groups = channels // GROUP
    heads = channels // HEAD_DIM
    factor = HEAD_DIM ** (-0.5)
    carriers_here = vc_s.shape[0]
    final_rows = wo.shape[0] // shards
    for j, off in enumerate(offsets):
        to = pl.multiple_of((place_ref[ROW] ^ off) * final_rows, 16)
        wo[pl.ds(to, final_rows), :] = finals[j][...]
    carriers = jnp.concatenate([part[...].astype(jnp.float32) for part in parts], axis=0)
    own = carriers[:carriers_here]
    carriers = layer_normalise(carriers).astype(jnp.bfloat16)
    own_norm = layer_normalise(own).astype(jnp.bfloat16)
    qc = (nt(own_norm, wt[:channels, :]) * factor).astype(jnp.bfloat16).astype(jnp.float32)
    kc = nt(carriers, wt[channels : 2 * channels, :]).astype(jnp.bfloat16)
    vc = nt(carriers, wt[2 * channels :, :]).astype(jnp.bfloat16)
    head_of = lax.broadcasted_iota(jnp.int32, (1, channels), 1) // HEAD_DIM
    stacked = jnp.concatenate([jnp.where(head_of == h, qc, 0.0) for h in range(heads)], axis=0)
    e = jnp.exp(nt(stacked.astype(jnp.bfloat16), kc))
    weights = (e / jnp.sum(e, axis=-1, keepdims=True)).astype(jnp.bfloat16)
    o = nn(weights, vc)
    mix = jnp.zeros((carriers_here, channels), jnp.float32)
    for h in range(heads):
        mix = jnp.where(head_of == h, o[h * carriers_here : (h + 1) * carriers_here, :], mix)
    renewed = own + nt(mix.astype(jnp.bfloat16), wo[...])
    for i in range(summary_ref.shape[0]):
        summary_ref[i] = renewed[i * per_row : (i + 1) * per_row, :].astype(jnp.bfloat16)
    fresh = nt(layer_normalise(renewed).astype(jnp.bfloat16), wt[channels:, :]).astype(jnp.bfloat16).astype(jnp.float32)
    vc_s[...] = fresh[:, channels:]
    same = (
        lax.broadcasted_iota(jnp.int32, (GROUP, GROUP), 0) // HEAD_DIM
        == lax.broadcasted_iota(jnp.int32, (GROUP, GROUP), 1) // HEAD_DIM
    )
    windows = kce.shape[0] // groups
    for w in range(windows):
        for g in range(groups):
            kce[w * groups + g] = jnp.where(same, fresh[w : w + 1, g * GROUP : (g + 1) * GROUP], 0.0).astype(jnp.bfloat16)


def attend_kernel(tall, broad, q_s, k_s, v_s, hide_ref, kce, vc_s, mix_s, pc_s, even_s, odd_s):
    groups, tiles = q_s.shape[0], hide_ref.shape[0]
    heads_in = GROUP // HEAD_DIM
    queries, span = TILE * TILE, 2 * TILE * TILE
    side = PATCH_SIDE // TILE
    wide = (tall + 1) * queries
    qi = lax.broadcasted_iota(jnp.int32, (queries, 2 * span), 0)
    ki = lax.broadcasted_iota(jnp.int32, (queries, 2 * span), 1)
    row_step = (ki % span) // TILE - qi // TILE
    col_step = (ki // span) * TILE + ki % TILE - qi % TILE
    seen = (row_step >= 0) & (row_step <= 2 * RADIUS) & (col_step >= 0) & (col_step <= 2 * RADIUS)
    band = jnp.where(seen, 0.0, HIDDEN)
    group_head = lax.broadcasted_iota(jnp.int32, (1, GROUP), 1) // HEAD_DIM
    only = [jnp.where(group_head == h, 1.0, 0.0).astype(jnp.bfloat16) for h in range(heads_in)]
    in_pair = LANES // HEAD_DIM
    pair_head = lax.broadcasted_iota(jnp.int32, (1, LANES), 1) // HEAD_DIM

    for c in range(broad):
        for w in range(tall // side):
            at = slice((c * tall + w * side) * queries, (c * tall + (w + 1) * side) * queries)
            window = w * (broad // side) + c // side
            for g in range(groups):
                pc_s[at, g * GROUP : (g + 1) * GROUP] = jnp.exp2(nt(q_s[g, at, :], kce[window * groups + g]))

    def keys_at(t):
        k0 = pl.multiple_of(t // tall * wide + t % tall * queries, queries)
        return k0, pl.multiple_of(k0 + wide, queries)

    def scores(t, ref):
        q_at = pl.multiple_of(t * queries, queries)
        k0, k1 = keys_at(t)
        for g in range(groups):
            q = q_s[g, pl.ds(q_at, queries), :]
            qq = jnp.concatenate([q * mask for mask in only], axis=0)
            k = jnp.concatenate([k_s[g, pl.ds(k0, span), :], k_s[g, pl.ds(k1, span), :]], axis=0)
            ref[g] = nt(qq, k)

    def finish(t, ref):
        q_at = pl.multiple_of(t * queries, queries)
        k0, k1 = keys_at(t)
        window = t % tall // side * (broad // side) + t // tall // side
        bias = band + hide_ref[t][0:1, :]
        for g in range(groups):
            p = jnp.exp2(ref[g].reshape(heads_in, queries, 2 * span) + bias[None])
            total = jnp.sum(p, axis=-1, keepdims=True)
            v = jnp.concatenate([v_s[g, pl.ds(k0, span), :], v_s[g, pl.ds(k1, span), :]], axis=0)
            o = nn(p.reshape(heads_in * queries, 2 * span).astype(jnp.bfloat16), v).reshape(heads_in, queries, GROUP)
            v_new = vc_s[pl.ds(window, 1), g * GROUP : (g + 1) * GROUP]
            for j in range(GROUP // LANES):
                lanes = slice(j * LANES, (j + 1) * LANES)
                at = slice(g * GROUP + j * LANES, g * GROUP + (j + 1) * LANES)
                kept, kept_total = o[j * in_pair, :, lanes], total[j * in_pair]
                for h in range(1, in_pair):
                    kept = jnp.where(pair_head == h, o[j * in_pair + h, :, lanes], kept)
                    kept_total = jnp.where(pair_head == h, total[j * in_pair + h], kept_total)
                new = pc_s[pl.ds(q_at, queries), at]
                mixed = (kept + new * v_new[:, lanes]) / (kept_total + new)
                mix_s[pl.ds(q_at, queries), at] = mixed.astype(jnp.bfloat16)

    scores(0, even_s)

    def two(i, _):
        t = 2 * i
        scores(t + 1, odd_s)
        finish(t, even_s)
        scores(jnp.minimum(t + 2, tiles - 1), even_s)
        finish(t + 1, odd_s)
        return 0

    lax.fori_loop(0, tiles // 2, two, 0)


def out_kernel(x_ref, mix_s, wo, out_hbm, out_ref, out_sems):
    rows, cols, channels = x_ref.shape
    going = []
    for pair in range(cols // (2 * TILE)):
        both = slice(2 * pair * TILE, 2 * (pair + 1) * TILE)
        for g in range(channels // GROUP):
            at = slice(g * GROUP, (g + 1) * GROUP)
            w = wo[at, :]
            y = nt(mix_s[2 * pair * rows * TILE : 2 * (pair + 1) * rows * TILE, :], w).reshape(2, rows, TILE, GROUP)
            y = jnp.concatenate([y[0], y[1]], axis=1) + x_ref[:, both, at].astype(jnp.float32)
            out_ref[pair, :, :, at] = y.astype(jnp.bfloat16)
        copy = pltpu.make_async_copy(out_ref.at[pair], out_hbm.at[:, both, :], out_sems.at[pair])
        copy.start()
        going.append(copy)
    for copy in going:
        copy.wait()


def local(grid_elements, summary_vectors, triple_projection, final_projection, genuine_flags):
    rows, cols, channels = grid_elements.shape
    wide_rows, wide_cols = rows + 2 * RADIUS, cols + 2 * RADIUS

    triple_t, final_t = triple_projection.T, final_projection.T
    vmem = pl.BlockSpec(memory_space=pltpu.VMEM)
    anywhere = pl.BlockSpec(memory_space=pl.ANY)
    scalars = pl.BlockSpec(memory_space=pltpu.SMEM)
    hbm = pl.BlockSpec(memory_space=pltpu.HBM)
    small = pltpu.CompilerParams(vmem_limit_bytes=8 * 1024 * 1024)
    row_strip = jax.ShapeDtypeStruct((RADIUS, cols, channels), jnp.bfloat16)
    col_strip = jax.ShapeDtypeStruct((wide_rows // 2, 2 * RADIUS, channels), jnp.bfloat16)

    row, col, img = lax.axis_size("row"), lax.axis_size("col"), lax.axis_size("img")
    row_at, col_at, img_at = lax.axis_index("row"), lax.axis_index("col"), lax.axis_index("img")
    row_bits = bits_of(row)
    far, rest = row_bits[0], row_bits[1:]
    piece_rows = triple_t.shape[0] * 5 // (8 * img) // 16 * 16
    relays = img if piece_rows else 0
    starts = [(img_at - k) % img for k in range(relays)] + [jnp.int32(relays)]
    place = [row_at == 0, row_at == row - 1, col_at == 0, col_at == col - 1, row_at % 2 == 0, col_at % 2 == 0, row_at, row_at // far]
    place = jnp.stack([jnp.asarray(p).astype(jnp.int32) for p in place + [start * piece_rows for start in starts]])

    mark, even_rows, odd_rows, x = pl.pallas_call(
        edge_kernel,
        out_shape=(
            pltpu.VMEM((rows, cols, LANES), jnp.bfloat16),
            pltpu.VMEM(row_strip.shape, jnp.bfloat16),
            pltpu.VMEM(row_strip.shape, jnp.bfloat16),
            pltpu.VMEM(grid_elements.shape, jnp.bfloat16),
        ),
        in_specs=[scalars, hbm, hbm],
        out_specs=(vmem,) * 4,
        scratch_shapes=[
            pltpu.VMEM((rows, cols), jnp.int32),
            pltpu.VMEM((rows * cols, cols), jnp.bfloat16),
            pltpu.SemaphoreType.DMA((2,)),
        ],
        compiler_params=small,
        cost_estimate=pl.CostEstimate(flops=1_000_000, bytes_accessed=1_000_000, transcendentals=0),
        name="edge_rows",
    )(place, *(pltpu.with_memory_space_constraint(a, pltpu.HBM) for a in (genuine_flags, grid_elements)))
    mine, last = pl.pallas_call(
        piece_kernel,
        out_shape=(
            pltpu.VMEM((max(piece_rows, 16), channels), jnp.bfloat16),
            pltpu.VMEM((triple_t.shape[0] - relays * piece_rows, channels), jnp.bfloat16),
        ),
        in_specs=[scalars, hbm],
        out_specs=(vmem, vmem),
        scratch_shapes=[pltpu.SemaphoreType.DMA((2,))],
        compiler_params=small,
        cost_estimate=pl.CostEstimate(flops=1_000_000, bytes_accessed=1_000_000, transcendentals=0),
        name="pieces",
    )(place, pltpu.with_memory_space_constraint(after(triple_t, even_rows), pltpu.HBM))
    xq = pl.pallas_call(
        own_kernel,
        out_shape=pltpu.VMEM((rows * cols, channels), jnp.bfloat16),
        in_specs=[vmem],
        out_specs=vmem,
        compiler_params=small,
        cost_estimate=pl.CostEstimate(flops=1_000_000, bytes_accessed=1_000_000, transcendentals=0),
        name="own_norm",
    )(x)
    even_rows, odd_rows = pair_swapped(even_rows, odd_rows, "row")

    far_pieces = []
    if relays:
        first = swapped(mine, "row", far)
    far_last = swapped(after(last, even_rows, odd_rows), "row", far)

    own_rows = summary_vectors.shape[0] * summary_vectors.shape[1]
    carrier_tiles = -(-own_rows // TILE)
    even_cols, odd_cols = pl.pallas_call(
        strip_kernel,
        out_shape=(
            pltpu.VMEM((col_strip.shape[0] + carrier_tiles, *col_strip.shape[1:]), jnp.bfloat16),
            pltpu.VMEM(col_strip.shape, jnp.bfloat16),
        ),
        in_specs=[scalars] + [vmem] * 5,
        out_specs=(vmem,) * 2,
        scratch_shapes=[pltpu.VMEM((carrier_tiles * TILE, channels), jnp.float32)],
        compiler_params=small,
        cost_estimate=pl.CostEstimate(flops=1_000_000, bytes_accessed=2_000_000, transcendentals=0),
        name="edge_columns",
    )(place, x, after(mark, xq), even_rows, odd_rows, summary_vectors)
    even_cols, odd_cols = pair_swapped(even_cols, odd_cols, "col")
    groups = channels // GROUP
    triples, offsets = [triple_t], [0]
    for bit in rest:
        triples = triples + [swapped(p, "row", bit) for p in triples]
        offsets = offsets + [o ^ bit for o in offsets]
    mid = pl.pallas_call(
        middle_kernel,
        out_shape=pltpu.VMEM(((wide_cols // TILE - 2) * wide_rows * TILE, channels), jnp.bfloat16),
        in_specs=[scalars] + [vmem] * 3,
        out_specs=vmem,
        scratch_shapes=[pltpu.VMEM(row_strip.shape, jnp.float32)] * 2,
        compiler_params=small,
        cost_estimate=pl.CostEstimate(flops=1_000_000, bytes_accessed=1_000_000, transcendentals=0),
        name="middle_blocks",
    )(place, xq, even_rows, odd_rows)
    whole, part, near = pl.pallas_call(
        functools.partial(early_kernel, offsets),
        out_shape=(
            pltpu.VMEM((3 * groups // 2, rows * cols, GROUP), jnp.bfloat16),
            pltpu.VMEM((mid.shape[0], GROUP // 2), jnp.bfloat16),
            pltpu.VMEM((3 * channels // 2, channels), jnp.bfloat16),
        ),
        in_specs=[scalars] + [vmem] * (len(triples) + 2),
        out_specs=(vmem,) * 3,
        compiler_params=pltpu.CompilerParams(vmem_limit_bytes=16 * 1024 * 1024),
        cost_estimate=pl.CostEstimate(flops=1_000_000, bytes_accessed=1_000_000, transcendentals=0),
        name="project_early",
    )(place, *triples, xq, mid)

    carriers = pl.pallas_call(
        carrier_pair_kernel,
        out_shape=pltpu.VMEM((2 * own_rows, channels), jnp.bfloat16),
        in_specs=[vmem, anywhere],
        out_specs=vmem,
        scratch_shapes=[
            pltpu.VMEM((carrier_tiles, TILE, channels), jnp.bfloat16),
            pltpu.VMEM((2 * own_rows, channels), jnp.float32),
            pltpu.SemaphoreType.DMA,
        ],
        compiler_params=small,
        cost_estimate=pl.CostEstimate(flops=1_000, bytes_accessed=1_000, transcendentals=0),
        name="carrier_pair",
    )(summary_vectors, after(even_cols, near))
    parts = [carriers]
    for bit in bits_of(col)[:-1]:
        carriers = carriers if len(parts) == 1 else jnp.concatenate(parts, axis=0)
        got = swapped(carriers, "col", 2 * bit - 1)
        parts.append(got)
    if relays:
        first = after(first, even_cols, odd_cols, parts[0])
        others = [lax.ppermute(first, "img", [(i, (i + k) % img) for i in range(img)]) for k in range(1, relays)]
        far_pieces = [first] + others
    far_pieces.append(far_last)

    tiles = (rows // TILE) * (cols // TILE)
    keys = 4 * TILE * TILE
    outer, hide = pl.pallas_call(
        outer_kernel,
        out_shape=(
            pltpu.VMEM((2 * wide_rows * TILE, channels), jnp.bfloat16),
            pltpu.VMEM((tiles, 8, keys), jnp.float32),
        ),
        in_specs=[scalars] + [vmem] * 6,
        out_specs=(vmem,) * 2,
        scratch_shapes=[
            *[pltpu.VMEM((RADIUS, 2 * TILE, channels), jnp.float32)] * 2,
            *[pltpu.VMEM(col_strip.shape, jnp.float32)] * 2,
            *[pltpu.VMEM((*shape.shape[:2], LANES), jnp.float32) for shape in (row_strip, row_strip, col_strip, col_strip)],
            pltpu.VMEM((wide_rows * wide_cols, LANES), jnp.bfloat16),
        ],
        compiler_params=pltpu.CompilerParams(vmem_limit_bytes=12 * 1024 * 1024),
        cost_estimate=pl.CostEstimate(flops=10_000_000, bytes_accessed=6_000_000, transcendentals=1000),
        name="outer_blocks",
    )(place, xq, mark, even_rows, odd_rows, even_cols, odd_cols)

    row_carriers = pl.pallas_call(
        join_kernel,
        out_shape=pltpu.VMEM((col * own_rows, channels), jnp.bfloat16),
        in_specs=[vmem] * len(parts),
        out_specs=vmem,
        compiler_params=small,
        cost_estimate=pl.CostEstimate(flops=1_000, bytes_accessed=1_000, transcendentals=0),
        name="join_carriers",
    )(*parts[:-1], after(parts[-1], outer))
    finals, carriers = [final_t], [row_carriers]
    for bit in rest:
        finals = finals + [swapped(p, "row", bit) for p in finals]
    for bit in row_bits:
        carriers = carriers + [swapped(p, "row", bit) for p in carriers]

    far_final = swapped(after(final_t, even_cols, odd_cols), "row", far)

    far_offsets = [far]
    far_pieces = [[after(piece, outer, got)] for piece in far_pieces]
    for bit in rest:
        far_pieces = [same + [swapped(p, "row", bit) for p in same] for same in far_pieces]
        far_offsets = far_offsets + [o ^ bit for o in far_offsets]

    numbered = [(off, number) for number in range(len(far_pieces)) for off in far_offsets]
    sources = [piece for same in far_pieces for piece in same]
    q, k, wt = pl.pallas_call(
        functools.partial(late_kernel, numbered, triple_t.shape[0]),
        out_shape=(
            jax.ShapeDtypeStruct((groups, rows * cols, GROUP), jnp.bfloat16),
            jax.ShapeDtypeStruct((groups, wide_rows * wide_cols, GROUP), jnp.bfloat16),
            jax.ShapeDtypeStruct((3 * channels, channels), jnp.bfloat16),
        ),
        in_specs=[scalars] + [vmem] * (len(sources) + 6),
        out_specs=(vmem,) * 3,
        scratch_shapes=[pltpu.SemaphoreType.DMA],
        compiler_params=pltpu.CompilerParams(vmem_limit_bytes=VMEM_BYTES),
        cost_estimate=pl.CostEstimate(flops=1_000_000, bytes_accessed=1_000_000, transcendentals=0),
        name="project_late",
    )(place, *sources, near, whole, part, xq, mid, outer)

    v = pl.pallas_call(
        value_kernel,
        out_shape=jax.ShapeDtypeStruct((groups, wide_rows * wide_cols, GROUP), jnp.bfloat16),
        in_specs=[scalars] + [vmem] * 4,
        out_specs=vmem,
        compiler_params=pltpu.CompilerParams(vmem_limit_bytes=VMEM_BYTES),
        cost_estimate=pl.CostEstimate(flops=3_000_000_000, bytes_accessed=7_000_000, transcendentals=0),
        name="values",
    )(place, wt, whole, mid, outer)

    far_finals = [after(far_final, q)]
    for bit in rest:
        far_finals = far_finals + [swapped(p, "row", bit) for p in far_finals]
    finals, offsets = finals + far_finals, offsets + far_offsets
    carriers_here = carrier_tiles * TILE
    summary_result, wo, kce, vc = pl.pallas_call(
        functools.partial(carrier_kernel, offsets),
        out_shape=(
            jax.ShapeDtypeStruct(summary_vectors.shape, jnp.bfloat16),
            jax.ShapeDtypeStruct((channels, channels), jnp.bfloat16),
            jax.ShapeDtypeStruct((own_rows * groups, GROUP, GROUP), jnp.bfloat16),
            jax.ShapeDtypeStruct((carriers_here, channels), jnp.float32),
        ),
        in_specs=[scalars] + [vmem] * (1 + len(carriers) + len(finals)),
        out_specs=(vmem,) * 4,
        compiler_params=pltpu.CompilerParams(vmem_limit_bytes=VMEM_BYTES),
        cost_estimate=pl.CostEstimate(flops=500_000_000, bytes_accessed=5_000_000, transcendentals=10_000),
        name="carriers",
    )(place, wt, *carriers, *finals)

    scores = (groups, GROUP // HEAD_DIM * TILE * TILE, keys)
    mix = pl.pallas_call(
        functools.partial(attend_kernel, rows // TILE, cols // TILE),
        out_shape=jax.ShapeDtypeStruct((rows * cols, channels), jnp.bfloat16),
        in_specs=[vmem] * 6,
        out_specs=vmem,
        scratch_shapes=[
            pltpu.VMEM((rows * cols, channels), jnp.float32),
            pltpu.VMEM(scores, jnp.float32),
            pltpu.VMEM(scores, jnp.float32),
        ],
        compiler_params=pltpu.CompilerParams(vmem_limit_bytes=VMEM_BYTES),
        cost_estimate=pl.CostEstimate(flops=4_000_000_000, bytes_accessed=12_000_000, transcendentals=4_000_000),
        name="attend",
    )(q, k, v, hide, kce, vc)

    out = pl.pallas_call(
        out_kernel,
        out_shape=jax.ShapeDtypeStruct(grid_elements.shape, jnp.bfloat16),
        in_specs=[vmem] * 3,
        out_specs=anywhere,
        scratch_shapes=[
            pltpu.VMEM((cols // (2 * TILE), rows, 2 * TILE, channels), jnp.bfloat16),
            pltpu.SemaphoreType.DMA((cols // (2 * TILE),)),
        ],
        compiler_params=pltpu.CompilerParams(vmem_limit_bytes=VMEM_BYTES),
        cost_estimate=pl.CostEstimate(flops=1_200_000_000, bytes_accessed=6_000_000, transcendentals=0),
        name="out",
    )(x, mix, wo)
    return (out, summary_result)


def solution(mesh):
    placed = (
        P(("img", "row"), "col", None),
        P(("img", "row"), "col", None),
        P(None, "row"),
        P(None, "row"),
        P(("img", "row"), "col"),
    )
    return jax.shard_map(
        local,
        mesh=mesh,
        in_specs=placed,
        out_specs=(P(("img", "row"), "col", None), P(("img", "row"), "col", None)),
        check_vma=False,
    )
```

```python
import functools

import jax
import jax.numpy as jnp
from jax import lax
from jax.experimental import pallas as pl
from jax.experimental.pallas import tpu as pltpu
from jax.sharding import PartitionSpec as P

HEAD_DIM = 64
PATCH_SIDE = 16
RADIUS = 4
TILE = 2 * RADIUS
LANES = 128
GROUP = 256
INVALID = 100.0
HIDDEN = -1e30
LOG2_E = 1.4426950408889634
EVEN_ROW, EVEN_COL, ROW, HALF, STARTS = 4, 5, 6, 7, 8
VMEM_BYTES = 26 * 1024 * 1024


def nt(a, b):
    return lax.dot_general(a, b, (((1,), (1,)), ((), ())), preferred_element_type=jnp.float32)


def nn(a, b):
    return lax.dot_general(a, b, (((1,), (0,)), ((), ())), preferred_element_type=jnp.float32)


def layer_normalise(lines):
    center = lines - jnp.mean(lines, axis=-1, keepdims=True)
    spread = jnp.mean(center * center, axis=-1, keepdims=True)
    return center * lax.rsqrt(spread + 1e-05)


def pair_swapped(even_block, odd_block, axis):
    count = lax.axis_size(axis)
    got = []
    for first, block in ((0, even_block), (1, odd_block)):
        pairs = [(i, i + 1) for i in range(first, count - 1, 2)]
        got.append(lax.ppermute(block, axis, pairs + [(b, a) for a, b in pairs]))
    return got


def swapped(block, axis, bit):
    count = lax.axis_size(axis)
    return lax.ppermute(block, axis, [(i, i ^ bit) for i in range(count)])


def after(block, *others):
    return lax.optimization_barrier((block, *others))[0]


def bits_of(count):
    bits, bit = [], count // 2
    while bit:
        bits.append(bit)
        bit //= 2
    return bits


def marked_lanes(lines, hidden):
    first = jnp.where(hidden, INVALID, lines[:, :, :LANES])
    return jnp.concatenate([first, lines[:, :, LANES:]], axis=2)


def edge_kernel(place_ref, flags_hbm, x_hbm, mark_ref, even_ref, odd_ref, x_ref, *scratch):
    flags_ref, spread, sems = scratch
    rows, cols = flags_ref.shape
    flags_copy = pltpu.make_async_copy(flags_hbm, flags_ref, sems.at[0])
    x_copy = pltpu.make_async_copy(x_hbm, x_ref, sems.at[1])
    flags_copy.start()
    x_copy.start()
    flags_copy.wait()
    row_at = lax.broadcasted_iota(jnp.int32, (cols, cols), 0)
    diagonal = row_at == lax.broadcasted_iota(jnp.int32, (cols, cols), 1)
    for r in range(rows):
        hidden = jnp.where(flags_ref[r : r + 1, :] > 0, 0.0, INVALID)
        spread[r * cols : (r + 1) * cols, :] = jnp.where(diagonal, hidden, 0.0).astype(jnp.bfloat16)
    marks = nn(spread[...], jnp.ones((cols, LANES), jnp.bfloat16)).reshape(rows, cols, LANES)
    mark_ref[...] = marks.astype(jnp.bfloat16)
    x_copy.wait()
    first, last = [
        marked_lanes(x_ref[at].astype(jnp.float32), marks[at] > INVALID / 2)
        for at in (slice(0, RADIUS), slice(rows - RADIUS, rows))
    ]
    even = place_ref[EVEN_ROW] > 0
    even_ref[...] = jnp.where(even, last, first).astype(jnp.bfloat16)
    odd_ref[...] = jnp.where(even, first, last).astype(jnp.bfloat16)


def piece_kernel(place_ref, triple_hbm, mine_ref, last_ref, sems):
    start = pl.multiple_of(place_ref[STARTS], 16)
    last = triple_hbm.shape[0] - last_ref.shape[0]
    copies = [
        pltpu.make_async_copy(triple_hbm.at[pl.ds(start, mine_ref.shape[0]), :], mine_ref, sems.at[0]),
        pltpu.make_async_copy(triple_hbm.at[last:, :], last_ref, sems.at[1]),
    ]
    for copy in copies:
        copy.start()
    for copy in copies:
        copy.wait()


def strip_kernel(place_ref, x_ref, mark_ref, even_rows_ref, odd_rows_ref, carriers_ref, even_ref, odd_ref, carriers_s):
    per_row = carriers_ref.shape[1]
    carriers_s[...] = jnp.zeros_like(carriers_s)
    for i in range(carriers_ref.shape[0]):
        carriers_s[i * per_row : (i + 1) * per_row, :] = carriers_ref[i].astype(jnp.float32)
    for i in range(carriers_s.shape[0] // TILE):
        even_ref[odd_ref.shape[0] + i] = carriers_s[i * TILE : (i + 1) * TILE, :].astype(jnp.bfloat16)
    rows, cols, channels = x_ref.shape
    middle = rows // 2
    low = lax.broadcasted_iota(jnp.int32, (1, TILE, 1), 1) < RADIUS
    even_row, even_col = place_ref[EVEN_ROW] > 0, place_ref[EVEN_COL] > 0
    for lane in range(0, channels, LANES):
        lanes = slice(lane, lane + LANES)
        strips = []
        for columns, last in ((slice(0, TILE), False), (slice(cols - TILE, cols), True)):

            def own(part):
                lines = x_ref[part, columns, lanes].astype(jnp.float32)
                if lane == 0:
                    lines = jnp.where(mark_ref[part, columns, :].astype(jnp.float32) > INVALID / 2, INVALID, lines)
                return lines

            even_rows = even_rows_ref[:, columns, lanes].astype(jnp.float32)
            odd_rows = odd_rows_ref[:, columns, lanes].astype(jnp.float32)
            top, bottom = jnp.where(even_row, odd_rows, even_rows), jnp.where(even_row, even_rows, odd_rows)
            upper = jnp.concatenate([top, own(slice(0, middle))], axis=0)
            lower = jnp.concatenate([own(slice(middle, rows)), bottom], axis=0)
            if last:
                upper = jnp.roll(upper, RADIUS, axis=1)
            else:
                lower = jnp.roll(lower, RADIUS, axis=1)
            strips.append(jnp.where(low, upper, lower))
        first, last = strips
        even_ref[: odd_ref.shape[0], :, lanes] = jnp.where(even_col, last, first).astype(jnp.bfloat16)
        odd_ref[:, :, lanes] = jnp.where(even_col, first, last).astype(jnp.bfloat16)


def carrier_pair_kernel(own_ref, got_hbm, out_ref, got_s, pair_s, sem):
    per_row, here = own_ref.shape[1], own_ref.shape[0] * own_ref.shape[1]
    tiles = got_s.shape[0]
    copy = pltpu.make_async_copy(got_hbm.at[got_hbm.shape[0] - tiles :], got_s, sem)
    copy.start()
    for i in range(own_ref.shape[0]):
        pair_s[i * per_row : (i + 1) * per_row, :] = own_ref[i].astype(jnp.float32)
    copy.wait()
    pair_s[here:, :] = got_s[...].astype(jnp.float32).reshape(tiles * TILE, -1)[:here]
    out_ref[...] = pair_s[...].astype(jnp.bfloat16)


def pack_kernel(final_ref, *refs):
    parts, out_ref = refs[:-1], refs[-1]
    rows = final_ref.shape[0]
    out_ref[:rows, :] = final_ref[...]
    carriers = jnp.concatenate([part[...].astype(jnp.float32) for part in parts], axis=0)
    out_ref[rows:, :] = carriers.astype(jnp.bfloat16)


def own_kernel(x_ref, xq_ref):
    rows, cols, _ = x_ref.shape
    step = 4

    def own(i, _):
        at = pl.multiple_of(i * step, step)
        y = layer_normalise(x_ref[pl.ds(at, step)].astype(jnp.float32))
        for c in range(cols // TILE):
            piece = y[:, c * TILE : (c + 1) * TILE, :].reshape(step * TILE, -1)
            to = pl.multiple_of(c * rows * TILE + at * TILE, step * TILE)
            xq_ref[pl.ds(to, step * TILE), :] = piece.astype(jnp.bfloat16)
        return 0

    lax.fori_loop(0, rows // step, own, 0)


def columns_of(lines):
    return [lines[:, c : c + TILE, :] for c in range(0, lines.shape[1], TILE)]


def tile_of(xq_ref, column, rows, at, step):
    first = pl.multiple_of(column * rows * TILE + at * TILE, step * TILE)
    return xq_ref[pl.ds(first, step * TILE), :].astype(jnp.float32).reshape(step, TILE, -1)


def store_lines(ref, block, wide_rows, at, lines):
    size = lines.shape[0] * TILE
    to = block * wide_rows * TILE + at * TILE
    to = to if isinstance(to, int) else pl.multiple_of(to, size)
    ref[pl.ds(to, size), :] = lines.reshape(size, -1).astype(jnp.bfloat16)


def middle_kernel(place_ref, xq_ref, even_rows_ref, odd_rows_ref, mid_ref, top_s, bottom_s):
    cols = even_rows_ref.shape[1]
    rows, step = xq_ref.shape[0] // cols, 2
    wide_rows = rows + 2 * RADIUS
    flip = place_ref[EVEN_ROW] > 0
    for i in range(0, RADIUS, step):
        a, b = even_rows_ref[i : i + step].astype(jnp.float32), odd_rows_ref[i : i + step].astype(jnp.float32)
        top_s[i : i + step] = layer_normalise(jnp.where(flip, b, a))
        bottom_s[i : i + step] = layer_normalise(jnp.where(flip, a, b))
    low = lax.broadcasted_iota(jnp.int32, (1, TILE, 1), 1) < RADIUS

    def merge(at, blocks):
        moved = [jnp.roll(block, RADIUS, axis=1) for block in blocks]
        for c in range(1, len(blocks)):
            store_lines(mid_ref, c - 1, wide_rows, at, jnp.where(low, moved[c - 1], moved[c]))

    for i in range(0, RADIUS, step):
        merge(i, columns_of(top_s[i : i + step]))
        merge(RADIUS + rows + i, columns_of(bottom_s[i : i + step]))

    def middle(i, _):
        at = pl.multiple_of(i * step, step)
        merge(RADIUS + at, [tile_of(xq_ref, c, rows, at, step) for c in range(cols // TILE)])
        return 0

    lax.fori_loop(0, rows // step, middle, 0)


def outer_kernel(place_ref, xq_ref, mark_ref, even_rows_ref, odd_rows_ref, even_cols_ref, odd_cols_ref, outer_ref, hide_ref, *scratch):
    rows, cols, _ = mark_ref.shape
    wide_rows, wide_cols = rows + 2 * RADIUS, cols + 2 * RADIUS
    half = wide_rows // 2
    step = 2
    top_s, bottom_s, left_s, right_s, top_ref, bottom_ref, left_ref, right_ref, flag_s = scratch
    flip = place_ref[EVEN_ROW] > 0
    a, b = even_rows_ref[...].astype(jnp.float32), odd_rows_ref[...].astype(jnp.float32)
    for lines, out, flags in ((jnp.where(flip, b, a), top_s, top_ref), (jnp.where(flip, a, b), bottom_s, bottom_ref)):
        ends = jnp.concatenate([lines[:, :TILE, :], lines[:, cols - TILE :, :]], axis=1)
        out[...] = layer_normalise(ends)
        flags[...] = lines[:, :, :LANES]
    flip = place_ref[EVEN_COL] > 0
    size = 5
    for i in range(0, odd_cols_ref.shape[0], size):
        a, b = even_cols_ref[i : i + size].astype(jnp.float32), odd_cols_ref[i : i + size].astype(jnp.float32)
        for lines, out, flags in ((jnp.where(flip, b, a), left_s, left_ref), (jnp.where(flip, a, b), right_s, right_ref)):
            out[i : i + size] = layer_normalise(lines)
            flags[i : i + size] = lines[:, :, :LANES]
    low = lax.broadcasted_iota(jnp.int32, (1, TILE, 1), 1) < RADIUS

    def lines_of(ref):
        return ref.astype(jnp.float32)

    def merge(at, blocks, left, right, to_ref):
        moved = [left] + [jnp.roll(block, RADIUS, axis=1) for block in blocks] + [right]
        for c in range(len(blocks) + 1):
            store_lines(to_ref, c, wide_rows, at, jnp.where(low, moved[c], moved[c + 1]))

    def merge_ends(at, first, last, left, right):
        store_lines(outer_ref, 0, wide_rows, at, jnp.where(low, left, jnp.roll(first, RADIUS, axis=1)))
        store_lines(outer_ref, 1, wide_rows, at, jnp.where(low, jnp.roll(last, RADIUS, axis=1), right))

    def sides(at, upper, left_ref, right_ref, lanes):
        if upper:
            at = at - half
            left, right = jnp.roll(lines_of(left_ref[pl.ds(at, step), :, lanes]), RADIUS, axis=1), lines_of(
                right_ref[pl.ds(at, step), :, lanes]
            )
        else:
            left, right = lines_of(left_ref[pl.ds(at, step), :, lanes]), jnp.roll(
                lines_of(right_ref[pl.ds(at, step), :, lanes]), RADIUS, axis=1
            )
        return left, right

    every, few = slice(None), slice(0, LANES)

    def hide_if(border, lines):
        return jnp.where(place_ref[border] > 0, INVALID, lines)

    def mark_sides(at, upper):
        left, right = sides(at, upper, left_ref, right_ref, few)
        return hide_if(2, left), hide_if(3, right)

    def band(at, ref, ref_s, first, upper):
        merge_ends(at, *columns_of(ref_s[first : first + step]), *sides(at, upper, left_s, right_s, every))
        marks = hide_if(int(upper), ref[first : first + step])
        beside = [hide_if(int(upper), side) for side in mark_sides(at, upper)]
        merge(at, columns_of(marks), *beside, flag_s)

    for i in range(0, RADIUS, step):
        band(i, top_ref, top_s, i, False)
        band(RADIUS + rows + i, bottom_ref, bottom_s, i, True)

    def middle(i, upper):
        at = pl.multiple_of(i * step, step)
        own = at - RADIUS
        ends = [tile_of(xq_ref, c, rows, own, step) for c in (0, cols // TILE - 1)]
        merge_ends(at, *ends, *sides(at, upper, left_s, right_s, every))
        merge(at, columns_of(mark_ref[pl.ds(own, step)].astype(jnp.float32)), *mark_sides(at, upper), flag_s)
        return 0

    lax.fori_loop(RADIUS // step, half // step, lambda i, _: middle(i, False), 0)
    lax.fori_loop(half // step, (RADIUS + rows) // step, lambda i, _: middle(i, True), 0)

    first_lane = (lax.broadcasted_iota(jnp.int32, (8, LANES), 1) == 0).astype(jnp.bfloat16)
    spans = []
    for c in range(wide_cols // TILE):
        lines = flag_s[c * wide_rows * TILE : (c + 1) * wide_rows * TILE, :]
        spans.append(jnp.where(nt(first_lane, lines) > INVALID / 2, HIDDEN, 0.0))
    tall = rows // TILE
    for c in range(cols // TILE):
        for r in range(tall):
            at = slice(r * TILE * TILE, r * TILE * TILE + 2 * TILE * TILE)
            hide_ref[c * tall + r] = jnp.concatenate([spans[c][:, at], spans[c + 1][:, at]], axis=1)


def column_chunks(channels, half):
    at, end = half * 3 * channels // 2, (half + 1) * 3 * channels // 2
    chunks = []
    while at < end:
        width = min(GROUP - at % GROUP, end - at)
        chunks.append((at, at // channels, at % channels // GROUP, at % GROUP, width))
        at += width
    return chunks


def numbered_chunks(channels, half):
    number, chunks = 0, []
    for chunk in column_chunks(channels, half):
        chunks.append((number, *chunk))
        number += chunk[-1] == GROUP
    return chunks


def project_lines(source, w, parts, factor, put):
    size = source.shape[0] // parts
    for m in range(0, source.shape[0], size):
        y = nt(source[m : m + size, :], w)
        put(slice(m, m + size), (y if factor == 1 else y * factor).astype(jnp.bfloat16))


QUERY_FACTOR = HEAD_DIM ** (-0.5) * LOG2_E


def early_kernel(offsets, place_ref, *refs):
    triples, refs = refs[: len(offsets)], refs[len(offsets) :]
    xq_ref, mid_ref, whole_ref, part_ref, near = refs
    channels = near.shape[1]
    triple_rows = near.shape[0] // len(offsets)
    for j, off in enumerate(offsets):
        to = pl.multiple_of(((place_ref[ROW] ^ off) % len(offsets)) * triple_rows, 16)
        near[pl.ds(to, triple_rows), :] = triples[j][...]

    def run(half):
        for number, at, section, _, _, width in numbered_chunks(channels, half):
            w = near[at - half * near.shape[0] : at - half * near.shape[0] + width, :]

            def put(lines, value, number=number, width=width):
                if width == GROUP:
                    whole_ref[number, lines, :] = value
                else:
                    part_ref[lines, :] = value

            if section == 0:
                project_lines(xq_ref, w, 2, QUERY_FACTOR, put)
            else:
                project_lines(mid_ref, w, 2, 1, put)

    for half in range(2):
        pl.when(place_ref[HALF] == half)(functools.partial(run, half))


def project_rest(half, sections, channels, near_at, far_at, sources, put, groups=None):
    xq_ref, mid_ref, outer_ref = sources
    edge, mid = outer_ref.shape[0] // 2, mid_ref.shape[0]
    for number, at, section, group, lane, width in numbered_chunks(channels, half):
        if section in sections and section > 0 and (groups is None or group in groups):
            w = near_at(at, width)
            for first, to in ((0, 0), (edge, edge + mid)):
                put(section, group, lane, width, slice(to, to + edge), nt(outer_ref[first : first + edge, :], w).astype(jnp.bfloat16))
    for at, section, group, lane, width in column_chunks(channels, 1 - half):
        if section not in sections or (groups is not None and group not in groups):
            continue
        w = far_at(at, width)
        if section == 0:
            project_lines(xq_ref, w, 2, QUERY_FACTOR, functools.partial(put, section, group, lane, width))
            continue
        for first, to in ((0, 0), (edge, edge + mid)):
            put(section, group, lane, width, slice(to, to + edge), nt(outer_ref[first : first + edge, :], w).astype(jnp.bfloat16))

        def put_mid(lines, value, section=section, group=group, lane=lane, width=width):
            put(section, group, lane, width, slice(edge + lines.start, edge + lines.stop), value)

        project_lines(mid_ref, w, 2, 1, put_mid)


def late_kernel(pieces, triple_rows, place_ref, *refs):
    sources, refs = refs[: len(pieces)], refs[len(pieces) :]
    near, whole_ref, part_ref, xq_ref, mid_ref, outer_ref, q_s, k_s, wt, near_sem = refs
    channels = wt.shape[1]
    edge, mid = outer_ref.shape[0] // 2, mid_ref.shape[0]
    for j, (off, start) in enumerate(pieces):
        to = pl.multiple_of((place_ref[ROW] ^ off) * triple_rows + place_ref[STARTS + start], 16)
        wt[pl.ds(to, sources[j].shape[0]), :] = sources[j][...]
    to = pl.multiple_of(place_ref[HALF] * near.shape[0], 16)
    near_copy = pltpu.make_async_copy(near, wt.at[pl.ds(to, near.shape[0]), :], near_sem)
    near_copy.start()

    def put(section, group, lane, width, lines, value):
        if section == 0:
            q_s[group, lines, :] = value
        else:
            k_s[group, lines, lane : lane + width] = value

    def run(half):
        for number, at, section, group, lane, width in numbered_chunks(channels, half):
            if section == 0:
                q_s[group] = whole_ref[number]
            elif section == 1 and width == GROUP:
                k_s[group, edge : edge + mid, :] = whole_ref[number, :mid, :]
            elif section == 1:
                k_s[group, edge : edge + mid, lane : lane + width] = part_ref[...]
        base = half * near.shape[0]
        project_rest(
            half, (0, 1), channels, lambda at, width: near[at - base : at - base + width, :], lambda at, width: wt[at : at + width, :],
            (xq_ref, mid_ref, outer_ref), put,
        )

    for half in range(2):
        pl.when(place_ref[HALF] == half)(functools.partial(run, half))
    near_copy.wait()


def value_kernel(first, place_ref, wt, whole_ref, mid_ref, outer_ref, v_s):
    here = range(first, first + v_s.shape[0])
    channels = wt.shape[1]
    edge, mid = outer_ref.shape[0] // 2, mid_ref.shape[0]

    def put(section, group, lane, width, lines, value):
        v_s[group - first, lines, lane : lane + width] = value

    def run(half):
        for number, at, section, group, lane, width in numbered_chunks(channels, half):
            if section == 2 and group in here:
                v_s[group - first, edge : edge + mid, :] = whole_ref[number, :mid, :]
        weights = lambda at, width: wt[at : at + width, :]
        project_rest(half, (2,), channels, weights, weights, (None, mid_ref, outer_ref), put, here)

    for half in range(2):
        pl.when(place_ref[HALF] == half)(functools.partial(run, half))


def carrier_kernel(offsets, place_ref, wt, *refs):
    shards = len(offsets)
    finals, refs = refs[:shards], refs[shards:]
    summary_ref, wo, kce, vc_s = refs
    per_row = summary_ref.shape[1]
    channels = wt.shape[1]
    groups = channels // GROUP
    heads = channels // HEAD_DIM
    factor = HEAD_DIM ** (-0.5)
    carriers_here = vc_s.shape[0]
    final_rows = wo.shape[0] // shards
    for j, off in enumerate(offsets):
        to = pl.multiple_of((place_ref[ROW] ^ off) * final_rows, 16)
        wo[pl.ds(to, final_rows), :] = finals[j][:final_rows, :]
    carriers = jnp.concatenate([final[final_rows:, :].astype(jnp.float32) for final in finals], axis=0)
    own = carriers[:carriers_here]
    carriers = layer_normalise(carriers).astype(jnp.bfloat16)
    own_norm = layer_normalise(own).astype(jnp.bfloat16)
    qc = (nt(own_norm, wt[:channels, :]) * factor).astype(jnp.bfloat16).astype(jnp.float32)
    kc = nt(carriers, wt[channels : 2 * channels, :]).astype(jnp.bfloat16)
    vc = nt(carriers, wt[2 * channels :, :]).astype(jnp.bfloat16)
    head_of = lax.broadcasted_iota(jnp.int32, (1, channels), 1) // HEAD_DIM
    stacked = jnp.concatenate([jnp.where(head_of == h, qc, 0.0) for h in range(heads)], axis=0)
    e = jnp.exp(nt(stacked.astype(jnp.bfloat16), kc))
    weights = (e / jnp.sum(e, axis=-1, keepdims=True)).astype(jnp.bfloat16)
    o = nn(weights, vc)
    mix = jnp.zeros((carriers_here, channels), jnp.float32)
    for h in range(heads):
        mix = jnp.where(head_of == h, o[h * carriers_here : (h + 1) * carriers_here, :], mix)
    renewed = own + nt(mix.astype(jnp.bfloat16), wo[...])
    for i in range(summary_ref.shape[0]):
        summary_ref[i] = renewed[i * per_row : (i + 1) * per_row, :].astype(jnp.bfloat16)
    fresh = nt(layer_normalise(renewed).astype(jnp.bfloat16), wt[channels:, :]).astype(jnp.bfloat16).astype(jnp.float32)
    vc_s[...] = fresh[:, channels:]
    same = (
        lax.broadcasted_iota(jnp.int32, (GROUP, GROUP), 0) // HEAD_DIM
        == lax.broadcasted_iota(jnp.int32, (GROUP, GROUP), 1) // HEAD_DIM
    )
    windows = kce.shape[0] // groups
    for w in range(windows):
        for g in range(groups):
            kce[w * groups + g] = jnp.where(same, fresh[w : w + 1, g * GROUP : (g + 1) * GROUP], 0.0).astype(jnp.bfloat16)


def attend_kernel(tall, broad, q_s, k_s, v_low, v_high, hide_ref, kce, vc_s, mix_s, pc_s, even_s, odd_s):
    groups, tiles = q_s.shape[0], hide_ref.shape[0]
    heads_in = GROUP // HEAD_DIM
    queries, span = TILE * TILE, 2 * TILE * TILE
    side = PATCH_SIDE // TILE
    wide = (tall + 1) * queries
    qi = lax.broadcasted_iota(jnp.int32, (queries, 2 * span), 0)
    ki = lax.broadcasted_iota(jnp.int32, (queries, 2 * span), 1)
    row_step = (ki % span) // TILE - qi // TILE
    col_step = (ki // span) * TILE + ki % TILE - qi % TILE
    seen = (row_step >= 0) & (row_step <= 2 * RADIUS) & (col_step >= 0) & (col_step <= 2 * RADIUS)
    band = jnp.where(seen, 0.0, HIDDEN)
    group_head = lax.broadcasted_iota(jnp.int32, (1, GROUP), 1) // HEAD_DIM
    only = [jnp.where(group_head == h, 1.0, 0.0).astype(jnp.bfloat16) for h in range(heads_in)]
    in_pair = LANES // HEAD_DIM
    pair_head = lax.broadcasted_iota(jnp.int32, (1, LANES), 1) // HEAD_DIM

    for c in range(broad):
        for w in range(tall // side):
            at = slice((c * tall + w * side) * queries, (c * tall + (w + 1) * side) * queries)
            window = w * (broad // side) + c // side
            for g in range(groups):
                pc_s[at, g * GROUP : (g + 1) * GROUP] = jnp.exp2(nt(q_s[g, at, :], kce[window * groups + g]))

    def keys_at(t):
        k0 = pl.multiple_of(t // tall * wide + t % tall * queries, queries)
        return k0, pl.multiple_of(k0 + wide, queries)

    def scores(t, ref):
        q_at = pl.multiple_of(t * queries, queries)
        k0, k1 = keys_at(t)
        for g in range(groups):
            q = q_s[g, pl.ds(q_at, queries), :]
            qq = jnp.concatenate([q * mask for mask in only], axis=0)
            k = jnp.concatenate([k_s[g, pl.ds(k0, span), :], k_s[g, pl.ds(k1, span), :]], axis=0)
            ref[g] = nt(qq, k)

    def finish(t, ref):
        q_at = pl.multiple_of(t * queries, queries)
        k0, k1 = keys_at(t)
        window = t % tall // side * (broad // side) + t // tall // side
        bias = band + hide_ref[t][0:1, :]
        for g in range(groups):
            p = jnp.exp2(ref[g].reshape(heads_in, queries, 2 * span) + bias[None])
            total = jnp.sum(p, axis=-1, keepdims=True)
            v_ref, at = (v_low, g) if g < v_low.shape[0] else (v_high, g - v_low.shape[0])
            v = jnp.concatenate([v_ref[at, pl.ds(k0, span), :], v_ref[at, pl.ds(k1, span), :]], axis=0)
            o = nn(p.reshape(heads_in * queries, 2 * span).astype(jnp.bfloat16), v).reshape(heads_in, queries, GROUP)
            v_new = vc_s[pl.ds(window, 1), g * GROUP : (g + 1) * GROUP]
            for j in range(GROUP // LANES):
                lanes = slice(j * LANES, (j + 1) * LANES)
                at = slice(g * GROUP + j * LANES, g * GROUP + (j + 1) * LANES)
                kept, kept_total = o[j * in_pair, :, lanes], total[j * in_pair]
                for h in range(1, in_pair):
                    kept = jnp.where(pair_head == h, o[j * in_pair + h, :, lanes], kept)
                    kept_total = jnp.where(pair_head == h, total[j * in_pair + h], kept_total)
                new = pc_s[pl.ds(q_at, queries), at]
                mixed = (kept + new * v_new[:, lanes]) / (kept_total + new)
                mix_s[pl.ds(q_at, queries), at] = mixed.astype(jnp.bfloat16)

    scores(0, even_s)

    def two(i, _):
        t = 2 * i
        scores(t + 1, odd_s)
        finish(t, even_s)
        scores(jnp.minimum(t + 2, tiles - 1), even_s)
        finish(t + 1, odd_s)
        return 0

    lax.fori_loop(0, tiles // 2, two, 0)


def out_kernel(x_ref, mix_s, wo, out_hbm, out_ref, out_sems):
    rows, cols, channels = x_ref.shape
    going = []
    for pair in range(cols // (2 * TILE)):
        both = slice(2 * pair * TILE, 2 * (pair + 1) * TILE)
        for g in range(channels // GROUP):
            at = slice(g * GROUP, (g + 1) * GROUP)
            w = wo[at, :]
            y = nt(mix_s[2 * pair * rows * TILE : 2 * (pair + 1) * rows * TILE, :], w).reshape(2, rows, TILE, GROUP)
            y = jnp.concatenate([y[0], y[1]], axis=1) + x_ref[:, both, at].astype(jnp.float32)
            out_ref[pair, :, :, at] = y.astype(jnp.bfloat16)
        copy = pltpu.make_async_copy(out_ref.at[pair], out_hbm.at[:, both, :], out_sems.at[pair])
        copy.start()
        going.append(copy)
    for copy in going:
        copy.wait()


def local(grid_elements, summary_vectors, triple_projection, final_projection, genuine_flags):
    rows, cols, channels = grid_elements.shape
    wide_rows, wide_cols = rows + 2 * RADIUS, cols + 2 * RADIUS

    triple_t, final_t = triple_projection.T, final_projection.T
    vmem = pl.BlockSpec(memory_space=pltpu.VMEM)
    anywhere = pl.BlockSpec(memory_space=pl.ANY)
    scalars = pl.BlockSpec(memory_space=pltpu.SMEM)
    hbm = pl.BlockSpec(memory_space=pltpu.HBM)
    small = pltpu.CompilerParams(vmem_limit_bytes=8 * 1024 * 1024)
    row_strip = jax.ShapeDtypeStruct((RADIUS, cols, channels), jnp.bfloat16)
    col_strip = jax.ShapeDtypeStruct((wide_rows // 2, 2 * RADIUS, channels), jnp.bfloat16)

    row, col, img = lax.axis_size("row"), lax.axis_size("col"), lax.axis_size("img")
    row_at, col_at, img_at = lax.axis_index("row"), lax.axis_index("col"), lax.axis_index("img")
    row_bits = bits_of(row)
    far, rest = row_bits[0], row_bits[1:]
    piece_rows = triple_t.shape[0] * 5 // (8 * img) // 16 * 16
    relays = img if piece_rows else 0
    starts = [(img_at - k) % img for k in range(relays)] + [jnp.int32(relays)]
    place = [row_at == 0, row_at == row - 1, col_at == 0, col_at == col - 1, row_at % 2 == 0, col_at % 2 == 0, row_at, row_at // far]
    place = jnp.stack([jnp.asarray(p).astype(jnp.int32) for p in place + [start * piece_rows for start in starts]])

    mark, even_rows, odd_rows, x = pl.pallas_call(
        edge_kernel,
        out_shape=(
            pltpu.VMEM((rows, cols, LANES), jnp.bfloat16),
            pltpu.VMEM(row_strip.shape, jnp.bfloat16),
            pltpu.VMEM(row_strip.shape, jnp.bfloat16),
            pltpu.VMEM(grid_elements.shape, jnp.bfloat16),
        ),
        in_specs=[scalars, hbm, hbm],
        out_specs=(vmem,) * 4,
        scratch_shapes=[
            pltpu.VMEM((rows, cols), jnp.int32),
            pltpu.VMEM((rows * cols, cols), jnp.bfloat16),
            pltpu.SemaphoreType.DMA((2,)),
        ],
        compiler_params=small,
        cost_estimate=pl.CostEstimate(flops=1_000_000, bytes_accessed=1_000_000, transcendentals=0),
        name="edge_rows",
    )(place, *(pltpu.with_memory_space_constraint(a, pltpu.HBM) for a in (genuine_flags, grid_elements)))
    mine, last = pl.pallas_call(
        piece_kernel,
        out_shape=(
            pltpu.VMEM((max(piece_rows, 16), channels), jnp.bfloat16),
            pltpu.VMEM((triple_t.shape[0] - relays * piece_rows, channels), jnp.bfloat16),
        ),
        in_specs=[scalars, hbm],
        out_specs=(vmem, vmem),
        scratch_shapes=[pltpu.SemaphoreType.DMA((2,))],
        compiler_params=small,
        cost_estimate=pl.CostEstimate(flops=1_000_000, bytes_accessed=1_000_000, transcendentals=0),
        name="pieces",
    )(place, pltpu.with_memory_space_constraint(after(triple_t, even_rows), pltpu.HBM))
    xq = pl.pallas_call(
        own_kernel,
        out_shape=pltpu.VMEM((rows * cols, channels), jnp.bfloat16),
        in_specs=[vmem],
        out_specs=vmem,
        compiler_params=small,
        cost_estimate=pl.CostEstimate(flops=1_000_000, bytes_accessed=1_000_000, transcendentals=0),
        name="own_norm",
    )(x)
    even_rows, odd_rows = pair_swapped(even_rows, odd_rows, "row")

    far_pieces = []
    if relays:
        first = swapped(mine, "row", far)
    far_last = swapped(after(last, even_rows, odd_rows), "row", far)

    own_rows = summary_vectors.shape[0] * summary_vectors.shape[1]
    carrier_tiles = -(-own_rows // TILE)
    even_cols, odd_cols = pl.pallas_call(
        strip_kernel,
        out_shape=(
            pltpu.VMEM((col_strip.shape[0] + carrier_tiles, *col_strip.shape[1:]), jnp.bfloat16),
            pltpu.VMEM(col_strip.shape, jnp.bfloat16),
        ),
        in_specs=[scalars] + [vmem] * 5,
        out_specs=(vmem,) * 2,
        scratch_shapes=[pltpu.VMEM((carrier_tiles * TILE, channels), jnp.float32)],
        compiler_params=small,
        cost_estimate=pl.CostEstimate(flops=1_000_000, bytes_accessed=2_000_000, transcendentals=0),
        name="edge_columns",
    )(place, x, after(mark, xq), even_rows, odd_rows, summary_vectors)
    even_cols, odd_cols = pair_swapped(even_cols, odd_cols, "col")
    groups = channels // GROUP
    triples, offsets = [triple_t], [0]
    for bit in rest:
        triples = triples + [swapped(p, "row", bit) for p in triples]
        offsets = offsets + [o ^ bit for o in offsets]
    mid = pl.pallas_call(
        middle_kernel,
        out_shape=pltpu.VMEM(((wide_cols // TILE - 2) * wide_rows * TILE, channels), jnp.bfloat16),
        in_specs=[scalars] + [vmem] * 3,
        out_specs=vmem,
        scratch_shapes=[pltpu.VMEM(row_strip.shape, jnp.float32)] * 2,
        compiler_params=small,
        cost_estimate=pl.CostEstimate(flops=1_000_000, bytes_accessed=1_000_000, transcendentals=0),
        name="middle_blocks",
    )(place, xq, even_rows, odd_rows)
    whole, part, near = pl.pallas_call(
        functools.partial(early_kernel, offsets),
        out_shape=(
            pltpu.VMEM((3 * groups // 2, rows * cols, GROUP), jnp.bfloat16),
            pltpu.VMEM((mid.shape[0], GROUP // 2), jnp.bfloat16),
            pltpu.VMEM((3 * channels // 2, channels), jnp.bfloat16),
        ),
        in_specs=[scalars] + [vmem] * (len(triples) + 2),
        out_specs=(vmem,) * 3,
        compiler_params=pltpu.CompilerParams(vmem_limit_bytes=16 * 1024 * 1024),
        cost_estimate=pl.CostEstimate(flops=1_000_000, bytes_accessed=1_000_000, transcendentals=0),
        name="project_early",
    )(place, *triples, xq, mid)

    carriers = pl.pallas_call(
        carrier_pair_kernel,
        out_shape=pltpu.VMEM((2 * own_rows, channels), jnp.bfloat16),
        in_specs=[vmem, anywhere],
        out_specs=vmem,
        scratch_shapes=[
            pltpu.VMEM((carrier_tiles, TILE, channels), jnp.bfloat16),
            pltpu.VMEM((2 * own_rows, channels), jnp.float32),
            pltpu.SemaphoreType.DMA,
        ],
        compiler_params=small,
        cost_estimate=pl.CostEstimate(flops=1_000, bytes_accessed=1_000, transcendentals=0),
        name="carrier_pair",
    )(summary_vectors, after(even_cols, near))
    parts = [carriers]
    for bit in bits_of(col)[:-1]:
        carriers = carriers if len(parts) == 1 else jnp.concatenate(parts, axis=0)
        got = swapped(carriers, "col", 2 * bit - 1)
        parts.append(got)
    if relays:
        first = after(first, even_cols, odd_cols, parts[0])
        others = [lax.ppermute(first, "img", [(i, (i + k) % img) for i in range(img)]) for k in range(1, relays)]
        far_pieces = [first] + others
    far_pieces.append(far_last)

    tiles = (rows // TILE) * (cols // TILE)
    keys = 4 * TILE * TILE
    outer, hide = pl.pallas_call(
        outer_kernel,
        out_shape=(
            pltpu.VMEM((2 * wide_rows * TILE, channels), jnp.bfloat16),
            pltpu.VMEM((tiles, 8, keys), jnp.float32),
        ),
        in_specs=[scalars] + [vmem] * 6,
        out_specs=(vmem,) * 2,
        scratch_shapes=[
            *[pltpu.VMEM((RADIUS, 2 * TILE, channels), jnp.float32)] * 2,
            *[pltpu.VMEM(col_strip.shape, jnp.float32)] * 2,
            *[pltpu.VMEM((*shape.shape[:2], LANES), jnp.float32) for shape in (row_strip, row_strip, col_strip, col_strip)],
            pltpu.VMEM((wide_rows * wide_cols, LANES), jnp.bfloat16),
        ],
        compiler_params=pltpu.CompilerParams(vmem_limit_bytes=12 * 1024 * 1024),
        cost_estimate=pl.CostEstimate(flops=10_000_000, bytes_accessed=6_000_000, transcendentals=1000),
        name="outer_blocks",
    )(place, xq, mark, even_rows, odd_rows, even_cols, odd_cols)

    final_pack = pl.pallas_call(
        pack_kernel,
        out_shape=pltpu.VMEM((final_t.shape[0] + col * own_rows, channels), jnp.bfloat16),
        in_specs=[vmem] * (1 + len(parts)),
        out_specs=vmem,
        compiler_params=small,
        cost_estimate=pl.CostEstimate(flops=1_000, bytes_accessed=1_000, transcendentals=0),
        name="final_pack",
    )(final_t, *parts[:-1], after(parts[-1], outer))
    finals = [final_pack]
    for bit in rest:
        finals = finals + [swapped(p, "row", bit) for p in finals]

    far_final = swapped(final_pack, "row", far)

    far_offsets = [far]
    far_pieces = [[after(piece, outer, got)] for piece in far_pieces]
    for bit in rest:
        far_pieces = [same + [swapped(p, "row", bit) for p in same] for same in far_pieces]
        far_offsets = far_offsets + [o ^ bit for o in far_offsets]

    numbered = [(off, number) for number in range(len(far_pieces)) for off in far_offsets]
    sources = [piece for same in far_pieces for piece in same]
    q, k, wt = pl.pallas_call(
        functools.partial(late_kernel, numbered, triple_t.shape[0]),
        out_shape=(
            jax.ShapeDtypeStruct((groups, rows * cols, GROUP), jnp.bfloat16),
            jax.ShapeDtypeStruct((groups, wide_rows * wide_cols, GROUP), jnp.bfloat16),
            jax.ShapeDtypeStruct((3 * channels, channels), jnp.bfloat16),
        ),
        in_specs=[scalars] + [vmem] * (len(sources) + 6),
        out_specs=(vmem,) * 3,
        scratch_shapes=[pltpu.SemaphoreType.DMA],
        compiler_params=pltpu.CompilerParams(vmem_limit_bytes=VMEM_BYTES),
        cost_estimate=pl.CostEstimate(flops=1_000_000, bytes_accessed=1_000_000, transcendentals=0),
        name="project_late",
    )(place, *sources, near, whole, part, xq, mid, outer)

    def values(first, count, wt):
        return pl.pallas_call(
            functools.partial(value_kernel, first),
            out_shape=jax.ShapeDtypeStruct((count, wide_rows * wide_cols, GROUP), jnp.bfloat16),
            in_specs=[scalars] + [vmem] * 4,
            out_specs=vmem,
            compiler_params=pltpu.CompilerParams(vmem_limit_bytes=VMEM_BYTES),
            cost_estimate=pl.CostEstimate(flops=3_000_000_000, bytes_accessed=7_000_000, transcendentals=0),
            name="values",
        )(place, wt, whole, mid, outer)

    split = groups // 2 + groups % 2
    v_low = values(0, split, wt)
    v_high = values(split, groups - split, after(wt, v_low))

    far_finals = [after(far_final, v_low)]
    for bit in rest:
        far_finals = far_finals + [swapped(p, "row", bit) for p in far_finals]
    finals, offsets = finals + far_finals, offsets + far_offsets
    carriers_here = carrier_tiles * TILE
    summary_result, wo, kce, vc = pl.pallas_call(
        functools.partial(carrier_kernel, offsets),
        out_shape=(
            jax.ShapeDtypeStruct(summary_vectors.shape, jnp.bfloat16),
            jax.ShapeDtypeStruct((channels, channels), jnp.bfloat16),
            jax.ShapeDtypeStruct((own_rows * groups, GROUP, GROUP), jnp.bfloat16),
            jax.ShapeDtypeStruct((carriers_here, channels), jnp.float32),
        ),
        in_specs=[scalars] + [vmem] * (1 + len(finals)),
        out_specs=(vmem,) * 4,
        compiler_params=pltpu.CompilerParams(vmem_limit_bytes=VMEM_BYTES),
        cost_estimate=pl.CostEstimate(flops=500_000_000, bytes_accessed=5_000_000, transcendentals=10_000),
        name="carriers",
    )(place, wt, *finals)

    scores = (groups, GROUP // HEAD_DIM * TILE * TILE, keys)
    mix = pl.pallas_call(
        functools.partial(attend_kernel, rows // TILE, cols // TILE),
        out_shape=jax.ShapeDtypeStruct((rows * cols, channels), jnp.bfloat16),
        in_specs=[vmem] * 7,
        out_specs=vmem,
        scratch_shapes=[
            pltpu.VMEM((rows * cols, channels), jnp.float32),
            pltpu.VMEM(scores, jnp.float32),
            pltpu.VMEM(scores, jnp.float32),
        ],
        compiler_params=pltpu.CompilerParams(vmem_limit_bytes=VMEM_BYTES),
        cost_estimate=pl.CostEstimate(flops=4_000_000_000, bytes_accessed=12_000_000, transcendentals=4_000_000),
        name="attend",
    )(q, k, v_low, v_high, hide, kce, vc)

    out = pl.pallas_call(
        out_kernel,
        out_shape=jax.ShapeDtypeStruct(grid_elements.shape, jnp.bfloat16),
        in_specs=[vmem] * 3,
        out_specs=anywhere,
        scratch_shapes=[
            pltpu.VMEM((cols // (2 * TILE), rows, 2 * TILE, channels), jnp.bfloat16),
            pltpu.SemaphoreType.DMA((cols // (2 * TILE),)),
        ],
        compiler_params=pltpu.CompilerParams(vmem_limit_bytes=VMEM_BYTES),
        cost_estimate=pl.CostEstimate(flops=1_200_000_000, bytes_accessed=6_000_000, transcendentals=0),
        name="out",
    )(x, mix, wo)
    return (out, summary_result)


def solution(mesh):
    placed = (
        P(("img", "row"), "col", None),
        P(("img", "row"), "col", None),
        P(None, "row"),
        P(None, "row"),
        P(("img", "row"), "col"),
    )
    return jax.shard_map(
        local,
        mesh=mesh,
        in_specs=placed,
        out_specs=(P(("img", "row"), "col", None), P(("img", "row"), "col", None)),
        check_vma=False,
    )
```

```python
import functools

import jax
import jax.numpy as jnp
from jax import lax
from jax.experimental import pallas as pl
from jax.experimental.pallas import tpu as pltpu
from jax.sharding import PartitionSpec as P

HEAD_DIM = 64
PATCH_SIDE = 16
RADIUS = 4
TILE = 2 * RADIUS
LANES = 128
GROUP = 256
INVALID = 100.0
HIDDEN = -1e30
LOG2_E = 1.4426950408889634
EVEN_ROW, EVEN_COL, ROW, HALF, STARTS = 4, 5, 6, 7, 8
VMEM_BYTES = 26 * 1024 * 1024


def nt(a, b):
    return lax.dot_general(a, b, (((1,), (1,)), ((), ())), preferred_element_type=jnp.float32)


def nn(a, b):
    return lax.dot_general(a, b, (((1,), (0,)), ((), ())), preferred_element_type=jnp.float32)


def layer_normalise(lines):
    center = lines - jnp.mean(lines, axis=-1, keepdims=True)
    spread = jnp.mean(center * center, axis=-1, keepdims=True)
    return center * lax.rsqrt(spread + 1e-05)


def pair_swapped(even_block, odd_block, axis):
    count = lax.axis_size(axis)
    got = []
    for first, block in ((0, even_block), (1, odd_block)):
        pairs = [(i, i + 1) for i in range(first, count - 1, 2)]
        got.append(lax.ppermute(block, axis, pairs + [(b, a) for a, b in pairs]))
    return got


def swapped(block, axis, bit):
    count = lax.axis_size(axis)
    return lax.ppermute(block, axis, [(i, i ^ bit) for i in range(count)])


def after(block, *others):
    return lax.optimization_barrier((block, *others))[0]


def bits_of(count):
    bits, bit = [], count // 2
    while bit:
        bits.append(bit)
        bit //= 2
    return bits


def marked_lanes(lines, hidden):
    first = jnp.where(hidden, INVALID, lines[:, :, :LANES])
    return jnp.concatenate([first, lines[:, :, LANES:]], axis=2)


def edge_kernel(place_ref, flags_hbm, x_hbm, mark_ref, even_ref, odd_ref, x_ref, *scratch):
    flags_ref, spread, sems = scratch
    rows, cols = flags_ref.shape
    flags_copy = pltpu.make_async_copy(flags_hbm, flags_ref, sems.at[0])
    x_copy = pltpu.make_async_copy(x_hbm, x_ref, sems.at[1])
    flags_copy.start()
    x_copy.start()
    flags_copy.wait()
    row_at = lax.broadcasted_iota(jnp.int32, (cols, cols), 0)
    diagonal = row_at == lax.broadcasted_iota(jnp.int32, (cols, cols), 1)
    for r in range(rows):
        hidden = jnp.where(flags_ref[r : r + 1, :] > 0, 0.0, INVALID)
        spread[r * cols : (r + 1) * cols, :] = jnp.where(diagonal, hidden, 0.0).astype(jnp.bfloat16)
    marks = nn(spread[...], jnp.ones((cols, LANES), jnp.bfloat16)).reshape(rows, cols, LANES)
    mark_ref[...] = marks.astype(jnp.bfloat16)
    x_copy.wait()
    first, last = [
        marked_lanes(x_ref[at].astype(jnp.float32), marks[at] > INVALID / 2)
        for at in (slice(0, RADIUS), slice(rows - RADIUS, rows))
    ]
    even = place_ref[EVEN_ROW] > 0
    even_ref[...] = jnp.where(even, last, first).astype(jnp.bfloat16)
    odd_ref[...] = jnp.where(even, first, last).astype(jnp.bfloat16)


def piece_kernel(place_ref, triple_hbm, mine_ref, last_ref, sems):
    start = pl.multiple_of(place_ref[STARTS], 16)
    last = triple_hbm.shape[0] - last_ref.shape[0]
    copies = [
        pltpu.make_async_copy(triple_hbm.at[pl.ds(start, mine_ref.shape[0]), :], mine_ref, sems.at[0]),
        pltpu.make_async_copy(triple_hbm.at[last:, :], last_ref, sems.at[1]),
    ]
    for copy in copies:
        copy.start()
    for copy in copies:
        copy.wait()


def strip_kernel(place_ref, x_ref, mark_ref, even_rows_ref, odd_rows_ref, carriers_ref, even_ref, odd_ref, carriers_s):
    per_row = carriers_ref.shape[1]
    carriers_s[...] = jnp.zeros_like(carriers_s)
    for i in range(carriers_ref.shape[0]):
        carriers_s[i * per_row : (i + 1) * per_row, :] = carriers_ref[i].astype(jnp.float32)
    for i in range(carriers_s.shape[0] // TILE):
        even_ref[odd_ref.shape[0] + i] = carriers_s[i * TILE : (i + 1) * TILE, :].astype(jnp.bfloat16)
    rows, cols, channels = x_ref.shape
    middle = rows // 2
    low = lax.broadcasted_iota(jnp.int32, (1, TILE, 1), 1) < RADIUS
    even_row, even_col = place_ref[EVEN_ROW] > 0, place_ref[EVEN_COL] > 0
    for lane in range(0, channels, LANES):
        lanes = slice(lane, lane + LANES)
        strips = []
        for columns, last in ((slice(0, TILE), False), (slice(cols - TILE, cols), True)):

            def own(part):
                lines = x_ref[part, columns, lanes].astype(jnp.float32)
                if lane == 0:
                    lines = jnp.where(mark_ref[part, columns, :].astype(jnp.float32) > INVALID / 2, INVALID, lines)
                return lines

            even_rows = even_rows_ref[:, columns, lanes].astype(jnp.float32)
            odd_rows = odd_rows_ref[:, columns, lanes].astype(jnp.float32)
            top, bottom = jnp.where(even_row, odd_rows, even_rows), jnp.where(even_row, even_rows, odd_rows)
            upper = jnp.concatenate([top, own(slice(0, middle))], axis=0)
            lower = jnp.concatenate([own(slice(middle, rows)), bottom], axis=0)
            if last:
                upper = jnp.roll(upper, RADIUS, axis=1)
            else:
                lower = jnp.roll(lower, RADIUS, axis=1)
            strips.append(jnp.where(low, upper, lower))
        first, last = strips
        even_ref[: odd_ref.shape[0], :, lanes] = jnp.where(even_col, last, first).astype(jnp.bfloat16)
        odd_ref[:, :, lanes] = jnp.where(even_col, first, last).astype(jnp.bfloat16)


def carrier_pair_kernel(own_ref, got_hbm, out_ref, got_s, pair_s, sem):
    per_row, here = own_ref.shape[1], own_ref.shape[0] * own_ref.shape[1]
    tiles = got_s.shape[0]
    copy = pltpu.make_async_copy(got_hbm.at[got_hbm.shape[0] - tiles :], got_s, sem)
    copy.start()
    for i in range(own_ref.shape[0]):
        pair_s[i * per_row : (i + 1) * per_row, :] = own_ref[i].astype(jnp.float32)
    copy.wait()
    pair_s[here:, :] = got_s[...].astype(jnp.float32).reshape(tiles * TILE, -1)[:here]
    out_ref[...] = pair_s[...].astype(jnp.bfloat16)


def pack_kernel(final_ref, *refs):
    parts, out_ref = refs[:-1], refs[-1]
    rows = final_ref.shape[0]
    out_ref[:rows, :] = final_ref[...]
    carriers = jnp.concatenate([part[...].astype(jnp.float32) for part in parts], axis=0)
    out_ref[rows:, :] = carriers.astype(jnp.bfloat16)


def own_kernel(x_ref, xq_ref):
    rows, cols, _ = x_ref.shape
    step = 4

    def own(i, _):
        at = pl.multiple_of(i * step, step)
        y = layer_normalise(x_ref[pl.ds(at, step)].astype(jnp.float32))
        for c in range(cols // TILE):
            piece = y[:, c * TILE : (c + 1) * TILE, :].reshape(step * TILE, -1)
            to = pl.multiple_of(c * rows * TILE + at * TILE, step * TILE)
            xq_ref[pl.ds(to, step * TILE), :] = piece.astype(jnp.bfloat16)
        return 0

    lax.fori_loop(0, rows // step, own, 0)


def columns_of(lines):
    return [lines[:, c : c + TILE, :] for c in range(0, lines.shape[1], TILE)]


def tile_of(xq_ref, column, rows, at, step):
    first = pl.multiple_of(column * rows * TILE + at * TILE, step * TILE)
    return xq_ref[pl.ds(first, step * TILE), :].astype(jnp.float32).reshape(step, TILE, -1)


def store_lines(ref, block, wide_rows, at, lines):
    size = lines.shape[0] * TILE
    to = block * wide_rows * TILE + at * TILE
    to = to if isinstance(to, int) else pl.multiple_of(to, size)
    ref[pl.ds(to, size), :] = lines.reshape(size, -1).astype(jnp.bfloat16)


def middle_kernel(place_ref, xq_ref, even_rows_ref, odd_rows_ref, mid_ref, top_s, bottom_s):
    cols = even_rows_ref.shape[1]
    rows, step = xq_ref.shape[0] // cols, 2
    wide_rows = rows + 2 * RADIUS
    flip = place_ref[EVEN_ROW] > 0
    for i in range(0, RADIUS, step):
        a, b = even_rows_ref[i : i + step].astype(jnp.float32), odd_rows_ref[i : i + step].astype(jnp.float32)
        top_s[i : i + step] = layer_normalise(jnp.where(flip, b, a))
        bottom_s[i : i + step] = layer_normalise(jnp.where(flip, a, b))
    low = lax.broadcasted_iota(jnp.int32, (1, TILE, 1), 1) < RADIUS

    def merge(at, blocks):
        moved = [jnp.roll(block, RADIUS, axis=1) for block in blocks]
        for c in range(1, len(blocks)):
            store_lines(mid_ref, c - 1, wide_rows, at, jnp.where(low, moved[c - 1], moved[c]))

    for i in range(0, RADIUS, step):
        merge(i, columns_of(top_s[i : i + step]))
        merge(RADIUS + rows + i, columns_of(bottom_s[i : i + step]))

    def middle(i, _):
        at = pl.multiple_of(i * step, step)
        merge(RADIUS + at, [tile_of(xq_ref, c, rows, at, step) for c in range(cols // TILE)])
        return 0

    lax.fori_loop(0, rows // step, middle, 0)


def outer_kernel(place_ref, xq_ref, mark_ref, even_rows_ref, odd_rows_ref, even_cols_ref, odd_cols_ref, outer_ref, hide_ref, *scratch):
    rows, cols, _ = mark_ref.shape
    wide_rows, wide_cols = rows + 2 * RADIUS, cols + 2 * RADIUS
    half = wide_rows // 2
    step = 2
    top_s, bottom_s, left_s, right_s, top_ref, bottom_ref, left_ref, right_ref, flag_s = scratch
    flip = place_ref[EVEN_ROW] > 0
    a, b = even_rows_ref[...].astype(jnp.float32), odd_rows_ref[...].astype(jnp.float32)
    for lines, out, flags in ((jnp.where(flip, b, a), top_s, top_ref), (jnp.where(flip, a, b), bottom_s, bottom_ref)):
        ends = jnp.concatenate([lines[:, :TILE, :], lines[:, cols - TILE :, :]], axis=1)
        out[...] = layer_normalise(ends)
        flags[...] = lines[:, :, :LANES]
    flip = place_ref[EVEN_COL] > 0
    size = 5
    for i in range(0, odd_cols_ref.shape[0], size):
        a, b = even_cols_ref[i : i + size].astype(jnp.float32), odd_cols_ref[i : i + size].astype(jnp.float32)
        for lines, out, flags in ((jnp.where(flip, b, a), left_s, left_ref), (jnp.where(flip, a, b), right_s, right_ref)):
            out[i : i + size] = layer_normalise(lines)
            flags[i : i + size] = lines[:, :, :LANES]
    low = lax.broadcasted_iota(jnp.int32, (1, TILE, 1), 1) < RADIUS

    def lines_of(ref):
        return ref.astype(jnp.float32)

    def merge(at, blocks, left, right, to_ref):
        moved = [left] + [jnp.roll(block, RADIUS, axis=1) for block in blocks] + [right]
        for c in range(len(blocks) + 1):
            store_lines(to_ref, c, wide_rows, at, jnp.where(low, moved[c], moved[c + 1]))

    def merge_ends(at, first, last, left, right):
        store_lines(outer_ref, 0, wide_rows, at, jnp.where(low, left, jnp.roll(first, RADIUS, axis=1)))
        store_lines(outer_ref, 1, wide_rows, at, jnp.where(low, jnp.roll(last, RADIUS, axis=1), right))

    def sides(at, upper, left_ref, right_ref, lanes):
        if upper:
            at = at - half
            left, right = jnp.roll(lines_of(left_ref[pl.ds(at, step), :, lanes]), RADIUS, axis=1), lines_of(
                right_ref[pl.ds(at, step), :, lanes]
            )
        else:
            left, right = lines_of(left_ref[pl.ds(at, step), :, lanes]), jnp.roll(
                lines_of(right_ref[pl.ds(at, step), :, lanes]), RADIUS, axis=1
            )
        return left, right

    every, few = slice(None), slice(0, LANES)

    def hide_if(border, lines):
        return jnp.where(place_ref[border] > 0, INVALID, lines)

    def mark_sides(at, upper):
        left, right = sides(at, upper, left_ref, right_ref, few)
        return hide_if(2, left), hide_if(3, right)

    def band(at, ref, ref_s, first, upper):
        merge_ends(at, *columns_of(ref_s[first : first + step]), *sides(at, upper, left_s, right_s, every))
        marks = hide_if(int(upper), ref[first : first + step])
        beside = [hide_if(int(upper), side) for side in mark_sides(at, upper)]
        merge(at, columns_of(marks), *beside, flag_s)

    for i in range(0, RADIUS, step):
        band(i, top_ref, top_s, i, False)
        band(RADIUS + rows + i, bottom_ref, bottom_s, i, True)

    def middle(i, upper):
        at = pl.multiple_of(i * step, step)
        own = at - RADIUS
        ends = [tile_of(xq_ref, c, rows, own, step) for c in (0, cols // TILE - 1)]
        merge_ends(at, *ends, *sides(at, upper, left_s, right_s, every))
        merge(at, columns_of(mark_ref[pl.ds(own, step)].astype(jnp.float32)), *mark_sides(at, upper), flag_s)
        return 0

    lax.fori_loop(RADIUS // step, half // step, lambda i, _: middle(i, False), 0)
    lax.fori_loop(half // step, (RADIUS + rows) // step, lambda i, _: middle(i, True), 0)

    first_lane = (lax.broadcasted_iota(jnp.int32, (8, LANES), 1) == 0).astype(jnp.bfloat16)
    spans = []
    for c in range(wide_cols // TILE):
        lines = flag_s[c * wide_rows * TILE : (c + 1) * wide_rows * TILE, :]
        spans.append(jnp.where(nt(first_lane, lines) > INVALID / 2, HIDDEN, 0.0))
    tall = rows // TILE
    for c in range(cols // TILE):
        for r in range(tall):
            at = slice(r * TILE * TILE, r * TILE * TILE + 2 * TILE * TILE)
            hide_ref[c * tall + r] = jnp.concatenate([spans[c][:, at], spans[c + 1][:, at]], axis=1)


def column_chunks(channels, half):
    at, end = half * 3 * channels // 2, (half + 1) * 3 * channels // 2
    chunks = []
    while at < end:
        width = min(GROUP - at % GROUP, end - at)
        chunks.append((at, at // channels, at % channels // GROUP, at % GROUP, width))
        at += width
    return chunks


def numbered_chunks(channels, half):
    number, chunks = 0, []
    for chunk in column_chunks(channels, half):
        chunks.append((number, *chunk))
        number += chunk[-1] == GROUP
    return chunks


def project_lines(source, w, parts, factor, put):
    size = source.shape[0] // parts
    for m in range(0, source.shape[0], size):
        y = nt(source[m : m + size, :], w)
        put(slice(m, m + size), (y if factor == 1 else y * factor).astype(jnp.bfloat16))


QUERY_FACTOR = HEAD_DIM ** (-0.5) * LOG2_E


def early_kernel(offsets, place_ref, *refs):
    triples, refs = refs[: len(offsets)], refs[len(offsets) :]
    xq_ref, mid_ref, whole_ref, part_ref, near = refs
    channels = near.shape[1]
    triple_rows = near.shape[0] // len(offsets)
    for j, off in enumerate(offsets):
        to = pl.multiple_of(((place_ref[ROW] ^ off) % len(offsets)) * triple_rows, 16)
        near[pl.ds(to, triple_rows), :] = triples[j][...]

    def run(half):
        for number, at, section, _, _, width in numbered_chunks(channels, half):
            w = near[at - half * near.shape[0] : at - half * near.shape[0] + width, :]

            def put(lines, value, number=number, width=width):
                if width == GROUP:
                    whole_ref[number, lines, :] = value
                else:
                    part_ref[lines, :] = value

            if section == 0:
                project_lines(xq_ref, w, 2, QUERY_FACTOR, put)
            else:
                project_lines(mid_ref, w, 2, 1, put)

    for half in range(2):
        pl.when(place_ref[HALF] == half)(functools.partial(run, half))


def project_rest(half, sections, channels, near_at, far_at, sources, put, groups=None):
    xq_ref, mid_ref, outer_ref = sources
    edge, mid = outer_ref.shape[0] // 2, mid_ref.shape[0]
    for number, at, section, group, lane, width in numbered_chunks(channels, half):
        if section in sections and section > 0 and (groups is None or group in groups):
            w = near_at(at, width)
            for first, to in ((0, 0), (edge, edge + mid)):
                put(section, group, lane, width, slice(to, to + edge), nt(outer_ref[first : first + edge, :], w).astype(jnp.bfloat16))
    for at, section, group, lane, width in column_chunks(channels, 1 - half):
        if section not in sections or (groups is not None and group not in groups):
            continue
        w = far_at(at, width)
        if section == 0:
            project_lines(xq_ref, w, 2, QUERY_FACTOR, functools.partial(put, section, group, lane, width))
            continue
        for first, to in ((0, 0), (edge, edge + mid)):
            put(section, group, lane, width, slice(to, to + edge), nt(outer_ref[first : first + edge, :], w).astype(jnp.bfloat16))

        def put_mid(lines, value, section=section, group=group, lane=lane, width=width):
            put(section, group, lane, width, slice(edge + lines.start, edge + lines.stop), value)

        project_lines(mid_ref, w, 2, 1, put_mid)


def late_kernel(pieces, triple_rows, place_ref, *refs):
    sources, refs = refs[: len(pieces)], refs[len(pieces) :]
    near, whole_ref, part_ref, xq_ref, mid_ref, outer_ref, q_s, k_s, wt, near_sem = refs
    channels = wt.shape[1]
    edge, mid = outer_ref.shape[0] // 2, mid_ref.shape[0]
    for j, (off, start) in enumerate(pieces):
        to = pl.multiple_of((place_ref[ROW] ^ off) * triple_rows + place_ref[STARTS + start], 16)
        wt[pl.ds(to, sources[j].shape[0]), :] = sources[j][...]
    to = pl.multiple_of(place_ref[HALF] * near.shape[0], 16)
    near_copy = pltpu.make_async_copy(near, wt.at[pl.ds(to, near.shape[0]), :], near_sem)
    near_copy.start()

    def put(section, group, lane, width, lines, value):
        if section == 0:
            q_s[group, lines, :] = value
        else:
            k_s[group, lines, lane : lane + width] = value

    def run(half):
        for number, at, section, group, lane, width in numbered_chunks(channels, half):
            if section == 0:
                q_s[group] = whole_ref[number]
            elif section == 1 and width == GROUP:
                k_s[group, edge : edge + mid, :] = whole_ref[number, :mid, :]
            elif section == 1:
                k_s[group, edge : edge + mid, lane : lane + width] = part_ref[...]
        base = half * near.shape[0]
        project_rest(
            half, (0, 1), channels, lambda at, width: near[at - base : at - base + width, :], lambda at, width: wt[at : at + width, :],
            (xq_ref, mid_ref, outer_ref), put,
        )

    for half in range(2):
        pl.when(place_ref[HALF] == half)(functools.partial(run, half))
    near_copy.wait()


def value_kernel(first, place_ref, wt, whole_ref, mid_ref, outer_ref, v_s):
    here = range(first, first + v_s.shape[0])
    channels = wt.shape[1]
    edge, mid = outer_ref.shape[0] // 2, mid_ref.shape[0]

    def put(section, group, lane, width, lines, value):
        v_s[group - first, lines, lane : lane + width] = value

    def run(half):
        for number, at, section, group, lane, width in numbered_chunks(channels, half):
            if section == 2 and group in here:
                v_s[group - first, edge : edge + mid, :] = whole_ref[number, :mid, :]
        weights = lambda at, width: wt[at : at + width, :]
        project_rest(half, (2,), channels, weights, weights, (None, mid_ref, outer_ref), put, here)

    for half in range(2):
        pl.when(place_ref[HALF] == half)(functools.partial(run, half))


def carrier_kernel(offsets, place_ref, wt, *refs):
    shards = len(offsets)
    finals, refs = refs[:shards], refs[shards:]
    summary_ref, wo, kce, vc_s = refs
    per_row = summary_ref.shape[1]
    channels = wt.shape[1]
    groups = channels // GROUP
    heads = channels // HEAD_DIM
    factor = HEAD_DIM ** (-0.5)
    carriers_here = vc_s.shape[0]
    final_rows = wo.shape[0] // shards
    for j, off in enumerate(offsets):
        to = pl.multiple_of((place_ref[ROW] ^ off) * final_rows, 16)
        wo[pl.ds(to, final_rows), :] = finals[j][:final_rows, :]
    carriers = jnp.concatenate([final[final_rows:, :].astype(jnp.float32) for final in finals], axis=0)
    own = carriers[:carriers_here]
    carriers = layer_normalise(carriers).astype(jnp.bfloat16)
    own_norm = layer_normalise(own).astype(jnp.bfloat16)
    qc = (nt(own_norm, wt[:channels, :]) * factor).astype(jnp.bfloat16).astype(jnp.float32)
    kc = nt(carriers, wt[channels : 2 * channels, :]).astype(jnp.bfloat16)
    vc = nt(carriers, wt[2 * channels :, :]).astype(jnp.bfloat16)
    head_of = lax.broadcasted_iota(jnp.int32, (1, channels), 1) // HEAD_DIM
    stacked = jnp.concatenate([jnp.where(head_of == h, qc, 0.0) for h in range(heads)], axis=0)
    e = jnp.exp(nt(stacked.astype(jnp.bfloat16), kc))
    weights = (e / jnp.sum(e, axis=-1, keepdims=True)).astype(jnp.bfloat16)
    o = nn(weights, vc)
    mix = jnp.zeros((carriers_here, channels), jnp.float32)
    for h in range(heads):
        mix = jnp.where(head_of == h, o[h * carriers_here : (h + 1) * carriers_here, :], mix)
    renewed = own + nt(mix.astype(jnp.bfloat16), wo[...])
    for i in range(summary_ref.shape[0]):
        summary_ref[i] = renewed[i * per_row : (i + 1) * per_row, :].astype(jnp.bfloat16)
    fresh = nt(layer_normalise(renewed).astype(jnp.bfloat16), wt[channels:, :]).astype(jnp.bfloat16).astype(jnp.float32)
    vc_s[...] = fresh[:, channels:]
    same = (
        lax.broadcasted_iota(jnp.int32, (GROUP, GROUP), 0) // HEAD_DIM
        == lax.broadcasted_iota(jnp.int32, (GROUP, GROUP), 1) // HEAD_DIM
    )
    windows = kce.shape[0] // groups
    for w in range(windows):
        for g in range(groups):
            kce[w * groups + g] = jnp.where(same, fresh[w : w + 1, g * GROUP : (g + 1) * GROUP], 0.0).astype(jnp.bfloat16)


def attend_kernel(tall, broad, q_s, k_s, v_low, v_high, hide_ref, kce, vc_s, mix_s, pc_s, even_s, odd_s):
    groups, tiles = q_s.shape[0], hide_ref.shape[0]
    heads_in = GROUP // HEAD_DIM
    queries, span = TILE * TILE, 2 * TILE * TILE
    side = PATCH_SIDE // TILE
    wide = (tall + 1) * queries
    qi = lax.broadcasted_iota(jnp.int32, (queries, 2 * span), 0)
    ki = lax.broadcasted_iota(jnp.int32, (queries, 2 * span), 1)
    row_step = (ki % span) // TILE - qi // TILE
    col_step = (ki // span) * TILE + ki % TILE - qi % TILE
    seen = (row_step >= 0) & (row_step <= 2 * RADIUS) & (col_step >= 0) & (col_step <= 2 * RADIUS)
    band = jnp.where(seen, 0.0, HIDDEN)
    group_head = lax.broadcasted_iota(jnp.int32, (1, GROUP), 1) // HEAD_DIM
    only = [jnp.where(group_head == h, 1.0, 0.0).astype(jnp.bfloat16) for h in range(heads_in)]
    in_pair = LANES // HEAD_DIM
    pair_head = lax.broadcasted_iota(jnp.int32, (1, LANES), 1) // HEAD_DIM

    for c in range(broad):
        for w in range(tall // side):
            at = slice((c * tall + w * side) * queries, (c * tall + (w + 1) * side) * queries)
            window = w * (broad // side) + c // side
            for g in range(groups):
                pc_s[at, g * GROUP : (g + 1) * GROUP] = jnp.exp2(nt(q_s[g, at, :], kce[window * groups + g]))

    def keys_at(t):
        k0 = pl.multiple_of(t // tall * wide + t % tall * queries, queries)
        return k0, pl.multiple_of(k0 + wide, queries)

    def scores(t, ref):
        q_at = pl.multiple_of(t * queries, queries)
        k0, k1 = keys_at(t)
        for g in range(groups):
            q = q_s[g, pl.ds(q_at, queries), :]
            qq = jnp.concatenate([q * mask for mask in only], axis=0)
            k = jnp.concatenate([k_s[g, pl.ds(k0, span), :], k_s[g, pl.ds(k1, span), :]], axis=0)
            ref[g] = nt(qq, k)

    def finish(t, ref):
        q_at = pl.multiple_of(t * queries, queries)
        k0, k1 = keys_at(t)
        window = t % tall // side * (broad // side) + t // tall // side
        bias = band + hide_ref[t][0:1, :]
        for g in range(groups):
            p = jnp.exp2(ref[g].reshape(heads_in, queries, 2 * span) + bias[None])
            total = jnp.sum(p, axis=-1, keepdims=True)
            v_ref, at = (v_low, g) if g < v_low.shape[0] else (v_high, g - v_low.shape[0])
            v = jnp.concatenate([v_ref[at, pl.ds(k0, span), :], v_ref[at, pl.ds(k1, span), :]], axis=0)
            o = nn(p.reshape(heads_in * queries, 2 * span).astype(jnp.bfloat16), v).reshape(heads_in, queries, GROUP)
            v_new = vc_s[pl.ds(window, 1), g * GROUP : (g + 1) * GROUP]
            for j in range(GROUP // LANES):
                lanes = slice(j * LANES, (j + 1) * LANES)
                at = slice(g * GROUP + j * LANES, g * GROUP + (j + 1) * LANES)
                kept, kept_total = o[j * in_pair, :, lanes], total[j * in_pair]
                for h in range(1, in_pair):
                    kept = jnp.where(pair_head == h, o[j * in_pair + h, :, lanes], kept)
                    kept_total = jnp.where(pair_head == h, total[j * in_pair + h], kept_total)
                new = pc_s[pl.ds(q_at, queries), at]
                mixed = (kept + new * v_new[:, lanes]) / (kept_total + new)
                mix_s[pl.ds(q_at, queries), at] = mixed.astype(jnp.bfloat16)

    scores(0, even_s)

    def two(i, _):
        t = 2 * i
        scores(t + 1, odd_s)
        finish(t, even_s)
        scores(jnp.minimum(t + 2, tiles - 1), even_s)
        finish(t + 1, odd_s)
        return 0

    lax.fori_loop(0, tiles // 2, two, 0)


def out_kernel(x_ref, mix_s, wo, out_hbm, out_ref, out_sems):
    rows, cols, channels = x_ref.shape
    going = []
    for pair in range(cols // (2 * TILE)):
        both = slice(2 * pair * TILE, 2 * (pair + 1) * TILE)
        for g in range(channels // GROUP):
            at = slice(g * GROUP, (g + 1) * GROUP)
            w = wo[at, :]
            y = nt(mix_s[2 * pair * rows * TILE : 2 * (pair + 1) * rows * TILE, :], w).reshape(2, rows, TILE, GROUP)
            y = jnp.concatenate([y[0], y[1]], axis=1) + x_ref[:, both, at].astype(jnp.float32)
            out_ref[pair, :, :, at] = y.astype(jnp.bfloat16)
        copy = pltpu.make_async_copy(out_ref.at[pair], out_hbm.at[:, both, :], out_sems.at[pair])
        copy.start()
        going.append(copy)
    for copy in going:
        copy.wait()


def local(grid_elements, summary_vectors, triple_projection, final_projection, genuine_flags):
    rows, cols, channels = grid_elements.shape
    wide_rows, wide_cols = rows + 2 * RADIUS, cols + 2 * RADIUS

    triple_t, final_t = triple_projection.T, final_projection.T
    vmem = pl.BlockSpec(memory_space=pltpu.VMEM)
    anywhere = pl.BlockSpec(memory_space=pl.ANY)
    scalars = pl.BlockSpec(memory_space=pltpu.SMEM)
    hbm = pl.BlockSpec(memory_space=pltpu.HBM)
    small = pltpu.CompilerParams(vmem_limit_bytes=8 * 1024 * 1024)
    row_strip = jax.ShapeDtypeStruct((RADIUS, cols, channels), jnp.bfloat16)
    col_strip = jax.ShapeDtypeStruct((wide_rows // 2, 2 * RADIUS, channels), jnp.bfloat16)

    row, col, img = lax.axis_size("row"), lax.axis_size("col"), lax.axis_size("img")
    row_at, col_at, img_at = lax.axis_index("row"), lax.axis_index("col"), lax.axis_index("img")
    row_bits = bits_of(row)
    far, rest = row_bits[0], row_bits[1:]
    piece_rows = triple_t.shape[0] * 5 // (8 * img) // 16 * 16
    relays = img if piece_rows else 0
    starts = [(img_at - k) % img for k in range(relays)] + [jnp.int32(relays)]
    place = [row_at == 0, row_at == row - 1, col_at == 0, col_at == col - 1, row_at % 2 == 0, col_at % 2 == 0, row_at, row_at // far]
    place = jnp.stack([jnp.asarray(p).astype(jnp.int32) for p in place + [start * piece_rows for start in starts]])

    mark, even_rows, odd_rows, x = pl.pallas_call(
        edge_kernel,
        out_shape=(
            pltpu.VMEM((rows, cols, LANES), jnp.bfloat16),
            pltpu.VMEM(row_strip.shape, jnp.bfloat16),
            pltpu.VMEM(row_strip.shape, jnp.bfloat16),
            pltpu.VMEM(grid_elements.shape, jnp.bfloat16),
        ),
        in_specs=[scalars, hbm, hbm],
        out_specs=(vmem,) * 4,
        scratch_shapes=[
            pltpu.VMEM((rows, cols), jnp.int32),
            pltpu.VMEM((rows * cols, cols), jnp.bfloat16),
            pltpu.SemaphoreType.DMA((2,)),
        ],
        compiler_params=small,
        cost_estimate=pl.CostEstimate(flops=1_000_000, bytes_accessed=1_000_000, transcendentals=0),
        name="edge_rows",
    )(place, *(pltpu.with_memory_space_constraint(a, pltpu.HBM) for a in (genuine_flags, grid_elements)))
    mine, last = pl.pallas_call(
        piece_kernel,
        out_shape=(
            pltpu.VMEM((max(piece_rows, 16), channels), jnp.bfloat16),
            pltpu.VMEM((triple_t.shape[0] - relays * piece_rows, channels), jnp.bfloat16),
        ),
        in_specs=[scalars, hbm],
        out_specs=(vmem, vmem),
        scratch_shapes=[pltpu.SemaphoreType.DMA((2,))],
        compiler_params=small,
        cost_estimate=pl.CostEstimate(flops=1_000_000, bytes_accessed=1_000_000, transcendentals=0),
        name="pieces",
    )(place, pltpu.with_memory_space_constraint(after(triple_t, even_rows), pltpu.HBM))
    xq = pl.pallas_call(
        own_kernel,
        out_shape=pltpu.VMEM((rows * cols, channels), jnp.bfloat16),
        in_specs=[vmem],
        out_specs=vmem,
        compiler_params=small,
        cost_estimate=pl.CostEstimate(flops=1_000_000, bytes_accessed=1_000_000, transcendentals=0),
        name="own_norm",
    )(x)
    even_rows, odd_rows = pair_swapped(even_rows, odd_rows, "row")

    far_pieces = []
    if relays:
        first = swapped(mine, "row", far)
    far_last = swapped(after(last, even_rows, odd_rows), "row", far)

    own_rows = summary_vectors.shape[0] * summary_vectors.shape[1]
    carrier_tiles = -(-own_rows // TILE)
    even_cols, odd_cols = pl.pallas_call(
        strip_kernel,
        out_shape=(
            pltpu.VMEM((col_strip.shape[0] + carrier_tiles, *col_strip.shape[1:]), jnp.bfloat16),
            pltpu.VMEM(col_strip.shape, jnp.bfloat16),
        ),
        in_specs=[scalars] + [vmem] * 5,
        out_specs=(vmem,) * 2,
        scratch_shapes=[pltpu.VMEM((carrier_tiles * TILE, channels), jnp.float32)],
        compiler_params=small,
        cost_estimate=pl.CostEstimate(flops=1_000_000, bytes_accessed=2_000_000, transcendentals=0),
        name="edge_columns",
    )(place, x, after(mark, xq), even_rows, odd_rows, summary_vectors)
    even_cols, odd_cols = pair_swapped(even_cols, odd_cols, "col")
    groups = channels // GROUP
    triples, offsets = [triple_t], [0]
    for bit in rest:
        triples = triples + [swapped(p, "row", bit) for p in triples]
        offsets = offsets + [o ^ bit for o in offsets]
    mid = pl.pallas_call(
        middle_kernel,
        out_shape=pltpu.VMEM(((wide_cols // TILE - 2) * wide_rows * TILE, channels), jnp.bfloat16),
        in_specs=[scalars] + [vmem] * 3,
        out_specs=vmem,
        scratch_shapes=[pltpu.VMEM(row_strip.shape, jnp.float32)] * 2,
        compiler_params=small,
        cost_estimate=pl.CostEstimate(flops=1_000_000, bytes_accessed=1_000_000, transcendentals=0),
        name="middle_blocks",
    )(place, xq, even_rows, odd_rows)
    whole, part, near = pl.pallas_call(
        functools.partial(early_kernel, offsets),
        out_shape=(
            pltpu.VMEM((3 * groups // 2, rows * cols, GROUP), jnp.bfloat16),
            pltpu.VMEM((mid.shape[0], GROUP // 2), jnp.bfloat16),
            pltpu.VMEM((3 * channels // 2, channels), jnp.bfloat16),
        ),
        in_specs=[scalars] + [vmem] * (len(triples) + 2),
        out_specs=(vmem,) * 3,
        compiler_params=pltpu.CompilerParams(vmem_limit_bytes=16 * 1024 * 1024),
        cost_estimate=pl.CostEstimate(flops=1_000_000, bytes_accessed=1_000_000, transcendentals=0),
        name="project_early",
    )(place, *triples, xq, mid)

    carriers = pl.pallas_call(
        carrier_pair_kernel,
        out_shape=pltpu.VMEM((2 * own_rows, channels), jnp.bfloat16),
        in_specs=[vmem, anywhere],
        out_specs=vmem,
        scratch_shapes=[
            pltpu.VMEM((carrier_tiles, TILE, channels), jnp.bfloat16),
            pltpu.VMEM((2 * own_rows, channels), jnp.float32),
            pltpu.SemaphoreType.DMA,
        ],
        compiler_params=small,
        cost_estimate=pl.CostEstimate(flops=1_000, bytes_accessed=1_000, transcendentals=0),
        name="carrier_pair",
    )(summary_vectors, after(even_cols, near))
    parts = [carriers]
    for bit in bits_of(col)[:-1]:
        carriers = carriers if len(parts) == 1 else jnp.concatenate(parts, axis=0)
        got = swapped(carriers, "col", 2 * bit - 1)
        parts.append(got)
    if relays:
        first = after(first, even_cols, odd_cols, parts[0])
        others = [lax.ppermute(first, "img", [(i, (i + k) % img) for i in range(img)]) for k in range(1, relays)]
        far_pieces = [first] + others
    far_pieces.append(far_last)

    tiles = (rows // TILE) * (cols // TILE)
    keys = 4 * TILE * TILE
    outer, hide = pl.pallas_call(
        outer_kernel,
        out_shape=(
            pltpu.VMEM((2 * wide_rows * TILE, channels), jnp.bfloat16),
            pltpu.VMEM((tiles, 8, keys), jnp.float32),
        ),
        in_specs=[scalars] + [vmem] * 6,
        out_specs=(vmem,) * 2,
        scratch_shapes=[
            *[pltpu.VMEM((RADIUS, 2 * TILE, channels), jnp.float32)] * 2,
            *[pltpu.VMEM(col_strip.shape, jnp.float32)] * 2,
            *[pltpu.VMEM((*shape.shape[:2], LANES), jnp.float32) for shape in (row_strip, row_strip, col_strip, col_strip)],
            pltpu.VMEM((wide_rows * wide_cols, LANES), jnp.bfloat16),
        ],
        compiler_params=pltpu.CompilerParams(vmem_limit_bytes=12 * 1024 * 1024),
        cost_estimate=pl.CostEstimate(flops=10_000_000, bytes_accessed=6_000_000, transcendentals=1000),
        name="outer_blocks",
    )(place, xq, mark, even_rows, odd_rows, even_cols, odd_cols)

    final_pack = pl.pallas_call(
        pack_kernel,
        out_shape=pltpu.VMEM((final_t.shape[0] + col * own_rows, channels), jnp.bfloat16),
        in_specs=[vmem] * (1 + len(parts)),
        out_specs=vmem,
        compiler_params=small,
        cost_estimate=pl.CostEstimate(flops=1_000, bytes_accessed=1_000, transcendentals=0),
        name="final_pack",
    )(final_t, *parts[:-1], after(parts[-1], outer))
    finals = [final_pack]
    for bit in rest:
        finals = finals + [swapped(p, "row", bit) for p in finals]

    far_final = swapped(final_pack, "row", far)

    far_offsets = [far]
    far_pieces = [[after(piece, outer, got)] for piece in far_pieces]
    for bit in rest:
        far_pieces = [same + [swapped(p, "row", bit) for p in same] for same in far_pieces]
        far_offsets = far_offsets + [o ^ bit for o in far_offsets]

    numbered = [(off, number) for number in range(len(far_pieces)) for off in far_offsets]
    sources = [piece for same in far_pieces for piece in same]
    q, k, wt = pl.pallas_call(
        functools.partial(late_kernel, numbered, triple_t.shape[0]),
        out_shape=(
            jax.ShapeDtypeStruct((groups, rows * cols, GROUP), jnp.bfloat16),
            jax.ShapeDtypeStruct((groups, wide_rows * wide_cols, GROUP), jnp.bfloat16),
            jax.ShapeDtypeStruct((3 * channels, channels), jnp.bfloat16),
        ),
        in_specs=[scalars] + [vmem] * (len(sources) + 6),
        out_specs=(vmem,) * 3,
        scratch_shapes=[pltpu.SemaphoreType.DMA],
        compiler_params=pltpu.CompilerParams(vmem_limit_bytes=VMEM_BYTES),
        cost_estimate=pl.CostEstimate(flops=1_000_000, bytes_accessed=1_000_000, transcendentals=0),
        name="project_late",
    )(place, *sources, near, whole, part, xq, mid, outer)

    def values(first, count, wt):
        return pl.pallas_call(
            functools.partial(value_kernel, first),
            out_shape=jax.ShapeDtypeStruct((count, wide_rows * wide_cols, GROUP), jnp.bfloat16),
            in_specs=[scalars] + [vmem] * 4,
            out_specs=vmem,
            compiler_params=pltpu.CompilerParams(vmem_limit_bytes=VMEM_BYTES),
            cost_estimate=pl.CostEstimate(flops=1_000, bytes_accessed=1_000, transcendentals=0),
            name="values",
        )(place, wt, whole, mid, outer)

    split = groups // 2 + groups % 2
    v_low = values(0, split, wt)
    v_high = values(split, groups - split, after(wt, v_low))

    far_finals = [after(far_final, v_low)]
    for bit in rest:
        far_finals = far_finals + [swapped(p, "row", bit) for p in far_finals]
    finals, offsets = finals + far_finals, offsets + far_offsets
    carriers_here = carrier_tiles * TILE
    summary_result, wo, kce, vc = pl.pallas_call(
        functools.partial(carrier_kernel, offsets),
        out_shape=(
            jax.ShapeDtypeStruct(summary_vectors.shape, jnp.bfloat16),
            jax.ShapeDtypeStruct((channels, channels), jnp.bfloat16),
            jax.ShapeDtypeStruct((own_rows * groups, GROUP, GROUP), jnp.bfloat16),
            jax.ShapeDtypeStruct((carriers_here, channels), jnp.float32),
        ),
        in_specs=[scalars] + [vmem] * (1 + len(finals)),
        out_specs=(vmem,) * 4,
        compiler_params=pltpu.CompilerParams(vmem_limit_bytes=VMEM_BYTES),
        cost_estimate=pl.CostEstimate(flops=500_000_000, bytes_accessed=5_000_000, transcendentals=10_000),
        name="carriers",
    )(place, wt, *finals)

    scores = (groups, GROUP // HEAD_DIM * TILE * TILE, keys)
    mix = pl.pallas_call(
        functools.partial(attend_kernel, rows // TILE, cols // TILE),
        out_shape=jax.ShapeDtypeStruct((rows * cols, channels), jnp.bfloat16),
        in_specs=[vmem] * 7,
        out_specs=vmem,
        scratch_shapes=[
            pltpu.VMEM((rows * cols, channels), jnp.float32),
            pltpu.VMEM(scores, jnp.float32),
            pltpu.VMEM(scores, jnp.float32),
        ],
        compiler_params=pltpu.CompilerParams(vmem_limit_bytes=VMEM_BYTES),
        cost_estimate=pl.CostEstimate(flops=4_000_000_000, bytes_accessed=12_000_000, transcendentals=4_000_000),
        name="attend",
    )(q, k, v_low, v_high, hide, kce, vc)

    out = pl.pallas_call(
        out_kernel,
        out_shape=jax.ShapeDtypeStruct(grid_elements.shape, jnp.bfloat16),
        in_specs=[vmem] * 3,
        out_specs=anywhere,
        scratch_shapes=[
            pltpu.VMEM((cols // (2 * TILE), rows, 2 * TILE, channels), jnp.bfloat16),
            pltpu.SemaphoreType.DMA((cols // (2 * TILE),)),
        ],
        compiler_params=pltpu.CompilerParams(vmem_limit_bytes=VMEM_BYTES),
        cost_estimate=pl.CostEstimate(flops=1_200_000_000, bytes_accessed=6_000_000, transcendentals=0),
        name="out",
    )(x, mix, wo)
    return (out, summary_result)


def solution(mesh):
    placed = (
        P(("img", "row"), "col", None),
        P(("img", "row"), "col", None),
        P(None, "row"),
        P(None, "row"),
        P(("img", "row"), "col"),
    )
    return jax.shard_map(
        local,
        mesh=mesh,
        in_specs=placed,
        out_specs=(P(("img", "row"), "col", None), P(("img", "row"), "col", None)),
        check_vma=False,
    )
```

```python
import functools

import jax
import jax.numpy as jnp
from jax import lax
from jax.experimental import pallas as pl
from jax.experimental.pallas import tpu as pltpu
from jax.sharding import PartitionSpec as P

HEAD_DIM = 64
PATCH_SIDE = 16
RADIUS = 4
TILE = 2 * RADIUS
LANES = 128
GROUP = 256
INVALID = 100.0
HIDDEN = -1e30
LOG2_E = 1.4426950408889634
EVEN_ROW, EVEN_COL, ROW, HALF, STARTS = 4, 5, 6, 7, 8
VMEM_BYTES = 26 * 1024 * 1024


def nt(a, b):
    return lax.dot_general(a, b, (((1,), (1,)), ((), ())), preferred_element_type=jnp.float32)


def nn(a, b):
    return lax.dot_general(a, b, (((1,), (0,)), ((), ())), preferred_element_type=jnp.float32)


def layer_normalise(lines):
    center = lines - jnp.mean(lines, axis=-1, keepdims=True)
    spread = jnp.mean(center * center, axis=-1, keepdims=True)
    return center * lax.rsqrt(spread + 1e-05)


def pair_swapped(even_block, odd_block, axis):
    count = lax.axis_size(axis)
    got = []
    for first, block in ((0, even_block), (1, odd_block)):
        pairs = [(i, i + 1) for i in range(first, count - 1, 2)]
        got.append(lax.ppermute(block, axis, pairs + [(b, a) for a, b in pairs]))
    return got


def swapped(block, axis, bit):
    count = lax.axis_size(axis)
    return lax.ppermute(block, axis, [(i, i ^ bit) for i in range(count)])


def after(block, *others):
    return lax.optimization_barrier((block, *others))[0]


def bits_of(count):
    bits, bit = [], count // 2
    while bit:
        bits.append(bit)
        bit //= 2
    return bits


def marked_lanes(lines, hidden):
    first = jnp.where(hidden, INVALID, lines[:, :, :LANES])
    return jnp.concatenate([first, lines[:, :, LANES:]], axis=2)


def edge_kernel(place_ref, flags_hbm, x_hbm, mark_ref, even_ref, odd_ref, x_ref, *scratch):
    flags_ref, spread, sems = scratch
    rows, cols = flags_ref.shape
    flags_copy = pltpu.make_async_copy(flags_hbm, flags_ref, sems.at[0])
    x_copy = pltpu.make_async_copy(x_hbm, x_ref, sems.at[1])
    flags_copy.start()
    x_copy.start()
    flags_copy.wait()
    row_at = lax.broadcasted_iota(jnp.int32, (cols, cols), 0)
    diagonal = row_at == lax.broadcasted_iota(jnp.int32, (cols, cols), 1)
    for r in range(rows):
        hidden = jnp.where(flags_ref[r : r + 1, :] > 0, 0.0, INVALID)
        spread[r * cols : (r + 1) * cols, :] = jnp.where(diagonal, hidden, 0.0).astype(jnp.bfloat16)
    marks = nn(spread[...], jnp.ones((cols, LANES), jnp.bfloat16)).reshape(rows, cols, LANES)
    mark_ref[...] = marks.astype(jnp.bfloat16)
    x_copy.wait()
    first, last = [
        marked_lanes(x_ref[at].astype(jnp.float32), marks[at] > INVALID / 2)
        for at in (slice(0, RADIUS), slice(rows - RADIUS, rows))
    ]
    even = place_ref[EVEN_ROW] > 0
    even_ref[...] = jnp.where(even, last, first).astype(jnp.bfloat16)
    odd_ref[...] = jnp.where(even, first, last).astype(jnp.bfloat16)


def piece_kernel(place_ref, triple_hbm, mine_ref, last_ref, sems):
    start = pl.multiple_of(place_ref[STARTS], 16)
    last = triple_hbm.shape[0] - last_ref.shape[0]
    copies = [
        pltpu.make_async_copy(triple_hbm.at[pl.ds(start, mine_ref.shape[0]), :], mine_ref, sems.at[0]),
        pltpu.make_async_copy(triple_hbm.at[last:, :], last_ref, sems.at[1]),
    ]
    for copy in copies:
        copy.start()
    for copy in copies:
        copy.wait()


def strip_kernel(place_ref, x_ref, mark_ref, even_rows_ref, odd_rows_ref, carriers_ref, even_ref, odd_ref, carriers_s):
    per_row = carriers_ref.shape[1]
    carriers_s[...] = jnp.zeros_like(carriers_s)
    for i in range(carriers_ref.shape[0]):
        carriers_s[i * per_row : (i + 1) * per_row, :] = carriers_ref[i].astype(jnp.float32)
    for i in range(carriers_s.shape[0] // TILE):
        even_ref[odd_ref.shape[0] + i] = carriers_s[i * TILE : (i + 1) * TILE, :].astype(jnp.bfloat16)
    rows, cols, channels = x_ref.shape
    middle = rows // 2
    low = lax.broadcasted_iota(jnp.int32, (1, TILE, 1), 1) < RADIUS
    even_row, even_col = place_ref[EVEN_ROW] > 0, place_ref[EVEN_COL] > 0
    for lane in range(0, channels, LANES):
        lanes = slice(lane, lane + LANES)
        strips = []
        for columns, last in ((slice(0, TILE), False), (slice(cols - TILE, cols), True)):

            def own(part):
                lines = x_ref[part, columns, lanes].astype(jnp.float32)
                if lane == 0:
                    lines = jnp.where(mark_ref[part, columns, :].astype(jnp.float32) > INVALID / 2, INVALID, lines)
                return lines

            even_rows = even_rows_ref[:, columns, lanes].astype(jnp.float32)
            odd_rows = odd_rows_ref[:, columns, lanes].astype(jnp.float32)
            top, bottom = jnp.where(even_row, odd_rows, even_rows), jnp.where(even_row, even_rows, odd_rows)
            upper = jnp.concatenate([top, own(slice(0, middle))], axis=0)
            lower = jnp.concatenate([own(slice(middle, rows)), bottom], axis=0)
            if last:
                upper = jnp.roll(upper, RADIUS, axis=1)
            else:
                lower = jnp.roll(lower, RADIUS, axis=1)
            strips.append(jnp.where(low, upper, lower))
        first, last = strips
        even_ref[: odd_ref.shape[0], :, lanes] = jnp.where(even_col, last, first).astype(jnp.bfloat16)
        odd_ref[:, :, lanes] = jnp.where(even_col, first, last).astype(jnp.bfloat16)


def carrier_pair_kernel(own_ref, got_hbm, out_ref, got_s, pair_s, sem):
    per_row, here = own_ref.shape[1], own_ref.shape[0] * own_ref.shape[1]
    tiles = got_s.shape[0]
    copy = pltpu.make_async_copy(got_hbm.at[got_hbm.shape[0] - tiles :], got_s, sem)
    copy.start()
    for i in range(own_ref.shape[0]):
        pair_s[i * per_row : (i + 1) * per_row, :] = own_ref[i].astype(jnp.float32)
    copy.wait()
    pair_s[here:, :] = got_s[...].astype(jnp.float32).reshape(tiles * TILE, -1)[:here]
    out_ref[...] = pair_s[...].astype(jnp.bfloat16)


def pack_kernel(final_ref, *refs):
    parts, out_ref = refs[:-1], refs[-1]
    rows = final_ref.shape[0]
    out_ref[:rows, :] = final_ref[...]
    carriers = jnp.concatenate([part[...].astype(jnp.float32) for part in parts], axis=0)
    out_ref[rows:, :] = carriers.astype(jnp.bfloat16)


def own_kernel(x_ref, xq_ref):
    rows, cols, _ = x_ref.shape
    step = 4

    def own(i, _):
        at = pl.multiple_of(i * step, step)
        y = layer_normalise(x_ref[pl.ds(at, step)].astype(jnp.float32))
        for c in range(cols // TILE):
            piece = y[:, c * TILE : (c + 1) * TILE, :].reshape(step * TILE, -1)
            to = pl.multiple_of(c * rows * TILE + at * TILE, step * TILE)
            xq_ref[pl.ds(to, step * TILE), :] = piece.astype(jnp.bfloat16)
        return 0

    lax.fori_loop(0, rows // step, own, 0)


def columns_of(lines):
    return [lines[:, c : c + TILE, :] for c in range(0, lines.shape[1], TILE)]


def tile_of(xq_ref, column, rows, at, step):
    first = pl.multiple_of(column * rows * TILE + at * TILE, step * TILE)
    return xq_ref[pl.ds(first, step * TILE), :].astype(jnp.float32).reshape(step, TILE, -1)


def store_lines(ref, block, wide_rows, at, lines):
    size = lines.shape[0] * TILE
    to = block * wide_rows * TILE + at * TILE
    to = to if isinstance(to, int) else pl.multiple_of(to, size)
    ref[pl.ds(to, size), :] = lines.reshape(size, -1).astype(jnp.bfloat16)


def middle_kernel(place_ref, xq_ref, even_rows_ref, odd_rows_ref, mid_ref, top_s, bottom_s):
    cols = even_rows_ref.shape[1]
    rows, step = xq_ref.shape[0] // cols, 2
    wide_rows = rows + 2 * RADIUS
    flip = place_ref[EVEN_ROW] > 0
    for i in range(0, RADIUS, step):
        a, b = even_rows_ref[i : i + step].astype(jnp.float32), odd_rows_ref[i : i + step].astype(jnp.float32)
        top_s[i : i + step] = layer_normalise(jnp.where(flip, b, a))
        bottom_s[i : i + step] = layer_normalise(jnp.where(flip, a, b))
    low = lax.broadcasted_iota(jnp.int32, (1, TILE, 1), 1) < RADIUS

    def merge(at, blocks):
        moved = [jnp.roll(block, RADIUS, axis=1) for block in blocks]
        for c in range(1, len(blocks)):
            store_lines(mid_ref, c - 1, wide_rows, at, jnp.where(low, moved[c - 1], moved[c]))

    for i in range(0, RADIUS, step):
        merge(i, columns_of(top_s[i : i + step]))
        merge(RADIUS + rows + i, columns_of(bottom_s[i : i + step]))

    def middle(i, _):
        at = pl.multiple_of(i * step, step)
        merge(RADIUS + at, [tile_of(xq_ref, c, rows, at, step) for c in range(cols // TILE)])
        return 0

    lax.fori_loop(0, rows // step, middle, 0)


def outer_kernel(place_ref, xq_ref, mark_ref, even_rows_ref, odd_rows_ref, even_cols_ref, odd_cols_ref, outer_ref, hide_ref, *scratch):
    rows, cols, _ = mark_ref.shape
    wide_rows, wide_cols = rows + 2 * RADIUS, cols + 2 * RADIUS
    half = wide_rows // 2
    step = 2
    top_s, bottom_s, left_s, right_s, top_ref, bottom_ref, left_ref, right_ref, flag_s = scratch
    flip = place_ref[EVEN_ROW] > 0
    a, b = even_rows_ref[...].astype(jnp.float32), odd_rows_ref[...].astype(jnp.float32)
    for lines, out, flags in ((jnp.where(flip, b, a), top_s, top_ref), (jnp.where(flip, a, b), bottom_s, bottom_ref)):
        ends = jnp.concatenate([lines[:, :TILE, :], lines[:, cols - TILE :, :]], axis=1)
        out[...] = layer_normalise(ends)
        flags[...] = lines[:, :, :LANES]
    flip = place_ref[EVEN_COL] > 0
    size = 5
    for i in range(0, odd_cols_ref.shape[0], size):
        a, b = even_cols_ref[i : i + size].astype(jnp.float32), odd_cols_ref[i : i + size].astype(jnp.float32)
        for lines, out, flags in ((jnp.where(flip, b, a), left_s, left_ref), (jnp.where(flip, a, b), right_s, right_ref)):
            out[i : i + size] = layer_normalise(lines)
            flags[i : i + size] = lines[:, :, :LANES]
    low = lax.broadcasted_iota(jnp.int32, (1, TILE, 1), 1) < RADIUS

    def lines_of(ref):
        return ref.astype(jnp.float32)

    def merge(at, blocks, left, right, to_ref):
        moved = [left] + [jnp.roll(block, RADIUS, axis=1) for block in blocks] + [right]
        for c in range(len(blocks) + 1):
            store_lines(to_ref, c, wide_rows, at, jnp.where(low, moved[c], moved[c + 1]))

    def merge_ends(at, first, last, left, right):
        store_lines(outer_ref, 0, wide_rows, at, jnp.where(low, left, jnp.roll(first, RADIUS, axis=1)))
        store_lines(outer_ref, 1, wide_rows, at, jnp.where(low, jnp.roll(last, RADIUS, axis=1), right))

    def sides(at, upper, left_ref, right_ref, lanes):
        if upper:
            at = at - half
            left, right = jnp.roll(lines_of(left_ref[pl.ds(at, step), :, lanes]), RADIUS, axis=1), lines_of(
                right_ref[pl.ds(at, step), :, lanes]
            )
        else:
            left, right = lines_of(left_ref[pl.ds(at, step), :, lanes]), jnp.roll(
                lines_of(right_ref[pl.ds(at, step), :, lanes]), RADIUS, axis=1
            )
        return left, right

    every, few = slice(None), slice(0, LANES)

    def hide_if(border, lines):
        return jnp.where(place_ref[border] > 0, INVALID, lines)

    def mark_sides(at, upper):
        left, right = sides(at, upper, left_ref, right_ref, few)
        return hide_if(2, left), hide_if(3, right)

    def band(at, ref, ref_s, first, upper):
        merge_ends(at, *columns_of(ref_s[first : first + step]), *sides(at, upper, left_s, right_s, every))
        marks = hide_if(int(upper), ref[first : first + step])
        beside = [hide_if(int(upper), side) for side in mark_sides(at, upper)]
        merge(at, columns_of(marks), *beside, flag_s)

    for i in range(0, RADIUS, step):
        band(i, top_ref, top_s, i, False)
        band(RADIUS + rows + i, bottom_ref, bottom_s, i, True)

    def middle(i, upper):
        at = pl.multiple_of(i * step, step)
        own = at - RADIUS
        ends = [tile_of(xq_ref, c, rows, own, step) for c in (0, cols // TILE - 1)]
        merge_ends(at, *ends, *sides(at, upper, left_s, right_s, every))
        merge(at, columns_of(mark_ref[pl.ds(own, step)].astype(jnp.float32)), *mark_sides(at, upper), flag_s)
        return 0

    lax.fori_loop(RADIUS // step, half // step, lambda i, _: middle(i, False), 0)
    lax.fori_loop(half // step, (RADIUS + rows) // step, lambda i, _: middle(i, True), 0)

    first_lane = (lax.broadcasted_iota(jnp.int32, (8, LANES), 1) == 0).astype(jnp.bfloat16)
    spans = []
    for c in range(wide_cols // TILE):
        lines = flag_s[c * wide_rows * TILE : (c + 1) * wide_rows * TILE, :]
        spans.append(jnp.where(nt(first_lane, lines) > INVALID / 2, HIDDEN, 0.0))
    tall = rows // TILE
    for c in range(cols // TILE):
        for r in range(tall):
            at = slice(r * TILE * TILE, r * TILE * TILE + 2 * TILE * TILE)
            hide_ref[c * tall + r] = jnp.concatenate([spans[c][:, at], spans[c + 1][:, at]], axis=1)


def column_chunks(channels, half):
    at, end = half * 3 * channels // 2, (half + 1) * 3 * channels // 2
    chunks = []
    while at < end:
        width = min(GROUP - at % GROUP, end - at)
        chunks.append((at, at // channels, at % channels // GROUP, at % GROUP, width))
        at += width
    return chunks


def numbered_chunks(channels, half):
    number, chunks = 0, []
    for chunk in column_chunks(channels, half):
        chunks.append((number, *chunk))
        number += chunk[-1] == GROUP
    return chunks


def project_lines(source, w, parts, factor, put):
    size = source.shape[0] // parts
    for m in range(0, source.shape[0], size):
        y = nt(source[m : m + size, :], w)
        put(slice(m, m + size), (y if factor == 1 else y * factor).astype(jnp.bfloat16))


QUERY_FACTOR = HEAD_DIM ** (-0.5) * LOG2_E


def early_kernel(offsets, place_ref, *refs):
    triples, refs = refs[: len(offsets)], refs[len(offsets) :]
    xq_ref, mid_ref, whole_ref, part_ref, near = refs
    channels = near.shape[1]
    triple_rows = near.shape[0] // len(offsets)
    for j, off in enumerate(offsets):
        to = pl.multiple_of(((place_ref[ROW] ^ off) % len(offsets)) * triple_rows, 16)
        near[pl.ds(to, triple_rows), :] = triples[j][...]

    def run(half):
        for number, at, section, _, _, width in numbered_chunks(channels, half):
            w = near[at - half * near.shape[0] : at - half * near.shape[0] + width, :]

            def put(lines, value, number=number, width=width):
                if width == GROUP:
                    whole_ref[number, lines, :] = value
                else:
                    part_ref[lines, :] = value

            if section == 0:
                project_lines(xq_ref, w, 2, QUERY_FACTOR, put)
            else:
                project_lines(mid_ref, w, 2, 1, put)

    for half in range(2):
        pl.when(place_ref[HALF] == half)(functools.partial(run, half))


def project_rest(half, sections, channels, near_at, far_at, sources, put, groups=None):
    xq_ref, mid_ref, outer_ref = sources
    edge, mid = outer_ref.shape[0] // 2, mid_ref.shape[0]
    for number, at, section, group, lane, width in numbered_chunks(channels, half):
        if section in sections and section > 0 and (groups is None or group in groups):
            w = near_at(at, width)
            for first, to in ((0, 0), (edge, edge + mid)):
                put(section, group, lane, width, slice(to, to + edge), nt(outer_ref[first : first + edge, :], w).astype(jnp.bfloat16))
    for at, section, group, lane, width in column_chunks(channels, 1 - half):
        if section not in sections or (groups is not None and group not in groups):
            continue
        w = far_at(at, width)
        if section == 0:
            project_lines(xq_ref, w, 2, QUERY_FACTOR, functools.partial(put, section, group, lane, width))
            continue
        for first, to in ((0, 0), (edge, edge + mid)):
            put(section, group, lane, width, slice(to, to + edge), nt(outer_ref[first : first + edge, :], w).astype(jnp.bfloat16))

        def put_mid(lines, value, section=section, group=group, lane=lane, width=width):
            put(section, group, lane, width, slice(edge + lines.start, edge + lines.stop), value)

        project_lines(mid_ref, w, 2, 1, put_mid)


def late_kernel(pieces, triple_rows, place_ref, *refs):
    sources, refs = refs[: len(pieces)], refs[len(pieces) :]
    near, whole_ref, part_ref, xq_ref, mid_ref, outer_ref, q_s, k_s, wt, near_sem = refs
    channels = wt.shape[1]
    edge, mid = outer_ref.shape[0] // 2, mid_ref.shape[0]
    for j, (off, start) in enumerate(pieces):
        to = pl.multiple_of((place_ref[ROW] ^ off) * triple_rows + place_ref[STARTS + start], 16)
        wt[pl.ds(to, sources[j].shape[0]), :] = sources[j][...]
    to = pl.multiple_of(place_ref[HALF] * near.shape[0], 16)
    near_copy = pltpu.make_async_copy(near, wt.at[pl.ds(to, near.shape[0]), :], near_sem)
    near_copy.start()

    def put(section, group, lane, width, lines, value):
        if section == 0:
            q_s[group, lines, :] = value
        else:
            k_s[group, lines, lane : lane + width] = value

    def run(half):
        for number, at, section, group, lane, width in numbered_chunks(channels, half):
            if section == 0:
                q_s[group] = whole_ref[number]
            elif section == 1 and width == GROUP:
                k_s[group, edge : edge + mid, :] = whole_ref[number, :mid, :]
            elif section == 1:
                k_s[group, edge : edge + mid, lane : lane + width] = part_ref[...]
        base = half * near.shape[0]
        project_rest(
            half, (0, 1), channels, lambda at, width: near[at - base : at - base + width, :], lambda at, width: wt[at : at + width, :],
            (xq_ref, mid_ref, outer_ref), put,
        )

    for half in range(2):
        pl.when(place_ref[HALF] == half)(functools.partial(run, half))
    near_copy.wait()


def value_kernel(first, place_ref, wt, whole_ref, mid_ref, outer_ref, v_s):
    here = range(first, first + v_s.shape[0])
    channels = wt.shape[1]
    edge, mid = outer_ref.shape[0] // 2, mid_ref.shape[0]

    def put(section, group, lane, width, lines, value):
        v_s[group - first, lines, lane : lane + width] = value

    def run(half):
        for number, at, section, group, lane, width in numbered_chunks(channels, half):
            if section == 2 and group in here:
                v_s[group - first, edge : edge + mid, :] = whole_ref[number, :mid, :]
        weights = lambda at, width: wt[at : at + width, :]
        project_rest(half, (2,), channels, weights, weights, (None, mid_ref, outer_ref), put, here)

    for half in range(2):
        pl.when(place_ref[HALF] == half)(functools.partial(run, half))


def carrier_kernel(offsets, place_ref, wt, *refs):
    shards = len(offsets)
    finals, refs = refs[:shards], refs[shards:]
    summary_ref, wo, kce, vc_s = refs
    per_row = summary_ref.shape[1]
    channels = wt.shape[1]
    groups = channels // GROUP
    heads = channels // HEAD_DIM
    factor = HEAD_DIM ** (-0.5)
    carriers_here = vc_s.shape[0]
    final_rows = wo.shape[0] // shards
    for j, off in enumerate(offsets):
        to = pl.multiple_of((place_ref[ROW] ^ off) * final_rows, 16)
        wo[pl.ds(to, final_rows), :] = finals[j][:final_rows, :]
    carriers = jnp.concatenate([final[final_rows:, :].astype(jnp.float32) for final in finals], axis=0)
    own = carriers[:carriers_here]
    carriers = layer_normalise(carriers).astype(jnp.bfloat16)
    own_norm = layer_normalise(own).astype(jnp.bfloat16)
    qc = (nt(own_norm, wt[:channels, :]) * factor).astype(jnp.bfloat16).astype(jnp.float32)
    kc = nt(carriers, wt[channels : 2 * channels, :]).astype(jnp.bfloat16)
    vc = nt(carriers, wt[2 * channels :, :]).astype(jnp.bfloat16)
    head_of = lax.broadcasted_iota(jnp.int32, (1, channels), 1) // HEAD_DIM
    stacked = jnp.concatenate([jnp.where(head_of == h, qc, 0.0) for h in range(heads)], axis=0)
    e = jnp.exp(nt(stacked.astype(jnp.bfloat16), kc))
    weights = (e / jnp.sum(e, axis=-1, keepdims=True)).astype(jnp.bfloat16)
    o = nn(weights, vc)
    mix = jnp.zeros((carriers_here, channels), jnp.float32)
    for h in range(heads):
        mix = jnp.where(head_of == h, o[h * carriers_here : (h + 1) * carriers_here, :], mix)
    renewed = own + nt(mix.astype(jnp.bfloat16), wo[...])
    for i in range(summary_ref.shape[0]):
        summary_ref[i] = renewed[i * per_row : (i + 1) * per_row, :].astype(jnp.bfloat16)
    fresh = nt(layer_normalise(renewed).astype(jnp.bfloat16), wt[channels:, :]).astype(jnp.bfloat16).astype(jnp.float32)
    vc_s[...] = fresh[:, channels:]
    same = (
        lax.broadcasted_iota(jnp.int32, (GROUP, GROUP), 0) // HEAD_DIM
        == lax.broadcasted_iota(jnp.int32, (GROUP, GROUP), 1) // HEAD_DIM
    )
    windows = kce.shape[0] // groups
    for w in range(windows):
        for g in range(groups):
            kce[w * groups + g] = jnp.where(same, fresh[w : w + 1, g * GROUP : (g + 1) * GROUP], 0.0).astype(jnp.bfloat16)


def attend_kernel(tall, broad, q_s, k_s, v_low, v_high, hide_ref, kce, vc_s, mix_s, pc_s, even_s, odd_s):
    groups, tiles = q_s.shape[0], hide_ref.shape[0]
    heads_in = GROUP // HEAD_DIM
    queries, span = TILE * TILE, 2 * TILE * TILE
    side = PATCH_SIDE // TILE
    wide = (tall + 1) * queries
    qi = lax.broadcasted_iota(jnp.int32, (queries, 2 * span), 0)
    ki = lax.broadcasted_iota(jnp.int32, (queries, 2 * span), 1)
    row_step = (ki % span) // TILE - qi // TILE
    col_step = (ki // span) * TILE + ki % TILE - qi % TILE
    seen = (row_step >= 0) & (row_step <= 2 * RADIUS) & (col_step >= 0) & (col_step <= 2 * RADIUS)
    band = jnp.where(seen, 0.0, HIDDEN)
    group_head = lax.broadcasted_iota(jnp.int32, (1, GROUP), 1) // HEAD_DIM
    only = [jnp.where(group_head == h, 1.0, 0.0).astype(jnp.bfloat16) for h in range(heads_in)]
    in_pair = LANES // HEAD_DIM
    pair_head = lax.broadcasted_iota(jnp.int32, (1, LANES), 1) // HEAD_DIM

    for c in range(broad):
        for w in range(tall // side):
            at = slice((c * tall + w * side) * queries, (c * tall + (w + 1) * side) * queries)
            window = w * (broad // side) + c // side
            for g in range(groups):
                pc_s[at, g * GROUP : (g + 1) * GROUP] = jnp.exp2(nt(q_s[g, at, :], kce[window * groups + g]))

    def keys_at(t):
        k0 = pl.multiple_of(t // tall * wide + t % tall * queries, queries)
        return k0, pl.multiple_of(k0 + wide, queries)

    def scores(t, ref):
        q_at = pl.multiple_of(t * queries, queries)
        k0, k1 = keys_at(t)
        for g in range(groups):
            q = q_s[g, pl.ds(q_at, queries), :]
            qq = jnp.concatenate([q * mask for mask in only], axis=0)
            k = jnp.concatenate([k_s[g, pl.ds(k0, span), :], k_s[g, pl.ds(k1, span), :]], axis=0)
            ref[g] = nt(qq, k)

    def finish(t, ref):
        q_at = pl.multiple_of(t * queries, queries)
        k0, k1 = keys_at(t)
        window = t % tall // side * (broad // side) + t // tall // side
        bias = band + hide_ref[t][0:1, :]
        for g in range(groups):
            p = jnp.exp2(ref[g].reshape(heads_in, queries, 2 * span) + bias[None])
            total = jnp.sum(p, axis=-1, keepdims=True)
            v_ref, at = (v_low, g) if g < v_low.shape[0] else (v_high, g - v_low.shape[0])
            v = jnp.concatenate([v_ref[at, pl.ds(k0, span), :], v_ref[at, pl.ds(k1, span), :]], axis=0)
            o = nn(p.reshape(heads_in * queries, 2 * span).astype(jnp.bfloat16), v).reshape(heads_in, queries, GROUP)
            v_new = vc_s[pl.ds(window, 1), g * GROUP : (g + 1) * GROUP]
            for j in range(GROUP // LANES):
                lanes = slice(j * LANES, (j + 1) * LANES)
                at = slice(g * GROUP + j * LANES, g * GROUP + (j + 1) * LANES)
                kept, kept_total = o[j * in_pair, :, lanes], total[j * in_pair]
                for h in range(1, in_pair):
                    kept = jnp.where(pair_head == h, o[j * in_pair + h, :, lanes], kept)
                    kept_total = jnp.where(pair_head == h, total[j * in_pair + h], kept_total)
                new = pc_s[pl.ds(q_at, queries), at]
                mixed = (kept + new * v_new[:, lanes]) / (kept_total + new)
                mix_s[pl.ds(q_at, queries), at] = mixed.astype(jnp.bfloat16)

    scores(0, even_s)

    def two(i, _):
        t = 2 * i
        scores(t + 1, odd_s)
        finish(t, even_s)
        scores(jnp.minimum(t + 2, tiles - 1), even_s)
        finish(t + 1, odd_s)
        return 0

    lax.fori_loop(0, tiles // 2, two, 0, unroll=2)


def out_kernel(x_ref, mix_s, wo, out_hbm, out_ref, out_sems):
    rows, cols, channels = x_ref.shape
    going = []
    for pair in range(cols // (2 * TILE)):
        both = slice(2 * pair * TILE, 2 * (pair + 1) * TILE)
        for g in range(channels // GROUP):
            at = slice(g * GROUP, (g + 1) * GROUP)
            w = wo[at, :]
            y = nt(mix_s[2 * pair * rows * TILE : 2 * (pair + 1) * rows * TILE, :], w).reshape(2, rows, TILE, GROUP)
            y = jnp.concatenate([y[0], y[1]], axis=1) + x_ref[:, both, at].astype(jnp.float32)
            out_ref[pair, :, :, at] = y.astype(jnp.bfloat16)
        copy = pltpu.make_async_copy(out_ref.at[pair], out_hbm.at[:, both, :], out_sems.at[pair])
        copy.start()
        going.append(copy)
    for copy in going:
        copy.wait()


def local(grid_elements, summary_vectors, triple_projection, final_projection, genuine_flags):
    rows, cols, channels = grid_elements.shape
    wide_rows, wide_cols = rows + 2 * RADIUS, cols + 2 * RADIUS

    triple_t, final_t = triple_projection.T, final_projection.T
    vmem = pl.BlockSpec(memory_space=pltpu.VMEM)
    anywhere = pl.BlockSpec(memory_space=pl.ANY)
    scalars = pl.BlockSpec(memory_space=pltpu.SMEM)
    hbm = pl.BlockSpec(memory_space=pltpu.HBM)
    small = pltpu.CompilerParams(vmem_limit_bytes=8 * 1024 * 1024)
    row_strip = jax.ShapeDtypeStruct((RADIUS, cols, channels), jnp.bfloat16)
    col_strip = jax.ShapeDtypeStruct((wide_rows // 2, 2 * RADIUS, channels), jnp.bfloat16)

    row, col, img = lax.axis_size("row"), lax.axis_size("col"), lax.axis_size("img")
    row_at, col_at, img_at = lax.axis_index("row"), lax.axis_index("col"), lax.axis_index("img")
    row_bits = bits_of(row)
    far, rest = row_bits[0], row_bits[1:]
    piece_rows = triple_t.shape[0] * 5 // (8 * img) // 16 * 16
    relays = img if piece_rows else 0
    starts = [(img_at - k) % img for k in range(relays)] + [jnp.int32(relays)]
    place = [row_at == 0, row_at == row - 1, col_at == 0, col_at == col - 1, row_at % 2 == 0, col_at % 2 == 0, row_at, row_at // far]
    place = jnp.stack([jnp.asarray(p).astype(jnp.int32) for p in place + [start * piece_rows for start in starts]])

    mark, even_rows, odd_rows, x = pl.pallas_call(
        edge_kernel,
        out_shape=(
            pltpu.VMEM((rows, cols, LANES), jnp.bfloat16),
            pltpu.VMEM(row_strip.shape, jnp.bfloat16),
            pltpu.VMEM(row_strip.shape, jnp.bfloat16),
            pltpu.VMEM(grid_elements.shape, jnp.bfloat16),
        ),
        in_specs=[scalars, hbm, hbm],
        out_specs=(vmem,) * 4,
        scratch_shapes=[
            pltpu.VMEM((rows, cols), jnp.int32),
            pltpu.VMEM((rows * cols, cols), jnp.bfloat16),
            pltpu.SemaphoreType.DMA((2,)),
        ],
        compiler_params=small,
        cost_estimate=pl.CostEstimate(flops=1_000_000, bytes_accessed=1_000_000, transcendentals=0),
        name="edge_rows",
    )(place, *(pltpu.with_memory_space_constraint(a, pltpu.HBM) for a in (genuine_flags, grid_elements)))
    mine, last = pl.pallas_call(
        piece_kernel,
        out_shape=(
            pltpu.VMEM((max(piece_rows, 16), channels), jnp.bfloat16),
            pltpu.VMEM((triple_t.shape[0] - relays * piece_rows, channels), jnp.bfloat16),
        ),
        in_specs=[scalars, hbm],
        out_specs=(vmem, vmem),
        scratch_shapes=[pltpu.SemaphoreType.DMA((2,))],
        compiler_params=small,
        cost_estimate=pl.CostEstimate(flops=1_000_000, bytes_accessed=1_000_000, transcendentals=0),
        name="pieces",
    )(place, pltpu.with_memory_space_constraint(after(triple_t, even_rows), pltpu.HBM))
    xq = pl.pallas_call(
        own_kernel,
        out_shape=pltpu.VMEM((rows * cols, channels), jnp.bfloat16),
        in_specs=[vmem],
        out_specs=vmem,
        compiler_params=small,
        cost_estimate=pl.CostEstimate(flops=1_000_000, bytes_accessed=1_000_000, transcendentals=0),
        name="own_norm",
    )(x)
    even_rows, odd_rows = pair_swapped(even_rows, odd_rows, "row")

    far_pieces = []
    if relays:
        first = swapped(mine, "row", far)
    far_last = swapped(after(last, even_rows, odd_rows), "row", far)

    own_rows = summary_vectors.shape[0] * summary_vectors.shape[1]
    carrier_tiles = -(-own_rows // TILE)
    even_cols, odd_cols = pl.pallas_call(
        strip_kernel,
        out_shape=(
            pltpu.VMEM((col_strip.shape[0] + carrier_tiles, *col_strip.shape[1:]), jnp.bfloat16),
            pltpu.VMEM(col_strip.shape, jnp.bfloat16),
        ),
        in_specs=[scalars] + [vmem] * 5,
        out_specs=(vmem,) * 2,
        scratch_shapes=[pltpu.VMEM((carrier_tiles * TILE, channels), jnp.float32)],
        compiler_params=small,
        cost_estimate=pl.CostEstimate(flops=1_000_000, bytes_accessed=2_000_000, transcendentals=0),
        name="edge_columns",
    )(place, x, after(mark, xq), even_rows, odd_rows, summary_vectors)
    even_cols, odd_cols = pair_swapped(even_cols, odd_cols, "col")
    groups = channels // GROUP
    triples, offsets = [triple_t], [0]
    for bit in rest:
        triples = triples + [swapped(p, "row", bit) for p in triples]
        offsets = offsets + [o ^ bit for o in offsets]
    mid = pl.pallas_call(
        middle_kernel,
        out_shape=pltpu.VMEM(((wide_cols // TILE - 2) * wide_rows * TILE, channels), jnp.bfloat16),
        in_specs=[scalars] + [vmem] * 3,
        out_specs=vmem,
        scratch_shapes=[pltpu.VMEM(row_strip.shape, jnp.float32)] * 2,
        compiler_params=small,
        cost_estimate=pl.CostEstimate(flops=1_000_000, bytes_accessed=1_000_000, transcendentals=0),
        name="middle_blocks",
    )(place, xq, even_rows, odd_rows)
    whole, part, near = pl.pallas_call(
        functools.partial(early_kernel, offsets),
        out_shape=(
            pltpu.VMEM((3 * groups // 2, rows * cols, GROUP), jnp.bfloat16),
            pltpu.VMEM((mid.shape[0], GROUP // 2), jnp.bfloat16),
            pltpu.VMEM((3 * channels // 2, channels), jnp.bfloat16),
        ),
        in_specs=[scalars] + [vmem] * (len(triples) + 2),
        out_specs=(vmem,) * 3,
        compiler_params=pltpu.CompilerParams(vmem_limit_bytes=16 * 1024 * 1024),
        cost_estimate=pl.CostEstimate(flops=1_000_000, bytes_accessed=1_000_000, transcendentals=0),
        name="project_early",
    )(place, *triples, xq, mid)

    carriers = pl.pallas_call(
        carrier_pair_kernel,
        out_shape=pltpu.VMEM((2 * own_rows, channels), jnp.bfloat16),
        in_specs=[vmem, anywhere],
        out_specs=vmem,
        scratch_shapes=[
            pltpu.VMEM((carrier_tiles, TILE, channels), jnp.bfloat16),
            pltpu.VMEM((2 * own_rows, channels), jnp.float32),
            pltpu.SemaphoreType.DMA,
        ],
        compiler_params=small,
        cost_estimate=pl.CostEstimate(flops=1_000, bytes_accessed=1_000, transcendentals=0),
        name="carrier_pair",
    )(summary_vectors, after(even_cols, near))
    parts = [carriers]
    for bit in bits_of(col)[:-1]:
        carriers = carriers if len(parts) == 1 else jnp.concatenate(parts, axis=0)
        got = swapped(carriers, "col", 2 * bit - 1)
        parts.append(got)
    if relays:
        first = after(first, even_cols, odd_cols, parts[0])
        others = [lax.ppermute(first, "img", [(i, (i + k) % img) for i in range(img)]) for k in range(1, relays)]
        far_pieces = [first] + others
    far_pieces.append(far_last)

    tiles = (rows // TILE) * (cols // TILE)
    keys = 4 * TILE * TILE
    outer, hide = pl.pallas_call(
        outer_kernel,
        out_shape=(
            pltpu.VMEM((2 * wide_rows * TILE, channels), jnp.bfloat16),
            pltpu.VMEM((tiles, 8, keys), jnp.float32),
        ),
        in_specs=[scalars] + [vmem] * 6,
        out_specs=(vmem,) * 2,
        scratch_shapes=[
            *[pltpu.VMEM((RADIUS, 2 * TILE, channels), jnp.float32)] * 2,
            *[pltpu.VMEM(col_strip.shape, jnp.float32)] * 2,
            *[pltpu.VMEM((*shape.shape[:2], LANES), jnp.float32) for shape in (row_strip, row_strip, col_strip, col_strip)],
            pltpu.VMEM((wide_rows * wide_cols, LANES), jnp.bfloat16),
        ],
        compiler_params=pltpu.CompilerParams(vmem_limit_bytes=12 * 1024 * 1024),
        cost_estimate=pl.CostEstimate(flops=10_000_000, bytes_accessed=6_000_000, transcendentals=1000),
        name="outer_blocks",
    )(place, xq, mark, even_rows, odd_rows, even_cols, odd_cols)

    final_pack = pl.pallas_call(
        pack_kernel,
        out_shape=pltpu.VMEM((final_t.shape[0] + col * own_rows, channels), jnp.bfloat16),
        in_specs=[vmem] * (1 + len(parts)),
        out_specs=vmem,
        compiler_params=small,
        cost_estimate=pl.CostEstimate(flops=1_000, bytes_accessed=1_000, transcendentals=0),
        name="final_pack",
    )(final_t, *parts[:-1], after(parts[-1], outer))
    finals = [final_pack]
    for bit in rest:
        finals = finals + [swapped(p, "row", bit) for p in finals]

    far_final = swapped(final_pack, "row", far)

    far_offsets = [far]
    far_pieces = [[after(piece, outer, got)] for piece in far_pieces]
    for bit in rest:
        far_pieces = [same + [swapped(p, "row", bit) for p in same] for same in far_pieces]
        far_offsets = far_offsets + [o ^ bit for o in far_offsets]

    numbered = [(off, number) for number in range(len(far_pieces)) for off in far_offsets]
    sources = [piece for same in far_pieces for piece in same]
    q, k, wt = pl.pallas_call(
        functools.partial(late_kernel, numbered, triple_t.shape[0]),
        out_shape=(
            jax.ShapeDtypeStruct((groups, rows * cols, GROUP), jnp.bfloat16),
            jax.ShapeDtypeStruct((groups, wide_rows * wide_cols, GROUP), jnp.bfloat16),
            jax.ShapeDtypeStruct((3 * channels, channels), jnp.bfloat16),
        ),
        in_specs=[scalars] + [vmem] * (len(sources) + 6),
        out_specs=(vmem,) * 3,
        scratch_shapes=[pltpu.SemaphoreType.DMA],
        compiler_params=pltpu.CompilerParams(vmem_limit_bytes=VMEM_BYTES),
        cost_estimate=pl.CostEstimate(flops=1_000_000, bytes_accessed=1_000_000, transcendentals=0),
        name="project_late",
    )(place, *sources, near, whole, part, xq, mid, outer)

    def values(first, count, wt):
        return pl.pallas_call(
            functools.partial(value_kernel, first),
            out_shape=jax.ShapeDtypeStruct((count, wide_rows * wide_cols, GROUP), jnp.bfloat16),
            in_specs=[scalars] + [vmem] * 4,
            out_specs=vmem,
            compiler_params=pltpu.CompilerParams(vmem_limit_bytes=VMEM_BYTES),
            cost_estimate=pl.CostEstimate(flops=1_000, bytes_accessed=1_000, transcendentals=0),
            name="values",
        )(place, wt, whole, mid, outer)

    split = groups // 2 + groups % 2
    v_low = values(0, split, wt)
    v_high = values(split, groups - split, after(wt, v_low))

    far_finals = [after(far_final, v_low)]
    for bit in rest:
        far_finals = far_finals + [swapped(p, "row", bit) for p in far_finals]
    finals, offsets = finals + far_finals, offsets + far_offsets
    carriers_here = carrier_tiles * TILE
    summary_result, wo, kce, vc = pl.pallas_call(
        functools.partial(carrier_kernel, offsets),
        out_shape=(
            jax.ShapeDtypeStruct(summary_vectors.shape, jnp.bfloat16),
            jax.ShapeDtypeStruct((channels, channels), jnp.bfloat16),
            jax.ShapeDtypeStruct((own_rows * groups, GROUP, GROUP), jnp.bfloat16),
            jax.ShapeDtypeStruct((carriers_here, channels), jnp.float32),
        ),
        in_specs=[scalars] + [vmem] * (1 + len(finals)),
        out_specs=(vmem,) * 4,
        compiler_params=pltpu.CompilerParams(vmem_limit_bytes=VMEM_BYTES),
        cost_estimate=pl.CostEstimate(flops=500_000_000, bytes_accessed=5_000_000, transcendentals=10_000),
        name="carriers",
    )(place, wt, *finals)

    scores = (groups, GROUP // HEAD_DIM * TILE * TILE, keys)
    mix = pl.pallas_call(
        functools.partial(attend_kernel, rows // TILE, cols // TILE),
        out_shape=jax.ShapeDtypeStruct((rows * cols, channels), jnp.bfloat16),
        in_specs=[vmem] * 7,
        out_specs=vmem,
        scratch_shapes=[
            pltpu.VMEM((rows * cols, channels), jnp.float32),
            pltpu.VMEM(scores, jnp.float32),
            pltpu.VMEM(scores, jnp.float32),
        ],
        compiler_params=pltpu.CompilerParams(vmem_limit_bytes=VMEM_BYTES),
        cost_estimate=pl.CostEstimate(flops=4_000_000_000, bytes_accessed=12_000_000, transcendentals=4_000_000),
        name="attend",
    )(q, k, v_low, v_high, hide, kce, vc)

    out = pl.pallas_call(
        out_kernel,
        out_shape=jax.ShapeDtypeStruct(grid_elements.shape, jnp.bfloat16),
        in_specs=[vmem] * 3,
        out_specs=anywhere,
        scratch_shapes=[
            pltpu.VMEM((cols // (2 * TILE), rows, 2 * TILE, channels), jnp.bfloat16),
            pltpu.SemaphoreType.DMA((cols // (2 * TILE),)),
        ],
        compiler_params=pltpu.CompilerParams(vmem_limit_bytes=VMEM_BYTES),
        cost_estimate=pl.CostEstimate(flops=1_200_000_000, bytes_accessed=6_000_000, transcendentals=0),
        name="out",
    )(x, mix, wo)
    return (out, summary_result)


def solution(mesh):
    placed = (
        P(("img", "row"), "col", None),
        P(("img", "row"), "col", None),
        P(None, "row"),
        P(None, "row"),
        P(("img", "row"), "col"),
    )
    return jax.shard_map(
        local,
        mesh=mesh,
        in_specs=placed,
        out_specs=(P(("img", "row"), "col", None), P(("img", "row"), "col", None)),
        check_vma=False,
    )
```

```python
import functools

import jax
import jax.numpy as jnp
from jax import lax
from jax.experimental import pallas as pl
from jax.experimental.pallas import tpu as pltpu
from jax.sharding import PartitionSpec as P

HEAD_DIM = 64
PATCH_SIDE = 16
RADIUS = 4
TILE = 2 * RADIUS
LANES = 128
GROUP = 256
INVALID = 100.0
HIDDEN = -1e30
LOG2_E = 1.4426950408889634
EVEN_ROW, EVEN_COL, ROW, HALF, STARTS = 4, 5, 6, 7, 8
VMEM_BYTES = 26 * 1024 * 1024


def nt(a, b):
    return lax.dot_general(a, b, (((1,), (1,)), ((), ())), preferred_element_type=jnp.float32)


def nn(a, b):
    return lax.dot_general(a, b, (((1,), (0,)), ((), ())), preferred_element_type=jnp.float32)


def layer_normalise(lines):
    center = lines - jnp.mean(lines, axis=-1, keepdims=True)
    spread = jnp.mean(center * center, axis=-1, keepdims=True)
    return center * lax.rsqrt(spread + 1e-05)


def pair_swapped(even_block, odd_block, axis):
    count = lax.axis_size(axis)
    got = []
    for first, block in ((0, even_block), (1, odd_block)):
        pairs = [(i, i + 1) for i in range(first, count - 1, 2)]
        got.append(lax.ppermute(block, axis, pairs + [(b, a) for a, b in pairs]))
    return got


def swapped(block, axis, bit):
    count = lax.axis_size(axis)
    return lax.ppermute(block, axis, [(i, i ^ bit) for i in range(count)])


def after(block, *others):
    return lax.optimization_barrier((block, *others))[0]


def bits_of(count):
    bits, bit = [], count // 2
    while bit:
        bits.append(bit)
        bit //= 2
    return bits


def marked_lanes(lines, hidden):
    first = jnp.where(hidden, INVALID, lines[:, :, :LANES])
    return jnp.concatenate([first, lines[:, :, LANES:]], axis=2)


def edge_kernel(place_ref, flags_hbm, x_hbm, mark_ref, even_ref, odd_ref, x_ref, *scratch):
    flags_ref, spread, sems = scratch
    rows, cols = flags_ref.shape
    flags_copy = pltpu.make_async_copy(flags_hbm, flags_ref, sems.at[0])
    x_copy = pltpu.make_async_copy(x_hbm, x_ref, sems.at[1])
    flags_copy.start()
    x_copy.start()
    flags_copy.wait()
    row_at = lax.broadcasted_iota(jnp.int32, (cols, cols), 0)
    diagonal = row_at == lax.broadcasted_iota(jnp.int32, (cols, cols), 1)
    for r in range(rows):
        hidden = jnp.where(flags_ref[r : r + 1, :] > 0, 0.0, INVALID)
        spread[r * cols : (r + 1) * cols, :] = jnp.where(diagonal, hidden, 0.0).astype(jnp.bfloat16)
    marks = nn(spread[...], jnp.ones((cols, LANES), jnp.bfloat16)).reshape(rows, cols, LANES)
    mark_ref[...] = marks.astype(jnp.bfloat16)
    x_copy.wait()
    first, last = [
        marked_lanes(x_ref[at].astype(jnp.float32), marks[at] > INVALID / 2)
        for at in (slice(0, RADIUS), slice(rows - RADIUS, rows))
    ]
    even = place_ref[EVEN_ROW] > 0
    even_ref[...] = jnp.where(even, last, first).astype(jnp.bfloat16)
    odd_ref[...] = jnp.where(even, first, last).astype(jnp.bfloat16)


def piece_kernel(place_ref, triple_hbm, mine_ref, last_ref, sems):
    start = pl.multiple_of(place_ref[STARTS], 16)
    last = triple_hbm.shape[0] - last_ref.shape[0]
    copies = [
        pltpu.make_async_copy(triple_hbm.at[pl.ds(start, mine_ref.shape[0]), :], mine_ref, sems.at[0]),
        pltpu.make_async_copy(triple_hbm.at[last:, :], last_ref, sems.at[1]),
    ]
    for copy in copies:
        copy.start()
    for copy in copies:
        copy.wait()


def strip_kernel(place_ref, x_ref, mark_ref, even_rows_ref, odd_rows_ref, carriers_ref, even_ref, odd_ref, carriers_s):
    per_row = carriers_ref.shape[1]
    carriers_s[...] = jnp.zeros_like(carriers_s)
    for i in range(carriers_ref.shape[0]):
        carriers_s[i * per_row : (i + 1) * per_row, :] = carriers_ref[i].astype(jnp.float32)
    for i in range(carriers_s.shape[0] // TILE):
        even_ref[odd_ref.shape[0] + i] = carriers_s[i * TILE : (i + 1) * TILE, :].astype(jnp.bfloat16)
    rows, cols, channels = x_ref.shape
    middle = rows // 2
    low = lax.broadcasted_iota(jnp.int32, (1, TILE, 1), 1) < RADIUS
    even_row, even_col = place_ref[EVEN_ROW] > 0, place_ref[EVEN_COL] > 0
    for lane in range(0, channels, LANES):
        lanes = slice(lane, lane + LANES)
        strips = []
        for columns, last in ((slice(0, TILE), False), (slice(cols - TILE, cols), True)):

            def own(part):
                lines = x_ref[part, columns, lanes].astype(jnp.float32)
                if lane == 0:
                    lines = jnp.where(mark_ref[part, columns, :].astype(jnp.float32) > INVALID / 2, INVALID, lines)
                return lines

            even_rows = even_rows_ref[:, columns, lanes].astype(jnp.float32)
            odd_rows = odd_rows_ref[:, columns, lanes].astype(jnp.float32)
            top, bottom = jnp.where(even_row, odd_rows, even_rows), jnp.where(even_row, even_rows, odd_rows)
            upper = jnp.concatenate([top, own(slice(0, middle))], axis=0)
            lower = jnp.concatenate([own(slice(middle, rows)), bottom], axis=0)
            if last:
                upper = jnp.roll(upper, RADIUS, axis=1)
            else:
                lower = jnp.roll(lower, RADIUS, axis=1)
            strips.append(jnp.where(low, upper, lower))
        first, last = strips
        even_ref[: odd_ref.shape[0], :, lanes] = jnp.where(even_col, last, first).astype(jnp.bfloat16)
        odd_ref[:, :, lanes] = jnp.where(even_col, first, last).astype(jnp.bfloat16)


def carrier_pair_kernel(own_ref, got_hbm, out_ref, got_s, pair_s, sem):
    per_row, here = own_ref.shape[1], own_ref.shape[0] * own_ref.shape[1]
    tiles = got_s.shape[0]
    copy = pltpu.make_async_copy(got_hbm.at[got_hbm.shape[0] - tiles :], got_s, sem)
    copy.start()
    for i in range(own_ref.shape[0]):
        pair_s[i * per_row : (i + 1) * per_row, :] = own_ref[i].astype(jnp.float32)
    copy.wait()
    pair_s[here:, :] = got_s[...].astype(jnp.float32).reshape(tiles * TILE, -1)[:here]
    out_ref[...] = pair_s[...].astype(jnp.bfloat16)


def pack_kernel(final_ref, *refs):
    parts, out_ref = refs[:-1], refs[-1]
    rows = final_ref.shape[0]
    out_ref[:rows, :] = final_ref[...]
    carriers = jnp.concatenate([part[...].astype(jnp.float32) for part in parts], axis=0)
    out_ref[rows:, :] = carriers.astype(jnp.bfloat16)


def own_kernel(x_ref, xq_ref):
    rows, cols, _ = x_ref.shape
    step = 4

    def own(i, _):
        at = pl.multiple_of(i * step, step)
        y = layer_normalise(x_ref[pl.ds(at, step)].astype(jnp.float32))
        for c in range(cols // TILE):
            piece = y[:, c * TILE : (c + 1) * TILE, :].reshape(step * TILE, -1)
            to = pl.multiple_of(c * rows * TILE + at * TILE, step * TILE)
            xq_ref[pl.ds(to, step * TILE), :] = piece.astype(jnp.bfloat16)
        return 0

    lax.fori_loop(0, rows // step, own, 0)


def columns_of(lines):
    return [lines[:, c : c + TILE, :] for c in range(0, lines.shape[1], TILE)]


def tile_of(xq_ref, column, rows, at, step):
    first = pl.multiple_of(column * rows * TILE + at * TILE, step * TILE)
    return xq_ref[pl.ds(first, step * TILE), :].astype(jnp.float32).reshape(step, TILE, -1)


def store_lines(ref, block, wide_rows, at, lines):
    size = lines.shape[0] * TILE
    to = block * wide_rows * TILE + at * TILE
    to = to if isinstance(to, int) else pl.multiple_of(to, size)
    ref[pl.ds(to, size), :] = lines.reshape(size, -1).astype(jnp.bfloat16)


def middle_kernel(place_ref, xq_ref, even_rows_ref, odd_rows_ref, mid_ref, top_s, bottom_s):
    cols = even_rows_ref.shape[1]
    rows, step = xq_ref.shape[0] // cols, 2
    wide_rows = rows + 2 * RADIUS
    flip = place_ref[EVEN_ROW] > 0
    for i in range(0, RADIUS, step):
        a, b = even_rows_ref[i : i + step].astype(jnp.float32), odd_rows_ref[i : i + step].astype(jnp.float32)
        top_s[i : i + step] = layer_normalise(jnp.where(flip, b, a))
        bottom_s[i : i + step] = layer_normalise(jnp.where(flip, a, b))
    low = lax.broadcasted_iota(jnp.int32, (1, TILE, 1), 1) < RADIUS

    def merge(at, blocks):
        moved = [jnp.roll(block, RADIUS, axis=1) for block in blocks]
        for c in range(1, len(blocks)):
            store_lines(mid_ref, c - 1, wide_rows, at, jnp.where(low, moved[c - 1], moved[c]))

    for i in range(0, RADIUS, step):
        merge(i, columns_of(top_s[i : i + step]))
        merge(RADIUS + rows + i, columns_of(bottom_s[i : i + step]))

    def middle(i, _):
        at = pl.multiple_of(i * step, step)
        merge(RADIUS + at, [tile_of(xq_ref, c, rows, at, step) for c in range(cols // TILE)])
        return 0

    lax.fori_loop(0, rows // step, middle, 0)


def outer_kernel(place_ref, xq_ref, mark_ref, even_rows_ref, odd_rows_ref, even_cols_ref, odd_cols_ref, outer_ref, hide_ref, *scratch):
    rows, cols, _ = mark_ref.shape
    wide_rows, wide_cols = rows + 2 * RADIUS, cols + 2 * RADIUS
    half = wide_rows // 2
    step = 2
    top_s, bottom_s, left_s, right_s, top_ref, bottom_ref, left_ref, right_ref, flag_s = scratch
    flip = place_ref[EVEN_ROW] > 0
    a, b = even_rows_ref[...].astype(jnp.float32), odd_rows_ref[...].astype(jnp.float32)
    for lines, out, flags in ((jnp.where(flip, b, a), top_s, top_ref), (jnp.where(flip, a, b), bottom_s, bottom_ref)):
        ends = jnp.concatenate([lines[:, :TILE, :], lines[:, cols - TILE :, :]], axis=1)
        out[...] = layer_normalise(ends)
        flags[...] = lines[:, :, :LANES]
    flip = place_ref[EVEN_COL] > 0
    size = 5
    for i in range(0, odd_cols_ref.shape[0], size):
        a, b = even_cols_ref[i : i + size].astype(jnp.float32), odd_cols_ref[i : i + size].astype(jnp.float32)
        for lines, out, flags in ((jnp.where(flip, b, a), left_s, left_ref), (jnp.where(flip, a, b), right_s, right_ref)):
            out[i : i + size] = layer_normalise(lines)
            flags[i : i + size] = lines[:, :, :LANES]
    low = lax.broadcasted_iota(jnp.int32, (1, TILE, 1), 1) < RADIUS

    def lines_of(ref):
        return ref.astype(jnp.float32)

    def merge(at, blocks, left, right, to_ref):
        moved = [left] + [jnp.roll(block, RADIUS, axis=1) for block in blocks] + [right]
        for c in range(len(blocks) + 1):
            store_lines(to_ref, c, wide_rows, at, jnp.where(low, moved[c], moved[c + 1]))

    def merge_ends(at, first, last, left, right):
        store_lines(outer_ref, 0, wide_rows, at, jnp.where(low, left, jnp.roll(first, RADIUS, axis=1)))
        store_lines(outer_ref, 1, wide_rows, at, jnp.where(low, jnp.roll(last, RADIUS, axis=1), right))

    def sides(at, upper, left_ref, right_ref, lanes):
        if upper:
            at = at - half
            left, right = jnp.roll(lines_of(left_ref[pl.ds(at, step), :, lanes]), RADIUS, axis=1), lines_of(
                right_ref[pl.ds(at, step), :, lanes]
            )
        else:
            left, right = lines_of(left_ref[pl.ds(at, step), :, lanes]), jnp.roll(
                lines_of(right_ref[pl.ds(at, step), :, lanes]), RADIUS, axis=1
            )
        return left, right

    every, few = slice(None), slice(0, LANES)

    def hide_if(border, lines):
        return jnp.where(place_ref[border] > 0, INVALID, lines)

    def mark_sides(at, upper):
        left, right = sides(at, upper, left_ref, right_ref, few)
        return hide_if(2, left), hide_if(3, right)

    def band(at, ref, ref_s, first, upper):
        merge_ends(at, *columns_of(ref_s[first : first + step]), *sides(at, upper, left_s, right_s, every))
        marks = hide_if(int(upper), ref[first : first + step])
        beside = [hide_if(int(upper), side) for side in mark_sides(at, upper)]
        merge(at, columns_of(marks), *beside, flag_s)

    for i in range(0, RADIUS, step):
        band(i, top_ref, top_s, i, False)
        band(RADIUS + rows + i, bottom_ref, bottom_s, i, True)

    def middle(i, upper):
        at = pl.multiple_of(i * step, step)
        own = at - RADIUS
        ends = [tile_of(xq_ref, c, rows, own, step) for c in (0, cols // TILE - 1)]
        merge_ends(at, *ends, *sides(at, upper, left_s, right_s, every))
        merge(at, columns_of(mark_ref[pl.ds(own, step)].astype(jnp.float32)), *mark_sides(at, upper), flag_s)
        return 0

    lax.fori_loop(RADIUS // step, half // step, lambda i, _: middle(i, False), 0)
    lax.fori_loop(half // step, (RADIUS + rows) // step, lambda i, _: middle(i, True), 0)

    first_lane = (lax.broadcasted_iota(jnp.int32, (8, LANES), 1) == 0).astype(jnp.bfloat16)
    spans = []
    for c in range(wide_cols // TILE):
        lines = flag_s[c * wide_rows * TILE : (c + 1) * wide_rows * TILE, :]
        spans.append(jnp.where(nt(first_lane, lines) > INVALID / 2, HIDDEN, 0.0))
    tall = rows // TILE
    for c in range(cols // TILE):
        for r in range(tall):
            at = slice(r * TILE * TILE, r * TILE * TILE + 2 * TILE * TILE)
            hide_ref[c * tall + r] = jnp.concatenate([spans[c][:, at], spans[c + 1][:, at]], axis=1)


def column_chunks(channels, half):
    at, end = half * 3 * channels // 2, (half + 1) * 3 * channels // 2
    chunks = []
    while at < end:
        width = min(GROUP - at % GROUP, end - at)
        chunks.append((at, at // channels, at % channels // GROUP, at % GROUP, width))
        at += width
    return chunks


def numbered_chunks(channels, half):
    number, chunks = 0, []
    for chunk in column_chunks(channels, half):
        chunks.append((number, *chunk))
        number += chunk[-1] == GROUP
    return chunks


def project_lines(source, w, parts, factor, put):
    size = source.shape[0] // parts
    for m in range(0, source.shape[0], size):
        y = nt(source[m : m + size, :], w)
        put(slice(m, m + size), (y if factor == 1 else y * factor).astype(jnp.bfloat16))


QUERY_FACTOR = HEAD_DIM ** (-0.5) * LOG2_E


def early_kernel(offsets, place_ref, *refs):
    triples, refs = refs[: len(offsets)], refs[len(offsets) :]
    xq_ref, mid_ref, whole_ref, part_ref, near = refs
    channels = near.shape[1]
    triple_rows = near.shape[0] // len(offsets)
    for j, off in enumerate(offsets):
        to = pl.multiple_of(((place_ref[ROW] ^ off) % len(offsets)) * triple_rows, 16)
        near[pl.ds(to, triple_rows), :] = triples[j][...]

    def run(half):
        for number, at, section, _, _, width in numbered_chunks(channels, half):
            w = near[at - half * near.shape[0] : at - half * near.shape[0] + width, :]

            def put(lines, value, number=number, width=width):
                if width == GROUP:
                    whole_ref[number, lines, :] = value
                else:
                    part_ref[lines, :] = value

            if section == 0:
                project_lines(xq_ref, w, 2, QUERY_FACTOR, put)
            else:
                project_lines(mid_ref, w, 2, 1, put)

    for half in range(2):
        pl.when(place_ref[HALF] == half)(functools.partial(run, half))


def project_rest(half, sections, channels, near_at, far_at, sources, put, groups=None):
    xq_ref, mid_ref, outer_ref = sources
    edge, mid = outer_ref.shape[0] // 2, mid_ref.shape[0]
    for number, at, section, group, lane, width in numbered_chunks(channels, half):
        if section in sections and section > 0 and (groups is None or group in groups):
            w = near_at(at, width)
            for first, to in ((0, 0), (edge, edge + mid)):
                put(section, group, lane, width, slice(to, to + edge), nt(outer_ref[first : first + edge, :], w).astype(jnp.bfloat16))
    for at, section, group, lane, width in column_chunks(channels, 1 - half):
        if section not in sections or (groups is not None and group not in groups):
            continue
        w = far_at(at, width)
        if section == 0:
            project_lines(xq_ref, w, 2, QUERY_FACTOR, functools.partial(put, section, group, lane, width))
            continue
        for first, to in ((0, 0), (edge, edge + mid)):
            put(section, group, lane, width, slice(to, to + edge), nt(outer_ref[first : first + edge, :], w).astype(jnp.bfloat16))

        def put_mid(lines, value, section=section, group=group, lane=lane, width=width):
            put(section, group, lane, width, slice(edge + lines.start, edge + lines.stop), value)

        project_lines(mid_ref, w, 2, 1, put_mid)


def late_kernel(pieces, triple_rows, place_ref, *refs):
    sources, refs = refs[: len(pieces)], refs[len(pieces) :]
    near, whole_ref, part_ref, xq_ref, mid_ref, outer_ref, q_s, k_s, wt, near_sem = refs
    channels = wt.shape[1]
    edge, mid = outer_ref.shape[0] // 2, mid_ref.shape[0]
    for j, (off, start) in enumerate(pieces):
        to = pl.multiple_of((place_ref[ROW] ^ off) * triple_rows + place_ref[STARTS + start], 16)
        wt[pl.ds(to, sources[j].shape[0]), :] = sources[j][...]
    to = pl.multiple_of(place_ref[HALF] * near.shape[0], 16)
    near_copy = pltpu.make_async_copy(near, wt.at[pl.ds(to, near.shape[0]), :], near_sem)
    near_copy.start()

    def put(section, group, lane, width, lines, value):
        if section == 0:
            q_s[group, lines, :] = value
        else:
            k_s[group, lines, lane : lane + width] = value

    def run(half):
        for number, at, section, group, lane, width in numbered_chunks(channels, half):
            if section == 0:
                q_s[group] = whole_ref[number]
            elif section == 1 and width == GROUP:
                k_s[group, edge : edge + mid, :] = whole_ref[number, :mid, :]
            elif section == 1:
                k_s[group, edge : edge + mid, lane : lane + width] = part_ref[...]
        base = half * near.shape[0]
        project_rest(
            half, (0, 1), channels, lambda at, width: near[at - base : at - base + width, :], lambda at, width: wt[at : at + width, :],
            (xq_ref, mid_ref, outer_ref), put,
        )

    for half in range(2):
        pl.when(place_ref[HALF] == half)(functools.partial(run, half))
    near_copy.wait()


def value_kernel(first, place_ref, wt, whole_ref, mid_ref, outer_ref, v_s):
    here = range(first, first + v_s.shape[0])
    channels = wt.shape[1]
    edge, mid = outer_ref.shape[0] // 2, mid_ref.shape[0]

    def put(section, group, lane, width, lines, value):
        v_s[group - first, lines, lane : lane + width] = value

    def run(half):
        for number, at, section, group, lane, width in numbered_chunks(channels, half):
            if section == 2 and group in here:
                v_s[group - first, edge : edge + mid, :] = whole_ref[number, :mid, :]
        weights = lambda at, width: wt[at : at + width, :]
        project_rest(half, (2,), channels, weights, weights, (None, mid_ref, outer_ref), put, here)

    for half in range(2):
        pl.when(place_ref[HALF] == half)(functools.partial(run, half))


def carrier_kernel(offsets, place_ref, wt, *refs):
    shards = len(offsets)
    finals, refs = refs[:shards], refs[shards:]
    summary_ref, wo, kce, vc_s = refs
    per_row = summary_ref.shape[1]
    channels = wt.shape[1]
    groups = channels // GROUP
    heads = channels // HEAD_DIM
    factor = HEAD_DIM ** (-0.5)
    carriers_here = vc_s.shape[0]
    final_rows = wo.shape[0] // shards
    for j, off in enumerate(offsets):
        to = pl.multiple_of((place_ref[ROW] ^ off) * final_rows, 16)
        wo[pl.ds(to, final_rows), :] = finals[j][:final_rows, :]
    carriers = jnp.concatenate([final[final_rows:, :].astype(jnp.float32) for final in finals], axis=0)
    own = carriers[:carriers_here]
    carriers = layer_normalise(carriers).astype(jnp.bfloat16)
    own_norm = layer_normalise(own).astype(jnp.bfloat16)
    qc = (nt(own_norm, wt[:channels, :]) * factor).astype(jnp.bfloat16).astype(jnp.float32)
    kc = nt(carriers, wt[channels : 2 * channels, :]).astype(jnp.bfloat16)
    vc = nt(carriers, wt[2 * channels :, :]).astype(jnp.bfloat16)
    head_of = lax.broadcasted_iota(jnp.int32, (1, channels), 1) // HEAD_DIM
    stacked = jnp.concatenate([jnp.where(head_of == h, qc, 0.0) for h in range(heads)], axis=0)
    e = jnp.exp(nt(stacked.astype(jnp.bfloat16), kc))
    weights = (e / jnp.sum(e, axis=-1, keepdims=True)).astype(jnp.bfloat16)
    o = nn(weights, vc)
    mix = jnp.zeros((carriers_here, channels), jnp.float32)
    for h in range(heads):
        mix = jnp.where(head_of == h, o[h * carriers_here : (h + 1) * carriers_here, :], mix)
    renewed = own + nt(mix.astype(jnp.bfloat16), wo[...])
    for i in range(summary_ref.shape[0]):
        summary_ref[i] = renewed[i * per_row : (i + 1) * per_row, :].astype(jnp.bfloat16)
    fresh = nt(layer_normalise(renewed).astype(jnp.bfloat16), wt[channels:, :]).astype(jnp.bfloat16).astype(jnp.float32)
    vc_s[...] = fresh[:, channels:]
    same = (
        lax.broadcasted_iota(jnp.int32, (GROUP, GROUP), 0) // HEAD_DIM
        == lax.broadcasted_iota(jnp.int32, (GROUP, GROUP), 1) // HEAD_DIM
    )
    windows = kce.shape[0] // groups
    for w in range(windows):
        for g in range(groups):
            kce[w * groups + g] = jnp.where(same, fresh[w : w + 1, g * GROUP : (g + 1) * GROUP], 0.0).astype(jnp.bfloat16)


def attend_kernel(tall, broad, q_s, k_s, v_low, v_high, hide_ref, kce, vc_s, mix_s, pc_s, even_s, odd_s):
    groups, tiles = q_s.shape[0], hide_ref.shape[0]
    heads_in = GROUP // HEAD_DIM
    queries, span = TILE * TILE, 2 * TILE * TILE
    side = PATCH_SIDE // TILE
    wide = (tall + 1) * queries
    qi = lax.broadcasted_iota(jnp.int32, (queries, 2 * span), 0)
    ki = lax.broadcasted_iota(jnp.int32, (queries, 2 * span), 1)
    row_step = (ki % span) // TILE - qi // TILE
    col_step = (ki // span) * TILE + ki % TILE - qi % TILE
    seen = (row_step >= 0) & (row_step <= 2 * RADIUS) & (col_step >= 0) & (col_step <= 2 * RADIUS)
    band = jnp.where(seen, 0.0, HIDDEN)
    group_head = lax.broadcasted_iota(jnp.int32, (1, GROUP), 1) // HEAD_DIM
    only = [jnp.where(group_head == h, 1.0, 0.0).astype(jnp.bfloat16) for h in range(heads_in)]
    in_pair = LANES // HEAD_DIM
    pair_head = lax.broadcasted_iota(jnp.int32, (1, LANES), 1) // HEAD_DIM

    for c in range(broad):
        for w in range(tall // side):
            at = slice((c * tall + w * side) * queries, (c * tall + (w + 1) * side) * queries)
            window = w * (broad // side) + c // side
            for g in range(groups):
                pc_s[at, g * GROUP : (g + 1) * GROUP] = jnp.exp2(nt(q_s[g, at, :], kce[window * groups + g]))

    def keys_at(t):
        k0 = pl.multiple_of(t // tall * wide + t % tall * queries, queries)
        return k0, pl.multiple_of(k0 + wide, queries)

    def scores(t, ref):
        q_at = pl.multiple_of(t * queries, queries)
        k0, k1 = keys_at(t)
        for g in range(groups):
            q = q_s[g, pl.ds(q_at, queries), :]
            qq = jnp.concatenate([q * mask for mask in only], axis=0)
            k = jnp.concatenate([k_s[g, pl.ds(k0, span), :], k_s[g, pl.ds(k1, span), :]], axis=0)
            ref[g] = nt(qq, k)

    def finish(t, ref):
        q_at = pl.multiple_of(t * queries, queries)
        k0, k1 = keys_at(t)
        window = t % tall // side * (broad // side) + t // tall // side
        bias = band + hide_ref[t][0:1, :]
        for g in range(groups):
            p = jnp.exp2(ref[g].reshape(heads_in, queries, 2 * span) + bias[None])
            total = jnp.sum(p, axis=-1, keepdims=True)
            v_ref, at = (v_low, g) if g < v_low.shape[0] else (v_high, g - v_low.shape[0])
            v = jnp.concatenate([v_ref[at, pl.ds(k0, span), :], v_ref[at, pl.ds(k1, span), :]], axis=0)
            o = nn(p.reshape(heads_in * queries, 2 * span).astype(jnp.bfloat16), v).reshape(heads_in, queries, GROUP)
            v_new = vc_s[pl.ds(window, 1), g * GROUP : (g + 1) * GROUP]
            for j in range(GROUP // LANES):
                lanes = slice(j * LANES, (j + 1) * LANES)
                at = slice(g * GROUP + j * LANES, g * GROUP + (j + 1) * LANES)
                kept, kept_total = o[j * in_pair, :, lanes], total[j * in_pair]
                for h in range(1, in_pair):
                    kept = jnp.where(pair_head == h, o[j * in_pair + h, :, lanes], kept)
                    kept_total = jnp.where(pair_head == h, total[j * in_pair + h], kept_total)
                new = pc_s[pl.ds(q_at, queries), at]
                mixed = (kept + new * v_new[:, lanes]) / (kept_total + new)
                mix_s[pl.ds(q_at, queries), at] = mixed.astype(jnp.bfloat16)

    scores(0, even_s)

    def two(i, _):
        t = 2 * i
        scores(t + 1, odd_s)
        finish(t, even_s)
        scores(jnp.minimum(t + 2, tiles - 1), even_s)
        finish(t + 1, odd_s)
        return 0

    lax.fori_loop(0, tiles // 2, two, 0, unroll=4)


def out_kernel(x_ref, mix_s, wo, out_hbm, out_ref, out_sems):
    rows, cols, channels = x_ref.shape
    going = []
    for pair in range(cols // (2 * TILE)):
        both = slice(2 * pair * TILE, 2 * (pair + 1) * TILE)
        for g in range(channels // GROUP):
            at = slice(g * GROUP, (g + 1) * GROUP)
            w = wo[at, :]
            y = nt(mix_s[2 * pair * rows * TILE : 2 * (pair + 1) * rows * TILE, :], w).reshape(2, rows, TILE, GROUP)
            y = jnp.concatenate([y[0], y[1]], axis=1) + x_ref[:, both, at].astype(jnp.float32)
            out_ref[pair, :, :, at] = y.astype(jnp.bfloat16)
        copy = pltpu.make_async_copy(out_ref.at[pair], out_hbm.at[:, both, :], out_sems.at[pair])
        copy.start()
        going.append(copy)
    for copy in going:
        copy.wait()


def local(grid_elements, summary_vectors, triple_projection, final_projection, genuine_flags):
    rows, cols, channels = grid_elements.shape
    wide_rows, wide_cols = rows + 2 * RADIUS, cols + 2 * RADIUS

    triple_t, final_t = triple_projection.T, final_projection.T
    vmem = pl.BlockSpec(memory_space=pltpu.VMEM)
    anywhere = pl.BlockSpec(memory_space=pl.ANY)
    scalars = pl.BlockSpec(memory_space=pltpu.SMEM)
    hbm = pl.BlockSpec(memory_space=pltpu.HBM)
    small = pltpu.CompilerParams(vmem_limit_bytes=8 * 1024 * 1024)
    row_strip = jax.ShapeDtypeStruct((RADIUS, cols, channels), jnp.bfloat16)
    col_strip = jax.ShapeDtypeStruct((wide_rows // 2, 2 * RADIUS, channels), jnp.bfloat16)

    row, col, img = lax.axis_size("row"), lax.axis_size("col"), lax.axis_size("img")
    row_at, col_at, img_at = lax.axis_index("row"), lax.axis_index("col"), lax.axis_index("img")
    row_bits = bits_of(row)
    far, rest = row_bits[0], row_bits[1:]
    piece_rows = triple_t.shape[0] * 5 // (8 * img) // 16 * 16
    relays = img if piece_rows else 0
    starts = [(img_at - k) % img for k in range(relays)] + [jnp.int32(relays)]
    place = [row_at == 0, row_at == row - 1, col_at == 0, col_at == col - 1, row_at % 2 == 0, col_at % 2 == 0, row_at, row_at // far]
    place = jnp.stack([jnp.asarray(p).astype(jnp.int32) for p in place + [start * piece_rows for start in starts]])

    mark, even_rows, odd_rows, x = pl.pallas_call(
        edge_kernel,
        out_shape=(
            pltpu.VMEM((rows, cols, LANES), jnp.bfloat16),
            pltpu.VMEM(row_strip.shape, jnp.bfloat16),
            pltpu.VMEM(row_strip.shape, jnp.bfloat16),
            pltpu.VMEM(grid_elements.shape, jnp.bfloat16),
        ),
        in_specs=[scalars, hbm, hbm],
        out_specs=(vmem,) * 4,
        scratch_shapes=[
            pltpu.VMEM((rows, cols), jnp.int32),
            pltpu.VMEM((rows * cols, cols), jnp.bfloat16),
            pltpu.SemaphoreType.DMA((2,)),
        ],
        compiler_params=small,
        cost_estimate=pl.CostEstimate(flops=1_000_000, bytes_accessed=1_000_000, transcendentals=0),
        name="edge_rows",
    )(place, *(pltpu.with_memory_space_constraint(a, pltpu.HBM) for a in (genuine_flags, grid_elements)))
    mine, last = pl.pallas_call(
        piece_kernel,
        out_shape=(
            pltpu.VMEM((max(piece_rows, 16), channels), jnp.bfloat16),
            pltpu.VMEM((triple_t.shape[0] - relays * piece_rows, channels), jnp.bfloat16),
        ),
        in_specs=[scalars, hbm],
        out_specs=(vmem, vmem),
        scratch_shapes=[pltpu.SemaphoreType.DMA((2,))],
        compiler_params=small,
        cost_estimate=pl.CostEstimate(flops=1_000_000, bytes_accessed=1_000_000, transcendentals=0),
        name="pieces",
    )(place, pltpu.with_memory_space_constraint(after(triple_t, even_rows), pltpu.HBM))
    xq = pl.pallas_call(
        own_kernel,
        out_shape=pltpu.VMEM((rows * cols, channels), jnp.bfloat16),
        in_specs=[vmem],
        out_specs=vmem,
        compiler_params=small,
        cost_estimate=pl.CostEstimate(flops=1_000_000, bytes_accessed=1_000_000, transcendentals=0),
        name="own_norm",
    )(x)
    even_rows, odd_rows = pair_swapped(even_rows, odd_rows, "row")

    far_pieces = []
    if relays:
        first = swapped(mine, "row", far)
    far_last = swapped(after(last, even_rows, odd_rows), "row", far)

    own_rows = summary_vectors.shape[0] * summary_vectors.shape[1]
    carrier_tiles = -(-own_rows // TILE)
    even_cols, odd_cols = pl.pallas_call(
        strip_kernel,
        out_shape=(
            pltpu.VMEM((col_strip.shape[0] + carrier_tiles, *col_strip.shape[1:]), jnp.bfloat16),
            pltpu.VMEM(col_strip.shape, jnp.bfloat16),
        ),
        in_specs=[scalars] + [vmem] * 5,
        out_specs=(vmem,) * 2,
        scratch_shapes=[pltpu.VMEM((carrier_tiles * TILE, channels), jnp.float32)],
        compiler_params=small,
        cost_estimate=pl.CostEstimate(flops=1_000_000, bytes_accessed=2_000_000, transcendentals=0),
        name="edge_columns",
    )(place, x, after(mark, xq), even_rows, odd_rows, summary_vectors)
    even_cols, odd_cols = pair_swapped(even_cols, odd_cols, "col")
    groups = channels // GROUP
    triples, offsets = [triple_t], [0]
    for bit in rest:
        triples = triples + [swapped(p, "row", bit) for p in triples]
        offsets = offsets + [o ^ bit for o in offsets]
    mid = pl.pallas_call(
        middle_kernel,
        out_shape=pltpu.VMEM(((wide_cols // TILE - 2) * wide_rows * TILE, channels), jnp.bfloat16),
        in_specs=[scalars] + [vmem] * 3,
        out_specs=vmem,
        scratch_shapes=[pltpu.VMEM(row_strip.shape, jnp.float32)] * 2,
        compiler_params=small,
        cost_estimate=pl.CostEstimate(flops=1_000_000, bytes_accessed=1_000_000, transcendentals=0),
        name="middle_blocks",
    )(place, xq, even_rows, odd_rows)
    whole, part, near = pl.pallas_call(
        functools.partial(early_kernel, offsets),
        out_shape=(
            pltpu.VMEM((3 * groups // 2, rows * cols, GROUP), jnp.bfloat16),
            pltpu.VMEM((mid.shape[0], GROUP // 2), jnp.bfloat16),
            pltpu.VMEM((3 * channels // 2, channels), jnp.bfloat16),
        ),
        in_specs=[scalars] + [vmem] * (len(triples) + 2),
        out_specs=(vmem,) * 3,
        compiler_params=pltpu.CompilerParams(vmem_limit_bytes=16 * 1024 * 1024),
        cost_estimate=pl.CostEstimate(flops=1_000_000, bytes_accessed=1_000_000, transcendentals=0),
        name="project_early",
    )(place, *triples, xq, mid)

    carriers = pl.pallas_call(
        carrier_pair_kernel,
        out_shape=pltpu.VMEM((2 * own_rows, channels), jnp.bfloat16),
        in_specs=[vmem, anywhere],
        out_specs=vmem,
        scratch_shapes=[
            pltpu.VMEM((carrier_tiles, TILE, channels), jnp.bfloat16),
            pltpu.VMEM((2 * own_rows, channels), jnp.float32),
            pltpu.SemaphoreType.DMA,
        ],
        compiler_params=small,
        cost_estimate=pl.CostEstimate(flops=1_000, bytes_accessed=1_000, transcendentals=0),
        name="carrier_pair",
    )(summary_vectors, after(even_cols, near))
    parts = [carriers]
    for bit in bits_of(col)[:-1]:
        carriers = carriers if len(parts) == 1 else jnp.concatenate(parts, axis=0)
        got = swapped(carriers, "col", 2 * bit - 1)
        parts.append(got)
    if relays:
        first = after(first, even_cols, odd_cols, parts[0])
        others = [lax.ppermute(first, "img", [(i, (i + k) % img) for i in range(img)]) for k in range(1, relays)]
        far_pieces = [first] + others
    far_pieces.append(far_last)

    tiles = (rows // TILE) * (cols // TILE)
    keys = 4 * TILE * TILE
    outer, hide = pl.pallas_call(
        outer_kernel,
        out_shape=(
            pltpu.VMEM((2 * wide_rows * TILE, channels), jnp.bfloat16),
            pltpu.VMEM((tiles, 8, keys), jnp.float32),
        ),
        in_specs=[scalars] + [vmem] * 6,
        out_specs=(vmem,) * 2,
        scratch_shapes=[
            *[pltpu.VMEM((RADIUS, 2 * TILE, channels), jnp.float32)] * 2,
            *[pltpu.VMEM(col_strip.shape, jnp.float32)] * 2,
            *[pltpu.VMEM((*shape.shape[:2], LANES), jnp.float32) for shape in (row_strip, row_strip, col_strip, col_strip)],
            pltpu.VMEM((wide_rows * wide_cols, LANES), jnp.bfloat16),
        ],
        compiler_params=pltpu.CompilerParams(vmem_limit_bytes=12 * 1024 * 1024),
        cost_estimate=pl.CostEstimate(flops=10_000_000, bytes_accessed=6_000_000, transcendentals=1000),
        name="outer_blocks",
    )(place, xq, mark, even_rows, odd_rows, even_cols, odd_cols)

    final_pack = pl.pallas_call(
        pack_kernel,
        out_shape=pltpu.VMEM((final_t.shape[0] + col * own_rows, channels), jnp.bfloat16),
        in_specs=[vmem] * (1 + len(parts)),
        out_specs=vmem,
        compiler_params=small,
        cost_estimate=pl.CostEstimate(flops=1_000, bytes_accessed=1_000, transcendentals=0),
        name="final_pack",
    )(final_t, *parts[:-1], after(parts[-1], outer))
    finals = [final_pack]
    for bit in rest:
        finals = finals + [swapped(p, "row", bit) for p in finals]

    far_final = swapped(final_pack, "row", far)

    far_offsets = [far]
    far_pieces = [[after(piece, outer, got)] for piece in far_pieces]
    for bit in rest:
        far_pieces = [same + [swapped(p, "row", bit) for p in same] for same in far_pieces]
        far_offsets = far_offsets + [o ^ bit for o in far_offsets]

    numbered = [(off, number) for number in range(len(far_pieces)) for off in far_offsets]
    sources = [piece for same in far_pieces for piece in same]
    q, k, wt = pl.pallas_call(
        functools.partial(late_kernel, numbered, triple_t.shape[0]),
        out_shape=(
            jax.ShapeDtypeStruct((groups, rows * cols, GROUP), jnp.bfloat16),
            jax.ShapeDtypeStruct((groups, wide_rows * wide_cols, GROUP), jnp.bfloat16),
            jax.ShapeDtypeStruct((3 * channels, channels), jnp.bfloat16),
        ),
        in_specs=[scalars] + [vmem] * (len(sources) + 6),
        out_specs=(vmem,) * 3,
        scratch_shapes=[pltpu.SemaphoreType.DMA],
        compiler_params=pltpu.CompilerParams(vmem_limit_bytes=VMEM_BYTES),
        cost_estimate=pl.CostEstimate(flops=1_000_000, bytes_accessed=1_000_000, transcendentals=0),
        name="project_late",
    )(place, *sources, near, whole, part, xq, mid, outer)

    def values(first, count, wt):
        return pl.pallas_call(
            functools.partial(value_kernel, first),
            out_shape=jax.ShapeDtypeStruct((count, wide_rows * wide_cols, GROUP), jnp.bfloat16),
            in_specs=[scalars] + [vmem] * 4,
            out_specs=vmem,
            compiler_params=pltpu.CompilerParams(vmem_limit_bytes=VMEM_BYTES),
            cost_estimate=pl.CostEstimate(flops=1_000, bytes_accessed=1_000, transcendentals=0),
            name="values",
        )(place, wt, whole, mid, outer)

    split = groups // 2 + groups % 2
    v_low = values(0, split, wt)
    v_high = values(split, groups - split, after(wt, v_low))

    far_finals = [after(far_final, v_low)]
    for bit in rest:
        far_finals = far_finals + [swapped(p, "row", bit) for p in far_finals]
    finals, offsets = finals + far_finals, offsets + far_offsets
    carriers_here = carrier_tiles * TILE
    summary_result, wo, kce, vc = pl.pallas_call(
        functools.partial(carrier_kernel, offsets),
        out_shape=(
            jax.ShapeDtypeStruct(summary_vectors.shape, jnp.bfloat16),
            jax.ShapeDtypeStruct((channels, channels), jnp.bfloat16),
            jax.ShapeDtypeStruct((own_rows * groups, GROUP, GROUP), jnp.bfloat16),
            jax.ShapeDtypeStruct((carriers_here, channels), jnp.float32),
        ),
        in_specs=[scalars] + [vmem] * (1 + len(finals)),
        out_specs=(vmem,) * 4,
        compiler_params=pltpu.CompilerParams(vmem_limit_bytes=VMEM_BYTES),
        cost_estimate=pl.CostEstimate(flops=500_000_000, bytes_accessed=5_000_000, transcendentals=10_000),
        name="carriers",
    )(place, wt, *finals)

    scores = (groups, GROUP // HEAD_DIM * TILE * TILE, keys)
    mix = pl.pallas_call(
        functools.partial(attend_kernel, rows // TILE, cols // TILE),
        out_shape=jax.ShapeDtypeStruct((rows * cols, channels), jnp.bfloat16),
        in_specs=[vmem] * 7,
        out_specs=vmem,
        scratch_shapes=[
            pltpu.VMEM((rows * cols, channels), jnp.float32),
            pltpu.VMEM(scores, jnp.float32),
            pltpu.VMEM(scores, jnp.float32),
        ],
        compiler_params=pltpu.CompilerParams(vmem_limit_bytes=VMEM_BYTES),
        cost_estimate=pl.CostEstimate(flops=4_000_000_000, bytes_accessed=12_000_000, transcendentals=4_000_000),
        name="attend",
    )(q, k, v_low, v_high, hide, kce, vc)

    out = pl.pallas_call(
        out_kernel,
        out_shape=jax.ShapeDtypeStruct(grid_elements.shape, jnp.bfloat16),
        in_specs=[vmem] * 3,
        out_specs=anywhere,
        scratch_shapes=[
            pltpu.VMEM((cols // (2 * TILE), rows, 2 * TILE, channels), jnp.bfloat16),
            pltpu.SemaphoreType.DMA((cols // (2 * TILE),)),
        ],
        compiler_params=pltpu.CompilerParams(vmem_limit_bytes=VMEM_BYTES),
        cost_estimate=pl.CostEstimate(flops=1_200_000_000, bytes_accessed=6_000_000, transcendentals=0),
        name="out",
    )(x, mix, wo)
    return (out, summary_result)


def solution(mesh):
    placed = (
        P(("img", "row"), "col", None),
        P(("img", "row"), "col", None),
        P(None, "row"),
        P(None, "row"),
        P(("img", "row"), "col"),
    )
    return jax.shard_map(
        local,
        mesh=mesh,
        in_specs=placed,
        out_specs=(P(("img", "row"), "col", None), P(("img", "row"), "col", None)),
        check_vma=False,
    )
```
